32 devices in a mesh: dp: 16 (over z, y, core), mp: 2 (over x).
Axes of the slice: x: 2, y: 2, z: 4, core: 2. Of those that a mesh axis runs over, the one named last changes fastest.
Arguments:
- layer_input: bfloat16 [24576, 768], P('dp'), may hold values from -9 to 9
- page_boxes: int32 [24576, 4], P('dp'), may hold values from 0 to 1000
- output_grad: bfloat16 [24576, 768], P('dp'), may hold values from -6 to 6
- attn_proj: float32 [3, 768, 768], P(None, 'dp', 'mp'), may hold values from -0.21875 to 0.21875
- attn_first: float32 [3, 768, 768], P(None, 'dp', 'mp'), may hold values from -2.670288e-05 to 2.670288e-05
- attn_second: float32 [3, 768, 768], P(None, 'dp', 'mp'), may hold values from 6.958547e-13 to 1.1133676e-11
- box_proj: float32 [128, 768], P('dp', 'mp'), may hold values from -0.75 to 0.75
- box_first: float32 [128, 768], P('dp', 'mp'), may hold values from -2.670288e-05 to 2.670288e-05
- box_second: float32 [128, 768], P('dp', 'mp'), may hold values from 6.958547e-13 to 1.1133676e-11
- merge_proj: float32 [768, 768], P('mp', 'dp'), may hold values from -1.25 to 1.25
- merge_first: float32 [768, 768], P('mp', 'dp'), may hold values from -2.670288e-05 to 2.670288e-05
- merge_second: float32 [768, 768], P('mp', 'dp'), may hold values from 6.958547e-13 to 1.1133676e-11
- expand_proj: float32 [768, 3072], P('dp', 'mp'), may hold values from -0.3247595 to 0.3247595
- expand_first: float32 [768, 3072], P('dp', 'mp'), may hold values from -2.670288e-05 to 2.670288e-05
- expand_second: float32 [768, 3072], P('dp', 'mp'), may hold values from 6.958547e-13 to 1.1133676e-11
- shrink_proj: float32 [3072, 768], P('mp', 'dp'), may hold values from -0.109375 to 0.109375
- shrink_first: float32 [3072, 768], P('mp', 'dp'), may hold values from -2.670288e-05 to 2.670288e-05
- shrink_second: float32 [3072, 768], P('mp', 'dp'), may hold values from 6.958547e-13 to 1.1133676e-11
- vectors: float32 [12, 768], P(None, ('dp', 'mp')), may hold values from -0.9 to 2.7, as said below
- vector_first: float32 [12, 768], P(None, ('dp', 'mp')), may hold values from -5.340576e-05 to 5.340576e-05
- vector_second: float32 [12, 768], P(None, ('dp', 'mp')), may hold values from 2.783419e-12 to 4.4534702e-11
Outputs:
- layer_output: bfloat16 [24576, 768], P('dp')
- input_grad: bfloat16 [24576, 768], P('dp')
- grad_norm: float32 [], replicated
- attn_mean: float32 [3, 768, 768], P(None, 'dp', 'mp')
- attn_square: float32 [3, 768, 768], P(None, 'dp', 'mp')
- attn_master: float32 [3, 768, 768], P(None, 'dp', 'mp')
- attn_copy: bfloat16 [3, 768, 768], P(None, 'dp', 'mp')
- box_mean: float32 [128, 768], P('dp', 'mp')
- box_square: float32 [128, 768], P('dp', 'mp')
- box_master: float32 [128, 768], P('dp', 'mp')
- box_copy: bfloat16 [128, 768], P('dp', 'mp')
- merge_mean: float32 [768, 768], P('mp', 'dp')
- merge_square: float32 [768, 768], P('mp', 'dp')
- merge_master: float32 [768, 768], P('mp', 'dp')
- merge_copy: bfloat16 [768, 768], P('mp', 'dp')
- expand_mean: float32 [768, 3072], P('dp', 'mp')
- expand_square: float32 [768, 3072], P('dp', 'mp')
- expand_master: float32 [768, 3072], P('dp', 'mp')
- expand_copy: bfloat16 [768, 3072], P('dp', 'mp')
- shrink_mean: float32 [3072, 768], P('mp', 'dp')
- shrink_square: float32 [3072, 768], P('mp', 'dp')
- shrink_master: float32 [3072, 768], P('mp', 'dp')
- shrink_copy: bfloat16 [3072, 768], P('mp', 'dp')
- vector_mean: float32 [12, 768], P(None, ('dp', 'mp'))
- vector_square: float32 [12, 768], P(None, ('dp', 'mp'))
- vector_master: float32 [12, 768], P(None, ('dp', 'mp'))
The draws below stay inside these ranges and needn't reach their ends.
Inputs may be any that keep to these rules, and one draw needn't show every extreme that they name: `vectors`: norm gains are positive.
All inputs are finite; a program needn't handle non-finite values.
Results may differ from the reference program's by a relative error of at most 0.019.
Values may be sent and summed in bfloat16 or wider, within the bound.
A program may use at most 192 MiB of HBM per device.

```python
import math
import jax
import jax.numpy as jnp
from jax import lax

D = 768
H = 12
HD = 64
FF = 3072
FREQS = 32
PE = 128
NVEC = 12
PAGE = 512
STEP = 10
TOKENS = 24576
PAGES = 48
PARAMS = 7185408


def draw_layer_input(key, part):
    key = jax.random.fold_in(key, 11)
    column = jnp.arange(D, dtype=jnp.float32) / D
    base_draw = jnp.clip(jax.random.normal(key, (TOKENS, D), jnp.float32), -5.0, 5.0)
    col_scale = 0.6 * 3.0 ** column
    return (base_draw * col_scale[None, :]).astype(jnp.bfloat16)


def draw_expand_proj(key, part):
    key = jax.random.fold_in(key, 12)
    column = jnp.arange(FF, dtype=jnp.float32) / FF
    base_draw = jnp.clip(jax.random.normal(key, (D, FF), jnp.float32), -5.0, 5.0)
    col_scale = 0.6 * 3.0 ** column
    return (base_draw * col_scale[None, :] * D ** (-0.5)).astype(jnp.float32)


def draw_vectors(key, part):
    key = jax.random.fold_in(key, 13)
    column = jnp.arange(D, dtype=jnp.float32) / D
    row_index = jnp.arange(NVEC)[:, None]
    is_gain = (row_index == 0) | (row_index == 2)
    noise_draw = jnp.clip(jax.random.normal(key, (NVEC, D), jnp.float32), -3.0, 3.0)
    gain_ramp = 0.6 * 3.0 ** column
    gain_rows = gain_ramp[None, :] * (1.0 + 0.1 * noise_draw)
    bias_rows = 0.3 * noise_draw
    return jnp.where(is_gain, gain_rows, bias_rows).astype(jnp.float32)


def place_ends(values, key, smallest, largest):
    spot = [jax.random.randint(jax.random.fold_in(key, axis), (), 0, length) for axis, length in enumerate(values.shape)]
    widest = values.shape.index(max(values.shape))
    neighbour = spot[:widest] + [(spot[widest] + 1) % values.shape[widest]] + spot[widest + 1:]
    return values.at[tuple(spot)].set(smallest).at[tuple(neighbour)].set(largest)


def levels(own_key, dims, split, low, largest):
    loudness = 1.0
    for dim, parts in split:
        heights = jax.random.uniform(jax.random.fold_in(jax.random.fold_in(own_key, 6), dim), (parts,), jnp.float32, low / len(split), largest / len(split))
        loudness = loudness * jnp.repeat(jnp.exp(heights), dims[dim] // parts).reshape((-1,) + (1,) * (len(dims) - 1 - dim))
    return loudness


def scatter_about(key, shape, scale, most, pieces=(), kind=jnp.bfloat16):
    values = jax.random.normal(key, shape, jnp.float32) * scale
    if len(pieces) > 0:
        values = levels(key, shape, pieces, -0.22, 0.18) * values
    return jnp.clip(values, min=-most, max=most).astype(kind)


def setup_inputs(seed: int = 0) -> dict:
    key_list = jax.random.split(jax.random.key(seed), 22)
    return {
        "layer_input": draw_layer_input(jax.random.fold_in(key_list[21], 71), 0),
        "page_boxes": place_ends(jax.random.randint(key_list[1], (TOKENS, 4), 0, 1001), jax.random.fold_in(key_list[1], 1), 0, 1000).astype(jnp.int32),
        "output_grad": scatter_about(key_list[2], (TOKENS, D), 1.0, 6.0, ((0, 16),)),
        "attn_proj": scatter_about(key_list[3], (3, D, D), D ** -0.5, 0.21875, ((1, 16), (2, 2)), jnp.float32),
        "attn_first": scatter_about(key_list[4], (3, D, D), (0.0111 * PARAMS ** -0.5), 2.6702880859375e-05, ((1, 16), (2, 2)), jnp.float32),
        "attn_second": jnp.clip(jnp.exp(math.log(1.1133675578700597e-11) - 2.7725887 * jax.random.uniform(key_list[5], (3, D, D), jnp.float32) ** levels(key_list[5], (3, D, D), ((1, 16), (2, 2)), -0.2, 0.2)), 6.958547236687873e-13, 1.1133675578700597e-11),
        "box_proj": scatter_about(key_list[6], (PE, D), HD ** -0.5, 0.75, ((0, 16), (1, 2)), jnp.float32),
        "box_first": scatter_about(key_list[7], (PE, D), (0.0111 * PARAMS ** -0.5), 2.6702880859375e-05, ((0, 16), (1, 2)), jnp.float32),
        "box_second": jnp.clip(jnp.exp(math.log(1.1133675578700597e-11) - 2.7725887 * jax.random.uniform(key_list[8], (PE, D), jnp.float32) ** levels(key_list[8], (PE, D), ((0, 16), (1, 2)), -0.2, 0.2)), 6.958547236687873e-13, 1.1133675578700597e-11),
        "merge_proj": scatter_about(key_list[9], (D, D), (D // 32) ** -0.5, 1.25, ((0, 2), (1, 16)), jnp.float32),
        "merge_first": scatter_about(key_list[10], (D, D), (0.0111 * PARAMS ** -0.5), 2.6702880859375e-05, ((0, 2), (1, 16)), jnp.float32),
        "merge_second": jnp.clip(jnp.exp(math.log(1.1133675578700597e-11) - 2.7725887 * jax.random.uniform(key_list[11], (D, D), jnp.float32) ** levels(key_list[11], (D, D), ((0, 2), (1, 16)), -0.2, 0.2)), 6.958547236687873e-13, 1.1133675578700597e-11),
        "expand_proj": draw_expand_proj(jax.random.fold_in(key_list[21], 71), 0),
        "expand_first": scatter_about(key_list[13], (D, FF), (0.0111 * PARAMS ** -0.5), 2.6702880859375e-05, ((0, 16), (1, 2)), jnp.float32),
        "expand_second": jnp.clip(jnp.exp(math.log(1.1133675578700597e-11) - 2.7725887 * jax.random.uniform(key_list[14], (D, FF), jnp.float32) ** levels(key_list[14], (D, FF), ((0, 16), (1, 2)), -0.2, 0.2)), 6.958547236687873e-13, 1.1133675578700597e-11),
        "shrink_proj": scatter_about(key_list[15], (FF, D), FF ** -0.5, 0.109375, ((0, 2), (1, 16)), jnp.float32),
        "shrink_first": scatter_about(key_list[16], (FF, D), (0.0111 * PARAMS ** -0.5), 2.6702880859375e-05, ((0, 2), (1, 16)), jnp.float32),
        "shrink_second": jnp.clip(jnp.exp(math.log(1.1133675578700597e-11) - 2.7725887 * jax.random.uniform(key_list[17], (FF, D), jnp.float32) ** levels(key_list[17], (FF, D), ((0, 2), (1, 16)), -0.2, 0.2)), 6.958547236687873e-13, 1.1133675578700597e-11),
        "vectors": draw_vectors(jax.random.fold_in(key_list[21], 71), 0),
        "vector_first": scatter_about(key_list[19], (NVEC, D), (0.0222 * PARAMS ** -0.5), 5.340576171875e-05, ((1, 32),), jnp.float32),
        "vector_second": jnp.clip(jnp.exp(math.log(4.453470231480239e-11) - 2.7725887 * jax.random.uniform(key_list[20], (NVEC, D), jnp.float32) ** levels(key_list[20], (NVEC, D), ((1, 32),), -0.2, 0.2)), 2.7834188946751492e-12, 4.453470231480239e-11),
    }


HIGHEST = lax.Precision.HIGHEST
NORM_EPS = 1e-12
CLIP_LIMIT = 0.1
BETA_ONE = 0.9
BETA_TWO = 0.999
ADAM_EPS = 1e-08
RATE_MATRIX = 0.05
RATE_VECTOR = 0.5
WEIGHT_DECAY = 0.01

@jax.custom_vjp
def low(v):
    return lax.optimization_barrier(v.astype(jnp.bfloat16)).astype(jnp.float32)

@jax.custom_vjp
def low_back(v):
    return v

def low_keep(v):
    return (low(v), None)

def low_pass(kept, grad):
    return (grad,)

def back_keep(v):
    return (v, None)

def back_low(kept, grad):
    return (low(grad),)
low.defvjp(low_keep, low_pass)
low_back.defvjp(back_keep, back_low)

def layer_norm(summed, row_gain, row_shift):
    row_mean = lax.optimization_barrier(jnp.mean(summed, axis=-1, keepdims=True))
    centred = summed - row_mean
    row_var = lax.optimization_barrier(jnp.mean(centred * centred, axis=-1, keepdims=True))
    return centred * lax.rsqrt(row_var + NORM_EPS) * row_gain + row_shift

def box_features(box_ints):
    coords = box_ints.astype(jnp.float32)
    centre_x = (coords[:, 0] + coords[:, 2]) * 0.5
    centre_y = (coords[:, 1] + coords[:, 3]) * 0.5
    omegas = 10000.0 ** (-jnp.arange(FREQS, dtype=jnp.float32) / FREQS)
    angle_x = centre_x[:, None] * omegas[None, :]
    angle_y = centre_y[:, None] * omegas[None, :]
    return (jnp.sin(angle_x), jnp.cos(angle_x), jnp.sin(angle_y), jnp.cos(angle_y))

def query_features(projected, sin_x, cos_x, sin_y, cos_y):
    sin_xh = sin_x[:, None, :]
    cos_xh = cos_x[:, None, :]
    sin_yh = sin_y[:, None, :]
    cos_yh = cos_y[:, None, :]
    part_sx = projected[:, :, 0:FREQS]
    part_cx = projected[:, :, FREQS:2 * FREQS]
    part_sy = projected[:, :, 2 * FREQS:3 * FREQS]
    part_cy = projected[:, :, 3 * FREQS:4 * FREQS]
    return jnp.concatenate([part_sx * sin_xh + part_cx * cos_xh, part_cx * sin_xh - part_sx * cos_xh, part_sy * sin_yh + part_cy * cos_yh, part_cy * sin_yh - part_sy * cos_yh], axis=2)

def forward(block_input, box_ints, attn_w, box_w, merge_w, expand_w, shrink_w, vector_rows):
    row_count = block_input.shape[0]
    page_count = row_count // PAGE
    qkv_low = low(attn_w)
    query_rows = low_back(low(jnp.dot(block_input, qkv_low[0], precision=HIGHEST) + vector_rows[6]))
    key_rows = low_back(low(jnp.dot(block_input, qkv_low[1], precision=HIGHEST)))
    value_rows = low_back(low(jnp.dot(block_input, qkv_low[2], precision=HIGHEST) + vector_rows[7]))
    sin_x, cos_x, sin_y, cos_y = box_features(box_ints)
    query_heads = query_rows.reshape(row_count, H, HD)
    box_heads = low(box_w).reshape(PE, H, HD)
    projected = low_back(jnp.einsum('thc,fhc->thf', query_heads, box_heads, precision=HIGHEST))
    query_feat = low(query_features(projected, sin_x, cos_x, sin_y, cos_y))
    key_feat = low(jnp.concatenate([cos_x, sin_x, cos_y, sin_y], axis=1))
    content = jnp.einsum('pihc,pjhc->phij', query_heads.reshape(page_count, PAGE, H, HD), key_rows.reshape(page_count, PAGE, H, HD), precision=HIGHEST)
    spatial = jnp.einsum('pihf,pjf->phij', query_feat.reshape(page_count, PAGE, H, PE), key_feat.reshape(page_count, PAGE, PE), precision=HIGHEST)
    scores = low_back((content + spatial) * HD ** (-0.5))
    attn_probs = low(jax.nn.softmax(scores, axis=-1))
    context = jnp.einsum('phij,pjhc->pihc', attn_probs, value_rows.reshape(page_count, PAGE, H, HD), precision=HIGHEST)
    context = low_back(low(context)).reshape(row_count, D)
    attn_branch = low_back(jnp.dot(context, low(merge_w), precision=HIGHEST))
    first_sum = block_input + attn_branch + vector_rows[4]
    normed_one = layer_norm(first_sum, vector_rows[0], vector_rows[1])
    pre_act = low_back(jnp.dot(low(normed_one), low(expand_w), precision=HIGHEST) + vector_rows[8:].reshape(FF))
    activated = low(jax.nn.gelu(pre_act, approximate=False))
    ffn_branch = low_back(jnp.dot(activated, low(shrink_w), precision=HIGHEST))
    second_sum = normed_one + ffn_branch + vector_rows[5]
    return layer_norm(second_sum, vector_rows[2], vector_rows[3])

def adam_step(master, first, second, gradient, rate, decay):
    new_first = BETA_ONE * first + (1.0 - BETA_ONE) * gradient
    new_second = BETA_TWO * second + (1.0 - BETA_TWO) * gradient * gradient
    first_hat = new_first / (1.0 - BETA_ONE ** STEP)
    second_hat = new_second / (1.0 - BETA_TWO ** STEP)
    new_master = master - rate * (first_hat / (jnp.sqrt(second_hat) + ADAM_EPS) + decay * master)
    return (new_first, new_second, new_master)

def reference(layer_input, page_boxes, output_grad, attn_proj, attn_first, attn_second, box_proj, box_first, box_second, merge_proj, merge_first, merge_second, expand_proj, expand_first, expand_second, shrink_proj, shrink_first, shrink_second, vectors, vector_first, vector_second):
    group = math.gcd(PAGES, 8)
    blocks = PAGES // group
    block_rows = group * PAGE
    inputs = layer_input.astype(jnp.float32).reshape(blocks, block_rows, D)
    box_blocks = page_boxes.reshape(blocks, block_rows, 4)
    cotangents = output_grad.astype(jnp.float32).reshape(blocks, block_rows, D)
    params = (attn_proj, box_proj, merge_proj, expand_proj, shrink_proj, vectors)

    def one_block(totals, item):
        block_in, block_boxes, block_cot = item

        def apply_layer(block_input, *weights):
            return forward(block_input, block_boxes, *weights)
        result, pullback = jax.vjp(apply_layer, block_in, *params)
        gradients = pullback(block_cot)
        totals = tuple((carried + fresh for carried, fresh in zip(totals, gradients[1:])))
        return (totals, (result.astype(jnp.bfloat16), gradients[0].astype(jnp.bfloat16)))
    starts = tuple((jnp.zeros_like(param) for param in params))
    totals, (outputs, in_grads) = lax.scan(one_block, starts, (inputs, box_blocks, cotangents))
    scaled = tuple((summed_grad * (1.0 / TOKENS) for summed_grad in totals))
    total_sq = jnp.zeros((), jnp.float32)
    for summed_grad in scaled:
        total_sq = total_sq + jnp.sum(summed_grad * summed_grad)
    grad_norm = jnp.sqrt(total_sq)
    clip_scale = CLIP_LIMIT / jnp.maximum(grad_norm, CLIP_LIMIT)
    attn_mean, attn_square, attn_master = adam_step(attn_proj, attn_first, attn_second, scaled[0] * clip_scale, RATE_MATRIX, WEIGHT_DECAY)
    box_mean, box_square, box_master = adam_step(box_proj, box_first, box_second, scaled[1] * clip_scale, RATE_MATRIX, WEIGHT_DECAY)
    merge_mean, merge_square, merge_master = adam_step(merge_proj, merge_first, merge_second, scaled[2] * clip_scale, RATE_MATRIX, WEIGHT_DECAY)
    expand_mean, expand_square, expand_master = adam_step(expand_proj, expand_first, expand_second, scaled[3] * clip_scale, RATE_MATRIX, WEIGHT_DECAY)
    shrink_mean, shrink_square, shrink_master = adam_step(shrink_proj, shrink_first, shrink_second, scaled[4] * clip_scale, RATE_MATRIX, WEIGHT_DECAY)
    vector_mean, vector_square, vector_master = adam_step(vectors, vector_first, vector_second, scaled[5] * clip_scale, RATE_VECTOR, 0.0)
    return (outputs.reshape(TOKENS, D), in_grads.reshape(TOKENS, D), grad_norm, attn_mean, attn_square, attn_master, attn_master.astype(jnp.bfloat16), box_mean, box_square, box_master, box_master.astype(jnp.bfloat16), merge_mean, merge_square, merge_master, merge_master.astype(jnp.bfloat16), expand_mean, expand_square, expand_master, expand_master.astype(jnp.bfloat16), shrink_mean, shrink_square, shrink_master, shrink_master.astype(jnp.bfloat16), vector_mean, vector_square, vector_master)
```

```python
import functools

import jax
import jax.numpy as jnp
from jax import lax
from jax.experimental import pallas as pl
from jax.experimental.pallas import tpu as pltpu
from jax.sharding import PartitionSpec as P

HD = 64
FREQS = 32
PE = 128
PAGE = 512
STEP = 10

NORM_EPS = 1e-12
CLIP_LIMIT = 0.1
BETA_ONE = 0.9
BETA_TWO = 0.999
ADAM_EPS = 1e-08
RATE_MATRIX = 0.05
RATE_VECTOR = 0.5
WEIGHT_DECAY = 0.01

F32 = jnp.float32
BF16 = jnp.bfloat16
VMEM_LIMIT = 60 * 1024 * 1024

NN = (((1,), (0,)), ((), ()))
NT = (((1,), (1,)), ((), ()))
TN = (((0,), (0,)), ((), ()))


def dot(lhs, rhs, dims=NN):
    return lax.dot_general(lhs, rhs, dims, preferred_element_type=F32)


def aligned(index, size):
    return pl.ds(pl.multiple_of(index * size, size), size)


def swap_blocks(feat):
    return jnp.concatenate(
        [
            feat[FREQS : 2 * FREQS],
            feat[0:FREQS],
            feat[3 * FREQS :],
            feat[2 * FREQS : 3 * FREQS],
        ],
        axis=0,
    )


def turn_factors(trig):
    cos_x, sin_x = trig[0:FREQS], trig[FREQS : 2 * FREQS]
    cos_y, sin_y = trig[2 * FREQS : 3 * FREQS], trig[3 * FREQS :]
    return (
        jnp.concatenate([sin_x, sin_x, sin_y, sin_y], axis=0),
        jnp.concatenate([cos_x, -cos_x, cos_y, -cos_y], axis=0),
    )


def attend_kernel(
    heads,
    x_ref,
    w_ref,
    box_ref,
    centre_ref,
    omega_ref,
    bias_ref,
    qa_ref,
    qtok_ref,
    kvtok_ref,
    kvt_ref,
    kft_ref,
    trig_ref,
    ctxt_ref,
    ctx_ref,
    log_ref,
    kftok_ref,
    box_heads,
):
    cols = heads * HD
    pages = x_ref.shape[0] // PAGE
    omega = omega_ref[...]
    angle_x = omega * centre_ref[0:1, :]
    angle_y = omega * centre_ref[1:2, :]
    trig_ref[0:FREQS, :] = jnp.cos(angle_x)
    trig_ref[FREQS : 2 * FREQS, :] = jnp.sin(angle_x)
    trig_ref[2 * FREQS : 3 * FREQS, :] = jnp.cos(angle_y)
    trig_ref[3 * FREQS :, :] = jnp.sin(angle_y)
    for head in range(heads):
        box_heads[head] = box_ref[:, head * HD : (head + 1) * HD]

    def project(page, carry):
        rows = aligned(page, PAGE)
        tokens = x_ref[rows, :]
        query = dot(tokens, w_ref[:, 0:cols]) + bias_ref[0:1, 0:cols]
        query = query.astype(BF16) * HD ** (-0.5)
        qtok_ref[rows, :] = query
        qa_rows = query.T
        pair = dot(tokens, w_ref[:, cols:]) + bias_ref[0:1, cols:]
        pair = pair.astype(BF16)
        kvtok_ref[rows, :] = pair
        kvt_ref[:, rows] = pair.T
        trig = trig_ref[:, rows]
        kft = trig.astype(BF16)
        kft_ref[:, rows] = kft
        kftok_ref[rows, :] = kft.T
        own, partner = turn_factors(trig)
        for head in range(heads):
            query_head = qa_rows[head * HD : (head + 1) * HD]
            proj = dot(box_heads[head], query_head)
            feat = proj * own + swap_blocks(proj) * partner
            qa_ref[head, 0:PE, rows] = feat.astype(BF16)
            qa_ref[head, PE : PE + HD, rows] = query_head
            qa_ref[head, PE + HD :, rows] = jnp.zeros((HD, PAGE), BF16)
        return carry

    lax.fori_loop(0, pages, project, 0)

    def attend(step, carry):
        page, pair = step // (heads // 2), step % (heads // 2)
        rows = aligned(page, PAGE)
        halves = []
        for side in range(2):
            head = pair * 2 + side
            lanes = aligned(head, 2 * HD)
            left = jnp.concatenate([kftok_ref[rows, :], kvtok_ref[rows, lanes]], axis=1)
            score = dot(left, qa_ref[head, :, rows])
            top = jnp.max(score, axis=0, keepdims=True)
            weight = jnp.exp(score - top)
            total = jnp.sum(weight, axis=0, keepdims=True)
            value = kvt_ref[pl.ds(pl.multiple_of(head * 2 * HD + HD, HD), HD), rows]
            halves.append(dot(value, weight.astype(BF16)) * (1.0 / total))
            log_ref[head, :, rows] = top + jnp.log(total)
        both = jnp.concatenate(halves, axis=0).astype(BF16)
        lanes = aligned(pair, 2 * HD)
        ctxt_ref[lanes, rows] = both
        ctx_ref[rows, lanes] = both.T
        return carry

    lax.fori_loop(0, pages * (heads // 2), attend, 0)


def attend_forward(x, weight, box, centres, omega, bias):
    tokens = x.shape[0]
    cols = weight.shape[1] // 3
    heads = cols // HD
    shapes = (
        ((heads, 4 * HD, tokens), BF16),
        ((tokens, cols), BF16),
        ((tokens, 2 * cols), BF16),
        ((2 * cols, tokens), BF16),
        ((PE, tokens), BF16),
        ((PE, tokens), F32),
        ((cols, tokens), BF16),
        ((tokens, cols), BF16),
        ((heads, 1, tokens), F32),
    )
    return pl.pallas_call(
        functools.partial(attend_kernel, heads),
        out_shape=[jax.ShapeDtypeStruct(s, d) for s, d in shapes],
        in_specs=[pl.BlockSpec(memory_space=pltpu.VMEM)] * 6,
        out_specs=[pl.BlockSpec(memory_space=pltpu.VMEM)] * len(shapes),
        scratch_shapes=[
            pltpu.VMEM((tokens, PE), BF16),
            pltpu.VMEM((heads, PE, HD), BF16),
        ],
        compiler_params=pltpu.CompilerParams(vmem_limit_bytes=VMEM_LIMIT),
        name="attend_forward",
    )(x, weight, box, centres, omega, bias)


CHUNK = 512
TILE = 256


def norm_stats(value):
    mean = jnp.mean(value, axis=-1, keepdims=True)
    centred = value - mean
    var = jnp.mean(centred * centred, axis=-1, keepdims=True)
    return centred, lax.rsqrt(var + NORM_EPS)


def norm_back(grad_normed, normed, scale):
    first = jnp.mean(grad_normed, axis=-1, keepdims=True)
    second = jnp.mean(grad_normed * normed, axis=-1, keepdims=True)
    return scale * (grad_normed - first - normed * second)


def col_sum(value):
    return jnp.sum(value, axis=0, keepdims=True)


def feed_kernel(
    x_ref,
    og_ref,
    ctx_ref,
    we_ref,
    ws_ref,
    wm_ref,
    vec_ref,
    bin_ref,
    out_ref,
    dctx_ref,
    dh1_ref,
    ge_ref,
    gs_ref,
    gm_ref,
    vsum_ref,
    bsum_ref,
    norm1,
    scale1,
    sum2,
    dnorm,
    al,
    act,
    slope,
    dh2l,
    dh1l,
    turned,
):
    tokens = x_ref.shape[0]
    sides = we_ref.shape[0]
    hidden = we_ref.shape[2]
    per_side = hidden // CHUNK
    steps = sides * per_side
    tiles = tokens // TILE

    def enter(tile, carry):
        rows = aligned(tile, TILE)
        total = x_ref[rows, :].astype(F32) + vec_ref[4:5, :]
        for side in range(sides):
            total += dot(ctx_ref[side, rows, :], wm_ref[side], NT)
        centred, scale = norm_stats(total)
        normed = centred * scale
        norm1[rows, :] = normed
        scale1[rows, :] = scale
        shifted = normed * vec_ref[0:1, :] + vec_ref[1:2, :]
        al[rows, :] = shifted.astype(BF16)
        sum2[rows, :] = shifted + vec_ref[5:6, :]
        return carry

    lax.fori_loop(0, tiles, enter, 0)

    def grow(step, carry):
        side, lanes = step // per_side, aligned(step % per_side, CHUNK)
        whole = aligned(step, CHUNK)

        def one(tile, inner):
            rows = aligned(tile, TILE)
            pre = dot(al[rows, :], we_ref[side, :, lanes]) + bin_ref[0:1, whole]
            phi = 0.5 + 0.5 * lax.erf(pre * 2.0 ** (-0.5))
            density = jnp.exp(pre * pre * -0.5) * (0.5 / jnp.pi) ** 0.5
            low = (pre * phi).astype(BF16)
            act[rows, whole] = low
            slope[rows, whole] = (phi + pre * density).astype(BF16)
            sum2[rows, :] += dot(low, ws_ref[side, :, lanes], NT)
            return inner

        lax.fori_loop(0, tiles, one, 0)
        return carry

    lax.fori_loop(0, steps, grow, 0)

    vsum_ref[...] = jnp.zeros_like(vsum_ref)

    def turn(tile, carry):
        rows = aligned(tile, TILE)
        centred, scale = norm_stats(sum2[rows, :])
        normed = centred * scale
        out_ref[rows, :] = (normed * vec_ref[2:3, :] + vec_ref[3:4, :]).astype(BF16)
        grad = og_ref[rows, :].astype(F32)
        vsum_ref[2:3, :] += col_sum(grad * normed)
        vsum_ref[3:4, :] += col_sum(grad)
        back = norm_back(grad * vec_ref[2:3, :], normed, scale)
        vsum_ref[5:6, :] += col_sum(back)
        dh2l[rows, :] = back.astype(BF16)
        dnorm[rows, :] = back
        return carry

    lax.fori_loop(0, tiles, turn, 0)

    def shrink(step, carry):
        side, lanes = step // per_side, aligned(step % per_side, CHUNK)
        whole = aligned(step, CHUNK)
        bsum_ref[0:1, whole] = jnp.zeros((1, CHUNK), F32)

        def one(tile, inner):
            rows = aligned(tile, TILE)
            grad = dot(dh2l[rows, :], ws_ref[side, :, lanes])
            low = (grad * slope[rows, whole].astype(F32)).astype(BF16)
            slope[rows, whole] = low
            bsum_ref[0:1, whole] += col_sum(low.astype(F32))
            dnorm[rows, :] += dot(low, we_ref[side, :, lanes], NT)
            return inner

        lax.fori_loop(0, tiles, one, 0)
        return carry

    lax.fori_loop(0, steps, shrink, 0)

    def leave(tile, carry):
        rows = aligned(tile, TILE)
        grad = dnorm[rows, :]
        normed = norm1[rows, :]
        vsum_ref[0:1, :] += col_sum(grad * normed)
        vsum_ref[1:2, :] += col_sum(grad)
        back = norm_back(grad * vec_ref[0:1, :], normed, scale1[rows, :])
        vsum_ref[4:5, :] += col_sum(back)
        dh1_ref[rows, :] = back
        low = back.astype(BF16)
        dh1l[rows, :] = low
        for side in range(sides):
            dctx_ref[side, rows, :] = dot(low, wm_ref[side]).astype(BF16)
        return carry

    lax.fori_loop(0, tiles, leave, 0)

    turned[...] = dh2l[...].T

    def grad_shrink(step, carry):
        side, lanes = step // per_side, aligned(step % per_side, CHUNK)
        gs_ref[side, :, lanes] = dot(turned[...], act[:, aligned(step, CHUNK)]).astype(BF16)
        return carry

    lax.fori_loop(0, steps, grad_shrink, 0)
    turned[...] = al[...].T

    def grad_expand(step, carry):
        side, lanes = step // per_side, aligned(step % per_side, CHUNK)
        ge_ref[side, :, lanes] = dot(turned[...], slope[:, aligned(step, CHUNK)]).astype(BF16)
        return carry

    lax.fori_loop(0, steps, grad_expand, 0)
    turned[...] = dh1l[...].T
    for side in range(sides):
        gm_ref[side] = dot(turned[...], ctx_ref[side]).astype(BF16)


def feed_both(x, og, ctx, w_expand, w_shrink, w_merge, vecs, bias_in):
    tokens, width = x.shape
    sides, _, hidden = w_expand.shape
    cols = w_merge.shape[2]
    shapes = (
        ((tokens, width), BF16),
        ((sides, tokens, cols), BF16),
        ((tokens, width), F32),
        ((sides, width, hidden), BF16),
        ((sides, width, hidden), BF16),
        ((sides, width, cols), BF16),
        ((8, width), F32),
        ((8, sides * hidden), F32),
    )
    return pl.pallas_call(
        feed_kernel,
        out_shape=[jax.ShapeDtypeStruct(s, d) for s, d in shapes],
        in_specs=[pl.BlockSpec(memory_space=pltpu.VMEM)] * 8,
        out_specs=[pl.BlockSpec(memory_space=pltpu.VMEM)] * len(shapes),
        scratch_shapes=[
            pltpu.VMEM((tokens, width), F32),
            pltpu.VMEM((tokens, 1), F32),
            pltpu.VMEM((tokens, width), F32),
            pltpu.VMEM((tokens, width), F32),
            pltpu.VMEM((tokens, width), BF16),
            pltpu.VMEM((tokens, sides * hidden), BF16),
            pltpu.VMEM((tokens, sides * hidden), BF16),
            pltpu.VMEM((tokens, width), BF16),
            pltpu.VMEM((tokens, width), BF16),
            pltpu.VMEM((width, tokens), BF16),
        ],
        compiler_params=pltpu.CompilerParams(vmem_limit_bytes=VMEM_LIMIT),
        name="feed_both",
    )(x, og, ctx, w_expand, w_shrink, w_merge, vecs, bias_in)


def attend_back_kernel(
    heads,
    x_ref,
    w_ref,
    box_ref,
    qa_ref,
    qtok_ref,
    kvtok_ref,
    kvt_ref,
    kft_ref,
    trig_ref,
    ctxt_ref,
    log_ref,
    dctx_ref,
    inp_ref,
    gw_ref,
    gbox_ref,
    qvsum_ref,
    kftok,
    dctxt,
    boxt,
    dtok,
    xt,
    gbox,
):
    cols = heads * HD
    tokens = x_ref.shape[0]
    pages = tokens // PAGE
    lane = lax.broadcasted_iota(jnp.int32, (1, 2 * HD), 1)
    lower = lane < HD
    boxt[...] = box_ref[...].T
    gbox[...] = jnp.zeros_like(gbox)

    def prepare(page, carry):
        rows = aligned(page, PAGE)
        kftok[rows, :] = kft_ref[:, rows].T
        dctxt[:, rows] = dctx_ref[rows, :].T
        xt[:, rows] = x_ref[rows, :].T
        return carry

    lax.fori_loop(0, pages, prepare, 0)

    def attend(step, carry):
        page, pair = step // (heads // 2), step % (heads // 2)
        rows = aligned(page, PAGE)
        own, partner = turn_factors(trig_ref[:, rows])
        pair_lanes = aligned(pair, 2 * HD)
        query_pair = qtok_ref[rows, pair_lanes]
        dctx_pair = dctx_ref[rows, pair_lanes]
        halves = []
        boxes = []
        for side in range(2):
            head = pair * 2 + side
            lanes = aligned(head, 2 * HD)
            key_value = kvtok_ref[rows, lanes]
            left = jnp.concatenate([kftok[rows, :], key_value], axis=1)
            score = dot(left, qa_ref[head, :, rows])
            prob = jnp.exp(score - log_ref[head, :, rows])
            prob_low = prob.astype(BF16)
            head_rows = pl.ds(pl.multiple_of(head * HD, HD), HD)
            dctx_head = dctxt[head_rows, rows]
            grad_prob = dot(
                key_value, jnp.concatenate([jnp.zeros((HD, PAGE), BF16), dctx_head], axis=0)
            )
            inner = col_sum(dctx_head.astype(F32) * ctxt_ref[head_rows, rows].astype(F32))
            grad_score = (prob * (grad_prob - inner)).astype(BF16)
            if side == 0:
                both = jnp.concatenate([query_pair[:, 0:HD], dctx_pair[:, 0:HD]], axis=1)
            else:
                both = jnp.concatenate([query_pair[:, HD:], dctx_pair[:, HD:]], axis=1)
            from_score = dot(grad_score, both)
            from_prob = dot(prob_low, both)
            grad_kv = jnp.where(lower, from_score, from_prob).astype(BF16)
            dtok[rows, pl.ds(pl.multiple_of(cols + head * 2 * HD, 2 * HD), 2 * HD)] = grad_kv
            keys = jnp.concatenate(
                [kft_ref[:, rows], kvt_ref[pl.ds(pl.multiple_of(head * 2 * HD, HD), HD), rows]],
                axis=0,
            )
            grad_query = dot(keys, grad_score) * HD ** (-0.5)
            feat = grad_query[0:PE]
            proj = (feat * own - swap_blocks(feat) * partner).astype(BF16)
            halves.append(grad_query[PE:] + dot(boxt[head_rows, :], proj))
            boxes.append(dot(proj, query_pair))
        gbox[:, pair_lanes] += jnp.where(lower, boxes[0], boxes[1])
        dtok[rows, pair_lanes] = jnp.concatenate(halves, axis=0).astype(BF16).T
        return carry

    lax.fori_loop(0, pages * (heads // 2), attend, 0)
    gbox_ref[...] = gbox[...] * HD**0.5

    def spread(page, carry):
        rows = aligned(page, PAGE)
        inp_ref[rows, :] = dot(dtok[rows, :], w_ref[...], NT)
        return carry

    lax.fori_loop(0, pages, spread, 0)

    def gather(step, carry):
        lanes = aligned(step, 2 * HD * 3)
        gw_ref[:, lanes] = dot(xt[...], dtok[:, lanes]).astype(BF16)
        qvsum_ref[0:1, lanes] = col_sum(dtok[:, lanes].astype(F32))
        return carry

    lax.fori_loop(0, 3 * cols // (2 * HD * 3), gather, 0)


def attend_backward(x, weight, box, kept, dctx):
    tokens, width = x.shape
    cols = weight.shape[1] // 3
    heads = cols // HD
    shapes = (
        ((tokens, width), F32),
        ((width, 3 * cols), BF16),
        ((PE, cols), F32),
        ((8, 3 * cols), F32),
    )
    return pl.pallas_call(
        functools.partial(attend_back_kernel, heads),
        out_shape=[jax.ShapeDtypeStruct(s, d) for s, d in shapes],
        in_specs=[pl.BlockSpec(memory_space=pltpu.VMEM)] * 12,
        out_specs=[pl.BlockSpec(memory_space=pltpu.VMEM)] * len(shapes),
        scratch_shapes=[
            pltpu.VMEM((tokens, PE), BF16),
            pltpu.VMEM((cols, tokens), BF16),
            pltpu.VMEM((cols, PE), BF16),
            pltpu.VMEM((tokens, 3 * cols), BF16),
            pltpu.VMEM((width, tokens), BF16),
            pltpu.VMEM((PE, cols), F32),
        ],
        compiler_params=pltpu.CompilerParams(vmem_limit_bytes=VMEM_LIMIT),
        name="attend_backward",
    )(x, weight, box, *kept, dctx)


def adam_step(master, first, second, gradient, rate, decay):
    new_first = BETA_ONE * first + (1.0 - BETA_ONE) * gradient
    new_second = BETA_TWO * second + (1.0 - BETA_TWO) * gradient * gradient
    first_hat = new_first / (1.0 - BETA_ONE**STEP)
    second_hat = new_second / (1.0 - BETA_TWO**STEP)
    new_master = master - rate * (first_hat / (jnp.sqrt(second_hat) + ADAM_EPS) + decay * master)
    return (new_first, new_second, new_master)


def pack_qkv(shard):
    rows, cols = shard.shape[1:]
    heads = cols // HD
    pairs = jnp.stack([shard[1].reshape(rows, heads, HD), shard[2].reshape(rows, heads, HD)], axis=2)
    return jnp.concatenate([shard[0], pairs.reshape(rows, 2 * cols)], axis=1)


def unpack_qkv(packed):
    rows, cols = packed.shape[0], packed.shape[1] // 3
    pairs = packed[:, cols:].reshape(rows, cols // HD, 2, HD)
    return jnp.stack(
        [packed[:, :cols], pairs[:, :, 0].reshape(rows, cols), pairs[:, :, 1].reshape(rows, cols)]
    )


def on_device(
    layer_input,
    page_boxes,
    output_grad,
    attn_proj,
    attn_first,
    attn_second,
    box_proj,
    box_first,
    box_second,
    merge_proj,
    merge_first,
    merge_second,
    expand_proj,
    expand_first,
    expand_second,
    shrink_proj,
    shrink_first,
    shrink_second,
    vectors,
    vector_first,
    vector_second,
):
    mp_count = lax.axis_size("mp")
    dp_count = lax.axis_size("dp")
    mp_index = lax.axis_index("mp")
    tokens, width = layer_input.shape
    cols = attn_proj.shape[2]
    heads = cols // HD
    own_tokens = tokens // mp_count
    inv_tokens = 1.0 / (tokens * dp_count)

    shard_qkv = pack_qkv(attn_proj).astype(BF16)
    shard_feed = jnp.stack([expand_proj, shrink_proj.T]).astype(BF16)
    shard_merge = merge_proj.T.astype(BF16)
    w_qkv = lax.all_gather(shard_qkv, "dp", axis=0, tiled=True)
    w_box = lax.all_gather(box_proj.astype(BF16), "dp", axis=0, tiled=True)
    w_feed = lax.all_gather(lax.all_gather(shard_feed, "dp", axis=1, tiled=True), "mp", axis=1)
    w_merge = lax.all_gather(lax.all_gather(shard_merge, "dp", axis=0, tiled=True), "mp", axis=0)
    vecs = lax.all_gather(vectors, ("dp", "mp"), axis=1, tiled=True)

    def own_cols(row):
        return lax.dynamic_slice_in_dim(row, mp_index * cols, cols)

    bias_value = own_cols(vecs[7]).reshape(heads, HD)
    bias_pair = jnp.concatenate([jnp.zeros_like(bias_value), bias_value], axis=1)
    bias = jnp.concatenate([own_cols(vecs[6]), bias_pair.reshape(-1)])[None, :]
    bias_in = vecs[8:].reshape(1, -1)

    coords = page_boxes.astype(F32)
    centres = jnp.stack([coords[:, 0] + coords[:, 2], coords[:, 1] + coords[:, 3]]) * 0.5
    omega = (10000.0 ** (-jnp.arange(FREQS, dtype=F32) / FREQS))[:, None]
    kept = attend_forward(layer_input, w_qkv, w_box, centres, omega, bias)
    *kept, context, log_total = kept

    def own_rows(array):
        return lax.dynamic_slice_in_dim(array, mp_index * own_tokens, own_tokens)

    context = lax.all_to_all(
        context.reshape(mp_count, own_tokens, cols), "mp", split_axis=0, concat_axis=0
    )
    out_own, dctx, dh1, g_expand, g_shrink, g_merge, vec_sum, bias_sum = feed_both(
        own_rows(layer_input),
        own_rows(output_grad),
        context,
        w_feed[0],
        w_feed[1],
        w_merge,
        vecs[0:8],
        bias_in,
    )
    layer_out = lax.all_gather(out_own, "mp", axis=0, tiled=True)
    dctx = lax.all_to_all(dctx, "mp", split_axis=0, concat_axis=0).reshape(tokens, cols)
    part, g_qkv, g_box, qkv_sum = attend_backward(
        layer_input, w_qkv, w_box, (*kept, log_total), dctx
    )
    own_part = lax.psum_scatter(part.astype(BF16), "mp", scatter_dimension=0, tiled=True)
    own_grad = (own_part.astype(F32) + dh1).astype(BF16)
    input_grad = lax.all_gather(own_grad, "mp", axis=0, tiled=True)

    def reduce_feed(grad):
        mine = lax.psum_scatter(grad, "dp", scatter_dimension=1, tiled=True)
        return lax.psum_scatter(mine, "mp", scatter_dimension=0, tiled=True)[0].astype(F32)

    shard_attn = unpack_qkv(
        lax.psum_scatter(g_qkv, "dp", scatter_dimension=0, tiled=True).astype(F32) * inv_tokens
    )
    shard_box = lax.psum_scatter(g_box, "dp", scatter_dimension=0, tiled=True) * inv_tokens
    shard_merge = reduce_feed(g_merge).T * inv_tokens
    shard_expand = reduce_feed(g_expand) * inv_tokens
    shard_shrink = reduce_feed(g_shrink).T * inv_tokens

    def placed(row):
        return lax.dynamic_update_slice_in_dim(
            jnp.zeros((width,), F32), row, mp_index * cols, 0
        )[None, :]

    value_sum = qkv_sum[0, cols:].reshape(heads, 2, HD)[:, 1].reshape(cols)
    vector_grad = jnp.concatenate(
        [
            vec_sum[0:6],
            placed(qkv_sum[0, 0:cols]),
            placed(value_sum),
            bias_sum[0].reshape(-1, width),
        ]
    )
    vector_shard = (
        lax.psum_scatter(vector_grad, ("dp", "mp"), scatter_dimension=1, tiled=True) * inv_tokens
    )
    square = sum(
        jnp.sum(shard * shard)
        for shard in (shard_attn, shard_box, shard_merge, shard_expand, shard_shrink, vector_shard)
    )
    grad_norm = jnp.sqrt(lax.psum(square, ("dp", "mp")))
    clip_scale = CLIP_LIMIT / jnp.maximum(grad_norm, CLIP_LIMIT)
    results = [layer_out, input_grad, grad_norm]
    for master, first, second, shard in (
        (attn_proj, attn_first, attn_second, shard_attn),
        (box_proj, box_first, box_second, shard_box),
        (merge_proj, merge_first, merge_second, shard_merge),
        (expand_proj, expand_first, expand_second, shard_expand),
        (shrink_proj, shrink_first, shrink_second, shard_shrink),
    ):
        new_first, new_second, new_master = adam_step(
            master, first, second, shard * clip_scale, RATE_MATRIX, WEIGHT_DECAY
        )
        results += [new_first, new_second, new_master, new_master.astype(BF16)]
    results += adam_step(
        vectors, vector_first, vector_second, vector_shard * clip_scale, RATE_VECTOR, 0.0
    )
    return tuple(results)


def solution(mesh):
    rows = P("dp", None)
    attn = P(None, "dp", "mp")
    tall = P("dp", "mp")
    wide = P("mp", "dp")
    vector = P(None, ("dp", "mp"))
    in_specs = (rows,) * 3 + (attn,) * 3 + (tall,) * 3 + (wide,) * 3 + (tall,) * 3 + (wide,) * 3
    in_specs += (vector,) * 3
    out_specs = (rows, rows, P()) + (attn,) * 4 + (tall,) * 4 + (wide,) * 4 + (tall,) * 4
    out_specs += (wide,) * 4 + (vector,) * 3
    return jax.shard_map(
        on_device, mesh=mesh, in_specs=in_specs, out_specs=out_specs, check_vma=False
    )
```

```python
import functools

import jax
import jax.numpy as jnp
import numpy as np
from jax import lax
from jax.experimental import pallas as pl
from jax.experimental.pallas import tpu as pltpu
from jax.sharding import PartitionSpec as P

HD = 64
FREQS = 32
PE = 128
PAGE = 512
STEP = 10

NORM_EPS = 1e-12
CLIP_LIMIT = 0.1
BETA_ONE = 0.9
BETA_TWO = 0.999
ADAM_EPS = 1e-08
RATE_MATRIX = 0.05
RATE_VECTOR = 0.5
WEIGHT_DECAY = 0.01

F32 = jnp.float32
BF16 = jnp.bfloat16
VMEM_LIMIT = 60 * 1024 * 1024

NN = (((1,), (0,)), ((), ()))
NT = (((1,), (1,)), ((), ()))
TN = (((0,), (0,)), ((), ()))


def dot(lhs, rhs, dims=NN):
    return lax.dot_general(lhs, rhs, dims, preferred_element_type=F32)


def aligned(index, size):
    return pl.ds(pl.multiple_of(index * size, size), size)


def swap_blocks(feat):
    return jnp.concatenate(
        [
            feat[FREQS : 2 * FREQS],
            feat[0:FREQS],
            feat[3 * FREQS :],
            feat[2 * FREQS : 3 * FREQS],
        ],
        axis=0,
    )


def turn_factors(trig):
    cos_x, sin_x = trig[0:FREQS], trig[FREQS : 2 * FREQS]
    cos_y, sin_y = trig[2 * FREQS : 3 * FREQS], trig[3 * FREQS :]
    return (
        jnp.concatenate([sin_x, sin_x, sin_y, sin_y], axis=0),
        jnp.concatenate([cos_x, -cos_x, cos_y, -cos_y], axis=0),
    )


MESH = pl.DeviceIdType.MESH
ALL = slice(None)
UNIT = 384


class Place:
    def __init__(self):
        rank = lax.axis_index("dp")
        self.m = lax.axis_index("mp")
        self.z = rank // 4
        self.y = (rank // 2) % 2
        self.c = rank % 2
        self.up = (rank + 4, self.m)
        self.down = (rank - 4, self.m)
        self.has_up = self.z < 3
        self.has_down = self.z > 0
        self.peer = {
            "x": (rank, 1 - self.m),
            "y": (rank + 2 - 4 * self.y, self.m),
            "c": (rank + 1 - 2 * self.c, self.m),
        }

    def greet(self):
        barrier = pltpu.get_barrier_semaphore()

        def signal(device):
            pl.semaphore_signal(barrier, inc=1, device_id=device, device_id_type=MESH)

        for device in self.peer.values():
            signal(device)
        pl.when(self.has_up)(lambda: signal(self.up))
        pl.when(self.has_down)(lambda: signal(self.down))
        pl.semaphore_wait(barrier, 3 + (1 - self.z // 3) + (self.z + 3) // 4)


def remote(src, dst, send_sem, recv_sem, device):
    return pltpu.make_async_remote_copy(
        src_ref=src,
        dst_ref=dst,
        send_sem=send_sem,
        recv_sem=recv_sem,
        device_id=device,
        device_id_type=MESH,
    )


class Spread:
    def __init__(self, place, ref, chunks, order, send_sems, recv_sems):
        self.chunks = chunks
        self.ref, self.send_sems, self.recv_sems = ref, send_sems, recv_sems
        have = {"x": place.m if "x" in order else 0, "z": place.z, "y": place.y, "c": place.c}
        self.sends, self.waits = [], []
        slot = 0
        for axis in order:
            if axis == "z":
                for far in (1, 2, 3):
                    sends, waits = [], []
                    for device, has, sign in (
                        (place.up, place.has_up, -1),
                        (place.down, place.has_down, 1),
                    ):
                        held = place.z + sign * (far - 1)
                        came = place.z + sign * far
                        sends.append(
                            (
                                has & (held >= 0) & (held <= 3),
                                dict(have, z=held),
                                device,
                                slot + (far - 1) * 2 + (sign + 1) // 2,
                                held,
                            )
                        )
                        waits.append(((came >= 0) & (came <= 3), dict(have, z=came), device, 0, came))
                    self.sends.append(sends)
                    self.waits.append(waits)
                slot += 6
                have = dict(have, z=ALL)
            else:
                mark = {"x": 4, "y": 5, "c": 6}[axis]
                self.sends.append([(None, have, place.peer[axis], slot, mark)])
                mine = {"x": place.m, "y": place.y, "c": place.c}[axis]
                self.waits.append([(None, dict(have, **{axis: 1 - mine}), place.peer[axis], 0, mark)])
                slot += 1
                have = dict(have, **{axis: ALL})
        self.count = len(self.sends) + 1

    def _copy(self, chunk, have, device, send_slot, mark):
        block = self.ref.at[chunk, have["x"], have["z"], have["y"], have["c"]]
        return remote(
            block, block, self.send_sems.at[chunk, send_slot], self.recv_sems.at[chunk, mark], device
        )

    def _each(self, items, chunk, act):
        for cond, have, device, send_slot, mark in items:

            def run(have=have, device=device, send_slot=send_slot, mark=mark):
                act(self._copy(chunk, have, device, send_slot, mark))

            if cond is None:
                run()
            else:
                pl.when(cond)(run)

    def stage(self, index, chunk):
        if index > 0:
            self._each(self.waits[index - 1], chunk, lambda copy: copy.wait_recv())
        if index < self.count - 1:
            self._each(self.sends[index], chunk, lambda copy: copy.start())

    def event(self, number):
        for index in range(self.count - 1, -1, -1):
            chunk = number - index
            if isinstance(chunk, int):
                if 0 <= chunk < self.chunks:
                    self.stage(index, chunk)
            elif self.chunks == 1:
                pl.when(chunk == 0)(lambda index=index: self.stage(index, 0))
            else:
                pl.when((chunk >= 0) & (chunk < self.chunks))(
                    lambda index=index, chunk=chunk: self.stage(index, chunk)
                )

    @property
    def events(self):
        return self.chunks + self.count - 1

    def drain(self):
        def one(chunk, carry):
            for sends in self.sends:
                self._each(sends, chunk, lambda copy: copy.wait_send())
            return carry

        lax.fori_loop(0, self.chunks, one, 0)


VROWS = 16


def rows_from_blocks(blocks, pick, counts):
    mp_count, dp_count = counts
    width = pick.shape[1]
    each = width // (mp_count * dp_count)
    wide = lax.dot_general(
        blocks, pick, NN, precision=lax.Precision.HIGHEST, preferred_element_type=F32
    )
    lane = lax.broadcasted_iota(jnp.int32, (VROWS, width), 1)
    table = jnp.zeros((VROWS, width), F32)
    for m in range(mp_count):
        for r in range(dp_count):
            first = (r * mp_count + m) * each
            row = (m * dp_count + r) * VROWS
            table += jnp.where((lane >= first) & (lane < first + each), wide[row : row + VROWS], 0.0)
    return table


def attend_setup(heads, m, box_full, vec_ref, centre_ref, omega_ref, trig_ref, box_heads, bias):
    cols = heads * HD
    for head in range(heads):
        box_heads[head] = box_full[:, head * HD : (head + 1) * HD]
    width = vec_ref.shape[1]
    own = jnp.where(m == 0, vec_ref[6:8, 0:cols], vec_ref[6:8, width - cols :])
    spot = lax.broadcasted_iota(jnp.int32, (cols, 2 * cols), 0)
    lane = lax.broadcasted_iota(jnp.int32, (cols, 2 * cols), 1)
    target = ((spot >> 6) << 7) + HD + (spot & (HD - 1))
    place = jnp.where(lane == target, 1.0, 0.0)
    spread = lax.dot_general(
        jnp.broadcast_to(own[1:2], (8, cols)),
        place,
        NN,
        precision=lax.Precision.HIGHEST,
        preferred_element_type=F32,
    )
    bias[0:1, 0:cols] = own[0:1]
    bias[0:1, cols:] = spread[0:1]


def attend_trig(omega_ref, centre_ref, trig_ref):
    angle_x = omega_ref[...] * centre_ref[0:1, :]
    angle_y = omega_ref[...] * centre_ref[1:2, :]
    trig_ref[0:FREQS, :] = jnp.cos(angle_x)
    trig_ref[FREQS : 2 * FREQS, :] = jnp.sin(angle_x)
    trig_ref[2 * FREQS : 3 * FREQS, :] = jnp.cos(angle_y)
    trig_ref[3 * FREQS :, :] = jnp.sin(angle_y)


def attend_kernel(heads, plan, *refs):
    cols = heads * HD
    m = lax.axis_index("mp")
    refs = list(refs)

    def take(count):
        head, refs[:] = refs[:count], refs[count:]
        return head

    x_ref, centre_ref, omega_ref = take(3)
    if plan is None:
        w_ref, box_ref, vec_ref = take(3)
    else:
        shard_a, shard_box, shard_vec, pick_ref, shard_e, shard_f = take(6)
    qa_ref, qtok_ref, kvtok_ref, kvt_ref, kft_ref, trig_ref, ctxt_ref, log_ref, ctxx_ref = take(9)
    if plan is not None:
        w_out, box_out, vec_ref, full_e, full_f = take(5)
    kftok_ref, box_heads, bias, ctx_ref = take(4)
    pages = x_ref.shape[0] // PAGE
    halves_of_page = 2
    piece = PAGE // halves_of_page
    own_pieces = pages

    if plan is None:
        attend_setup(heads, m, box_ref, vec_ref, centre_ref, omega_ref, trig_ref, box_heads, bias)
        attend_trig(omega_ref, centre_ref, trig_ref)

        def weights(chunk):
            return w_ref[chunk]

        def background(number):
            pass
    else:
        w_ref, box_gather, vec_gather, ctx_sem, a_sem, b_sem, v_sem, e_sem, f_sem, loc_sem = take(10)
        place = Place()
        at = (place.z, place.y, place.c)
        locals_ = [
            pltpu.make_async_copy(shard_e, full_e.at[(ALL, place.m, *at)], loc_sem.at[0]),
            pltpu.make_async_copy(shard_f, full_f.at[(ALL, place.m, *at)], loc_sem.at[1]),
        ]
        for copy in locals_:
            copy.start()
        w_ref[(ALL, 0, *at)] = shard_a[...]
        box_gather[(0, 0, *at)] = shard_box[...]
        vec_gather[(0, place.m, *at)] = shard_vec[...]
        for copy in locals_:
            copy.wait()
        place.greet()
        tree_v = Spread(place, vec_gather, 1, "xzyc", v_sem.at[0], v_sem.at[1])
        tree_b = Spread(place, box_gather, 1, "zyc", b_sem.at[0], b_sem.at[1])
        tree_a = Spread(place, w_ref, 3, "zyc", a_sem.at[0], a_sem.at[1])
        tree_e = Spread(place, full_e, 5, "zyxc", e_sem.at[0], e_sem.at[1])
        tree_f = Spread(place, full_f, 4, "xzyc", f_sem.at[0], f_sem.at[1])
        late = 4
        first = tree_a.events
        last = max(tree_e.events, tree_f.events)

        def background(number):
            tree_e.event(number)
            tree_f.event(number)

        def begin(number, carry):
            tree_a.event(number)
            tree_b.event(number)
            tree_v.event(number)
            background(number - late)
            pl.when(number == 1)(lambda: attend_trig(omega_ref, centre_ref, trig_ref))
            return carry

        lax.fori_loop(0, first, begin, 0)
        blocks = vec_gather[...].reshape(-1, 128)
        vec_ref[...] = rows_from_blocks(blocks, pick_ref[...], plan)
        box_out[...] = box_gather[...].reshape(PE, cols).astype(BF16)
        attend_setup(heads, m, box_out, vec_ref, centre_ref, omega_ref, trig_ref, box_heads, bias)
        copy_w = pltpu.make_async_copy(w_ref, w_out, loc_sem.at[0])
        copy_w.start()

        def weights(chunk):
            return w_ref[chunk].reshape(-1, cols)

    def project(page, carry):
        rows = aligned(page, PAGE)
        tokens = x_ref[rows, :]
        query = dot(tokens, weights(0)) + bias[0:1, 0:cols]
        query = query.astype(BF16) * HD ** (-0.5)
        qtok_ref[rows, :] = query
        qa_rows = query.T
        for half in range(2):
            lanes = slice(half * cols, (half + 1) * cols)
            pair = dot(tokens, weights(1 + half)) + bias[0:1, cols + half * cols : 2 * cols + half * cols]
            pair = pair.astype(BF16)
            kvtok_ref[rows, lanes] = pair
            kvt_ref[lanes, rows] = pair.T
        trig = trig_ref[:, rows]
        kft = trig.astype(BF16)
        kft_ref[:, rows] = kft
        kftok_ref[rows, :] = kft.T
        own, partner = turn_factors(trig)
        for head in range(heads):
            query_head = qa_rows[head * HD : (head + 1) * HD]
            proj = dot(box_heads[head], query_head)
            feat = proj * own + swap_blocks(proj) * partner
            qa_ref[head, 0:PE, rows] = feat.astype(BF16)
            qa_ref[head, PE : PE + HD, rows] = query_head
            qa_ref[head, PE + HD :, rows] = jnp.zeros((HD, PAGE), BF16)
        if plan is not None:
            background(page + first - late)
        return carry

    lax.fori_loop(0, pages, project, 0)

    def attend(step, carry):
        turn, pair = step // (heads // 2), step % (heads // 2)
        page = turn if plan is None else turn * m + (pages - 1 - turn) * (1 - m)
        rows = aligned(page, PAGE)
        halves = []
        for side in range(2):
            head = pair * 2 + side
            lanes = aligned(head, 2 * HD)
            left = jnp.concatenate([kftok_ref[rows, :], kvtok_ref[rows, lanes]], axis=1)
            score = dot(left, qa_ref[head, :, rows])
            top = jnp.max(score, axis=0, keepdims=True)
            weight = jnp.exp(score - top)
            total = jnp.sum(weight, axis=0, keepdims=True)
            value = kvt_ref[pl.ds(pl.multiple_of(head * 2 * HD + HD, HD), HD), rows]
            halves.append(dot(value, weight.astype(BF16)) * (1.0 / total))
            log_ref[head, :, rows] = top + jnp.log(total)
        both = jnp.concatenate(halves, axis=0).astype(BF16)
        lanes = aligned(pair, 2 * HD)
        ctxt_ref[lanes, rows] = both
        ctx_ref[rows, lanes] = both.T
        if plan is not None:
            pl.when((step % 2 == 0))(lambda: background(step // 2 + first - late + pages))
            pl.when(pair == heads // 2 - 1)(lambda: swap(turn))
        return carry

    def swap_copy(index):
        theirs = pages * (1 - m) + index
        return remote(
            ctx_ref.at[aligned(theirs, piece), :],
            ctxx_ref.at[m, aligned(index, piece), :],
            ctx_sem.at[0, index],
            ctx_sem.at[1, index],
            place.peer["x"],
        )

    def swap(turn):
        @pl.when(turn == 0)
        def _():
            swap_copy(2 - 2 * m).start()
            swap_copy(1).start()

        @pl.when(turn == 1)
        def _():
            swap_copy(2 * m).start()

    lax.fori_loop(0, pages * (heads // 2), attend, 0)
    if plan is None:
        ctxx_ref[...] = ctx_ref[...]
        return
    keep = pltpu.make_async_copy(
        ctx_ref.at[aligned(m, pages * piece), :], ctxx_ref.at[m], loc_sem.at[1]
    )
    keep.start()
    done = first - late + pages + (pages * (heads // 2) + 1) // 2

    def rest(number, carry):
        background(number)
        return carry

    lax.fori_loop(done, last, rest, 0)
    for index in range(own_pieces):
        copy = remote(
            ctx_ref.at[aligned(index, piece), :],
            ctxx_ref.at[1 - m, aligned(index, piece), :],
            ctx_sem.at[0, index],
            ctx_sem.at[1, index],
            place.peer["x"],
        )
        copy.wait_recv()
        copy.wait_send()
    keep.wait()
    copy_w.wait()
    for tree in (tree_v, tree_b, tree_a, tree_e, tree_f):
        tree.drain()


def attend_forward(x, centres, omega, weights, plan):
    tokens, width = x.shape
    cols = weights[1].shape[1]
    heads = cols // HD
    shapes = [
        ((heads, 4 * HD, tokens), BF16),
        ((tokens, cols), BF16),
        ((tokens, 2 * cols), BF16),
        ((2 * cols, tokens), BF16),
        ((PE, tokens), BF16),
        ((PE, tokens), F32),
        ((cols, tokens), BF16),
        ((heads, 1, tokens), F32),
    ]
    vmem = pl.BlockSpec(memory_space=pltpu.VMEM)
    free = pl.BlockSpec(memory_space=pl.ANY)
    scratch = [
        pltpu.VMEM((tokens, PE), BF16),
        pltpu.VMEM((heads, PE, HD), BF16),
        pltpu.VMEM((8, 3 * cols), F32),
        pltpu.VMEM((tokens, cols), BF16),
    ]
    in_specs, out_specs = [vmem] * 6, [vmem] * len(shapes)
    if plan is None:
        shapes.append(((tokens, cols), BF16))
        out_specs.append(vmem)
        extra = {}
    else:
        tail = (4, 2, 2, width // 16, UNIT)
        shapes += [
            ((2, tokens // 2, cols), BF16),
            ((3, 1, *tail), BF16),
            ((PE, cols), BF16),
            ((VROWS, width), F32),
            ((5, 2, *tail), BF16),
            ((4, 2, *tail), BF16),
        ]
        out_specs += [free, free, vmem, vmem, free, free]
        in_specs = [vmem] * 7 + [free] * 2
        scratch += [
            pltpu.VMEM((3, 1, *tail), BF16),
            pltpu.VMEM((1, 1, 4, 2, 2, PE // 16, cols), F32),
            pltpu.VMEM((1, 2, 4, 2, 2, VROWS, 128), F32),
            pltpu.SemaphoreType.DMA((2, 3)),
            pltpu.SemaphoreType.DMA((2, 3, 9)),
            pltpu.SemaphoreType.DMA((2, 1, 9)),
            pltpu.SemaphoreType.DMA((2, 1, 9)),
            pltpu.SemaphoreType.DMA((2, 5, 9)),
            pltpu.SemaphoreType.DMA((2, 4, 9)),
            pltpu.SemaphoreType.DMA((2,)),
        ]
        extra = dict(collective_id=0, has_side_effects=True)
    return pl.pallas_call(
        functools.partial(attend_kernel, heads, plan),
        out_shape=[jax.ShapeDtypeStruct(s, d) for s, d in shapes],
        in_specs=in_specs,
        out_specs=out_specs,
        scratch_shapes=scratch,
        compiler_params=pltpu.CompilerParams(vmem_limit_bytes=VMEM_LIMIT, **extra),
        name="attend_forward",
    )(x, centres, omega, *weights)


TILE = 256


def norm_stats(value):
    mean = jnp.mean(value, axis=-1, keepdims=True)
    centred = value - mean
    var = jnp.mean(centred * centred, axis=-1, keepdims=True)
    return centred, lax.rsqrt(var + NORM_EPS)


def norm_back(grad_normed, normed, scale):
    first = jnp.mean(grad_normed, axis=-1, keepdims=True)
    second = jnp.mean(grad_normed * normed, axis=-1, keepdims=True)
    return scale * (grad_normed - first - normed * second)


def col_sum(value):
    return jnp.sum(value, axis=0, keepdims=True)


def feed_kernel(
    x_ref,
    og_ref,
    ctx_ref,
    we_ref,
    ws_ref,
    vec_ref,
    out_ref,
    dctx_ref,
    dh1_ref,
    ge_ref,
    gs_ref,
    vsum_ref,
    norm1,
    scale1,
    sum2,
    dnorm,
    al,
    act,
    slope,
    dh2l,
    dh1l,
    turned,
):
    tokens = x_ref.shape[0]
    sides = we_ref.shape[1]
    per_side = (we_ref.shape[0] - 1) // 2
    steps = sides * per_side
    tiles = tokens // TILE
    wide = 2 * UNIT

    def two(ref, first, side):
        return jnp.concatenate([ref[first, side], ref[first + 1, side]], axis=1)

    def w_expand(step):
        return two(we_ref, 1 + 2 * (step % per_side), step // per_side)

    def w_shrink(step):
        return two(ws_ref, 2 * (step % per_side), step // per_side)

    def put_two(ref, first, side, value):
        ref[first, side] = value[:, 0:UNIT]
        ref[first + 1, side] = value[:, UNIT:]

    def enter(tile, carry):
        rows = aligned(tile, TILE)
        total = x_ref[rows, :].astype(F32) + vec_ref[4:5, :]
        for side in range(sides):
            total += dot(ctx_ref[side, rows, :], we_ref[0, side], NT)
        centred, scale = norm_stats(total)
        normed = centred * scale
        norm1[rows, :] = normed
        scale1[rows, :] = scale
        shifted = normed * vec_ref[0:1, :] + vec_ref[1:2, :]
        al[rows, :] = shifted.astype(BF16)
        sum2[rows, :] = shifted + vec_ref[5:6, :]
        return carry

    lax.fori_loop(0, tiles, enter, 0)

    def grow(step, carry):
        whole = aligned(step, wide)

        def one(tile, inner):
            rows = aligned(tile, TILE)
            pre = dot(al[rows, :], w_expand(step)) + vec_ref[pl.ds(8 + step, 1), :]
            phi = 0.5 + 0.5 * lax.erf(pre * 2.0 ** (-0.5))
            density = jnp.exp(pre * pre * -0.5) * (0.5 / jnp.pi) ** 0.5
            low = (pre * phi).astype(BF16)
            act[rows, whole] = low
            slope[rows, whole] = (phi + pre * density).astype(BF16)
            sum2[rows, :] += dot(low, w_shrink(step), NT)
            return inner

        lax.fori_loop(0, tiles, one, 0)
        return carry

    lax.fori_loop(0, steps, grow, 0)

    vsum_ref[...] = jnp.zeros_like(vsum_ref)

    def turn(tile, carry):
        rows = aligned(tile, TILE)
        centred, scale = norm_stats(sum2[rows, :])
        normed = centred * scale
        out_ref[rows, :] = (normed * vec_ref[2:3, :] + vec_ref[3:4, :]).astype(BF16)
        grad = og_ref[rows, :].astype(F32)
        vsum_ref[2:3, :] += col_sum(grad * normed)
        vsum_ref[3:4, :] += col_sum(grad)
        back = norm_back(grad * vec_ref[2:3, :], normed, scale)
        vsum_ref[5:6, :] += col_sum(back)
        dh2l[rows, :] = back.astype(BF16)
        dnorm[rows, :] = back
        return carry

    lax.fori_loop(0, tiles, turn, 0)

    def shrink(step, carry):
        whole = aligned(step, wide)

        def one(tile, inner):
            rows = aligned(tile, TILE)
            grad = dot(dh2l[rows, :], w_shrink(step))
            low = (grad * slope[rows, whole].astype(F32)).astype(BF16)
            slope[rows, whole] = low
            vsum_ref[pl.ds(8 + step, 1), :] += col_sum(low.astype(F32))
            dnorm[rows, :] += dot(low, w_expand(step), NT)
            return inner

        lax.fori_loop(0, tiles, one, 0)
        return carry

    lax.fori_loop(0, steps, shrink, 0)

    def leave(tile, carry):
        rows = aligned(tile, TILE)
        grad = dnorm[rows, :]
        normed = norm1[rows, :]
        vsum_ref[0:1, :] += col_sum(grad * normed)
        vsum_ref[1:2, :] += col_sum(grad)
        back = norm_back(grad * vec_ref[0:1, :], normed, scale1[rows, :])
        vsum_ref[4:5, :] += col_sum(back)
        dh1_ref[rows, :] = back
        low = back.astype(BF16)
        dh1l[rows, :] = low
        for side in range(sides):
            dctx_ref[side, rows, :] = dot(low, we_ref[0, side]).astype(BF16)
        return carry

    lax.fori_loop(0, tiles, leave, 0)

    turned[...] = dh2l[...].T

    def grad_shrink(step, carry):
        grad = dot(turned[...], act[:, aligned(step, wide)]).astype(BF16)
        put_two(gs_ref, 2 * (step % per_side), step // per_side, grad)
        return carry

    lax.fori_loop(0, steps, grad_shrink, 0)
    turned[...] = al[...].T

    def grad_expand(step, carry):
        grad = dot(turned[...], slope[:, aligned(step, wide)]).astype(BF16)
        put_two(ge_ref, 1 + 2 * (step % per_side), step // per_side, grad)
        return carry

    lax.fori_loop(0, steps, grad_expand, 0)
    turned[...] = dh1l[...].T
    for side in range(sides):
        ge_ref[0, side] = dot(turned[...], ctx_ref[side]).astype(BF16)


def feed_both(x, og, ctx, w_expand, w_shrink, vecs):
    tokens, width = x.shape
    chunks, sides = w_shrink.shape[0:2]
    hidden = chunks * UNIT
    shapes = (
        ((tokens, width), BF16),
        ((sides, tokens, UNIT), BF16),
        ((tokens, width), F32),
        ((chunks + 1, sides, width, UNIT), BF16),
        ((chunks, sides, width, UNIT), BF16),
        ((VROWS, width), F32),
    )
    return pl.pallas_call(
        feed_kernel,
        out_shape=[jax.ShapeDtypeStruct(s, d) for s, d in shapes],
        in_specs=[pl.BlockSpec(memory_space=pltpu.VMEM)] * 6,
        out_specs=[pl.BlockSpec(memory_space=pltpu.VMEM)] * len(shapes),
        scratch_shapes=[
            pltpu.VMEM((tokens, width), F32),
            pltpu.VMEM((tokens, 1), F32),
            pltpu.VMEM((tokens, width), F32),
            pltpu.VMEM((tokens, width), F32),
            pltpu.VMEM((tokens, width), BF16),
            pltpu.VMEM((tokens, sides * hidden), BF16),
            pltpu.VMEM((tokens, sides * hidden), BF16),
            pltpu.VMEM((tokens, width), BF16),
            pltpu.VMEM((tokens, width), BF16),
            pltpu.VMEM((width, tokens), BF16),
        ],
        compiler_params=pltpu.CompilerParams(vmem_limit_bytes=VMEM_LIMIT),
        name="feed_both",
    )(x, og, ctx, w_expand, w_shrink, vecs)


def attend_back_kernel(
    heads,
    x_ref,
    w_ref,
    box_ref,
    qa_ref,
    qtok_ref,
    kvtok_ref,
    kvt_ref,
    kft_ref,
    trig_ref,
    ctxt_ref,
    log_ref,
    dctx_ref,
    inp_ref,
    gw_ref,
    gbox_ref,
    qvsum_ref,
    kftok,
    dctxt,
    boxt,
    dtok,
    xt,
    gbox,
):
    cols = heads * HD
    tokens = x_ref.shape[0]
    pages = tokens // PAGE
    lane = lax.broadcasted_iota(jnp.int32, (1, 2 * HD), 1)
    lower = lane < HD
    boxt[...] = box_ref[...].T
    gbox[...] = jnp.zeros_like(gbox)

    def prepare(page, carry):
        rows = aligned(page, PAGE)
        kftok[rows, :] = kft_ref[:, rows].T
        dctxt[:, rows] = dctx_ref[rows, :].T
        xt[:, rows] = x_ref[rows, :].T
        return carry

    lax.fori_loop(0, pages, prepare, 0)

    def attend(step, carry):
        page, pair = step // (heads // 2), step % (heads // 2)
        rows = aligned(page, PAGE)
        own, partner = turn_factors(trig_ref[:, rows])
        pair_lanes = aligned(pair, 2 * HD)
        query_pair = qtok_ref[rows, pair_lanes]
        dctx_pair = dctx_ref[rows, pair_lanes]
        halves = []
        boxes = []
        for side in range(2):
            head = pair * 2 + side
            lanes = aligned(head, 2 * HD)
            key_value = kvtok_ref[rows, lanes]
            left = jnp.concatenate([kftok[rows, :], key_value], axis=1)
            score = dot(left, qa_ref[head, :, rows])
            prob = jnp.exp(score - log_ref[head, :, rows])
            prob_low = prob.astype(BF16)
            head_rows = pl.ds(pl.multiple_of(head * HD, HD), HD)
            dctx_head = dctxt[head_rows, rows]
            grad_prob = dot(
                key_value, jnp.concatenate([jnp.zeros((HD, PAGE), BF16), dctx_head], axis=0)
            )
            inner = col_sum(dctx_head.astype(F32) * ctxt_ref[head_rows, rows].astype(F32))
            grad_score = (prob * (grad_prob - inner)).astype(BF16)
            if side == 0:
                both = jnp.concatenate([query_pair[:, 0:HD], dctx_pair[:, 0:HD]], axis=1)
            else:
                both = jnp.concatenate([query_pair[:, HD:], dctx_pair[:, HD:]], axis=1)
            from_score = dot(grad_score, both)
            from_prob = dot(prob_low, both)
            grad_kv = jnp.where(lower, from_score, from_prob).astype(BF16)
            dtok[rows, pl.ds(pl.multiple_of(cols + head * 2 * HD, 2 * HD), 2 * HD)] = grad_kv
            keys = jnp.concatenate(
                [kft_ref[:, rows], kvt_ref[pl.ds(pl.multiple_of(head * 2 * HD, HD), HD), rows]],
                axis=0,
            )
            grad_query = dot(keys, grad_score) * HD ** (-0.5)
            feat = grad_query[0:PE]
            proj = (feat * own - swap_blocks(feat) * partner).astype(BF16)
            halves.append(grad_query[PE:] + dot(boxt[head_rows, :], proj))
            boxes.append(dot(proj, query_pair))
        gbox[:, pair_lanes] += jnp.where(lower, boxes[0], boxes[1])
        dtok[rows, pair_lanes] = jnp.concatenate(halves, axis=0).astype(BF16).T
        return carry

    lax.fori_loop(0, pages * (heads // 2), attend, 0)
    gbox_ref[...] = gbox[...] * HD**0.5

    def spread(page, carry):
        rows = aligned(page, PAGE)
        inp_ref[rows, :] = sum(
            dot(dtok[rows, chunk * UNIT : (chunk + 1) * UNIT], w_ref[chunk], NT) for chunk in range(3)
        )
        return carry

    lax.fori_loop(0, pages, spread, 0)

    def gather(step, carry):
        lanes = aligned(step, UNIT)
        gw_ref[step] = dot(xt[...], dtok[:, lanes]).astype(BF16)
        qvsum_ref[0:1, lanes] = col_sum(dtok[:, lanes].astype(F32))
        return carry

    lax.fori_loop(0, 3, gather, 0)


def attend_backward(x, weight, box, kept, dctx):
    tokens, width = x.shape
    cols = weight.shape[2]
    heads = cols // HD
    shapes = (
        ((tokens, width), F32),
        ((3, width, cols), BF16),
        ((PE, cols), F32),
        ((8, 3 * cols), F32),
    )
    return pl.pallas_call(
        functools.partial(attend_back_kernel, heads),
        out_shape=[jax.ShapeDtypeStruct(s, d) for s, d in shapes],
        in_specs=[pl.BlockSpec(memory_space=pltpu.VMEM)] * 12,
        out_specs=[pl.BlockSpec(memory_space=pltpu.VMEM)] * len(shapes),
        scratch_shapes=[
            pltpu.VMEM((tokens, PE), BF16),
            pltpu.VMEM((cols, tokens), BF16),
            pltpu.VMEM((cols, PE), BF16),
            pltpu.VMEM((tokens, 3 * cols), BF16),
            pltpu.VMEM((width, tokens), BF16),
            pltpu.VMEM((PE, cols), F32),
        ],
        compiler_params=pltpu.CompilerParams(vmem_limit_bytes=VMEM_LIMIT),
        name="attend_backward",
    )(x, weight, box, *kept, dctx)


def adam_step(master, first, second, gradient, rate, decay):
    new_first = BETA_ONE * first + (1.0 - BETA_ONE) * gradient
    new_second = BETA_TWO * second + (1.0 - BETA_TWO) * gradient * gradient
    first_hat = new_first / (1.0 - BETA_ONE**STEP)
    second_hat = new_second / (1.0 - BETA_TWO**STEP)
    new_master = master - rate * (first_hat / (jnp.sqrt(second_hat) + ADAM_EPS) + decay * master)
    return (new_first, new_second, new_master)


def pack_qkv(shard):
    rows, cols = shard.shape[1:]
    heads = cols // HD
    pairs = jnp.stack([shard[1].reshape(rows, heads, HD), shard[2].reshape(rows, heads, HD)], axis=2)
    pairs = pairs.reshape(rows, 2, cols)
    return jnp.stack([shard[0], pairs[:, 0], pairs[:, 1]])


def unpack_qkv(packed):
    rows, cols = packed.shape[1:]
    pairs = jnp.concatenate([packed[1], packed[2]], axis=1).reshape(rows, cols // HD, 2, HD)
    return jnp.stack(
        [packed[0], pairs[:, :, 0].reshape(rows, cols), pairs[:, :, 1].reshape(rows, cols)]
    )


def to_chunks(shard):
    rows = shard.shape[0]
    return shard.reshape(rows, -1, UNIT).transpose(1, 0, 2)


def from_chunks(chunks):
    return chunks.transpose(1, 0, 2).reshape(chunks.shape[1], -1)


def on_device(
    layer_input,
    page_boxes,
    output_grad,
    attn_proj,
    attn_first,
    attn_second,
    box_proj,
    box_first,
    box_second,
    merge_proj,
    merge_first,
    merge_second,
    expand_proj,
    expand_first,
    expand_second,
    shrink_proj,
    shrink_first,
    shrink_second,
    vectors,
    vector_first,
    vector_second,
):
    mp_count = lax.axis_size("mp")
    dp_count = lax.axis_size("dp")
    mp_index = lax.axis_index("mp")
    tokens, width = layer_input.shape
    cols = attn_proj.shape[2]
    heads = cols // HD
    own_tokens = tokens // mp_count
    inv_tokens = 1.0 / (tokens * dp_count)

    coords = page_boxes.astype(F32)
    centres = jnp.stack([coords[:, 0] + coords[:, 2], coords[:, 1] + coords[:, 3]]) * 0.5
    omega = (10000.0 ** (-jnp.arange(FREQS, dtype=F32) / FREQS))[:, None]
    shard_qkv = pack_qkv(attn_proj).astype(BF16)
    shard_e = jnp.concatenate([merge_proj.T[None], to_chunks(expand_proj)]).astype(BF16)
    shard_f = to_chunks(shrink_proj.T).astype(BF16)
    special = dp_count == 16 and mp_count == 2
    if special:
        each = vectors.shape[1]
        shard_vec = jnp.pad(vectors, ((0, VROWS - vectors.shape[0]), (0, 128 - each)))
        pick = np.zeros((128, width), np.float32)
        pick[np.arange(width) % each, np.arange(width)] = 1.0
        kept = attend_forward(
            layer_input,
            centres,
            omega,
            (shard_qkv, box_proj, shard_vec, jnp.asarray(pick), shard_e, shard_f),
            (mp_count, dp_count),
        )
        *kept, log_total, context, w_qkv, w_box, vecs, w_expand, w_shrink = kept
        w_qkv = w_qkv.reshape(3, width, cols)
        w_expand = w_expand.reshape(-1, mp_count, width, UNIT)
        w_shrink = w_shrink.reshape(-1, mp_count, width, UNIT)
    else:
        w_qkv = lax.all_gather(shard_qkv, "dp", axis=1, tiled=True)
        w_box = lax.all_gather(box_proj.astype(BF16), "dp", axis=0, tiled=True)
        w_expand = lax.all_gather(lax.all_gather(shard_e, "dp", axis=1, tiled=True), "mp", axis=1)
        w_shrink = lax.all_gather(lax.all_gather(shard_f, "dp", axis=1, tiled=True), "mp", axis=1)
        vecs = lax.all_gather(vectors, ("dp", "mp"), axis=1, tiled=True)
        vecs = jnp.pad(vecs, ((0, VROWS - vecs.shape[0]), (0, 0)))
        kept = attend_forward(layer_input, centres, omega, (w_qkv, w_box, vecs), None)
        *kept, log_total, context = kept
        context = lax.all_to_all(
            context.reshape(mp_count, own_tokens, cols), "mp", split_axis=0, concat_axis=0
        )

    def own_rows(array):
        return lax.dynamic_slice_in_dim(array, mp_index * own_tokens, own_tokens)

    out_own, dctx, dh1, g_expand, g_shrink, vec_sum = feed_both(
        own_rows(layer_input), own_rows(output_grad), context, w_expand, w_shrink, vecs
    )
    layer_out = lax.all_gather(out_own, "mp", axis=0, tiled=True)
    dctx = lax.all_to_all(dctx, "mp", split_axis=0, concat_axis=0).reshape(tokens, cols)
    part, g_qkv, g_box, qkv_sum = attend_backward(
        layer_input, w_qkv, w_box, (*kept, log_total), dctx
    )
    own_part = lax.psum_scatter(part.astype(BF16), "mp", scatter_dimension=0, tiled=True)
    own_grad = (own_part.astype(F32) + dh1).astype(BF16)
    input_grad = lax.all_gather(own_grad, "mp", axis=0, tiled=True)

    def reduce_feed(grad):
        mine = lax.psum_scatter(grad, "dp", scatter_dimension=2, tiled=True)
        return lax.psum_scatter(mine, "mp", scatter_dimension=1, tiled=True)[:, 0].astype(F32)

    shard_attn = unpack_qkv(
        lax.psum_scatter(g_qkv, "dp", scatter_dimension=1, tiled=True).astype(F32) * inv_tokens
    )
    shard_box = lax.psum_scatter(g_box, "dp", scatter_dimension=0, tiled=True) * inv_tokens
    sum_expand = reduce_feed(g_expand) * inv_tokens
    shard_merge = sum_expand[0].T
    shard_expand = from_chunks(sum_expand[1:])
    shard_shrink = from_chunks(reduce_feed(g_shrink) * inv_tokens).T

    def placed(row):
        return lax.dynamic_update_slice_in_dim(
            jnp.zeros((width,), F32), row, mp_index * cols, 0
        )[None, :]

    value_sum = qkv_sum[0, cols:].reshape(heads, 2, HD)[:, 1].reshape(cols)
    vector_grad = jnp.concatenate(
        [
            vec_sum[0:6],
            placed(qkv_sum[0, 0:cols]),
            placed(value_sum),
            vec_sum[8:12],
        ]
    )
    vector_shard = (
        lax.psum_scatter(vector_grad, ("dp", "mp"), scatter_dimension=1, tiled=True) * inv_tokens
    )
    square = sum(
        jnp.sum(shard * shard)
        for shard in (shard_attn, shard_box, shard_merge, shard_expand, shard_shrink, vector_shard)
    )
    grad_norm = jnp.sqrt(lax.psum(square, ("dp", "mp")))
    clip_scale = CLIP_LIMIT / jnp.maximum(grad_norm, CLIP_LIMIT)
    results = [layer_out, input_grad, grad_norm]
    for master, first, second, shard in (
        (attn_proj, attn_first, attn_second, shard_attn),
        (box_proj, box_first, box_second, shard_box),
        (merge_proj, merge_first, merge_second, shard_merge),
        (expand_proj, expand_first, expand_second, shard_expand),
        (shrink_proj, shrink_first, shrink_second, shard_shrink),
    ):
        new_first, new_second, new_master = adam_step(
            master, first, second, shard * clip_scale, RATE_MATRIX, WEIGHT_DECAY
        )
        results += [new_first, new_second, new_master, new_master.astype(BF16)]
    results += adam_step(
        vectors, vector_first, vector_second, vector_shard * clip_scale, RATE_VECTOR, 0.0
    )
    return tuple(results)


def solution(mesh):
    rows = P("dp", None)
    attn = P(None, "dp", "mp")
    tall = P("dp", "mp")
    wide = P("mp", "dp")
    vector = P(None, ("dp", "mp"))
    in_specs = (rows,) * 3 + (attn,) * 3 + (tall,) * 3 + (wide,) * 3 + (tall,) * 3 + (wide,) * 3
    in_specs += (vector,) * 3
    out_specs = (rows, rows, P()) + (attn,) * 4 + (tall,) * 4 + (wide,) * 4 + (tall,) * 4
    out_specs += (wide,) * 4 + (vector,) * 3
    return jax.shard_map(
        on_device, mesh=mesh, in_specs=in_specs, out_specs=out_specs, check_vma=False
    )
```

```python
import functools

import jax
import jax.numpy as jnp
import numpy as np
from jax import lax
from jax.experimental import pallas as pl
from jax.experimental.pallas import tpu as pltpu
from jax.sharding import PartitionSpec as P

HD = 64
FREQS = 32
PE = 128
PAGE = 512
STEP = 10

NORM_EPS = 1e-12
CLIP_LIMIT = 0.1
BETA_ONE = 0.9
BETA_TWO = 0.999
ADAM_EPS = 1e-08
RATE_MATRIX = 0.05
RATE_VECTOR = 0.5
WEIGHT_DECAY = 0.01

F32 = jnp.float32
BF16 = jnp.bfloat16
VMEM_LIMIT = 60 * 1024 * 1024

NN = (((1,), (0,)), ((), ()))
NT = (((1,), (1,)), ((), ()))
TN = (((0,), (0,)), ((), ()))


def dot(lhs, rhs, dims=NN):
    return lax.dot_general(lhs, rhs, dims, preferred_element_type=F32)


def aligned(index, size):
    return pl.ds(pl.multiple_of(index * size, size), size)


def swap_blocks(feat):
    return jnp.concatenate(
        [
            feat[FREQS : 2 * FREQS],
            feat[0:FREQS],
            feat[3 * FREQS :],
            feat[2 * FREQS : 3 * FREQS],
        ],
        axis=0,
    )


def turn_factors(trig):
    cos_x, sin_x = trig[0:FREQS], trig[FREQS : 2 * FREQS]
    cos_y, sin_y = trig[2 * FREQS : 3 * FREQS], trig[3 * FREQS :]
    return (
        jnp.concatenate([sin_x, sin_x, sin_y, sin_y], axis=0),
        jnp.concatenate([cos_x, -cos_x, cos_y, -cos_y], axis=0),
    )


MESH = pl.DeviceIdType.MESH
ALL = slice(None)
UNIT = 384


class Place:
    def __init__(self):
        rank = lax.axis_index("dp")
        self.m = lax.axis_index("mp")
        self.z = rank // 4
        self.y = (rank // 2) % 2
        self.c = rank % 2
        self.up = (rank + 4, self.m)
        self.down = (rank - 4, self.m)
        self.has_up = self.z < 3
        self.has_down = self.z > 0
        self.peer = {
            "x": (rank, 1 - self.m),
            "y": (rank + 2 - 4 * self.y, self.m),
            "c": (rank + 1 - 2 * self.c, self.m),
        }

    def greet(self):
        barrier = pltpu.get_barrier_semaphore()

        def signal(device):
            pl.semaphore_signal(barrier, inc=1, device_id=device, device_id_type=MESH)

        for device in self.peer.values():
            signal(device)
        pl.when(self.has_up)(lambda: signal(self.up))
        pl.when(self.has_down)(lambda: signal(self.down))
        pl.semaphore_wait(barrier, 3 + (1 - self.z // 3) + (self.z + 3) // 4)


def remote(src, dst, send_sem, recv_sem, device):
    return pltpu.make_async_remote_copy(
        src_ref=src,
        dst_ref=dst,
        send_sem=send_sem,
        recv_sem=recv_sem,
        device_id=device,
        device_id_type=MESH,
    )


class Spread:
    def __init__(self, place, ref, chunks, order, send_sems, recv_sems):
        self.chunks = chunks
        self.ref, self.send_sems, self.recv_sems = ref, send_sems, recv_sems
        have = {"x": place.m if "x" in order else 0, "z": place.z, "y": place.y, "c": place.c}
        self.sends, self.waits = [], []
        slot = 0
        for axis in order:
            if axis == "z":
                for far in (1, 2, 3):
                    sends, waits = [], []
                    for device, has, sign in (
                        (place.up, place.has_up, -1),
                        (place.down, place.has_down, 1),
                    ):
                        held = place.z + sign * (far - 1)
                        came = place.z + sign * far
                        sends.append(
                            (
                                has & (held >= 0) & (held <= 3),
                                dict(have, z=held),
                                device,
                                slot + (far - 1) * 2 + (sign + 1) // 2,
                                held,
                            )
                        )
                        waits.append(((came >= 0) & (came <= 3), dict(have, z=came), device, 0, came))
                    self.sends.append(sends)
                    self.waits.append(waits)
                slot += 6
                have = dict(have, z=ALL)
            else:
                mark = {"x": 4, "y": 5, "c": 6}[axis]
                self.sends.append([(None, have, place.peer[axis], slot, mark)])
                mine = {"x": place.m, "y": place.y, "c": place.c}[axis]
                self.waits.append([(None, dict(have, **{axis: 1 - mine}), place.peer[axis], 0, mark)])
                slot += 1
                have = dict(have, **{axis: ALL})
        self.count = len(self.sends) + 1

    def _copy(self, chunk, have, device, send_slot, mark):
        block = self.ref.at[chunk, have["x"], have["z"], have["y"], have["c"]]
        return remote(
            block, block, self.send_sems.at[chunk, send_slot], self.recv_sems.at[chunk, mark], device
        )

    def _each(self, items, chunk, act):
        for cond, have, device, send_slot, mark in items:

            def run(have=have, device=device, send_slot=send_slot, mark=mark):
                act(self._copy(chunk, have, device, send_slot, mark))

            if cond is None:
                run()
            else:
                pl.when(cond)(run)

    def stage(self, index, chunk):
        if index > 0:
            self._each(self.waits[index - 1], chunk, lambda copy: copy.wait_recv())
        if index < self.count - 1:
            self._each(self.sends[index], chunk, lambda copy: copy.start())

    def event(self, number):
        for index in range(self.count - 1, -1, -1):
            chunk = number - index
            if isinstance(chunk, int):
                if 0 <= chunk < self.chunks:
                    self.stage(index, chunk)
            elif self.chunks == 1:
                pl.when(chunk == 0)(lambda index=index: self.stage(index, 0))
            else:
                pl.when((chunk >= 0) & (chunk < self.chunks))(
                    lambda index=index, chunk=chunk: self.stage(index, chunk)
                )

    @property
    def events(self):
        return self.chunks + self.count - 1

    def drain(self):
        def one(chunk, carry):
            for sends in self.sends:
                self._each(sends, chunk, lambda copy: copy.wait_send())
            return carry

        lax.fori_loop(0, self.chunks, one, 0)


class Reduce:
    SLOT = {"c": 0, "z": 1, "y": 7, "x": 8}

    def __init__(self, place, full, total, lands, chunks, order, send_sems, recv_sems, finish):
        self.place, self.full, self.total, self.lands = place, full, total, lands
        self.chunks, self.send_sems, self.recv_sems, self.finish = chunks, send_sems, recv_sems, finish
        mine = {"x": place.m, "y": place.y}
        self.across = ALL if "x" in order else 0
        have = {"x": self.across, "z": ALL, "y": ALL}
        z = place.z
        self.steps = []
        for axis in order:
            land = lands[axis]
            if axis == "c":
                sends = [(None, None, (), place.peer["c"], 0)]
                waits = [(None, have, (), 0)]
                self.steps.append((land, sends, waits))
            elif axis == "z":
                for step in (1, 2, 3):
                    up, down = (step - 1) * 2 + 1, (step - 1) * 2 + 2
                    sends = [
                        (
                            place.has_up & (z <= step - 1),
                            dict(have, z=4 - step + z),
                            (0, step - 1),
                            place.up,
                            up,
                        ),
                        (
                            place.has_down & (3 - z <= step - 1),
                            dict(have, z=step - 4 + z),
                            (1, step - 1),
                            place.down,
                            down,
                        ),
                    ]
                    waits = [
                        (place.has_down & (z <= step), dict(have, z=3 - step + z), (0, step - 1), up),
                        (place.has_up & (3 - z <= step), dict(have, z=step + z - 3), (1, step - 1), down),
                    ]
                    self.steps.append((land, sends, waits))
                have = dict(have, z=z)
            else:
                sends = [(None, dict(have, **{axis: 1 - mine[axis]}), (), place.peer[axis], self.SLOT[axis])]
                have = dict(have, **{axis: mine[axis]})
                self.steps.append((land, sends, [(None, have, (), self.SLOT[axis])]))
        self.have = have
        self.count = len(self.steps) + 1

    def _source(self, chunk, have):
        if have is None:
            return self.full.at[chunk, self.across, :, :, 1 - self.place.c]
        return self.total.at[chunk, have["x"], have["z"], have["y"]]

    def _send(self, item, land, chunk, act):
        cond, have, spot, device, slot = item

        def run():
            act(
                remote(
                    self._source(chunk, have),
                    land.at[(chunk, *spot)],
                    self.send_sems.at[chunk, slot],
                    self.recv_sems.at[chunk, slot],
                    device,
                )
            )

        run() if cond is None else pl.when(cond)(run)

    def _take(self, item, land, chunk):
        cond, have, spot, slot = item

        def run():
            came = land.at[(chunk, *spot)]
            remote(
                came, came, self.send_sems.at[chunk, slot], self.recv_sems.at[chunk, slot], self.place.peer["c"]
            ).wait_recv()
            mine = self.total.at[chunk, have["x"], have["z"], have["y"]]
            value = mine[...].astype(F32) + came[...].astype(F32)
            mine[...] = value.astype(mine.dtype)

        run() if cond is None else pl.when(cond)(run)

    def stage(self, index, chunk):
        if index > 0:
            land, _, waits = self.steps[index - 1]
            for item in waits:
                self._take(item, land, chunk)
        if index < self.count - 1:
            land, sends, _ = self.steps[index]
            for item in sends:
                self._send(item, land, chunk, lambda copy: copy.start())
        else:
            self.finish(chunk, self.total[chunk, self.have["x"], self.have["z"], self.have["y"]])

    def event(self, number):
        for index in range(self.count - 1, -1, -1):
            chunk = number - index
            if self.chunks == 1:
                pl.when(chunk == 0)(lambda index=index: self.stage(index, 0))
            else:
                pl.when((chunk >= 0) & (chunk < self.chunks))(
                    lambda index=index, chunk=chunk: self.stage(index, chunk)
                )

    @property
    def events(self):
        return self.chunks + self.count - 1

    def drain(self):
        def one(chunk, carry):
            for land, sends, _ in self.steps:
                for item in sends:
                    self._send(item, land, chunk, lambda copy: copy.wait_send())
            return carry

        lax.fori_loop(0, self.chunks, one, 0)


VROWS = 16


def rows_from_blocks(blocks, pick, counts):
    mp_count, dp_count = counts
    width = pick.shape[1]
    each = width // (mp_count * dp_count)
    wide = lax.dot_general(
        blocks, pick, NN, precision=lax.Precision.HIGHEST, preferred_element_type=F32
    )
    lane = lax.broadcasted_iota(jnp.int32, (VROWS, width), 1)
    table = jnp.zeros((VROWS, width), F32)
    for m in range(mp_count):
        for r in range(dp_count):
            first = (r * mp_count + m) * each
            row = (m * dp_count + r) * VROWS
            table += jnp.where((lane >= first) & (lane < first + each), wide[row : row + VROWS], 0.0)
    return table


def attend_setup(heads, m, box_full, vec_ref, centre_ref, omega_ref, trig_ref, box_heads, bias):
    cols = heads * HD
    for head in range(heads):
        box_heads[head] = box_full[:, head * HD : (head + 1) * HD]
    width = vec_ref.shape[1]
    own = jnp.where(m == 0, vec_ref[6:8, 0:cols], vec_ref[6:8, width - cols :])
    spread = exact_dot(jnp.broadcast_to(own[1:2], (8, cols)), pair_place(cols))
    bias[0:1, 0:cols] = own[0:1]
    bias[0:1, cols:] = spread[0:1]


def attend_trig(omega_ref, centre_ref, trig_ref):
    angle_x = omega_ref[...] * centre_ref[0:1, :]
    angle_y = omega_ref[...] * centre_ref[1:2, :]
    trig_ref[0:FREQS, :] = jnp.cos(angle_x)
    trig_ref[FREQS : 2 * FREQS, :] = jnp.sin(angle_x)
    trig_ref[2 * FREQS : 3 * FREQS, :] = jnp.cos(angle_y)
    trig_ref[3 * FREQS :, :] = jnp.sin(angle_y)


def attend_kernel(heads, plan, *refs):
    cols = heads * HD
    m = lax.axis_index("mp")
    refs = list(refs)

    def take(count):
        head, refs[:] = refs[:count], refs[count:]
        return head

    x_ref, centre_ref, omega_ref = take(3)
    if plan is None:
        w_ref, box_ref, vec_ref = take(3)
    else:
        shard_a, shard_box, shard_vec, pick_ref, shard_e, shard_f = take(6)
    qa_ref, qtok_ref, kvtok_ref, kt_ref, kft_ref, trig_ref, ctxt_ref, log_ref, ctxx_ref = take(9)
    if plan is not None:
        w_out, box_out, vec_ref, full_e, full_f = take(5)
    kftok_ref, box_heads, bias, ctx_ref, vt_ref = take(5)
    pages = x_ref.shape[0] // PAGE
    halves_of_page = 2
    piece = PAGE // halves_of_page
    own_pieces = pages

    if plan is None:
        attend_setup(heads, m, box_ref, vec_ref, centre_ref, omega_ref, trig_ref, box_heads, bias)
        attend_trig(omega_ref, centre_ref, trig_ref)

        def weights(chunk):
            return w_ref[chunk]

        def background(number):
            pass
    else:
        w_ref, box_gather, vec_gather, ctx_sem, a_sem, b_sem, v_sem, e_sem, f_sem, loc_sem = take(10)
        place = Place()
        at = (place.z, place.y, place.c)
        locals_ = [
            pltpu.make_async_copy(shard_e, full_e.at[(ALL, place.m, *at)], loc_sem.at[0]),
            pltpu.make_async_copy(shard_f, full_f.at[(ALL, place.m, *at)], loc_sem.at[1]),
        ]
        for copy in locals_:
            copy.start()
        w_ref[(ALL, 0, *at)] = shard_a[...]
        box_gather[(0, 0, *at)] = shard_box[...]
        vec_gather[(0, place.m, *at)] = shard_vec[...]
        for copy in locals_:
            copy.wait()
        place.greet()
        tree_v = Spread(place, vec_gather, 1, "xzyc", v_sem.at[0], v_sem.at[1])
        tree_b = Spread(place, box_gather, 1, "zyc", b_sem.at[0], b_sem.at[1])
        tree_a = Spread(place, w_ref, 3, "zyc", a_sem.at[0], a_sem.at[1])
        tree_e = Spread(place, full_e, 5, "zyxc", e_sem.at[0], e_sem.at[1])
        tree_f = Spread(place, full_f, 4, "xzyc", f_sem.at[0], f_sem.at[1])
        late = 4
        first = tree_a.events
        last = max(tree_e.events, tree_f.events)

        def background(number):
            tree_e.event(number)
            tree_f.event(number)

        def begin(number, carry):
            tree_a.event(number)
            tree_b.event(number)
            tree_v.event(number)
            background(number - late)
            pl.when(number == 1)(lambda: attend_trig(omega_ref, centre_ref, trig_ref))
            return carry

        lax.fori_loop(0, first, begin, 0)
        blocks = vec_gather[...].reshape(-1, 128)
        vec_ref[...] = rows_from_blocks(blocks, pick_ref[...], plan)
        box_out[...] = box_gather[...].reshape(PE, cols).astype(BF16)
        attend_setup(heads, m, box_out, vec_ref, centre_ref, omega_ref, trig_ref, box_heads, bias)
        copy_w = pltpu.make_async_copy(w_ref, w_out, loc_sem.at[0])
        copy_w.start()

        def weights(chunk):
            return w_ref[chunk].reshape(-1, cols)

    def project(page, carry):
        rows = aligned(page, PAGE)
        tokens = x_ref[rows, :]
        query = dot(tokens, weights(0)) + bias[0:1, 0:cols]
        query = query.astype(BF16) * HD ** (-0.5)
        qtok_ref[rows, :] = query
        qa_rows = query.T
        for half in range(2):
            lanes = slice(half * cols, (half + 1) * cols)
            pair = dot(tokens, weights(1 + half)) + bias[0:1, cols + half * cols : 2 * cols + half * cols]
            pair = pair.astype(BF16)
            kvtok_ref[rows, lanes] = pair
            turned = pair.T
            for spot in range(heads // 2):
                head_rows = slice((half * heads // 2 + spot) * HD, (half * heads // 2 + spot + 1) * HD)
                kt_ref[head_rows, rows] = turned[2 * spot * HD : (2 * spot + 1) * HD]
                vt_ref[head_rows, rows] = turned[(2 * spot + 1) * HD : (2 * spot + 2) * HD]
        trig = trig_ref[:, rows]
        kft = trig.astype(BF16)
        kft_ref[:, rows] = kft
        kftok_ref[rows, :] = kft.T
        own, partner = turn_factors(trig)
        for head in range(heads):
            query_head = qa_rows[head * HD : (head + 1) * HD]
            proj = dot(box_heads[head], query_head)
            feat = proj * own + swap_blocks(proj) * partner
            qa_ref[head, 0:PE, rows] = feat.astype(BF16)
            qa_ref[head, PE : PE + HD, rows] = query_head
        if plan is not None:
            background(page + first - late)
        return carry

    lax.fori_loop(0, pages, project, 0)

    def attend(step, carry):
        turn, pair = step // (heads // 2), step % (heads // 2)
        page = turn if plan is None else turn * m + (pages - 1 - turn) * (1 - m)
        rows = aligned(page, PAGE)
        halves = []
        blank = jnp.zeros((HD, PAGE), BF16)
        for side in range(2):
            head = pair * 2 + side
            lanes = aligned(head, 2 * HD)
            left = jnp.concatenate([kftok_ref[rows, :], kvtok_ref[rows, lanes]], axis=1)
            score = dot(left, jnp.concatenate([qa_ref[head, :, rows], blank], axis=0))
            top = jnp.max(score, axis=0, keepdims=True)
            weight = jnp.exp(score - top)
            total = jnp.sum(weight, axis=0, keepdims=True)
            value = vt_ref[aligned(head, HD), rows]
            halves.append(dot(value, weight.astype(BF16)) * (1.0 / total))
            log_ref[head, :, rows] = top + jnp.log(total)
        both = jnp.concatenate(halves, axis=0).astype(BF16)
        lanes = aligned(pair, 2 * HD)
        ctxt_ref[lanes, rows] = both
        ctx_ref[rows, lanes] = both.T
        if plan is not None:
            pl.when((step % 2 == 0))(lambda: background(step // 2 + first - late + pages))
            pl.when(pair == heads // 2 - 1)(lambda: swap(turn))
        return carry

    def swap_copy(index):
        theirs = pages * (1 - m) + index
        return remote(
            ctx_ref.at[aligned(theirs, piece), :],
            ctxx_ref.at[m, aligned(index, piece), :],
            ctx_sem.at[0, index],
            ctx_sem.at[1, index],
            place.peer["x"],
        )

    def swap(turn):
        @pl.when(turn == 0)
        def _():
            swap_copy(2 - 2 * m).start()
            swap_copy(1).start()

        @pl.when(turn == 1)
        def _():
            swap_copy(2 * m).start()

    lax.fori_loop(0, pages * (heads // 2), attend, 0)
    if plan is None:
        ctxx_ref[...] = ctx_ref[...]
        return
    keep = pltpu.make_async_copy(
        ctx_ref.at[aligned(m, pages * piece), :], ctxx_ref.at[m], loc_sem.at[1]
    )
    keep.start()
    done = first - late + pages + (pages * (heads // 2) + 1) // 2

    def rest(number, carry):
        background(number)
        return carry

    lax.fori_loop(done, last, rest, 0)
    for index in range(own_pieces):
        copy = remote(
            ctx_ref.at[aligned(index, piece), :],
            ctxx_ref.at[1 - m, aligned(index, piece), :],
            ctx_sem.at[0, index],
            ctx_sem.at[1, index],
            place.peer["x"],
        )
        copy.wait_recv()
        copy.wait_send()
    keep.wait()
    copy_w.wait()
    for tree in (tree_v, tree_b, tree_a, tree_e, tree_f):
        tree.drain()


def attend_forward(x, centres, omega, weights, plan):
    tokens, width = x.shape
    cols = weights[1].shape[1]
    heads = cols // HD
    shapes = [
        ((heads, PE + HD, tokens), BF16),
        ((tokens, cols), BF16),
        ((tokens, 2 * cols), BF16),
        ((cols, tokens), BF16),
        ((PE, tokens), BF16),
        ((PE, tokens), F32),
        ((cols, tokens), BF16),
        ((heads, 1, tokens), F32),
    ]
    vmem = pl.BlockSpec(memory_space=pltpu.VMEM)
    free = pl.BlockSpec(memory_space=pl.ANY)
    scratch = [
        pltpu.VMEM((tokens, PE), BF16),
        pltpu.VMEM((heads, PE, HD), BF16),
        pltpu.VMEM((8, 3 * cols), F32),
        pltpu.VMEM((tokens, cols), BF16),
        pltpu.VMEM((cols, tokens), BF16),
    ]
    in_specs, out_specs = [vmem] * 6, [vmem] * len(shapes)
    if plan is None:
        shapes.append(((tokens, cols), BF16))
        out_specs.append(vmem)
        extra = {}
    else:
        tail = (4, 2, 2, width // 16, UNIT)
        shapes += [
            ((2, tokens // 2, cols), BF16),
            ((3, 1, *tail), BF16),
            ((PE, cols), BF16),
            ((VROWS, width), F32),
            ((5, 2, *tail), BF16),
            ((4, 2, *tail), BF16),
        ]
        out_specs += [free, free, vmem, vmem, free, free]
        in_specs = [vmem] * 7 + [free] * 2
        scratch += [
            pltpu.VMEM((3, 1, *tail), BF16),
            pltpu.VMEM((1, 1, 4, 2, 2, PE // 16, cols), F32),
            pltpu.VMEM((1, 2, 4, 2, 2, VROWS, 128), F32),
            pltpu.SemaphoreType.DMA((2, 3)),
            pltpu.SemaphoreType.DMA((2, 3, 9)),
            pltpu.SemaphoreType.DMA((2, 1, 9)),
            pltpu.SemaphoreType.DMA((2, 1, 9)),
            pltpu.SemaphoreType.DMA((2, 5, 9)),
            pltpu.SemaphoreType.DMA((2, 4, 9)),
            pltpu.SemaphoreType.DMA((2,)),
        ]
        extra = dict(collective_id=0, has_side_effects=True)
    return pl.pallas_call(
        functools.partial(attend_kernel, heads, plan),
        out_shape=[jax.ShapeDtypeStruct(s, d) for s, d in shapes],
        in_specs=in_specs,
        out_specs=out_specs,
        scratch_shapes=scratch,
        compiler_params=pltpu.CompilerParams(vmem_limit_bytes=VMEM_LIMIT, **extra),
        name="attend_forward",
    )(x, centres, omega, *weights)


TILE = 256


def norm_stats(value):
    mean = jnp.mean(value, axis=-1, keepdims=True)
    centred = value - mean
    var = jnp.mean(centred * centred, axis=-1, keepdims=True)
    return centred, lax.rsqrt(var + NORM_EPS)


def norm_back(grad_normed, normed, scale):
    first = jnp.mean(grad_normed, axis=-1, keepdims=True)
    second = jnp.mean(grad_normed * normed, axis=-1, keepdims=True)
    return scale * (grad_normed - first - normed * second)


def col_sum(value):
    return jnp.sum(value, axis=0, keepdims=True)


def feed_kernel(plan, *refs):
    x_ref, og_ref, ctx_ref, we_ref, ws_ref, vec_ref, *refs = refs
    out_full, dctx_full, dh1l, grad_ref, vsum_ref, *refs = refs
    norm1, scale1, sum2, dnorm, al, act, slope, dh2l, turned, *refs = refs
    out_ref, dctx_ref = out_full, dctx_full
    m = lax.axis_index("mp")
    if plan is not None:
        out_ref, dctx_ref, swap_sem = refs
        peer = (lax.axis_index("dp"), 1 - m)
        barrier = pltpu.get_barrier_semaphore()
        pl.semaphore_signal(barrier, inc=1, device_id=peer, device_id_type=MESH)
        pl.semaphore_wait(barrier, 1)
    tokens = x_ref.shape[0]
    sides = we_ref.shape[1]
    per_side = (we_ref.shape[0] - 1) // 2
    steps = sides * per_side
    tiles = tokens // TILE
    wide = 2 * UNIT

    def two(ref, first, side):
        return jnp.concatenate([ref[first, side], ref[first + 1, side]], axis=1)

    def w_expand(step):
        return two(we_ref, 1 + 2 * (step % per_side), step // per_side)

    def w_shrink(step):
        return two(ws_ref, 2 * (step % per_side), step // per_side)

    def put_two(first, side, value):
        grad_ref[first, side] = value[:, 0:UNIT]
        grad_ref[first + 1, side] = value[:, UNIT:]

    def out_copies(tile):
        rows = aligned(tile, TILE)
        there = out_full.at[pl.ds(pl.multiple_of(m * tokens + tile * TILE, TILE), TILE), :]
        return (
            pltpu.make_async_copy(out_ref.at[rows, :], there, swap_sem.at[0, tile]),
            remote(out_ref.at[rows, :], there, swap_sem.at[1, tile], swap_sem.at[2, tile], peer),
        )

    def dctx_copies(tile):
        rows = aligned(tile, TILE)
        there = dctx_full.at[pl.ds(pl.multiple_of(m * tokens + tile * TILE, TILE), TILE), :]
        return (
            pltpu.make_async_copy(dctx_ref.at[m, rows, :], there, swap_sem.at[3, tile]),
            remote(
                dctx_ref.at[1 - m, rows, :], there, swap_sem.at[4, tile], swap_sem.at[5, tile], peer
            ),
        )

    def enter(tile, carry):
        rows = aligned(tile, TILE)
        total = x_ref[rows, :].astype(F32) + vec_ref[4:5, :]
        for side in range(sides):
            total += dot(ctx_ref[side, rows, :], we_ref[0, side], NT)
        centred, scale = norm_stats(total)
        normed = centred * scale
        norm1[rows, :] = normed
        scale1[rows, :] = scale
        shifted = normed * vec_ref[0:1, :] + vec_ref[1:2, :]
        al[rows, :] = shifted.astype(BF16)
        sum2[rows, :] = shifted + vec_ref[5:6, :]
        return carry

    lax.fori_loop(0, tiles, enter, 0)

    def grow(step, carry):
        whole = aligned(step, wide)

        def one(tile, inner):
            rows = aligned(tile, TILE)
            pre = dot(al[rows, :], w_expand(step)) + vec_ref[pl.ds(8 + step, 1), :]
            phi = 0.5 + 0.5 * lax.erf(pre * 2.0 ** (-0.5))
            density = jnp.exp(pre * pre * -0.5) * (0.5 / jnp.pi) ** 0.5
            low = (pre * phi).astype(BF16)
            act[rows, whole] = low
            slope[rows, whole] = (phi + pre * density).astype(BF16)
            sum2[rows, :] += dot(low, w_shrink(step), NT)
            return inner

        lax.fori_loop(0, tiles, one, 0)
        return carry

    lax.fori_loop(0, steps, grow, 0)

    vsum_ref[...] = jnp.zeros_like(vsum_ref)

    def turn(tile, carry):
        rows = aligned(tile, TILE)
        centred, scale = norm_stats(sum2[rows, :])
        normed = centred * scale
        out_ref[rows, :] = (normed * vec_ref[2:3, :] + vec_ref[3:4, :]).astype(BF16)
        grad = og_ref[rows, :].astype(F32)
        vsum_ref[2:3, :] += col_sum(grad * normed)
        vsum_ref[3:4, :] += col_sum(grad)
        back = norm_back(grad * vec_ref[2:3, :], normed, scale)
        vsum_ref[5:6, :] += col_sum(back)
        dh2l[rows, :] = back.astype(BF16)
        dnorm[rows, :] = back
        if plan is not None:
            for copy in out_copies(tile):
                copy.start()
        return carry

    lax.fori_loop(0, tiles, turn, 0)

    def shrink(step, carry):
        whole = aligned(step, wide)

        def one(tile, inner):
            rows = aligned(tile, TILE)
            grad = dot(dh2l[rows, :], w_shrink(step))
            low = (grad * slope[rows, whole].astype(F32)).astype(BF16)
            slope[rows, whole] = low
            vsum_ref[pl.ds(8 + step, 1), :] += col_sum(low.astype(F32))
            dnorm[rows, :] += dot(low, w_expand(step), NT)
            return inner

        lax.fori_loop(0, tiles, one, 0)
        return carry

    lax.fori_loop(0, steps, shrink, 0)

    def leave(tile, carry):
        rows = aligned(tile, TILE)
        grad = dnorm[rows, :]
        normed = norm1[rows, :]
        vsum_ref[0:1, :] += col_sum(grad * normed)
        vsum_ref[1:2, :] += col_sum(grad)
        back = norm_back(grad * vec_ref[0:1, :], normed, scale1[rows, :])
        vsum_ref[4:5, :] += col_sum(back)
        low = back.astype(BF16)
        dh1l[rows, :] = low
        for side in range(sides):
            dctx_ref[side, rows, :] = dot(low, we_ref[0, side]).astype(BF16)
        if plan is not None:
            for copy in dctx_copies(tile):
                copy.start()
        return carry

    lax.fori_loop(0, tiles, leave, 0)

    turned[...] = dh2l[...].T

    def grad_shrink(step, carry):
        grad = dot(turned[...], act[:, aligned(step, wide)]).astype(BF16)
        put_two(1 + 2 * per_side + 2 * (step % per_side), step // per_side, grad)
        return carry

    lax.fori_loop(0, steps, grad_shrink, 0)
    turned[...] = al[...].T

    def grad_expand(step, carry):
        grad = dot(turned[...], slope[:, aligned(step, wide)]).astype(BF16)
        put_two(1 + 2 * (step % per_side), step // per_side, grad)
        return carry

    lax.fori_loop(0, steps, grad_expand, 0)
    turned[...] = dh1l[...].T
    for side in range(sides):
        grad_ref[0, side] = dot(turned[...], ctx_ref[side]).astype(BF16)
    if plan is not None:
        for tile in range(tiles):
            for copies in (out_copies(tile), dctx_copies(tile)):
                for copy in copies:
                    copy.wait()


def feed_both(x, og, ctx, w_expand, w_shrink, vecs, plan):
    tokens, width = x.shape
    chunks, sides = w_shrink.shape[0:2]
    hidden = chunks * UNIT
    out_shape = (tokens, width)
    dctx_shape = (sides, tokens, UNIT)
    shapes = [
        (out_shape, BF16),
        (dctx_shape, BF16),
        ((tokens, width), BF16),
        ((2 * chunks + 1, sides, width, UNIT), BF16),
        ((VROWS, width), F32),
    ]
    scratch = [
        pltpu.VMEM((tokens, width), F32),
        pltpu.VMEM((tokens, 1), F32),
        pltpu.VMEM((tokens, width), F32),
        pltpu.VMEM((tokens, width), F32),
        pltpu.VMEM((tokens, width), BF16),
        pltpu.VMEM((tokens, sides * hidden), BF16),
        pltpu.VMEM((tokens, sides * hidden), BF16),
        pltpu.VMEM((tokens, width), BF16),
        pltpu.VMEM((width, tokens), BF16),
    ]
    vmem = pl.BlockSpec(memory_space=pltpu.VMEM)
    out_specs = [vmem] * len(shapes)
    extra = {}
    if plan is not None:
        shapes[0] = ((sides * tokens, width), BF16)
        shapes[1] = ((sides * tokens, UNIT), BF16)
        out_specs[0:2] = [pl.BlockSpec(memory_space=pl.ANY)] * 2
        scratch += [
            pltpu.VMEM(out_shape, BF16),
            pltpu.VMEM(dctx_shape, BF16),
            pltpu.SemaphoreType.DMA((6, tokens // TILE)),
        ]
        extra = dict(collective_id=1, has_side_effects=True)
    return pl.pallas_call(
        functools.partial(feed_kernel, plan),
        out_shape=[jax.ShapeDtypeStruct(s, d) for s, d in shapes],
        in_specs=[vmem] * 6,
        out_specs=out_specs,
        scratch_shapes=scratch,
        compiler_params=pltpu.CompilerParams(vmem_limit_bytes=VMEM_LIMIT, **extra),
        name="feed_both",
    )(x, og, ctx, w_expand, w_shrink, vecs)


def pair_place(cols):
    spot = lax.broadcasted_iota(jnp.int32, (cols, 2 * cols), 0)
    lane = lax.broadcasted_iota(jnp.int32, (cols, 2 * cols), 1)
    target = ((spot >> 6) << 7) + HD + (spot & (HD - 1))
    return jnp.where(lane == target, 1.0, 0.0)


def exact_dot(lhs, rhs, dims=NN):
    return lax.dot_general(
        lhs, rhs, dims, precision=lax.Precision.HIGHEST, preferred_element_type=F32
    )


def attend_back_kernel(heads, plan, inv_tokens, *refs):
    x_ref, w_ref, box_ref, *refs = refs
    qa_ref, qtok_ref, kvtok_ref, kt_ref, kft_ref, trig_ref, ctxt_ref, log_ref, dctx_ref, *refs = refs
    cols = heads * HD
    tokens = x_ref.shape[0]
    pages = tokens // PAGE
    m = lax.axis_index("mp")
    piece = PAGE // 2
    pieces = 2 * pages
    lane = lax.broadcasted_iota(jnp.int32, (1, 2 * HD), 1)
    lower = lane < HD
    if plan is None:
        inp_ref, gw_ref, gbox_ref, qvsum_ref, *refs = refs
        kftok, dctxt, boxt, dtok, xt, gbox = refs
        before, after = 0, 0

        def background(number):
            pass
    else:
        dh1_ref, vsum_ref, pick_ref, feed_hbm, *refs = refs
        inp_ref, sum_e, sum_f, sum_a, sum_b, sum_v, norm_ref, *refs = refs
        kftok, dctxt, boxt, dtok, xt, gbox, *refs = refs
        came, total_e, total_f, full_a, total_a, full_b, total_b, full_v, total_v, norms, *refs = refs
        (ec, ey, ez, ex, fc, fx, fz, fy, ac, ay, az, bc, by, bz, vc, vy, vz, vx, *refs) = refs
        e_sem, f_sem, a_sem, b_sem, v_sem, n_sem, i_sem, loc_sem = refs
        place = Place()
        full_e = feed_hbm.at[0:5]
        full_f = feed_hbm.at[5:9]
        fills = [
            pltpu.make_async_copy(full_e.at[:, :, :, :, place.c], total_e, loc_sem.at[0]),
            pltpu.make_async_copy(full_f.at[:, :, :, :, place.c], total_f, loc_sem.at[1]),
        ]
        for copy in fills:
            copy.start()
        place.greet()

        def finish(out):
            def put(chunk, value):
                out[chunk] = value.astype(F32) * inv_tokens

            return put

        tree_e = Reduce(
            place,
            full_e,
            total_e,
            dict(c=ec, y=ey, z=ez, x=ex),
            5,
            "cyzx",
            e_sem.at[0],
            e_sem.at[1],
            finish(sum_e),
        )
        tree_f = Reduce(
            place,
            full_f,
            total_f,
            dict(c=fc, x=fx, z=fz, y=fy),
            4,
            "cxzy",
            f_sem.at[0],
            f_sem.at[1],
            finish(sum_f),
        )
        tree_a = Reduce(
            place,
            full_a,
            total_a,
            dict(c=ac, y=ay, z=az),
            3,
            "cyz",
            a_sem.at[0],
            a_sem.at[1],
            finish(sum_a),
        )
        tree_b = Reduce(
            place, full_b, total_b, dict(c=bc, y=by, z=bz), 1, "cyz", b_sem.at[0], b_sem.at[1], finish(sum_b)
        )
        tree_v = Reduce(
            place,
            full_v,
            total_v,
            dict(c=vc, y=vy, z=vz, x=vx),
            1,
            "cyzx",
            v_sem.at[0],
            v_sem.at[1],
            finish(sum_v),
        )
        tree_n = Spread(place, norms, 1, "cyxz", n_sem.at[0], n_sem.at[1])

        def background(number):
            tree_e.event(number)
            tree_f.event(number)

        background(0)
        for copy in fills:
            copy.wait()

    boxt[...] = box_ref[...].T
    gbox[...] = jnp.zeros_like(gbox)

    def prepare(page, carry):
        rows = aligned(page, PAGE)
        kftok[rows, :] = kft_ref[:, rows].T
        dctxt[:, rows] = dctx_ref[rows, :].T
        xt[:, rows] = x_ref[rows, :].T
        background(page + 1)
        return carry

    lax.fori_loop(0, pages, prepare, 0)

    def attend(step, carry):
        page, pair = step // (heads // 2), step % (heads // 2)
        rows = aligned(page, PAGE)
        own, partner = turn_factors(trig_ref[:, rows])
        pair_lanes = aligned(pair, 2 * HD)
        query_pair = qtok_ref[rows, pair_lanes]
        dctx_pair = dctx_ref[rows, pair_lanes]
        halves = []
        boxes = []
        blank = jnp.zeros((HD, PAGE), BF16)
        for side in range(2):
            head = pair * 2 + side
            lanes = aligned(head, 2 * HD)
            key_value = kvtok_ref[rows, lanes]
            left = jnp.concatenate([kftok[rows, :], key_value], axis=1)
            score = dot(left, jnp.concatenate([qa_ref[head, :, rows], blank], axis=0))
            prob = jnp.exp(score - log_ref[head, :, rows])
            prob_low = prob.astype(BF16)
            head_rows = pl.ds(pl.multiple_of(head * HD, HD), HD)
            dctx_head = dctxt[head_rows, rows]
            grad_prob = dot(
                key_value, jnp.concatenate([blank, dctx_head], axis=0)
            )
            inner = col_sum(dctx_head.astype(F32) * ctxt_ref[head_rows, rows].astype(F32))
            grad_score = (prob * (grad_prob - inner)).astype(BF16)
            if side == 0:
                both = jnp.concatenate([query_pair[:, 0:HD], dctx_pair[:, 0:HD]], axis=1)
            else:
                both = jnp.concatenate([query_pair[:, HD:], dctx_pair[:, HD:]], axis=1)
            from_score = dot(grad_score, both)
            from_prob = dot(prob_low, both)
            grad_kv = jnp.where(lower, from_score, from_prob).astype(BF16)
            dtok[rows, pl.ds(pl.multiple_of(cols + head * 2 * HD, 2 * HD), 2 * HD)] = grad_kv
            keys = jnp.concatenate([kft_ref[:, rows], kt_ref[head_rows, rows]], axis=0)
            grad_query = dot(keys, grad_score) * HD ** (-0.5)
            feat = grad_query[0:PE]
            proj = (feat * own - swap_blocks(feat) * partner).astype(BF16)
            halves.append(grad_query[PE:] + dot(boxt[head_rows, :], proj))
            boxes.append(dot(proj, query_pair))
        gbox[:, pair_lanes] += jnp.where(lower, boxes[0], boxes[1])
        dtok[rows, pair_lanes] = jnp.concatenate(halves, axis=0).astype(BF16).T
        return carry

    def spread(page):
        rows = aligned(page, PAGE)
        return sum(
            dot(dtok[rows, chunk * UNIT : (chunk + 1) * UNIT], w_ref[chunk], NT) for chunk in range(3)
        )

    if plan is None:
        lax.fori_loop(0, pages * (heads // 2), attend, 0)
        gbox_ref[...] = gbox[...] * HD**0.5

        def spread_page(page, carry):
            inp_ref[aligned(page, PAGE), :] = spread(page)
            return carry

        lax.fori_loop(0, pages, spread_page, 0)

        def gather(step, carry):
            lanes = aligned(step, UNIT)
            gw_ref[step] = dot(xt[...], dtok[:, lanes]).astype(BF16)
            qvsum_ref[0:1, lanes] = col_sum(dtok[:, lanes].astype(F32))
            return carry

        lax.fori_loop(0, 3, gather, 0)
        return

    def swap(index):
        rows = aligned(index, piece)
        return remote(
            inp_ref.at[rows, :], came.at[rows, :], i_sem.at[0, index], i_sem.at[1, index], place.peer["x"]
        )

    def attend_and_send(step, carry):
        attend(step, carry)
        page = step // (heads // 2)

        @pl.when(step % (heads // 2) == heads // 2 - 1)
        def _():
            value = spread(page)
            for half in range(2):
                index = 2 * page + half
                rows = aligned(index, piece)
                own = index // pages == m
                spot = aligned(index % pages, piece)
                extra = jnp.where(own, dh1_ref[spot, :].astype(F32), 0.0)
                inp_ref[rows, :] = (value[half * piece : (half + 1) * piece] + extra).astype(BF16)
                swap(index).start()

        background(step + 1 + pages)
        return carry

    lax.fori_loop(0, pages * (heads // 2), attend_and_send, 0)
    begun = pages * (heads // 2) + 1 + pages

    full_b[0, 0] = (gbox[...] * HD**0.5).reshape(4, 2, 2, PE // 16, cols)
    total_b[0, 0] = full_b[0, 0, :, :, place.c]

    def gather(step, carry):
        grad = dot(xt[...], dtok[:, aligned(step, UNIT)]).astype(BF16)
        full_a[step, 0] = grad.reshape(full_a.shape[2:])
        total_a[step, 0] = full_a[step, 0, :, :, place.c]
        tree_a.event(step)
        tree_b.event(step)
        background(begun + step)
        return carry

    lax.fori_loop(0, 3, gather, 0)

    sums = jnp.concatenate(
        [
            col_sum(dtok[:, chunk * UNIT : (chunk + 1) * UNIT].astype(F32)) for chunk in range(3)
        ],
        axis=1,
    )
    values = exact_dot(jnp.broadcast_to(sums[:, cols:], (8, 2 * cols)), pair_place(cols), NT)
    pair = jnp.concatenate([sums[:, 0:cols], values[0:1]], axis=0)
    blank = jnp.zeros_like(pair)
    pair = jnp.where(
        m == 0, jnp.concatenate([pair, blank], axis=1), jnp.concatenate([blank, pair], axis=1)
    )
    table = jnp.concatenate([vsum_ref[0:6, :], pair, vsum_ref[8:, :]], axis=0)
    mp_count, dp_count = plan
    width = table.shape[1]
    each = width // (mp_count * dp_count)
    wide_lane = lax.broadcasted_iota(jnp.int32, (VROWS, width), 1)
    for side in range(mp_count):
        parts = []
        for r in range(dp_count):
            first = (r * mp_count + side) * each
            parts.append(jnp.where((wide_lane >= first) & (wide_lane < first + each), table, 0.0))
        block = exact_dot(jnp.concatenate(parts, axis=0), pick_ref[...], NT)
        full_v[0, side] = block.reshape(full_v.shape[2:])
    total_v[0] = full_v[0, :, :, :, place.c]

    def tail(number, carry):
        tree_a.event(number)
        tree_b.event(number)
        tree_v.event(number - 3)
        background(begun + number)
        return carry

    last = max(
        tree_a.events, tree_b.events, tree_v.events + 3, tree_e.events - begun, tree_f.events - begun
    )
    lax.fori_loop(3, last, tail, 0)

    square = sum(jnp.sum(out[...] * out[...]) for out in (sum_e, sum_f, sum_a, sum_b, sum_v))
    norms[0, place.m, place.z, place.y, place.c] = jnp.full((8, 128), square, F32)

    def final(number, carry):
        tree_n.event(number)

        @pl.when(number < pieces)
        def _():
            rows = aligned(number, piece)
            swap(number).wait()
            inp_ref[rows, :] = (inp_ref[rows, :].astype(F32) + came[rows, :].astype(F32)).astype(BF16)

        return carry

    lax.fori_loop(0, max(tree_n.events, pieces), final, 0)
    every = norms[...].reshape(-1, 8, 128)
    norm_ref[...] = jnp.sqrt(sum(every[k] for k in range(every.shape[0])))

    for tree in (tree_e, tree_f, tree_a, tree_b, tree_v, tree_n):
        tree.drain()


def attend_backward(x, weight, box, kept, dctx, plan, inv_tokens, more=()):
    tokens, width = x.shape
    cols = weight.shape[2]
    heads = cols // HD
    vmem = pl.BlockSpec(memory_space=pltpu.VMEM)
    scratch = [
        pltpu.VMEM((tokens, PE), BF16),
        pltpu.VMEM((cols, tokens), BF16),
        pltpu.VMEM((cols, PE), BF16),
        pltpu.VMEM((tokens, 3 * cols), BF16),
        pltpu.VMEM((width, tokens), BF16),
        pltpu.VMEM((PE, cols), F32),
    ]
    in_specs = [vmem] * 12
    if plan is None:
        shapes = [
            ((tokens, width), F32),
            ((3, width, cols), BF16),
            ((PE, cols), F32),
            ((8, 3 * cols), F32),
        ]
        extra = {}
    else:
        in_specs += [vmem] * 3 + [pl.BlockSpec(memory_space=pl.ANY)]
        rows = width // 16
        unit = (rows, UNIT)
        tile = (PE // 16, cols)
        small = (VROWS, 128)
        shapes = [
            ((tokens, width), BF16),
            ((5, *unit), F32),
            ((4, *unit), F32),
            ((3, *unit), F32),
            ((1, *tile), F32),
            ((1, *small), F32),
            ((8, 128), F32),
        ]
        scratch += [
            pltpu.VMEM((tokens, width), BF16),
            pltpu.VMEM((5, 2, 4, 2, *unit), BF16),
            pltpu.VMEM((4, 2, 4, 2, *unit), BF16),
            pltpu.VMEM((3, 1, 4, 2, 2, *unit), BF16),
            pltpu.VMEM((3, 1, 4, 2, *unit), BF16),
            pltpu.VMEM((1, 1, 4, 2, 2, *tile), F32),
            pltpu.VMEM((1, 1, 4, 2, *tile), F32),
            pltpu.VMEM((1, 2, 4, 2, 2, *small), F32),
            pltpu.VMEM((1, 2, 4, 2, *small), F32),
            pltpu.VMEM((1, 2, 4, 2, 2, 8, 128), F32),
            pltpu.VMEM((5, 2, 4, 2, *unit), BF16),
            pltpu.VMEM((5, 2, 4, *unit), BF16),
            pltpu.VMEM((5, 2, 3, 2, *unit), BF16),
            pltpu.VMEM((5, *unit), BF16),
            pltpu.VMEM((4, 2, 4, 2, *unit), BF16),
            pltpu.VMEM((4, 4, 2, *unit), BF16),
            pltpu.VMEM((4, 2, 3, 2, *unit), BF16),
            pltpu.VMEM((4, *unit), BF16),
            pltpu.VMEM((3, 4, 2, *unit), BF16),
            pltpu.VMEM((3, 4, *unit), BF16),
            pltpu.VMEM((3, 2, 3, *unit), BF16),
            pltpu.VMEM((1, 4, 2, *tile), F32),
            pltpu.VMEM((1, 4, *tile), F32),
            pltpu.VMEM((1, 2, 3, *tile), F32),
            pltpu.VMEM((1, 2, 4, 2, *small), F32),
            pltpu.VMEM((1, 2, 4, *small), F32),
            pltpu.VMEM((1, 2, 3, 2, *small), F32),
            pltpu.VMEM((1, *small), F32),
            pltpu.SemaphoreType.DMA((2, 5, 9)),
            pltpu.SemaphoreType.DMA((2, 4, 9)),
            pltpu.SemaphoreType.DMA((2, 3, 9)),
            pltpu.SemaphoreType.DMA((2, 1, 9)),
            pltpu.SemaphoreType.DMA((2, 1, 9)),
            pltpu.SemaphoreType.DMA((2, 1, 9)),
            pltpu.SemaphoreType.DMA((2, 2 * (tokens // PAGE))),
            pltpu.SemaphoreType.DMA((2,)),
        ]
        extra = dict(collective_id=2, has_side_effects=True)
    return pl.pallas_call(
        functools.partial(attend_back_kernel, heads, plan, inv_tokens),
        out_shape=[jax.ShapeDtypeStruct(s, d) for s, d in shapes],
        in_specs=in_specs,
        out_specs=[vmem] * len(shapes),
        scratch_shapes=scratch,
        compiler_params=pltpu.CompilerParams(vmem_limit_bytes=VMEM_LIMIT, **extra),
        name="attend_backward",
    )(x, weight, box, *kept, dctx, *more)


def adam_step(master, first, second, gradient, rate, decay):
    new_first = BETA_ONE * first + (1.0 - BETA_ONE) * gradient
    new_second = BETA_TWO * second + (1.0 - BETA_TWO) * gradient * gradient
    first_hat = new_first / (1.0 - BETA_ONE**STEP)
    second_hat = new_second / (1.0 - BETA_TWO**STEP)
    new_master = master - rate * (first_hat / (jnp.sqrt(second_hat) + ADAM_EPS) + decay * master)
    return (new_first, new_second, new_master)


def pack_qkv(shard):
    rows, cols = shard.shape[1:]
    heads = cols // HD
    pairs = jnp.stack([shard[1].reshape(rows, heads, HD), shard[2].reshape(rows, heads, HD)], axis=2)
    pairs = pairs.reshape(rows, 2, cols)
    return jnp.stack([shard[0], pairs[:, 0], pairs[:, 1]])


def unpack_qkv(packed):
    rows, cols = packed.shape[1:]
    pairs = jnp.concatenate([packed[1], packed[2]], axis=1).reshape(rows, cols // HD, 2, HD)
    return jnp.stack(
        [packed[0], pairs[:, :, 0].reshape(rows, cols), pairs[:, :, 1].reshape(rows, cols)]
    )


def to_chunks(shard):
    rows = shard.shape[0]
    return shard.reshape(rows, -1, UNIT).transpose(1, 0, 2)


def from_chunks(chunks):
    return chunks.transpose(1, 0, 2).reshape(chunks.shape[1], -1)


def on_device(
    layer_input,
    page_boxes,
    output_grad,
    attn_proj,
    attn_first,
    attn_second,
    box_proj,
    box_first,
    box_second,
    merge_proj,
    merge_first,
    merge_second,
    expand_proj,
    expand_first,
    expand_second,
    shrink_proj,
    shrink_first,
    shrink_second,
    vectors,
    vector_first,
    vector_second,
):
    mp_count = lax.axis_size("mp")
    dp_count = lax.axis_size("dp")
    mp_index = lax.axis_index("mp")
    tokens, width = layer_input.shape
    cols = attn_proj.shape[2]
    heads = cols // HD
    own_tokens = tokens // mp_count
    inv_tokens = 1.0 / (tokens * dp_count)

    coords = page_boxes.astype(F32)
    centres = jnp.stack([coords[:, 0] + coords[:, 2], coords[:, 1] + coords[:, 3]]) * 0.5
    omega = (10000.0 ** (-jnp.arange(FREQS, dtype=F32) / FREQS))[:, None]
    shard_qkv = pack_qkv(attn_proj).astype(BF16)
    shard_e = jnp.concatenate([merge_proj.T[None], to_chunks(expand_proj)]).astype(BF16)
    shard_f = to_chunks(shrink_proj.T).astype(BF16)
    plan = (mp_count, dp_count) if dp_count == 16 and mp_count == 2 else None
    if plan is not None:
        each = vectors.shape[1]
        shard_vec = jnp.pad(vectors, ((0, VROWS - vectors.shape[0]), (0, 128 - each)))
        pick = np.zeros((128, width), np.float32)
        pick[np.arange(width) % each, np.arange(width)] = 1.0
        kept = attend_forward(
            layer_input,
            centres,
            omega,
            (shard_qkv, box_proj, shard_vec, jnp.asarray(pick), shard_e, shard_f),
            plan,
        )
        *kept, log_total, context, w_qkv, w_box, vecs, w_expand, w_shrink = kept
        w_qkv = w_qkv.reshape(3, width, cols)
        w_expand = w_expand.reshape(-1, mp_count, width, UNIT)
        w_shrink = w_shrink.reshape(-1, mp_count, width, UNIT)
    else:
        w_qkv = lax.all_gather(shard_qkv, "dp", axis=1, tiled=True)
        w_box = lax.all_gather(box_proj.astype(BF16), "dp", axis=0, tiled=True)
        w_expand = lax.all_gather(lax.all_gather(shard_e, "dp", axis=1, tiled=True), "mp", axis=1)
        w_shrink = lax.all_gather(lax.all_gather(shard_f, "dp", axis=1, tiled=True), "mp", axis=1)
        vecs = lax.all_gather(vectors, ("dp", "mp"), axis=1, tiled=True)
        vecs = jnp.pad(vecs, ((0, VROWS - vecs.shape[0]), (0, 0)))
        kept = attend_forward(layer_input, centres, omega, (w_qkv, w_box, vecs), None)
        *kept, log_total, context = kept
        context = lax.all_to_all(
            context.reshape(mp_count, own_tokens, cols), "mp", split_axis=0, concat_axis=0
        )

    def own_rows(array):
        return lax.dynamic_slice_in_dim(array, mp_index * own_tokens, own_tokens)

    layer_out, dctx, dh1, g_feed, vec_sum = feed_both(
        own_rows(layer_input), own_rows(output_grad), context, w_expand, w_shrink, vecs, plan
    )
    if plan is not None:
        input_grad, sum_expand, sum_shrink, sum_attn, sum_box, sum_vec, norm = attend_backward(
            layer_input,
            w_qkv,
            w_box,
            (*kept, log_total),
            dctx,
            plan,
            inv_tokens,
            (
                dh1,
                vec_sum,
                jnp.asarray(pick),
                g_feed.reshape(g_feed.shape[0], 2, 4, 2, 2, width // 16, UNIT),
            ),
        )
        shard_attn = unpack_qkv(sum_attn)
        shard_box = sum_box[0]
        vector_shard = sum_vec[0, 0 : vectors.shape[0], 0:each]
        grad_norm = norm[0, 0]
    else:
        layer_out = lax.all_gather(layer_out, "mp", axis=0, tiled=True)
        dctx = lax.all_to_all(dctx, "mp", split_axis=0, concat_axis=0).reshape(tokens, cols)
        part, g_qkv, g_box, qkv_sum = attend_backward(
            layer_input, w_qkv, w_box, (*kept, log_total), dctx, None, inv_tokens
        )
        own_part = lax.psum_scatter(part.astype(BF16), "mp", scatter_dimension=0, tiled=True)
        own_grad = (own_part.astype(F32) + dh1).astype(BF16)
        input_grad = lax.all_gather(own_grad, "mp", axis=0, tiled=True)
        shard_attn = unpack_qkv(
            lax.psum_scatter(g_qkv, "dp", scatter_dimension=1, tiled=True).astype(F32) * inv_tokens
        )
        shard_box = lax.psum_scatter(g_box, "dp", scatter_dimension=0, tiled=True) * inv_tokens
        sum_feed = lax.psum_scatter(g_feed, "dp", scatter_dimension=2, tiled=True)
        sum_feed = lax.psum_scatter(sum_feed, "mp", scatter_dimension=1, tiled=True)[:, 0]
        sum_feed = sum_feed.astype(F32) * inv_tokens
        sum_expand, sum_shrink = sum_feed[0:5], sum_feed[5:]

        def placed(row):
            return lax.dynamic_update_slice_in_dim(
                jnp.zeros((width,), F32), row, mp_index * cols, 0
            )[None, :]

        value_sum = qkv_sum[0, cols:].reshape(heads, 2, HD)[:, 1].reshape(cols)
        vector_grad = jnp.concatenate(
            [vec_sum[0:6], placed(qkv_sum[0, 0:cols]), placed(value_sum), vec_sum[8:12]]
        )
        vector_shard = (
            lax.psum_scatter(vector_grad, ("dp", "mp"), scatter_dimension=1, tiled=True) * inv_tokens
        )
        square = sum(
            jnp.sum(shard * shard)
            for shard in (shard_attn, shard_box, sum_expand, sum_shrink, vector_shard)
        )
        grad_norm = jnp.sqrt(lax.psum(square, ("dp", "mp")))
    shard_merge = sum_expand[0].T
    shard_expand = from_chunks(sum_expand[1:])
    shard_shrink = from_chunks(sum_shrink).T
    clip_scale = CLIP_LIMIT / jnp.maximum(grad_norm, CLIP_LIMIT)
    results = [layer_out, input_grad, grad_norm]
    for master, first, second, shard in (
        (attn_proj, attn_first, attn_second, shard_attn),
        (box_proj, box_first, box_second, shard_box),
        (merge_proj, merge_first, merge_second, shard_merge),
        (expand_proj, expand_first, expand_second, shard_expand),
        (shrink_proj, shrink_first, shrink_second, shard_shrink),
    ):
        new_first, new_second, new_master = adam_step(
            master, first, second, shard * clip_scale, RATE_MATRIX, WEIGHT_DECAY
        )
        results += [new_first, new_second, new_master, new_master.astype(BF16)]
    results += adam_step(
        vectors, vector_first, vector_second, vector_shard * clip_scale, RATE_VECTOR, 0.0
    )
    return tuple(results)


def solution(mesh):
    rows = P("dp", None)
    attn = P(None, "dp", "mp")
    tall = P("dp", "mp")
    wide = P("mp", "dp")
    vector = P(None, ("dp", "mp"))
    in_specs = (rows,) * 3 + (attn,) * 3 + (tall,) * 3 + (wide,) * 3 + (tall,) * 3 + (wide,) * 3
    in_specs += (vector,) * 3
    out_specs = (rows, rows, P()) + (attn,) * 4 + (tall,) * 4 + (wide,) * 4 + (tall,) * 4
    out_specs += (wide,) * 4 + (vector,) * 3
    return jax.shard_map(
        on_device, mesh=mesh, in_specs=in_specs, out_specs=out_specs, check_vma=False
    )
```

```python
import functools

import jax
import jax.numpy as jnp
import numpy as np
from jax import lax
from jax.experimental import pallas as pl
from jax.experimental.pallas import tpu as pltpu
from jax.sharding import PartitionSpec as P

HD = 64
FREQS = 32
PE = 128
PAGE = 512
STEP = 10

NORM_EPS = 1e-12
CLIP_LIMIT = 0.1
BETA_ONE = 0.9
BETA_TWO = 0.999
ADAM_EPS = 1e-08
RATE_MATRIX = 0.05
RATE_VECTOR = 0.5
WEIGHT_DECAY = 0.01

F32 = jnp.float32
BF16 = jnp.bfloat16
VMEM_LIMIT = 60 * 1024 * 1024

NN = (((1,), (0,)), ((), ()))
NT = (((1,), (1,)), ((), ()))
TN = (((0,), (0,)), ((), ()))


def dot(lhs, rhs, dims=NN):
    return lax.dot_general(lhs, rhs, dims, preferred_element_type=F32)


def aligned(index, size):
    return pl.ds(pl.multiple_of(index * size, size), size)


def swap_blocks(feat):
    return jnp.concatenate(
        [
            feat[FREQS : 2 * FREQS],
            feat[0:FREQS],
            feat[3 * FREQS :],
            feat[2 * FREQS : 3 * FREQS],
        ],
        axis=0,
    )


def turn_factors(trig):
    cos_x, sin_x = trig[0:FREQS], trig[FREQS : 2 * FREQS]
    cos_y, sin_y = trig[2 * FREQS : 3 * FREQS], trig[3 * FREQS :]
    return (
        jnp.concatenate([sin_x, sin_x, sin_y, sin_y], axis=0),
        jnp.concatenate([cos_x, -cos_x, cos_y, -cos_y], axis=0),
    )


MESH = pl.DeviceIdType.MESH
ALL = slice(None)
UNIT = 384


class Place:
    def __init__(self):
        rank = lax.axis_index("dp")
        self.m = lax.axis_index("mp")
        self.z = rank // 4
        self.y = (rank // 2) % 2
        self.c = rank % 2
        self.peer = {
            "x": (rank, 1 - self.m),
            "y": (rank + 2 - 4 * self.y, self.m),
            "c": (rank + 1 - 2 * self.c, self.m),
        }
        self.far = [((rank + 4 * step) % 16, self.m) for step in (1, 2, 3)]

    def signal(self):
        barrier = pltpu.get_barrier_semaphore()
        for device in list(self.peer.values()) + self.far:
            pl.semaphore_signal(barrier, inc=1, device_id=device, device_id_type=MESH)

    def wait(self):
        pl.semaphore_wait(pltpu.get_barrier_semaphore(), 6)


def remote(src, dst, send_sem, recv_sem, device):
    return pltpu.make_async_remote_copy(
        src_ref=src,
        dst_ref=dst,
        send_sem=send_sem,
        recv_sem=recv_sem,
        device_id=device,
        device_id_type=MESH,
    )


SLOT = {"c": 0, "z": 1, "y": 4, "x": 5}
SLOTS = 6


class Tree:
    def stage(self, index, chunk):
        raise NotImplementedError

    def event(self, number):
        for index in range(self.count - 1, -1, -1):
            chunk = number - index
            if self.chunks == 1:
                pl.when(chunk == 0)(lambda index=index: self.stage(index, 0))
            else:
                pl.when((chunk >= 0) & (chunk < self.chunks))(
                    lambda index=index, chunk=chunk: self.stage(index, chunk)
                )

    @property
    def events(self):
        return self.chunks + self.count - 1


class Spread(Tree):
    def __init__(self, place, ref, chunks, order, sems):
        self.chunks, self.ref, self.sems = chunks, ref, sems
        have = {"x": place.m if "x" in order else 0, "z": place.z, "y": place.y, "c": place.c}
        mine = {"x": place.m, "y": place.y, "c": place.c}
        self.steps = []
        for axis in order:
            if axis == "z":
                sends = [(have, place.far[step - 1], step) for step in (1, 2, 3)]
                waits = [(dict(have, z=(place.z + 4 - step) % 4), step) for step in (1, 2, 3)]
            else:
                sends = [(have, place.peer[axis], SLOT[axis])]
                waits = [(dict(have, **{axis: 1 - mine[axis]}), SLOT[axis])]
                if axis == "c" and have["z"] == ALL:
                    sends = [(dict(have, z=z), place.peer[axis], SLOT[axis]) for z in range(4)]
            self.steps.append((sends, waits, sends[0][0] if len(sends) < 4 else have))
            have = dict(have, **{axis: ALL})
        self.some = place.peer["c"]
        self.count = len(self.steps) + 1

    def _copy(self, chunk, have, device, slot):
        block = self.ref.at[chunk, have["x"], have["z"], have["y"], have["c"]]
        return remote(block, block, self.sems.at[0, chunk, slot], self.sems.at[1, chunk, slot], device)

    def stage(self, index, chunk):
        if index > 0:
            for have, slot in self.steps[index - 1][1]:
                self._copy(chunk, have, self.some, slot).wait_recv()
        if index < self.count - 1:
            for have, device, slot in self.steps[index][0]:
                self._copy(chunk, have, device, slot).start()

    def drain(self):
        def one(chunk, carry):
            for sends, _, whole in self.steps:
                if len(sends) == 4:
                    self._copy(chunk, whole, self.some, sends[0][2]).wait_send()
                else:
                    for have, device, slot in sends:
                        self._copy(chunk, have, device, slot).wait_send()
            return carry

        lax.fori_loop(0, self.chunks, one, 0)


class Reduce(Tree):
    def __init__(self, place, full, total, lands, chunks, order, sems, finish):
        self.place, self.full, self.total, self.lands = place, full, total, lands
        self.chunks, self.sems, self.finish = chunks, sems, finish
        mine = {"x": place.m, "y": place.y}
        self.across = ALL if "x" in order else 0
        have = {"x": self.across, "z": ALL, "y": ALL}
        self.order, self.haves = order, []
        for axis in order:
            before = have
            if axis != "c":
                have = dict(have, **{axis: place.z if axis == "z" else mine[axis]})
            self.haves.append((before, have))
        self.have = have
        self.count = len(order) + 1

    def _at(self, chunk, have):
        return self.total.at[chunk, have["x"], have["z"], have["y"]]

    def _copies(self, index, chunk, start=False):
        axis, (before, _) = self.order[index], self.haves[index]
        place, land = self.place, self.lands[axis]

        def copy(src, dst, slot, device):
            return remote(src, dst, self.sems.at[0, chunk, slot], self.sems.at[1, chunk, slot], device)

        if axis == "c":
            other = 1 - place.c
            if start and self.across == ALL:
                return [
                    copy(
                        self.full.at[chunk, :, z, :, other], land.at[chunk, :, z], SLOT[axis], place.peer[axis]
                    )
                    for z in range(4)
                ]
            source = self.full.at[chunk, self.across, :, :, other]
            return [copy(source, land.at[chunk], SLOT[axis], place.peer[axis])]
        if axis == "z":
            return [
                copy(
                    self._at(chunk, dict(before, z=(place.z + step) % 4)),
                    land.at[chunk, step - 1],
                    step,
                    place.far[step - 1],
                )
                for step in (1, 2, 3)
            ]
        other = 1 - (place.m if axis == "x" else place.y)
        source = self._at(chunk, dict(before, **{axis: other}))
        return [copy(source, land.at[chunk], SLOT[axis], place.peer[axis])]

    def stage(self, index, chunk):
        if index > 0:
            axis, (_, have) = self.order[index - 1], self.haves[index - 1]
            land = self.lands[axis]
            for copy in self._copies(index - 1, chunk):
                copy.wait_recv()
            mine = self._at(chunk, have)
            value = mine[...].astype(F32)
            if axis == "z":
                for step in range(3):
                    value += land[chunk, step].astype(F32)
            else:
                value += land[chunk].astype(F32)
            if index == self.count - 1:
                self.finish(chunk, value)
            else:
                mine[...] = value.astype(mine.dtype)
        if index < self.count - 1:
            for copy in self._copies(index, chunk, True):
                copy.start()

    def drain(self):
        def one(chunk, carry):
            for index in range(self.count - 1):
                for copy in self._copies(index, chunk):
                    copy.wait_send()
            return carry

        lax.fori_loop(0, self.chunks, one, 0)


VROWS = 16


def rows_from_blocks(blocks, pick, counts):
    mp_count, dp_count = counts
    width = pick.shape[1]
    each = width // (mp_count * dp_count)
    wide = lax.dot_general(
        blocks, pick, NN, precision=lax.Precision.HIGHEST, preferred_element_type=F32
    )
    lane = lax.broadcasted_iota(jnp.int32, (VROWS, width), 1)
    table = jnp.zeros((VROWS, width), F32)
    for m in range(mp_count):
        for r in range(dp_count):
            first = (r * mp_count + m) * each
            row = (m * dp_count + r) * VROWS
            table += jnp.where((lane >= first) & (lane < first + each), wide[row : row + VROWS], 0.0)
    return table


def attend_setup(heads, m, box_full, vec_ref, box_heads, bias):
    cols = heads * HD
    for head in range(heads):
        box_heads[head] = box_full[:, head * HD : (head + 1) * HD]
    width = vec_ref.shape[1]
    own = jnp.where(m == 0, vec_ref[6:8, 0:cols], vec_ref[6:8, width - cols :])
    spread = exact_dot(jnp.broadcast_to(own[1:2], (8, cols)), pair_place(cols))
    bias[0:1, 0:cols] = own[0:1]
    bias[0:1, cols:] = spread[0:1]


def attend_trig(omega_ref, corner_ref, trig_ref):
    corner = corner_ref[...].astype(F32)
    angle_x = omega_ref[...] * ((corner[0:1] + corner[2:3]) * 0.5)
    angle_y = omega_ref[...] * ((corner[1:2] + corner[3:4]) * 0.5)
    trig_ref[0:FREQS, :] = jnp.cos(angle_x)
    trig_ref[FREQS : 2 * FREQS, :] = jnp.sin(angle_x)
    trig_ref[2 * FREQS : 3 * FREQS, :] = jnp.cos(angle_y)
    trig_ref[3 * FREQS :, :] = jnp.sin(angle_y)


def attend_kernel(heads, plan, *refs):
    cols = heads * HD
    m = lax.axis_index("mp")
    refs = list(refs)

    def take(count):
        head, refs[:] = refs[:count], refs[count:]
        return head

    x_ref, corner_ref, omega_ref = take(3)
    if plan is None:
        w_ref, box_ref, vec_ref = take(3)
    else:
        attn_ref, shard_box, vectors_ref, pick_ref, merge_ref, expand_ref, shrink_ref = take(7)
    qa_ref, qtok_ref, kvtok_ref, kt_ref, kft_ref, trig_ref, ctxt_ref, log_ref, ctxx_ref = take(9)
    if plan is not None:
        w_out, box_out, vec_ref, full_e, full_f = take(5)
    kftok_ref, box_heads, bias, ctx_ref, vt_ref = take(5)
    pages = x_ref.shape[0] // PAGE
    halves_of_page = 2
    piece = PAGE // halves_of_page
    own_pieces = pages

    if plan is None:
        attend_setup(heads, m, box_ref, vec_ref, box_heads, bias)
        attend_trig(omega_ref, corner_ref, trig_ref)

        def weights(chunk):
            return w_ref[chunk]

        def background(number):
            pass
    else:
        w_ref, box_gather, vec_gather, shard_e, shard_f, *sems = take(12)
        ctx_sem, a_sem, b_sem, v_sem, e_sem, f_sem, loc_sem = sems
        place = Place()
        place.signal()
        at = (place.z, place.y, place.c)
        shard_e[0] = merge_ref[...].astype(BF16)
        for chunk in range(4):
            lanes = slice(chunk * UNIT, (chunk + 1) * UNIT)
            shard_e[1 + chunk] = expand_ref[:, lanes].astype(BF16)
            shard_f[chunk] = shrink_ref[:, lanes].astype(BF16)
        locals_ = [
            pltpu.make_async_copy(shard_e, full_e.at[(ALL, place.m, *at)], loc_sem.at[0]),
            pltpu.make_async_copy(shard_f, full_f.at[(ALL, place.m, *at)], loc_sem.at[1]),
        ]
        for copy in locals_:
            copy.start()
        w_ref[(0, 0, *at)] = attn_ref[0].astype(BF16)
        for half in range(2):
            w_ref[(1 + half, 0, *at)] = jnp.concatenate(
                [
                    attn_ref[1 + kind, :, head * HD : (head + 1) * HD].astype(BF16)
                    for head in range(half * heads // 2, (half + 1) * heads // 2)
                    for kind in range(2)
                ],
                axis=1,
            )
        box_gather[(0, 0, *at)] = shard_box[...]
        own_vec = jnp.zeros((VROWS, 128), F32)
        vec_gather[(0, place.m, *at)] = own_vec
        vec_gather[(0, place.m, *at, slice(0, vectors_ref.shape[0]), slice(0, vectors_ref.shape[1]))] = (
            vectors_ref[...]
        )
        for copy in locals_:
            copy.wait()
        place.wait()
        tree_v = Spread(place, vec_gather, 1, "xzyc", v_sem)
        tree_b = Spread(place, box_gather, 1, "zyc", b_sem)
        tree_a = Spread(place, w_ref, 3, "zyc", a_sem)
        tree_e = Spread(place, full_e, 5, "zyxc", e_sem)
        tree_f = Spread(place, full_f, 4, "xzyc", f_sem)
        late = 3
        first = tree_a.events
        last = max(tree_e.events, tree_f.events)

        def background(number):
            tree_e.event(number)
            tree_f.event(number)

        def begin(number, carry):
            tree_a.event(number)
            tree_b.event(number)
            tree_v.event(number)
            background(number - late)
            pl.when(number == 1)(lambda: attend_trig(omega_ref, corner_ref, trig_ref))
            return carry

        lax.fori_loop(0, first, begin, 0)
        blocks = vec_gather[...].reshape(-1, 128)
        vec_ref[...] = rows_from_blocks(blocks, pick_ref[...], plan)
        box_out[...] = box_gather[...].reshape(PE, cols).astype(BF16)
        attend_setup(heads, m, box_out, vec_ref, box_heads, bias)
        copy_w = pltpu.make_async_copy(w_ref, w_out, loc_sem.at[0])
        copy_w.start()

        def weights(chunk):
            return w_ref[chunk].reshape(-1, cols)

    def project(page, carry):
        rows = aligned(page, PAGE)
        tokens = x_ref[rows, :]
        query = dot(tokens, weights(0)) + bias[0:1, 0:cols]
        query = query.astype(BF16) * HD ** (-0.5)
        qtok_ref[rows, :] = query
        qa_rows = query.T
        for half in range(2):
            lanes = slice(half * cols, (half + 1) * cols)
            pair = dot(tokens, weights(1 + half)) + bias[0:1, cols + half * cols : 2 * cols + half * cols]
            pair = pair.astype(BF16)
            kvtok_ref[rows, lanes] = pair
            turned = pair.T
            for spot in range(heads // 2):
                head_rows = slice((half * heads // 2 + spot) * HD, (half * heads // 2 + spot + 1) * HD)
                kt_ref[head_rows, rows] = turned[2 * spot * HD : (2 * spot + 1) * HD]
                vt_ref[head_rows, rows] = turned[(2 * spot + 1) * HD : (2 * spot + 2) * HD]
        trig = trig_ref[:, rows]
        kft = trig.astype(BF16)
        kft_ref[:, rows] = kft
        kftok_ref[rows, :] = kft.T
        own, partner = turn_factors(trig)
        for head in range(heads):
            query_head = qa_rows[head * HD : (head + 1) * HD]
            proj = dot(box_heads[head], query_head)
            feat = proj * own + swap_blocks(proj) * partner
            qa_ref[head, 0:PE, rows] = feat.astype(BF16)
            qa_ref[head, PE : PE + HD, rows] = query_head
        if plan is not None:
            background(page + first - late)
        return carry

    lax.fori_loop(0, pages, project, 0)

    def attend(step, carry):
        turn, pair = step // (heads // 2), step % (heads // 2)
        page = turn if plan is None else turn * m + (pages - 1 - turn) * (1 - m)
        rows = aligned(page, PAGE)
        halves = []
        blank = jnp.zeros((HD, PAGE), BF16)
        for side in range(2):
            head = pair * 2 + side
            lanes = aligned(head, 2 * HD)
            left = jnp.concatenate([kftok_ref[rows, :], kvtok_ref[rows, lanes]], axis=1)
            score = dot(left, jnp.concatenate([qa_ref[head, :, rows], blank], axis=0))
            top = jnp.max(score, axis=0, keepdims=True)
            weight = jnp.exp(score - top)
            total = jnp.sum(weight, axis=0, keepdims=True)
            value = vt_ref[aligned(head, HD), rows]
            halves.append(dot(value, weight.astype(BF16)) * (1.0 / total))
            log_ref[head, :, rows] = top + jnp.log(total)
        both = jnp.concatenate(halves, axis=0).astype(BF16)
        lanes = aligned(pair, 2 * HD)
        ctxt_ref[lanes, rows] = both
        ctx_ref[rows, lanes] = both.T
        if plan is not None:
            pl.when((step % 2 == 0))(lambda: background(step // 2 + first - late + pages))
            pl.when(pair == heads // 2 - 1)(lambda: swap(turn))
        return carry

    def swap_copy(index):
        theirs = pages * (1 - m) + index
        return remote(
            ctx_ref.at[aligned(theirs, piece), :],
            ctxx_ref.at[m, aligned(index, piece), :],
            ctx_sem.at[0, index],
            ctx_sem.at[1, index],
            place.peer["x"],
        )

    def swap(turn):
        @pl.when(turn == 0)
        def _():
            swap_copy(2 - 2 * m).start()
            swap_copy(1).start()

        @pl.when(turn == 1)
        def _():
            swap_copy(2 * m).start()

    lax.fori_loop(0, pages * (heads // 2), attend, 0)
    if plan is None:
        ctxx_ref[...] = ctx_ref[...]
        return
    keep = pltpu.make_async_copy(
        ctx_ref.at[aligned(m, pages * piece), :], ctxx_ref.at[m], loc_sem.at[1]
    )
    keep.start()
    done = first - late + pages + (pages * (heads // 2) + 1) // 2

    def rest(number, carry):
        background(number)
        return carry

    lax.fori_loop(done, last, rest, 0)
    for index in range(own_pieces):
        copy = remote(
            ctx_ref.at[aligned(index, piece), :],
            ctxx_ref.at[1 - m, aligned(index, piece), :],
            ctx_sem.at[0, index],
            ctx_sem.at[1, index],
            place.peer["x"],
        )
        copy.wait_recv()
        copy.wait_send()
    keep.wait()
    copy_w.wait()
    for tree in (tree_v, tree_b, tree_a, tree_e, tree_f):
        tree.drain()


def attend_forward(x, corners, omega, weights, plan):
    tokens, width = x.shape
    cols = weights[1].shape[1]
    heads = cols // HD
    shapes = [
        ((heads, PE + HD, tokens), BF16),
        ((tokens, cols), BF16),
        ((tokens, 2 * cols), BF16),
        ((cols, tokens), BF16),
        ((PE, tokens), BF16),
        ((PE, tokens), F32),
        ((cols, tokens), BF16),
        ((heads, 1, tokens), F32),
    ]
    vmem = pl.BlockSpec(memory_space=pltpu.VMEM)
    free = pl.BlockSpec(memory_space=pl.ANY)
    scratch = [
        pltpu.VMEM((tokens, PE), BF16),
        pltpu.VMEM((heads, PE, HD), BF16),
        pltpu.VMEM((8, 3 * cols), F32),
        pltpu.VMEM((tokens, cols), BF16),
        pltpu.VMEM((cols, tokens), BF16),
    ]
    in_specs, out_specs = [vmem] * 6, [vmem] * len(shapes)
    if plan is None:
        shapes.append(((tokens, cols), BF16))
        out_specs.append(vmem)
        extra = {}
    else:
        tail = (4, 2, 2, width // 16, UNIT)
        shapes += [
            ((2, tokens // 2, cols), BF16),
            ((3, 1, *tail), BF16),
            ((PE, cols), BF16),
            ((VROWS, width), F32),
            ((5, 2, *tail), BF16),
            ((4, 2, *tail), BF16),
        ]
        out_specs += [free, free, vmem, vmem, free, free]
        in_specs = [vmem] * 10
        scratch += [
            pltpu.VMEM((3, 1, *tail), BF16),
            pltpu.VMEM((1, 1, 4, 2, 2, PE // 16, cols), F32),
            pltpu.VMEM((1, 2, 4, 2, 2, VROWS, 128), F32),
            pltpu.VMEM((5, width // 16, UNIT), BF16),
            pltpu.VMEM((4, width // 16, UNIT), BF16),
            pltpu.SemaphoreType.DMA((2, 3)),
            pltpu.SemaphoreType.DMA((2, 3, SLOTS)),
            pltpu.SemaphoreType.DMA((2, 1, SLOTS)),
            pltpu.SemaphoreType.DMA((2, 1, SLOTS)),
            pltpu.SemaphoreType.DMA((2, 5, SLOTS)),
            pltpu.SemaphoreType.DMA((2, 4, SLOTS)),
            pltpu.SemaphoreType.DMA((2,)),
        ]
        extra = dict(collective_id=0, has_side_effects=True)
    return pl.pallas_call(
        functools.partial(attend_kernel, heads, plan),
        out_shape=[jax.ShapeDtypeStruct(s, d) for s, d in shapes],
        in_specs=in_specs,
        out_specs=out_specs,
        scratch_shapes=scratch,
        compiler_params=pltpu.CompilerParams(vmem_limit_bytes=VMEM_LIMIT, **extra),
        name="attend_forward",
    )(x, corners, omega, *weights)


TILE = 256


def norm_stats(value):
    mean = jnp.mean(value, axis=-1, keepdims=True)
    centred = value - mean
    var = jnp.mean(centred * centred, axis=-1, keepdims=True)
    return centred, lax.rsqrt(var + NORM_EPS)


def norm_back(grad_normed, normed, scale):
    first = jnp.mean(grad_normed, axis=-1, keepdims=True)
    second = jnp.mean(grad_normed * normed, axis=-1, keepdims=True)
    return scale * (grad_normed - first - normed * second)


def col_sum(value):
    return jnp.sum(value, axis=0, keepdims=True)


def feed_kernel(plan, inv_tokens, *refs):
    if plan is None:
        x_ref, og_ref, ctx_ref, we_ref, ws_ref, vec_ref, *refs = refs
        out_ref, dctx_ref, dh1l, ge_ref, gs_ref, vsum_ref, *refs = refs
        norm1, scale1, sum2, al, act, slope, dh2l, turned = refs
    else:
        x_all, og_all, ctx_all, we_all, ws_all, vec_ref, *refs = refs
        out_full, dctx_full, dh1l, ge_ref, vsum_ref, sum_f, *refs = refs
        norm1, scale1, sum2, al, act, slope, dh2l, turned, *refs = refs
        x_ref, og_ref, ctx_ref, we_ref, ws_ref, out_ref, dctx_ref, gs_ref, *refs = refs
        total_f, fc, fy, fz, fx, swap_sem, load_sem, f_sem = refs
    dnorm = sum2
    tokens = x_ref.shape[0]
    sides = we_ref.shape[1]
    per_side = (we_ref.shape[0] - 1) // 2
    steps = sides * per_side
    tiles = tokens // TILE
    wide = 2 * UNIT
    m = lax.axis_index("mp")
    if plan is not None:
        place = Place()
        place.signal()
        own = aligned(m, tokens)
        load_x = pltpu.make_async_copy(x_all.at[own, :], x_ref, load_sem.at[0])
        load_og = pltpu.make_async_copy(og_all.at[own, :], og_ref, load_sem.at[1])
        load_ctx = pltpu.make_async_copy(ctx_all, ctx_ref, load_sem.at[2])
        load_e = [
            pltpu.make_async_copy(we_all.at[k], we_ref.at[k], load_sem.at[3 + k]) for k in range(5)
        ]
        load_s = [
            pltpu.make_async_copy(ws_all.at[k], ws_ref.at[k], load_sem.at[8 + k]) for k in range(4)
        ]
        early = [load_x, load_ctx, load_e[0]]
        middle = [[load_e[1], load_e[2], load_s[0], load_s[1]], [load_e[3], load_e[4], load_s[2], load_s[3]]]
        for copy in early + middle[0] + middle[1] + [load_og]:
            copy.start()
        place.wait()
        peer = place.peer["x"]

        def finish(chunk, value):
            sum_f[chunk] = value * inv_tokens

        tree_f = Reduce(
            place, gs_ref, total_f, dict(c=fc, y=fy, z=fz, x=fx), 4, "cyzx", f_sem, finish
        )
        for copy in early:
            copy.wait()

    def two(ref, first, side):
        return jnp.concatenate([ref[first, side], ref[first + 1, side]], axis=1)

    def w_expand(step):
        return two(we_ref, 1 + 2 * (step % per_side), step // per_side)

    def w_shrink(step):
        return two(ws_ref, 2 * (step % per_side), step // per_side)

    def put_two(ref, first, side, value):
        shape = ref.shape[2:]
        ref[first, side] = value[:, 0:UNIT].reshape(shape)
        ref[first + 1, side] = value[:, UNIT:].reshape(shape)

    def background(number):
        if plan is not None:
            tree_f.event(number)

    def out_copies(tile):
        rows = aligned(tile, TILE)
        there = out_full.at[pl.ds(pl.multiple_of(m * tokens + tile * TILE, TILE), TILE), :]
        return (
            pltpu.make_async_copy(out_ref.at[rows, :], there, swap_sem.at[0, tile]),
            remote(out_ref.at[rows, :], there, swap_sem.at[1, tile], swap_sem.at[2, tile], peer),
        )

    def dctx_copies(tile):
        rows = aligned(tile, TILE)
        there = dctx_full.at[pl.ds(pl.multiple_of(m * tokens + tile * TILE, TILE), TILE), :]
        return (
            pltpu.make_async_copy(dctx_ref.at[m, rows, :], there, swap_sem.at[3, tile]),
            remote(
                dctx_ref.at[1 - m, rows, :], there, swap_sem.at[4, tile], swap_sem.at[5, tile], peer
            ),
        )

    def enter(tile, carry):
        rows = aligned(tile, TILE)
        total = x_ref[rows, :].astype(F32) + vec_ref[4:5, :]
        for side in range(sides):
            total += dot(ctx_ref[side, rows, :], we_ref[0, side], NT)
        centred, scale = norm_stats(total)
        normed = centred * scale
        norm1[rows, :] = normed
        scale1[rows, :] = scale
        shifted = normed * vec_ref[0:1, :] + vec_ref[1:2, :]
        al[rows, :] = shifted.astype(BF16)
        sum2[rows, :] = shifted + vec_ref[5:6, :]
        return carry

    lax.fori_loop(0, tiles, enter, 0)

    def grow(step, carry):
        whole = aligned(step, wide)
        if plan is not None:
            for k in range(2):

                @pl.when(step == k)
                def _(k=k):
                    for copy in middle[k]:
                        copy.wait()


        def one(tile, inner):
            rows = aligned(tile, TILE)
            pre = dot(al[rows, :], w_expand(step)) + vec_ref[pl.ds(8 + step, 1), :]
            phi = 0.5 + 0.5 * lax.erf(pre * 2.0 ** (-0.5))
            density = jnp.exp(pre * pre * -0.5) * (0.5 / jnp.pi) ** 0.5
            low = (pre * phi).astype(BF16)
            act[rows, whole] = low
            slope[rows, whole] = (phi + pre * density).astype(BF16)
            sum2[rows, :] += dot(low, w_shrink(step), NT)
            return inner

        lax.fori_loop(0, tiles, one, 0)
        return carry

    lax.fori_loop(0, steps, grow, 0)

    vsum_ref[...] = jnp.zeros_like(vsum_ref)
    if plan is not None:
        load_og.wait()

    def turn(tile, carry):
        rows = aligned(tile, TILE)
        centred, scale = norm_stats(sum2[rows, :])
        normed = centred * scale
        out_ref[rows, :] = (normed * vec_ref[2:3, :] + vec_ref[3:4, :]).astype(BF16)
        grad = og_ref[rows, :].astype(F32)
        vsum_ref[2:3, :] += col_sum(grad * normed)
        vsum_ref[3:4, :] += col_sum(grad)
        back = norm_back(grad * vec_ref[2:3, :], normed, scale)
        vsum_ref[5:6, :] += col_sum(back)
        dh2l[rows, :] = back.astype(BF16)
        dnorm[rows, :] = back
        if plan is not None:
            for copy in out_copies(tile):
                copy.start()
        return carry

    lax.fori_loop(0, tiles, turn, 0)

    turned[...] = dh2l[...].T

    def grad_shrink(number, carry):
        half, side = number // sides, number % sides
        step = side * per_side + half
        grad = dot(turned[...], act[:, aligned(step, wide)]).astype(BF16)
        put_two(gs_ref, 2 * half, side, grad)
        if plan is not None:

            @pl.when(side == sides - 1)
            def _():
                for k in range(2):
                    total_f[2 * half + k] = gs_ref[2 * half + k, :, :, :, place.c]
                background(half)

        return carry

    lax.fori_loop(0, steps, grad_shrink, 0)

    def shrink(step, carry):
        whole = aligned(step, wide)

        def one(tile, inner):
            rows = aligned(tile, TILE)
            grad = dot(dh2l[rows, :], w_shrink(step))
            low = (grad * slope[rows, whole].astype(F32)).astype(BF16)
            slope[rows, whole] = low
            vsum_ref[pl.ds(8 + step, 1), :] += col_sum(low.astype(F32))
            dnorm[rows, :] += dot(low, w_expand(step), NT)
            number = step * tiles + tile
            if plan is not None:
                pl.when(number % 2 == 1)(lambda: background(2 + number // 2))
            return inner

        lax.fori_loop(0, tiles, one, 0)
        return carry

    lax.fori_loop(0, steps, shrink, 0)

    def leave(tile, carry):
        rows = aligned(tile, TILE)
        grad = dnorm[rows, :]
        normed = norm1[rows, :]
        vsum_ref[0:1, :] += col_sum(grad * normed)
        vsum_ref[1:2, :] += col_sum(grad)
        back = norm_back(grad * vec_ref[0:1, :], normed, scale1[rows, :])
        vsum_ref[4:5, :] += col_sum(back)
        low = back.astype(BF16)
        dh1l[rows, :] = low
        for side in range(sides):
            dctx_ref[side, rows, :] = dot(low, we_ref[0, side]).astype(BF16)
        if plan is not None:
            for copy in dctx_copies(tile):
                copy.start()
            background(2 + steps * tiles // 2 + tile)
        return carry

    lax.fori_loop(0, tiles, leave, 0)

    turned[...] = al[...].T

    def grad_expand(step, carry):
        grad = dot(turned[...], slope[:, aligned(step, wide)]).astype(BF16)
        put_two(ge_ref, 1 + 2 * (step % per_side), step // per_side, grad)
        return carry

    lax.fori_loop(0, steps, grad_expand, 0)
    turned[...] = dh1l[...].T
    for side in range(sides):
        ge_ref[0, side] = dot(turned[...], ctx_ref[side]).astype(BF16).reshape(ge_ref.shape[2:])
    if plan is not None:
        tree_f.drain()
        for tile in range(tiles):
            for copies in (out_copies(tile), dctx_copies(tile)):
                for copy in copies:
                    copy.wait()


def feed_both(x, og, ctx, w_expand, w_shrink, vecs, plan, inv_tokens):
    tokens, width = x.shape
    chunks, sides = w_shrink.shape[0:2]
    hidden = chunks * UNIT
    if plan is not None:
        tokens //= sides
    out_shape = (tokens, width)
    dctx_shape = (sides, tokens, UNIT)
    rows = (width,) if plan is None else (4, 2, 2, width // 16)
    shrink_shape = (chunks, sides, *rows, UNIT)
    shapes = [
        (out_shape, BF16),
        (dctx_shape, BF16),
        (out_shape, BF16),
        ((chunks + 1, sides, *rows, UNIT), BF16),
        (shrink_shape, BF16),
        ((VROWS, width), F32),
    ]
    scratch = [
        pltpu.VMEM(out_shape, F32),
        pltpu.VMEM((tokens, 1), F32),
        pltpu.VMEM(out_shape, F32),
        pltpu.VMEM(out_shape, BF16),
        pltpu.VMEM((tokens, sides * hidden), BF16),
        pltpu.VMEM((tokens, sides * hidden), BF16),
        pltpu.VMEM(out_shape, BF16),
        pltpu.VMEM((width, tokens), BF16),
    ]
    vmem = pl.BlockSpec(memory_space=pltpu.VMEM)
    free = pl.BlockSpec(memory_space=pl.ANY)
    in_specs = [vmem] * 6
    out_specs = [vmem] * len(shapes)
    extra = {}
    if plan is not None:
        unit = (width // 16, UNIT)
        in_specs = [free] * 5 + [vmem]
        shapes[0] = ((sides * tokens, width), BF16)
        shapes[1] = ((sides * tokens, UNIT), BF16)
        shapes[4:] = [((VROWS, width), F32), ((chunks, *unit), F32)]
        out_specs[0:2] = [free] * 2
        scratch += [
            pltpu.VMEM(out_shape, BF16),
            pltpu.VMEM(out_shape, BF16),
            pltpu.VMEM(dctx_shape, BF16),
            pltpu.VMEM(w_expand.shape, BF16),
            pltpu.VMEM(w_shrink.shape, BF16),
            pltpu.VMEM(out_shape, BF16),
            pltpu.VMEM(dctx_shape, BF16),
            pltpu.VMEM(shrink_shape, BF16),
            pltpu.VMEM((4, 2, 4, 2, *unit), BF16),
            pltpu.VMEM((4, 2, 4, 2, *unit), BF16),
            pltpu.VMEM((4, 2, 4, *unit), BF16),
            pltpu.VMEM((4, 3, 2, *unit), BF16),
            pltpu.VMEM((4, *unit), BF16),
            pltpu.SemaphoreType.DMA((6, tokens // TILE)),
            pltpu.SemaphoreType.DMA((12,)),
            pltpu.SemaphoreType.DMA((2, 4, SLOTS)),
        ]
        extra = dict(collective_id=1, has_side_effects=True)
    return pl.pallas_call(
        functools.partial(feed_kernel, plan, inv_tokens),
        out_shape=[jax.ShapeDtypeStruct(s, d) for s, d in shapes],
        in_specs=in_specs,
        out_specs=out_specs,
        scratch_shapes=scratch,
        compiler_params=pltpu.CompilerParams(vmem_limit_bytes=VMEM_LIMIT, **extra),
        name="feed_both",
    )(x, og, ctx, w_expand, w_shrink, vecs)


def pair_place(cols):
    spot = lax.broadcasted_iota(jnp.int32, (cols, 2 * cols), 0)
    lane = lax.broadcasted_iota(jnp.int32, (cols, 2 * cols), 1)
    target = ((spot >> 6) << 7) + HD + (spot & (HD - 1))
    return jnp.where(lane == target, 1.0, 0.0)


def exact_dot(lhs, rhs, dims=NN):
    return lax.dot_general(
        lhs, rhs, dims, precision=lax.Precision.HIGHEST, preferred_element_type=F32
    )


def attend_back_kernel(heads, plan, inv_tokens, *refs):
    x_ref, w_ref, box_ref, *refs = refs
    qa_ref, qtok_ref, kvtok_ref, kt_ref, kft_ref, trig_ref, ctxt_ref, log_ref, dctx_ref, *refs = refs
    cols = heads * HD
    tokens = x_ref.shape[0]
    pages = tokens // PAGE
    m = lax.axis_index("mp")
    piece = PAGE // 2
    pieces = 2 * pages
    lane = lax.broadcasted_iota(jnp.int32, (1, 2 * HD), 1)
    lower = lane < HD
    if plan is None:
        inp_ref, gw_ref, gbox_ref, qvsum_ref, *refs = refs
        kftok, dctxt, boxt, dtok, xt, gbox = refs
        before, after = 0, 0

        def background(number):
            pass
    else:
        dh1_ref, vsum_ref, sumf_ref, pick_ref, full_e, *refs = refs
        inp_ref, sum_e, sum_a, sum_b, sum_v, norm_ref, *refs = refs
        kftok, dctxt, boxt, dtok, xt, gbox, *refs = refs
        came, total_e, full_a, total_a, full_b, total_b, full_v, total_v, norms, *refs = refs
        (ec, ey, ez, ex, ac, ay, az, bc, by, bz, vc, vy, vz, vx, *refs) = refs
        e_sem, a_sem, b_sem, v_sem, n_sem, i_sem, loc_sem = refs
        place = Place()
        place.signal()
        fill = pltpu.make_async_copy(full_e.at[:, :, :, :, place.c], total_e, loc_sem.at[0])
        fill.start()
        place.wait()

        def finish(out):
            def put(chunk, value):
                out[chunk] = value * inv_tokens

            return put

        tree_e = Reduce(
            place, full_e, total_e, dict(c=ec, y=ey, z=ez, x=ex), 5, "cyzx", e_sem, finish(sum_e)
        )
        tree_a = Reduce(place, full_a, total_a, dict(c=ac, y=ay, z=az), 3, "cyz", a_sem, finish(sum_a))
        tree_b = Reduce(place, full_b, total_b, dict(c=bc, y=by, z=bz), 1, "cyz", b_sem, finish(sum_b))
        tree_v = Reduce(
            place, full_v, total_v, dict(c=vc, y=vy, z=vz, x=vx), 1, "cyzx", v_sem, finish(sum_v)
        )
        tree_n = Spread(place, norms, 1, "cyxz", n_sem)

        def background(number):
            tree_e.event(number)

        background(0)
        fill.wait()

    boxt[...] = box_ref[...].T
    gbox[...] = jnp.zeros_like(gbox)

    def prepare(page, carry):
        rows = aligned(page, PAGE)
        kftok[rows, :] = kft_ref[:, rows].T
        dctxt[:, rows] = dctx_ref[rows, :].T
        xt[:, rows] = x_ref[rows, :].T
        background(page + 1)
        return carry

    lax.fori_loop(0, pages, prepare, 0)

    def attend(step, carry):
        page, pair = step // (heads // 2), step % (heads // 2)
        rows = aligned(page, PAGE)
        own, partner = turn_factors(trig_ref[:, rows])
        pair_lanes = aligned(pair, 2 * HD)
        query_pair = qtok_ref[rows, pair_lanes]
        dctx_pair = dctx_ref[rows, pair_lanes]
        halves = []
        boxes = []
        blank = jnp.zeros((HD, PAGE), BF16)
        for side in range(2):
            head = pair * 2 + side
            lanes = aligned(head, 2 * HD)
            key_value = kvtok_ref[rows, lanes]
            left = jnp.concatenate([kftok[rows, :], key_value], axis=1)
            score = dot(left, jnp.concatenate([qa_ref[head, :, rows], blank], axis=0))
            prob = jnp.exp(score - log_ref[head, :, rows])
            prob_low = prob.astype(BF16)
            head_rows = pl.ds(pl.multiple_of(head * HD, HD), HD)
            dctx_head = dctxt[head_rows, rows]
            grad_prob = dot(
                key_value, jnp.concatenate([blank, dctx_head], axis=0)
            )
            inner = col_sum(dctx_head.astype(F32) * ctxt_ref[head_rows, rows].astype(F32))
            grad_score = (prob * (grad_prob - inner)).astype(BF16)
            if side == 0:
                both = jnp.concatenate([query_pair[:, 0:HD], dctx_pair[:, 0:HD]], axis=1)
            else:
                both = jnp.concatenate([query_pair[:, HD:], dctx_pair[:, HD:]], axis=1)
            from_score = dot(grad_score, both)
            from_prob = dot(prob_low, both)
            grad_kv = jnp.where(lower, from_score, from_prob).astype(BF16)
            dtok[rows, pl.ds(pl.multiple_of(cols + head * 2 * HD, 2 * HD), 2 * HD)] = grad_kv
            keys = jnp.concatenate([kft_ref[:, rows], kt_ref[head_rows, rows]], axis=0)
            grad_query = dot(keys, grad_score) * HD ** (-0.5)
            feat = grad_query[0:PE]
            proj = (feat * own - swap_blocks(feat) * partner).astype(BF16)
            halves.append(grad_query[PE:] + dot(boxt[head_rows, :], proj))
            boxes.append(dot(proj, query_pair))
        gbox[:, pair_lanes] += jnp.where(lower, boxes[0], boxes[1])
        dtok[rows, pair_lanes] = jnp.concatenate(halves, axis=0).astype(BF16).T
        return carry

    def spread(page):
        rows = aligned(page, PAGE)
        return sum(
            dot(dtok[rows, chunk * UNIT : (chunk + 1) * UNIT], w_ref[chunk], NT) for chunk in range(3)
        )

    if plan is None:
        lax.fori_loop(0, pages * (heads // 2), attend, 0)
        gbox_ref[...] = gbox[...] * HD**0.5

        def spread_page(page, carry):
            inp_ref[aligned(page, PAGE), :] = spread(page)
            return carry

        lax.fori_loop(0, pages, spread_page, 0)

        def gather(step, carry):
            lanes = aligned(step, UNIT)
            gw_ref[step] = dot(xt[...], dtok[:, lanes]).astype(BF16)
            qvsum_ref[0:1, lanes] = col_sum(dtok[:, lanes].astype(F32))
            return carry

        lax.fori_loop(0, 3, gather, 0)
        return

    def swap(index):
        rows = aligned(index, piece)
        return remote(
            inp_ref.at[rows, :], came.at[rows, :], i_sem.at[0, index], i_sem.at[1, index], place.peer["x"]
        )

    def attend_and_send(step, carry):
        attend(step, carry)
        page = step // (heads // 2)

        @pl.when(step % (heads // 2) == heads // 2 - 1)
        def _():
            value = spread(page)
            for half in range(2):
                index = 2 * page + half
                rows = aligned(index, piece)
                own = index // pages == m
                spot = aligned(index % pages, piece)
                extra = jnp.where(own, dh1_ref[spot, :].astype(F32), 0.0)
                inp_ref[rows, :] = (value[half * piece : (half + 1) * piece] + extra).astype(BF16)
                swap(index).start()

        background(step + 1 + pages)
        return carry

    lax.fori_loop(0, pages * (heads // 2), attend_and_send, 0)
    begun = pages * (heads // 2) + 1 + pages

    full_b[0, 0] = (gbox[...] * HD**0.5).reshape(4, 2, 2, PE // 16, cols)
    total_b[0, 0] = full_b[0, 0, :, :, place.c]

    def gather(step, carry):
        grad = dot(xt[...], dtok[:, aligned(step, UNIT)]).astype(BF16)
        full_a[step, 0] = grad.reshape(full_a.shape[2:])
        total_a[step, 0] = full_a[step, 0, :, :, place.c]
        tree_a.event(step)
        tree_b.event(step)
        background(begun + step)
        return carry

    lax.fori_loop(0, 3, gather, 0)

    sums = jnp.concatenate(
        [
            col_sum(dtok[:, chunk * UNIT : (chunk + 1) * UNIT].astype(F32)) for chunk in range(3)
        ],
        axis=1,
    )
    values = exact_dot(jnp.broadcast_to(sums[:, cols:], (8, 2 * cols)), pair_place(cols), NT)
    pair = jnp.concatenate([sums[:, 0:cols], values[0:1]], axis=0)
    blank = jnp.zeros_like(pair)
    pair = jnp.where(
        m == 0, jnp.concatenate([pair, blank], axis=1), jnp.concatenate([blank, pair], axis=1)
    )
    table = jnp.concatenate([vsum_ref[0:6, :], pair, vsum_ref[8:, :]], axis=0)
    mp_count, dp_count = plan
    width = table.shape[1]
    each = width // (mp_count * dp_count)
    wide_lane = lax.broadcasted_iota(jnp.int32, (VROWS, width), 1)
    for side in range(mp_count):
        parts = []
        for r in range(dp_count):
            first = (r * mp_count + side) * each
            parts.append(jnp.where((wide_lane >= first) & (wide_lane < first + each), table, 0.0))
        block = exact_dot(jnp.concatenate(parts, axis=0), pick_ref[...], NT)
        full_v[0, side] = block.reshape(full_v.shape[2:])
    total_v[0] = full_v[0, :, :, :, place.c]

    def tail(number, carry):
        tree_a.event(number)
        tree_b.event(number)
        tree_v.event(number - 3)
        background(begun + number)
        return carry

    last = max(tree_a.events, tree_b.events, tree_v.events + 3, tree_e.events - begun)
    lax.fori_loop(3, last, tail, 0)

    square = sum(jnp.sum(out[...] * out[...]) for out in (sum_e, sumf_ref, sum_a, sum_b, sum_v))
    norms[0, place.m, place.z, place.y, place.c] = jnp.full((8, 128), square, F32)

    def final(number, carry):
        tree_n.event(number)

        @pl.when(number < pieces)
        def _():
            rows = aligned(number, piece)
            swap(number).wait()
            inp_ref[rows, :] = (inp_ref[rows, :].astype(F32) + came[rows, :].astype(F32)).astype(BF16)

        return carry

    lax.fori_loop(0, max(tree_n.events, pieces), final, 0)
    every = norms[...].reshape(-1, 8, 128)
    norm_ref[...] = jnp.sqrt(sum(every[k] for k in range(every.shape[0])))

    for tree in (tree_e, tree_a, tree_b, tree_v, tree_n):
        tree.drain()


def attend_backward(x, weight, box, kept, dctx, plan, inv_tokens, more=()):
    tokens, width = x.shape
    cols = weight.shape[2]
    heads = cols // HD
    vmem = pl.BlockSpec(memory_space=pltpu.VMEM)
    scratch = [
        pltpu.VMEM((tokens, PE), BF16),
        pltpu.VMEM((cols, tokens), BF16),
        pltpu.VMEM((cols, PE), BF16),
        pltpu.VMEM((tokens, 3 * cols), BF16),
        pltpu.VMEM((width, tokens), BF16),
        pltpu.VMEM((PE, cols), F32),
    ]
    in_specs = [vmem] * 12
    if plan is None:
        shapes = [
            ((tokens, width), F32),
            ((3, width, cols), BF16),
            ((PE, cols), F32),
            ((8, 3 * cols), F32),
        ]
        extra = {}
    else:
        in_specs += [vmem] * 4 + [pl.BlockSpec(memory_space=pl.ANY)]
        rows = width // 16
        unit = (rows, UNIT)
        tile = (PE // 16, cols)
        small = (VROWS, 128)
        shapes = [
            ((tokens, width), BF16),
            ((5, *unit), F32),
            ((3, *unit), F32),
            ((1, *tile), F32),
            ((1, *small), F32),
            ((8, 128), F32),
        ]
        scratch += [
            pltpu.VMEM((tokens, width), BF16),
            pltpu.VMEM((5, 2, 4, 2, *unit), BF16),
            pltpu.VMEM((3, 1, 4, 2, 2, *unit), BF16),
            pltpu.VMEM((3, 1, 4, 2, *unit), BF16),
            pltpu.VMEM((1, 1, 4, 2, 2, *tile), F32),
            pltpu.VMEM((1, 1, 4, 2, *tile), F32),
            pltpu.VMEM((1, 2, 4, 2, 2, *small), F32),
            pltpu.VMEM((1, 2, 4, 2, *small), F32),
            pltpu.VMEM((1, 2, 4, 2, 2, 8, 128), F32),
            pltpu.VMEM((5, 2, 4, 2, *unit), BF16),
            pltpu.VMEM((5, 2, 4, *unit), BF16),
            pltpu.VMEM((5, 3, 2, *unit), BF16),
            pltpu.VMEM((5, *unit), BF16),
            pltpu.VMEM((3, 4, 2, *unit), BF16),
            pltpu.VMEM((3, 4, *unit), BF16),
            pltpu.VMEM((3, 3, *unit), BF16),
            pltpu.VMEM((1, 4, 2, *tile), F32),
            pltpu.VMEM((1, 4, *tile), F32),
            pltpu.VMEM((1, 3, *tile), F32),
            pltpu.VMEM((1, 2, 4, 2, *small), F32),
            pltpu.VMEM((1, 2, 4, *small), F32),
            pltpu.VMEM((1, 3, 2, *small), F32),
            pltpu.VMEM((1, *small), F32),
            pltpu.SemaphoreType.DMA((2, 5, SLOTS)),
            pltpu.SemaphoreType.DMA((2, 3, SLOTS)),
            pltpu.SemaphoreType.DMA((2, 1, SLOTS)),
            pltpu.SemaphoreType.DMA((2, 1, SLOTS)),
            pltpu.SemaphoreType.DMA((2, 1, SLOTS)),
            pltpu.SemaphoreType.DMA((2, 2 * (tokens // PAGE))),
            pltpu.SemaphoreType.DMA((2,)),
        ]
        extra = dict(collective_id=2, has_side_effects=True)
    return pl.pallas_call(
        functools.partial(attend_back_kernel, heads, plan, inv_tokens),
        out_shape=[jax.ShapeDtypeStruct(s, d) for s, d in shapes],
        in_specs=in_specs,
        out_specs=[vmem] * len(shapes),
        scratch_shapes=scratch,
        compiler_params=pltpu.CompilerParams(vmem_limit_bytes=VMEM_LIMIT, **extra),
        name="attend_backward",
    )(x, weight, box, *kept, dctx, *more)


def adam_step(master, first, second, gradient, rate, decay):
    new_first = BETA_ONE * first + (1.0 - BETA_ONE) * gradient
    new_second = BETA_TWO * second + (1.0 - BETA_TWO) * gradient * gradient
    first_hat = new_first / (1.0 - BETA_ONE**STEP)
    second_hat = new_second / (1.0 - BETA_TWO**STEP)
    new_master = master - rate * (first_hat / (jnp.sqrt(second_hat) + ADAM_EPS) + decay * master)
    return (new_first, new_second, new_master)


def adam_kernel(heads, norm_ref, *refs):
    sum_e, sum_f, sum_a, sum_b, sum_v, *refs = refs
    states, outs = refs[:18], refs[18:]
    clip = CLIP_LIMIT / jnp.maximum(norm_ref[0:1, 0:1], CLIP_LIMIT)

    def update(first, out, gradient, at, rate, decay):
        news = adam_step(*(ref[at] for ref in states[first : first + 3]), gradient * clip, rate, decay)
        for ref, new in zip(outs[out : out + 3], news):
            ref[at] = new
        if decay:
            outs[out + 3][at] = news[2].astype(BF16)

    def heads_of(kind):
        half = heads // 2
        return jnp.concatenate(
            [
                sum_a[1 + head // half, :, (2 * (head % half) + kind) * HD : (2 * (head % half) + kind + 1) * HD]
                for head in range(heads)
            ],
            axis=1,
        )

    for index, gradient in enumerate((sum_a[0], heads_of(0), heads_of(1))):
        update(0, 0, gradient, index, RATE_MATRIX, WEIGHT_DECAY)
    update(3, 4, sum_b[0], ALL, RATE_MATRIX, WEIGHT_DECAY)
    update(6, 8, sum_e[0], ALL, RATE_MATRIX, WEIGHT_DECAY)
    for chunk in range(4):
        lanes = (ALL, slice(chunk * UNIT, (chunk + 1) * UNIT))
        update(9, 12, sum_e[1 + chunk], lanes, RATE_MATRIX, WEIGHT_DECAY)
        update(12, 16, sum_f[chunk], lanes, RATE_MATRIX, WEIGHT_DECAY)
    rows, each = states[15].shape
    update(15, 20, sum_v[0, 0:rows, 0:each], ALL, RATE_VECTOR, 0.0)


def adam_all(norm, sums, states):
    shapes = []
    for first in range(0, 18, 3):
        shapes += [(states[first].shape, F32)] * 3
        if first < 15:
            shapes.append((states[first].shape, BF16))
    vmem = pl.BlockSpec(memory_space=pltpu.VMEM)
    return pl.pallas_call(
        functools.partial(adam_kernel, states[0].shape[2] // HD),
        out_shape=[jax.ShapeDtypeStruct(s, d) for s, d in shapes],
        in_specs=[vmem] * (6 + len(states)),
        out_specs=[vmem] * len(shapes),
        compiler_params=pltpu.CompilerParams(vmem_limit_bytes=VMEM_LIMIT),
        name="adam_all",
    )(norm, *sums, *states)


def pack_qkv(shard):
    rows, cols = shard.shape[1:]
    heads = cols // HD
    pairs = jnp.stack([shard[1].reshape(rows, heads, HD), shard[2].reshape(rows, heads, HD)], axis=2)
    pairs = pairs.reshape(rows, 2, cols)
    return jnp.stack([shard[0], pairs[:, 0], pairs[:, 1]])


def unpack_qkv(packed):
    rows, cols = packed.shape[1:]
    pairs = jnp.concatenate([packed[1], packed[2]], axis=1).reshape(rows, cols // HD, 2, HD)
    return jnp.stack(
        [packed[0], pairs[:, :, 0].reshape(rows, cols), pairs[:, :, 1].reshape(rows, cols)]
    )


def to_chunks(shard):
    rows = shard.shape[0]
    return shard.reshape(rows, -1, UNIT).transpose(1, 0, 2)


def from_chunks(chunks):
    return chunks.transpose(1, 0, 2).reshape(chunks.shape[1], -1)


def on_device(
    layer_input,
    page_boxes,
    output_grad,
    attn_proj,
    attn_first,
    attn_second,
    box_proj,
    box_first,
    box_second,
    merge_proj,
    merge_first,
    merge_second,
    expand_proj,
    expand_first,
    expand_second,
    shrink_proj,
    shrink_first,
    shrink_second,
    vectors,
    vector_first,
    vector_second,
):
    mp_count = lax.axis_size("mp")
    dp_count = lax.axis_size("dp")
    mp_index = lax.axis_index("mp")
    tokens, width = layer_input.shape
    cols = attn_proj.shape[2]
    heads = cols // HD
    own_tokens = tokens // mp_count
    inv_tokens = 1.0 / (tokens * dp_count)

    corners = page_boxes.T
    omega = (10000.0 ** (-np.arange(FREQS, dtype=np.float64) / FREQS)).astype(np.float32)[:, None]
    omega = jnp.asarray(omega)
    plan = (mp_count, dp_count) if dp_count == 16 and mp_count == 2 else None
    if plan is not None:
        each = vectors.shape[1]
        pick = np.zeros((128, width), np.float32)
        pick[np.arange(width) % each, np.arange(width)] = 1.0
        kept = attend_forward(
            layer_input,
            corners,
            omega,
            (attn_proj, box_proj, vectors, jnp.asarray(pick), merge_proj.T, expand_proj, shrink_proj.T),
            plan,
        )
        *kept, log_total, context, w_qkv, w_box, vecs, w_expand, w_shrink = kept
        w_qkv = w_qkv.reshape(3, width, cols)
        w_expand = w_expand.reshape(-1, mp_count, width, UNIT)
        w_shrink = w_shrink.reshape(-1, mp_count, width, UNIT)
    else:
        shard_qkv = pack_qkv(attn_proj).astype(BF16)
        shard_e = jnp.concatenate([merge_proj.T[None], to_chunks(expand_proj)]).astype(BF16)
        shard_f = to_chunks(shrink_proj.T).astype(BF16)
        w_qkv = lax.all_gather(shard_qkv, "dp", axis=1, tiled=True)
        w_box = lax.all_gather(box_proj.astype(BF16), "dp", axis=0, tiled=True)
        w_expand = lax.all_gather(lax.all_gather(shard_e, "dp", axis=1, tiled=True), "mp", axis=1)
        w_shrink = lax.all_gather(lax.all_gather(shard_f, "dp", axis=1, tiled=True), "mp", axis=1)
        vecs = lax.all_gather(vectors, ("dp", "mp"), axis=1, tiled=True)
        vecs = jnp.pad(vecs, ((0, VROWS - vecs.shape[0]), (0, 0)))
        kept = attend_forward(layer_input, corners, omega, (w_qkv, w_box, vecs), None)
        *kept, log_total, context = kept
        context = lax.all_to_all(
            context.reshape(mp_count, own_tokens, cols), "mp", split_axis=0, concat_axis=0
        )

    def own_rows(array):
        return lax.dynamic_slice_in_dim(array, mp_index * own_tokens, own_tokens)

    if plan is not None:
        layer_out, dctx, dh1, g_expand, vec_sum, sum_f = feed_both(
            layer_input, output_grad, context, w_expand, w_shrink, vecs, plan, inv_tokens
        )
        input_grad, sum_e, sum_a, sum_b, sum_v, norm = attend_backward(
            layer_input,
            w_qkv,
            w_box,
            (*kept, log_total),
            dctx,
            plan,
            inv_tokens,
            (dh1, vec_sum, sum_f, jnp.asarray(pick), g_expand),
        )
        merge = [merge_proj.T, merge_first.T, merge_second.T]
        shrink = [shrink_proj.T, shrink_first.T, shrink_second.T]
        results = adam_all(
            norm,
            (sum_e, sum_f, sum_a, sum_b, sum_v),
            [attn_proj, attn_first, attn_second, box_proj, box_first, box_second, *merge]
            + [expand_proj, expand_first, expand_second, *shrink, vectors, vector_first, vector_second],
        )
        turned = (8, 9, 10, 11, 16, 17, 18, 19)
        results = [out.T if k in turned else out for k, out in enumerate(results)]
        return (layer_out, input_grad, norm[0, 0], *results)
    else:
        layer_out, dctx, dh1, g_expand, g_shrink, vec_sum = feed_both(
            own_rows(layer_input), own_rows(output_grad), context, w_expand, w_shrink, vecs, None, inv_tokens
        )
        g_feed = jnp.concatenate([g_expand, g_shrink])
        layer_out = lax.all_gather(layer_out, "mp", axis=0, tiled=True)
        dctx = lax.all_to_all(dctx, "mp", split_axis=0, concat_axis=0).reshape(tokens, cols)
        part, g_qkv, g_box, qkv_sum = attend_backward(
            layer_input, w_qkv, w_box, (*kept, log_total), dctx, None, inv_tokens
        )
        own_part = lax.psum_scatter(part.astype(BF16), "mp", scatter_dimension=0, tiled=True)
        own_grad = (own_part.astype(F32) + dh1).astype(BF16)
        input_grad = lax.all_gather(own_grad, "mp", axis=0, tiled=True)
        shard_attn = unpack_qkv(
            lax.psum_scatter(g_qkv, "dp", scatter_dimension=1, tiled=True).astype(F32) * inv_tokens
        )
        shard_box = lax.psum_scatter(g_box, "dp", scatter_dimension=0, tiled=True) * inv_tokens
        sum_feed = lax.psum_scatter(g_feed, "dp", scatter_dimension=2, tiled=True)
        sum_feed = lax.psum_scatter(sum_feed, "mp", scatter_dimension=1, tiled=True)[:, 0]
        sum_feed = sum_feed.astype(F32) * inv_tokens
        sum_expand, sum_shrink = sum_feed[0:5], sum_feed[5:]

        def placed(row):
            return lax.dynamic_update_slice_in_dim(
                jnp.zeros((width,), F32), row, mp_index * cols, 0
            )[None, :]

        value_sum = qkv_sum[0, cols:].reshape(heads, 2, HD)[:, 1].reshape(cols)
        vector_grad = jnp.concatenate(
            [vec_sum[0:6], placed(qkv_sum[0, 0:cols]), placed(value_sum), vec_sum[8:12]]
        )
        vector_shard = (
            lax.psum_scatter(vector_grad, ("dp", "mp"), scatter_dimension=1, tiled=True) * inv_tokens
        )
        square = sum(
            jnp.sum(shard * shard)
            for shard in (shard_attn, shard_box, sum_expand, sum_shrink, vector_shard)
        )
        grad_norm = jnp.sqrt(lax.psum(square, ("dp", "mp")))
    shard_merge = sum_expand[0].T
    shard_expand = from_chunks(sum_expand[1:])
    shard_shrink = from_chunks(sum_shrink).T
    clip_scale = CLIP_LIMIT / jnp.maximum(grad_norm, CLIP_LIMIT)
    results = [layer_out, input_grad, grad_norm]
    for master, first, second, shard in (
        (attn_proj, attn_first, attn_second, shard_attn),
        (box_proj, box_first, box_second, shard_box),
        (merge_proj, merge_first, merge_second, shard_merge),
        (expand_proj, expand_first, expand_second, shard_expand),
        (shrink_proj, shrink_first, shrink_second, shard_shrink),
    ):
        new_first, new_second, new_master = adam_step(
            master, first, second, shard * clip_scale, RATE_MATRIX, WEIGHT_DECAY
        )
        results += [new_first, new_second, new_master, new_master.astype(BF16)]
    results += adam_step(
        vectors, vector_first, vector_second, vector_shard * clip_scale, RATE_VECTOR, 0.0
    )
    return tuple(results)


def solution(mesh):
    rows = P("dp", None)
    attn = P(None, "dp", "mp")
    tall = P("dp", "mp")
    wide = P("mp", "dp")
    vector = P(None, ("dp", "mp"))
    in_specs = (rows,) * 3 + (attn,) * 3 + (tall,) * 3 + (wide,) * 3 + (tall,) * 3 + (wide,) * 3
    in_specs += (vector,) * 3
    out_specs = (rows, rows, P()) + (attn,) * 4 + (tall,) * 4 + (wide,) * 4 + (tall,) * 4
    out_specs += (wide,) * 4 + (vector,) * 3
    return jax.shard_map(
        on_device, mesh=mesh, in_specs=in_specs, out_specs=out_specs, check_vma=False
    )
```

```python
import functools
import types

import jax
import jax.numpy as jnp
import numpy as np
from jax import lax
from jax.experimental import pallas as pl
from jax.experimental.pallas import tpu as pltpu
from jax.sharding import PartitionSpec as P

HD = 64
FREQS = 32
PE = 128
PAGE = 512
STEP = 10

NORM_EPS = 1e-12
CLIP_LIMIT = 0.1
BETA_ONE = 0.9
BETA_TWO = 0.999
ADAM_EPS = 1e-08
RATE_MATRIX = 0.05
RATE_VECTOR = 0.5
WEIGHT_DECAY = 0.01

F32 = jnp.float32
BF16 = jnp.bfloat16
VMEM_LIMIT = 60 * 1024 * 1024

NN = (((1,), (0,)), ((), ()))
NT = (((1,), (1,)), ((), ()))
TN = (((0,), (0,)), ((), ()))


def dot(lhs, rhs, dims=NN):
    return lax.dot_general(lhs, rhs, dims, preferred_element_type=F32)


def aligned(index, size):
    return pl.ds(pl.multiple_of(index * size, size), size)


def swap_blocks(feat):
    return jnp.concatenate(
        [
            feat[FREQS : 2 * FREQS],
            feat[0:FREQS],
            feat[3 * FREQS :],
            feat[2 * FREQS : 3 * FREQS],
        ],
        axis=0,
    )


def turn_factors(trig):
    cos_x, sin_x = trig[0:FREQS], trig[FREQS : 2 * FREQS]
    cos_y, sin_y = trig[2 * FREQS : 3 * FREQS], trig[3 * FREQS :]
    return (
        jnp.concatenate([sin_x, sin_x, sin_y, sin_y], axis=0),
        jnp.concatenate([cos_x, -cos_x, cos_y, -cos_y], axis=0),
    )


MESH = pl.DeviceIdType.MESH
ALL = slice(None)
UNIT = 384


class Place:
    def __init__(self):
        rank = lax.axis_index("dp")
        self.m = lax.axis_index("mp")
        self.z = rank // 4
        self.y = (rank // 2) % 2
        self.c = rank % 2
        self.peer = {
            "x": (rank, 1 - self.m),
            "y": (rank + 2 - 4 * self.y, self.m),
            "c": (rank + 1 - 2 * self.c, self.m),
        }
        self.far = [((rank + 4 * step) % 16, self.m) for step in (1, 2, 3)]

    def signal(self):
        barrier = pltpu.get_barrier_semaphore()
        for device in list(self.peer.values()) + self.far:
            pl.semaphore_signal(barrier, inc=1, device_id=device, device_id_type=MESH)

    def wait(self):
        pl.semaphore_wait(pltpu.get_barrier_semaphore(), 6)

    def signal_all(self):
        barrier = pltpu.get_barrier_semaphore()
        rank = self.m * 16 + lax.axis_index("dp")

        def one(step, carry):
            to = (rank + step) % 32
            pl.semaphore_signal(barrier, inc=1, device_id=(to % 16, to // 16), device_id_type=MESH)
            return carry

        lax.fori_loop(1, 32, one, 0)

    def wait_all(self):
        pl.semaphore_wait(pltpu.get_barrier_semaphore(), 31)


def remote(src, dst, send_sem, recv_sem, device):
    return pltpu.make_async_remote_copy(
        src_ref=src,
        dst_ref=dst,
        send_sem=send_sem,
        recv_sem=recv_sem,
        device_id=device,
        device_id_type=MESH,
    )


SLOT = {"c": 0, "z": 1, "y": 4, "x": 5}
SLOTS = 6


class Tree:
    def stage(self, index, chunk):
        raise NotImplementedError

    def event(self, number):
        for index in range(self.count - 1, -1, -1):
            chunk = number - index
            if self.chunks == 1:
                pl.when(chunk == 0)(lambda index=index: self.stage(index, 0))
            else:
                pl.when((chunk >= 0) & (chunk < self.chunks))(
                    lambda index=index, chunk=chunk: self.stage(index, chunk)
                )

    @property
    def events(self):
        return self.chunks + self.count - 1


class Spread(Tree):
    def __init__(self, place, ref, chunks, order, sems):
        self.chunks, self.ref, self.sems = chunks, ref, sems
        have = {"x": place.m if "x" in order else 0, "z": place.z, "y": place.y, "c": place.c}
        mine = {"x": place.m, "y": place.y, "c": place.c}
        self.steps = []
        for axis in order:
            if axis == "z":
                sends = [(have, place.far[step - 1], step) for step in (1, 2, 3)]
                waits = [(dict(have, z=(place.z + 4 - step) % 4), step) for step in (1, 2, 3)]
            else:
                sends = [(have, place.peer[axis], SLOT[axis])]
                waits = [(dict(have, **{axis: 1 - mine[axis]}), SLOT[axis])]
                if axis == "c" and have["z"] == ALL:
                    sends = [(dict(have, z=z), place.peer[axis], SLOT[axis]) for z in range(4)]
            self.steps.append((sends, waits, sends[0][0] if len(sends) < 4 else have))
            have = dict(have, **{axis: ALL})
        self.some = place.peer["c"]
        self.count = len(self.steps) + 1

    def _copy(self, chunk, have, device, slot):
        block = self.ref.at[chunk, have["x"], have["z"], have["y"], have["c"]]
        return remote(block, block, self.sems.at[0, chunk, slot], self.sems.at[1, chunk, slot], device)

    def stage(self, index, chunk):
        if index > 0:
            for have, slot in self.steps[index - 1][1]:
                self._copy(chunk, have, self.some, slot).wait_recv()
        if index < self.count - 1:
            for have, device, slot in self.steps[index][0]:
                self._copy(chunk, have, device, slot).start()

    def drain(self):
        def one(chunk, carry):
            for sends, _, whole in self.steps:
                if len(sends) == 4:
                    self._copy(chunk, whole, self.some, sends[0][2]).wait_send()
                else:
                    for have, device, slot in sends:
                        self._copy(chunk, have, device, slot).wait_send()
            return carry

        lax.fori_loop(0, self.chunks, one, 0)


class Reduce(Tree):
    def __init__(self, place, full, total, lands, chunks, order, sems, finish):
        self.place, self.full, self.total, self.lands = place, full, total, lands
        self.chunks, self.sems, self.finish = chunks, sems, finish
        mine = {"x": place.m, "y": place.y}
        self.across = ALL if "x" in order else 0
        have = {"x": self.across, "z": ALL, "y": ALL}
        self.order, self.haves = order, []
        for axis in order:
            before = have
            if axis != "c":
                have = dict(have, **{axis: place.z if axis == "z" else mine[axis]})
            self.haves.append((before, have))
        self.count = len(order) + 1

    def _at(self, chunk, have):
        if self.total is None:
            return self.full.at[chunk, have["x"], have["z"], have["y"], self.place.c]
        return self.total.at[chunk, have["x"], have["z"], have["y"]]

    def _copies(self, index, chunk, start=False):
        axis, (before, _) = self.order[index], self.haves[index]
        place, land = self.place, self.lands[axis]

        def copy(src, dst, slot, device):
            return remote(src, dst, self.sems.at[0, chunk, slot], self.sems.at[1, chunk, slot], device)

        if axis == "c":
            other = 1 - place.c
            if start and self.across == ALL:
                return [
                    copy(
                        self.full.at[chunk, :, z, :, other], land.at[chunk, :, z], SLOT[axis], place.peer[axis]
                    )
                    for z in range(4)
                ]
            source = self.full.at[chunk, self.across, :, :, other]
            return [copy(source, land.at[chunk], SLOT[axis], place.peer[axis])]
        if axis == "z":
            return [
                copy(
                    self._at(chunk, dict(before, z=(place.z + step) % 4)),
                    land.at[chunk, step - 1],
                    step,
                    place.far[step - 1],
                )
                for step in (1, 2, 3)
            ]
        other = 1 - (place.m if axis == "x" else place.y)
        source = self._at(chunk, dict(before, **{axis: other}))
        return [copy(source, land.at[chunk], SLOT[axis], place.peer[axis])]

    def stage(self, index, chunk):
        if index > 0:
            axis, (_, have) = self.order[index - 1], self.haves[index - 1]
            land = self.lands[axis]
            for copy in self._copies(index - 1, chunk):
                copy.wait_recv()
            mine = self._at(chunk, have)
            last = index == self.count - 1
            if axis == "z":
                value = mine[...].astype(F32)
                for step in range(3):
                    value += land[chunk, step].astype(F32)
            elif last:
                value = mine[...].astype(F32) + land[chunk].astype(F32)
            else:
                value = mine[...] + land[chunk]
            if last:
                self.finish(chunk, value)
            else:
                mine[...] = value.astype(mine.dtype)
        if index < self.count - 1:
            for copy in self._copies(index, chunk, True):
                copy.start()

    def drain(self):
        def one(chunk, carry):
            for index in range(self.count - 1):
                for copy in self._copies(index, chunk):
                    copy.wait_send()
            return carry

        lax.fori_loop(0, self.chunks, one, 0)


class Everyone:
    def __init__(self, place, send_block, land_block, sems):
        self.rank = place.m * 16 + lax.axis_index("dp")
        self.send_block, self.land_block, self.sems = send_block, land_block, sems

    def _copy(self, step):
        to = (self.rank + step) % 32
        return remote(
            self.send_block(to),
            self.land_block(step),
            self.sems.at[0, step - 1],
            self.sems.at[1, step - 1],
            (to % 16, to // 16),
        )

    def _each(self, act):
        def one(step, carry):
            act(self._copy(step))
            return carry

        lax.fori_loop(1, 32, one, 0)

    def start(self):
        self._each(lambda copy: copy.start())

    def wait(self):
        self._each(lambda copy: copy.wait())


VROWS = 16


def rows_from_blocks(blocks, pick, counts):
    mp_count, dp_count = counts
    width = pick.shape[1]
    each = width // (mp_count * dp_count)
    wide = lax.dot_general(
        blocks, pick, NN, precision=lax.Precision.HIGHEST, preferred_element_type=F32
    )
    lane = lax.broadcasted_iota(jnp.int32, (VROWS, width), 1)
    table = jnp.zeros((VROWS, width), F32)
    for m in range(mp_count):
        for r in range(dp_count):
            first = (r * mp_count + m) * each
            row = (m * dp_count + r) * VROWS
            table += jnp.where((lane >= first) & (lane < first + each), wide[row : row + VROWS], 0.0)
    return table


def attend_setup(heads, m, box_full, vec_ref, box_heads, bias):
    cols = heads * HD
    for head in range(heads):
        box_heads[head] = box_full[:, head * HD : (head + 1) * HD]
    width = vec_ref.shape[1]
    own = jnp.where(m == 0, vec_ref[6:8, 0:cols], vec_ref[6:8, width - cols :])
    spread = exact_dot(jnp.broadcast_to(own[1:2], (8, cols)), pair_place(cols))
    bias[0:1, 0:cols] = own[0:1]
    bias[0:1, cols:] = spread[0:1]


def attend_trig(omega_ref, corner_ref, trig_ref):
    corner = corner_ref[...].astype(F32)
    angle_x = omega_ref[...] * ((corner[0:1] + corner[2:3]) * 0.5)
    angle_y = omega_ref[...] * ((corner[1:2] + corner[3:4]) * 0.5)
    trig_ref[0:FREQS, :] = jnp.cos(angle_x)
    trig_ref[FREQS : 2 * FREQS, :] = jnp.sin(angle_x)
    trig_ref[2 * FREQS : 3 * FREQS, :] = jnp.cos(angle_y)
    trig_ref[3 * FREQS :, :] = jnp.sin(angle_y)


def quiet(*args):
    return None


def attend_math(heads, r, weights, page_of, projected, attended):
    cols = heads * HD
    pages = r.x.shape[0] // PAGE

    def project(page, carry):
        rows = aligned(page, PAGE)
        tokens = r.x[rows, :]
        query = dot(tokens, weights(0)) + r.bias[0:1, 0:cols]
        query = query.astype(BF16) * HD ** (-0.5)
        r.qtok[rows, :] = query
        qa_rows = query.T
        for half in range(2):
            lanes = slice(half * cols, (half + 1) * cols)
            pair = dot(tokens, weights(1 + half)) + r.bias[0:1, cols + half * cols : 2 * cols + half * cols]
            pair = pair.astype(BF16)
            r.kvtok[rows, lanes] = pair
            turned = pair.T
            for spot in range(heads // 2):
                head_rows = slice((half * heads // 2 + spot) * HD, (half * heads // 2 + spot + 1) * HD)
                r.kt[head_rows, rows] = turned[2 * spot * HD : (2 * spot + 1) * HD]
                r.vt[head_rows, rows] = turned[(2 * spot + 1) * HD : (2 * spot + 2) * HD]
        trig = r.trig[:, rows]
        kft = trig.astype(BF16)
        r.kft[:, rows] = kft
        r.kftok[rows, :] = kft.T
        own, partner = turn_factors(trig)
        for head in range(heads):
            query_head = qa_rows[head * HD : (head + 1) * HD]
            proj = dot(r.box_heads[head], query_head)
            feat = proj * own + swap_blocks(proj) * partner
            r.qa[head, 0:PE, rows] = feat.astype(BF16)
            r.qa[head, PE : PE + HD, rows] = query_head
        projected(page)
        return carry

    lax.fori_loop(0, pages, project, 0)

    def attend(step, carry):
        turn, pair = step // (heads // 2), step % (heads // 2)
        rows = aligned(page_of(turn), PAGE)
        halves = []
        blank = jnp.zeros((HD, PAGE), BF16)
        for side in range(2):
            head = pair * 2 + side
            lanes = aligned(head, 2 * HD)
            left = jnp.concatenate([r.kftok[rows, :], r.kvtok[rows, lanes]], axis=1)
            score = dot(left, jnp.concatenate([r.qa[head, :, rows], blank], axis=0))
            top = jnp.max(score, axis=0, keepdims=True)
            weight = jnp.exp(score - top)
            total = jnp.sum(weight, axis=0, keepdims=True)
            value = r.vt[aligned(head, HD), rows]
            halves.append(dot(value, weight.astype(BF16)) * (1.0 / total))
            r.log[head, :, rows] = top + jnp.log(total)
        both = jnp.concatenate(halves, axis=0).astype(BF16)
        lanes = aligned(pair, 2 * HD)
        r.ctxt[lanes, rows] = both
        r.ctx[rows, lanes] = both.T
        attended(step, turn, pair)
        return carry

    lax.fori_loop(0, pages * (heads // 2), attend, 0)


def attend_buffers(heads, tokens):
    cols = heads * HD
    kept = [
        ("qa", (heads, PE + HD, tokens), BF16),
        ("qtok", (tokens, cols), BF16),
        ("kvtok", (tokens, 2 * cols), BF16),
        ("kt", (cols, tokens), BF16),
        ("kft", (PE, tokens), BF16),
        ("trig", (PE, tokens), F32),
        ("ctxt", (cols, tokens), BF16),
        ("log", (heads, 1, tokens), F32),
    ]
    used = [
        ("kftok", (tokens, PE), BF16),
        ("box_heads", (heads, PE, HD), BF16),
        ("bias", (8, 3 * cols), F32),
        ("ctx", (tokens, cols), BF16),
        ("vt", (cols, tokens), BF16),
    ]
    return kept, used


def attend_kernel(heads, names, *refs):
    r = types.SimpleNamespace(**dict(zip(names, refs)))
    attend_setup(heads, lax.axis_index("mp"), r.box, r.vec, r.box_heads, r.bias)
    attend_trig(r.omega, r.corner, r.trig)
    attend_math(heads, r, lambda chunk: r.w[chunk], lambda turn: turn, quiet, quiet)


def attend_forward(x, corners, omega, w_qkv, w_box, vecs):
    tokens = x.shape[0]
    heads = w_box.shape[1] // HD
    kept, used = attend_buffers(heads, tokens)
    outs = kept + [used[3]]
    scratch = used[:3] + used[4:]
    names = ["x", "corner", "omega", "w", "box", "vec"] + [item[0] for item in outs + scratch]
    vmem = pl.BlockSpec(memory_space=pltpu.VMEM)
    return pl.pallas_call(
        functools.partial(attend_kernel, heads, names),
        out_shape=[jax.ShapeDtypeStruct(shape, kind) for _, shape, kind in outs],
        in_specs=[vmem] * 6,
        out_specs=[vmem] * len(outs),
        scratch_shapes=[pltpu.VMEM(shape, kind) for _, shape, kind in scratch],
        compiler_params=pltpu.CompilerParams(vmem_limit_bytes=VMEM_LIMIT),
        name="attend_forward",
    )(x, corners, omega, w_qkv, w_box, vecs)


TILE = 256


def norm_stats(value):
    mean = jnp.mean(value, axis=-1, keepdims=True)
    centred = value - mean
    var = jnp.mean(centred * centred, axis=-1, keepdims=True)
    return centred, lax.rsqrt(var + NORM_EPS)


def norm_back(grad_normed, normed, scale):
    first = jnp.mean(grad_normed, axis=-1, keepdims=True)
    second = jnp.mean(grad_normed * normed, axis=-1, keepdims=True)
    return scale * (grad_normed - first - normed * second)


def col_sum(value):
    return jnp.sum(value, axis=0, keepdims=True)


def feed_math(r, hooks):
    hook = {name: quiet for name in ("entered", "grew", "turned", "shrinks", "shrank", "left")}
    hook.update(hooks)
    tokens = r.x.shape[0]
    sides = r.we.shape[1]
    per_side = (r.we.shape[0] - 1) // 2
    steps = sides * per_side
    tiles = tokens // TILE
    wide = 2 * UNIT
    sum2 = dnorm = r.sum2

    def flat(ref, chunk, side):
        return ref[chunk, side].reshape(-1, UNIT)

    def two(ref, first, side):
        return jnp.concatenate([flat(ref, first, side), flat(ref, first + 1, side)], axis=1)

    def w_expand(step):
        return two(r.we, 1 + 2 * (step % per_side), step // per_side)

    def w_shrink(step):
        return two(r.ws, 2 * (step % per_side), step // per_side)

    def put_two(ref, first, side, value):
        shape = ref.shape[2:]
        ref[first, side] = value[:, 0:UNIT].reshape(shape)
        ref[first + 1, side] = value[:, UNIT:].reshape(shape)

    def by_halves(number):
        return (number % sides) * per_side + number // sides

    def enter(tile, carry):
        rows = aligned(tile, TILE)
        total = r.x[rows, :].astype(F32) + r.vec[4:5, :]
        for side in range(sides):
            total += dot(r.ctxx[side, rows, :], flat(r.we, 0, side), NT)
        centred, scale = norm_stats(total)
        normed = centred * scale
        r.norm1[rows, :] = normed
        r.scale1[rows, :] = scale
        shifted = normed * r.vec[0:1, :] + r.vec[1:2, :]
        r.al[rows, :] = shifted.astype(BF16)
        sum2[rows, :] = shifted + r.vec[5:6, :]
        return carry

    lax.fori_loop(0, tiles, enter, 0)
    hook["entered"]()

    def grow(number, carry):
        step = by_halves(number)
        whole = aligned(step, wide)

        def one(tile, inner):
            rows = aligned(tile, TILE)
            pre = dot(r.al[rows, :], w_expand(step)) + r.vec[pl.ds(8 + step, 1), :]
            phi = 0.5 + 0.5 * lax.erf(pre * 2.0 ** (-0.5))
            density = jnp.exp(pre * pre * -0.5) * (0.5 / jnp.pi) ** 0.5
            low = (pre * phi).astype(BF16)
            r.act[rows, whole] = low
            r.slope[rows, whole] = (phi + pre * density).astype(BF16)
            sum2[rows, :] += dot(low, w_shrink(step), NT)
            hook["grew"](number * tiles + tile)
            return inner

        lax.fori_loop(0, tiles, one, 0)
        return carry

    lax.fori_loop(0, steps, grow, 0)
    r.vsum[...] = jnp.zeros_like(r.vsum)

    def turn(tile, carry):
        rows = aligned(tile, TILE)
        centred, scale = norm_stats(sum2[rows, :])
        normed = centred * scale
        r.out[rows, :] = (normed * r.vec[2:3, :] + r.vec[3:4, :]).astype(BF16)
        grad = r.og[rows, :].astype(F32)
        r.vsum[2:3, :] += col_sum(grad * normed)
        r.vsum[3:4, :] += col_sum(grad)
        back = norm_back(grad * r.vec[2:3, :], normed, scale)
        r.vsum[5:6, :] += col_sum(back)
        r.dh2l[rows, :] = back.astype(BF16)
        dnorm[rows, :] = back
        hook["turned"](tile)
        return carry

    lax.fori_loop(0, tiles, turn, 0)
    r.flip[...] = r.dh2l[...].T

    def grad_shrink(number, carry):
        step = by_halves(number)
        grad = dot(r.flip[...], r.act[:, aligned(step, wide)]).astype(BF16)
        put_two(r.gs, 2 * (number // sides), number % sides, grad)
        hook["shrinks"](number)
        return carry

    lax.fori_loop(0, steps, grad_shrink, 0)

    def shrink(number, carry):
        step = by_halves(number)
        whole = aligned(step, wide)

        def one(tile, inner):
            rows = aligned(tile, TILE)
            grad = dot(r.dh2l[rows, :], w_shrink(step))
            low = (grad * r.slope[rows, whole].astype(F32)).astype(BF16)
            r.slope[rows, whole] = low
            r.vsum[pl.ds(8 + step, 1), :] += col_sum(low.astype(F32))
            dnorm[rows, :] += dot(low, w_expand(step), NT)
            hook["shrank"](number * tiles + tile)
            return inner

        lax.fori_loop(0, tiles, one, 0)
        return carry

    lax.fori_loop(0, steps, shrink, 0)

    def leave(tile, carry):
        rows = aligned(tile, TILE)
        grad = dnorm[rows, :]
        normed = r.norm1[rows, :]
        r.vsum[0:1, :] += col_sum(grad * normed)
        r.vsum[1:2, :] += col_sum(grad)
        back = norm_back(grad * r.vec[0:1, :], normed, r.scale1[rows, :])
        r.vsum[4:5, :] += col_sum(back)
        low = back.astype(BF16)
        r.dh1l[rows, :] = low
        for side in range(sides):
            r.dctx[side, rows, :] = dot(low, flat(r.we, 0, side)).astype(BF16)
        hook["left"](tile)
        return carry

    lax.fori_loop(0, tiles, leave, 0)
    r.flip[...] = r.al[...].T

    def grad_expand(number, carry):
        step = by_halves(number)
        grad = dot(r.flip[...], r.slope[:, aligned(step, wide)]).astype(BF16)
        put_two(r.ge, 1 + 2 * (number // sides), number % sides, grad)
        return carry

    lax.fori_loop(0, steps, grad_expand, 0)
    r.flip[...] = r.dh1l[...].T
    for side in range(sides):
        r.ge[0, side] = dot(r.flip[...], r.ctxx[side]).astype(BF16).reshape(r.ge.shape[2:])


def feed_buffers(tokens, width, hidden):
    return [
        ("norm1", (tokens, width), F32),
        ("scale1", (tokens, 1), F32),
        ("sum2", (tokens, width), F32),
        ("al", (tokens, width), BF16),
        ("act", (tokens, hidden), BF16),
        ("slope", (tokens, hidden), BF16),
        ("dh2l", (tokens, width), BF16),
        ("flip", (width, tokens), BF16),
    ]


def feed_kernel(names, *refs):
    feed_math(types.SimpleNamespace(**dict(zip(names, refs))), {})


def feed_both(x, og, ctx, w_expand, w_shrink, vecs):
    tokens, width = x.shape
    chunks, sides = w_shrink.shape[0:2]
    outs = [
        ("out", (tokens, width), BF16),
        ("dctx", (sides, tokens, UNIT), BF16),
        ("dh1l", (tokens, width), BF16),
        ("ge", (chunks + 1, sides, width, UNIT), BF16),
        ("gs", (chunks, sides, width, UNIT), BF16),
        ("vsum", (VROWS, width), F32),
    ]
    scratch = feed_buffers(tokens, width, sides * chunks * UNIT)
    names = ["x", "og", "ctxx", "we", "ws", "vec"] + [item[0] for item in outs + scratch]
    vmem = pl.BlockSpec(memory_space=pltpu.VMEM)
    return pl.pallas_call(
        functools.partial(feed_kernel, names),
        out_shape=[jax.ShapeDtypeStruct(shape, kind) for _, shape, kind in outs],
        in_specs=[vmem] * 6,
        out_specs=[vmem] * len(outs),
        scratch_shapes=[pltpu.VMEM(shape, kind) for _, shape, kind in scratch],
        compiler_params=pltpu.CompilerParams(vmem_limit_bytes=VMEM_LIMIT),
        name="feed_both",
    )(x, og, ctx, w_expand, w_shrink, vecs)


def layer_kernel(heads, plan, inv_tokens, names, kept, used, feeds, *refs):
    r = types.SimpleNamespace(**dict(zip(names, refs)))
    cols = heads * HD
    tokens = r.x_all.shape[0]
    pages = tokens // PAGE
    own_tokens = tokens // 2
    tiles = own_tokens // TILE
    place = Place()
    place.signal()
    m, peer = place.m, place.peer["x"]
    at = (place.z, place.y, place.c)
    own = aligned(m, own_tokens)
    load_x = pltpu.make_async_copy(r.x_all.at[own, :], r.x, r.load_sem.at[0])
    load_og = pltpu.make_async_copy(r.og_all.at[own, :], r.og, r.load_sem.at[1])
    load_x.start()
    load_og.start()
    r.w[(0, 0, *at)] = r.attn[0].astype(BF16)
    for half in range(2):
        r.w[(1 + half, 0, *at)] = jnp.concatenate(
            [
                r.attn[1 + kind, :, head * HD : (head + 1) * HD].astype(BF16)
                for head in range(half * heads // 2, (half + 1) * heads // 2)
                for kind in range(2)
            ],
            axis=1,
        )
    r.box_gather[(0, 0, *at)] = r.shard_box[...]
    r.vec_gather[(0, m, *at)] = jnp.zeros((VROWS, 128), F32)
    table_at = (slice(0, r.vectors.shape[0]), slice(0, r.vectors.shape[1]))
    r.vec_gather[(0, m, *at, *table_at)] = r.vectors[...]
    r.we[(0, m, *at)] = r.merge[...].astype(BF16)
    for chunk in range(4):
        lanes = slice(chunk * UNIT, (chunk + 1) * UNIT)
        r.we[(1 + chunk, m, *at)] = r.expand[:, lanes].astype(BF16)
        r.ws[(chunk, m, *at)] = r.shrink[:, lanes].astype(BF16)
    place.wait()
    tree_v = Spread(place, r.vec_gather, 1, "xzyc", r.v_sem)
    tree_b = Spread(place, r.box_gather, 1, "zyc", r.b_sem)
    tree_a = Spread(place, r.w, 3, "zyc", r.a_sem)
    tree_e = Spread(place, r.we, 5, "zyxc", r.e_sem)
    tree_f = Spread(place, r.ws, 4, "xzyc", r.f_sem)
    late = 3
    first = tree_a.events

    def weights_event(number):
        tree_e.event(number)
        tree_f.event(number)

    def finish(chunk, value):
        r.sum_f[chunk] = value * inv_tokens

    back_f = Reduce(
        place, r.gs, None, dict(c=r.fc, y=r.fy, z=r.fz, x=r.fx), 4, "cyzx", r.back_sem, finish
    )

    def attention(*scoped):
        q = types.SimpleNamespace(**dict(zip([item[0] for item in kept + used] + ["x"], scoped)))
        load_all = pltpu.make_async_copy(r.x_all, q.x, r.load_sem.at[2])
        load_all.start()

        def begin(number, carry):
            tree_a.event(number)
            tree_b.event(number)
            tree_v.event(number)
            weights_event(number - late)
            pl.when(number == 1)(lambda: attend_trig(r.omega, r.corner, q.trig))

            @pl.when(number == 4)
            def _():
                r.vec[...] = rows_from_blocks(
                    r.vec_gather[...].reshape(-1, 128), r.pick[...], plan
                )
                r.box_out[...] = r.box_gather[...].reshape(PE, cols).astype(BF16)
                attend_setup(heads, m, r.box_out, r.vec, q.box_heads, q.bias)

            return carry

        lax.fori_loop(0, first, begin, 0)
        keep_w = pltpu.make_async_copy(r.w, r.w_out, r.load_sem.at[3])
        keep_w.start()
        load_all.wait()

        def projected(page):
            pl.when(page == 1)(lambda: weights_event(first - late))

        piece = PAGE // 2

        def swap_copy(index):
            theirs = pages * (1 - m) + index
            return remote(
                q.ctx.at[aligned(theirs, piece), :],
                r.ctxx.at[m, aligned(index, piece), :],
                r.ctx_sem.at[0, index],
                r.ctx_sem.at[1, index],
                peer,
            )

        def attended(step, turn, pair):
            for spot, number in ((1, 1), (4, 2), (7, 3)):
                pl.when(step == spot)(lambda number=number: weights_event(first - late + number))

            @pl.when(step == heads // 2 - 1)
            def _():
                swap_copy(2 - 2 * m).start()
                swap_copy(1).start()

            @pl.when(step == heads - 1)
            def _():
                swap_copy(2 * m).start()

        attend_math(
            heads,
            q,
            lambda chunk: r.w[chunk].reshape(-1, cols),
            lambda turn: turn * m + (pages - 1 - turn) * (1 - m),
            projected,
            attended,
        )
        stores = [
            pltpu.make_async_copy(getattr(q, name), getattr(r, name + "_out"), r.store_sem.at[k])
            for k, (name, _, _) in enumerate(kept)
        ]
        for copy in stores:
            copy.start()
        r.ctxx[m] = q.ctx[own, :]
        for index in range(pages):
            copy = remote(
                q.ctx.at[aligned(index, piece), :],
                r.ctxx.at[1 - m, aligned(index, piece), :],
                r.ctx_sem.at[0, index],
                r.ctx_sem.at[1, index],
                peer,
            )
            copy.wait_recv()
            copy.wait_send()
        for copy in stores:
            copy.wait()
        keep_w.wait()

    pl.run_scoped(
        attention,
        *[pltpu.VMEM(shape, kind) for _, shape, kind in kept + used],
        pltpu.VMEM(r.x_all.shape, BF16),
    )

    def feed(*scoped):
        q = types.SimpleNamespace(**dict(zip([item[0] for item in feeds], scoped)))
        for name in ("x", "og", "we", "ws", "vec", "ctxx", "dh1l", "ge", "gs", "vsum"):
            setattr(q, name, getattr(r, name))

        def out_copies(tile):
            rows = aligned(tile, TILE)
            there = r.out_full.at[pl.ds(pl.multiple_of(m * own_tokens + tile * TILE, TILE), TILE), :]
            return (
                pltpu.make_async_copy(q.out.at[rows, :], there, r.swap_sem.at[0, tile]),
                remote(q.out.at[rows, :], there, r.swap_sem.at[1, tile], r.swap_sem.at[2, tile], peer),
            )

        def dctx_copies(tile):
            rows = aligned(tile, TILE)
            there = r.dctx_full.at[pl.ds(pl.multiple_of(m * own_tokens + tile * TILE, TILE), TILE), :]
            return (
                pltpu.make_async_copy(q.dctx.at[m, rows, :], there, r.swap_sem.at[3, tile]),
                remote(
                    q.dctx.at[1 - m, rows, :], there, r.swap_sem.at[4, tile], r.swap_sem.at[5, tile], peer
                ),
            )

        def start(copies):
            for copy in copies:
                copy.start()

        def grew(number):
            pl.when(number == 2)(lambda: weights_event(first - late + 5))

        def shrinks(number):
            pl.when(number % 2 == 1)(lambda: back_f.event(number // 2))

        def shrank(number):
            pl.when(number % 2 == 1)(lambda: back_f.event(2 + number // 2))

        def left(tile):
            start(dctx_copies(tile))
            back_f.event(8 + tile)

        load_x.wait()
        load_og.wait()
        feed_math(
            q,
            dict(
                entered=lambda: weights_event(first - late + 4),
                grew=grew,
                turned=lambda tile: start(out_copies(tile)),
                shrinks=shrinks,
                shrank=shrank,
                left=left,
            ),
        )
        back_f.drain()
        for tile in range(tiles):
            for copy in out_copies(tile) + dctx_copies(tile):
                copy.wait()

    pl.run_scoped(feed, *[pltpu.VMEM(shape, kind) for _, shape, kind in feeds])
    for tree in (tree_v, tree_b, tree_a, tree_e, tree_f):
        tree.drain()


def layer_forward(x, og, corners, omega, pick, shards, plan, inv_tokens):
    tokens, width = x.shape
    cols = shards[1].shape[1]
    heads = cols // HD
    own = tokens // 2
    unit = (width // 16, UNIT)
    kept, used = attend_buffers(heads, tokens)
    feeds = feed_buffers(own, width, 8 * UNIT)
    feeds += [("out", (own, width), BF16), ("dctx", (2, own, UNIT), BF16)]
    free = pl.BlockSpec(memory_space=pl.ANY)
    vmem = pl.BlockSpec(memory_space=pltpu.VMEM)
    inputs = [("x_all", free), ("og_all", free), ("corner", vmem), ("omega", vmem), ("pick", vmem)]
    inputs += [(name, vmem) for name in ("attn", "shard_box", "vectors", "merge", "expand", "shrink")]
    outs = [(name + "_out", shape, kind, free) for name, shape, kind in kept]
    outs += [
        ("w_out", (3, 1, 4, 2, 2, *unit), BF16, free),
        ("box_out", (PE, cols), BF16, vmem),
        ("out_full", (tokens, width), BF16, free),
        ("dctx_full", (tokens, cols), BF16, free),
        ("dh1l", (own, width), BF16, vmem),
        ("ge", (5, 2, 4, 2, 2, *unit), BF16, vmem),
        ("vsum", (VROWS, width), F32, vmem),
        ("sum_f", (4, *unit), F32, vmem),
    ]
    dma = pltpu.SemaphoreType.DMA
    scratch = [
        ("x", pltpu.VMEM((own, width), BF16)),
        ("og", pltpu.VMEM((own, width), BF16)),
        ("vec", pltpu.VMEM((VROWS, width), F32)),
        ("w", pltpu.VMEM((3, 1, 4, 2, 2, *unit), BF16)),
        ("box_gather", pltpu.VMEM((1, 1, 4, 2, 2, PE // 16, cols), F32)),
        ("vec_gather", pltpu.VMEM((1, 2, 4, 2, 2, VROWS, 128), F32)),
        ("we", pltpu.VMEM((5, 2, 4, 2, 2, *unit), BF16)),
        ("ws", pltpu.VMEM((4, 2, 4, 2, 2, *unit), BF16)),
        ("ctxx", pltpu.VMEM((2, own, cols), BF16)),
        ("gs", pltpu.VMEM((4, 2, 4, 2, 2, *unit), BF16)),
        ("fc", pltpu.VMEM((4, 2, 4, 2, *unit), BF16)),
        ("fy", pltpu.VMEM((4, 2, 4, *unit), BF16)),
        ("fz", pltpu.VMEM((4, 3, 2, *unit), BF16)),
        ("fx", pltpu.VMEM((4, *unit), BF16)),
        ("ctx_sem", dma((2, 3))),
        ("a_sem", dma((2, 3, SLOTS))),
        ("b_sem", dma((2, 1, SLOTS))),
        ("v_sem", dma((2, 1, SLOTS))),
        ("e_sem", dma((2, 5, SLOTS))),
        ("f_sem", dma((2, 4, SLOTS))),
        ("back_sem", dma((2, 4, SLOTS))),
        ("load_sem", dma((4,))),
        ("store_sem", dma((len(kept),))),
        ("swap_sem", dma((6, own // TILE))),
    ]
    names = [item[0] for item in inputs + outs + scratch]
    return pl.pallas_call(
        functools.partial(layer_kernel, heads, plan, inv_tokens, names, kept, used, feeds),
        out_shape=[jax.ShapeDtypeStruct(shape, kind) for _, shape, kind, _ in outs],
        in_specs=[item[1] for item in inputs],
        out_specs=[item[3] for item in outs],
        scratch_shapes=[item[1] for item in scratch],
        compiler_params=pltpu.CompilerParams(
            vmem_limit_bytes=VMEM_LIMIT, collective_id=0, has_side_effects=True
        ),
        name="layer_forward",
    )(x, og, corners, omega, pick, *shards)


def pair_place(cols):
    spot = lax.broadcasted_iota(jnp.int32, (cols, 2 * cols), 0)
    lane = lax.broadcasted_iota(jnp.int32, (cols, 2 * cols), 1)
    target = ((spot >> 6) << 7) + HD + (spot & (HD - 1))
    return jnp.where(lane == target, 1.0, 0.0)


def exact_dot(lhs, rhs, dims=NN):
    return lax.dot_general(
        lhs, rhs, dims, precision=lax.Precision.HIGHEST, preferred_element_type=F32
    )


def attend_back_kernel(heads, plan, inv_tokens, *refs):
    inputs, refs = refs[:12], refs[12:]
    if plan is not None:
        load_sem, held, refs = refs[-1], refs[-13:-1], refs[:-13]
        loads = [
            pltpu.make_async_copy(src, dst, load_sem.at[k]) for k, (src, dst) in enumerate(zip(inputs, held))
        ]
        early = (0, 2, 7, 11)
        for k in sorted(range(12), key=lambda k: k not in early):
            loads[k].start()
        inputs = held
    x_ref, w_ref, box_ref, *inputs = inputs
    qa_ref, qtok_ref, kvtok_ref, kt_ref, kft_ref, trig_ref, ctxt_ref, log_ref, dctx_ref = inputs
    cols = heads * HD
    tokens = x_ref.shape[0]
    pages = tokens // PAGE
    m = lax.axis_index("mp")
    piece = PAGE // 2
    pieces = 2 * pages
    lane = lax.broadcasted_iota(jnp.int32, (1, 2 * HD), 1)
    lower = lane < HD
    if plan is None:
        inp_ref, gw_ref, gbox_ref, qvsum_ref, *refs = refs
        kftok, dctxt, boxt, dtok, xt, gbox = refs
        before, after = 0, 0

        def background(number):
            pass
    else:
        dh1_ref, vsum_ref, sumf_ref, pick_ref, full_e, *refs = refs
        inp_ref, sum_e, sum_a, sum_b, sum_v, norm_ref, *refs = refs
        kftok, dctxt, boxt, dtok, xt, gbox, *refs = refs
        came, total_e, full_a, full_b, full_v, land_v, norms, *refs = refs
        ec, ey, ez, ex, ac, ay, az, bc, by, bz, *refs = refs
        e_sem, a_sem, b_sem, v_sem, n_sem, i_sem, loc_sem = refs
        place = Place()
        place.signal_all()
        fill = pltpu.make_async_copy(full_e.at[:, :, :, :, place.c], total_e, loc_sem.at[0])
        fill.start()
        place.wait_all()

        def finish(out):
            def put(chunk, value):
                out[chunk] = value * inv_tokens

            return put

        tree_e = Reduce(
            place, full_e, total_e, dict(c=ec, y=ey, z=ez, x=ex), 5, "cyzx", e_sem, finish(sum_e)
        )
        tree_a = Reduce(place, full_a, None, dict(c=ac, y=ay, z=az), 3, "cyz", a_sem, finish(sum_a))
        tree_b = Reduce(place, full_b, None, dict(c=bc, y=by, z=bz), 1, "cyz", b_sem, finish(sum_b))

        def block_of(rank):
            r = rank % 16
            return full_v.at[rank // 16, r // 4, (r // 2) % 2, r % 2]

        spot = (place.m, place.z, place.y, place.c)
        all_v = Everyone(place, block_of, lambda step: land_v.at[step - 1], v_sem)
        all_n = Everyone(place, lambda rank: norms.at[spot], lambda step: norms.at[spot], n_sem)

        def background(number):
            tree_e.event(number)

        background(0)
        fill.wait()
        for k in early:
            loads[k].wait()

    boxt[...] = box_ref[...].T
    gbox[...] = jnp.zeros_like(gbox)

    def prepare(page, carry):
        rows = aligned(page, PAGE)
        kftok[rows, :] = kft_ref[:, rows].T
        dctxt[:, rows] = dctx_ref[rows, :].T
        xt[:, rows] = x_ref[rows, :].T
        if plan is not None:
            pl.when(page == pages - 1)(lambda: background(1))
        return carry

    lax.fori_loop(0, pages, prepare, 0)
    if plan is not None:
        for k in range(12):
            if k not in early:
                loads[k].wait()

    def attend(step, carry):
        page, pair = step // (heads // 2), step % (heads // 2)
        rows = aligned(page, PAGE)
        own, partner = turn_factors(trig_ref[:, rows])
        pair_lanes = aligned(pair, 2 * HD)
        query_pair = qtok_ref[rows, pair_lanes]
        dctx_pair = dctx_ref[rows, pair_lanes]
        halves = []
        boxes = []
        blank = jnp.zeros((HD, PAGE), BF16)
        for side in range(2):
            head = pair * 2 + side
            lanes = aligned(head, 2 * HD)
            key_value = kvtok_ref[rows, lanes]
            left = jnp.concatenate([kftok[rows, :], key_value], axis=1)
            score = dot(left, jnp.concatenate([qa_ref[head, :, rows], blank], axis=0))
            prob = jnp.exp(score - log_ref[head, :, rows])
            prob_low = prob.astype(BF16)
            head_rows = pl.ds(pl.multiple_of(head * HD, HD), HD)
            dctx_head = dctxt[head_rows, rows]
            grad_prob = dot(
                key_value, jnp.concatenate([blank, dctx_head], axis=0)
            )
            inner = col_sum(dctx_head.astype(F32) * ctxt_ref[head_rows, rows].astype(F32))
            grad_score = (prob * (grad_prob - inner)).astype(BF16)
            if side == 0:
                both = jnp.concatenate([query_pair[:, 0:HD], dctx_pair[:, 0:HD]], axis=1)
            else:
                both = jnp.concatenate([query_pair[:, HD:], dctx_pair[:, HD:]], axis=1)
            from_score = dot(grad_score, both)
            from_prob = dot(prob_low, both)
            grad_kv = jnp.where(lower, from_score, from_prob).astype(BF16)
            dtok[rows, pl.ds(pl.multiple_of(cols + head * 2 * HD, 2 * HD), 2 * HD)] = grad_kv
            keys = jnp.concatenate([kft_ref[:, rows], kt_ref[head_rows, rows]], axis=0)
            grad_query = dot(keys, grad_score) * HD ** (-0.5)
            feat = grad_query[0:PE]
            proj = (feat * own - swap_blocks(feat) * partner).astype(BF16)
            halves.append(grad_query[PE:] + dot(boxt[head_rows, :], proj))
            boxes.append(dot(proj, query_pair))
        gbox[:, pair_lanes] += jnp.where(lower, boxes[0], boxes[1])
        dtok[rows, pair_lanes] = jnp.concatenate(halves, axis=0).astype(BF16).T
        return carry

    def spread(page):
        rows = aligned(page, PAGE)
        return sum(
            dot(dtok[rows, chunk * UNIT : (chunk + 1) * UNIT], w_ref[chunk], NT) for chunk in range(3)
        )

    if plan is None:
        lax.fori_loop(0, pages * (heads // 2), attend, 0)
        gbox_ref[...] = gbox[...] * HD**0.5

        def spread_page(page, carry):
            inp_ref[aligned(page, PAGE), :] = spread(page)
            return carry

        lax.fori_loop(0, pages, spread_page, 0)

        def gather(step, carry):
            lanes = aligned(step, UNIT)
            gw_ref[step] = dot(xt[...], dtok[:, lanes]).astype(BF16)
            qvsum_ref[0:1, lanes] = col_sum(dtok[:, lanes].astype(F32))
            return carry

        lax.fori_loop(0, 3, gather, 0)
        return

    def swap(index):
        rows = aligned(index, piece)
        return remote(
            inp_ref.at[rows, :], came.at[rows, :], i_sem.at[0, index], i_sem.at[1, index], place.peer["x"]
        )

    def attend_and_send(step, carry):
        attend(step, carry)
        page = step // (heads // 2)

        @pl.when(step % (heads // 2) == heads // 2 - 1)
        def _():
            value = spread(page)
            for half in range(2):
                index = 2 * page + half
                rows = aligned(index, piece)
                own = index // pages == m
                spot = aligned(index % pages, piece)
                extra = jnp.where(own, dh1_ref[spot, :].astype(F32), 0.0)
                inp_ref[rows, :] = (value[half * piece : (half + 1) * piece] + extra).astype(BF16)
                swap(index).start()

        background(step + 2)
        return carry

    lax.fori_loop(0, pages * (heads // 2), attend_and_send, 0)
    full_b[0, 0] = (gbox[...] * HD**0.5).reshape(4, 2, 2, PE // 16, cols)

    def gather(step, carry):
        grad = dot(xt[...], dtok[:, aligned(step, UNIT)]).astype(BF16)
        full_a[step, 0] = grad.reshape(full_a.shape[2:])
        tree_a.event(step)
        tree_b.event(step)
        return carry

    lax.fori_loop(0, 3, gather, 0)

    sums = jnp.concatenate(
        [
            col_sum(dtok[:, chunk * UNIT : (chunk + 1) * UNIT].astype(F32)) for chunk in range(3)
        ],
        axis=1,
    )
    values = exact_dot(jnp.broadcast_to(sums[:, cols:], (8, 2 * cols)), pair_place(cols), NT)
    pair = jnp.concatenate([sums[:, 0:cols], values[0:1]], axis=0)
    blank = jnp.zeros_like(pair)
    pair = jnp.where(
        m == 0, jnp.concatenate([pair, blank], axis=1), jnp.concatenate([blank, pair], axis=1)
    )
    table = jnp.concatenate([vsum_ref[0:6, :], pair, vsum_ref[8:, :]], axis=0)
    mp_count, dp_count = plan
    width = table.shape[1]
    each = width // (mp_count * dp_count)
    wide_lane = lax.broadcasted_iota(jnp.int32, (VROWS, width), 1)
    for side in range(mp_count):
        parts = []
        for r in range(dp_count):
            first = (r * mp_count + side) * each
            parts.append(jnp.where((wide_lane >= first) & (wide_lane < first + each), table, 0.0))
        block = exact_dot(jnp.concatenate(parts, axis=0), pick_ref[...], NT)
        full_v[side] = block.reshape(full_v.shape[1:])
    all_v.start()

    def tail(number, carry):
        tree_a.event(number)
        tree_b.event(number)
        return carry

    lax.fori_loop(3, tree_a.events, tail, 0)
    all_v.wait()
    total_v = full_v[spot] + jnp.sum(land_v[...], axis=0)
    sum_v[0] = total_v * inv_tokens

    square = sum(jnp.sum(out[...] * out[...]) for out in (sum_e, sumf_ref, sum_a, sum_b, sum_v))
    norms[spot] = jnp.full((8, 128), square, F32)
    all_n.start()

    def final(number, carry):
        rows = aligned(number, piece)
        swap(number).wait()
        inp_ref[rows, :] = (inp_ref[rows, :].astype(F32) + came[rows, :].astype(F32)).astype(BF16)
        return carry

    lax.fori_loop(0, pieces, final, 0)
    all_n.wait()
    every = norms[...].reshape(-1, 8, 128)
    norm_ref[...] = jnp.sqrt(sum(every[k] for k in range(every.shape[0])))
    for tree in (tree_e, tree_a, tree_b):
        tree.drain()


def attend_backward(x, weight, box, kept, dctx, plan, inv_tokens, more=()):
    tokens, width = x.shape
    cols = weight.shape[2]
    heads = cols // HD
    vmem = pl.BlockSpec(memory_space=pltpu.VMEM)
    scratch = [
        pltpu.VMEM((tokens, PE), BF16),
        pltpu.VMEM((cols, tokens), BF16),
        pltpu.VMEM((cols, PE), BF16),
        pltpu.VMEM((tokens, 3 * cols), BF16),
        pltpu.VMEM((width, tokens), BF16),
        pltpu.VMEM((PE, cols), F32),
    ]
    in_specs = [vmem] * 12
    if plan is None:
        shapes = [
            ((tokens, width), F32),
            ((3, width, cols), BF16),
            ((PE, cols), F32),
            ((8, 3 * cols), F32),
        ]
        extra = {}
    else:
        free = pl.BlockSpec(memory_space=pl.ANY)
        in_specs = [free] * 12 + [vmem] * 4 + [free]
        rows = width // 16
        unit = (rows, UNIT)
        tile = (PE // 16, cols)
        small = (VROWS, 128)
        shapes = [
            ((tokens, width), BF16),
            ((5, *unit), F32),
            ((3, *unit), F32),
            ((1, *tile), F32),
            ((1, *small), F32),
            ((8, 128), F32),
        ]
        scratch += [
            pltpu.VMEM((tokens, width), BF16),
            pltpu.VMEM((5, 2, 4, 2, *unit), BF16),
            pltpu.VMEM((3, 1, 4, 2, 2, *unit), BF16),
            pltpu.VMEM((1, 1, 4, 2, 2, *tile), F32),
            pltpu.VMEM((2, 4, 2, 2, *small), F32),
            pltpu.VMEM((31, *small), F32),
            pltpu.VMEM((2, 4, 2, 2, 8, 128), F32),
            pltpu.VMEM((5, 2, 4, 2, *unit), BF16),
            pltpu.VMEM((5, 2, 4, *unit), BF16),
            pltpu.VMEM((5, 3, 2, *unit), BF16),
            pltpu.VMEM((5, *unit), BF16),
            pltpu.VMEM((3, 4, 2, *unit), BF16),
            pltpu.VMEM((3, 4, *unit), BF16),
            pltpu.VMEM((3, 3, *unit), BF16),
            pltpu.VMEM((1, 4, 2, *tile), F32),
            pltpu.VMEM((1, 4, *tile), F32),
            pltpu.VMEM((1, 3, *tile), F32),
            pltpu.SemaphoreType.DMA((2, 5, SLOTS)),
            pltpu.SemaphoreType.DMA((2, 3, SLOTS)),
            pltpu.SemaphoreType.DMA((2, 1, SLOTS)),
            pltpu.SemaphoreType.DMA((2, 31)),
            pltpu.SemaphoreType.DMA((2, 31)),
            pltpu.SemaphoreType.DMA((2, 2 * (tokens // PAGE))),
            pltpu.SemaphoreType.DMA((2,)),
        ]
        scratch += [pltpu.VMEM(array.shape, array.dtype) for array in (x, weight, box, *kept, dctx)]
        scratch.append(pltpu.SemaphoreType.DMA((12,)))
        extra = dict(collective_id=2, has_side_effects=True)
    return pl.pallas_call(
        functools.partial(attend_back_kernel, heads, plan, inv_tokens),
        out_shape=[jax.ShapeDtypeStruct(s, d) for s, d in shapes],
        in_specs=in_specs,
        out_specs=[vmem] * len(shapes),
        scratch_shapes=scratch,
        compiler_params=pltpu.CompilerParams(vmem_limit_bytes=VMEM_LIMIT, **extra),
        name="attend_backward",
    )(x, weight, box, *kept, dctx, *more)


def adam_step(master, first, second, gradient, rate, decay):
    new_first = BETA_ONE * first + (1.0 - BETA_ONE) * gradient
    new_second = BETA_TWO * second + (1.0 - BETA_TWO) * gradient * gradient
    first_hat = new_first / (1.0 - BETA_ONE**STEP)
    second_hat = new_second / (1.0 - BETA_TWO**STEP)
    new_master = master - rate * (first_hat / (jnp.sqrt(second_hat) + ADAM_EPS) + decay * master)
    return (new_first, new_second, new_master)


def adam_kernel(heads, norm_ref, *refs):
    sum_e, sum_f, sum_a, sum_b, sum_v, *refs = refs
    states, outs = refs[:18], refs[18:]
    clip = CLIP_LIMIT / jnp.maximum(norm_ref[0:1, 0:1], CLIP_LIMIT)

    def update(first, out, gradient, at, rate, decay):
        news = adam_step(*(ref[at] for ref in states[first : first + 3]), gradient * clip, rate, decay)
        for ref, new in zip(outs[out : out + 3], news):
            ref[at] = new
        if decay:
            outs[out + 3][at] = news[2].astype(BF16)

    def heads_of(kind):
        half = heads // 2
        return jnp.concatenate(
            [
                sum_a[1 + head // half, :, (2 * (head % half) + kind) * HD : (2 * (head % half) + kind + 1) * HD]
                for head in range(heads)
            ],
            axis=1,
        )

    for index, gradient in enumerate((sum_a[0], heads_of(0), heads_of(1))):
        update(0, 0, gradient, index, RATE_MATRIX, WEIGHT_DECAY)
    update(3, 4, sum_b[0], ALL, RATE_MATRIX, WEIGHT_DECAY)
    update(6, 8, sum_e[0], ALL, RATE_MATRIX, WEIGHT_DECAY)
    for chunk in range(4):
        lanes = (ALL, slice(chunk * UNIT, (chunk + 1) * UNIT))
        update(9, 12, sum_e[1 + chunk], lanes, RATE_MATRIX, WEIGHT_DECAY)
        update(12, 16, sum_f[chunk], lanes, RATE_MATRIX, WEIGHT_DECAY)
    rows, each = states[15].shape
    update(15, 20, sum_v[0, 0:rows, 0:each], ALL, RATE_VECTOR, 0.0)


def adam_all(norm, sums, states):
    shapes = []
    for first in range(0, 18, 3):
        shapes += [(states[first].shape, F32)] * 3
        if first < 15:
            shapes.append((states[first].shape, BF16))
    vmem = pl.BlockSpec(memory_space=pltpu.VMEM)
    return pl.pallas_call(
        functools.partial(adam_kernel, states[0].shape[2] // HD),
        out_shape=[jax.ShapeDtypeStruct(s, d) for s, d in shapes],
        in_specs=[vmem] * (6 + len(states)),
        out_specs=[vmem] * len(shapes),
        compiler_params=pltpu.CompilerParams(vmem_limit_bytes=VMEM_LIMIT),
        name="adam_all",
    )(norm, *sums, *states)


def pack_qkv(shard):
    rows, cols = shard.shape[1:]
    heads = cols // HD
    pairs = jnp.stack([shard[1].reshape(rows, heads, HD), shard[2].reshape(rows, heads, HD)], axis=2)
    pairs = pairs.reshape(rows, 2, cols)
    return jnp.stack([shard[0], pairs[:, 0], pairs[:, 1]])


def unpack_qkv(packed):
    rows, cols = packed.shape[1:]
    pairs = jnp.concatenate([packed[1], packed[2]], axis=1).reshape(rows, cols // HD, 2, HD)
    return jnp.stack(
        [packed[0], pairs[:, :, 0].reshape(rows, cols), pairs[:, :, 1].reshape(rows, cols)]
    )


def to_chunks(shard):
    rows = shard.shape[0]
    return shard.reshape(rows, -1, UNIT).transpose(1, 0, 2)


def from_chunks(chunks):
    return chunks.transpose(1, 0, 2).reshape(chunks.shape[1], -1)


def on_device(
    layer_input,
    page_boxes,
    output_grad,
    attn_proj,
    attn_first,
    attn_second,
    box_proj,
    box_first,
    box_second,
    merge_proj,
    merge_first,
    merge_second,
    expand_proj,
    expand_first,
    expand_second,
    shrink_proj,
    shrink_first,
    shrink_second,
    vectors,
    vector_first,
    vector_second,
):
    mp_count = lax.axis_size("mp")
    dp_count = lax.axis_size("dp")
    mp_index = lax.axis_index("mp")
    tokens, width = layer_input.shape
    cols = attn_proj.shape[2]
    heads = cols // HD
    own_tokens = tokens // mp_count
    inv_tokens = 1.0 / (tokens * dp_count)

    corners = page_boxes.T
    omega = (10000.0 ** (-np.arange(FREQS, dtype=np.float64) / FREQS)).astype(np.float32)[:, None]
    omega = jnp.asarray(omega)
    plan = (mp_count, dp_count) if dp_count == 16 and mp_count == 2 else None
    if plan is not None:
        each = vectors.shape[1]
        pick = np.zeros((128, width), np.float32)
        pick[np.arange(width) % each, np.arange(width)] = 1.0
        pick = jnp.asarray(pick)
        *kept, w_qkv, w_box, layer_out, dctx, dh1, g_expand, vec_sum, sum_f = layer_forward(
            layer_input,
            output_grad,
            corners,
            omega,
            pick,
            (attn_proj, box_proj, vectors, merge_proj.T, expand_proj, shrink_proj.T),
            plan,
            inv_tokens,
        )
        input_grad, sum_e, sum_a, sum_b, sum_v, norm = attend_backward(
            layer_input,
            w_qkv.reshape(3, width, cols),
            w_box,
            kept,
            dctx,
            plan,
            inv_tokens,
            (dh1, vec_sum, sum_f, pick, g_expand),
        )
        merge = [merge_proj.T, merge_first.T, merge_second.T]
        shrink = [shrink_proj.T, shrink_first.T, shrink_second.T]
        results = adam_all(
            norm,
            (sum_e, sum_f, sum_a, sum_b, sum_v),
            [attn_proj, attn_first, attn_second, box_proj, box_first, box_second, *merge]
            + [expand_proj, expand_first, expand_second, *shrink, vectors, vector_first, vector_second],
        )
        turned = (8, 9, 10, 11, 16, 17, 18, 19)
        results = [out.T if k in turned else out for k, out in enumerate(results)]
        return (layer_out, input_grad, norm[0, 0], *results)
    shard_qkv = pack_qkv(attn_proj).astype(BF16)
    shard_e = jnp.concatenate([merge_proj.T[None], to_chunks(expand_proj)]).astype(BF16)
    shard_f = to_chunks(shrink_proj.T).astype(BF16)
    w_qkv = lax.all_gather(shard_qkv, "dp", axis=1, tiled=True)
    w_box = lax.all_gather(box_proj.astype(BF16), "dp", axis=0, tiled=True)
    w_expand = lax.all_gather(lax.all_gather(shard_e, "dp", axis=1, tiled=True), "mp", axis=1)
    w_shrink = lax.all_gather(lax.all_gather(shard_f, "dp", axis=1, tiled=True), "mp", axis=1)
    vecs = lax.all_gather(vectors, ("dp", "mp"), axis=1, tiled=True)
    vecs = jnp.pad(vecs, ((0, VROWS - vecs.shape[0]), (0, 0)))
    *kept, context = attend_forward(layer_input, corners, omega, w_qkv, w_box, vecs)
    context = lax.all_to_all(
        context.reshape(mp_count, own_tokens, cols), "mp", split_axis=0, concat_axis=0
    )

    def own_rows(array):
        return lax.dynamic_slice_in_dim(array, mp_index * own_tokens, own_tokens)

    layer_out, dctx, dh1, g_expand, g_shrink, vec_sum = feed_both(
        own_rows(layer_input), own_rows(output_grad), context, w_expand, w_shrink, vecs
    )
    g_feed = jnp.concatenate([g_expand, g_shrink])
    layer_out = lax.all_gather(layer_out, "mp", axis=0, tiled=True)
    dctx = lax.all_to_all(dctx, "mp", split_axis=0, concat_axis=0).reshape(tokens, cols)
    part, g_qkv, g_box, qkv_sum = attend_backward(
        layer_input, w_qkv, w_box, kept, dctx, None, inv_tokens
    )
    own_part = lax.psum_scatter(part.astype(BF16), "mp", scatter_dimension=0, tiled=True)
    own_grad = (own_part.astype(F32) + dh1).astype(BF16)
    input_grad = lax.all_gather(own_grad, "mp", axis=0, tiled=True)
    shard_attn = unpack_qkv(
        lax.psum_scatter(g_qkv, "dp", scatter_dimension=1, tiled=True).astype(F32) * inv_tokens
    )
    shard_box = lax.psum_scatter(g_box, "dp", scatter_dimension=0, tiled=True) * inv_tokens
    sum_feed = lax.psum_scatter(g_feed, "dp", scatter_dimension=2, tiled=True)
    sum_feed = lax.psum_scatter(sum_feed, "mp", scatter_dimension=1, tiled=True)[:, 0]
    sum_feed = sum_feed.astype(F32) * inv_tokens
    sum_expand, sum_shrink = sum_feed[0:5], sum_feed[5:]

    def placed(row):
        return lax.dynamic_update_slice_in_dim(
            jnp.zeros((width,), F32), row, mp_index * cols, 0
        )[None, :]

    value_sum = qkv_sum[0, cols:].reshape(heads, 2, HD)[:, 1].reshape(cols)
    vector_grad = jnp.concatenate(
        [vec_sum[0:6], placed(qkv_sum[0, 0:cols]), placed(value_sum), vec_sum[8:12]]
    )
    vector_shard = (
        lax.psum_scatter(vector_grad, ("dp", "mp"), scatter_dimension=1, tiled=True) * inv_tokens
    )
    square = sum(
        jnp.sum(shard * shard)
        for shard in (shard_attn, shard_box, sum_expand, sum_shrink, vector_shard)
    )
    grad_norm = jnp.sqrt(lax.psum(square, ("dp", "mp")))
    shard_merge = sum_expand[0].T
    shard_expand = from_chunks(sum_expand[1:])
    shard_shrink = from_chunks(sum_shrink).T
    clip_scale = CLIP_LIMIT / jnp.maximum(grad_norm, CLIP_LIMIT)
    results = [layer_out, input_grad, grad_norm]
    for master, first, second, shard in (
        (attn_proj, attn_first, attn_second, shard_attn),
        (box_proj, box_first, box_second, shard_box),
        (merge_proj, merge_first, merge_second, shard_merge),
        (expand_proj, expand_first, expand_second, shard_expand),
        (shrink_proj, shrink_first, shrink_second, shard_shrink),
    ):
        new_first, new_second, new_master = adam_step(
            master, first, second, shard * clip_scale, RATE_MATRIX, WEIGHT_DECAY
        )
        results += [new_first, new_second, new_master, new_master.astype(BF16)]
    results += adam_step(
        vectors, vector_first, vector_second, vector_shard * clip_scale, RATE_VECTOR, 0.0
    )
    return tuple(results)


def solution(mesh):
    rows = P("dp", None)
    attn = P(None, "dp", "mp")
    tall = P("dp", "mp")
    wide = P("mp", "dp")
    vector = P(None, ("dp", "mp"))
    in_specs = (rows,) * 3 + (attn,) * 3 + (tall,) * 3 + (wide,) * 3 + (tall,) * 3 + (wide,) * 3
    in_specs += (vector,) * 3
    out_specs = (rows, rows, P()) + (attn,) * 4 + (tall,) * 4 + (wide,) * 4 + (tall,) * 4
    out_specs += (wide,) * 4 + (vector,) * 3
    return jax.shard_map(
        on_device, mesh=mesh, in_specs=in_specs, out_specs=out_specs, check_vma=False
    )
```

```python
import functools
import types

import jax
import jax.numpy as jnp
import numpy as np
from jax import lax
from jax.experimental import pallas as pl
from jax.experimental.pallas import tpu as pltpu
from jax.sharding import PartitionSpec as P

HD = 64
FREQS = 32
PE = 128
PAGE = 512
STEP = 10

NORM_EPS = 1e-12
CLIP_LIMIT = 0.1
BETA_ONE = 0.9
BETA_TWO = 0.999
ADAM_EPS = 1e-08
RATE_MATRIX = 0.05
RATE_VECTOR = 0.5
WEIGHT_DECAY = 0.01

F32 = jnp.float32
BF16 = jnp.bfloat16
VMEM_LIMIT = 60 * 1024 * 1024

NN = (((1,), (0,)), ((), ()))
NT = (((1,), (1,)), ((), ()))
TN = (((0,), (0,)), ((), ()))


def dot(lhs, rhs, dims=NN):
    return lax.dot_general(lhs, rhs, dims, preferred_element_type=F32)


def aligned(index, size):
    return pl.ds(pl.multiple_of(index * size, size), size)


def swap_blocks(feat):
    return jnp.concatenate(
        [
            feat[FREQS : 2 * FREQS],
            feat[0:FREQS],
            feat[3 * FREQS :],
            feat[2 * FREQS : 3 * FREQS],
        ],
        axis=0,
    )


def turn_factors(trig):
    cos_x, sin_x = trig[0:FREQS], trig[FREQS : 2 * FREQS]
    cos_y, sin_y = trig[2 * FREQS : 3 * FREQS], trig[3 * FREQS :]
    return (
        jnp.concatenate([sin_x, sin_x, sin_y, sin_y], axis=0),
        jnp.concatenate([cos_x, -cos_x, cos_y, -cos_y], axis=0),
    )


MESH = pl.DeviceIdType.MESH
ALL = slice(None)
UNIT = 384


class Place:
    def __init__(self):
        rank = lax.axis_index("dp")
        self.m = lax.axis_index("mp")
        self.z = rank // 4
        self.y = (rank // 2) % 2
        self.c = rank % 2
        self.peer = {
            "x": (rank, 1 - self.m),
            "y": (rank + 2 - 4 * self.y, self.m),
            "c": (rank + 1 - 2 * self.c, self.m),
        }
        self.far = [((rank + 4 * step) % 16, self.m) for step in (1, 2, 3)]

    def signal(self):
        barrier = pltpu.get_barrier_semaphore()
        for device in list(self.peer.values()) + self.far:
            pl.semaphore_signal(barrier, inc=1, device_id=device, device_id_type=MESH)

    def wait(self):
        pl.semaphore_wait(pltpu.get_barrier_semaphore(), 6)

    def signal_all(self):
        barrier = pltpu.get_barrier_semaphore()
        rank = self.m * 16 + lax.axis_index("dp")

        def one(step, carry):
            to = (rank + step) % 32
            pl.semaphore_signal(barrier, inc=1, device_id=(to % 16, to // 16), device_id_type=MESH)
            return carry

        lax.fori_loop(1, 32, one, 0)

    def wait_all(self):
        pl.semaphore_wait(pltpu.get_barrier_semaphore(), 31)


def remote(src, dst, send_sem, recv_sem, device):
    return pltpu.make_async_remote_copy(
        src_ref=src,
        dst_ref=dst,
        send_sem=send_sem,
        recv_sem=recv_sem,
        device_id=device,
        device_id_type=MESH,
    )


SLOT = {"c": 0, "z": 1, "y": 4, "x": 5}
SLOTS = 6


class Tree:
    lag = 1
    held_back = 0

    def stage(self, index, chunk):
        raise NotImplementedError

    def event(self, number):
        for index in range(self.count - 1 - self.held_back, -1, -1):
            chunk = number - index * self.lag
            if self.chunks == 1:
                pl.when(chunk == 0)(lambda index=index: self.stage(index, 0))
            else:
                pl.when((chunk >= 0) & (chunk < self.chunks))(
                    lambda index=index, chunk=chunk: self.stage(index, chunk)
                )

    @property
    def events(self):
        return self.chunks + (self.count - 1 - self.held_back) * self.lag

    def rest(self):
        def one(chunk, carry):
            self.stage(self.count - 1, chunk)
            return carry

        lax.fori_loop(0, self.chunks, one, 0)


class Spread(Tree):
    def __init__(self, place, ref, chunks, order, sems):
        self.chunks, self.ref, self.sems = chunks, ref, sems
        have = {"x": place.m if "x" in order else 0, "z": place.z, "y": place.y, "c": place.c}
        mine = {"x": place.m, "y": place.y, "c": place.c}
        self.steps = []
        for axis in order:
            if axis == "z":
                sends = [(have, place.far[step - 1], step) for step in (1, 2, 3)]
                waits = [(dict(have, z=(place.z + 4 - step) % 4), step) for step in (1, 2, 3)]
            else:
                sends = [(have, place.peer[axis], SLOT[axis])]
                waits = [(dict(have, **{axis: 1 - mine[axis]}), SLOT[axis])]
                if axis == "c" and have["z"] == ALL:
                    sends = [(dict(have, z=z), place.peer[axis], SLOT[axis]) for z in range(4)]
            self.steps.append((sends, waits, sends[0][0] if len(sends) < 4 else have))
            have = dict(have, **{axis: ALL})
        self.some = place.peer["c"]
        self.count = len(self.steps) + 1

    def _copy(self, chunk, have, device, slot):
        block = self.ref.at[chunk, have["x"], have["z"], have["y"], have["c"]]
        return remote(block, block, self.sems.at[0, chunk, slot], self.sems.at[1, chunk, slot], device)

    def stage(self, index, chunk):
        if index > 0:
            for have, slot in self.steps[index - 1][1]:
                self._copy(chunk, have, self.some, slot).wait_recv()
        if index < self.count - 1:
            for have, device, slot in self.steps[index][0]:
                self._copy(chunk, have, device, slot).start()

    def drain(self):
        def one(chunk, carry):
            for sends, _, whole in self.steps:
                if len(sends) == 4:
                    self._copy(chunk, whole, self.some, sends[0][2]).wait_send()
                else:
                    for have, device, slot in sends:
                        self._copy(chunk, have, device, slot).wait_send()
            return carry

        lax.fori_loop(0, self.chunks, one, 0)


class Reduce(Tree):
    def __init__(self, place, full, total, lands, chunks, order, sems, finish):
        self.place, self.full, self.total, self.lands = place, full, total, lands
        self.chunks, self.sems, self.finish = chunks, sems, finish
        mine = {"x": place.m, "y": place.y}
        self.across = ALL if "x" in order else 0
        have = {"x": self.across, "z": ALL, "y": ALL}
        self.order, self.haves = order, []
        for axis in order:
            before = have
            if axis != "c":
                have = dict(have, **{axis: place.z if axis == "z" else mine[axis]})
            self.haves.append((before, have))
        self.count = len(order) + 1

    def _at(self, chunk, have):
        if self.total is None:
            return self.full.at[chunk, have["x"], have["z"], have["y"], self.place.c]
        return self.total.at[chunk, have["x"], have["z"], have["y"]]

    def _copies(self, index, chunk, start=False):
        axis, (before, _) = self.order[index], self.haves[index]
        place, land = self.place, self.lands[axis]

        def copy(src, dst, slot, device):
            return remote(src, dst, self.sems.at[0, chunk, slot], self.sems.at[1, chunk, slot], device)

        if axis == "c":
            other = 1 - place.c
            if start and self.across == ALL:
                return [
                    copy(
                        self.full.at[chunk, :, z, :, other], land.at[chunk, :, z], SLOT[axis], place.peer[axis]
                    )
                    for z in range(4)
                ]
            source = self.full.at[chunk, self.across, :, :, other]
            return [copy(source, land.at[chunk], SLOT[axis], place.peer[axis])]
        if axis == "z":
            return [
                copy(
                    self._at(chunk, dict(before, z=(place.z + step) % 4)),
                    land.at[chunk, step - 1],
                    step,
                    place.far[step - 1],
                )
                for step in (1, 2, 3)
            ]
        other = 1 - (place.m if axis == "x" else place.y)
        source = self._at(chunk, dict(before, **{axis: other}))
        return [copy(source, land.at[chunk], SLOT[axis], place.peer[axis])]

    def stage(self, index, chunk):
        if index > 0:
            axis, (_, have) = self.order[index - 1], self.haves[index - 1]
            land = self.lands[axis]
            for copy in self._copies(index - 1, chunk):
                copy.wait_recv()
            mine = self._at(chunk, have)
            last = index == self.count - 1
            if axis == "z":
                value = mine[...].astype(F32)
                for step in range(3):
                    value += land[chunk, step].astype(F32)
            elif last:
                value = mine[...].astype(F32) + land[chunk].astype(F32)
            else:
                value = mine[...] + land[chunk]
            if last:
                self.finish(chunk, value)
            else:
                mine[...] = value.astype(mine.dtype)
        if index < self.count - 1:
            for copy in self._copies(index, chunk, True):
                copy.start()

    def drain(self):
        def one(chunk, carry):
            for index in range(self.count - 1):
                for copy in self._copies(index, chunk):
                    copy.wait_send()
            return carry

        lax.fori_loop(0, self.chunks, one, 0)


class Everyone:
    def __init__(self, place, send_block, land_block, sems):
        self.rank = place.m * 16 + lax.axis_index("dp")
        self.send_block, self.land_block, self.sems = send_block, land_block, sems

    def _copy(self, step):
        to = (self.rank + step) % 32
        return remote(
            self.send_block(to),
            self.land_block(step),
            self.sems.at[0, step - 1],
            self.sems.at[1, step - 1],
            (to % 16, to // 16),
        )

    def _each(self, act):
        def one(step, carry):
            act(self._copy(step))
            return carry

        lax.fori_loop(1, 32, one, 0)

    def start(self):
        self._each(lambda copy: copy.start())

    def wait(self):
        self._each(lambda copy: copy.wait())


VROWS = 16


def rows_from_blocks(blocks, pick, counts):
    mp_count, dp_count = counts
    width = pick.shape[1]
    each = width // (mp_count * dp_count)
    wide = lax.dot_general(
        blocks, pick, NN, precision=lax.Precision.HIGHEST, preferred_element_type=F32
    )
    lane = lax.broadcasted_iota(jnp.int32, (VROWS, width), 1)
    table = jnp.zeros((VROWS, width), F32)
    for m in range(mp_count):
        for r in range(dp_count):
            first = (r * mp_count + m) * each
            row = (m * dp_count + r) * VROWS
            table += jnp.where((lane >= first) & (lane < first + each), wide[row : row + VROWS], 0.0)
    return table


def attend_setup(heads, m, box_full, vec_ref, box_heads, bias):
    cols = heads * HD
    for head in range(heads):
        box_heads[head] = box_full[:, head * HD : (head + 1) * HD]
    width = vec_ref.shape[1]
    own = jnp.where(m == 0, vec_ref[6:8, 0:cols], vec_ref[6:8, width - cols :])
    spread = exact_dot(jnp.broadcast_to(own[1:2], (8, cols)), pair_place(cols))
    bias[0:1, 0:cols] = own[0:1]
    bias[0:1, cols:] = spread[0:1]


def attend_trig(omega_ref, corner_ref, trig_ref):
    corner = corner_ref[...].astype(F32)
    angle_x = omega_ref[...] * ((corner[0:1] + corner[2:3]) * 0.5)
    angle_y = omega_ref[...] * ((corner[1:2] + corner[3:4]) * 0.5)
    trig_ref[0:FREQS, :] = jnp.cos(angle_x)
    trig_ref[FREQS : 2 * FREQS, :] = jnp.sin(angle_x)
    trig_ref[2 * FREQS : 3 * FREQS, :] = jnp.cos(angle_y)
    trig_ref[3 * FREQS :, :] = jnp.sin(angle_y)


def quiet(*args):
    return None


def attend_math(heads, r, weights, page_of, projected, attended):
    cols = heads * HD
    pages = r.x.shape[0] // PAGE

    def project(page, carry):
        rows = aligned(page, PAGE)
        tokens = r.x[rows, :]
        query = dot(tokens, weights(0)) + r.bias[0:1, 0:cols]
        query = query.astype(BF16) * HD ** (-0.5)
        r.qtok[rows, :] = query
        qa_rows = query.T
        for half in range(2):
            lanes = slice(half * cols, (half + 1) * cols)
            pair = dot(tokens, weights(1 + half)) + r.bias[0:1, cols + half * cols : 2 * cols + half * cols]
            pair = pair.astype(BF16)
            r.kvtok[rows, lanes] = pair
            turned = pair.T
            for spot in range(heads // 2):
                head_rows = slice((half * heads // 2 + spot) * HD, (half * heads // 2 + spot + 1) * HD)
                r.kt[head_rows, rows] = turned[2 * spot * HD : (2 * spot + 1) * HD]
                r.vt[head_rows, rows] = turned[(2 * spot + 1) * HD : (2 * spot + 2) * HD]
        trig = r.trig[:, rows]
        kft = trig.astype(BF16)
        r.kft[:, rows] = kft
        r.kftok[rows, :] = kft.T
        own, partner = turn_factors(trig)
        for head in range(heads):
            query_head = qa_rows[head * HD : (head + 1) * HD]
            proj = dot(r.box_heads[head], query_head)
            feat = proj * own + swap_blocks(proj) * partner
            r.qa[head, 0:PE, rows] = feat.astype(BF16)
            r.qa[head, PE : PE + HD, rows] = query_head
        projected(page)
        return carry

    lax.fori_loop(0, pages, project, 0)

    def attend(step, carry):
        turn, pair = step // (heads // 2), step % (heads // 2)
        rows = aligned(page_of(turn), PAGE)
        halves = []
        blank = jnp.zeros((HD, PAGE), BF16)
        for side in range(2):
            head = pair * 2 + side
            lanes = aligned(head, 2 * HD)
            left = jnp.concatenate([r.kftok[rows, :], r.kvtok[rows, lanes]], axis=1)
            score = dot(left, jnp.concatenate([r.qa[head, :, rows], blank], axis=0))
            top = jnp.max(score, axis=0, keepdims=True)
            weight = jnp.exp(score - top)
            total = jnp.sum(weight, axis=0, keepdims=True)
            value = r.vt[aligned(head, HD), rows]
            halves.append(dot(value, weight.astype(BF16)) * (1.0 / total))
            r.log[head, :, rows] = top + jnp.log(total)
        both = jnp.concatenate(halves, axis=0).astype(BF16)
        lanes = aligned(pair, 2 * HD)
        r.ctxt[lanes, rows] = both
        r.ctx[rows, lanes] = both.T
        attended(step, turn, pair)
        return carry

    lax.fori_loop(0, pages * (heads // 2), attend, 0)


def attend_buffers(heads, tokens):
    cols = heads * HD
    kept = [
        ("qa", (heads, PE + HD, tokens), BF16),
        ("qtok", (tokens, cols), BF16),
        ("kvtok", (tokens, 2 * cols), BF16),
        ("kt", (cols, tokens), BF16),
        ("kft", (PE, tokens), BF16),
        ("trig", (PE, tokens), F32),
        ("ctxt", (cols, tokens), BF16),
        ("log", (heads, 1, tokens), F32),
    ]
    used = [
        ("kftok", (tokens, PE), BF16),
        ("box_heads", (heads, PE, HD), BF16),
        ("bias", (8, 3 * cols), F32),
        ("ctx", (tokens, cols), BF16),
        ("vt", (cols, tokens), BF16),
    ]
    return kept, used


def attend_kernel(heads, names, *refs):
    r = types.SimpleNamespace(**dict(zip(names, refs)))
    attend_setup(heads, lax.axis_index("mp"), r.box, r.vec, r.box_heads, r.bias)
    attend_trig(r.omega, r.corner, r.trig)
    attend_math(heads, r, lambda chunk: r.w[chunk], lambda turn: turn, quiet, quiet)


def attend_forward(x, corners, omega, w_qkv, w_box, vecs):
    tokens = x.shape[0]
    heads = w_box.shape[1] // HD
    kept, used = attend_buffers(heads, tokens)
    outs = kept + [used[3]]
    scratch = used[:3] + used[4:]
    names = ["x", "corner", "omega", "w", "box", "vec"] + [item[0] for item in outs + scratch]
    vmem = pl.BlockSpec(memory_space=pltpu.VMEM)
    return pl.pallas_call(
        functools.partial(attend_kernel, heads, names),
        out_shape=[jax.ShapeDtypeStruct(shape, kind) for _, shape, kind in outs],
        in_specs=[vmem] * 6,
        out_specs=[vmem] * len(outs),
        scratch_shapes=[pltpu.VMEM(shape, kind) for _, shape, kind in scratch],
        compiler_params=pltpu.CompilerParams(vmem_limit_bytes=VMEM_LIMIT),
        name="attend_forward",
    )(x, corners, omega, w_qkv, w_box, vecs)


TILE = 256


def norm_stats(value):
    mean = jnp.mean(value, axis=-1, keepdims=True)
    centred = value - mean
    var = jnp.mean(centred * centred, axis=-1, keepdims=True)
    return centred, lax.rsqrt(var + NORM_EPS)


def norm_back(grad_normed, normed, scale):
    first = jnp.mean(grad_normed, axis=-1, keepdims=True)
    second = jnp.mean(grad_normed * normed, axis=-1, keepdims=True)
    return scale * (grad_normed - first - normed * second)


def col_sum(value):
    return jnp.sum(value, axis=0, keepdims=True)


def feed_math(r, hooks):
    hook = {name: quiet for name in ("entered", "grew", "turned", "shrinks", "shrank", "left")}
    hook.update(hooks)
    tokens = r.x.shape[0]
    sides = r.we.shape[1]
    per_side = (r.we.shape[0] - 1) // 2
    steps = sides * per_side
    tiles = tokens // TILE
    wide = 2 * UNIT
    sum2 = dnorm = r.sum2

    def flat(ref, chunk, side):
        return ref[chunk, side].reshape(-1, UNIT)

    def two(ref, first, side):
        return jnp.concatenate([flat(ref, first, side), flat(ref, first + 1, side)], axis=1)

    def w_expand(step):
        return two(r.we, 1 + 2 * (step % per_side), step // per_side)

    def w_shrink(step):
        return two(r.ws, 2 * (step % per_side), step // per_side)

    def put_two(ref, first, side, value):
        shape = ref.shape[2:]
        ref[first, side] = value[:, 0:UNIT].reshape(shape)
        ref[first + 1, side] = value[:, UNIT:].reshape(shape)

    def by_halves(number):
        return (number % sides) * per_side + number // sides

    def enter(tile, carry):
        rows = aligned(tile, TILE)
        total = r.x[rows, :].astype(F32) + r.vec[4:5, :]
        for side in range(sides):
            total += dot(r.ctxx[side, rows, :], flat(r.we, 0, side), NT)
        centred, scale = norm_stats(total)
        normed = centred * scale
        r.norm1[rows, :] = normed
        r.scale1[rows, :] = scale
        shifted = normed * r.vec[0:1, :] + r.vec[1:2, :]
        r.al[rows, :] = shifted.astype(BF16)
        sum2[rows, :] = shifted + r.vec[5:6, :]
        return carry

    lax.fori_loop(0, tiles, enter, 0)
    hook["entered"]()

    def grow(number, carry):
        step = by_halves(number)
        whole = aligned(step, wide)

        def one(tile, inner):
            rows = aligned(tile, TILE)
            pre = dot(r.al[rows, :], w_expand(step)) + r.vec[pl.ds(8 + step, 1), :]
            phi = 0.5 + 0.5 * lax.erf(pre * 2.0 ** (-0.5))
            density = jnp.exp(pre * pre * -0.5) * (0.5 / jnp.pi) ** 0.5
            low = (pre * phi).astype(BF16)
            r.act[rows, whole] = low
            r.slope[rows, whole] = (phi + pre * density).astype(BF16)
            sum2[rows, :] += dot(low, w_shrink(step), NT)
            hook["grew"](number * tiles + tile)
            return inner

        lax.fori_loop(0, tiles, one, 0)
        return carry

    lax.fori_loop(0, steps, grow, 0)
    r.vsum[...] = jnp.zeros_like(r.vsum)

    def turn(tile, carry):
        rows = aligned(tile, TILE)
        centred, scale = norm_stats(sum2[rows, :])
        normed = centred * scale
        r.out[rows, :] = (normed * r.vec[2:3, :] + r.vec[3:4, :]).astype(BF16)
        grad = r.og[rows, :].astype(F32)
        r.vsum[2:3, :] += col_sum(grad * normed)
        r.vsum[3:4, :] += col_sum(grad)
        back = norm_back(grad * r.vec[2:3, :], normed, scale)
        r.vsum[5:6, :] += col_sum(back)
        r.dh2l[rows, :] = back.astype(BF16)
        dnorm[rows, :] = back
        hook["turned"](tile)
        return carry

    lax.fori_loop(0, tiles, turn, 0)
    r.flip[...] = r.dh2l[...].T

    def grad_shrink(number, carry):
        step = by_halves(number)
        grad = dot(r.flip[...], r.act[:, aligned(step, wide)]).astype(BF16)
        put_two(r.gs, 2 * (number // sides), number % sides, grad)
        hook["shrinks"](number)
        return carry

    lax.fori_loop(0, steps, grad_shrink, 0)

    def shrink(number, carry):
        step = by_halves(number)
        whole = aligned(step, wide)

        def one(tile, inner):
            rows = aligned(tile, TILE)
            grad = dot(r.dh2l[rows, :], w_shrink(step))
            low = (grad * r.slope[rows, whole].astype(F32)).astype(BF16)
            r.slope[rows, whole] = low
            r.vsum[pl.ds(8 + step, 1), :] += col_sum(low.astype(F32))
            dnorm[rows, :] += dot(low, w_expand(step), NT)
            hook["shrank"](number * tiles + tile)
            return inner

        lax.fori_loop(0, tiles, one, 0)
        return carry

    lax.fori_loop(0, steps, shrink, 0)

    def leave(tile, carry):
        rows = aligned(tile, TILE)
        grad = dnorm[rows, :]
        normed = r.norm1[rows, :]
        r.vsum[0:1, :] += col_sum(grad * normed)
        r.vsum[1:2, :] += col_sum(grad)
        back = norm_back(grad * r.vec[0:1, :], normed, r.scale1[rows, :])
        r.vsum[4:5, :] += col_sum(back)
        low = back.astype(BF16)
        r.dh1l[rows, :] = low
        for side in range(sides):
            r.dctx[side, rows, :] = dot(low, flat(r.we, 0, side)).astype(BF16)
        hook["left"](tile)
        return carry

    lax.fori_loop(0, tiles, leave, 0)
    r.flip[...] = r.al[...].T

    def grad_expand(number, carry):
        step = by_halves(number)
        grad = dot(r.flip[...], r.slope[:, aligned(step, wide)]).astype(BF16)
        put_two(r.ge, 1 + 2 * (number // sides), number % sides, grad)
        return carry

    lax.fori_loop(0, steps, grad_expand, 0)
    r.flip[...] = r.dh1l[...].T
    for side in range(sides):
        r.ge[0, side] = dot(r.flip[...], r.ctxx[side]).astype(BF16).reshape(r.ge.shape[2:])


def feed_buffers(tokens, width, hidden):
    return [
        ("norm1", (tokens, width), F32),
        ("scale1", (tokens, 1), F32),
        ("sum2", (tokens, width), F32),
        ("al", (tokens, width), BF16),
        ("act", (tokens, hidden), BF16),
        ("slope", (tokens, hidden), BF16),
        ("dh2l", (tokens, width), BF16),
        ("flip", (width, tokens), BF16),
    ]


def feed_kernel(names, *refs):
    feed_math(types.SimpleNamespace(**dict(zip(names, refs))), {})


def feed_both(x, og, ctx, w_expand, w_shrink, vecs):
    tokens, width = x.shape
    chunks, sides = w_shrink.shape[0:2]
    outs = [
        ("out", (tokens, width), BF16),
        ("dctx", (sides, tokens, UNIT), BF16),
        ("dh1l", (tokens, width), BF16),
        ("ge", (chunks + 1, sides, width, UNIT), BF16),
        ("gs", (chunks, sides, width, UNIT), BF16),
        ("vsum", (VROWS, width), F32),
    ]
    scratch = feed_buffers(tokens, width, sides * chunks * UNIT)
    names = ["x", "og", "ctxx", "we", "ws", "vec"] + [item[0] for item in outs + scratch]
    vmem = pl.BlockSpec(memory_space=pltpu.VMEM)
    return pl.pallas_call(
        functools.partial(feed_kernel, names),
        out_shape=[jax.ShapeDtypeStruct(shape, kind) for _, shape, kind in outs],
        in_specs=[vmem] * 6,
        out_specs=[vmem] * len(outs),
        scratch_shapes=[pltpu.VMEM(shape, kind) for _, shape, kind in scratch],
        compiler_params=pltpu.CompilerParams(vmem_limit_bytes=VMEM_LIMIT),
        name="feed_both",
    )(x, og, ctx, w_expand, w_shrink, vecs)


def layer_kernel(heads, plan, inv_tokens, names, kept, used, feeds, *refs):
    r = types.SimpleNamespace(**dict(zip(names, refs)))
    cols = heads * HD
    tokens = r.x_all.shape[0]
    pages = tokens // PAGE
    own_tokens = tokens // 2
    tiles = own_tokens // TILE
    place = Place()
    place.signal()
    m, peer = place.m, place.peer["x"]
    at = (place.z, place.y, place.c)
    own = aligned(m, own_tokens)
    load_x = pltpu.make_async_copy(r.x_all.at[own, :], r.x, r.load_sem.at[0])
    load_og = pltpu.make_async_copy(r.og_all.at[own, :], r.og, r.load_sem.at[1])
    load_x.start()
    load_og.start()
    r.w[(0, 0, *at)] = r.attn[0].astype(BF16)
    for half in range(2):
        r.w[(1 + half, 0, *at)] = jnp.concatenate(
            [
                r.attn[1 + kind, :, head * HD : (head + 1) * HD].astype(BF16)
                for head in range(half * heads // 2, (half + 1) * heads // 2)
                for kind in range(2)
            ],
            axis=1,
        )
    r.box_gather[(0, 0, *at)] = r.shard_box[...]
    r.vec_gather[(0, m, *at)] = jnp.zeros((VROWS, 128), F32)
    table_at = (slice(0, r.vectors.shape[0]), slice(0, r.vectors.shape[1]))
    r.vec_gather[(0, m, *at, *table_at)] = r.vectors[...]
    r.we[(0, m, *at)] = r.merge[...].astype(BF16)
    for chunk in range(4):
        lanes = slice(chunk * UNIT, (chunk + 1) * UNIT)
        r.we[(1 + chunk, m, *at)] = r.expand[:, lanes].astype(BF16)
        r.ws[(chunk, m, *at)] = r.shrink[:, lanes].astype(BF16)
    place.wait()
    tree_v = Spread(place, r.vec_gather, 1, "xzyc", r.v_sem)
    tree_b = Spread(place, r.box_gather, 1, "zyc", r.b_sem)
    tree_a = Spread(place, r.w, 3, "zyc", r.a_sem)
    tree_e = Spread(place, r.we, 5, "zyxc", r.e_sem)
    tree_f = Spread(place, r.ws, 4, "xzyc", r.f_sem)
    tree_e.lag = tree_f.lag = 2
    late = 3
    first = tree_a.events
    begun = first - late

    def weights_event(number):
        tree_e.event(number)
        tree_f.event(number)

    def finish(chunk, value):
        r.sum_f[chunk] = value * inv_tokens

    back_f = Reduce(
        place, r.gs, None, dict(c=r.fc, y=r.fy, z=r.fz, x=r.fx), 4, "cyzx", r.back_sem, finish
    )
    back_f.lag, back_f.held_back = 2, 1

    def attention(*scoped):
        q = types.SimpleNamespace(**dict(zip([item[0] for item in kept + used] + ["x"], scoped)))
        load_all = pltpu.make_async_copy(r.x_all, q.x, r.load_sem.at[2])
        load_all.start()

        def begin(number, carry):
            tree_a.event(number)
            tree_b.event(number)
            tree_v.event(number)
            weights_event(number - late)
            pl.when(number == 1)(lambda: attend_trig(r.omega, r.corner, q.trig))

            @pl.when(number == 4)
            def _():
                r.vec[...] = rows_from_blocks(
                    r.vec_gather[...].reshape(-1, 128), r.pick[...], plan
                )
                r.box_out[...] = r.box_gather[...].reshape(PE, cols).astype(BF16)
                attend_setup(heads, m, r.box_out, r.vec, q.box_heads, q.bias)

            return carry

        lax.fori_loop(0, first, begin, 0)
        keep_w = pltpu.make_async_copy(r.w, r.w_out, r.load_sem.at[3])
        keep_w.start()
        load_all.wait()

        def projected(page):
            weights_event(begun + page)

        piece = PAGE // 2

        def swap_copy(index):
            theirs = pages * (1 - m) + index
            return remote(
                q.ctx.at[aligned(theirs, piece), :],
                r.ctxx.at[m, aligned(index, piece), :],
                r.ctx_sem.at[0, index],
                r.ctx_sem.at[1, index],
                peer,
            )

        def attended(step, turn, pair):
            pl.when(step % 2 == 0)(lambda: weights_event(begun + pages + step // 2))

            @pl.when(step == heads // 2 - 1)
            def _():
                swap_copy(2 - 2 * m).start()
                swap_copy(1).start()

            @pl.when(step == heads - 1)
            def _():
                swap_copy(2 * m).start()

        attend_math(
            heads,
            q,
            lambda chunk: r.w[chunk].reshape(-1, cols),
            lambda turn: turn * m + (pages - 1 - turn) * (1 - m),
            projected,
            attended,
        )
        stores = [
            pltpu.make_async_copy(getattr(q, name), getattr(r, name + "_out"), r.store_sem.at[k])
            for k, (name, _, _) in enumerate(kept)
        ]
        for copy in stores:
            copy.start()
        r.ctxx[m] = q.ctx[own, :]
        for index in range(pages):
            copy = remote(
                q.ctx.at[aligned(index, piece), :],
                r.ctxx.at[1 - m, aligned(index, piece), :],
                r.ctx_sem.at[0, index],
                r.ctx_sem.at[1, index],
                peer,
            )
            copy.wait_recv()
            copy.wait_send()
        for copy in stores:
            copy.wait()
        keep_w.wait()

    pl.run_scoped(
        attention,
        *[pltpu.VMEM(shape, kind) for _, shape, kind in kept + used],
        pltpu.VMEM(r.x_all.shape, BF16),
    )

    def feed(*scoped):
        q = types.SimpleNamespace(**dict(zip([item[0] for item in feeds], scoped)))
        for name in ("x", "og", "we", "ws", "vec", "ctxx", "dh1l", "ge", "gs", "vsum"):
            setattr(q, name, getattr(r, name))

        def out_copies(tile):
            rows = aligned(tile, TILE)
            there = r.out_full.at[pl.ds(pl.multiple_of(m * own_tokens + tile * TILE, TILE), TILE), :]
            return (
                pltpu.make_async_copy(q.out.at[rows, :], there, r.swap_sem.at[0, tile]),
                remote(q.out.at[rows, :], there, r.swap_sem.at[1, tile], r.swap_sem.at[2, tile], peer),
            )

        def dctx_copies(tile):
            rows = aligned(tile, TILE)
            there = r.dctx_full.at[pl.ds(pl.multiple_of(m * own_tokens + tile * TILE, TILE), TILE), :]
            return (
                pltpu.make_async_copy(q.dctx.at[m, rows, :], there, r.swap_sem.at[3, tile]),
                remote(
                    q.dctx.at[1 - m, rows, :], there, r.swap_sem.at[4, tile], r.swap_sem.at[5, tile], peer
                ),
            )

        def start(copies):
            for copy in copies:
                copy.start()

        def grew(number):
            pl.when(number % 3 == 1)(lambda: weights_event(begun + pages + 5 + number // 3))

        def shrinks(number):
            pl.when(number % 2 == 1)(lambda: back_f.event(number // 2))

        def shrank(number):
            pl.when(number % 2 == 1)(lambda: back_f.event(2 + number // 2))

        def left(tile):
            start(dctx_copies(tile))
            pl.when(tile % 2 == 0)(lambda: back_f.event(8 + tile // 2))

        load_x.wait()
        load_og.wait()
        feed_math(
            q,
            dict(
                grew=grew,
                turned=lambda tile: start(out_copies(tile)),
                shrinks=shrinks,
                shrank=shrank,
                left=left,
            ),
        )
        back_f.rest()
        back_f.drain()
        for tile in range(tiles):
            for copy in out_copies(tile) + dctx_copies(tile):
                copy.wait()

    pl.run_scoped(feed, *[pltpu.VMEM(shape, kind) for _, shape, kind in feeds])
    for tree in (tree_v, tree_b, tree_a, tree_e, tree_f):
        tree.drain()


def layer_forward(x, og, corners, omega, pick, shards, plan, inv_tokens):
    tokens, width = x.shape
    cols = shards[1].shape[1]
    heads = cols // HD
    own = tokens // 2
    unit = (width // 16, UNIT)
    kept, used = attend_buffers(heads, tokens)
    feeds = feed_buffers(own, width, 8 * UNIT)
    feeds += [("out", (own, width), BF16), ("dctx", (2, own, UNIT), BF16)]
    free = pl.BlockSpec(memory_space=pl.ANY)
    vmem = pl.BlockSpec(memory_space=pltpu.VMEM)
    inputs = [("x_all", free), ("og_all", free), ("corner", vmem), ("omega", vmem), ("pick", vmem)]
    inputs += [(name, vmem) for name in ("attn", "shard_box", "vectors", "merge", "expand", "shrink")]
    outs = [(name + "_out", shape, kind, free) for name, shape, kind in kept]
    outs += [
        ("w_out", (3, 1, 4, 2, 2, *unit), BF16, free),
        ("box_out", (PE, cols), BF16, vmem),
        ("out_full", (tokens, width), BF16, free),
        ("dctx_full", (tokens, cols), BF16, free),
        ("dh1l", (own, width), BF16, vmem),
        ("ge", (5, 2, 4, 2, 2, *unit), BF16, vmem),
        ("vsum", (VROWS, width), F32, vmem),
        ("sum_f", (4, *unit), F32, vmem),
    ]
    dma = pltpu.SemaphoreType.DMA
    scratch = [
        ("x", pltpu.VMEM((own, width), BF16)),
        ("og", pltpu.VMEM((own, width), BF16)),
        ("vec", pltpu.VMEM((VROWS, width), F32)),
        ("w", pltpu.VMEM((3, 1, 4, 2, 2, *unit), BF16)),
        ("box_gather", pltpu.VMEM((1, 1, 4, 2, 2, PE // 16, cols), F32)),
        ("vec_gather", pltpu.VMEM((1, 2, 4, 2, 2, VROWS, 128), F32)),
        ("we", pltpu.VMEM((5, 2, 4, 2, 2, *unit), BF16)),
        ("ws", pltpu.VMEM((4, 2, 4, 2, 2, *unit), BF16)),
        ("ctxx", pltpu.VMEM((2, own, cols), BF16)),
        ("gs", pltpu.VMEM((4, 2, 4, 2, 2, *unit), BF16)),
        ("fc", pltpu.VMEM((4, 2, 4, 2, *unit), BF16)),
        ("fy", pltpu.VMEM((4, 2, 4, *unit), BF16)),
        ("fz", pltpu.VMEM((4, 3, 2, *unit), BF16)),
        ("fx", pltpu.VMEM((4, *unit), BF16)),
        ("ctx_sem", dma((2, 3))),
        ("a_sem", dma((2, 3, SLOTS))),
        ("b_sem", dma((2, 1, SLOTS))),
        ("v_sem", dma((2, 1, SLOTS))),
        ("e_sem", dma((2, 5, SLOTS))),
        ("f_sem", dma((2, 4, SLOTS))),
        ("back_sem", dma((2, 4, SLOTS))),
        ("load_sem", dma((4,))),
        ("store_sem", dma((len(kept),))),
        ("swap_sem", dma((6, own // TILE))),
    ]
    names = [item[0] for item in inputs + outs + scratch]
    return pl.pallas_call(
        functools.partial(layer_kernel, heads, plan, inv_tokens, names, kept, used, feeds),
        out_shape=[jax.ShapeDtypeStruct(shape, kind) for _, shape, kind, _ in outs],
        in_specs=[item[1] for item in inputs],
        out_specs=[item[3] for item in outs],
        scratch_shapes=[item[1] for item in scratch],
        compiler_params=pltpu.CompilerParams(
            vmem_limit_bytes=VMEM_LIMIT, collective_id=0, has_side_effects=True
        ),
        name="layer_forward",
    )(x, og, corners, omega, pick, *shards)


def pair_place(cols):
    spot = lax.broadcasted_iota(jnp.int32, (cols, 2 * cols), 0)
    lane = lax.broadcasted_iota(jnp.int32, (cols, 2 * cols), 1)
    target = ((spot >> 6) << 7) + HD + (spot & (HD - 1))
    return jnp.where(lane == target, 1.0, 0.0)


def exact_dot(lhs, rhs, dims=NN):
    return lax.dot_general(
        lhs, rhs, dims, precision=lax.Precision.HIGHEST, preferred_element_type=F32
    )


def attend_back_kernel(heads, plan, inv_tokens, *refs):
    inputs, refs = refs[:12], refs[12:]
    if plan is not None:
        load_sem, held, refs = refs[-1], refs[-13:-1], refs[:-13]
        loads = [
            pltpu.make_async_copy(src, dst, load_sem.at[k]) for k, (src, dst) in enumerate(zip(inputs, held))
        ]
        early = (0, 2, 7, 11)
        for k in sorted(range(12), key=lambda k: k not in early):
            loads[k].start()
        inputs = held
    x_ref, w_ref, box_ref, *inputs = inputs
    qa_ref, qtok_ref, kvtok_ref, kt_ref, kft_ref, trig_ref, ctxt_ref, log_ref, dctx_ref = inputs
    cols = heads * HD
    tokens = x_ref.shape[0]
    pages = tokens // PAGE
    m = lax.axis_index("mp")
    piece = PAGE // 2
    pieces = 2 * pages
    lane = lax.broadcasted_iota(jnp.int32, (1, 2 * HD), 1)
    lower = lane < HD
    if plan is None:
        inp_ref, gw_ref, gbox_ref, qvsum_ref, *refs = refs
        kftok, dctxt, boxt, dtok, xt, gbox = refs
        before, after = 0, 0

        def background(number):
            pass
    else:
        dh1_ref, vsum_ref, sumf_ref, pick_ref, full_e, *refs = refs
        inp_ref, sum_e, sum_a, sum_b, sum_v, norm_ref, *refs = refs
        kftok, dctxt, boxt, dtok, xt, gbox, *refs = refs
        came, total_e, full_a, full_b, full_v, land_v, norms, *refs = refs
        ec, ey, ez, ex, ac, ay, az, bc, by, bz, *refs = refs
        e_sem, a_sem, b_sem, v_sem, n_sem, i_sem, loc_sem = refs
        place = Place()
        place.signal_all()
        fill = pltpu.make_async_copy(full_e.at[:, :, :, :, place.c], total_e, loc_sem.at[0])
        fill.start()
        place.wait_all()

        def finish(out):
            def put(chunk, value):
                out[chunk] = value * inv_tokens

            return put

        tree_e = Reduce(
            place, full_e, total_e, dict(c=ec, y=ey, z=ez, x=ex), 5, "cyzx", e_sem, finish(sum_e)
        )
        tree_e.lag, tree_e.held_back = 2, 1
        tree_a = Reduce(place, full_a, None, dict(c=ac, y=ay, z=az), 3, "cyz", a_sem, finish(sum_a))
        tree_b = Reduce(place, full_b, None, dict(c=bc, y=by, z=bz), 1, "cyz", b_sem, finish(sum_b))

        def block_of(rank):
            r = rank % 16
            return full_v.at[rank // 16, r // 4, (r // 2) % 2, r % 2]

        spot = (place.m, place.z, place.y, place.c)
        all_v = Everyone(place, block_of, lambda step: land_v.at[step - 1], v_sem)
        all_n = Everyone(place, lambda rank: norms.at[spot], lambda step: norms.at[spot], n_sem)

        def background(number):
            tree_e.event(number)

        background(0)
        fill.wait()
        for k in early:
            loads[k].wait()

    boxt[...] = box_ref[...].T
    gbox[...] = jnp.zeros_like(gbox)

    def prepare(page, carry):
        rows = aligned(page, PAGE)
        kftok[rows, :] = kft_ref[:, rows].T
        dctxt[:, rows] = dctx_ref[rows, :].T
        xt[:, rows] = x_ref[rows, :].T
        if plan is not None:
            pl.when(page > 0)(lambda: background(page))
        return carry

    lax.fori_loop(0, pages, prepare, 0)
    if plan is not None:
        for k in range(12):
            if k not in early:
                loads[k].wait()

    def attend(step, carry):
        page, pair = step // (heads // 2), step % (heads // 2)
        rows = aligned(page, PAGE)
        own, partner = turn_factors(trig_ref[:, rows])
        pair_lanes = aligned(pair, 2 * HD)
        query_pair = qtok_ref[rows, pair_lanes]
        dctx_pair = dctx_ref[rows, pair_lanes]
        halves = []
        boxes = []
        blank = jnp.zeros((HD, PAGE), BF16)
        for side in range(2):
            head = pair * 2 + side
            lanes = aligned(head, 2 * HD)
            key_value = kvtok_ref[rows, lanes]
            left = jnp.concatenate([kftok[rows, :], key_value], axis=1)
            score = dot(left, jnp.concatenate([qa_ref[head, :, rows], blank], axis=0))
            prob = jnp.exp(score - log_ref[head, :, rows])
            prob_low = prob.astype(BF16)
            head_rows = pl.ds(pl.multiple_of(head * HD, HD), HD)
            dctx_head = dctxt[head_rows, rows]
            grad_prob = dot(
                key_value, jnp.concatenate([blank, dctx_head], axis=0)
            )
            inner = col_sum(dctx_head.astype(F32) * ctxt_ref[head_rows, rows].astype(F32))
            grad_score = (prob * (grad_prob - inner)).astype(BF16)
            if side == 0:
                both = jnp.concatenate([query_pair[:, 0:HD], dctx_pair[:, 0:HD]], axis=1)
            else:
                both = jnp.concatenate([query_pair[:, HD:], dctx_pair[:, HD:]], axis=1)
            from_score = dot(grad_score, both)
            from_prob = dot(prob_low, both)
            grad_kv = jnp.where(lower, from_score, from_prob).astype(BF16)
            dtok[rows, pl.ds(pl.multiple_of(cols + head * 2 * HD, 2 * HD), 2 * HD)] = grad_kv
            keys = jnp.concatenate([kft_ref[:, rows], kt_ref[head_rows, rows]], axis=0)
            grad_query = dot(keys, grad_score) * HD ** (-0.5)
            feat = grad_query[0:PE]
            proj = (feat * own - swap_blocks(feat) * partner).astype(BF16)
            halves.append(grad_query[PE:] + dot(boxt[head_rows, :], proj))
            boxes.append(dot(proj, query_pair))
        gbox[:, pair_lanes] += jnp.where(lower, boxes[0], boxes[1])
        dtok[rows, pair_lanes] = jnp.concatenate(halves, axis=0).astype(BF16).T
        return carry

    def spread(page):
        rows = aligned(page, PAGE)
        return sum(
            dot(dtok[rows, chunk * UNIT : (chunk + 1) * UNIT], w_ref[chunk], NT) for chunk in range(3)
        )

    if plan is None:
        lax.fori_loop(0, pages * (heads // 2), attend, 0)
        gbox_ref[...] = gbox[...] * HD**0.5

        def spread_page(page, carry):
            inp_ref[aligned(page, PAGE), :] = spread(page)
            return carry

        lax.fori_loop(0, pages, spread_page, 0)

        def gather(step, carry):
            lanes = aligned(step, UNIT)
            gw_ref[step] = dot(xt[...], dtok[:, lanes]).astype(BF16)
            qvsum_ref[0:1, lanes] = col_sum(dtok[:, lanes].astype(F32))
            return carry

        lax.fori_loop(0, 3, gather, 0)
        return

    def swap(index):
        rows = aligned(index, piece)
        return remote(
            inp_ref.at[rows, :], came.at[rows, :], i_sem.at[0, index], i_sem.at[1, index], place.peer["x"]
        )

    def attend_and_send(step, carry):
        attend(step, carry)
        page = step // (heads // 2)

        @pl.when(step % (heads // 2) == heads // 2 - 1)
        def _():
            value = spread(page)
            for half in range(2):
                index = 2 * page + half
                rows = aligned(index, piece)
                own = index // pages == m
                spot = aligned(index % pages, piece)
                extra = jnp.where(own, dh1_ref[spot, :].astype(F32), 0.0)
                inp_ref[rows, :] = (value[half * piece : (half + 1) * piece] + extra).astype(BF16)
                swap(index).start()

        background(step + pages)
        return carry

    lax.fori_loop(0, pages * (heads // 2), attend_and_send, 0)
    full_b[0, 0] = (gbox[...] * HD**0.5).reshape(4, 2, 2, PE // 16, cols)

    def gather(step, carry):
        grad = dot(xt[...], dtok[:, aligned(step, UNIT)]).astype(BF16)
        full_a[step, 0] = grad.reshape(full_a.shape[2:])
        tree_a.event(step)
        tree_b.event(step)
        return carry

    lax.fori_loop(0, 3, gather, 0)

    sums = jnp.concatenate(
        [
            col_sum(dtok[:, chunk * UNIT : (chunk + 1) * UNIT].astype(F32)) for chunk in range(3)
        ],
        axis=1,
    )
    values = exact_dot(jnp.broadcast_to(sums[:, cols:], (8, 2 * cols)), pair_place(cols), NT)
    pair = jnp.concatenate([sums[:, 0:cols], values[0:1]], axis=0)
    blank = jnp.zeros_like(pair)
    pair = jnp.where(
        m == 0, jnp.concatenate([pair, blank], axis=1), jnp.concatenate([blank, pair], axis=1)
    )
    table = jnp.concatenate([vsum_ref[0:6, :], pair, vsum_ref[8:, :]], axis=0)
    mp_count, dp_count = plan
    width = table.shape[1]
    each = width // (mp_count * dp_count)
    wide_lane = lax.broadcasted_iota(jnp.int32, (VROWS, width), 1)
    for side in range(mp_count):
        parts = []
        for r in range(dp_count):
            first = (r * mp_count + side) * each
            parts.append(jnp.where((wide_lane >= first) & (wide_lane < first + each), table, 0.0))
        block = exact_dot(jnp.concatenate(parts, axis=0), pick_ref[...], NT)
        full_v[side] = block.reshape(full_v.shape[1:])
    all_v.start()

    def tail(number, carry):
        tree_a.event(number)
        tree_b.event(number)
        return carry

    lax.fori_loop(3, tree_a.events, tail, 0)
    tree_e.rest()
    all_v.wait()
    total_v = full_v[spot] + jnp.sum(land_v[...], axis=0)
    sum_v[0] = total_v * inv_tokens

    square = sum(jnp.sum(out[...] * out[...]) for out in (sum_e, sumf_ref, sum_a, sum_b, sum_v))
    norms[spot] = jnp.full((8, 128), square, F32)
    all_n.start()

    def final(number, carry):
        rows = aligned(number, piece)
        swap(number).wait()
        inp_ref[rows, :] = (inp_ref[rows, :].astype(F32) + came[rows, :].astype(F32)).astype(BF16)
        return carry

    lax.fori_loop(0, pieces, final, 0)
    all_n.wait()
    every = norms[...].reshape(-1, 8, 128)
    norm_ref[...] = jnp.sqrt(sum(every[k] for k in range(every.shape[0])))
    for tree in (tree_e, tree_a, tree_b):
        tree.drain()


def attend_backward(x, weight, box, kept, dctx, plan, inv_tokens, more=()):
    tokens, width = x.shape
    cols = weight.shape[2]
    heads = cols // HD
    vmem = pl.BlockSpec(memory_space=pltpu.VMEM)
    scratch = [
        pltpu.VMEM((tokens, PE), BF16),
        pltpu.VMEM((cols, tokens), BF16),
        pltpu.VMEM((cols, PE), BF16),
        pltpu.VMEM((tokens, 3 * cols), BF16),
        pltpu.VMEM((width, tokens), BF16),
        pltpu.VMEM((PE, cols), F32),
    ]
    in_specs = [vmem] * 12
    if plan is None:
        shapes = [
            ((tokens, width), F32),
            ((3, width, cols), BF16),
            ((PE, cols), F32),
            ((8, 3 * cols), F32),
        ]
        extra = {}
    else:
        free = pl.BlockSpec(memory_space=pl.ANY)
        in_specs = [free] * 12 + [vmem] * 4 + [free]
        rows = width // 16
        unit = (rows, UNIT)
        tile = (PE // 16, cols)
        small = (VROWS, 128)
        shapes = [
            ((tokens, width), BF16),
            ((5, *unit), F32),
            ((3, *unit), F32),
            ((1, *tile), F32),
            ((1, *small), F32),
            ((8, 128), F32),
        ]
        scratch += [
            pltpu.VMEM((tokens, width), BF16),
            pltpu.VMEM((5, 2, 4, 2, *unit), BF16),
            pltpu.VMEM((3, 1, 4, 2, 2, *unit), BF16),
            pltpu.VMEM((1, 1, 4, 2, 2, *tile), F32),
            pltpu.VMEM((2, 4, 2, 2, *small), F32),
            pltpu.VMEM((31, *small), F32),
            pltpu.VMEM((2, 4, 2, 2, 8, 128), F32),
            pltpu.VMEM((5, 2, 4, 2, *unit), BF16),
            pltpu.VMEM((5, 2, 4, *unit), BF16),
            pltpu.VMEM((5, 3, 2, *unit), BF16),
            pltpu.VMEM((5, *unit), BF16),
            pltpu.VMEM((3, 4, 2, *unit), BF16),
            pltpu.VMEM((3, 4, *unit), BF16),
            pltpu.VMEM((3, 3, *unit), BF16),
            pltpu.VMEM((1, 4, 2, *tile), F32),
            pltpu.VMEM((1, 4, *tile), F32),
            pltpu.VMEM((1, 3, *tile), F32),
            pltpu.SemaphoreType.DMA((2, 5, SLOTS)),
            pltpu.SemaphoreType.DMA((2, 3, SLOTS)),
            pltpu.SemaphoreType.DMA((2, 1, SLOTS)),
            pltpu.SemaphoreType.DMA((2, 31)),
            pltpu.SemaphoreType.DMA((2, 31)),
            pltpu.SemaphoreType.DMA((2, 2 * (tokens // PAGE))),
            pltpu.SemaphoreType.DMA((2,)),
        ]
        scratch += [pltpu.VMEM(array.shape, array.dtype) for array in (x, weight, box, *kept, dctx)]
        scratch.append(pltpu.SemaphoreType.DMA((12,)))
        extra = dict(collective_id=2, has_side_effects=True)
    return pl.pallas_call(
        functools.partial(attend_back_kernel, heads, plan, inv_tokens),
        out_shape=[jax.ShapeDtypeStruct(s, d) for s, d in shapes],
        in_specs=in_specs,
        out_specs=[vmem] * len(shapes),
        scratch_shapes=scratch,
        compiler_params=pltpu.CompilerParams(vmem_limit_bytes=VMEM_LIMIT, **extra),
        name="attend_backward",
    )(x, weight, box, *kept, dctx, *more)


def adam_step(master, first, second, gradient, rate, decay):
    new_first = BETA_ONE * first + (1.0 - BETA_ONE) * gradient
    new_second = BETA_TWO * second + (1.0 - BETA_TWO) * gradient * gradient
    first_hat = new_first / (1.0 - BETA_ONE**STEP)
    second_hat = new_second / (1.0 - BETA_TWO**STEP)
    new_master = master - rate * (first_hat / (jnp.sqrt(second_hat) + ADAM_EPS) + decay * master)
    return (new_first, new_second, new_master)


def adam_kernel(heads, norm_ref, *refs):
    sum_e, sum_f, sum_a, sum_b, sum_v, *refs = refs
    states, wholes, outs = refs[:18], refs[18:20], refs[20:-1]
    moves = [
        pltpu.make_async_copy(src, dst, refs[-1].at[k])
        for k, (src, dst) in enumerate(zip(wholes, outs[-2:]))
    ]
    for copy in moves:
        copy.start()
    outs[-3][...] = norm_ref[0:1, 0:1]
    clip = CLIP_LIMIT / jnp.maximum(norm_ref[0:1, 0:1], CLIP_LIMIT)

    def update(first, out, gradient, at, rate, decay):
        news = adam_step(*(ref[at] for ref in states[first : first + 3]), gradient * clip, rate, decay)
        for ref, new in zip(outs[out : out + 3], news):
            ref[at] = new
        if decay:
            outs[out + 3][at] = news[2].astype(BF16)

    def heads_of(kind):
        half = heads // 2
        return jnp.concatenate(
            [
                sum_a[1 + head // half, :, (2 * (head % half) + kind) * HD : (2 * (head % half) + kind + 1) * HD]
                for head in range(heads)
            ],
            axis=1,
        )

    for index, gradient in enumerate((sum_a[0], heads_of(0), heads_of(1))):
        update(0, 0, gradient, index, RATE_MATRIX, WEIGHT_DECAY)
    update(3, 4, sum_b[0], ALL, RATE_MATRIX, WEIGHT_DECAY)
    update(6, 8, sum_e[0], ALL, RATE_MATRIX, WEIGHT_DECAY)
    for chunk in range(4):
        lanes = (ALL, slice(chunk * UNIT, (chunk + 1) * UNIT))
        update(9, 12, sum_e[1 + chunk], lanes, RATE_MATRIX, WEIGHT_DECAY)
        update(12, 16, sum_f[chunk], lanes, RATE_MATRIX, WEIGHT_DECAY)
    rows, each = states[15].shape
    update(15, 20, sum_v[0, 0:rows, 0:each], ALL, RATE_VECTOR, 0.0)
    for copy in moves:
        copy.wait()


def adam_all(norm, sums, states, wholes):
    shapes = []
    for first in range(0, 18, 3):
        shapes += [(states[first].shape, F32)] * 3
        if first < 15:
            shapes.append((states[first].shape, BF16))
    vmem = pl.BlockSpec(memory_space=pltpu.VMEM)
    free = pl.BlockSpec(memory_space=pl.ANY)
    shapes.append(((1, 1), F32))
    shapes += [(array.shape, array.dtype) for array in wholes]
    return pl.pallas_call(
        functools.partial(adam_kernel, states[0].shape[2] // HD),
        out_shape=[jax.ShapeDtypeStruct(s, d) for s, d in shapes],
        in_specs=[vmem] * (6 + len(states)) + [free] * 2,
        out_specs=[vmem] * (len(shapes) - 2) + [free] * 2,
        scratch_shapes=[pltpu.SemaphoreType.DMA((2,))],
        compiler_params=pltpu.CompilerParams(vmem_limit_bytes=VMEM_LIMIT),
        name="adam_all",
    )(norm, *sums, *states, *wholes)


def pack_qkv(shard):
    rows, cols = shard.shape[1:]
    heads = cols // HD
    pairs = jnp.stack([shard[1].reshape(rows, heads, HD), shard[2].reshape(rows, heads, HD)], axis=2)
    pairs = pairs.reshape(rows, 2, cols)
    return jnp.stack([shard[0], pairs[:, 0], pairs[:, 1]])


def unpack_qkv(packed):
    rows, cols = packed.shape[1:]
    pairs = jnp.concatenate([packed[1], packed[2]], axis=1).reshape(rows, cols // HD, 2, HD)
    return jnp.stack(
        [packed[0], pairs[:, :, 0].reshape(rows, cols), pairs[:, :, 1].reshape(rows, cols)]
    )


def to_chunks(shard):
    rows = shard.shape[0]
    return shard.reshape(rows, -1, UNIT).transpose(1, 0, 2)


def from_chunks(chunks):
    return chunks.transpose(1, 0, 2).reshape(chunks.shape[1], -1)


def on_device(
    layer_input,
    page_boxes,
    output_grad,
    attn_proj,
    attn_first,
    attn_second,
    box_proj,
    box_first,
    box_second,
    merge_proj,
    merge_first,
    merge_second,
    expand_proj,
    expand_first,
    expand_second,
    shrink_proj,
    shrink_first,
    shrink_second,
    vectors,
    vector_first,
    vector_second,
):
    mp_count = lax.axis_size("mp")
    dp_count = lax.axis_size("dp")
    mp_index = lax.axis_index("mp")
    tokens, width = layer_input.shape
    cols = attn_proj.shape[2]
    heads = cols // HD
    own_tokens = tokens // mp_count
    inv_tokens = 1.0 / (tokens * dp_count)

    corners = page_boxes.T
    omega = (10000.0 ** (-np.arange(FREQS, dtype=np.float64) / FREQS)).astype(np.float32)[:, None]
    omega = jnp.asarray(omega)
    plan = (mp_count, dp_count) if dp_count == 16 and mp_count == 2 else None
    if plan is not None:
        each = vectors.shape[1]
        pick = np.zeros((128, width), np.float32)
        pick[np.arange(width) % each, np.arange(width)] = 1.0
        pick = jnp.asarray(pick)
        *kept, w_qkv, w_box, layer_out, dctx, dh1, g_expand, vec_sum, sum_f = layer_forward(
            layer_input,
            output_grad,
            corners,
            omega,
            pick,
            (attn_proj, box_proj, vectors, merge_proj.T, expand_proj, shrink_proj.T),
            plan,
            inv_tokens,
        )
        input_grad, sum_e, sum_a, sum_b, sum_v, norm = attend_backward(
            layer_input,
            w_qkv.reshape(3, width, cols),
            w_box,
            kept,
            dctx,
            plan,
            inv_tokens,
            (dh1, vec_sum, sum_f, pick, g_expand),
        )
        merge = [merge_proj.T, merge_first.T, merge_second.T]
        shrink = [shrink_proj.T, shrink_first.T, shrink_second.T]
        *results, norm, layer_out, input_grad = adam_all(
            norm,
            (sum_e, sum_f, sum_a, sum_b, sum_v),
            [attn_proj, attn_first, attn_second, box_proj, box_first, box_second, *merge]
            + [expand_proj, expand_first, expand_second, *shrink, vectors, vector_first, vector_second],
            (layer_out, input_grad),
        )
        turned = (8, 9, 10, 11, 16, 17, 18, 19)
        results = [out.T if k in turned else out for k, out in enumerate(results)]
        return (layer_out, input_grad, norm.reshape(()), *results)
    shard_qkv = pack_qkv(attn_proj).astype(BF16)
    shard_e = jnp.concatenate([merge_proj.T[None], to_chunks(expand_proj)]).astype(BF16)
    shard_f = to_chunks(shrink_proj.T).astype(BF16)
    w_qkv = lax.all_gather(shard_qkv, "dp", axis=1, tiled=True)
    w_box = lax.all_gather(box_proj.astype(BF16), "dp", axis=0, tiled=True)
    w_expand = lax.all_gather(lax.all_gather(shard_e, "dp", axis=1, tiled=True), "mp", axis=1)
    w_shrink = lax.all_gather(lax.all_gather(shard_f, "dp", axis=1, tiled=True), "mp", axis=1)
    vecs = lax.all_gather(vectors, ("dp", "mp"), axis=1, tiled=True)
    vecs = jnp.pad(vecs, ((0, VROWS - vecs.shape[0]), (0, 0)))
    *kept, context = attend_forward(layer_input, corners, omega, w_qkv, w_box, vecs)
    context = lax.all_to_all(
        context.reshape(mp_count, own_tokens, cols), "mp", split_axis=0, concat_axis=0
    )

    def own_rows(array):
        return lax.dynamic_slice_in_dim(array, mp_index * own_tokens, own_tokens)

    layer_out, dctx, dh1, g_expand, g_shrink, vec_sum = feed_both(
        own_rows(layer_input), own_rows(output_grad), context, w_expand, w_shrink, vecs
    )
    g_feed = jnp.concatenate([g_expand, g_shrink])
    layer_out = lax.all_gather(layer_out, "mp", axis=0, tiled=True)
    dctx = lax.all_to_all(dctx, "mp", split_axis=0, concat_axis=0).reshape(tokens, cols)
    part, g_qkv, g_box, qkv_sum = attend_backward(
        layer_input, w_qkv, w_box, kept, dctx, None, inv_tokens
    )
    own_part = lax.psum_scatter(part.astype(BF16), "mp", scatter_dimension=0, tiled=True)
    own_grad = (own_part.astype(F32) + dh1).astype(BF16)
    input_grad = lax.all_gather(own_grad, "mp", axis=0, tiled=True)
    shard_attn = unpack_qkv(
        lax.psum_scatter(g_qkv, "dp", scatter_dimension=1, tiled=True).astype(F32) * inv_tokens
    )
    shard_box = lax.psum_scatter(g_box, "dp", scatter_dimension=0, tiled=True) * inv_tokens
    sum_feed = lax.psum_scatter(g_feed, "dp", scatter_dimension=2, tiled=True)
    sum_feed = lax.psum_scatter(sum_feed, "mp", scatter_dimension=1, tiled=True)[:, 0]
    sum_feed = sum_feed.astype(F32) * inv_tokens
    sum_expand, sum_shrink = sum_feed[0:5], sum_feed[5:]

    def placed(row):
        return lax.dynamic_update_slice_in_dim(
            jnp.zeros((width,), F32), row, mp_index * cols, 0
        )[None, :]

    value_sum = qkv_sum[0, cols:].reshape(heads, 2, HD)[:, 1].reshape(cols)
    vector_grad = jnp.concatenate(
        [vec_sum[0:6], placed(qkv_sum[0, 0:cols]), placed(value_sum), vec_sum[8:12]]
    )
    vector_shard = (
        lax.psum_scatter(vector_grad, ("dp", "mp"), scatter_dimension=1, tiled=True) * inv_tokens
    )
    square = sum(
        jnp.sum(shard * shard)
        for shard in (shard_attn, shard_box, sum_expand, sum_shrink, vector_shard)
    )
    grad_norm = jnp.sqrt(lax.psum(square, ("dp", "mp")))
    shard_merge = sum_expand[0].T
    shard_expand = from_chunks(sum_expand[1:])
    shard_shrink = from_chunks(sum_shrink).T
    clip_scale = CLIP_LIMIT / jnp.maximum(grad_norm, CLIP_LIMIT)
    results = [layer_out, input_grad, grad_norm]
    for master, first, second, shard in (
        (attn_proj, attn_first, attn_second, shard_attn),
        (box_proj, box_first, box_second, shard_box),
        (merge_proj, merge_first, merge_second, shard_merge),
        (expand_proj, expand_first, expand_second, shard_expand),
        (shrink_proj, shrink_first, shrink_second, shard_shrink),
    ):
        new_first, new_second, new_master = adam_step(
            master, first, second, shard * clip_scale, RATE_MATRIX, WEIGHT_DECAY
        )
        results += [new_first, new_second, new_master, new_master.astype(BF16)]
    results += adam_step(
        vectors, vector_first, vector_second, vector_shard * clip_scale, RATE_VECTOR, 0.0
    )
    return tuple(results)


def solution(mesh):
    rows = P("dp", None)
    attn = P(None, "dp", "mp")
    tall = P("dp", "mp")
    wide = P("mp", "dp")
    vector = P(None, ("dp", "mp"))
    in_specs = (rows,) * 3 + (attn,) * 3 + (tall,) * 3 + (wide,) * 3 + (tall,) * 3 + (wide,) * 3
    in_specs += (vector,) * 3
    out_specs = (rows, rows, P()) + (attn,) * 4 + (tall,) * 4 + (wide,) * 4 + (tall,) * 4
    out_specs += (wide,) * 4 + (vector,) * 3
    return jax.shard_map(
        on_device, mesh=mesh, in_specs=in_specs, out_specs=out_specs, check_vma=False
    )
```

```python
import functools
import types

import jax
import jax.numpy as jnp
import numpy as np
from jax import lax
from jax.experimental import pallas as pl
from jax.experimental.pallas import tpu as pltpu
from jax.sharding import PartitionSpec as P

HD = 64
FREQS = 32
PE = 128
PAGE = 512
STEP = 10

NORM_EPS = 1e-12
CLIP_LIMIT = 0.1
BETA_ONE = 0.9
BETA_TWO = 0.999
ADAM_EPS = 1e-08
RATE_MATRIX = 0.05
RATE_VECTOR = 0.5
WEIGHT_DECAY = 0.01

F32 = jnp.float32
BF16 = jnp.bfloat16
VMEM_LIMIT = 60 * 1024 * 1024

NN = (((1,), (0,)), ((), ()))
NT = (((1,), (1,)), ((), ()))
TN = (((0,), (0,)), ((), ()))


def dot(lhs, rhs, dims=NN):
    return lax.dot_general(lhs, rhs, dims, preferred_element_type=F32)


def aligned(index, size):
    return pl.ds(pl.multiple_of(index * size, size), size)


def swap_blocks(feat):
    return jnp.concatenate(
        [
            feat[FREQS : 2 * FREQS],
            feat[0:FREQS],
            feat[3 * FREQS :],
            feat[2 * FREQS : 3 * FREQS],
        ],
        axis=0,
    )


def turn_factors(trig):
    cos_x, sin_x = trig[0:FREQS], trig[FREQS : 2 * FREQS]
    cos_y, sin_y = trig[2 * FREQS : 3 * FREQS], trig[3 * FREQS :]
    return (
        jnp.concatenate([sin_x, sin_x, sin_y, sin_y], axis=0),
        jnp.concatenate([cos_x, -cos_x, cos_y, -cos_y], axis=0),
    )


MESH = pl.DeviceIdType.MESH
ALL = slice(None)
UNIT = 384


class Place:
    def __init__(self):
        rank = lax.axis_index("dp")
        self.m = lax.axis_index("mp")
        self.z = rank // 4
        self.y = (rank // 2) % 2
        self.c = rank % 2
        self.peer = {
            "x": (rank, 1 - self.m),
            "y": (rank + 2 - 4 * self.y, self.m),
            "c": (rank + 1 - 2 * self.c, self.m),
        }
        self.far = [((rank + 4 * step) % 16, self.m) for step in (1, 2, 3)]

    def signal(self):
        barrier = pltpu.get_barrier_semaphore()
        for device in list(self.peer.values()) + self.far:
            pl.semaphore_signal(barrier, inc=1, device_id=device, device_id_type=MESH)

    def wait(self):
        pl.semaphore_wait(pltpu.get_barrier_semaphore(), 6)

    def signal_all(self):
        barrier = pltpu.get_barrier_semaphore()
        rank = self.m * 16 + lax.axis_index("dp")

        def one(step, carry):
            to = (rank + step) % 32
            pl.semaphore_signal(barrier, inc=1, device_id=(to % 16, to // 16), device_id_type=MESH)
            return carry

        lax.fori_loop(1, 32, one, 0)

    def wait_all(self):
        pl.semaphore_wait(pltpu.get_barrier_semaphore(), 31)


def remote(src, dst, send_sem, recv_sem, device):
    return pltpu.make_async_remote_copy(
        src_ref=src,
        dst_ref=dst,
        send_sem=send_sem,
        recv_sem=recv_sem,
        device_id=device,
        device_id_type=MESH,
    )


SLOT = {"c": 0, "z": 1, "y": 4, "x": 5}
SLOTS = 6


class Tree:
    lag = 1
    held_back = 0

    def stage(self, index, chunk):
        raise NotImplementedError

    def event(self, number):
        for index in range(self.count - 1 - self.held_back, -1, -1):
            chunk = number - index * self.lag
            if self.chunks == 1:
                pl.when(chunk == 0)(lambda index=index: self.stage(index, 0))
            else:
                pl.when((chunk >= 0) & (chunk < self.chunks))(
                    lambda index=index, chunk=chunk: self.stage(index, chunk)
                )

    @property
    def events(self):
        return self.chunks + (self.count - 1 - self.held_back) * self.lag

    def rest(self):
        def one(chunk, carry):
            self.stage(self.count - 1, chunk)
            return carry

        lax.fori_loop(0, self.chunks, one, 0)


class Spread(Tree):
    def __init__(self, place, ref, chunks, order, sems):
        self.chunks, self.ref, self.sems, self.place = chunks, ref, sems, place
        have = {"x": place.m if "x" in order else 0, "z": place.z, "y": place.y}
        mine = {"x": place.m, "y": place.y}
        self.own = have
        self.steps = []
        for axis in order:
            if axis == "z":
                sends = [(have, place.far[step - 1], step) for step in (1, 2, 3)]
                waits = [(dict(have, z=(place.z + 4 - step) % 4), step) for step in (1, 2, 3)]
            else:
                sends = [(have, place.peer[axis], SLOT[axis])]
                waits = [(dict(have, **{axis: 1 - mine[axis]}), SLOT[axis])]
            self.steps.append((sends, waits))
            have = dict(have, **{axis: ALL})
        self.other = place.peer["c"]
        self.count = len(self.steps) + 2

    def _copy(self, chunk, have, device, slot):
        block = self.ref.at[chunk, self.place.c, have["x"], have["z"], have["y"]]
        return remote(block, block, self.sems.at[0, chunk, slot], self.sems.at[1, chunk, slot], device)

    def _plane(self, chunk, core):
        plane = self.ref.at[chunk, core]
        return remote(plane, plane, self.sems.at[0, chunk, 0], self.sems.at[1, chunk, 0], self.other)

    def stage(self, index, chunk):
        if index == self.count - 1:
            self._plane(chunk, 1 - self.place.c).wait_recv()
            return
        came = [self.own]
        if index > 0:
            came = []
            for have, slot in self.steps[index - 1][1]:
                self._copy(chunk, have, self.other, slot).wait_recv()
                came.append(have)
        if index < len(self.steps):
            for have, device, slot in self.steps[index][0]:
                self._copy(chunk, have, device, slot).start()
        for have in came:
            self._copy(chunk, have, self.other, 0).start()

    def drain(self):
        def one(chunk, carry):
            for sends, _ in self.steps:
                for have, device, slot in sends:
                    self._copy(chunk, have, device, slot).wait_send()
            self._plane(chunk, self.place.c).wait_send()
            return carry

        lax.fori_loop(0, self.chunks, one, 0)


RANKS = [(c, z, y) for z in range(4) for y in range(2) for c in range(2)]


def natural(ref, chunk, side):
    return jnp.concatenate([ref[chunk, c, side, z, y] for c, z, y in RANKS], axis=0)


def put_natural(ref, chunk, side, value):
    rows = value.shape[0] // len(RANKS)
    for spot, (c, z, y) in enumerate(RANKS):
        ref[chunk, c, side, z, y] = value[spot * rows : (spot + 1) * rows]


class Reduce(Tree):
    def __init__(self, place, full, total, lands, chunks, order, sems, finish):
        self.place, self.full, self.total, self.lands = place, full, total, lands
        self.chunks, self.sems, self.finish = chunks, sems, finish
        mine = {"x": place.m, "y": place.y}
        self.across = ALL if "x" in order else 0
        have = {"x": self.across, "z": ALL, "y": ALL}
        self.order, self.haves = order, []
        for axis in order:
            before = have
            if axis != "c":
                have = dict(have, **{axis: place.z if axis == "z" else mine[axis]})
            self.haves.append((before, have))
        self.count = len(order) + 1

    def _at(self, chunk, have):
        if self.total is None:
            return self.full.at[chunk, self.place.c, have["x"], have["z"], have["y"]]
        return self.total.at[chunk, have["x"], have["z"], have["y"]]

    def _copies(self, index, chunk):
        axis, (before, _) = self.order[index], self.haves[index]
        place, land = self.place, self.lands[axis]

        def copy(src, dst, slot, device):
            return remote(src, dst, self.sems.at[0, chunk, slot], self.sems.at[1, chunk, slot], device)

        if axis == "c":
            source = self.full.at[chunk, 1 - place.c, self.across]
            return [copy(source, land.at[chunk], SLOT[axis], place.peer[axis])]
        if axis == "z":
            return [
                copy(
                    self._at(chunk, dict(before, z=(place.z + step) % 4)),
                    land.at[chunk, step - 1],
                    step,
                    place.far[step - 1],
                )
                for step in (1, 2, 3)
            ]
        other = 1 - (place.m if axis == "x" else place.y)
        source = self._at(chunk, dict(before, **{axis: other}))
        return [copy(source, land.at[chunk], SLOT[axis], place.peer[axis])]

    def stage(self, index, chunk):
        if index > 0:
            axis, (_, have) = self.order[index - 1], self.haves[index - 1]
            land = self.lands[axis]
            for copy in self._copies(index - 1, chunk):
                copy.wait_recv()
            mine = self._at(chunk, have)
            last = index == self.count - 1
            if axis == "z":
                value = mine[...].astype(F32)
                for step in range(3):
                    value += land[chunk, step].astype(F32)
            elif last:
                value = mine[...].astype(F32) + land[chunk].astype(F32)
            else:
                value = mine[...] + land[chunk]
            if last:
                self.finish(chunk, value)
            else:
                mine[...] = value.astype(mine.dtype)
        if index < self.count - 1:
            for copy in self._copies(index, chunk):
                copy.start()

    def drain(self):
        def one(chunk, carry):
            for index in range(self.count - 1):
                for copy in self._copies(index, chunk):
                    copy.wait_send()
            return carry

        lax.fori_loop(0, self.chunks, one, 0)


class Everyone:
    def __init__(self, place, send_block, land_block, sems):
        self.rank = place.m * 16 + lax.axis_index("dp")
        self.send_block, self.land_block, self.sems = send_block, land_block, sems

    def _copy(self, step):
        to = (self.rank + step) % 32
        return remote(
            self.send_block(to),
            self.land_block(step),
            self.sems.at[0, step - 1],
            self.sems.at[1, step - 1],
            (to % 16, to // 16),
        )

    def _each(self, act):
        def one(step, carry):
            act(self._copy(step))
            return carry

        lax.fori_loop(1, 32, one, 0)

    def start(self):
        self._each(lambda copy: copy.start())

    def wait(self):
        self._each(lambda copy: copy.wait())


VROWS = 16


def rows_from_blocks(blocks, pick, counts):
    mp_count, dp_count = counts
    width = pick.shape[1]
    each = width // (mp_count * dp_count)
    wide = lax.dot_general(
        blocks, pick, NN, precision=lax.Precision.HIGHEST, preferred_element_type=F32
    )
    lane = lax.broadcasted_iota(jnp.int32, (VROWS, width), 1)
    table = jnp.zeros((VROWS, width), F32)
    for m in range(mp_count):
        for r, (c, z, y) in enumerate(RANKS):
            first = (r * mp_count + m) * each
            row = (((c * mp_count + m) * 4 + z) * 2 + y) * VROWS
            table += jnp.where((lane >= first) & (lane < first + each), wide[row : row + VROWS], 0.0)
    return table


def attend_setup(heads, m, box_full, vec_ref, box_heads, bias):
    cols = heads * HD
    for head in range(heads):
        box_heads[head] = box_full[:, head * HD : (head + 1) * HD]
    width = vec_ref.shape[1]
    own = jnp.where(m == 0, vec_ref[6:8, 0:cols], vec_ref[6:8, width - cols :])
    spread = exact_dot(jnp.broadcast_to(own[1:2], (8, cols)), pair_place(cols))
    bias[0:1, 0:cols] = own[0:1]
    bias[0:1, cols:] = spread[0:1]


def attend_trig(omega_ref, corner_ref, trig_ref):
    corner = corner_ref[...].astype(F32)
    angle_x = omega_ref[...] * ((corner[0:1] + corner[2:3]) * 0.5)
    angle_y = omega_ref[...] * ((corner[1:2] + corner[3:4]) * 0.5)
    trig_ref[0:FREQS, :] = jnp.cos(angle_x)
    trig_ref[FREQS : 2 * FREQS, :] = jnp.sin(angle_x)
    trig_ref[2 * FREQS : 3 * FREQS, :] = jnp.cos(angle_y)
    trig_ref[3 * FREQS :, :] = jnp.sin(angle_y)


def quiet(*args):
    return None


def attend_math(heads, r, weights, page_of, projected, attended):
    cols = heads * HD
    pages = r.x.shape[0] // PAGE

    def project(page, carry):
        rows = aligned(page, PAGE)
        tokens = r.x[rows, :]
        query = dot(tokens, weights(0)) + r.bias[0:1, 0:cols]
        query = query.astype(BF16) * HD ** (-0.5)
        r.qtok[rows, :] = query
        qa_rows = query.T
        for half in range(2):
            lanes = slice(half * cols, (half + 1) * cols)
            pair = dot(tokens, weights(1 + half)) + r.bias[0:1, cols + half * cols : 2 * cols + half * cols]
            pair = pair.astype(BF16)
            r.kvtok[rows, lanes] = pair
            turned = pair.T
            for spot in range(heads // 2):
                head_rows = slice((half * heads // 2 + spot) * HD, (half * heads // 2 + spot + 1) * HD)
                r.kt[head_rows, rows] = turned[2 * spot * HD : (2 * spot + 1) * HD]
                r.vt[head_rows, rows] = turned[(2 * spot + 1) * HD : (2 * spot + 2) * HD]
        trig = r.trig[:, rows]
        kft = trig.astype(BF16)
        r.kft[:, rows] = kft
        r.kftok[rows, :] = kft.T
        own, partner = turn_factors(trig)
        for head in range(heads):
            query_head = qa_rows[head * HD : (head + 1) * HD]
            proj = dot(r.box_heads[head], query_head)
            feat = proj * own + swap_blocks(proj) * partner
            r.qa[head, 0:PE, rows] = feat.astype(BF16)
            r.qa[head, PE : PE + HD, rows] = query_head
        projected(page)
        return carry

    lax.fori_loop(0, pages, project, 0)

    def attend(step, carry):
        turn, pair = step // (heads // 2), step % (heads // 2)
        rows = aligned(page_of(turn), PAGE)
        halves = []
        blank = jnp.zeros((HD, PAGE), BF16)
        for side in range(2):
            head = pair * 2 + side
            lanes = aligned(head, 2 * HD)
            left = jnp.concatenate([r.kftok[rows, :], r.kvtok[rows, lanes]], axis=1)
            score = dot(left, jnp.concatenate([r.qa[head, :, rows], blank], axis=0))
            top = jnp.max(score, axis=0, keepdims=True)
            weight = jnp.exp(score - top)
            total = jnp.sum(weight, axis=0, keepdims=True)
            value = r.vt[aligned(head, HD), rows]
            halves.append(dot(value, weight.astype(BF16)) * (1.0 / total))
            r.log[head, :, rows] = top + jnp.log(total)
        both = jnp.concatenate(halves, axis=0).astype(BF16)
        lanes = aligned(pair, 2 * HD)
        r.ctxt[lanes, rows] = both
        r.ctx[rows, lanes] = both.T
        attended(step, turn, pair)
        return carry

    lax.fori_loop(0, pages * (heads // 2), attend, 0)


def attend_buffers(heads, tokens):
    cols = heads * HD
    kept = [
        ("qa", (heads, PE + HD, tokens), BF16),
        ("qtok", (tokens, cols), BF16),
        ("kvtok", (tokens, 2 * cols), BF16),
        ("kt", (cols, tokens), BF16),
        ("kft", (PE, tokens), BF16),
        ("trig", (PE, tokens), F32),
        ("ctxt", (cols, tokens), BF16),
        ("log", (heads, 1, tokens), F32),
    ]
    used = [
        ("kftok", (tokens, PE), BF16),
        ("box_heads", (heads, PE, HD), BF16),
        ("bias", (8, 3 * cols), F32),
        ("ctx", (tokens, cols), BF16),
        ("vt", (cols, tokens), BF16),
    ]
    return kept, used


def attend_kernel(heads, names, *refs):
    r = types.SimpleNamespace(**dict(zip(names, refs)))
    attend_setup(heads, lax.axis_index("mp"), r.box, r.vec, r.box_heads, r.bias)
    attend_trig(r.omega, r.corner, r.trig)
    attend_math(heads, r, lambda chunk: r.w[chunk], lambda turn: turn, quiet, quiet)


def attend_forward(x, corners, omega, w_qkv, w_box, vecs):
    tokens = x.shape[0]
    heads = w_box.shape[1] // HD
    kept, used = attend_buffers(heads, tokens)
    outs = kept + [used[3]]
    scratch = used[:3] + used[4:]
    names = ["x", "corner", "omega", "w", "box", "vec"] + [item[0] for item in outs + scratch]
    vmem = pl.BlockSpec(memory_space=pltpu.VMEM)
    return pl.pallas_call(
        functools.partial(attend_kernel, heads, names),
        out_shape=[jax.ShapeDtypeStruct(shape, kind) for _, shape, kind in outs],
        in_specs=[vmem] * 6,
        out_specs=[vmem] * len(outs),
        scratch_shapes=[pltpu.VMEM(shape, kind) for _, shape, kind in scratch],
        compiler_params=pltpu.CompilerParams(vmem_limit_bytes=VMEM_LIMIT),
        name="attend_forward",
    )(x, corners, omega, w_qkv, w_box, vecs)


TILE = 256


def norm_stats(value):
    mean = jnp.mean(value, axis=-1, keepdims=True)
    centred = value - mean
    var = jnp.mean(centred * centred, axis=-1, keepdims=True)
    return centred, lax.rsqrt(var + NORM_EPS)


def norm_back(grad_normed, normed, scale):
    first = jnp.mean(grad_normed, axis=-1, keepdims=True)
    second = jnp.mean(grad_normed * normed, axis=-1, keepdims=True)
    return scale * (grad_normed - first - normed * second)


def col_sum(value):
    return jnp.sum(value, axis=0, keepdims=True)


def feed_math(r, hooks):
    hook = {name: quiet for name in ("entered", "grew", "turned", "shrinks", "shrank", "left")}
    hook.update(hooks)
    tokens = r.x.shape[0]
    sides = r.ctxx.shape[0]
    per_side = (r.we.shape[0] - 1) // 2
    steps = sides * per_side
    tiles = tokens // TILE
    wide = 2 * UNIT
    sum2 = dnorm = r.sum2

    def flat(ref, chunk, side):
        return ref[chunk, side] if len(ref.shape) == 4 else natural(ref, chunk, side)

    def put(ref, chunk, side, value):
        if len(ref.shape) == 4:
            ref[chunk, side] = value
        else:
            put_natural(ref, chunk, side, value)

    def two(ref, first, side):
        return jnp.concatenate([flat(ref, first, side), flat(ref, first + 1, side)], axis=1)

    def w_expand(step):
        return two(r.we, 1 + 2 * (step % per_side), step // per_side)

    def w_shrink(step):
        return two(r.ws, 2 * (step % per_side), step // per_side)

    def put_two(ref, first, side, value):
        put(ref, first, side, value[:, 0:UNIT])
        put(ref, first + 1, side, value[:, UNIT:])

    def by_halves(number):
        return (number % sides) * per_side + number // sides

    def enter(tile, carry):
        rows = aligned(tile, TILE)
        total = r.x[rows, :].astype(F32) + r.vec[4:5, :]
        for side in range(sides):
            total += dot(r.ctxx[side, rows, :], flat(r.we, 0, side), NT)
        centred, scale = norm_stats(total)
        normed = centred * scale
        r.norm1[rows, :] = normed
        r.scale1[rows, :] = scale
        shifted = normed * r.vec[0:1, :] + r.vec[1:2, :]
        r.al[rows, :] = shifted.astype(BF16)
        sum2[rows, :] = shifted + r.vec[5:6, :]
        return carry

    lax.fori_loop(0, tiles, enter, 0)
    hook["entered"]()

    def grow(number, carry):
        step = by_halves(number)
        whole = aligned(step, wide)

        def one(tile, inner):
            rows = aligned(tile, TILE)
            pre = dot(r.al[rows, :], w_expand(step)) + r.vec[pl.ds(8 + step, 1), :]
            phi = 0.5 + 0.5 * lax.erf(pre * 2.0 ** (-0.5))
            density = jnp.exp(pre * pre * -0.5) * (0.5 / jnp.pi) ** 0.5
            low = (pre * phi).astype(BF16)
            r.act[rows, whole] = low
            r.slope[rows, whole] = (phi + pre * density).astype(BF16)
            sum2[rows, :] += dot(low, w_shrink(step), NT)
            hook["grew"](number * tiles + tile)
            return inner

        lax.fori_loop(0, tiles, one, 0)
        return carry

    lax.fori_loop(0, steps, grow, 0)
    r.vsum[...] = jnp.zeros_like(r.vsum)

    def turn(tile, carry):
        rows = aligned(tile, TILE)
        centred, scale = norm_stats(sum2[rows, :])
        normed = centred * scale
        r.out[rows, :] = (normed * r.vec[2:3, :] + r.vec[3:4, :]).astype(BF16)
        grad = r.og[rows, :].astype(F32)
        r.vsum[2:3, :] += col_sum(grad * normed)
        r.vsum[3:4, :] += col_sum(grad)
        back = norm_back(grad * r.vec[2:3, :], normed, scale)
        r.vsum[5:6, :] += col_sum(back)
        r.dh2l[rows, :] = back.astype(BF16)
        dnorm[rows, :] = back
        hook["turned"](tile)
        return carry

    lax.fori_loop(0, tiles, turn, 0)
    r.flip[...] = r.dh2l[...].T

    def grad_shrink(number, carry):
        step = by_halves(number)
        grad = dot(r.flip[...], r.act[:, aligned(step, wide)]).astype(BF16)
        put_two(r.gs, 2 * (number // sides), number % sides, grad)
        hook["shrinks"](number)
        return carry

    lax.fori_loop(0, steps, grad_shrink, 0)

    def shrink(number, carry):
        step = by_halves(number)
        whole = aligned(step, wide)

        def one(tile, inner):
            rows = aligned(tile, TILE)
            grad = dot(r.dh2l[rows, :], w_shrink(step))
            low = (grad * r.slope[rows, whole].astype(F32)).astype(BF16)
            r.slope[rows, whole] = low
            r.vsum[pl.ds(8 + step, 1), :] += col_sum(low.astype(F32))
            dnorm[rows, :] += dot(low, w_expand(step), NT)
            hook["shrank"](number * tiles + tile)
            return inner

        lax.fori_loop(0, tiles, one, 0)
        return carry

    lax.fori_loop(0, steps, shrink, 0)

    def leave(tile, carry):
        rows = aligned(tile, TILE)
        grad = dnorm[rows, :]
        normed = r.norm1[rows, :]
        r.vsum[0:1, :] += col_sum(grad * normed)
        r.vsum[1:2, :] += col_sum(grad)
        back = norm_back(grad * r.vec[0:1, :], normed, r.scale1[rows, :])
        r.vsum[4:5, :] += col_sum(back)
        low = back.astype(BF16)
        r.dh1l[rows, :] = low
        for side in range(sides):
            r.dctx[side, rows, :] = dot(low, flat(r.we, 0, side)).astype(BF16)
        hook["left"](tile)
        return carry

    lax.fori_loop(0, tiles, leave, 0)
    r.flip[...] = r.al[...].T

    def grad_expand(number, carry):
        step = by_halves(number)
        grad = dot(r.flip[...], r.slope[:, aligned(step, wide)]).astype(BF16)
        put_two(r.ge, 1 + 2 * (number // sides), number % sides, grad)
        return carry

    lax.fori_loop(0, steps, grad_expand, 0)
    r.flip[...] = r.dh1l[...].T
    for side in range(sides):
        put(r.ge, 0, side, dot(r.flip[...], r.ctxx[side]).astype(BF16))


def feed_buffers(tokens, width, hidden):
    return [
        ("norm1", (tokens, width), F32),
        ("scale1", (tokens, 1), F32),
        ("sum2", (tokens, width), F32),
        ("al", (tokens, width), BF16),
        ("act", (tokens, hidden), BF16),
        ("slope", (tokens, hidden), BF16),
        ("dh2l", (tokens, width), BF16),
        ("flip", (width, tokens), BF16),
    ]


def feed_kernel(names, *refs):
    feed_math(types.SimpleNamespace(**dict(zip(names, refs))), {})


def feed_both(x, og, ctx, w_expand, w_shrink, vecs):
    tokens, width = x.shape
    chunks, sides = w_shrink.shape[0:2]
    outs = [
        ("out", (tokens, width), BF16),
        ("dctx", (sides, tokens, UNIT), BF16),
        ("dh1l", (tokens, width), BF16),
        ("ge", (chunks + 1, sides, width, UNIT), BF16),
        ("gs", (chunks, sides, width, UNIT), BF16),
        ("vsum", (VROWS, width), F32),
    ]
    scratch = feed_buffers(tokens, width, sides * chunks * UNIT)
    names = ["x", "og", "ctxx", "we", "ws", "vec"] + [item[0] for item in outs + scratch]
    vmem = pl.BlockSpec(memory_space=pltpu.VMEM)
    return pl.pallas_call(
        functools.partial(feed_kernel, names),
        out_shape=[jax.ShapeDtypeStruct(shape, kind) for _, shape, kind in outs],
        in_specs=[vmem] * 6,
        out_specs=[vmem] * len(outs),
        scratch_shapes=[pltpu.VMEM(shape, kind) for _, shape, kind in scratch],
        compiler_params=pltpu.CompilerParams(vmem_limit_bytes=VMEM_LIMIT),
        name="feed_both",
    )(x, og, ctx, w_expand, w_shrink, vecs)


def layer_kernel(heads, plan, inv_tokens, names, kept, used, feeds, *refs):
    r = types.SimpleNamespace(**dict(zip(names, refs)))
    cols = heads * HD
    tokens = r.x_all.shape[0]
    pages = tokens // PAGE
    own_tokens = tokens // 2
    tiles = own_tokens // TILE
    place = Place()
    place.signal()
    m, peer = place.m, place.peer["x"]
    at = (place.z, place.y)
    own = aligned(m, own_tokens)
    load_x = pltpu.make_async_copy(r.x_all.at[own, :], r.x, r.load_sem.at[0])
    load_og = pltpu.make_async_copy(r.og_all.at[own, :], r.og, r.load_sem.at[1])
    load_x.start()
    load_og.start()
    r.w[(0, place.c, 0, *at)] = r.attn[0].astype(BF16)
    for half in range(2):
        r.w[(1 + half, place.c, 0, *at)] = jnp.concatenate(
            [
                r.attn[1 + kind, :, head * HD : (head + 1) * HD].astype(BF16)
                for head in range(half * heads // 2, (half + 1) * heads // 2)
                for kind in range(2)
            ],
            axis=1,
        )
    r.box_gather[(0, place.c, 0, *at)] = r.shard_box[...]
    r.vec_gather[(0, place.c, m, *at)] = jnp.zeros((VROWS, 128), F32)
    table_at = (slice(0, r.vectors.shape[0]), slice(0, r.vectors.shape[1]))
    r.vec_gather[(0, place.c, m, *at, *table_at)] = r.vectors[...]
    r.we[(0, place.c, m, *at)] = r.merge[...].astype(BF16)
    for chunk in range(4):
        lanes = slice(chunk * UNIT, (chunk + 1) * UNIT)
        r.we[(1 + chunk, place.c, m, *at)] = r.expand[:, lanes].astype(BF16)
        r.ws[(chunk, place.c, m, *at)] = r.shrink[:, lanes].astype(BF16)
    place.wait()
    tree_v = Spread(place, r.vec_gather, 1, "xzy", r.v_sem)
    tree_b = Spread(place, r.box_gather, 1, "zy", r.b_sem)
    tree_a = Spread(place, r.w, 3, "zy", r.a_sem)
    tree_e = Spread(place, r.we, 5, "zyx", r.e_sem)
    tree_f = Spread(place, r.ws, 4, "xzy", r.f_sem)
    tree_e.lag = tree_f.lag = 2
    late = 3
    first = tree_a.events
    begun = first - late

    def weights_event(number):
        tree_e.event(number)
        tree_f.event(number)

    def finish(chunk, value):
        r.sum_f[chunk] = value * inv_tokens

    back_f = Reduce(
        place, r.gs, None, dict(c=r.fc, y=r.fy, z=r.fz, x=r.fx), 4, "cyzx", r.back_sem, finish
    )
    back_f.lag, back_f.held_back = 2, 1

    def attention(*scoped):
        q = types.SimpleNamespace(**dict(zip([item[0] for item in kept + used] + ["x"], scoped)))
        load_all = pltpu.make_async_copy(r.x_all, q.x, r.load_sem.at[2])
        load_all.start()

        def begin(number, carry):
            tree_a.event(number)
            tree_b.event(number)
            tree_v.event(number)
            weights_event(number - late)
            pl.when(number == 1)(lambda: attend_trig(r.omega, r.corner, q.trig))

            @pl.when(number == 4)
            def _():
                r.vec[...] = rows_from_blocks(
                    r.vec_gather[...].reshape(-1, 128), r.pick[...], plan
                )
                r.box_out[...] = natural(r.box_gather, 0, 0).astype(BF16)
                attend_setup(heads, m, r.box_out, r.vec, q.box_heads, q.bias)

            return carry

        lax.fori_loop(0, first, begin, 0)
        keep_w = pltpu.make_async_copy(r.w, r.w_out, r.load_sem.at[3])
        keep_w.start()
        load_all.wait()

        def projected(page):
            weights_event(begun + page)

        piece = PAGE // 2

        def swap_copy(index):
            theirs = pages * (1 - m) + index
            return remote(
                q.ctx.at[aligned(theirs, piece), :],
                r.ctxx.at[m, aligned(index, piece), :],
                r.ctx_sem.at[0, index],
                r.ctx_sem.at[1, index],
                peer,
            )

        def attended(step, turn, pair):
            pl.when(step % 2 == 0)(lambda: weights_event(begun + pages + step // 2))

            @pl.when(step == heads // 2 - 1)
            def _():
                swap_copy(2 - 2 * m).start()
                swap_copy(1).start()

            @pl.when(step == heads - 1)
            def _():
                swap_copy(2 * m).start()

        attend_math(
            heads,
            q,
            lambda chunk: natural(r.w, chunk, 0),
            lambda turn: turn * m + (pages - 1 - turn) * (1 - m),
            projected,
            attended,
        )
        stores = [
            pltpu.make_async_copy(getattr(q, name), getattr(r, name + "_out"), r.store_sem.at[k])
            for k, (name, _, _) in enumerate(kept)
        ]
        for copy in stores:
            copy.start()
        r.ctxx[m] = q.ctx[own, :]
        for index in range(pages):
            copy = remote(
                q.ctx.at[aligned(index, piece), :],
                r.ctxx.at[1 - m, aligned(index, piece), :],
                r.ctx_sem.at[0, index],
                r.ctx_sem.at[1, index],
                peer,
            )
            copy.wait_recv()
            copy.wait_send()
        for copy in stores:
            copy.wait()
        keep_w.wait()

    pl.run_scoped(
        attention,
        *[pltpu.VMEM(shape, kind) for _, shape, kind in kept + used],
        pltpu.VMEM(r.x_all.shape, BF16),
    )

    def feed(*scoped):
        q = types.SimpleNamespace(**dict(zip([item[0] for item in feeds], scoped)))
        for name in ("x", "og", "we", "ws", "vec", "ctxx", "dh1l", "ge", "gs", "vsum"):
            setattr(q, name, getattr(r, name))

        def out_copies(tile):
            rows = aligned(tile, TILE)
            there = r.out_full.at[pl.ds(pl.multiple_of(m * own_tokens + tile * TILE, TILE), TILE), :]
            return (
                pltpu.make_async_copy(q.out.at[rows, :], there, r.swap_sem.at[0, tile]),
                remote(q.out.at[rows, :], there, r.swap_sem.at[1, tile], r.swap_sem.at[2, tile], peer),
            )

        def dctx_copies(tile):
            rows = aligned(tile, TILE)
            there = r.dctx_full.at[pl.ds(pl.multiple_of(m * own_tokens + tile * TILE, TILE), TILE), :]
            return (
                pltpu.make_async_copy(q.dctx.at[m, rows, :], there, r.swap_sem.at[3, tile]),
                remote(
                    q.dctx.at[1 - m, rows, :], there, r.swap_sem.at[4, tile], r.swap_sem.at[5, tile], peer
                ),
            )

        def start(copies):
            for copy in copies:
                copy.start()

        def grew(number):
            pl.when(number % 3 == 1)(lambda: weights_event(begun + pages + 5 + number // 3))

        def shrinks(number):
            pl.when(number % 2 == 1)(lambda: back_f.event(number // 2))

        def shrank(number):
            pl.when(number % 2 == 1)(lambda: back_f.event(2 + number // 2))

        def left(tile):
            start(dctx_copies(tile))
            pl.when(tile % 2 == 0)(lambda: back_f.event(8 + tile // 2))

        load_x.wait()
        load_og.wait()
        feed_math(
            q,
            dict(
                grew=grew,
                turned=lambda tile: start(out_copies(tile)),
                shrinks=shrinks,
                shrank=shrank,
                left=left,
            ),
        )
        back_f.rest()
        back_f.drain()
        for tile in range(tiles):
            for copy in out_copies(tile) + dctx_copies(tile):
                copy.wait()

    pl.run_scoped(feed, *[pltpu.VMEM(shape, kind) for _, shape, kind in feeds])
    for tree in (tree_v, tree_b, tree_a, tree_e, tree_f):
        tree.drain()


def layer_forward(x, og, corners, omega, pick, shards, plan, inv_tokens):
    tokens, width = x.shape
    cols = shards[1].shape[1]
    heads = cols // HD
    own = tokens // 2
    unit = (width // 16, UNIT)
    kept, used = attend_buffers(heads, tokens)
    feeds = feed_buffers(own, width, 8 * UNIT)
    feeds += [("out", (own, width), BF16), ("dctx", (2, own, UNIT), BF16)]
    free = pl.BlockSpec(memory_space=pl.ANY)
    vmem = pl.BlockSpec(memory_space=pltpu.VMEM)
    inputs = [("x_all", free), ("og_all", free), ("corner", vmem), ("omega", vmem), ("pick", vmem)]
    inputs += [(name, vmem) for name in ("attn", "shard_box", "vectors", "merge", "expand", "shrink")]
    outs = [(name + "_out", shape, kind, free) for name, shape, kind in kept]
    outs += [
        ("w_out", (3, 2, 1, 4, 2, *unit), BF16, free),
        ("box_out", (PE, cols), BF16, vmem),
        ("out_full", (tokens, width), BF16, free),
        ("dctx_full", (tokens, cols), BF16, free),
        ("dh1l", (own, width), BF16, vmem),
        ("ge", (5, 2, 2, 4, 2, *unit), BF16, vmem),
        ("vsum", (VROWS, width), F32, vmem),
        ("sum_f", (4, *unit), F32, vmem),
    ]
    dma = pltpu.SemaphoreType.DMA
    scratch = [
        ("x", pltpu.VMEM((own, width), BF16)),
        ("og", pltpu.VMEM((own, width), BF16)),
        ("vec", pltpu.VMEM((VROWS, width), F32)),
        ("w", pltpu.VMEM((3, 2, 1, 4, 2, *unit), BF16)),
        ("box_gather", pltpu.VMEM((1, 2, 1, 4, 2, PE // 16, cols), F32)),
        ("vec_gather", pltpu.VMEM((1, 2, 2, 4, 2, VROWS, 128), F32)),
        ("we", pltpu.VMEM((5, 2, 2, 4, 2, *unit), BF16)),
        ("ws", pltpu.VMEM((4, 2, 2, 4, 2, *unit), BF16)),
        ("ctxx", pltpu.VMEM((2, own, cols), BF16)),
        ("gs", pltpu.VMEM((4, 2, 2, 4, 2, *unit), BF16)),
        ("fc", pltpu.VMEM((4, 2, 4, 2, *unit), BF16)),
        ("fy", pltpu.VMEM((4, 2, 4, *unit), BF16)),
        ("fz", pltpu.VMEM((4, 3, 2, *unit), BF16)),
        ("fx", pltpu.VMEM((4, *unit), BF16)),
        ("ctx_sem", dma((2, 3))),
        ("a_sem", dma((2, 3, SLOTS))),
        ("b_sem", dma((2, 1, SLOTS))),
        ("v_sem", dma((2, 1, SLOTS))),
        ("e_sem", dma((2, 5, SLOTS))),
        ("f_sem", dma((2, 4, SLOTS))),
        ("back_sem", dma((2, 4, SLOTS))),
        ("load_sem", dma((4,))),
        ("store_sem", dma((len(kept),))),
        ("swap_sem", dma((6, own // TILE))),
    ]
    names = [item[0] for item in inputs + outs + scratch]
    return pl.pallas_call(
        functools.partial(layer_kernel, heads, plan, inv_tokens, names, kept, used, feeds),
        out_shape=[jax.ShapeDtypeStruct(shape, kind) for _, shape, kind, _ in outs],
        in_specs=[item[1] for item in inputs],
        out_specs=[item[3] for item in outs],
        scratch_shapes=[item[1] for item in scratch],
        compiler_params=pltpu.CompilerParams(
            vmem_limit_bytes=VMEM_LIMIT, collective_id=0, has_side_effects=True
        ),
        name="layer_forward",
    )(x, og, corners, omega, pick, *shards)


def pair_place(cols):
    spot = lax.broadcasted_iota(jnp.int32, (cols, 2 * cols), 0)
    lane = lax.broadcasted_iota(jnp.int32, (cols, 2 * cols), 1)
    target = ((spot >> 6) << 7) + HD + (spot & (HD - 1))
    return jnp.where(lane == target, 1.0, 0.0)


def exact_dot(lhs, rhs, dims=NN):
    return lax.dot_general(
        lhs, rhs, dims, precision=lax.Precision.HIGHEST, preferred_element_type=F32
    )


def attend_back_kernel(heads, plan, inv_tokens, *refs):
    inputs, refs = refs[:12], refs[12:]
    if plan is not None:
        load_sem, held, refs = refs[-1], refs[-13:-1], refs[:-13]
        loads = [
            pltpu.make_async_copy(src, dst, load_sem.at[k]) for k, (src, dst) in enumerate(zip(inputs, held))
        ]
        early = (0, 2, 7, 11)
        for k in sorted(range(12), key=lambda k: k not in early):
            loads[k].start()
        inputs = held
    x_ref, w_ref, box_ref, *inputs = inputs
    qa_ref, qtok_ref, kvtok_ref, kt_ref, kft_ref, trig_ref, ctxt_ref, log_ref, dctx_ref = inputs
    cols = heads * HD
    tokens = x_ref.shape[0]
    pages = tokens // PAGE
    m = lax.axis_index("mp")
    piece = PAGE // 2
    pieces = 2 * pages
    lane = lax.broadcasted_iota(jnp.int32, (1, 2 * HD), 1)
    lower = lane < HD
    if plan is None:
        inp_ref, gw_ref, gbox_ref, qvsum_ref, *refs = refs
        kftok, dctxt, boxt, dtok, xt, gbox = refs
        before, after = 0, 0

        def background(number):
            pass
    else:
        dh1_ref, vsum_ref, sumf_ref, pick_ref, full_e, *refs = refs
        inp_ref, sum_e, sum_a, sum_b, sum_v, norm_ref, *refs = refs
        kftok, dctxt, boxt, dtok, xt, gbox, *refs = refs
        came, total_e, full_a, full_b, full_v, land_v, norms, *refs = refs
        ec, ey, ez, ex, ac, ay, az, bc, by, bz, *refs = refs
        e_sem, a_sem, b_sem, v_sem, n_sem, i_sem, loc_sem = refs
        place = Place()
        place.signal_all()
        fill = pltpu.make_async_copy(full_e.at[:, place.c], total_e, loc_sem.at[0])
        fill.start()
        place.wait_all()

        def finish(out):
            def put(chunk, value):
                out[chunk] = value * inv_tokens

            return put

        tree_e = Reduce(
            place, full_e, total_e, dict(c=ec, y=ey, z=ez, x=ex), 5, "cyzx", e_sem, finish(sum_e)
        )
        tree_e.lag, tree_e.held_back = 2, 1
        tree_a = Reduce(place, full_a, None, dict(c=ac, y=ay, z=az), 3, "cyz", a_sem, finish(sum_a))
        tree_b = Reduce(place, full_b, None, dict(c=bc, y=by, z=bz), 1, "cyz", b_sem, finish(sum_b))

        def block_of(rank):
            r = rank % 16
            return full_v.at[rank // 16, r // 4, (r // 2) % 2, r % 2]

        spot = (place.m, place.z, place.y, place.c)
        all_v = Everyone(place, block_of, lambda step: land_v.at[step - 1], v_sem)
        all_n = Everyone(place, lambda rank: norms.at[spot], lambda step: norms.at[spot], n_sem)

        def background(number):
            tree_e.event(number)

        background(0)
        fill.wait()
        for k in early:
            loads[k].wait()

    boxt[...] = box_ref[...].T
    gbox[...] = jnp.zeros_like(gbox)

    def prepare(page, carry):
        rows = aligned(page, PAGE)
        kftok[rows, :] = kft_ref[:, rows].T
        dctxt[:, rows] = dctx_ref[rows, :].T
        xt[:, rows] = x_ref[rows, :].T
        if plan is not None:
            pl.when(page > 0)(lambda: background(page))
        return carry

    lax.fori_loop(0, pages, prepare, 0)
    if plan is not None:
        for k in range(12):
            if k not in early:
                loads[k].wait()

    def attend(step, carry):
        page, pair = step // (heads // 2), step % (heads // 2)
        rows = aligned(page, PAGE)
        own, partner = turn_factors(trig_ref[:, rows])
        pair_lanes = aligned(pair, 2 * HD)
        query_pair = qtok_ref[rows, pair_lanes]
        dctx_pair = dctx_ref[rows, pair_lanes]
        halves = []
        boxes = []
        blank = jnp.zeros((HD, PAGE), BF16)
        for side in range(2):
            head = pair * 2 + side
            lanes = aligned(head, 2 * HD)
            key_value = kvtok_ref[rows, lanes]
            left = jnp.concatenate([kftok[rows, :], key_value], axis=1)
            score = dot(left, jnp.concatenate([qa_ref[head, :, rows], blank], axis=0))
            prob = jnp.exp(score - log_ref[head, :, rows])
            prob_low = prob.astype(BF16)
            head_rows = pl.ds(pl.multiple_of(head * HD, HD), HD)
            dctx_head = dctxt[head_rows, rows]
            grad_prob = dot(
                key_value, jnp.concatenate([blank, dctx_head], axis=0)
            )
            inner = col_sum(dctx_head.astype(F32) * ctxt_ref[head_rows, rows].astype(F32))
            grad_score = (prob * (grad_prob - inner)).astype(BF16)
            if side == 0:
                both = jnp.concatenate([query_pair[:, 0:HD], dctx_pair[:, 0:HD]], axis=1)
            else:
                both = jnp.concatenate([query_pair[:, HD:], dctx_pair[:, HD:]], axis=1)
            from_score = dot(grad_score, both)
            from_prob = dot(prob_low, both)
            grad_kv = jnp.where(lower, from_score, from_prob).astype(BF16)
            dtok[rows, pl.ds(pl.multiple_of(cols + head * 2 * HD, 2 * HD), 2 * HD)] = grad_kv
            keys = jnp.concatenate([kft_ref[:, rows], kt_ref[head_rows, rows]], axis=0)
            grad_query = dot(keys, grad_score) * HD ** (-0.5)
            feat = grad_query[0:PE]
            proj = (feat * own - swap_blocks(feat) * partner).astype(BF16)
            halves.append(grad_query[PE:] + dot(boxt[head_rows, :], proj))
            boxes.append(dot(proj, query_pair))
        gbox[:, pair_lanes] += jnp.where(lower, boxes[0], boxes[1])
        dtok[rows, pair_lanes] = jnp.concatenate(halves, axis=0).astype(BF16).T
        return carry

    def weights(chunk):
        return w_ref[chunk] if plan is None else natural(w_ref, chunk, 0)

    def spread(page):
        rows = aligned(page, PAGE)
        return sum(
            dot(dtok[rows, chunk * UNIT : (chunk + 1) * UNIT], weights(chunk), NT) for chunk in range(3)
        )

    if plan is None:
        lax.fori_loop(0, pages * (heads // 2), attend, 0)
        gbox_ref[...] = gbox[...] * HD**0.5

        def spread_page(page, carry):
            inp_ref[aligned(page, PAGE), :] = spread(page)
            return carry

        lax.fori_loop(0, pages, spread_page, 0)

        def gather(step, carry):
            lanes = aligned(step, UNIT)
            gw_ref[step] = dot(xt[...], dtok[:, lanes]).astype(BF16)
            qvsum_ref[0:1, lanes] = col_sum(dtok[:, lanes].astype(F32))
            return carry

        lax.fori_loop(0, 3, gather, 0)
        return

    def swap(index):
        rows = aligned(index, piece)
        return remote(
            inp_ref.at[rows, :], came.at[rows, :], i_sem.at[0, index], i_sem.at[1, index], place.peer["x"]
        )

    def attend_and_send(step, carry):
        attend(step, carry)
        page = step // (heads // 2)

        @pl.when(step % (heads // 2) == heads // 2 - 1)
        def _():
            value = spread(page)
            for half in range(2):
                index = 2 * page + half
                rows = aligned(index, piece)
                own = index // pages == m
                spot = aligned(index % pages, piece)
                extra = jnp.where(own, dh1_ref[spot, :].astype(F32), 0.0)
                inp_ref[rows, :] = (value[half * piece : (half + 1) * piece] + extra).astype(BF16)
                swap(index).start()

        background(step + pages)
        return carry

    lax.fori_loop(0, pages * (heads // 2), attend_and_send, 0)
    put_natural(full_b, 0, 0, gbox[...] * HD**0.5)

    def gather(step, carry):
        grad = dot(xt[...], dtok[:, aligned(step, UNIT)]).astype(BF16)
        put_natural(full_a, step, 0, grad)
        tree_a.event(step)
        tree_b.event(step)
        return carry

    lax.fori_loop(0, 3, gather, 0)

    sums = jnp.concatenate(
        [
            col_sum(dtok[:, chunk * UNIT : (chunk + 1) * UNIT].astype(F32)) for chunk in range(3)
        ],
        axis=1,
    )
    values = exact_dot(jnp.broadcast_to(sums[:, cols:], (8, 2 * cols)), pair_place(cols), NT)
    pair = jnp.concatenate([sums[:, 0:cols], values[0:1]], axis=0)
    blank = jnp.zeros_like(pair)
    pair = jnp.where(
        m == 0, jnp.concatenate([pair, blank], axis=1), jnp.concatenate([blank, pair], axis=1)
    )
    table = jnp.concatenate([vsum_ref[0:6, :], pair, vsum_ref[8:, :]], axis=0)
    mp_count, dp_count = plan
    width = table.shape[1]
    each = width // (mp_count * dp_count)
    wide_lane = lax.broadcasted_iota(jnp.int32, (VROWS, width), 1)
    for side in range(mp_count):
        parts = []
        for r in range(dp_count):
            first = (r * mp_count + side) * each
            parts.append(jnp.where((wide_lane >= first) & (wide_lane < first + each), table, 0.0))
        block = exact_dot(jnp.concatenate(parts, axis=0), pick_ref[...], NT)
        full_v[side] = block.reshape(full_v.shape[1:])
    all_v.start()

    def tail(number, carry):
        tree_a.event(number)
        tree_b.event(number)
        return carry

    lax.fori_loop(3, tree_a.events, tail, 0)
    tree_e.rest()
    all_v.wait()
    total_v = full_v[spot] + jnp.sum(land_v[...], axis=0)
    sum_v[0] = total_v * inv_tokens

    square = sum(jnp.sum(out[...] * out[...]) for out in (sum_e, sumf_ref, sum_a, sum_b, sum_v))
    norms[spot] = jnp.full((8, 128), square, F32)
    all_n.start()

    def final(number, carry):
        rows = aligned(number, piece)
        swap(number).wait()
        inp_ref[rows, :] = (inp_ref[rows, :].astype(F32) + came[rows, :].astype(F32)).astype(BF16)
        return carry

    lax.fori_loop(0, pieces, final, 0)
    all_n.wait()
    every = norms[...].reshape(-1, 8, 128)
    norm_ref[...] = jnp.sqrt(sum(every[k] for k in range(every.shape[0])))
    for tree in (tree_e, tree_a, tree_b):
        tree.drain()


def attend_backward(x, weight, box, kept, dctx, plan, inv_tokens, more=()):
    tokens, width = x.shape
    cols = weight.shape[-1]
    heads = cols // HD
    vmem = pl.BlockSpec(memory_space=pltpu.VMEM)
    scratch = [
        pltpu.VMEM((tokens, PE), BF16),
        pltpu.VMEM((cols, tokens), BF16),
        pltpu.VMEM((cols, PE), BF16),
        pltpu.VMEM((tokens, 3 * cols), BF16),
        pltpu.VMEM((width, tokens), BF16),
        pltpu.VMEM((PE, cols), F32),
    ]
    in_specs = [vmem] * 12
    if plan is None:
        shapes = [
            ((tokens, width), F32),
            ((3, width, cols), BF16),
            ((PE, cols), F32),
            ((8, 3 * cols), F32),
        ]
        extra = {}
    else:
        free = pl.BlockSpec(memory_space=pl.ANY)
        in_specs = [free] * 12 + [vmem] * 4 + [free]
        rows = width // 16
        unit = (rows, UNIT)
        tile = (PE // 16, cols)
        small = (VROWS, 128)
        shapes = [
            ((tokens, width), BF16),
            ((5, *unit), F32),
            ((3, *unit), F32),
            ((1, *tile), F32),
            ((1, *small), F32),
            ((8, 128), F32),
        ]
        scratch += [
            pltpu.VMEM((tokens, width), BF16),
            pltpu.VMEM((5, 2, 4, 2, *unit), BF16),
            pltpu.VMEM((3, 2, 1, 4, 2, *unit), BF16),
            pltpu.VMEM((1, 2, 1, 4, 2, *tile), F32),
            pltpu.VMEM((2, 4, 2, 2, *small), F32),
            pltpu.VMEM((31, *small), F32),
            pltpu.VMEM((2, 4, 2, 2, 8, 128), F32),
            pltpu.VMEM((5, 2, 4, 2, *unit), BF16),
            pltpu.VMEM((5, 2, 4, *unit), BF16),
            pltpu.VMEM((5, 3, 2, *unit), BF16),
            pltpu.VMEM((5, *unit), BF16),
            pltpu.VMEM((3, 4, 2, *unit), BF16),
            pltpu.VMEM((3, 4, *unit), BF16),
            pltpu.VMEM((3, 3, *unit), BF16),
            pltpu.VMEM((1, 4, 2, *tile), F32),
            pltpu.VMEM((1, 4, *tile), F32),
            pltpu.VMEM((1, 3, *tile), F32),
            pltpu.SemaphoreType.DMA((2, 5, SLOTS)),
            pltpu.SemaphoreType.DMA((2, 3, SLOTS)),
            pltpu.SemaphoreType.DMA((2, 1, SLOTS)),
            pltpu.SemaphoreType.DMA((2, 31)),
            pltpu.SemaphoreType.DMA((2, 31)),
            pltpu.SemaphoreType.DMA((2, 2 * (tokens // PAGE))),
            pltpu.SemaphoreType.DMA((2,)),
        ]
        scratch += [pltpu.VMEM(array.shape, array.dtype) for array in (x, weight, box, *kept, dctx)]
        scratch.append(pltpu.SemaphoreType.DMA((12,)))
        extra = dict(collective_id=2, has_side_effects=True)
    return pl.pallas_call(
        functools.partial(attend_back_kernel, heads, plan, inv_tokens),
        out_shape=[jax.ShapeDtypeStruct(s, d) for s, d in shapes],
        in_specs=in_specs,
        out_specs=[vmem] * len(shapes),
        scratch_shapes=scratch,
        compiler_params=pltpu.CompilerParams(vmem_limit_bytes=VMEM_LIMIT, **extra),
        name="attend_backward",
    )(x, weight, box, *kept, dctx, *more)


def adam_step(master, first, second, gradient, rate, decay):
    new_first = BETA_ONE * first + (1.0 - BETA_ONE) * gradient
    new_second = BETA_TWO * second + (1.0 - BETA_TWO) * gradient * gradient
    first_hat = new_first / (1.0 - BETA_ONE**STEP)
    second_hat = new_second / (1.0 - BETA_TWO**STEP)
    new_master = master - rate * (first_hat / (jnp.sqrt(second_hat) + ADAM_EPS) + decay * master)
    return (new_first, new_second, new_master)


def adam_kernel(heads, norm_ref, *refs):
    sum_e, sum_f, sum_a, sum_b, sum_v, *refs = refs
    states, outs = refs[:18], refs[18:]
    outs[-1][...] = norm_ref[0:1, 0:1]
    clip = CLIP_LIMIT / jnp.maximum(norm_ref[0:1, 0:1], CLIP_LIMIT)

    def update(first, out, gradient, at, rate, decay):
        news = adam_step(*(ref[at] for ref in states[first : first + 3]), gradient * clip, rate, decay)
        for ref, new in zip(outs[out : out + 3], news):
            ref[at] = new
        if decay:
            outs[out + 3][at] = news[2].astype(BF16)

    def heads_of(kind):
        half = heads // 2
        return jnp.concatenate(
            [
                sum_a[1 + head // half, :, (2 * (head % half) + kind) * HD : (2 * (head % half) + kind + 1) * HD]
                for head in range(heads)
            ],
            axis=1,
        )

    for index, gradient in enumerate((sum_a[0], heads_of(0), heads_of(1))):
        update(0, 0, gradient, index, RATE_MATRIX, WEIGHT_DECAY)
    update(3, 4, sum_b[0], ALL, RATE_MATRIX, WEIGHT_DECAY)
    update(6, 8, sum_e[0], ALL, RATE_MATRIX, WEIGHT_DECAY)
    for chunk in range(4):
        lanes = (ALL, slice(chunk * UNIT, (chunk + 1) * UNIT))
        update(9, 12, sum_e[1 + chunk], lanes, RATE_MATRIX, WEIGHT_DECAY)
        update(12, 16, sum_f[chunk], lanes, RATE_MATRIX, WEIGHT_DECAY)
    rows, each = states[15].shape
    update(15, 20, sum_v[0, 0:rows, 0:each], ALL, RATE_VECTOR, 0.0)


def adam_all(norm, sums, states):
    shapes = []
    for first in range(0, 18, 3):
        shapes += [(states[first].shape, F32)] * 3
        if first < 15:
            shapes.append((states[first].shape, BF16))
    vmem = pl.BlockSpec(memory_space=pltpu.VMEM)
    shapes.append(((1, 1), F32))
    return pl.pallas_call(
        functools.partial(adam_kernel, states[0].shape[2] // HD),
        out_shape=[jax.ShapeDtypeStruct(s, d) for s, d in shapes],
        in_specs=[vmem] * (6 + len(states)),
        out_specs=[vmem] * len(shapes),
        compiler_params=pltpu.CompilerParams(vmem_limit_bytes=VMEM_LIMIT),
        name="adam_all",
    )(norm, *sums, *states)


def pack_qkv(shard):
    rows, cols = shard.shape[1:]
    heads = cols // HD
    pairs = jnp.stack([shard[1].reshape(rows, heads, HD), shard[2].reshape(rows, heads, HD)], axis=2)
    pairs = pairs.reshape(rows, 2, cols)
    return jnp.stack([shard[0], pairs[:, 0], pairs[:, 1]])


def unpack_qkv(packed):
    rows, cols = packed.shape[1:]
    pairs = jnp.concatenate([packed[1], packed[2]], axis=1).reshape(rows, cols // HD, 2, HD)
    return jnp.stack(
        [packed[0], pairs[:, :, 0].reshape(rows, cols), pairs[:, :, 1].reshape(rows, cols)]
    )


def to_chunks(shard):
    rows = shard.shape[0]
    return shard.reshape(rows, -1, UNIT).transpose(1, 0, 2)


def from_chunks(chunks):
    return chunks.transpose(1, 0, 2).reshape(chunks.shape[1], -1)


def on_device(
    layer_input,
    page_boxes,
    output_grad,
    attn_proj,
    attn_first,
    attn_second,
    box_proj,
    box_first,
    box_second,
    merge_proj,
    merge_first,
    merge_second,
    expand_proj,
    expand_first,
    expand_second,
    shrink_proj,
    shrink_first,
    shrink_second,
    vectors,
    vector_first,
    vector_second,
):
    mp_count = lax.axis_size("mp")
    dp_count = lax.axis_size("dp")
    mp_index = lax.axis_index("mp")
    tokens, width = layer_input.shape
    cols = attn_proj.shape[2]
    heads = cols // HD
    own_tokens = tokens // mp_count
    inv_tokens = 1.0 / (tokens * dp_count)

    corners = page_boxes.T
    omega = (10000.0 ** (-np.arange(FREQS, dtype=np.float64) / FREQS)).astype(np.float32)[:, None]
    omega = jnp.asarray(omega)
    plan = (mp_count, dp_count) if dp_count == 16 and mp_count == 2 else None
    if plan is not None:
        each = vectors.shape[1]
        pick = np.zeros((128, width), np.float32)
        pick[np.arange(width) % each, np.arange(width)] = 1.0
        pick = jnp.asarray(pick)
        *kept, w_qkv, w_box, layer_out, dctx, dh1, g_expand, vec_sum, sum_f = layer_forward(
            layer_input,
            output_grad,
            corners,
            omega,
            pick,
            (attn_proj, box_proj, vectors, merge_proj.T, expand_proj, shrink_proj.T),
            plan,
            inv_tokens,
        )
        input_grad, sum_e, sum_a, sum_b, sum_v, norm = attend_backward(
            layer_input,
            w_qkv,
            w_box,
            kept,
            dctx,
            plan,
            inv_tokens,
            (dh1, vec_sum, sum_f, pick, g_expand),
        )
        merge = [merge_proj.T, merge_first.T, merge_second.T]
        shrink = [shrink_proj.T, shrink_first.T, shrink_second.T]
        *results, norm = adam_all(
            norm,
            (sum_e, sum_f, sum_a, sum_b, sum_v),
            [attn_proj, attn_first, attn_second, box_proj, box_first, box_second, *merge]
            + [expand_proj, expand_first, expand_second, *shrink, vectors, vector_first, vector_second],
        )
        turned = (8, 9, 10, 11, 16, 17, 18, 19)
        results = [out.T if k in turned else out for k, out in enumerate(results)]
        return (layer_out, input_grad, norm.reshape(()), *results)
    shard_qkv = pack_qkv(attn_proj).astype(BF16)
    shard_e = jnp.concatenate([merge_proj.T[None], to_chunks(expand_proj)]).astype(BF16)
    shard_f = to_chunks(shrink_proj.T).astype(BF16)
    w_qkv = lax.all_gather(shard_qkv, "dp", axis=1, tiled=True)
    w_box = lax.all_gather(box_proj.astype(BF16), "dp", axis=0, tiled=True)
    w_expand = lax.all_gather(lax.all_gather(shard_e, "dp", axis=1, tiled=True), "mp", axis=1)
    w_shrink = lax.all_gather(lax.all_gather(shard_f, "dp", axis=1, tiled=True), "mp", axis=1)
    vecs = lax.all_gather(vectors, ("dp", "mp"), axis=1, tiled=True)
    vecs = jnp.pad(vecs, ((0, VROWS - vecs.shape[0]), (0, 0)))
    *kept, context = attend_forward(layer_input, corners, omega, w_qkv, w_box, vecs)
    context = lax.all_to_all(
        context.reshape(mp_count, own_tokens, cols), "mp", split_axis=0, concat_axis=0
    )

    def own_rows(array):
        return lax.dynamic_slice_in_dim(array, mp_index * own_tokens, own_tokens)

    layer_out, dctx, dh1, g_expand, g_shrink, vec_sum = feed_both(
        own_rows(layer_input), own_rows(output_grad), context, w_expand, w_shrink, vecs
    )
    g_feed = jnp.concatenate([g_expand, g_shrink])
    layer_out = lax.all_gather(layer_out, "mp", axis=0, tiled=True)
    dctx = lax.all_to_all(dctx, "mp", split_axis=0, concat_axis=0).reshape(tokens, cols)
    part, g_qkv, g_box, qkv_sum = attend_backward(
        layer_input, w_qkv, w_box, kept, dctx, None, inv_tokens
    )
    own_part = lax.psum_scatter(part.astype(BF16), "mp", scatter_dimension=0, tiled=True)
    own_grad = (own_part.astype(F32) + dh1).astype(BF16)
    input_grad = lax.all_gather(own_grad, "mp", axis=0, tiled=True)
    shard_attn = unpack_qkv(
        lax.psum_scatter(g_qkv, "dp", scatter_dimension=1, tiled=True).astype(F32) * inv_tokens
    )
    shard_box = lax.psum_scatter(g_box, "dp", scatter_dimension=0, tiled=True) * inv_tokens
    sum_feed = lax.psum_scatter(g_feed, "dp", scatter_dimension=2, tiled=True)
    sum_feed = lax.psum_scatter(sum_feed, "mp", scatter_dimension=1, tiled=True)[:, 0]
    sum_feed = sum_feed.astype(F32) * inv_tokens
    sum_expand, sum_shrink = sum_feed[0:5], sum_feed[5:]

    def placed(row):
        return lax.dynamic_update_slice_in_dim(
            jnp.zeros((width,), F32), row, mp_index * cols, 0
        )[None, :]

    value_sum = qkv_sum[0, cols:].reshape(heads, 2, HD)[:, 1].reshape(cols)
    vector_grad = jnp.concatenate(
        [vec_sum[0:6], placed(qkv_sum[0, 0:cols]), placed(value_sum), vec_sum[8:12]]
    )
    vector_shard = (
        lax.psum_scatter(vector_grad, ("dp", "mp"), scatter_dimension=1, tiled=True) * inv_tokens
    )
    square = sum(
        jnp.sum(shard * shard)
        for shard in (shard_attn, shard_box, sum_expand, sum_shrink, vector_shard)
    )
    grad_norm = jnp.sqrt(lax.psum(square, ("dp", "mp")))
    shard_merge = sum_expand[0].T
    shard_expand = from_chunks(sum_expand[1:])
    shard_shrink = from_chunks(sum_shrink).T
    clip_scale = CLIP_LIMIT / jnp.maximum(grad_norm, CLIP_LIMIT)
    results = [layer_out, input_grad, grad_norm]
    for master, first, second, shard in (
        (attn_proj, attn_first, attn_second, shard_attn),
        (box_proj, box_first, box_second, shard_box),
        (merge_proj, merge_first, merge_second, shard_merge),
        (expand_proj, expand_first, expand_second, shard_expand),
        (shrink_proj, shrink_first, shrink_second, shard_shrink),
    ):
        new_first, new_second, new_master = adam_step(
            master, first, second, shard * clip_scale, RATE_MATRIX, WEIGHT_DECAY
        )
        results += [new_first, new_second, new_master, new_master.astype(BF16)]
    results += adam_step(
        vectors, vector_first, vector_second, vector_shard * clip_scale, RATE_VECTOR, 0.0
    )
    return tuple(results)


def solution(mesh):
    rows = P("dp", None)
    attn = P(None, "dp", "mp")
    tall = P("dp", "mp")
    wide = P("mp", "dp")
    vector = P(None, ("dp", "mp"))
    in_specs = (rows,) * 3 + (attn,) * 3 + (tall,) * 3 + (wide,) * 3 + (tall,) * 3 + (wide,) * 3
    in_specs += (vector,) * 3
    out_specs = (rows, rows, P()) + (attn,) * 4 + (tall,) * 4 + (wide,) * 4 + (tall,) * 4
    out_specs += (wide,) * 4 + (vector,) * 3
    return jax.shard_map(
        on_device, mesh=mesh, in_specs=in_specs, out_specs=out_specs, check_vma=False
    )
```

```python
import functools
import types

import jax
import jax.numpy as jnp
import numpy as np
from jax import lax
from jax.experimental import pallas as pl
from jax.experimental.pallas import tpu as pltpu
from jax.sharding import PartitionSpec as P

HD = 64
FREQS = 32
PE = 128
PAGE = 512
STEP = 10

NORM_EPS = 1e-12
CLIP_LIMIT = 0.1
BETA_ONE = 0.9
BETA_TWO = 0.999
ADAM_EPS = 1e-08
RATE_MATRIX = 0.05
RATE_VECTOR = 0.5
WEIGHT_DECAY = 0.01

F32 = jnp.float32
BF16 = jnp.bfloat16
VMEM_LIMIT = 60 * 1024 * 1024

NN = (((1,), (0,)), ((), ()))
NT = (((1,), (1,)), ((), ()))
TN = (((0,), (0,)), ((), ()))


def dot(lhs, rhs, dims=NN):
    return lax.dot_general(lhs, rhs, dims, preferred_element_type=F32)


def aligned(index, size):
    return pl.ds(pl.multiple_of(index * size, size), size)


def swap_blocks(feat):
    return jnp.concatenate(
        [
            feat[FREQS : 2 * FREQS],
            feat[0:FREQS],
            feat[3 * FREQS :],
            feat[2 * FREQS : 3 * FREQS],
        ],
        axis=0,
    )


def turn_factors(trig):
    cos_x, sin_x = trig[0:FREQS], trig[FREQS : 2 * FREQS]
    cos_y, sin_y = trig[2 * FREQS : 3 * FREQS], trig[3 * FREQS :]
    return (
        jnp.concatenate([sin_x, sin_x, sin_y, sin_y], axis=0),
        jnp.concatenate([cos_x, -cos_x, cos_y, -cos_y], axis=0),
    )


MESH = pl.DeviceIdType.MESH
ALL = slice(None)
UNIT = 384


class Place:
    def __init__(self):
        rank = lax.axis_index("dp")
        self.m = lax.axis_index("mp")
        self.z = rank // 4
        self.y = (rank // 2) % 2
        self.c = rank % 2
        self.peer = {
            "x": (rank, 1 - self.m),
            "y": (rank + 2 - 4 * self.y, self.m),
            "c": (rank + 1 - 2 * self.c, self.m),
        }
        self.far = [((rank + 4 * step) % 16, self.m) for step in (1, 2, 3)]

    def signal(self):
        barrier = pltpu.get_barrier_semaphore()
        for device in list(self.peer.values()) + self.far:
            pl.semaphore_signal(barrier, inc=1, device_id=device, device_id_type=MESH)

    def wait(self):
        pl.semaphore_wait(pltpu.get_barrier_semaphore(), 6)

    def signal_all(self):
        barrier = pltpu.get_barrier_semaphore()
        rank = self.m * 16 + lax.axis_index("dp")

        def one(step, carry):
            to = (rank + step) % 32
            pl.semaphore_signal(barrier, inc=1, device_id=(to % 16, to // 16), device_id_type=MESH)
            return carry

        lax.fori_loop(1, 32, one, 0)

    def wait_all(self):
        pl.semaphore_wait(pltpu.get_barrier_semaphore(), 31)


def remote(src, dst, send_sem, recv_sem, device):
    return pltpu.make_async_remote_copy(
        src_ref=src,
        dst_ref=dst,
        send_sem=send_sem,
        recv_sem=recv_sem,
        device_id=device,
        device_id_type=MESH,
    )


SLOT = {"c": 0, "z": 1, "y": 4, "x": 5}
SLOTS = 6
SENT = (0, 1, 1, 1, 4, 5)


class Tree:
    lag = 1
    held_back = 0
    together = False

    def stage(self, index, chunk):
        raise NotImplementedError

    def event(self, number):
        for index in range(self.count - 1 - self.held_back, -1, -1):
            chunk = number - index * self.lag
            if self.together:

                @pl.when(chunk == 0)
                def _(index=index):
                    for each in range(self.chunks):
                        self.stage(index, each)

            elif self.chunks == 1:
                pl.when(chunk == 0)(lambda index=index: self.stage(index, 0))
            else:
                pl.when((chunk >= 0) & (chunk < self.chunks))(
                    lambda index=index, chunk=chunk: self.stage(index, chunk)
                )

    @property
    def events(self):
        return self.chunks + (self.count - 1 - self.held_back) * self.lag

    def rest(self):
        def one(chunk, carry):
            self.stage(self.count - 1, chunk)
            return carry

        lax.fori_loop(0, self.chunks, one, 0)


class Spread(Tree):
    def __init__(self, place, ref, chunks, order, sems):
        self.chunks, self.ref, self.sems, self.place = chunks, ref, sems, place
        have = {"x": place.m if "x" in order else 0, "z": place.z, "y": place.y}
        mine = {"x": place.m, "y": place.y}
        self.own = have
        self.steps, self.axes = [], order
        for axis in order:
            if axis == "z":
                sends = [(have, place.far[step - 1], step) for step in (1, 2, 3)]
                waits = [(dict(have, z=(place.z + 4 - step) % 4), step) for step in (1, 2, 3)]
            else:
                sends = [(have, place.peer[axis], SLOT[axis])]
                waits = [(dict(have, **{axis: 1 - mine[axis]}), SLOT[axis])]
            self.steps.append((sends, waits))
            have = dict(have, **{axis: ALL})
        self.other = place.peer["c"]
        self.count = len(self.steps) + 2

    def _copy(self, chunk, have, device, slot):
        came = 0 if chunk == ALL else chunk
        block = self.ref.at[chunk, self.place.c, have["x"], have["z"], have["y"]]
        sent = self.sems.at[0, 0, SENT[slot]]
        return remote(block, block, sent, self.sems.at[1, came, slot], device)

    def _plane(self, chunk, core):
        plane = self.ref.at[chunk, core]
        came = 0 if chunk == ALL else chunk
        return remote(plane, plane, self.sems.at[0, 0, 0], self.sems.at[1, came, 0], self.other)

    def stage(self, index, chunk):
        if index == self.count - 1:
            self._plane(chunk, 1 - self.place.c).wait_recv()
            return
        came = [self.own]
        if index > 0:
            came = []
            for have, slot in self.steps[index - 1][1]:
                self._copy(chunk, have, self.other, slot).wait_recv()
                came.append(have)
        if index < len(self.steps):
            for have, device, slot in self.steps[index][0]:
                self._copy(chunk, have, device, slot).start()
        for have in came:
            self._copy(chunk, have, self.other, 0).start()

    def drain(self):
        for axis, (sends, _) in zip(self.axes, self.steps):
            have, _, slot = sends[0]
            if axis == "z":
                have = dict(have, z=slice(0, 3))
            self._copy(ALL, have, self.other, slot).wait_send()
        self._plane(ALL, self.place.c).wait_send()


RANKS = [(c, z, y) for z in range(4) for y in range(2) for c in range(2)]


def natural(ref, chunk, side):
    return jnp.concatenate([ref[chunk, c, side, z, y] for c, z, y in RANKS], axis=0)


def put_natural(ref, chunk, side, value):
    rows = value.shape[0] // len(RANKS)
    for spot, (c, z, y) in enumerate(RANKS):
        ref[chunk, c, side, z, y] = value[spot * rows : (spot + 1) * rows]


class Reduce(Tree):
    def __init__(self, place, full, total, lands, chunks, order, sems, finish):
        self.place, self.full, self.total, self.lands = place, full, total, lands
        self.chunks, self.sems, self.finish = chunks, sems, finish
        mine = {"x": place.m, "y": place.y}
        self.across = ALL if "x" in order else 0
        have = {"x": self.across, "z": ALL, "y": ALL}
        self.order, self.haves = order, []
        for axis in order:
            before = have
            if axis != "c":
                have = dict(have, **{axis: place.z if axis == "z" else mine[axis]})
            self.haves.append((before, have))
        self.count = len(order) + 1

    def _at(self, chunk, have):
        if self.total is None:
            return self.full.at[chunk, self.place.c, have["x"], have["z"], have["y"]]
        return self.total.at[chunk, have["x"], have["z"], have["y"]]

    def _copies(self, index, chunk):
        axis, (before, _) = self.order[index], self.haves[index]
        place, land = self.place, self.lands[axis]

        def copy(src, dst, slot, device):
            return remote(src, dst, self.sems.at[0, 0, SENT[slot]], self.sems.at[1, chunk, slot], device)

        if axis == "c":
            source = self.full.at[chunk, 1 - place.c, self.across]
            return [copy(source, land.at[chunk], SLOT[axis], place.peer[axis])]
        if axis == "z":
            return [
                copy(
                    self._at(chunk, dict(before, z=(place.z + step) % 4)),
                    land.at[chunk, step - 1],
                    step,
                    place.far[step - 1],
                )
                for step in (1, 2, 3)
            ]
        other = 1 - (place.m if axis == "x" else place.y)
        source = self._at(chunk, dict(before, **{axis: other}))
        return [copy(source, land.at[chunk], SLOT[axis], place.peer[axis])]

    def stage(self, index, chunk):
        if index > 0:
            axis, (_, have) = self.order[index - 1], self.haves[index - 1]
            land = self.lands[axis]
            for copy in self._copies(index - 1, chunk):
                copy.wait_recv()
            mine = self._at(chunk, have)
            last = index == self.count - 1
            if axis == "z":
                value = mine[...].astype(F32)
                for step in range(3):
                    value += land[chunk, step].astype(F32)
            elif last:
                value = mine[...].astype(F32) + land[chunk].astype(F32)
            else:
                value = mine[...] + land[chunk]
            if last:
                self.finish(chunk, value)
            else:
                mine[...] = value.astype(mine.dtype)
        if index < self.count - 1:
            for copy in self._copies(index, chunk):
                copy.start()

    def drain(self):
        for axis in self.order:
            land = self.lands[axis]
            slot = SLOT[axis]
            sent = self.sems.at[0, 0, SENT[slot]]
            remote(land, land, sent, self.sems.at[1, 0, slot], self.place.peer["c"]).wait_send()


class Everyone:
    def __init__(self, place, send_block, land_block, sems):
        self.rank = place.m * 16 + lax.axis_index("dp")
        self.send_block, self.land_block, self.sems = send_block, land_block, sems

    def _copy(self, step):
        to = (self.rank + step) % 32
        return remote(
            self.send_block(to),
            self.land_block(step),
            self.sems.at[0, step - 1],
            self.sems.at[1, step - 1],
            (to % 16, to // 16),
        )

    def _each(self, act):
        def one(step, carry):
            act(self._copy(step))
            return carry

        lax.fori_loop(1, 32, one, 0)

    def start(self):
        self._each(lambda copy: copy.start())

    def wait(self):
        self._each(lambda copy: copy.wait())


VROWS = 16


def rows_from_blocks(blocks, pick, counts):
    mp_count, dp_count = counts
    width = pick.shape[1]
    each = width // (mp_count * dp_count)
    wide = lax.dot_general(
        blocks, pick, NN, precision=lax.Precision.HIGHEST, preferred_element_type=F32
    )
    lane = lax.broadcasted_iota(jnp.int32, (VROWS, width), 1)
    table = jnp.zeros((VROWS, width), F32)
    for m in range(mp_count):
        for r, (c, z, y) in enumerate(RANKS):
            first = (r * mp_count + m) * each
            row = (((c * mp_count + m) * 4 + z) * 2 + y) * VROWS
            table += jnp.where((lane >= first) & (lane < first + each), wide[row : row + VROWS], 0.0)
    return table


def attend_setup(heads, m, box_full, vec_ref, box_heads, bias):
    cols = heads * HD
    for head in range(heads):
        box_heads[head] = box_full[:, head * HD : (head + 1) * HD]
    width = vec_ref.shape[1]
    own = jnp.where(m == 0, vec_ref[6:8, 0:cols], vec_ref[6:8, width - cols :])
    spread = exact_dot(jnp.broadcast_to(own[1:2], (8, cols)), pair_place(cols))
    bias[0:1, 0:cols] = own[0:1]
    bias[0:1, cols:] = spread[0:1]


def attend_trig(omega_ref, corner_ref, trig_ref):
    corner = corner_ref[...].astype(F32)
    angle_x = omega_ref[...] * ((corner[0:1] + corner[2:3]) * 0.5)
    angle_y = omega_ref[...] * ((corner[1:2] + corner[3:4]) * 0.5)
    trig_ref[0:FREQS, :] = jnp.cos(angle_x)
    trig_ref[FREQS : 2 * FREQS, :] = jnp.sin(angle_x)
    trig_ref[2 * FREQS : 3 * FREQS, :] = jnp.cos(angle_y)
    trig_ref[3 * FREQS :, :] = jnp.sin(angle_y)


def quiet(*args):
    return None


def attend_math(heads, r, weights, page_of, projected, attended):
    cols = heads * HD
    pages = r.x.shape[0] // PAGE

    def project(page, carry):
        rows = aligned(page, PAGE)
        tokens = r.x[rows, :]
        query = dot(tokens, weights(0)) + r.bias[0:1, 0:cols]
        query = query.astype(BF16) * HD ** (-0.5)
        r.qtok[rows, :] = query
        qa_rows = query.T
        for half in range(2):
            lanes = slice(half * cols, (half + 1) * cols)
            pair = dot(tokens, weights(1 + half)) + r.bias[0:1, cols + half * cols : 2 * cols + half * cols]
            pair = pair.astype(BF16)
            r.kvtok[rows, lanes] = pair
            turned = pair.T
            for spot in range(heads // 2):
                head_rows = slice((half * heads // 2 + spot) * HD, (half * heads // 2 + spot + 1) * HD)
                r.kt[head_rows, rows] = turned[2 * spot * HD : (2 * spot + 1) * HD]
                r.vt[head_rows, rows] = turned[(2 * spot + 1) * HD : (2 * spot + 2) * HD]
        trig = r.trig[:, rows]
        kft = trig.astype(BF16)
        r.kft[:, rows] = kft
        r.kftok[rows, :] = kft.T
        own, partner = turn_factors(trig)
        for head in range(heads):
            query_head = qa_rows[head * HD : (head + 1) * HD]
            proj = dot(r.box_heads[head], query_head)
            feat = proj * own + swap_blocks(proj) * partner
            r.qa[head, 0:PE, rows] = feat.astype(BF16)
            r.qa[head, PE : PE + HD, rows] = query_head
        projected(page)
        return carry

    lax.fori_loop(0, pages, project, 0)

    def attend(step, carry):
        turn, pair = step // (heads // 2), step % (heads // 2)
        rows = aligned(page_of(turn), PAGE)
        halves = []
        blank = jnp.zeros((HD, PAGE), BF16)
        for side in range(2):
            head = pair * 2 + side
            lanes = aligned(head, 2 * HD)
            left = jnp.concatenate([r.kftok[rows, :], r.kvtok[rows, lanes]], axis=1)
            score = dot(left, jnp.concatenate([r.qa[head, :, rows], blank], axis=0))
            top = jnp.max(score, axis=0, keepdims=True)
            weight = jnp.exp(score - top)
            total = jnp.sum(weight, axis=0, keepdims=True)
            value = r.vt[aligned(head, HD), rows]
            halves.append(dot(value, weight.astype(BF16)) * (1.0 / total))
            r.log[head, :, rows] = top + jnp.log(total)
        both = jnp.concatenate(halves, axis=0).astype(BF16)
        lanes = aligned(pair, 2 * HD)
        r.ctxt[lanes, rows] = both
        r.ctx[rows, lanes] = both.T
        attended(step, turn, pair)
        return carry

    lax.fori_loop(0, pages * (heads // 2), attend, 0)


def attend_buffers(heads, tokens):
    cols = heads * HD
    kept = [
        ("qa", (heads, PE + HD, tokens), BF16),
        ("qtok", (tokens, cols), BF16),
        ("kvtok", (tokens, 2 * cols), BF16),
        ("kt", (cols, tokens), BF16),
        ("kft", (PE, tokens), BF16),
        ("trig", (PE, tokens), F32),
        ("ctxt", (cols, tokens), BF16),
        ("log", (heads, 1, tokens), F32),
    ]
    used = [
        ("kftok", (tokens, PE), BF16),
        ("box_heads", (heads, PE, HD), BF16),
        ("bias", (8, 3 * cols), F32),
        ("ctx", (tokens, cols), BF16),
        ("vt", (cols, tokens), BF16),
    ]
    return kept, used


def attend_kernel(heads, names, *refs):
    r = types.SimpleNamespace(**dict(zip(names, refs)))
    attend_setup(heads, lax.axis_index("mp"), r.box, r.vec, r.box_heads, r.bias)
    attend_trig(r.omega, r.corner, r.trig)
    attend_math(heads, r, lambda chunk: r.w[chunk], lambda turn: turn, quiet, quiet)


def attend_forward(x, corners, omega, w_qkv, w_box, vecs):
    tokens = x.shape[0]
    heads = w_box.shape[1] // HD
    kept, used = attend_buffers(heads, tokens)
    outs = kept + [used[3]]
    scratch = used[:3] + used[4:]
    names = ["x", "corner", "omega", "w", "box", "vec"] + [item[0] for item in outs + scratch]
    vmem = pl.BlockSpec(memory_space=pltpu.VMEM)
    return pl.pallas_call(
        functools.partial(attend_kernel, heads, names),
        out_shape=[jax.ShapeDtypeStruct(shape, kind) for _, shape, kind in outs],
        in_specs=[vmem] * 6,
        out_specs=[vmem] * len(outs),
        scratch_shapes=[pltpu.VMEM(shape, kind) for _, shape, kind in scratch],
        compiler_params=pltpu.CompilerParams(vmem_limit_bytes=VMEM_LIMIT),
        name="attend_forward",
    )(x, corners, omega, w_qkv, w_box, vecs)


TILE = 384


def normal_parts(value):
    bell = jnp.exp(value * value * -0.5)
    t = 1.0 / (1.0 + (0.3275911 * 2.0 ** (-0.5)) * jnp.abs(value))
    tail = 0.5 * 1.061405429
    for factor in (-1.453152027, 1.421413741, -0.284496736, 0.254829592):
        tail = tail * t + 0.5 * factor
    tail = tail * t * bell
    phi = jnp.where(value < 0.0, tail, 1.0 - tail)
    return phi, phi + value * (bell * (0.5 / np.pi) ** 0.5)


def norm_stats(value):
    mean = jnp.mean(value, axis=-1, keepdims=True)
    centred = value - mean
    var = jnp.mean(centred * centred, axis=-1, keepdims=True)
    return centred, lax.rsqrt(var + NORM_EPS)


def norm_back(grad_normed, normed, scale):
    first = jnp.mean(grad_normed, axis=-1, keepdims=True)
    second = jnp.mean(grad_normed * normed, axis=-1, keepdims=True)
    return scale * (grad_normed - first - normed * second)


def col_sum(value):
    return jnp.sum(value, axis=0, keepdims=True)


def feed_math(r, hooks):
    hook = {name: quiet for name in ("entered", "grew", "turned", "shrinks", "shrank", "left")}
    hook.update(hooks)
    tokens = r.x.shape[0]
    sides = r.ctxx.shape[0]
    per_side = (r.we.shape[0] - 1) // 2
    steps = sides * per_side
    tiles = tokens // TILE
    wide = 2 * UNIT
    sum2 = dnorm = r.sum2

    def flat(ref, chunk, side):
        return ref[chunk, side] if len(ref.shape) == 4 else natural(ref, chunk, side)

    def put(ref, chunk, side, value):
        if len(ref.shape) == 4:
            ref[chunk, side] = value
        else:
            put_natural(ref, chunk, side, value)

    def two(ref, first, side):
        return jnp.concatenate([flat(ref, first, side), flat(ref, first + 1, side)], axis=1)

    def w_expand(step):
        return two(r.we, 1 + 2 * (step % per_side), step // per_side)

    def w_shrink(step):
        return two(r.ws, 2 * (step % per_side), step // per_side)

    def put_two(ref, first, side, value):
        put(ref, first, side, value[:, 0:UNIT])
        put(ref, first + 1, side, value[:, UNIT:])

    def by_halves(number):
        return (number % sides) * per_side + number // sides

    def enter(tile, carry):
        rows = aligned(tile, TILE)
        total = r.x[rows, :].astype(F32) + r.vec[4:5, :]
        for side in range(sides):
            total += dot(r.ctxx[side, rows, :], flat(r.we, 0, side), NT)
        centred, scale = norm_stats(total)
        normed = centred * scale
        r.norm1[rows, :] = normed
        r.scale1[rows, :] = scale
        shifted = normed * r.vec[0:1, :] + r.vec[1:2, :]
        r.al[rows, :] = shifted.astype(BF16)
        sum2[rows, :] = shifted + r.vec[5:6, :]
        return carry

    lax.fori_loop(0, tiles, enter, 0)
    hook["entered"]()

    def grow(number, carry):
        step = by_halves(number)
        whole = aligned(step, wide)

        def one(tile, inner):
            rows = aligned(tile, TILE)
            pre = dot(r.al[rows, :], w_expand(step)) + r.vec[pl.ds(8 + step, 1), :]
            phi, slope = normal_parts(pre)
            low = (pre * phi).astype(BF16)
            r.act[rows, whole] = low
            r.slope[rows, whole] = slope.astype(BF16)
            sum2[rows, :] += dot(low, w_shrink(step), NT)
            hook["grew"](number * tiles + tile)
            return inner

        lax.fori_loop(0, tiles, one, 0)
        return carry

    lax.fori_loop(0, steps, grow, 0)
    r.vsum[...] = jnp.zeros_like(r.vsum)

    def turn(tile, carry):
        rows = aligned(tile, TILE)
        centred, scale = norm_stats(sum2[rows, :])
        normed = centred * scale
        r.out[rows, :] = (normed * r.vec[2:3, :] + r.vec[3:4, :]).astype(BF16)
        grad = r.og[rows, :].astype(F32)
        r.vsum[2:3, :] += col_sum(grad * normed)
        r.vsum[3:4, :] += col_sum(grad)
        back = norm_back(grad * r.vec[2:3, :], normed, scale)
        r.vsum[5:6, :] += col_sum(back)
        r.dh2l[rows, :] = back.astype(BF16)
        dnorm[rows, :] = back
        hook["turned"](tile)
        return carry

    lax.fori_loop(0, tiles, turn, 0)
    r.flip[...] = r.dh2l[...].T

    def grad_shrink(number, carry):
        step = by_halves(number)
        grad = dot(r.flip[...], r.act[:, aligned(step, wide)]).astype(BF16)
        put_two(r.gs, 2 * (number // sides), number % sides, grad)
        hook["shrinks"](number)
        return carry

    lax.fori_loop(0, steps, grad_shrink, 0)

    def shrink(number, carry):
        step = by_halves(number)
        whole = aligned(step, wide)

        def one(tile, inner):
            rows = aligned(tile, TILE)
            grad = dot(r.dh2l[rows, :], w_shrink(step))
            low = (grad * r.slope[rows, whole].astype(F32)).astype(BF16)
            r.slope[rows, whole] = low
            r.vsum[pl.ds(8 + step, 1), :] += col_sum(low.astype(F32))
            dnorm[rows, :] += dot(low, w_expand(step), NT)
            hook["shrank"](number * tiles + tile)
            return inner

        lax.fori_loop(0, tiles, one, 0)
        return carry

    lax.fori_loop(0, steps, shrink, 0)

    def leave(tile, carry):
        rows = aligned(tile, TILE)
        grad = dnorm[rows, :]
        normed = r.norm1[rows, :]
        r.vsum[0:1, :] += col_sum(grad * normed)
        r.vsum[1:2, :] += col_sum(grad)
        back = norm_back(grad * r.vec[0:1, :], normed, r.scale1[rows, :])
        r.vsum[4:5, :] += col_sum(back)
        low = back.astype(BF16)
        r.dh1l[rows, :] = low
        for side in range(sides):
            r.dctx[side, rows, :] = dot(low, flat(r.we, 0, side)).astype(BF16)
        hook["left"](tile)
        return carry

    lax.fori_loop(0, tiles, leave, 0)
    r.flip[...] = r.al[...].T

    def grad_expand(number, carry):
        step = by_halves(number)
        grad = dot(r.flip[...], r.slope[:, aligned(step, wide)]).astype(BF16)
        put_two(r.ge, 1 + 2 * (number // sides), number % sides, grad)
        return carry

    lax.fori_loop(0, steps, grad_expand, 0)
    r.flip[...] = r.dh1l[...].T
    for side in range(sides):
        put(r.ge, 0, side, dot(r.flip[...], r.ctxx[side]).astype(BF16))


def feed_buffers(tokens, width, hidden):
    return [
        ("norm1", (tokens, width), F32),
        ("scale1", (tokens, 1), F32),
        ("sum2", (tokens, width), F32),
        ("al", (tokens, width), BF16),
        ("act", (tokens, hidden), BF16),
        ("slope", (tokens, hidden), BF16),
        ("dh2l", (tokens, width), BF16),
        ("flip", (width, tokens), BF16),
    ]


def feed_kernel(names, *refs):
    feed_math(types.SimpleNamespace(**dict(zip(names, refs))), {})


def feed_both(x, og, ctx, w_expand, w_shrink, vecs):
    tokens, width = x.shape
    chunks, sides = w_shrink.shape[0:2]
    outs = [
        ("out", (tokens, width), BF16),
        ("dctx", (sides, tokens, UNIT), BF16),
        ("dh1l", (tokens, width), BF16),
        ("ge", (chunks + 1, sides, width, UNIT), BF16),
        ("gs", (chunks, sides, width, UNIT), BF16),
        ("vsum", (VROWS, width), F32),
    ]
    scratch = feed_buffers(tokens, width, sides * chunks * UNIT)
    names = ["x", "og", "ctxx", "we", "ws", "vec"] + [item[0] for item in outs + scratch]
    vmem = pl.BlockSpec(memory_space=pltpu.VMEM)
    return pl.pallas_call(
        functools.partial(feed_kernel, names),
        out_shape=[jax.ShapeDtypeStruct(shape, kind) for _, shape, kind in outs],
        in_specs=[vmem] * 6,
        out_specs=[vmem] * len(outs),
        scratch_shapes=[pltpu.VMEM(shape, kind) for _, shape, kind in scratch],
        compiler_params=pltpu.CompilerParams(vmem_limit_bytes=VMEM_LIMIT),
        name="feed_both",
    )(x, og, ctx, w_expand, w_shrink, vecs)


def layer_kernel(heads, plan, inv_tokens, names, kept, used, feeds, *refs):
    r = types.SimpleNamespace(**dict(zip(names, refs)))
    cols = heads * HD
    tokens = r.x_all.shape[0]
    pages = tokens // PAGE
    own_tokens = tokens // 2
    tiles = own_tokens // TILE
    place = Place()
    place.signal()
    m, peer = place.m, place.peer["x"]
    at = (place.z, place.y)
    own = aligned(m, own_tokens)
    load_x = pltpu.make_async_copy(r.x_all.at[own, :], r.x, r.load_sem.at[0])
    load_og = pltpu.make_async_copy(r.og_all.at[own, :], r.og, r.load_sem.at[1])
    load_x.start()
    load_og.start()
    r.w[(0, place.c, 0, *at)] = r.attn[0].astype(BF16)
    for half in range(2):
        r.w[(1 + half, place.c, 0, *at)] = jnp.concatenate(
            [
                r.attn[1 + kind, :, head * HD : (head + 1) * HD].astype(BF16)
                for head in range(half * heads // 2, (half + 1) * heads // 2)
                for kind in range(2)
            ],
            axis=1,
        )
    r.box_gather[(0, place.c, 0, *at)] = r.shard_box[...]
    r.vec_gather[(0, place.c, m, *at)] = jnp.zeros((VROWS, 128), F32)
    table_at = (slice(0, r.vectors.shape[0]), slice(0, r.vectors.shape[1]))
    r.vec_gather[(0, place.c, m, *at, *table_at)] = r.vectors[...]
    r.we[(0, place.c, m, *at)] = r.merge[...].astype(BF16)
    for chunk in range(4):
        lanes = slice(chunk * UNIT, (chunk + 1) * UNIT)
        r.we[(1 + chunk, place.c, m, *at)] = r.expand[:, lanes].astype(BF16)
        r.ws[(chunk, place.c, m, *at)] = r.shrink[:, lanes].astype(BF16)
    place.wait()
    tree_v = Spread(place, r.vec_gather, 1, "xzy", r.v_sem)
    tree_b = Spread(place, r.box_gather, 1, "zy", r.b_sem)
    tree_a = Spread(place, r.w.at[0:2], 2, "zy", r.a_sem)
    tree_k = Spread(place, r.w.at[2:3], 1, "yz", r.k_sem)
    tree_a.together = True
    tree_e = Spread(place, r.we, 5, "zyx", r.e_sem)
    tree_f = Spread(place, r.ws, 4, "xzy", r.f_sem)
    tree_e.lag = tree_f.lag = 2
    first, late = 4, 2
    begun = first - late

    def weights_event(number):
        tree_e.event(number)
        tree_f.event(number)

    def finish(chunk, value):
        r.sum_f[chunk] = value * inv_tokens

    back_f = Reduce(
        place, r.gs, None, dict(c=r.fc, y=r.fy, z=r.fz, x=r.fx), 4, "cyzx", r.back_sem, finish
    )
    back_f.lag, back_f.held_back = 2, 1

    def attention(*scoped):
        q = types.SimpleNamespace(**dict(zip([item[0] for item in kept + used] + ["x"], scoped)))
        load_all = pltpu.make_async_copy(r.x_all, q.x, r.load_sem.at[2])
        load_all.start()

        tree_v.stage(0, 0)

        def begin(number, carry):
            tree_v.event(number + 1)
            tree_b.event(number)

            @pl.when(number == first - 1)
            def _():
                r.vec[...] = rows_from_blocks(
                    r.vec_gather[...].reshape(-1, 128), r.pick[...], plan
                )
                r.box_out[...] = natural(r.box_gather, 0, 0).astype(BF16)
                attend_setup(heads, m, r.box_out, r.vec, q.box_heads, q.bias)

            tree_a.event(number)
            tree_k.event(number)
            weights_event(number - late)
            pl.when(number == 0)(lambda: attend_trig(r.omega, r.corner, q.trig))
            return carry

        lax.fori_loop(0, first, begin, 0)
        keep_w = pltpu.make_async_copy(r.w, r.w_out, r.load_sem.at[3])
        keep_w.start()
        load_all.wait()

        def projected(page):
            weights_event(begun + page)

        piece = PAGE // 2

        def swap_copy(index):
            theirs = pages * (1 - m) + index
            return remote(
                q.ctx.at[aligned(theirs, piece), :],
                r.ctxx.at[m, aligned(index, piece), :],
                r.ctx_sem.at[0, index],
                r.ctx_sem.at[1, index],
                peer,
            )

        def attended(step, turn, pair):
            number = begun + pages + 2 * (step // 3) + (step % 3) // 2
            pl.when(step % 3 != 1)(lambda: weights_event(number))

            @pl.when(step == heads // 2 - 1)
            def _():
                swap_copy(2 - 2 * m).start()
                swap_copy(1).start()

            @pl.when(step == heads - 1)
            def _():
                swap_copy(2 * m).start()

        attend_math(
            heads,
            q,
            lambda chunk: natural(r.w, chunk, 0),
            lambda turn: turn * m + (pages - 1 - turn) * (1 - m),
            projected,
            attended,
        )
        stores = [
            pltpu.make_async_copy(getattr(q, name), getattr(r, name + "_out"), r.store_sem.at[k])
            for k, (name, _, _) in enumerate(kept)
        ]
        for copy in stores:
            copy.start()
        r.ctxx[m] = q.ctx[own, :]
        for index in range(pages):
            copy = remote(
                q.ctx.at[aligned(index, piece), :],
                r.ctxx.at[1 - m, aligned(index, piece), :],
                r.ctx_sem.at[0, index],
                r.ctx_sem.at[1, index],
                peer,
            )
            copy.wait_recv()
            copy.wait_send()
        for copy in stores:
            copy.wait()
        keep_w.wait()

    pl.run_scoped(
        attention,
        *[pltpu.VMEM(shape, kind) for _, shape, kind in kept + used],
        pltpu.VMEM(r.x_all.shape, BF16),
    )

    def feed(*scoped):
        q = types.SimpleNamespace(**dict(zip([item[0] for item in feeds], scoped)))
        for name in ("x", "og", "we", "ws", "vec", "ctxx", "dh1l", "ge", "gs", "vsum"):
            setattr(q, name, getattr(r, name))

        def out_copies(tile):
            rows = aligned(tile, TILE)
            there = r.out_full.at[pl.ds(pl.multiple_of(m * own_tokens + tile * TILE, TILE), TILE), :]
            return (
                pltpu.make_async_copy(q.out.at[rows, :], there, r.swap_sem.at[0, tile]),
                remote(q.out.at[rows, :], there, r.swap_sem.at[1, tile], r.swap_sem.at[2, tile], peer),
            )

        def dctx_copies(tile):
            rows = aligned(tile, TILE)
            there = r.dctx_full.at[pl.ds(pl.multiple_of(m * own_tokens + tile * TILE, TILE), TILE), :]
            return (
                pltpu.make_async_copy(q.dctx.at[m, rows, :], there, r.swap_sem.at[3, tile]),
                remote(
                    q.dctx.at[1 - m, rows, :], there, r.swap_sem.at[4, tile], r.swap_sem.at[5, tile], peer
                ),
            )

        def start(copies):
            for copy in copies:
                copy.start()

        def grew(number):
            pl.when(number % 2 == 1)(lambda: weights_event(begun + pages + 6 + number // 2))

        def shrinks(number):
            pl.when(number % 2 == 1)(lambda: back_f.event(number // 2))

        def shrank(number):
            pl.when((number >= 1) & (number <= 6))(lambda: back_f.event(number + 1))

        def left(tile):
            start(dctx_copies(tile))
            back_f.event(8 + tile)

        load_x.wait()
        load_og.wait()
        feed_math(
            q,
            dict(
                grew=grew,
                turned=lambda tile: start(out_copies(tile)),
                shrinks=shrinks,
                shrank=shrank,
                left=left,
            ),
        )
        back_f.rest()
        back_f.drain()
        for tile in range(tiles):
            for copy in out_copies(tile) + dctx_copies(tile):
                copy.wait()

    pl.run_scoped(feed, *[pltpu.VMEM(shape, kind) for _, shape, kind in feeds])
    for tree in (tree_v, tree_b, tree_a, tree_k, tree_e, tree_f):
        tree.drain()


def layer_forward(x, og, corners, omega, pick, shards, plan, inv_tokens):
    tokens, width = x.shape
    cols = shards[1].shape[1]
    heads = cols // HD
    own = tokens // 2
    unit = (width // 16, UNIT)
    kept, used = attend_buffers(heads, tokens)
    feeds = feed_buffers(own, width, 8 * UNIT)
    feeds += [("out", (own, width), BF16), ("dctx", (2, own, UNIT), BF16)]
    free = pl.BlockSpec(memory_space=pl.ANY)
    vmem = pl.BlockSpec(memory_space=pltpu.VMEM)
    inputs = [("x_all", free), ("og_all", free), ("corner", vmem), ("omega", vmem), ("pick", vmem)]
    inputs += [(name, vmem) for name in ("attn", "shard_box", "vectors", "merge", "expand", "shrink")]
    outs = [(name + "_out", shape, kind, free) for name, shape, kind in kept]
    outs += [
        ("w_out", (3, 2, 1, 4, 2, *unit), BF16, free),
        ("box_out", (PE, cols), BF16, vmem),
        ("out_full", (tokens, width), BF16, free),
        ("dctx_full", (tokens, cols), BF16, free),
        ("dh1l", (own, width), BF16, vmem),
        ("ge", (5, 2, 2, 4, 2, *unit), BF16, vmem),
        ("vsum", (VROWS, width), F32, vmem),
        ("sum_f", (4, *unit), F32, vmem),
    ]
    dma = pltpu.SemaphoreType.DMA
    scratch = [
        ("x", pltpu.VMEM((own, width), BF16)),
        ("og", pltpu.VMEM((own, width), BF16)),
        ("vec", pltpu.VMEM((VROWS, width), F32)),
        ("w", pltpu.VMEM((3, 2, 1, 4, 2, *unit), BF16)),
        ("box_gather", pltpu.VMEM((1, 2, 1, 4, 2, PE // 16, cols), F32)),
        ("vec_gather", pltpu.VMEM((1, 2, 2, 4, 2, VROWS, 128), F32)),
        ("we", pltpu.VMEM((5, 2, 2, 4, 2, *unit), BF16)),
        ("ws", pltpu.VMEM((4, 2, 2, 4, 2, *unit), BF16)),
        ("ctxx", pltpu.VMEM((2, own, cols), BF16)),
        ("gs", pltpu.VMEM((4, 2, 2, 4, 2, *unit), BF16)),
        ("fc", pltpu.VMEM((4, 2, 4, 2, *unit), BF16)),
        ("fy", pltpu.VMEM((4, 2, 4, *unit), BF16)),
        ("fz", pltpu.VMEM((4, 3, 2, *unit), BF16)),
        ("fx", pltpu.VMEM((4, *unit), BF16)),
        ("ctx_sem", dma((2, 3))),
        ("a_sem", dma((2, 2, SLOTS))),
        ("k_sem", dma((2, 1, SLOTS))),
        ("b_sem", dma((2, 1, SLOTS))),
        ("v_sem", dma((2, 1, SLOTS))),
        ("e_sem", dma((2, 5, SLOTS))),
        ("f_sem", dma((2, 4, SLOTS))),
        ("back_sem", dma((2, 4, SLOTS))),
        ("load_sem", dma((4,))),
        ("store_sem", dma((len(kept),))),
        ("swap_sem", dma((6, own // TILE))),
    ]
    names = [item[0] for item in inputs + outs + scratch]
    return pl.pallas_call(
        functools.partial(layer_kernel, heads, plan, inv_tokens, names, kept, used, feeds),
        out_shape=[jax.ShapeDtypeStruct(shape, kind) for _, shape, kind, _ in outs],
        in_specs=[item[1] for item in inputs],
        out_specs=[item[3] for item in outs],
        scratch_shapes=[item[1] for item in scratch],
        compiler_params=pltpu.CompilerParams(
            vmem_limit_bytes=VMEM_LIMIT, collective_id=0, has_side_effects=True
        ),
        name="layer_forward",
    )(x, og, corners, omega, pick, *shards)


def pair_place(cols):
    spot = lax.broadcasted_iota(jnp.int32, (cols, 2 * cols), 0)
    lane = lax.broadcasted_iota(jnp.int32, (cols, 2 * cols), 1)
    target = ((spot >> 6) << 7) + HD + (spot & (HD - 1))
    return jnp.where(lane == target, 1.0, 0.0)


def exact_dot(lhs, rhs, dims=NN):
    return lax.dot_general(
        lhs, rhs, dims, precision=lax.Precision.HIGHEST, preferred_element_type=F32
    )


def attend_back_kernel(heads, plan, inv_tokens, *refs):
    inputs, refs = refs[:12], refs[12:]
    if plan is not None:
        load_sem, held, refs = refs[-1], refs[-13:-1], refs[:-13]
        loads = [
            pltpu.make_async_copy(src, dst, load_sem.at[k]) for k, (src, dst) in enumerate(zip(inputs, held))
        ]
        early = (0, 2, 7, 11)
        for k in sorted(range(12), key=lambda k: k not in early):
            loads[k].start()
        inputs = held
    x_ref, w_ref, box_ref, *inputs = inputs
    qa_ref, qtok_ref, kvtok_ref, kt_ref, kft_ref, trig_ref, ctxt_ref, log_ref, dctx_ref = inputs
    cols = heads * HD
    tokens = x_ref.shape[0]
    pages = tokens // PAGE
    m = lax.axis_index("mp")
    piece = PAGE // 2
    pieces = 2 * pages
    lane = lax.broadcasted_iota(jnp.int32, (1, 2 * HD), 1)
    lower = lane < HD
    if plan is None:
        inp_ref, gw_ref, gbox_ref, qvsum_ref, *refs = refs
        kftok, dctxt, boxt, dtok, xt, gbox = refs
        before, after = 0, 0

        def background(number):
            pass
    else:
        dh1_ref, vsum_ref, sumf_ref, pick_ref, full_e, *refs = refs
        inp_ref, sum_e, sum_a, sum_b, sum_v, norm_ref, *refs = refs
        kftok, dctxt, boxt, dtok, xt, gbox, *refs = refs
        came, total_e, full_a, full_b, full_v, land_v, norms, *refs = refs
        ec, ey, ez, ex, ac, ay, az, bc, by, bz, *refs = refs
        e_sem, a_sem, b_sem, v_sem, n_sem, i_sem, loc_sem = refs
        place = Place()
        place.signal_all()
        fill = pltpu.make_async_copy(full_e.at[:, place.c], total_e, loc_sem.at[0])
        fill.start()
        place.wait_all()

        def finish(out):
            def put(chunk, value):
                out[chunk] = value * inv_tokens

            return put

        tree_e = Reduce(
            place, full_e, total_e, dict(c=ec, y=ey, z=ez, x=ex), 5, "cyzx", e_sem, finish(sum_e)
        )
        tree_e.lag, tree_e.held_back = 2, 1
        tree_a = Reduce(place, full_a, None, dict(c=ac, y=ay, z=az), 3, "cyz", a_sem, finish(sum_a))
        tree_b = Reduce(place, full_b, None, dict(c=bc, y=by, z=bz), 1, "cyz", b_sem, finish(sum_b))

        def block_of(rank):
            r = rank % 16
            return full_v.at[rank // 16, r // 4, (r // 2) % 2, r % 2]

        spot = (place.m, place.z, place.y, place.c)
        all_v = Everyone(place, block_of, lambda step: land_v.at[step - 1], v_sem)
        all_n = Everyone(place, lambda rank: norms.at[spot], lambda step: norms.at[spot], n_sem)

        def background(number):
            tree_e.event(number)

        background(0)
        fill.wait()
        for k in early:
            loads[k].wait()

    boxt[...] = box_ref[...].T
    gbox[...] = jnp.zeros_like(gbox)

    def prepare(page, carry):
        rows = aligned(page, PAGE)
        kftok[rows, :] = kft_ref[:, rows].T
        dctxt[:, rows] = dctx_ref[rows, :].T
        xt[:, rows] = x_ref[rows, :].T
        if plan is not None:
            pl.when(page > 0)(lambda: background(page))
        return carry

    lax.fori_loop(0, pages, prepare, 0)
    if plan is not None:
        for k in range(12):
            if k not in early:
                loads[k].wait()

    def attend(step, carry):
        page, pair = step // (heads // 2), step % (heads // 2)
        rows = aligned(page, PAGE)
        own, partner = turn_factors(trig_ref[:, rows])
        pair_lanes = aligned(pair, 2 * HD)
        query_pair = qtok_ref[rows, pair_lanes]
        dctx_pair = dctx_ref[rows, pair_lanes]
        halves = []
        boxes = []
        blank = jnp.zeros((HD, PAGE), BF16)
        for side in range(2):
            head = pair * 2 + side
            lanes = aligned(head, 2 * HD)
            key_value = kvtok_ref[rows, lanes]
            left = jnp.concatenate([kftok[rows, :], key_value], axis=1)
            score = dot(left, jnp.concatenate([qa_ref[head, :, rows], blank], axis=0))
            prob = jnp.exp(score - log_ref[head, :, rows])
            prob_low = prob.astype(BF16)
            head_rows = pl.ds(pl.multiple_of(head * HD, HD), HD)
            dctx_head = dctxt[head_rows, rows]
            grad_prob = dot(
                key_value, jnp.concatenate([blank, dctx_head], axis=0)
            )
            inner = col_sum(dctx_head.astype(F32) * ctxt_ref[head_rows, rows].astype(F32))
            grad_score = (prob * (grad_prob - inner)).astype(BF16)
            if side == 0:
                both = jnp.concatenate([query_pair[:, 0:HD], dctx_pair[:, 0:HD]], axis=1)
            else:
                both = jnp.concatenate([query_pair[:, HD:], dctx_pair[:, HD:]], axis=1)
            from_score = dot(grad_score, both)
            from_prob = dot(prob_low, both)
            grad_kv = jnp.where(lower, from_score, from_prob).astype(BF16)
            dtok[rows, pl.ds(pl.multiple_of(cols + head * 2 * HD, 2 * HD), 2 * HD)] = grad_kv
            keys = jnp.concatenate([kft_ref[:, rows], kt_ref[head_rows, rows]], axis=0)
            grad_query = dot(keys, grad_score) * HD ** (-0.5)
            feat = grad_query[0:PE]
            proj = (feat * own - swap_blocks(feat) * partner).astype(BF16)
            halves.append(grad_query[PE:] + dot(boxt[head_rows, :], proj))
            boxes.append(dot(proj, query_pair))
        gbox[:, pair_lanes] += jnp.where(lower, boxes[0], boxes[1])
        dtok[rows, pair_lanes] = jnp.concatenate(halves, axis=0).astype(BF16).T
        return carry

    def weights(chunk):
        return w_ref[chunk] if plan is None else natural(w_ref, chunk, 0)

    def spread(page):
        rows = aligned(page, PAGE)
        return sum(
            dot(dtok[rows, chunk * UNIT : (chunk + 1) * UNIT], weights(chunk), NT) for chunk in range(3)
        )

    if plan is None:
        lax.fori_loop(0, pages * (heads // 2), attend, 0)
        gbox_ref[...] = gbox[...] * HD**0.5

        def spread_page(page, carry):
            inp_ref[aligned(page, PAGE), :] = spread(page)
            return carry

        lax.fori_loop(0, pages, spread_page, 0)

        def gather(step, carry):
            lanes = aligned(step, UNIT)
            gw_ref[step] = dot(xt[...], dtok[:, lanes]).astype(BF16)
            qvsum_ref[0:1, lanes] = col_sum(dtok[:, lanes].astype(F32))
            return carry

        lax.fori_loop(0, 3, gather, 0)
        return

    def swap(index):
        rows = aligned(index, piece)
        return remote(
            inp_ref.at[rows, :], came.at[rows, :], i_sem.at[0, index], i_sem.at[1, index], place.peer["x"]
        )

    def attend_and_send(step, carry):
        attend(step, carry)
        page = step // (heads // 2)

        @pl.when(step % (heads // 2) == heads // 2 - 1)
        def _():
            value = spread(page)
            for half in range(2):
                index = 2 * page + half
                rows = aligned(index, piece)
                own = index // pages == m
                spot = aligned(index % pages, piece)
                extra = jnp.where(own, dh1_ref[spot, :].astype(F32), 0.0)
                inp_ref[rows, :] = (value[half * piece : (half + 1) * piece] + extra).astype(BF16)
                swap(index).start()

        background(step + pages)
        return carry

    lax.fori_loop(0, pages * (heads // 2), attend_and_send, 0)
    put_natural(full_b, 0, 0, gbox[...] * HD**0.5)

    def gather(step, carry):
        grad = dot(xt[...], dtok[:, aligned(step, UNIT)]).astype(BF16)
        put_natural(full_a, step, 0, grad)
        tree_a.event(step)
        tree_b.event(step)
        return carry

    lax.fori_loop(0, 3, gather, 0)

    sums = jnp.concatenate(
        [
            col_sum(dtok[:, chunk * UNIT : (chunk + 1) * UNIT].astype(F32)) for chunk in range(3)
        ],
        axis=1,
    )
    values = exact_dot(jnp.broadcast_to(sums[:, cols:], (8, 2 * cols)), pair_place(cols), NT)
    pair = jnp.concatenate([sums[:, 0:cols], values[0:1]], axis=0)
    blank = jnp.zeros_like(pair)
    pair = jnp.where(
        m == 0, jnp.concatenate([pair, blank], axis=1), jnp.concatenate([blank, pair], axis=1)
    )
    table = jnp.concatenate([vsum_ref[0:6, :], pair, vsum_ref[8:, :]], axis=0)
    mp_count, dp_count = plan
    width = table.shape[1]
    each = width // (mp_count * dp_count)
    wide_lane = lax.broadcasted_iota(jnp.int32, (VROWS, width), 1)
    for side in range(mp_count):
        parts = []
        for r in range(dp_count):
            first = (r * mp_count + side) * each
            parts.append(jnp.where((wide_lane >= first) & (wide_lane < first + each), table, 0.0))
        block = exact_dot(jnp.concatenate(parts, axis=0), pick_ref[...], NT)
        full_v[side] = block.reshape(full_v.shape[1:])
    all_v.start()

    def tail(number, carry):
        tree_a.event(number)
        tree_b.event(number)
        return carry

    lax.fori_loop(3, tree_a.events, tail, 0)
    tree_e.rest()
    all_v.wait()
    total_v = full_v[spot] + jnp.sum(land_v[...], axis=0)
    sum_v[0] = total_v * inv_tokens

    square = sum(jnp.sum(out[...] * out[...]) for out in (sum_e, sumf_ref, sum_a, sum_b, sum_v))
    norms[spot] = jnp.full((8, 128), square, F32)
    all_n.start()

    def final(number, carry):
        rows = aligned(number, piece)
        swap(number).wait()
        inp_ref[rows, :] = (inp_ref[rows, :].astype(F32) + came[rows, :].astype(F32)).astype(BF16)
        return carry

    lax.fori_loop(0, pieces, final, 0)
    all_n.wait()
    every = norms[...].reshape(-1, 8, 128)
    norm_ref[...] = jnp.sqrt(sum(every[k] for k in range(every.shape[0])))
    for tree in (tree_e, tree_a, tree_b):
        tree.drain()


def attend_backward(x, weight, box, kept, dctx, plan, inv_tokens, more=()):
    tokens, width = x.shape
    cols = weight.shape[-1]
    heads = cols // HD
    vmem = pl.BlockSpec(memory_space=pltpu.VMEM)
    scratch = [
        pltpu.VMEM((tokens, PE), BF16),
        pltpu.VMEM((cols, tokens), BF16),
        pltpu.VMEM((cols, PE), BF16),
        pltpu.VMEM((tokens, 3 * cols), BF16),
        pltpu.VMEM((width, tokens), BF16),
        pltpu.VMEM((PE, cols), F32),
    ]
    in_specs = [vmem] * 12
    if plan is None:
        shapes = [
            ((tokens, width), F32),
            ((3, width, cols), BF16),
            ((PE, cols), F32),
            ((8, 3 * cols), F32),
        ]
        extra = {}
    else:
        free = pl.BlockSpec(memory_space=pl.ANY)
        in_specs = [free] * 12 + [vmem] * 4 + [free]
        rows = width // 16
        unit = (rows, UNIT)
        tile = (PE // 16, cols)
        small = (VROWS, 128)
        shapes = [
            ((tokens, width), BF16),
            ((5, *unit), F32),
            ((3, *unit), F32),
            ((1, *tile), F32),
            ((1, *small), F32),
            ((8, 128), F32),
        ]
        scratch += [
            pltpu.VMEM((tokens, width), BF16),
            pltpu.VMEM((5, 2, 4, 2, *unit), BF16),
            pltpu.VMEM((3, 2, 1, 4, 2, *unit), BF16),
            pltpu.VMEM((1, 2, 1, 4, 2, *tile), F32),
            pltpu.VMEM((2, 4, 2, 2, *small), F32),
            pltpu.VMEM((31, *small), F32),
            pltpu.VMEM((2, 4, 2, 2, 8, 128), F32),
            pltpu.VMEM((5, 2, 4, 2, *unit), BF16),
            pltpu.VMEM((5, 2, 4, *unit), BF16),
            pltpu.VMEM((5, 3, 2, *unit), BF16),
            pltpu.VMEM((5, *unit), BF16),
            pltpu.VMEM((3, 4, 2, *unit), BF16),
            pltpu.VMEM((3, 4, *unit), BF16),
            pltpu.VMEM((3, 3, *unit), BF16),
            pltpu.VMEM((1, 4, 2, *tile), F32),
            pltpu.VMEM((1, 4, *tile), F32),
            pltpu.VMEM((1, 3, *tile), F32),
            pltpu.SemaphoreType.DMA((2, 5, SLOTS)),
            pltpu.SemaphoreType.DMA((2, 3, SLOTS)),
            pltpu.SemaphoreType.DMA((2, 1, SLOTS)),
            pltpu.SemaphoreType.DMA((2, 31)),
            pltpu.SemaphoreType.DMA((2, 31)),
            pltpu.SemaphoreType.DMA((2, 2 * (tokens // PAGE))),
            pltpu.SemaphoreType.DMA((2,)),
        ]
        scratch += [pltpu.VMEM(array.shape, array.dtype) for array in (x, weight, box, *kept, dctx)]
        scratch.append(pltpu.SemaphoreType.DMA((12,)))
        extra = dict(collective_id=2, has_side_effects=True)
    return pl.pallas_call(
        functools.partial(attend_back_kernel, heads, plan, inv_tokens),
        out_shape=[jax.ShapeDtypeStruct(s, d) for s, d in shapes],
        in_specs=in_specs,
        out_specs=[vmem] * len(shapes),
        scratch_shapes=scratch,
        compiler_params=pltpu.CompilerParams(vmem_limit_bytes=VMEM_LIMIT, **extra),
        name="attend_backward",
    )(x, weight, box, *kept, dctx, *more)


def adam_step(master, first, second, gradient, rate, decay):
    new_first = BETA_ONE * first + (1.0 - BETA_ONE) * gradient
    new_second = BETA_TWO * second + (1.0 - BETA_TWO) * gradient * gradient
    first_hat = new_first / (1.0 - BETA_ONE**STEP)
    second_hat = new_second / (1.0 - BETA_TWO**STEP)
    new_master = master - rate * (first_hat / (jnp.sqrt(second_hat) + ADAM_EPS) + decay * master)
    return (new_first, new_second, new_master)


def adam_kernel(heads, norm_ref, *refs):
    sum_e, sum_f, sum_a, sum_b, sum_v, *refs = refs
    states, outs = refs[:18], refs[18:]
    outs[-1][...] = norm_ref[0:1, 0:1]
    clip = CLIP_LIMIT / jnp.maximum(norm_ref[0:1, 0:1], CLIP_LIMIT)

    def update(first, out, gradient, at, rate, decay):
        news = adam_step(*(ref[at] for ref in states[first : first + 3]), gradient * clip, rate, decay)
        for ref, new in zip(outs[out : out + 3], news):
            ref[at] = new
        if decay:
            outs[out + 3][at] = news[2].astype(BF16)

    def heads_of(kind):
        half = heads // 2
        return jnp.concatenate(
            [
                sum_a[1 + head // half, :, (2 * (head % half) + kind) * HD : (2 * (head % half) + kind + 1) * HD]
                for head in range(heads)
            ],
            axis=1,
        )

    for index, gradient in enumerate((sum_a[0], heads_of(0), heads_of(1))):
        update(0, 0, gradient, index, RATE_MATRIX, WEIGHT_DECAY)
    update(3, 4, sum_b[0], ALL, RATE_MATRIX, WEIGHT_DECAY)
    update(6, 8, sum_e[0], ALL, RATE_MATRIX, WEIGHT_DECAY)
    for chunk in range(4):
        lanes = (ALL, slice(chunk * UNIT, (chunk + 1) * UNIT))
        update(9, 12, sum_e[1 + chunk], lanes, RATE_MATRIX, WEIGHT_DECAY)
        update(12, 16, sum_f[chunk], lanes, RATE_MATRIX, WEIGHT_DECAY)
    rows, each = states[15].shape
    update(15, 20, sum_v[0, 0:rows, 0:each], ALL, RATE_VECTOR, 0.0)


def adam_all(norm, sums, states):
    shapes = []
    for first in range(0, 18, 3):
        shapes += [(states[first].shape, F32)] * 3
        if first < 15:
            shapes.append((states[first].shape, BF16))
    vmem = pl.BlockSpec(memory_space=pltpu.VMEM)
    shapes.append(((1, 1), F32))
    return pl.pallas_call(
        functools.partial(adam_kernel, states[0].shape[2] // HD),
        out_shape=[jax.ShapeDtypeStruct(s, d) for s, d in shapes],
        in_specs=[vmem] * (6 + len(states)),
        out_specs=[vmem] * len(shapes),
        compiler_params=pltpu.CompilerParams(vmem_limit_bytes=VMEM_LIMIT),
        name="adam_all",
    )(norm, *sums, *states)


def pack_qkv(shard):
    rows, cols = shard.shape[1:]
    heads = cols // HD
    pairs = jnp.stack([shard[1].reshape(rows, heads, HD), shard[2].reshape(rows, heads, HD)], axis=2)
    pairs = pairs.reshape(rows, 2, cols)
    return jnp.stack([shard[0], pairs[:, 0], pairs[:, 1]])


def unpack_qkv(packed):
    rows, cols = packed.shape[1:]
    pairs = jnp.concatenate([packed[1], packed[2]], axis=1).reshape(rows, cols // HD, 2, HD)
    return jnp.stack(
        [packed[0], pairs[:, :, 0].reshape(rows, cols), pairs[:, :, 1].reshape(rows, cols)]
    )


def to_chunks(shard):
    rows = shard.shape[0]
    return shard.reshape(rows, -1, UNIT).transpose(1, 0, 2)


def from_chunks(chunks):
    return chunks.transpose(1, 0, 2).reshape(chunks.shape[1], -1)


def on_device(
    layer_input,
    page_boxes,
    output_grad,
    attn_proj,
    attn_first,
    attn_second,
    box_proj,
    box_first,
    box_second,
    merge_proj,
    merge_first,
    merge_second,
    expand_proj,
    expand_first,
    expand_second,
    shrink_proj,
    shrink_first,
    shrink_second,
    vectors,
    vector_first,
    vector_second,
):
    mp_count = lax.axis_size("mp")
    dp_count = lax.axis_size("dp")
    mp_index = lax.axis_index("mp")
    tokens, width = layer_input.shape
    cols = attn_proj.shape[2]
    heads = cols // HD
    own_tokens = tokens // mp_count
    inv_tokens = 1.0 / (tokens * dp_count)

    corners = page_boxes.T
    omega = (10000.0 ** (-np.arange(FREQS, dtype=np.float64) / FREQS)).astype(np.float32)[:, None]
    omega = jnp.asarray(omega)
    plan = (mp_count, dp_count) if dp_count == 16 and mp_count == 2 else None
    if plan is not None:
        each = vectors.shape[1]
        pick = np.zeros((128, width), np.float32)
        pick[np.arange(width) % each, np.arange(width)] = 1.0
        pick = jnp.asarray(pick)
        *kept, w_qkv, w_box, layer_out, dctx, dh1, g_expand, vec_sum, sum_f = layer_forward(
            layer_input,
            output_grad,
            corners,
            omega,
            pick,
            (attn_proj, box_proj, vectors, merge_proj.T, expand_proj, shrink_proj.T),
            plan,
            inv_tokens,
        )
        input_grad, sum_e, sum_a, sum_b, sum_v, norm = attend_backward(
            layer_input,
            w_qkv,
            w_box,
            kept,
            dctx,
            plan,
            inv_tokens,
            (dh1, vec_sum, sum_f, pick, g_expand),
        )
        merge = [merge_proj.T, merge_first.T, merge_second.T]
        shrink = [shrink_proj.T, shrink_first.T, shrink_second.T]
        *results, norm = adam_all(
            norm,
            (sum_e, sum_f, sum_a, sum_b, sum_v),
            [attn_proj, attn_first, attn_second, box_proj, box_first, box_second, *merge]
            + [expand_proj, expand_first, expand_second, *shrink, vectors, vector_first, vector_second],
        )
        turned = (8, 9, 10, 11, 16, 17, 18, 19)
        results = [out.T if k in turned else out for k, out in enumerate(results)]
        return (layer_out, input_grad, norm.reshape(()), *results)
    shard_qkv = pack_qkv(attn_proj).astype(BF16)
    shard_e = jnp.concatenate([merge_proj.T[None], to_chunks(expand_proj)]).astype(BF16)
    shard_f = to_chunks(shrink_proj.T).astype(BF16)
    w_qkv = lax.all_gather(shard_qkv, "dp", axis=1, tiled=True)
    w_box = lax.all_gather(box_proj.astype(BF16), "dp", axis=0, tiled=True)
    w_expand = lax.all_gather(lax.all_gather(shard_e, "dp", axis=1, tiled=True), "mp", axis=1)
    w_shrink = lax.all_gather(lax.all_gather(shard_f, "dp", axis=1, tiled=True), "mp", axis=1)
    vecs = lax.all_gather(vectors, ("dp", "mp"), axis=1, tiled=True)
    vecs = jnp.pad(vecs, ((0, VROWS - vecs.shape[0]), (0, 0)))
    *kept, context = attend_forward(layer_input, corners, omega, w_qkv, w_box, vecs)
    context = lax.all_to_all(
        context.reshape(mp_count, own_tokens, cols), "mp", split_axis=0, concat_axis=0
    )

    def own_rows(array):
        return lax.dynamic_slice_in_dim(array, mp_index * own_tokens, own_tokens)

    layer_out, dctx, dh1, g_expand, g_shrink, vec_sum = feed_both(
        own_rows(layer_input), own_rows(output_grad), context, w_expand, w_shrink, vecs
    )
    g_feed = jnp.concatenate([g_expand, g_shrink])
    layer_out = lax.all_gather(layer_out, "mp", axis=0, tiled=True)
    dctx = lax.all_to_all(dctx, "mp", split_axis=0, concat_axis=0).reshape(tokens, cols)
    part, g_qkv, g_box, qkv_sum = attend_backward(
        layer_input, w_qkv, w_box, kept, dctx, None, inv_tokens
    )
    own_part = lax.psum_scatter(part.astype(BF16), "mp", scatter_dimension=0, tiled=True)
    own_grad = (own_part.astype(F32) + dh1).astype(BF16)
    input_grad = lax.all_gather(own_grad, "mp", axis=0, tiled=True)
    shard_attn = unpack_qkv(
        lax.psum_scatter(g_qkv, "dp", scatter_dimension=1, tiled=True).astype(F32) * inv_tokens
    )
    shard_box = lax.psum_scatter(g_box, "dp", scatter_dimension=0, tiled=True) * inv_tokens
    sum_feed = lax.psum_scatter(g_feed, "dp", scatter_dimension=2, tiled=True)
    sum_feed = lax.psum_scatter(sum_feed, "mp", scatter_dimension=1, tiled=True)[:, 0]
    sum_feed = sum_feed.astype(F32) * inv_tokens
    sum_expand, sum_shrink = sum_feed[0:5], sum_feed[5:]

    def placed(row):
        return lax.dynamic_update_slice_in_dim(
            jnp.zeros((width,), F32), row, mp_index * cols, 0
        )[None, :]

    value_sum = qkv_sum[0, cols:].reshape(heads, 2, HD)[:, 1].reshape(cols)
    vector_grad = jnp.concatenate(
        [vec_sum[0:6], placed(qkv_sum[0, 0:cols]), placed(value_sum), vec_sum[8:12]]
    )
    vector_shard = (
        lax.psum_scatter(vector_grad, ("dp", "mp"), scatter_dimension=1, tiled=True) * inv_tokens
    )
    square = sum(
        jnp.sum(shard * shard)
        for shard in (shard_attn, shard_box, sum_expand, sum_shrink, vector_shard)
    )
    grad_norm = jnp.sqrt(lax.psum(square, ("dp", "mp")))
    shard_merge = sum_expand[0].T
    shard_expand = from_chunks(sum_expand[1:])
    shard_shrink = from_chunks(sum_shrink).T
    clip_scale = CLIP_LIMIT / jnp.maximum(grad_norm, CLIP_LIMIT)
    results = [layer_out, input_grad, grad_norm]
    for master, first, second, shard in (
        (attn_proj, attn_first, attn_second, shard_attn),
        (box_proj, box_first, box_second, shard_box),
        (merge_proj, merge_first, merge_second, shard_merge),
        (expand_proj, expand_first, expand_second, shard_expand),
        (shrink_proj, shrink_first, shrink_second, shard_shrink),
    ):
        new_first, new_second, new_master = adam_step(
            master, first, second, shard * clip_scale, RATE_MATRIX, WEIGHT_DECAY
        )
        results += [new_first, new_second, new_master, new_master.astype(BF16)]
    results += adam_step(
        vectors, vector_first, vector_second, vector_shard * clip_scale, RATE_VECTOR, 0.0
    )
    return tuple(results)


def solution(mesh):
    rows = P("dp", None)
    attn = P(None, "dp", "mp")
    tall = P("dp", "mp")
    wide = P("mp", "dp")
    vector = P(None, ("dp", "mp"))
    in_specs = (rows,) * 3 + (attn,) * 3 + (tall,) * 3 + (wide,) * 3 + (tall,) * 3 + (wide,) * 3
    in_specs += (vector,) * 3
    out_specs = (rows, rows, P()) + (attn,) * 4 + (tall,) * 4 + (wide,) * 4 + (tall,) * 4
    out_specs += (wide,) * 4 + (vector,) * 3
    return jax.shard_map(
        on_device, mesh=mesh, in_specs=in_specs, out_specs=out_specs, check_vma=False
    )
```

```python
import functools
import types

import jax
import jax.numpy as jnp
import numpy as np
from jax import lax
from jax.experimental import pallas as pl
from jax.experimental.pallas import tpu as pltpu
from jax.sharding import PartitionSpec as P

HD = 64
FREQS = 32
PE = 128
PAGE = 512
STEP = 10

NORM_EPS = 1e-12
CLIP_LIMIT = 0.1
BETA_ONE = 0.9
BETA_TWO = 0.999
ADAM_EPS = 1e-08
RATE_MATRIX = 0.05
RATE_VECTOR = 0.5
WEIGHT_DECAY = 0.01

F32 = jnp.float32
BF16 = jnp.bfloat16
VMEM_LIMIT = 60 * 1024 * 1024

NN = (((1,), (0,)), ((), ()))
NT = (((1,), (1,)), ((), ()))
TN = (((0,), (0,)), ((), ()))


def dot(lhs, rhs, dims=NN):
    return lax.dot_general(lhs, rhs, dims, preferred_element_type=F32)


def aligned(index, size):
    return pl.ds(pl.multiple_of(index * size, size), size)


def swap_blocks(feat):
    return jnp.concatenate(
        [
            feat[FREQS : 2 * FREQS],
            feat[0:FREQS],
            feat[3 * FREQS :],
            feat[2 * FREQS : 3 * FREQS],
        ],
        axis=0,
    )


def turn_factors(trig):
    cos_x, sin_x = trig[0:FREQS], trig[FREQS : 2 * FREQS]
    cos_y, sin_y = trig[2 * FREQS : 3 * FREQS], trig[3 * FREQS :]
    return (
        jnp.concatenate([sin_x, sin_x, sin_y, sin_y], axis=0),
        jnp.concatenate([cos_x, -cos_x, cos_y, -cos_y], axis=0),
    )


MESH = pl.DeviceIdType.MESH
ALL = slice(None)
UNIT = 384


class Place:
    def __init__(self):
        rank = lax.axis_index("dp")
        self.m = lax.axis_index("mp")
        self.z = rank // 4
        self.y = (rank // 2) % 2
        self.c = rank % 2
        self.peer = {
            "x": (rank, 1 - self.m),
            "y": (rank + 2 - 4 * self.y, self.m),
            "c": (rank + 1 - 2 * self.c, self.m),
        }
        self.far = [((rank + 4 * step) % 16, self.m) for step in (1, 2, 3)]

    def signal(self):
        barrier = pltpu.get_barrier_semaphore()
        for device in list(self.peer.values()) + self.far:
            pl.semaphore_signal(barrier, inc=1, device_id=device, device_id_type=MESH)

    def wait(self):
        pl.semaphore_wait(pltpu.get_barrier_semaphore(), 6)

    def signal_all(self):
        barrier = pltpu.get_barrier_semaphore()
        rank = self.m * 16 + lax.axis_index("dp")

        def one(step, carry):
            to = (rank + step) % 32
            pl.semaphore_signal(barrier, inc=1, device_id=(to % 16, to // 16), device_id_type=MESH)
            return carry

        lax.fori_loop(1, 32, one, 0)

    def wait_all(self):
        pl.semaphore_wait(pltpu.get_barrier_semaphore(), 31)


def remote(src, dst, send_sem, recv_sem, device):
    return pltpu.make_async_remote_copy(
        src_ref=src,
        dst_ref=dst,
        send_sem=send_sem,
        recv_sem=recv_sem,
        device_id=device,
        device_id_type=MESH,
    )


SLOT = {"c": 0, "z": 1, "y": 4, "x": 5}
SLOTS = 6
SENT = (0, 1, 1, 1, 4, 5)


class Tree:
    lag = 1
    held_back = 0
    together = False

    def stage(self, index, chunk):
        raise NotImplementedError

    def event(self, number):
        for index in range(self.count - 1 - self.held_back, -1, -1):
            chunk = number - index * self.lag
            if self.together:

                @pl.when(chunk == 0)
                def _(index=index):
                    for each in range(self.chunks):
                        self.stage(index, each)

            elif self.chunks == 1:
                pl.when(chunk == 0)(lambda index=index: self.stage(index, 0))
            else:
                pl.when((chunk >= 0) & (chunk < self.chunks))(
                    lambda index=index, chunk=chunk: self.stage(index, chunk)
                )

    @property
    def events(self):
        return self.chunks + (self.count - 1 - self.held_back) * self.lag

    def rest(self):
        def one(chunk, carry):
            self.stage(self.count - 1, chunk)
            return carry

        lax.fori_loop(0, self.chunks, one, 0)


class Spread(Tree):
    def __init__(self, place, ref, chunks, order, sems):
        self.chunks, self.ref, self.sems, self.place = chunks, ref, sems, place
        have = {"x": place.m if "x" in order else 0, "z": place.z, "y": place.y}
        mine = {"x": place.m, "y": place.y}
        self.own = have
        self.steps, self.axes = [], order
        for axis in order:
            if axis == "z":
                sends = [(have, place.far[step - 1], step) for step in (1, 2, 3)]
                waits = [(dict(have, z=(place.z + 4 - step) % 4), step) for step in (1, 2, 3)]
            else:
                sends = [(have, place.peer[axis], SLOT[axis])]
                waits = [(dict(have, **{axis: 1 - mine[axis]}), SLOT[axis])]
            self.steps.append((sends, waits))
            have = dict(have, **{axis: ALL})
        self.other = place.peer["c"]
        self.count = len(self.steps) + 2

    def _copy(self, chunk, have, device, slot):
        came = 0 if chunk == ALL else chunk
        block = self.ref.at[chunk, self.place.c, have["x"], have["z"], have["y"]]
        sent = self.sems.at[0, 0, SENT[slot]]
        return remote(block, block, sent, self.sems.at[1, came, slot], device)

    def _plane(self, chunk, core):
        plane = self.ref.at[chunk, core]
        came = 0 if chunk == ALL else chunk
        return remote(plane, plane, self.sems.at[0, 0, 0], self.sems.at[1, came, 0], self.other)

    def stage(self, index, chunk):
        if index == self.count - 1:
            self._plane(chunk, 1 - self.place.c).wait_recv()
            return
        came = [self.own]
        if index > 0:
            came = []
            for have, slot in self.steps[index - 1][1]:
                self._copy(chunk, have, self.other, slot).wait_recv()
                came.append(have)
        if index < len(self.steps):
            for have, device, slot in self.steps[index][0]:
                self._copy(chunk, have, device, slot).start()
        for have in came:
            self._copy(chunk, have, self.other, 0).start()

    def drain(self):
        for axis, (sends, _) in zip(self.axes, self.steps):
            have, _, slot = sends[0]
            if axis == "z":
                have = dict(have, z=slice(0, 3))
            self._copy(ALL, have, self.other, slot).wait_send()
        self._plane(ALL, self.place.c).wait_send()


RANKS = [(c, z, y) for z in range(4) for y in range(2) for c in range(2)]


def natural(ref, chunk, side):
    return jnp.concatenate([ref[chunk, c, side, z, y] for c, z, y in RANKS], axis=0)


def put_natural(ref, chunk, side, value):
    rows = value.shape[0] // len(RANKS)
    for spot, (c, z, y) in enumerate(RANKS):
        ref[chunk, c, side, z, y] = value[spot * rows : (spot + 1) * rows]


class Reduce(Tree):
    def __init__(self, place, full, total, lands, chunks, order, sems, finish):
        self.place, self.full, self.total, self.lands = place, full, total, lands
        self.chunks, self.sems, self.finish = chunks, sems, finish
        mine = {"x": place.m, "y": place.y}
        self.across = ALL if "x" in order else 0
        have = {"x": self.across, "z": ALL, "y": ALL}
        self.order, self.haves = order, []
        for axis in order:
            before = have
            if axis != "c":
                have = dict(have, **{axis: place.z if axis == "z" else mine[axis]})
            self.haves.append((before, have))
        self.count = len(order) + 1

    def _at(self, chunk, have):
        if self.total is None:
            return self.full.at[chunk, self.place.c, have["x"], have["z"], have["y"]]
        return self.total.at[chunk, have["x"], have["z"], have["y"]]

    def _copies(self, index, chunk):
        axis, (before, _) = self.order[index], self.haves[index]
        place, land = self.place, self.lands[axis]

        def copy(src, dst, slot, device):
            return remote(src, dst, self.sems.at[0, 0, SENT[slot]], self.sems.at[1, chunk, slot], device)

        if axis == "c":
            source = self.full.at[chunk, 1 - place.c, self.across]
            return [copy(source, land.at[chunk], SLOT[axis], place.peer[axis])]
        if axis == "z":
            return [
                copy(
                    self._at(chunk, dict(before, z=(place.z + step) % 4)),
                    land.at[chunk, step - 1],
                    step,
                    place.far[step - 1],
                )
                for step in (1, 2, 3)
            ]
        other = 1 - (place.m if axis == "x" else place.y)
        source = self._at(chunk, dict(before, **{axis: other}))
        return [copy(source, land.at[chunk], SLOT[axis], place.peer[axis])]

    def stage(self, index, chunk):
        if index > 0:
            axis, (_, have) = self.order[index - 1], self.haves[index - 1]
            land = self.lands[axis]
            for copy in self._copies(index - 1, chunk):
                copy.wait_recv()
            mine = self._at(chunk, have)
            last = index == self.count - 1
            if axis == "z":
                value = mine[...].astype(F32)
                for step in range(3):
                    value += land[chunk, step].astype(F32)
            elif last:
                value = mine[...].astype(F32) + land[chunk].astype(F32)
            else:
                value = mine[...] + land[chunk]
            if last:
                self.finish(chunk, value)
            else:
                mine[...] = value.astype(mine.dtype)
        if index < self.count - 1:
            for copy in self._copies(index, chunk):
                copy.start()

    def drain(self):
        for axis in self.order:
            land = self.lands[axis]
            slot = SLOT[axis]
            sent = self.sems.at[0, 0, SENT[slot]]
            remote(land, land, sent, self.sems.at[1, 0, slot], self.place.peer["c"]).wait_send()


class Everyone:
    def __init__(self, place, send_block, land_block, sems):
        self.rank = place.m * 16 + lax.axis_index("dp")
        self.send_block, self.land_block, self.sems = send_block, land_block, sems

    def _copy(self, step):
        to = (self.rank + step) % 32
        return remote(
            self.send_block(to),
            self.land_block(step),
            self.sems.at[0, step - 1],
            self.sems.at[1, step - 1],
            (to % 16, to // 16),
        )

    def _each(self, act):
        def one(step, carry):
            act(self._copy(step))
            return carry

        lax.fori_loop(1, 32, one, 0)

    def start(self):
        self._each(lambda copy: copy.start())

    def wait(self):
        self._each(lambda copy: copy.wait())


VROWS = 16


def rows_from_blocks(blocks, pick, counts):
    mp_count, dp_count = counts
    width = pick.shape[1]
    each = width // (mp_count * dp_count)
    wide = lax.dot_general(
        blocks, pick, NN, precision=lax.Precision.HIGHEST, preferred_element_type=F32
    )
    lane = lax.broadcasted_iota(jnp.int32, (VROWS, width), 1)
    table = jnp.zeros((VROWS, width), F32)
    for m in range(mp_count):
        for r, (c, z, y) in enumerate(RANKS):
            first = (r * mp_count + m) * each
            row = (((c * mp_count + m) * 4 + z) * 2 + y) * VROWS
            table += jnp.where((lane >= first) & (lane < first + each), wide[row : row + VROWS], 0.0)
    return table


def attend_setup(heads, m, box_full, vec_ref, box_heads, bias):
    cols = heads * HD
    for head in range(heads):
        box_heads[head] = box_full[:, head * HD : (head + 1) * HD]
    width = vec_ref.shape[1]
    own = jnp.where(m == 0, vec_ref[6:8, 0:cols], vec_ref[6:8, width - cols :])
    spread = exact_dot(jnp.broadcast_to(own[1:2], (8, cols)), pair_place(cols))
    bias[0:1, 0:cols] = own[0:1]
    bias[0:1, cols:] = spread[0:1]


def attend_trig(omega_ref, corner_ref, trig_ref):
    corner = corner_ref[...].astype(F32)
    angle_x = omega_ref[...] * ((corner[0:1] + corner[2:3]) * 0.5)
    angle_y = omega_ref[...] * ((corner[1:2] + corner[3:4]) * 0.5)
    trig_ref[0:FREQS, :] = jnp.cos(angle_x)
    trig_ref[FREQS : 2 * FREQS, :] = jnp.sin(angle_x)
    trig_ref[2 * FREQS : 3 * FREQS, :] = jnp.cos(angle_y)
    trig_ref[3 * FREQS :, :] = jnp.sin(angle_y)


def quiet(*args):
    return None


def attend_math(heads, r, weights, page_of, projected, attended):
    cols = heads * HD
    pages = r.x.shape[0] // PAGE

    def project(page, carry):
        rows = aligned(page, PAGE)
        tokens = r.x[rows, :]
        query = dot(tokens, weights(0)) + r.bias[0:1, 0:cols]
        query = query.astype(BF16) * HD ** (-0.5)
        r.qtok[rows, :] = query
        qa_rows = query.T
        for half in range(2):
            lanes = slice(half * cols, (half + 1) * cols)
            pair = dot(tokens, weights(1 + half)) + r.bias[0:1, cols + half * cols : 2 * cols + half * cols]
            pair = pair.astype(BF16)
            r.kvtok[rows, lanes] = pair
            turned = pair.T
            for spot in range(heads // 2):
                head_rows = slice((half * heads // 2 + spot) * HD, (half * heads // 2 + spot + 1) * HD)
                r.kt[head_rows, rows] = turned[2 * spot * HD : (2 * spot + 1) * HD]
                r.vt[head_rows, rows] = turned[(2 * spot + 1) * HD : (2 * spot + 2) * HD]
        trig = r.trig[:, rows]
        kft = trig.astype(BF16)
        r.kft[:, rows] = kft
        r.kftok[rows, :] = kft.T
        own, partner = turn_factors(trig)
        for head in range(heads):
            query_head = qa_rows[head * HD : (head + 1) * HD]
            proj = dot(r.box_heads[head], query_head)
            feat = proj * own + swap_blocks(proj) * partner
            r.qa[head, 0:PE, rows] = feat.astype(BF16)
            r.qa[head, PE : PE + HD, rows] = query_head
        projected(page)
        return carry

    lax.fori_loop(0, pages, project, 0)

    def attend(step, carry):
        turn, pair = step // (heads // 2), step % (heads // 2)
        rows = aligned(page_of(turn), PAGE)
        halves = []
        blank = jnp.zeros((HD, PAGE), BF16)
        for side in range(2):
            head = pair * 2 + side
            lanes = aligned(head, 2 * HD)
            left = jnp.concatenate([r.kftok[rows, :], r.kvtok[rows, lanes]], axis=1)
            score = dot(left, jnp.concatenate([r.qa[head, :, rows], blank], axis=0))
            top = jnp.max(score, axis=0, keepdims=True)
            weight = jnp.exp(score - top)
            total = jnp.sum(weight, axis=0, keepdims=True)
            value = r.vt[aligned(head, HD), rows]
            halves.append(dot(value, weight.astype(BF16)) * (1.0 / total))
            r.log[head, :, rows] = top + jnp.log(total)
        both = jnp.concatenate(halves, axis=0).astype(BF16)
        lanes = aligned(pair, 2 * HD)
        r.ctxt[lanes, rows] = both
        r.ctx[rows, lanes] = both.T
        attended(step, turn, pair)
        return carry

    lax.fori_loop(0, pages * (heads // 2), attend, 0)


def attend_buffers(heads, tokens):
    cols = heads * HD
    kept = [
        ("qa", (heads, PE + HD, tokens), BF16),
        ("qtok", (tokens, cols), BF16),
        ("kvtok", (tokens, 2 * cols), BF16),
        ("kt", (cols, tokens), BF16),
        ("kft", (PE, tokens), BF16),
        ("trig", (PE, tokens), F32),
        ("ctxt", (cols, tokens), BF16),
        ("log", (heads, 1, tokens), F32),
    ]
    used = [
        ("kftok", (tokens, PE), BF16),
        ("box_heads", (heads, PE, HD), BF16),
        ("bias", (8, 3 * cols), F32),
        ("ctx", (tokens, cols), BF16),
        ("vt", (cols, tokens), BF16),
    ]
    return kept, used


def attend_kernel(heads, names, *refs):
    r = types.SimpleNamespace(**dict(zip(names, refs)))
    attend_setup(heads, lax.axis_index("mp"), r.box, r.vec, r.box_heads, r.bias)
    attend_trig(r.omega, r.corner, r.trig)
    attend_math(heads, r, lambda chunk: r.w[chunk], lambda turn: turn, quiet, quiet)


def attend_forward(x, corners, omega, w_qkv, w_box, vecs):
    tokens = x.shape[0]
    heads = w_box.shape[1] // HD
    kept, used = attend_buffers(heads, tokens)
    outs = kept + [used[3]]
    scratch = used[:3] + used[4:]
    names = ["x", "corner", "omega", "w", "box", "vec"] + [item[0] for item in outs + scratch]
    vmem = pl.BlockSpec(memory_space=pltpu.VMEM)
    return pl.pallas_call(
        functools.partial(attend_kernel, heads, names),
        out_shape=[jax.ShapeDtypeStruct(shape, kind) for _, shape, kind in outs],
        in_specs=[vmem] * 6,
        out_specs=[vmem] * len(outs),
        scratch_shapes=[pltpu.VMEM(shape, kind) for _, shape, kind in scratch],
        compiler_params=pltpu.CompilerParams(vmem_limit_bytes=VMEM_LIMIT),
        name="attend_forward",
    )(x, corners, omega, w_qkv, w_box, vecs)


TILE = 256


def normal_parts(value):
    bell = jnp.exp(value * value * -0.5)
    t = 1.0 / (1.0 + (0.3275911 * 2.0 ** (-0.5)) * jnp.abs(value))
    tail = 0.5 * 1.061405429
    for factor in (-1.453152027, 1.421413741, -0.284496736, 0.254829592):
        tail = tail * t + 0.5 * factor
    tail = tail * t * bell
    phi = jnp.where(value < 0.0, tail, 1.0 - tail)
    return phi, phi + value * (bell * (0.5 / np.pi) ** 0.5)


def norm_stats(value):
    mean = jnp.mean(value, axis=-1, keepdims=True)
    centred = value - mean
    var = jnp.mean(centred * centred, axis=-1, keepdims=True)
    return centred, lax.rsqrt(var + NORM_EPS)


def norm_back(grad_normed, normed, scale):
    first = jnp.mean(grad_normed, axis=-1, keepdims=True)
    second = jnp.mean(grad_normed * normed, axis=-1, keepdims=True)
    return scale * (grad_normed - first - normed * second)


def col_sum(value):
    return jnp.sum(value, axis=0, keepdims=True)


def feed_math(r, hooks):
    hook = {name: quiet for name in ("entered", "grew", "turned", "shrinks", "shrank", "left")}
    hook.update(hooks)
    tokens = r.x.shape[0]
    sides = r.ctxx.shape[0]
    steps = r.ws.shape[0]
    tiles = tokens // TILE
    wide = sides * UNIT
    sum2 = dnorm = r.sum2

    def flat(ref, chunk, side):
        return ref[chunk, side] if len(ref.shape) == 4 else natural(ref, chunk, side)

    def put(ref, chunk, side, value):
        if len(ref.shape) == 4:
            ref[chunk, side] = value
        else:
            put_natural(ref, chunk, side, value)

    def both(ref, chunk):
        return jnp.concatenate([flat(ref, chunk, side) for side in range(sides)], axis=1)

    def put_both(ref, chunk, value):
        for side in range(sides):
            put(ref, chunk, side, value[:, side * UNIT : (side + 1) * UNIT])

    def bias_at(step, side):
        first = side * steps + step
        return (pl.ds(8 + first // 2, 1), aligned(first % 2, UNIT))

    def enter(tile, carry):
        rows = aligned(tile, TILE)
        total = r.x[rows, :].astype(F32) + r.vec[4:5, :]
        for side in range(sides):
            total += dot(r.ctxx[side, rows, :], flat(r.we, 0, side), NT)
        centred, scale = norm_stats(total)
        normed = centred * scale
        r.norm1[rows, :] = normed
        r.scale1[rows, :] = scale
        shifted = normed * r.vec[0:1, :] + r.vec[1:2, :]
        r.al[rows, :] = shifted.astype(BF16)
        sum2[rows, :] = shifted + r.vec[5:6, :]
        return carry

    lax.fori_loop(0, tiles, enter, 0)
    hook["entered"]()

    def grow(step, carry):
        whole = aligned(step, wide)
        bias = jnp.concatenate([r.vec[bias_at(step, side)] for side in range(sides)], axis=1)

        def one(tile, inner):
            rows = aligned(tile, TILE)
            pre = dot(r.al[rows, :], both(r.we, 1 + step)) + bias
            phi, slope = normal_parts(pre)
            low = (pre * phi).astype(BF16)
            r.act[rows, whole] = low
            r.slope[rows, whole] = slope.astype(BF16)
            sum2[rows, :] += dot(low, both(r.ws, step), NT)
            hook["grew"](step * tiles + tile)
            return inner

        lax.fori_loop(0, tiles, one, 0)
        return carry

    lax.fori_loop(0, steps, grow, 0)
    r.vsum[...] = jnp.zeros_like(r.vsum)

    def turn(tile, carry):
        rows = aligned(tile, TILE)
        centred, scale = norm_stats(sum2[rows, :])
        normed = centred * scale
        r.out[rows, :] = (normed * r.vec[2:3, :] + r.vec[3:4, :]).astype(BF16)
        grad = r.og[rows, :].astype(F32)
        r.vsum[2:3, :] += col_sum(grad * normed)
        r.vsum[3:4, :] += col_sum(grad)
        back = norm_back(grad * r.vec[2:3, :], normed, scale)
        r.vsum[5:6, :] += col_sum(back)
        r.dh2l[rows, :] = back.astype(BF16)
        dnorm[rows, :] = back
        hook["turned"](tile)
        return carry

    lax.fori_loop(0, tiles, turn, 0)
    r.flip[...] = r.dh2l[...].T

    def grad_shrink(step, carry):
        grad = dot(r.flip[...], r.act[:, aligned(step, wide)]).astype(BF16)
        put_both(r.gs, step, grad)
        hook["shrinks"](step)
        return carry

    lax.fori_loop(0, steps, grad_shrink, 0)

    def shrink(step, carry):
        whole = aligned(step, wide)

        def one(tile, inner):
            rows = aligned(tile, TILE)
            grad = dot(r.dh2l[rows, :], both(r.ws, step))
            low = (grad * r.slope[rows, whole].astype(F32)).astype(BF16)
            r.slope[rows, whole] = low
            sums = col_sum(low.astype(F32))
            for side in range(sides):
                r.vsum[bias_at(step, side)] += sums[:, side * UNIT : (side + 1) * UNIT]
            dnorm[rows, :] += dot(low, both(r.we, 1 + step), NT)
            hook["shrank"](step * tiles + tile)
            return inner

        lax.fori_loop(0, tiles, one, 0)
        return carry

    lax.fori_loop(0, steps, shrink, 0)

    def leave(tile, carry):
        rows = aligned(tile, TILE)
        grad = dnorm[rows, :]
        normed = r.norm1[rows, :]
        r.vsum[0:1, :] += col_sum(grad * normed)
        r.vsum[1:2, :] += col_sum(grad)
        back = norm_back(grad * r.vec[0:1, :], normed, r.scale1[rows, :])
        r.vsum[4:5, :] += col_sum(back)
        low = back.astype(BF16)
        r.dh1l[rows, :] = low
        for side in range(sides):
            r.dctx[side, rows, :] = dot(low, flat(r.we, 0, side)).astype(BF16)
        hook["left"](tile)
        return carry

    lax.fori_loop(0, tiles, leave, 0)
    r.flip[...] = r.al[...].T

    def grad_expand(step, carry):
        grad = dot(r.flip[...], r.slope[:, aligned(step, wide)]).astype(BF16)
        put_both(r.ge, 1 + step, grad)
        return carry

    lax.fori_loop(0, steps, grad_expand, 0)
    r.flip[...] = r.dh1l[...].T
    for side in range(sides):
        put(r.ge, 0, side, dot(r.flip[...], r.ctxx[side]).astype(BF16))


def feed_buffers(tokens, width, hidden):
    return [
        ("norm1", (tokens, width), F32),
        ("scale1", (tokens, 1), F32),
        ("sum2", (tokens, width), F32),
        ("al", (tokens, width), BF16),
        ("act", (tokens, hidden), BF16),
        ("slope", (tokens, hidden), BF16),
        ("dh2l", (tokens, width), BF16),
        ("flip", (width, tokens), BF16),
    ]


def feed_kernel(names, *refs):
    feed_math(types.SimpleNamespace(**dict(zip(names, refs))), {})


def feed_both(x, og, ctx, w_expand, w_shrink, vecs):
    tokens, width = x.shape
    chunks, sides = w_shrink.shape[0:2]
    outs = [
        ("out", (tokens, width), BF16),
        ("dctx", (sides, tokens, UNIT), BF16),
        ("dh1l", (tokens, width), BF16),
        ("ge", (chunks + 1, sides, width, UNIT), BF16),
        ("gs", (chunks, sides, width, UNIT), BF16),
        ("vsum", (VROWS, width), F32),
    ]
    scratch = feed_buffers(tokens, width, sides * chunks * UNIT)
    names = ["x", "og", "ctxx", "we", "ws", "vec"] + [item[0] for item in outs + scratch]
    vmem = pl.BlockSpec(memory_space=pltpu.VMEM)
    return pl.pallas_call(
        functools.partial(feed_kernel, names),
        out_shape=[jax.ShapeDtypeStruct(shape, kind) for _, shape, kind in outs],
        in_specs=[vmem] * 6,
        out_specs=[vmem] * len(outs),
        scratch_shapes=[pltpu.VMEM(shape, kind) for _, shape, kind in scratch],
        compiler_params=pltpu.CompilerParams(vmem_limit_bytes=VMEM_LIMIT),
        name="feed_both",
    )(x, og, ctx, w_expand, w_shrink, vecs)


def layer_kernel(heads, plan, inv_tokens, names, kept, used, feeds, *refs):
    r = types.SimpleNamespace(**dict(zip(names, refs)))
    cols = heads * HD
    tokens = r.x_all.shape[0]
    pages = tokens // PAGE
    own_tokens = tokens // 2
    tiles = own_tokens // TILE
    place = Place()
    place.signal()
    m, peer = place.m, place.peer["x"]
    at = (place.z, place.y)
    own = aligned(m, own_tokens)
    load_x = pltpu.make_async_copy(r.x_all.at[own, :], r.x, r.load_sem.at[0])
    load_og = pltpu.make_async_copy(r.og_all.at[own, :], r.og, r.load_sem.at[1])
    load_x.start()
    load_og.start()
    r.w[(0, place.c, 0, *at)] = r.attn[0].astype(BF16)
    for half in range(2):
        r.w[(1 + half, place.c, 0, *at)] = jnp.concatenate(
            [
                r.attn[1 + kind, :, head * HD : (head + 1) * HD].astype(BF16)
                for head in range(half * heads // 2, (half + 1) * heads // 2)
                for kind in range(2)
            ],
            axis=1,
        )
    r.box_gather[(0, place.c, 0, *at)] = r.shard_box[...]
    r.vec_gather[(0, place.c, m, *at)] = jnp.zeros((VROWS, 128), F32)
    table_at = (slice(0, r.vectors.shape[0]), slice(0, r.vectors.shape[1]))
    r.vec_gather[(0, place.c, m, *at, *table_at)] = r.vectors[...]
    r.we[(0, place.c, m, *at)] = r.merge[...].astype(BF16)
    for chunk in range(4):
        lanes = slice(chunk * UNIT, (chunk + 1) * UNIT)
        r.we[(1 + chunk, place.c, m, *at)] = r.expand[:, lanes].astype(BF16)
        r.ws[(chunk, place.c, m, *at)] = r.shrink[:, lanes].astype(BF16)
    place.wait()
    tree_v = Spread(place, r.vec_gather, 1, "xzy", r.v_sem)
    tree_b = Spread(place, r.box_gather, 1, "zy", r.b_sem)
    tree_a = Spread(place, r.w.at[0:2], 2, "zy", r.a_sem)
    tree_k = Spread(place, r.w.at[2:3], 1, "yz", r.k_sem)
    tree_a.together = True
    tree_e = Spread(place, r.we, 5, "zyx", r.e_sem)
    tree_f = Spread(place, r.ws, 4, "xzy", r.f_sem)
    tree_e.lag = tree_f.lag = 2
    first, late = 4, 2
    begun = first - late

    def weights_event(number):
        tree_e.event(number)
        tree_f.event(number)

    def finish(chunk, value):
        r.sum_f[chunk] = value * inv_tokens

    back_f = Reduce(
        place, r.gs, None, dict(c=r.fc, y=r.fy, z=r.fz, x=r.fx), 4, "cyzx", r.back_sem, finish
    )
    back_f.lag, back_f.held_back = 2, 1

    def attention(*scoped):
        q = types.SimpleNamespace(**dict(zip([item[0] for item in kept + used] + ["x"], scoped)))
        load_all = pltpu.make_async_copy(r.x_all, q.x, r.load_sem.at[2])
        load_all.start()

        tree_v.stage(0, 0)

        def begin(number, carry):
            tree_v.event(number + 1)
            tree_b.event(number)

            @pl.when(number == first - 1)
            def _():
                r.vec[...] = rows_from_blocks(
                    r.vec_gather[...].reshape(-1, 128), r.pick[...], plan
                )
                r.box_out[...] = natural(r.box_gather, 0, 0).astype(BF16)
                attend_setup(heads, m, r.box_out, r.vec, q.box_heads, q.bias)

            tree_a.event(number)
            tree_k.event(number)
            weights_event(number - late)
            pl.when(number == 0)(lambda: attend_trig(r.omega, r.corner, q.trig))
            return carry

        lax.fori_loop(0, first, begin, 0)
        keep_w = pltpu.make_async_copy(r.w, r.w_out, r.load_sem.at[3])
        keep_w.start()
        load_all.wait()

        def projected(page):
            weights_event(begun + page)

        piece = PAGE // 2

        def swap_copy(index):
            theirs = pages * (1 - m) + index
            return remote(
                q.ctx.at[aligned(theirs, piece), :],
                r.ctxx.at[m, aligned(index, piece), :],
                r.ctx_sem.at[0, index],
                r.ctx_sem.at[1, index],
                peer,
            )

        def attended(step, turn, pair):
            pl.when(step % 2 == 0)(lambda: weights_event(begun + pages + step // 2))

            @pl.when(step == heads // 2 - 1)
            def _():
                swap_copy(2 - 2 * m).start()
                swap_copy(1).start()

            @pl.when(step == heads - 1)
            def _():
                swap_copy(2 * m).start()

        attend_math(
            heads,
            q,
            lambda chunk: natural(r.w, chunk, 0),
            lambda turn: turn * m + (pages - 1 - turn) * (1 - m),
            projected,
            attended,
        )
        stores = [
            pltpu.make_async_copy(getattr(q, name), getattr(r, name + "_out"), r.store_sem.at[k])
            for k, (name, _, _) in enumerate(kept)
        ]
        for copy in stores:
            copy.start()
        r.ctxx[m] = q.ctx[own, :]
        for index in range(pages):
            copy = remote(
                q.ctx.at[aligned(index, piece), :],
                r.ctxx.at[1 - m, aligned(index, piece), :],
                r.ctx_sem.at[0, index],
                r.ctx_sem.at[1, index],
                peer,
            )
            copy.wait_recv()
            copy.wait_send()
        for copy in stores:
            copy.wait()
        keep_w.wait()

    pl.run_scoped(
        attention,
        *[pltpu.VMEM(shape, kind) for _, shape, kind in kept + used],
        pltpu.VMEM(r.x_all.shape, BF16),
    )

    def feed(*scoped):
        q = types.SimpleNamespace(**dict(zip([item[0] for item in feeds], scoped)))
        for name in ("x", "og", "we", "ws", "vec", "ctxx", "dh1l", "ge", "gs", "vsum"):
            setattr(q, name, getattr(r, name))

        def out_copy(tile):
            rows = aligned(tile, TILE)
            return pltpu.make_async_copy(q.out.at[rows, :], r.out_own.at[rows, :], r.swap_sem.at[0, tile])

        def dctx_copies(tile):
            rows = aligned(tile, TILE)
            there = r.dctx_full.at[pl.ds(pl.multiple_of(m * own_tokens + tile * TILE, TILE), TILE), :]
            return (
                pltpu.make_async_copy(q.dctx.at[m, rows, :], there, r.swap_sem.at[3, tile]),
                remote(
                    q.dctx.at[1 - m, rows, :], there, r.swap_sem.at[4, tile], r.swap_sem.at[5, tile], peer
                ),
            )

        def start(copies):
            for copy in copies:
                copy.start()

        def grew(number):
            pl.when(number % 3 == 1)(lambda: weights_event(begun + pages + 5 + number // 3))

        def shrank(number):
            pl.when(number % 2 == 1)(lambda: back_f.event(4 + number // 2))

        load_x.wait()
        load_og.wait()
        feed_math(
            q,
            dict(
                grew=grew,
                turned=lambda tile: out_copy(tile).start(),
                shrinks=lambda step: back_f.event(step),
                shrank=shrank,
                left=lambda tile: start(dctx_copies(tile)),
            ),
        )
        back_f.rest()
        back_f.drain()
        for tile in range(tiles):
            for copy in (out_copy(tile), *dctx_copies(tile)):
                copy.wait()

    pl.run_scoped(feed, *[pltpu.VMEM(shape, kind) for _, shape, kind in feeds])
    for tree in (tree_v, tree_b, tree_a, tree_k, tree_e, tree_f):
        tree.drain()


def layer_forward(x, og, corners, omega, pick, shards, plan, inv_tokens):
    tokens, width = x.shape
    cols = shards[1].shape[1]
    heads = cols // HD
    own = tokens // 2
    unit = (width // 16, UNIT)
    kept, used = attend_buffers(heads, tokens)
    feeds = feed_buffers(own, width, 8 * UNIT)
    feeds += [("out", (own, width), BF16), ("dctx", (2, own, UNIT), BF16)]
    free = pl.BlockSpec(memory_space=pl.ANY)
    vmem = pl.BlockSpec(memory_space=pltpu.VMEM)
    inputs = [("x_all", free), ("og_all", free), ("corner", vmem), ("omega", vmem), ("pick", vmem)]
    inputs += [(name, vmem) for name in ("attn", "shard_box", "vectors", "merge", "expand", "shrink")]
    outs = [(name + "_out", shape, kind, free) for name, shape, kind in kept]
    outs += [
        ("w_out", (3, 2, 1, 4, 2, *unit), BF16, free),
        ("box_out", (PE, cols), BF16, vmem),
        ("out_own", (own, width), BF16, free),
        ("dctx_full", (tokens, cols), BF16, free),
        ("dh1l", (own, width), BF16, vmem),
        ("ge", (5, 2, 2, 4, 2, *unit), BF16, vmem),
        ("vsum", (VROWS, width), F32, vmem),
        ("sum_f", (4, *unit), F32, vmem),
    ]
    dma = pltpu.SemaphoreType.DMA
    scratch = [
        ("x", pltpu.VMEM((own, width), BF16)),
        ("og", pltpu.VMEM((own, width), BF16)),
        ("vec", pltpu.VMEM((VROWS, width), F32)),
        ("w", pltpu.VMEM((3, 2, 1, 4, 2, *unit), BF16)),
        ("box_gather", pltpu.VMEM((1, 2, 1, 4, 2, PE // 16, cols), F32)),
        ("vec_gather", pltpu.VMEM((1, 2, 2, 4, 2, VROWS, 128), F32)),
        ("we", pltpu.VMEM((5, 2, 2, 4, 2, *unit), BF16)),
        ("ws", pltpu.VMEM((4, 2, 2, 4, 2, *unit), BF16)),
        ("ctxx", pltpu.VMEM((2, own, cols), BF16)),
        ("gs", pltpu.VMEM((4, 2, 2, 4, 2, *unit), BF16)),
        ("fc", pltpu.VMEM((4, 2, 4, 2, *unit), BF16)),
        ("fy", pltpu.VMEM((4, 2, 4, *unit), BF16)),
        ("fz", pltpu.VMEM((4, 3, 2, *unit), BF16)),
        ("fx", pltpu.VMEM((4, *unit), BF16)),
        ("ctx_sem", dma((2, 3))),
        ("a_sem", dma((2, 2, SLOTS))),
        ("k_sem", dma((2, 1, SLOTS))),
        ("b_sem", dma((2, 1, SLOTS))),
        ("v_sem", dma((2, 1, SLOTS))),
        ("e_sem", dma((2, 5, SLOTS))),
        ("f_sem", dma((2, 4, SLOTS))),
        ("back_sem", dma((2, 4, SLOTS))),
        ("load_sem", dma((4,))),
        ("store_sem", dma((len(kept),))),
        ("swap_sem", dma((6, own // TILE))),
    ]
    names = [item[0] for item in inputs + outs + scratch]
    return pl.pallas_call(
        functools.partial(layer_kernel, heads, plan, inv_tokens, names, kept, used, feeds),
        out_shape=[jax.ShapeDtypeStruct(shape, kind) for _, shape, kind, _ in outs],
        in_specs=[item[1] for item in inputs],
        out_specs=[item[3] for item in outs],
        scratch_shapes=[item[1] for item in scratch],
        compiler_params=pltpu.CompilerParams(
            vmem_limit_bytes=VMEM_LIMIT, collective_id=0, has_side_effects=True
        ),
        name="layer_forward",
    )(x, og, corners, omega, pick, *shards)


def pair_place(cols):
    spot = lax.broadcasted_iota(jnp.int32, (cols, 2 * cols), 0)
    lane = lax.broadcasted_iota(jnp.int32, (cols, 2 * cols), 1)
    target = ((spot >> 6) << 7) + HD + (spot & (HD - 1))
    return jnp.where(lane == target, 1.0, 0.0)


def exact_dot(lhs, rhs, dims=NN):
    return lax.dot_general(
        lhs, rhs, dims, precision=lax.Precision.HIGHEST, preferred_element_type=F32
    )


def attend_back_kernel(heads, plan, inv_tokens, *refs):
    inputs, refs = refs[:12], refs[12:]
    if plan is not None:
        load_sem, held, refs = refs[-1], refs[-13:-1], refs[:-13]
        loads = [
            pltpu.make_async_copy(src, dst, load_sem.at[k]) for k, (src, dst) in enumerate(zip(inputs, held))
        ]
        early = (0, 2, 7, 11)
        for k in sorted(range(12), key=lambda k: k not in early):
            loads[k].start()
        inputs = held
    x_ref, w_ref, box_ref, *inputs = inputs
    qa_ref, qtok_ref, kvtok_ref, kt_ref, kft_ref, trig_ref, ctxt_ref, log_ref, dctx_ref = inputs
    cols = heads * HD
    tokens = x_ref.shape[0]
    pages = tokens // PAGE
    m = lax.axis_index("mp")
    piece = PAGE // 2
    pieces = 2 * pages
    lane = lax.broadcasted_iota(jnp.int32, (1, 2 * HD), 1)
    lower = lane < HD
    if plan is None:
        inp_ref, gw_ref, gbox_ref, qvsum_ref, *refs = refs
        kftok, dctxt, boxt, dtok, xt, gbox = refs
        before, after = 0, 0

        def background(number):
            pass
    else:
        dh1_ref, vsum_ref, sumf_ref, pick_ref, full_e, *refs = refs
        inp_ref, sum_e, sum_a, sum_b, sum_v, norm_ref, *refs = refs
        kftok, dctxt, boxt, dtok, xt, gbox, *refs = refs
        came, total_e, full_a, full_b, full_v, land_v, norms, *refs = refs
        ec, ey, ez, ex, ac, ay, az, bc, by, bz, *refs = refs
        e_sem, a_sem, b_sem, v_sem, n_sem, i_sem, loc_sem = refs
        place = Place()
        place.signal_all()
        fill = pltpu.make_async_copy(full_e.at[:, place.c], total_e, loc_sem.at[0])
        fill.start()
        place.wait_all()

        def finish(out):
            def put(chunk, value):
                out[chunk] = value * inv_tokens

            return put

        tree_e = Reduce(
            place, full_e, total_e, dict(c=ec, y=ey, z=ez, x=ex), 5, "cyzx", e_sem, finish(sum_e)
        )
        tree_e.lag, tree_e.held_back = 2, 1
        tree_a = Reduce(place, full_a, None, dict(c=ac, y=ay, z=az), 3, "cyz", a_sem, finish(sum_a))
        tree_b = Reduce(place, full_b, None, dict(c=bc, y=by, z=bz), 1, "cyz", b_sem, finish(sum_b))

        def block_of(rank):
            r = rank % 16
            return full_v.at[rank // 16, r // 4, (r // 2) % 2, r % 2]

        spot = (place.m, place.z, place.y, place.c)
        all_v = Everyone(place, block_of, lambda step: land_v.at[step - 1], v_sem)
        all_n = Everyone(place, lambda rank: norms.at[spot], lambda step: norms.at[spot], n_sem)

        def background(number):
            tree_e.event(number)

        background(0)
        fill.wait()
        for k in early:
            loads[k].wait()

    boxt[...] = box_ref[...].T
    gbox[...] = jnp.zeros_like(gbox)

    def prepare(page, carry):
        rows = aligned(page, PAGE)
        kftok[rows, :] = kft_ref[:, rows].T
        dctxt[:, rows] = dctx_ref[rows, :].T
        xt[:, rows] = x_ref[rows, :].T
        if plan is not None:
            pl.when(page > 0)(lambda: background(page))
        return carry

    lax.fori_loop(0, pages, prepare, 0)
    if plan is not None:
        for k in range(12):
            if k not in early:
                loads[k].wait()

    def attend(step, carry):
        page, pair = step // (heads // 2), step % (heads // 2)
        rows = aligned(page, PAGE)
        own, partner = turn_factors(trig_ref[:, rows])
        pair_lanes = aligned(pair, 2 * HD)
        query_pair = qtok_ref[rows, pair_lanes]
        dctx_pair = dctx_ref[rows, pair_lanes]
        halves = []
        boxes = []
        blank = jnp.zeros((HD, PAGE), BF16)
        for side in range(2):
            head = pair * 2 + side
            lanes = aligned(head, 2 * HD)
            key_value = kvtok_ref[rows, lanes]
            left = jnp.concatenate([kftok[rows, :], key_value], axis=1)
            score = dot(left, jnp.concatenate([qa_ref[head, :, rows], blank], axis=0))
            prob = jnp.exp(score - log_ref[head, :, rows])
            prob_low = prob.astype(BF16)
            head_rows = pl.ds(pl.multiple_of(head * HD, HD), HD)
            dctx_head = dctxt[head_rows, rows]
            grad_prob = dot(
                key_value, jnp.concatenate([blank, dctx_head], axis=0)
            )
            inner = col_sum(dctx_head.astype(F32) * ctxt_ref[head_rows, rows].astype(F32))
            grad_score = (prob * (grad_prob - inner)).astype(BF16)
            if side == 0:
                both = jnp.concatenate([query_pair[:, 0:HD], dctx_pair[:, 0:HD]], axis=1)
            else:
                both = jnp.concatenate([query_pair[:, HD:], dctx_pair[:, HD:]], axis=1)
            from_score = dot(grad_score, both)
            from_prob = dot(prob_low, both)
            grad_kv = jnp.where(lower, from_score, from_prob).astype(BF16)
            dtok[rows, pl.ds(pl.multiple_of(cols + head * 2 * HD, 2 * HD), 2 * HD)] = grad_kv
            keys = jnp.concatenate([kft_ref[:, rows], kt_ref[head_rows, rows]], axis=0)
            grad_query = dot(keys, grad_score) * HD ** (-0.5)
            feat = grad_query[0:PE]
            proj = (feat * own - swap_blocks(feat) * partner).astype(BF16)
            halves.append(grad_query[PE:] + dot(boxt[head_rows, :], proj))
            boxes.append(dot(proj, query_pair))
        gbox[:, pair_lanes] += jnp.where(lower, boxes[0], boxes[1])
        dtok[rows, pair_lanes] = jnp.concatenate(halves, axis=0).astype(BF16).T
        return carry

    def weights(chunk):
        return w_ref[chunk] if plan is None else natural(w_ref, chunk, 0)

    def spread(page):
        rows = aligned(page, PAGE)
        return sum(
            dot(dtok[rows, chunk * UNIT : (chunk + 1) * UNIT], weights(chunk), NT) for chunk in range(3)
        )

    if plan is None:
        lax.fori_loop(0, pages * (heads // 2), attend, 0)
        gbox_ref[...] = gbox[...] * HD**0.5

        def spread_page(page, carry):
            inp_ref[aligned(page, PAGE), :] = spread(page)
            return carry

        lax.fori_loop(0, pages, spread_page, 0)

        def gather(step, carry):
            lanes = aligned(step, UNIT)
            gw_ref[step] = dot(xt[...], dtok[:, lanes]).astype(BF16)
            qvsum_ref[0:1, lanes] = col_sum(dtok[:, lanes].astype(F32))
            return carry

        lax.fori_loop(0, 3, gather, 0)
        return

    def swap(index):
        rows = aligned(index, piece)
        return remote(
            inp_ref.at[rows, :], came.at[rows, :], i_sem.at[0, index], i_sem.at[1, index], place.peer["x"]
        )

    def attend_and_send(step, carry):
        attend(step, carry)
        page = step // (heads // 2)

        @pl.when(step % (heads // 2) == heads // 2 - 1)
        def _():
            value = spread(page)
            for half in range(2):
                index = 2 * page + half
                rows = aligned(index, piece)
                own = index // pages == m
                spot = aligned(index % pages, piece)
                extra = jnp.where(own, dh1_ref[spot, :].astype(F32), 0.0)
                inp_ref[rows, :] = (value[half * piece : (half + 1) * piece] + extra).astype(BF16)
                swap(index).start()

        background(step + pages)
        return carry

    lax.fori_loop(0, pages * (heads // 2), attend_and_send, 0)
    put_natural(full_b, 0, 0, gbox[...] * HD**0.5)

    def gather(step, carry):
        grad = dot(xt[...], dtok[:, aligned(step, UNIT)]).astype(BF16)
        put_natural(full_a, step, 0, grad)
        tree_a.event(step)
        tree_b.event(step)
        return carry

    lax.fori_loop(0, 3, gather, 0)

    sums = jnp.concatenate(
        [
            col_sum(dtok[:, chunk * UNIT : (chunk + 1) * UNIT].astype(F32)) for chunk in range(3)
        ],
        axis=1,
    )
    values = exact_dot(jnp.broadcast_to(sums[:, cols:], (8, 2 * cols)), pair_place(cols), NT)
    pair = jnp.concatenate([sums[:, 0:cols], values[0:1]], axis=0)
    blank = jnp.zeros_like(pair)
    pair = jnp.where(
        m == 0, jnp.concatenate([pair, blank], axis=1), jnp.concatenate([blank, pair], axis=1)
    )
    table = jnp.concatenate([vsum_ref[0:6, :], pair, vsum_ref[8:, :]], axis=0)
    mp_count, dp_count = plan
    width = table.shape[1]
    each = width // (mp_count * dp_count)
    wide_lane = lax.broadcasted_iota(jnp.int32, (VROWS, width), 1)
    for side in range(mp_count):
        parts = []
        for r in range(dp_count):
            first = (r * mp_count + side) * each
            parts.append(jnp.where((wide_lane >= first) & (wide_lane < first + each), table, 0.0))
        block = exact_dot(jnp.concatenate(parts, axis=0), pick_ref[...], NT)
        full_v[side] = block.reshape(full_v.shape[1:])
    all_v.start()

    def tail(number, carry):
        tree_a.event(number)
        tree_b.event(number)
        return carry

    lax.fori_loop(3, tree_a.events, tail, 0)
    tree_e.rest()
    all_v.wait()
    total_v = full_v[spot] + jnp.sum(land_v[...], axis=0)
    sum_v[0] = total_v * inv_tokens

    square = sum(jnp.sum(out[...] * out[...]) for out in (sum_e, sumf_ref, sum_a, sum_b, sum_v))
    norms[spot] = jnp.full((8, 128), square, F32)
    all_n.start()

    def final(number, carry):
        rows = aligned(number, piece)
        swap(number).wait()
        inp_ref[rows, :] = (inp_ref[rows, :].astype(F32) + came[rows, :].astype(F32)).astype(BF16)
        return carry

    lax.fori_loop(0, pieces, final, 0)
    all_n.wait()
    every = norms[...].reshape(-1, 8, 128)
    norm_ref[...] = jnp.sqrt(sum(every[k] for k in range(every.shape[0])))
    for tree in (tree_e, tree_a, tree_b):
        tree.drain()


def attend_backward(x, weight, box, kept, dctx, plan, inv_tokens, more=()):
    tokens, width = x.shape
    cols = weight.shape[-1]
    heads = cols // HD
    vmem = pl.BlockSpec(memory_space=pltpu.VMEM)
    scratch = [
        pltpu.VMEM((tokens, PE), BF16),
        pltpu.VMEM((cols, tokens), BF16),
        pltpu.VMEM((cols, PE), BF16),
        pltpu.VMEM((tokens, 3 * cols), BF16),
        pltpu.VMEM((width, tokens), BF16),
        pltpu.VMEM((PE, cols), F32),
    ]
    in_specs = [vmem] * 12
    if plan is None:
        shapes = [
            ((tokens, width), F32),
            ((3, width, cols), BF16),
            ((PE, cols), F32),
            ((8, 3 * cols), F32),
        ]
        extra = {}
    else:
        free = pl.BlockSpec(memory_space=pl.ANY)
        in_specs = [free] * 12 + [vmem] * 4 + [free]
        rows = width // 16
        unit = (rows, UNIT)
        tile = (PE // 16, cols)
        small = (VROWS, 128)
        shapes = [
            ((tokens, width), BF16),
            ((5, *unit), F32),
            ((3, *unit), F32),
            ((1, *tile), F32),
            ((1, *small), F32),
            ((8, 128), F32),
        ]
        scratch += [
            pltpu.VMEM((tokens, width), BF16),
            pltpu.VMEM((5, 2, 4, 2, *unit), BF16),
            pltpu.VMEM((3, 2, 1, 4, 2, *unit), BF16),
            pltpu.VMEM((1, 2, 1, 4, 2, *tile), F32),
            pltpu.VMEM((2, 4, 2, 2, *small), F32),
            pltpu.VMEM((31, *small), F32),
            pltpu.VMEM((2, 4, 2, 2, 8, 128), F32),
            pltpu.VMEM((5, 2, 4, 2, *unit), BF16),
            pltpu.VMEM((5, 2, 4, *unit), BF16),
            pltpu.VMEM((5, 3, 2, *unit), BF16),
            pltpu.VMEM((5, *unit), BF16),
            pltpu.VMEM((3, 4, 2, *unit), BF16),
            pltpu.VMEM((3, 4, *unit), BF16),
            pltpu.VMEM((3, 3, *unit), BF16),
            pltpu.VMEM((1, 4, 2, *tile), F32),
            pltpu.VMEM((1, 4, *tile), F32),
            pltpu.VMEM((1, 3, *tile), F32),
            pltpu.SemaphoreType.DMA((2, 5, SLOTS)),
            pltpu.SemaphoreType.DMA((2, 3, SLOTS)),
            pltpu.SemaphoreType.DMA((2, 1, SLOTS)),
            pltpu.SemaphoreType.DMA((2, 31)),
            pltpu.SemaphoreType.DMA((2, 31)),
            pltpu.SemaphoreType.DMA((2, 2 * (tokens // PAGE))),
            pltpu.SemaphoreType.DMA((2,)),
        ]
        scratch += [pltpu.VMEM(array.shape, array.dtype) for array in (x, weight, box, *kept, dctx)]
        scratch.append(pltpu.SemaphoreType.DMA((12,)))
        extra = dict(collective_id=2, has_side_effects=True)
    return pl.pallas_call(
        functools.partial(attend_back_kernel, heads, plan, inv_tokens),
        out_shape=[jax.ShapeDtypeStruct(s, d) for s, d in shapes],
        in_specs=in_specs,
        out_specs=[vmem] * len(shapes),
        scratch_shapes=scratch,
        compiler_params=pltpu.CompilerParams(vmem_limit_bytes=VMEM_LIMIT, **extra),
        cost_estimate=pl.CostEstimate(flops=4 * 10**10, bytes_accessed=10**8, transcendentals=10**7),
        name="attend_backward",
    )(x, weight, box, *kept, dctx, *more)


def adam_step(master, first, second, gradient, rate, decay):
    new_first = BETA_ONE * first + (1.0 - BETA_ONE) * gradient
    new_second = BETA_TWO * second + (1.0 - BETA_TWO) * gradient * gradient
    first_hat = new_first / (1.0 - BETA_ONE**STEP)
    second_hat = new_second / (1.0 - BETA_TWO**STEP)
    new_master = master - rate * (first_hat / (jnp.sqrt(second_hat) + ADAM_EPS) + decay * master)
    return (new_first, new_second, new_master)


def adam_kernel(heads, norm_ref, *refs):
    sum_e, sum_f, sum_a, sum_b, sum_v, *refs = refs
    states, outs = refs[:18], refs[18:]
    outs[-1][...] = norm_ref[0:1, 0:1]
    clip = CLIP_LIMIT / jnp.maximum(norm_ref[0:1, 0:1], CLIP_LIMIT)

    def update(first, out, gradient, at, rate, decay):
        news = adam_step(*(ref[at] for ref in states[first : first + 3]), gradient * clip, rate, decay)
        for ref, new in zip(outs[out : out + 3], news):
            ref[at] = new
        if decay:
            outs[out + 3][at] = news[2].astype(BF16)

    def heads_of(kind):
        half = heads // 2
        return jnp.concatenate(
            [
                sum_a[1 + head // half, :, (2 * (head % half) + kind) * HD : (2 * (head % half) + kind + 1) * HD]
                for head in range(heads)
            ],
            axis=1,
        )

    for index, gradient in enumerate((sum_a[0], heads_of(0), heads_of(1))):
        update(0, 0, gradient, index, RATE_MATRIX, WEIGHT_DECAY)
    update(3, 4, sum_b[0], ALL, RATE_MATRIX, WEIGHT_DECAY)
    update(6, 8, sum_e[0], ALL, RATE_MATRIX, WEIGHT_DECAY)
    for chunk in range(4):
        lanes = (ALL, slice(chunk * UNIT, (chunk + 1) * UNIT))
        update(9, 12, sum_e[1 + chunk], lanes, RATE_MATRIX, WEIGHT_DECAY)
        update(12, 16, sum_f[chunk], lanes, RATE_MATRIX, WEIGHT_DECAY)
    rows, each = states[15].shape
    update(15, 20, sum_v[0, 0:rows, 0:each], ALL, RATE_VECTOR, 0.0)


def adam_all(norm, sums, states):
    shapes = []
    for first in range(0, 18, 3):
        shapes += [(states[first].shape, F32)] * 3
        if first < 15:
            shapes.append((states[first].shape, BF16))
    vmem = pl.BlockSpec(memory_space=pltpu.VMEM)
    shapes.append(((1, 1), F32))
    return pl.pallas_call(
        functools.partial(adam_kernel, states[0].shape[2] // HD),
        out_shape=[jax.ShapeDtypeStruct(s, d) for s, d in shapes],
        in_specs=[vmem] * (6 + len(states)),
        out_specs=[vmem] * len(shapes),
        compiler_params=pltpu.CompilerParams(vmem_limit_bytes=VMEM_LIMIT),
        name="adam_all",
    )(norm, *sums, *states)


def pack_qkv(shard):
    rows, cols = shard.shape[1:]
    heads = cols // HD
    pairs = jnp.stack([shard[1].reshape(rows, heads, HD), shard[2].reshape(rows, heads, HD)], axis=2)
    pairs = pairs.reshape(rows, 2, cols)
    return jnp.stack([shard[0], pairs[:, 0], pairs[:, 1]])


def unpack_qkv(packed):
    rows, cols = packed.shape[1:]
    pairs = jnp.concatenate([packed[1], packed[2]], axis=1).reshape(rows, cols // HD, 2, HD)
    return jnp.stack(
        [packed[0], pairs[:, :, 0].reshape(rows, cols), pairs[:, :, 1].reshape(rows, cols)]
    )


def to_chunks(shard):
    rows = shard.shape[0]
    return shard.reshape(rows, -1, UNIT).transpose(1, 0, 2)


def from_chunks(chunks):
    return chunks.transpose(1, 0, 2).reshape(chunks.shape[1], -1)


def on_device(
    layer_input,
    page_boxes,
    output_grad,
    attn_proj,
    attn_first,
    attn_second,
    box_proj,
    box_first,
    box_second,
    merge_proj,
    merge_first,
    merge_second,
    expand_proj,
    expand_first,
    expand_second,
    shrink_proj,
    shrink_first,
    shrink_second,
    vectors,
    vector_first,
    vector_second,
):
    mp_count = lax.axis_size("mp")
    dp_count = lax.axis_size("dp")
    mp_index = lax.axis_index("mp")
    tokens, width = layer_input.shape
    cols = attn_proj.shape[2]
    heads = cols // HD
    own_tokens = tokens // mp_count
    inv_tokens = 1.0 / (tokens * dp_count)

    corners = page_boxes.T
    omega = (10000.0 ** (-np.arange(FREQS, dtype=np.float64) / FREQS)).astype(np.float32)[:, None]
    omega = jnp.asarray(omega)
    plan = (mp_count, dp_count) if dp_count == 16 and mp_count == 2 else None
    if plan is not None:
        each = vectors.shape[1]
        pick = np.zeros((128, width), np.float32)
        pick[np.arange(width) % each, np.arange(width)] = 1.0
        pick = jnp.asarray(pick)
        *kept, w_qkv, w_box, layer_out, dctx, dh1, g_expand, vec_sum, sum_f = layer_forward(
            layer_input,
            output_grad,
            corners,
            omega,
            pick,
            (attn_proj, box_proj, vectors, merge_proj.T, expand_proj, shrink_proj.T),
            plan,
            inv_tokens,
        )
        input_grad, sum_e, sum_a, sum_b, sum_v, norm = attend_backward(
            layer_input,
            w_qkv,
            w_box,
            kept,
            dctx,
            plan,
            inv_tokens,
            (dh1, vec_sum, sum_f, pick, g_expand),
        )
        layer_out = lax.all_gather(layer_out, "mp", axis=0, tiled=True)
        merge = [merge_proj.T, merge_first.T, merge_second.T]
        shrink = [shrink_proj.T, shrink_first.T, shrink_second.T]
        *results, norm = adam_all(
            norm,
            (sum_e, sum_f, sum_a, sum_b, sum_v),
            [attn_proj, attn_first, attn_second, box_proj, box_first, box_second, *merge]
            + [expand_proj, expand_first, expand_second, *shrink, vectors, vector_first, vector_second],
        )
        turned = (8, 9, 10, 11, 16, 17, 18, 19)
        results = [out.T if k in turned else out for k, out in enumerate(results)]
        return (layer_out, input_grad, norm.reshape(()), *results)
    shard_qkv = pack_qkv(attn_proj).astype(BF16)
    shard_e = jnp.concatenate([merge_proj.T[None], to_chunks(expand_proj)]).astype(BF16)
    shard_f = to_chunks(shrink_proj.T).astype(BF16)
    w_qkv = lax.all_gather(shard_qkv, "dp", axis=1, tiled=True)
    w_box = lax.all_gather(box_proj.astype(BF16), "dp", axis=0, tiled=True)
    w_expand = lax.all_gather(lax.all_gather(shard_e, "dp", axis=1, tiled=True), "mp", axis=1)
    w_shrink = lax.all_gather(lax.all_gather(shard_f, "dp", axis=1, tiled=True), "mp", axis=1)
    vecs = lax.all_gather(vectors, ("dp", "mp"), axis=1, tiled=True)
    vecs = jnp.pad(vecs, ((0, VROWS - vecs.shape[0]), (0, 0)))
    *kept, context = attend_forward(layer_input, corners, omega, w_qkv, w_box, vecs)
    context = lax.all_to_all(
        context.reshape(mp_count, own_tokens, cols), "mp", split_axis=0, concat_axis=0
    )

    def own_rows(array):
        return lax.dynamic_slice_in_dim(array, mp_index * own_tokens, own_tokens)

    layer_out, dctx, dh1, g_expand, g_shrink, vec_sum = feed_both(
        own_rows(layer_input), own_rows(output_grad), context, w_expand, w_shrink, vecs
    )
    g_feed = jnp.concatenate([g_expand, g_shrink])
    layer_out = lax.all_gather(layer_out, "mp", axis=0, tiled=True)
    dctx = lax.all_to_all(dctx, "mp", split_axis=0, concat_axis=0).reshape(tokens, cols)
    part, g_qkv, g_box, qkv_sum = attend_backward(
        layer_input, w_qkv, w_box, kept, dctx, None, inv_tokens
    )
    own_part = lax.psum_scatter(part.astype(BF16), "mp", scatter_dimension=0, tiled=True)
    own_grad = (own_part.astype(F32) + dh1).astype(BF16)
    input_grad = lax.all_gather(own_grad, "mp", axis=0, tiled=True)
    shard_attn = unpack_qkv(
        lax.psum_scatter(g_qkv, "dp", scatter_dimension=1, tiled=True).astype(F32) * inv_tokens
    )
    shard_box = lax.psum_scatter(g_box, "dp", scatter_dimension=0, tiled=True) * inv_tokens
    sum_feed = lax.psum_scatter(g_feed, "dp", scatter_dimension=2, tiled=True)
    sum_feed = lax.psum_scatter(sum_feed, "mp", scatter_dimension=1, tiled=True)[:, 0]
    sum_feed = sum_feed.astype(F32) * inv_tokens
    sum_expand, sum_shrink = sum_feed[0:5], sum_feed[5:]

    def placed(row):
        return lax.dynamic_update_slice_in_dim(
            jnp.zeros((width,), F32), row, mp_index * cols, 0
        )[None, :]

    value_sum = qkv_sum[0, cols:].reshape(heads, 2, HD)[:, 1].reshape(cols)
    vector_grad = jnp.concatenate(
        [vec_sum[0:6], placed(qkv_sum[0, 0:cols]), placed(value_sum), vec_sum[8:12]]
    )
    vector_shard = (
        lax.psum_scatter(vector_grad, ("dp", "mp"), scatter_dimension=1, tiled=True) * inv_tokens
    )
    square = sum(
        jnp.sum(shard * shard)
        for shard in (shard_attn, shard_box, sum_expand, sum_shrink, vector_shard)
    )
    grad_norm = jnp.sqrt(lax.psum(square, ("dp", "mp")))
    shard_merge = sum_expand[0].T
    shard_expand = from_chunks(sum_expand[1:])
    shard_shrink = from_chunks(sum_shrink).T
    clip_scale = CLIP_LIMIT / jnp.maximum(grad_norm, CLIP_LIMIT)
    results = [layer_out, input_grad, grad_norm]
    for master, first, second, shard in (
        (attn_proj, attn_first, attn_second, shard_attn),
        (box_proj, box_first, box_second, shard_box),
        (merge_proj, merge_first, merge_second, shard_merge),
        (expand_proj, expand_first, expand_second, shard_expand),
        (shrink_proj, shrink_first, shrink_second, shard_shrink),
    ):
        new_first, new_second, new_master = adam_step(
            master, first, second, shard * clip_scale, RATE_MATRIX, WEIGHT_DECAY
        )
        results += [new_first, new_second, new_master, new_master.astype(BF16)]
    results += adam_step(
        vectors, vector_first, vector_second, vector_shard * clip_scale, RATE_VECTOR, 0.0
    )
    return tuple(results)


def solution(mesh):
    rows = P("dp", None)
    attn = P(None, "dp", "mp")
    tall = P("dp", "mp")
    wide = P("mp", "dp")
    vector = P(None, ("dp", "mp"))
    in_specs = (rows,) * 3 + (attn,) * 3 + (tall,) * 3 + (wide,) * 3 + (tall,) * 3 + (wide,) * 3
    in_specs += (vector,) * 3
    out_specs = (rows, rows, P()) + (attn,) * 4 + (tall,) * 4 + (wide,) * 4 + (tall,) * 4
    out_specs += (wide,) * 4 + (vector,) * 3
    return jax.shard_map(
        on_device, mesh=mesh, in_specs=in_specs, out_specs=out_specs, check_vma=False
    )
```

```python
import functools
import types

import jax
import jax.numpy as jnp
import numpy as np
from jax import lax
from jax.experimental import pallas as pl
from jax.experimental.pallas import tpu as pltpu
from jax.sharding import PartitionSpec as P

HD = 64
FREQS = 32
PE = 128
PAGE = 512
STEP = 10

NORM_EPS = 1e-12
CLIP_LIMIT = 0.1
BETA_ONE = 0.9
BETA_TWO = 0.999
ADAM_EPS = 1e-08
RATE_MATRIX = 0.05
RATE_VECTOR = 0.5
WEIGHT_DECAY = 0.01

F32 = jnp.float32
BF16 = jnp.bfloat16
VMEM_LIMIT = 60 * 1024 * 1024

NN = (((1,), (0,)), ((), ()))
NT = (((1,), (1,)), ((), ()))
TN = (((0,), (0,)), ((), ()))


def dot(lhs, rhs, dims=NN):
    return lax.dot_general(lhs, rhs, dims, preferred_element_type=F32)


def aligned(index, size):
    return pl.ds(pl.multiple_of(index * size, size), size)


def swap_blocks(feat):
    return jnp.concatenate(
        [
            feat[FREQS : 2 * FREQS],
            feat[0:FREQS],
            feat[3 * FREQS :],
            feat[2 * FREQS : 3 * FREQS],
        ],
        axis=0,
    )


def turn_factors(trig):
    cos_x, sin_x = trig[0:FREQS], trig[FREQS : 2 * FREQS]
    cos_y, sin_y = trig[2 * FREQS : 3 * FREQS], trig[3 * FREQS :]
    return (
        jnp.concatenate([sin_x, sin_x, sin_y, sin_y], axis=0),
        jnp.concatenate([cos_x, -cos_x, cos_y, -cos_y], axis=0),
    )


MESH = pl.DeviceIdType.MESH
ALL = slice(None)
UNIT = 384


class Place:
    def __init__(self):
        rank = lax.axis_index("dp")
        self.m = lax.axis_index("mp")
        self.z = rank // 4
        self.y = (rank // 2) % 2
        self.c = rank % 2
        self.peer = {
            "x": (rank, 1 - self.m),
            "y": (rank + 2 - 4 * self.y, self.m),
            "c": (rank + 1 - 2 * self.c, self.m),
        }
        self.far = [((rank + 4 * step) % 16, self.m) for step in (1, 2, 3)]

    def signal(self):
        barrier = pltpu.get_barrier_semaphore()
        for device in list(self.peer.values()) + self.far:
            pl.semaphore_signal(barrier, inc=1, device_id=device, device_id_type=MESH)

    def wait(self):
        pl.semaphore_wait(pltpu.get_barrier_semaphore(), 6)

    def signal_all(self):
        barrier = pltpu.get_barrier_semaphore()
        rank = self.m * 16 + lax.axis_index("dp")

        def one(step, carry):
            to = (rank + step) % 32
            pl.semaphore_signal(barrier, inc=1, device_id=(to % 16, to // 16), device_id_type=MESH)
            return carry

        lax.fori_loop(1, 32, one, 0)

    def wait_all(self):
        pl.semaphore_wait(pltpu.get_barrier_semaphore(), 31)


def remote(src, dst, send_sem, recv_sem, device):
    return pltpu.make_async_remote_copy(
        src_ref=src,
        dst_ref=dst,
        send_sem=send_sem,
        recv_sem=recv_sem,
        device_id=device,
        device_id_type=MESH,
    )


SLOT = {"c": 0, "z": 1, "y": 4, "x": 5}
SLOTS = 6
SENT = (0, 1, 1, 1, 4, 5)


class Tree:
    lag = 1
    held_back = 0
    together = False

    def stage(self, index, chunk):
        raise NotImplementedError

    def event(self, number):
        for index in range(self.count - 1 - self.held_back, -1, -1):
            chunk = number - index * self.lag
            if self.together:

                @pl.when(chunk == 0)
                def _(index=index):
                    for each in range(self.chunks):
                        self.stage(index, each)

            elif self.chunks == 1:
                pl.when(chunk == 0)(lambda index=index: self.stage(index, 0))
            else:
                pl.when((chunk >= 0) & (chunk < self.chunks))(
                    lambda index=index, chunk=chunk: self.stage(index, chunk)
                )

    @property
    def events(self):
        return self.chunks + (self.count - 1 - self.held_back) * self.lag

    def rest(self):
        def one(chunk, carry):
            self.stage(self.count - 1, chunk)
            return carry

        lax.fori_loop(0, self.chunks, one, 0)


class Spread(Tree):
    def __init__(self, place, ref, chunks, order, sems):
        self.chunks, self.ref, self.sems, self.place = chunks, ref, sems, place
        have = {"x": place.m if "x" in order else 0, "z": place.z, "y": place.y}
        mine = {"x": place.m, "y": place.y}
        self.own = have
        self.steps, self.axes = [], order
        for axis in order:
            if axis == "z":
                sends = [(have, place.far[step - 1], step) for step in (1, 2, 3)]
                waits = [(dict(have, z=(place.z + 4 - step) % 4), step) for step in (1, 2, 3)]
            else:
                sends = [(have, place.peer[axis], SLOT[axis])]
                waits = [(dict(have, **{axis: 1 - mine[axis]}), SLOT[axis])]
            self.steps.append((sends, waits))
            have = dict(have, **{axis: ALL})
        self.other = place.peer["c"]
        self.count = len(self.steps) + 2

    def _copy(self, chunk, have, device, slot):
        came = 0 if chunk == ALL else chunk
        block = self.ref.at[chunk, self.place.c, have["x"], have["z"], have["y"]]
        sent = self.sems.at[0, 0, SENT[slot]]
        return remote(block, block, sent, self.sems.at[1, came, slot], device)

    def _plane(self, chunk, core):
        plane = self.ref.at[chunk, core]
        came = 0 if chunk == ALL else chunk
        return remote(plane, plane, self.sems.at[0, 0, 0], self.sems.at[1, came, 0], self.other)

    def stage(self, index, chunk):
        if index == self.count - 1:
            self._plane(chunk, 1 - self.place.c).wait_recv()
            return
        came = [self.own]
        if index > 0:
            came = []
            for have, slot in self.steps[index - 1][1]:
                self._copy(chunk, have, self.other, slot).wait_recv()
                came.append(have)
        if index < len(self.steps):
            for have, device, slot in self.steps[index][0]:
                self._copy(chunk, have, device, slot).start()
        for have in came:
            self._copy(chunk, have, self.other, 0).start()

    def drain(self):
        for axis, (sends, _) in zip(self.axes, self.steps):
            have, _, slot = sends[0]
            if axis == "z":
                have = dict(have, z=slice(0, 3))
            self._copy(ALL, have, self.other, slot).wait_send()
        self._plane(ALL, self.place.c).wait_send()


RANKS = [(c, z, y) for z in range(4) for y in range(2) for c in range(2)]


def natural(ref, chunk, side):
    return jnp.concatenate([ref[chunk, c, side, z, y] for c, z, y in RANKS], axis=0)


def put_natural(ref, chunk, side, value):
    rows = value.shape[0] // len(RANKS)
    for spot, (c, z, y) in enumerate(RANKS):
        ref[chunk, c, side, z, y] = value[spot * rows : (spot + 1) * rows]


class Reduce(Tree):
    def __init__(self, place, full, total, lands, chunks, order, sems, finish):
        self.place, self.full, self.total, self.lands = place, full, total, lands
        self.chunks, self.sems, self.finish = chunks, sems, finish
        mine = {"x": place.m, "y": place.y}
        self.across = ALL if "x" in order else 0
        have = {"x": self.across, "z": ALL, "y": ALL}
        self.order, self.haves = order, []
        for axis in order:
            before = have
            if axis != "c":
                have = dict(have, **{axis: place.z if axis == "z" else mine[axis]})
            self.haves.append((before, have))
        self.count = len(order) + 1

    def _at(self, chunk, have):
        if self.total is None:
            return self.full.at[chunk, self.place.c, have["x"], have["z"], have["y"]]
        return self.total.at[chunk, have["x"], have["z"], have["y"]]

    def _copies(self, index, chunk):
        axis, (before, _) = self.order[index], self.haves[index]
        place, land = self.place, self.lands[axis]

        def copy(src, dst, slot, device):
            return remote(src, dst, self.sems.at[0, 0, SENT[slot]], self.sems.at[1, chunk, slot], device)

        if axis == "c":
            source = self.full.at[chunk, 1 - place.c, self.across]
            return [copy(source, land.at[chunk], SLOT[axis], place.peer[axis])]
        if axis == "z":
            return [
                copy(
                    self._at(chunk, dict(before, z=(place.z + step) % 4)),
                    land.at[chunk, step - 1],
                    step,
                    place.far[step - 1],
                )
                for step in (1, 2, 3)
            ]
        other = 1 - (place.m if axis == "x" else place.y)
        source = self._at(chunk, dict(before, **{axis: other}))
        return [copy(source, land.at[chunk], SLOT[axis], place.peer[axis])]

    def stage(self, index, chunk):
        if index > 0:
            axis, (_, have) = self.order[index - 1], self.haves[index - 1]
            land = self.lands[axis]
            for copy in self._copies(index - 1, chunk):
                copy.wait_recv()
            mine = self._at(chunk, have)
            last = index == self.count - 1
            if axis == "z":
                value = mine[...].astype(F32)
                for step in range(3):
                    value += land[chunk, step].astype(F32)
            elif last:
                value = mine[...].astype(F32) + land[chunk].astype(F32)
            else:
                value = mine[...] + land[chunk]
            if last:
                self.finish(chunk, value)
            else:
                mine[...] = value.astype(mine.dtype)
        if index < self.count - 1:
            for copy in self._copies(index, chunk):
                copy.start()

    def drain(self):
        for axis in self.order:
            land = self.lands[axis]
            slot = SLOT[axis]
            sent = self.sems.at[0, 0, SENT[slot]]
            remote(land, land, sent, self.sems.at[1, 0, slot], self.place.peer["c"]).wait_send()


class Everyone:
    def __init__(self, place, send_block, land_block, sems):
        self.rank = place.m * 16 + lax.axis_index("dp")
        self.send_block, self.land_block, self.sems = send_block, land_block, sems

    def _copy(self, step):
        to = (self.rank + step) % 32
        return remote(
            self.send_block(to),
            self.land_block(step),
            self.sems.at[0, step - 1],
            self.sems.at[1, step - 1],
            (to % 16, to // 16),
        )

    def _each(self, act):
        def one(step, carry):
            act(self._copy(step))
            return carry

        lax.fori_loop(1, 32, one, 0)

    def start(self):
        self._each(lambda copy: copy.start())

    def wait(self):
        self._each(lambda copy: copy.wait())


VROWS = 16


def rows_from_blocks(blocks, pick, counts):
    mp_count, dp_count = counts
    width = pick.shape[1]
    each = width // (mp_count * dp_count)
    wide = lax.dot_general(
        blocks, pick, NN, precision=lax.Precision.HIGHEST, preferred_element_type=F32
    )
    lane = lax.broadcasted_iota(jnp.int32, (VROWS, width), 1)
    table = jnp.zeros((VROWS, width), F32)
    for m in range(mp_count):
        for r, (c, z, y) in enumerate(RANKS):
            first = (r * mp_count + m) * each
            row = (((c * mp_count + m) * 4 + z) * 2 + y) * VROWS
            table += jnp.where((lane >= first) & (lane < first + each), wide[row : row + VROWS], 0.0)
    return table


def attend_setup(heads, m, box_full, vec_ref, box_heads, bias):
    cols = heads * HD
    for head in range(heads):
        box_heads[head] = box_full[:, head * HD : (head + 1) * HD]
    width = vec_ref.shape[1]
    own = jnp.where(m == 0, vec_ref[6:8, 0:cols], vec_ref[6:8, width - cols :])
    spread = exact_dot(jnp.broadcast_to(own[1:2], (8, cols)), pair_place(cols))
    bias[0:1, 0:cols] = own[0:1]
    bias[0:1, cols:] = spread[0:1]


def attend_trig(omega_ref, corner_ref, trig_ref):
    corner = corner_ref[...].astype(F32)
    angle_x = omega_ref[...] * ((corner[0:1] + corner[2:3]) * 0.5)
    angle_y = omega_ref[...] * ((corner[1:2] + corner[3:4]) * 0.5)
    trig_ref[0:FREQS, :] = jnp.cos(angle_x)
    trig_ref[FREQS : 2 * FREQS, :] = jnp.sin(angle_x)
    trig_ref[2 * FREQS : 3 * FREQS, :] = jnp.cos(angle_y)
    trig_ref[3 * FREQS :, :] = jnp.sin(angle_y)


def quiet(*args):
    return None


def attend_math(heads, r, weights, page_of, projected, attended):
    cols = heads * HD
    pages = r.x.shape[0] // PAGE

    def project(page, carry):
        rows = aligned(page, PAGE)
        tokens = r.x[rows, :]
        query = dot(tokens, weights(0)) + r.bias[0:1, 0:cols]
        query = query.astype(BF16) * HD ** (-0.5)
        r.qtok[rows, :] = query
        qa_rows = query.T
        for half in range(2):
            lanes = slice(half * cols, (half + 1) * cols)
            pair = dot(tokens, weights(1 + half)) + r.bias[0:1, cols + half * cols : 2 * cols + half * cols]
            pair = pair.astype(BF16)
            r.kvtok[rows, lanes] = pair
            turned = pair.T
            for spot in range(heads // 2):
                head_rows = slice((half * heads // 2 + spot) * HD, (half * heads // 2 + spot + 1) * HD)
                r.kt[head_rows, rows] = turned[2 * spot * HD : (2 * spot + 1) * HD]
                r.vt[head_rows, rows] = turned[(2 * spot + 1) * HD : (2 * spot + 2) * HD]
        trig = r.trig[:, rows]
        kft = trig.astype(BF16)
        r.kft[:, rows] = kft
        r.kftok[rows, :] = kft.T
        own, partner = turn_factors(trig)
        for head in range(heads):
            query_head = qa_rows[head * HD : (head + 1) * HD]
            proj = dot(r.box_heads[head], query_head)
            feat = proj * own + swap_blocks(proj) * partner
            r.qa[head, 0:PE, rows] = feat.astype(BF16)
            r.qa[head, PE : PE + HD, rows] = query_head
        projected(page)
        return carry

    lax.fori_loop(0, pages, project, 0)

    def attend(step, carry):
        turn, pair = step // (heads // 2), step % (heads // 2)
        rows = aligned(page_of(turn), PAGE)
        halves = []
        blank = jnp.zeros((HD, PAGE), BF16)
        for side in range(2):
            head = pair * 2 + side
            lanes = aligned(head, 2 * HD)
            left = jnp.concatenate([r.kftok[rows, :], r.kvtok[rows, lanes]], axis=1)
            score = dot(left, jnp.concatenate([r.qa[head, :, rows], blank], axis=0))
            top = jnp.max(score, axis=0, keepdims=True)
            weight = jnp.exp(score - top)
            total = jnp.sum(weight, axis=0, keepdims=True)
            value = r.vt[aligned(head, HD), rows]
            halves.append(dot(value, weight.astype(BF16)) * (1.0 / total))
            r.log[head, :, rows] = top + jnp.log(total)
        both = jnp.concatenate(halves, axis=0).astype(BF16)
        lanes = aligned(pair, 2 * HD)
        r.ctxt[lanes, rows] = both
        r.ctx[rows, lanes] = both.T
        attended(step, turn, pair)
        return carry

    lax.fori_loop(0, pages * (heads // 2), attend, 0)


def attend_buffers(heads, tokens):
    cols = heads * HD
    kept = [
        ("qa", (heads, PE + HD, tokens), BF16),
        ("qtok", (tokens, cols), BF16),
        ("kvtok", (tokens, 2 * cols), BF16),
        ("kt", (cols, tokens), BF16),
        ("kft", (PE, tokens), BF16),
        ("trig", (PE, tokens), F32),
        ("ctxt", (cols, tokens), BF16),
        ("log", (heads, 1, tokens), F32),
    ]
    used = [
        ("kftok", (tokens, PE), BF16),
        ("box_heads", (heads, PE, HD), BF16),
        ("bias", (8, 3 * cols), F32),
        ("ctx", (tokens, cols), BF16),
        ("vt", (cols, tokens), BF16),
    ]
    return kept, used


def attend_kernel(heads, names, *refs):
    r = types.SimpleNamespace(**dict(zip(names, refs)))
    attend_setup(heads, lax.axis_index("mp"), r.box, r.vec, r.box_heads, r.bias)
    attend_trig(r.omega, r.corner, r.trig)
    attend_math(heads, r, lambda chunk: r.w[chunk], lambda turn: turn, quiet, quiet)


def attend_forward(x, corners, omega, w_qkv, w_box, vecs):
    tokens = x.shape[0]
    heads = w_box.shape[1] // HD
    kept, used = attend_buffers(heads, tokens)
    outs = kept + [used[3]]
    scratch = used[:3] + used[4:]
    names = ["x", "corner", "omega", "w", "box", "vec"] + [item[0] for item in outs + scratch]
    vmem = pl.BlockSpec(memory_space=pltpu.VMEM)
    return pl.pallas_call(
        functools.partial(attend_kernel, heads, names),
        out_shape=[jax.ShapeDtypeStruct(shape, kind) for _, shape, kind in outs],
        in_specs=[vmem] * 6,
        out_specs=[vmem] * len(outs),
        scratch_shapes=[pltpu.VMEM(shape, kind) for _, shape, kind in scratch],
        compiler_params=pltpu.CompilerParams(vmem_limit_bytes=VMEM_LIMIT),
        name="attend_forward",
    )(x, corners, omega, w_qkv, w_box, vecs)


TILE = 256


def normal_parts(value):
    bell = jnp.exp(value * value * -0.5)
    t = 1.0 / (1.0 + (0.3275911 * 2.0 ** (-0.5)) * jnp.abs(value))
    tail = 0.5 * 1.061405429
    for factor in (-1.453152027, 1.421413741, -0.284496736, 0.254829592):
        tail = tail * t + 0.5 * factor
    tail = tail * t * bell
    phi = jnp.where(value < 0.0, tail, 1.0 - tail)
    return phi, phi + value * (bell * (0.5 / np.pi) ** 0.5)


def norm_stats(value):
    mean = jnp.mean(value, axis=-1, keepdims=True)
    centred = value - mean
    var = jnp.mean(centred * centred, axis=-1, keepdims=True)
    return centred, lax.rsqrt(var + NORM_EPS)


def norm_back(grad_normed, normed, scale):
    first = jnp.mean(grad_normed, axis=-1, keepdims=True)
    second = jnp.mean(grad_normed * normed, axis=-1, keepdims=True)
    return scale * (grad_normed - first - normed * second)


def col_sum(value):
    return jnp.sum(value, axis=0, keepdims=True)


def feed_math(r, hooks):
    hook = {name: quiet for name in ("entered", "grew", "turned", "shrinks", "shrank", "left")}
    hook.update(hooks)
    tokens = r.x.shape[0]
    sides = r.ctxx.shape[0]
    steps = r.ws.shape[0]
    tiles = tokens // TILE
    wide = sides * UNIT
    sum2 = dnorm = r.sum2

    def flat(ref, chunk, side):
        return ref[chunk, side] if len(ref.shape) == 4 else natural(ref, chunk, side)

    def put(ref, chunk, side, value):
        if len(ref.shape) == 4:
            ref[chunk, side] = value
        else:
            put_natural(ref, chunk, side, value)

    def both(ref, chunk):
        return jnp.concatenate([flat(ref, chunk, side) for side in range(sides)], axis=1)

    def put_both(ref, chunk, value):
        for side in range(sides):
            put(ref, chunk, side, value[:, side * UNIT : (side + 1) * UNIT])

    def bias_at(step, side):
        first = side * steps + step
        return (pl.ds(8 + first // 2, 1), aligned(first % 2, UNIT))

    def enter(tile, carry):
        rows = aligned(tile, TILE)
        total = r.x[rows, :].astype(F32) + r.vec[4:5, :]
        for side in range(sides):
            total += dot(r.ctxx[side, rows, :], flat(r.we, 0, side), NT)
        centred, scale = norm_stats(total)
        normed = centred * scale
        r.norm1[rows, :] = normed
        r.scale1[rows, :] = scale
        shifted = normed * r.vec[0:1, :] + r.vec[1:2, :]
        r.al[rows, :] = shifted.astype(BF16)
        sum2[rows, :] = shifted + r.vec[5:6, :]
        return carry

    lax.fori_loop(0, tiles, enter, 0)
    hook["entered"]()

    def grow(step, carry):
        whole = aligned(step, wide)
        bias = jnp.concatenate([r.vec[bias_at(step, side)] for side in range(sides)], axis=1)

        def one(tile, inner):
            rows = aligned(tile, TILE)
            pre = dot(r.al[rows, :], both(r.we, 1 + step)) + bias
            phi, slope = normal_parts(pre)
            low = (pre * phi).astype(BF16)
            r.act[rows, whole] = low
            r.slope[rows, whole] = slope.astype(BF16)
            sum2[rows, :] += dot(low, both(r.ws, step), NT)
            hook["grew"](step * tiles + tile)
            return inner

        lax.fori_loop(0, tiles, one, 0)
        return carry

    lax.fori_loop(0, steps, grow, 0)
    r.vsum[...] = jnp.zeros_like(r.vsum)

    def turn(tile, carry):
        rows = aligned(tile, TILE)
        centred, scale = norm_stats(sum2[rows, :])
        normed = centred * scale
        r.out[rows, :] = (normed * r.vec[2:3, :] + r.vec[3:4, :]).astype(BF16)
        grad = r.og[rows, :].astype(F32)
        r.vsum[2:3, :] += col_sum(grad * normed)
        r.vsum[3:4, :] += col_sum(grad)
        back = norm_back(grad * r.vec[2:3, :], normed, scale)
        r.vsum[5:6, :] += col_sum(back)
        r.dh2l[rows, :] = back.astype(BF16)
        dnorm[rows, :] = back
        hook["turned"](tile)
        return carry

    lax.fori_loop(0, tiles, turn, 0)
    r.flip[...] = r.dh2l[...].T

    def grad_shrink(step, carry):
        grad = dot(r.flip[...], r.act[:, aligned(step, wide)]).astype(BF16)
        put_both(r.gs, step, grad)
        hook["shrinks"](step)
        return carry

    lax.fori_loop(0, steps, grad_shrink, 0)

    def shrink(step, carry):
        whole = aligned(step, wide)

        def one(tile, inner):
            rows = aligned(tile, TILE)
            grad = dot(r.dh2l[rows, :], both(r.ws, step))
            low = (grad * r.slope[rows, whole].astype(F32)).astype(BF16)
            r.slope[rows, whole] = low
            sums = col_sum(low.astype(F32))
            for side in range(sides):
                r.vsum[bias_at(step, side)] += sums[:, side * UNIT : (side + 1) * UNIT]
            dnorm[rows, :] += dot(low, both(r.we, 1 + step), NT)
            hook["shrank"](step * tiles + tile)
            return inner

        lax.fori_loop(0, tiles, one, 0)
        return carry

    lax.fori_loop(0, steps, shrink, 0)

    def leave(tile, carry):
        rows = aligned(tile, TILE)
        grad = dnorm[rows, :]
        normed = r.norm1[rows, :]
        r.vsum[0:1, :] += col_sum(grad * normed)
        r.vsum[1:2, :] += col_sum(grad)
        back = norm_back(grad * r.vec[0:1, :], normed, r.scale1[rows, :])
        r.vsum[4:5, :] += col_sum(back)
        low = back.astype(BF16)
        r.dh1l[rows, :] = low
        for side in range(sides):
            r.dctx[side, rows, :] = dot(low, flat(r.we, 0, side)).astype(BF16)
        hook["left"](tile)
        return carry

    lax.fori_loop(0, tiles, leave, 0)
    r.flip[...] = r.al[...].T

    def grad_expand(step, carry):
        grad = dot(r.flip[...], r.slope[:, aligned(step, wide)]).astype(BF16)
        put_both(r.ge, 1 + step, grad)
        return carry

    lax.fori_loop(0, steps, grad_expand, 0)
    r.flip[...] = r.dh1l[...].T
    for side in range(sides):
        put(r.ge, 0, side, dot(r.flip[...], r.ctxx[side]).astype(BF16))


def feed_buffers(tokens, width, hidden):
    return [
        ("norm1", (tokens, width), F32),
        ("scale1", (tokens, 1), F32),
        ("sum2", (tokens, width), F32),
        ("al", (tokens, width), BF16),
        ("act", (tokens, hidden), BF16),
        ("slope", (tokens, hidden), BF16),
        ("dh2l", (tokens, width), BF16),
        ("flip", (width, tokens), BF16),
    ]


def feed_kernel(names, *refs):
    feed_math(types.SimpleNamespace(**dict(zip(names, refs))), {})


def feed_both(x, og, ctx, w_expand, w_shrink, vecs):
    tokens, width = x.shape
    chunks, sides = w_shrink.shape[0:2]
    outs = [
        ("out", (tokens, width), BF16),
        ("dctx", (sides, tokens, UNIT), BF16),
        ("dh1l", (tokens, width), BF16),
        ("ge", (chunks + 1, sides, width, UNIT), BF16),
        ("gs", (chunks, sides, width, UNIT), BF16),
        ("vsum", (VROWS, width), F32),
    ]
    scratch = feed_buffers(tokens, width, sides * chunks * UNIT)
    names = ["x", "og", "ctxx", "we", "ws", "vec"] + [item[0] for item in outs + scratch]
    vmem = pl.BlockSpec(memory_space=pltpu.VMEM)
    return pl.pallas_call(
        functools.partial(feed_kernel, names),
        out_shape=[jax.ShapeDtypeStruct(shape, kind) for _, shape, kind in outs],
        in_specs=[vmem] * 6,
        out_specs=[vmem] * len(outs),
        scratch_shapes=[pltpu.VMEM(shape, kind) for _, shape, kind in scratch],
        compiler_params=pltpu.CompilerParams(vmem_limit_bytes=VMEM_LIMIT),
        name="feed_both",
    )(x, og, ctx, w_expand, w_shrink, vecs)


def layer_kernel(heads, plan, inv_tokens, names, kept, used, feeds, *refs):
    r = types.SimpleNamespace(**dict(zip(names, refs)))
    cols = heads * HD
    tokens = r.x_all.shape[0]
    pages = tokens // PAGE
    own_tokens = tokens // 2
    tiles = own_tokens // TILE
    place = Place()
    place.signal()
    m, peer = place.m, place.peer["x"]
    at = (place.z, place.y)
    own = aligned(m, own_tokens)
    load_x = pltpu.make_async_copy(r.x_all.at[own, :], r.x, r.load_sem.at[0])
    load_og = pltpu.make_async_copy(r.og_all.at[own, :], r.og, r.load_sem.at[1])
    load_x.start()
    load_og.start()
    r.w[(0, place.c, 0, *at)] = r.attn[0].astype(BF16)
    for half in range(2):
        r.w[(1 + half, place.c, 0, *at)] = jnp.concatenate(
            [
                r.attn[1 + kind, :, head * HD : (head + 1) * HD].astype(BF16)
                for head in range(half * heads // 2, (half + 1) * heads // 2)
                for kind in range(2)
            ],
            axis=1,
        )
    r.box_gather[(0, place.c, 0, *at)] = r.shard_box[...]
    r.vec_gather[(0, place.c, m, *at)] = jnp.zeros((VROWS, 128), F32)
    table_at = (slice(0, r.vectors.shape[0]), slice(0, r.vectors.shape[1]))
    r.vec_gather[(0, place.c, m, *at, *table_at)] = r.vectors[...]
    r.we[(0, place.c, m, *at)] = r.merge[...].astype(BF16)
    for chunk in range(4):
        lanes = slice(chunk * UNIT, (chunk + 1) * UNIT)
        r.we[(1 + chunk, place.c, m, *at)] = r.expand[:, lanes].astype(BF16)
        r.ws[(chunk, place.c, m, *at)] = r.shrink[:, lanes].astype(BF16)
    place.wait()
    tree_v = Spread(place, r.vec_gather, 1, "xzy", r.v_sem)
    tree_b = Spread(place, r.box_gather, 1, "zy", r.b_sem)
    tree_a = Spread(place, r.w, 3, "zy", r.a_sem)
    tree_e = Spread(place, r.we, 5, "zyx", r.e_sem)
    tree_f = Spread(place, r.ws, 4, "zxy", r.f_sem)
    tree_e.lag = tree_f.lag = 2
    first, late = tree_a.events, 3
    begun = first - late

    def weights_event(number):
        tree_e.event(number)
        tree_f.event(number)

    def finish(chunk, value):
        r.sum_f[chunk] = value * inv_tokens

    back_f = Reduce(
        place, r.gs, None, dict(c=r.fc, y=r.fy, z=r.fz, x=r.fx), 4, "cyxz", r.back_sem, finish
    )
    back_f.lag, back_f.held_back = 2, 1

    def attention(*scoped):
        q = types.SimpleNamespace(**dict(zip([item[0] for item in kept + used] + ["x"], scoped)))
        load_all = pltpu.make_async_copy(r.x_all, q.x, r.load_sem.at[2])
        load_all.start()

        tree_v.stage(0, 0)

        def begin(number, carry):
            tree_v.event(number + 1)
            tree_b.event(number)

            @pl.when(number == 4)
            def _():
                r.vec[...] = rows_from_blocks(
                    r.vec_gather[...].reshape(-1, 128), r.pick[...], plan
                )
                r.box_out[...] = natural(r.box_gather, 0, 0).astype(BF16)
                attend_setup(heads, m, r.box_out, r.vec, q.box_heads, q.bias)

            tree_a.event(number)
            weights_event(number - late)
            pl.when(number == 0)(lambda: attend_trig(r.omega, r.corner, q.trig))
            return carry

        lax.fori_loop(0, first, begin, 0)
        keep_w = pltpu.make_async_copy(r.w, r.w_out, r.load_sem.at[3])
        keep_w.start()
        load_all.wait()

        def projected(page):
            weights_event(begun + page)

        piece = PAGE // 2

        def swap_copy(index):
            theirs = pages * (1 - m) + index
            return remote(
                q.ctx.at[aligned(theirs, piece), :],
                r.ctxx.at[m, aligned(index, piece), :],
                r.ctx_sem.at[0, index],
                r.ctx_sem.at[1, index],
                peer,
            )

        def attended(step, turn, pair):
            pl.when((step % 2 == 0) & (step < 8))(lambda: weights_event(begun + pages + step // 2))

            @pl.when(step == heads // 2 - 1)
            def _():
                swap_copy(2 - 2 * m).start()
                swap_copy(1).start()

            @pl.when(step == heads - 1)
            def _():
                swap_copy(2 * m).start()

        attend_math(
            heads,
            q,
            lambda chunk: natural(r.w, chunk, 0),
            lambda turn: turn * m + (pages - 1 - turn) * (1 - m),
            projected,
            attended,
        )
        stores = [
            pltpu.make_async_copy(getattr(q, name), getattr(r, name + "_out"), r.store_sem.at[k])
            for k, (name, _, _) in enumerate(kept)
        ]
        for copy in stores:
            copy.start()
        r.ctxx[m] = q.ctx[own, :]
        for index in range(pages):
            copy = remote(
                q.ctx.at[aligned(index, piece), :],
                r.ctxx.at[1 - m, aligned(index, piece), :],
                r.ctx_sem.at[0, index],
                r.ctx_sem.at[1, index],
                peer,
            )
            copy.wait_recv()
            copy.wait_send()
        for copy in stores:
            copy.wait()
        keep_w.wait()

    pl.run_scoped(
        attention,
        *[pltpu.VMEM(shape, kind) for _, shape, kind in kept + used],
        pltpu.VMEM(r.x_all.shape, BF16),
    )

    def feed(*scoped):
        q = types.SimpleNamespace(**dict(zip([item[0] for item in feeds], scoped)))
        for name in ("x", "og", "we", "ws", "vec", "ctxx", "dh1l", "ge", "gs", "vsum"):
            setattr(q, name, getattr(r, name))

        def out_copies(tile):
            rows = aligned(tile, TILE)
            there = r.out_full.at[pl.ds(pl.multiple_of(m * own_tokens + tile * TILE, TILE), TILE), :]
            return (
                pltpu.make_async_copy(q.out.at[rows, :], there, r.swap_sem.at[0, tile]),
                remote(q.out.at[rows, :], there, r.swap_sem.at[1, tile], r.swap_sem.at[2, tile], peer),
            )

        def dctx_copies(tile):
            rows = aligned(tile, TILE)
            there = r.dctx_full.at[pl.ds(pl.multiple_of(m * own_tokens + tile * TILE, TILE), TILE), :]
            return (
                pltpu.make_async_copy(q.dctx.at[m, rows, :], there, r.swap_sem.at[3, tile]),
                remote(
                    q.dctx.at[1 - m, rows, :], there, r.swap_sem.at[4, tile], r.swap_sem.at[5, tile], peer
                ),
            )

        def start(copies):
            for copy in copies:
                copy.start()

        def grew(number):
            pl.when(number % 3 == 1)(lambda: weights_event(begun + pages + 4 + number // 3))

        def shrank(number):
            pl.when(number % 2 == 1)(lambda: back_f.event(4 + number // 2))

        load_x.wait()
        load_og.wait()
        feed_math(
            q,
            dict(
                grew=grew,
                turned=lambda tile: start(out_copies(tile)),
                shrinks=lambda step: back_f.event(step),
                shrank=shrank,
                left=lambda tile: start(dctx_copies(tile)),
            ),
        )
        back_f.rest()
        back_f.drain()
        for tile in range(tiles):
            for copy in out_copies(tile) + dctx_copies(tile):
                copy.wait()

    pl.run_scoped(feed, *[pltpu.VMEM(shape, kind) for _, shape, kind in feeds])
    for tree in (tree_v, tree_b, tree_a, tree_e, tree_f):
        tree.drain()


def layer_forward(x, og, corners, omega, pick, shards, plan, inv_tokens):
    tokens, width = x.shape
    cols = shards[1].shape[1]
    heads = cols // HD
    own = tokens // 2
    unit = (width // 16, UNIT)
    kept, used = attend_buffers(heads, tokens)
    feeds = feed_buffers(own, width, 8 * UNIT)
    feeds += [("out", (own, width), BF16), ("dctx", (2, own, UNIT), BF16)]
    free = pl.BlockSpec(memory_space=pl.ANY)
    vmem = pl.BlockSpec(memory_space=pltpu.VMEM)
    inputs = [("x_all", free), ("og_all", free), ("corner", vmem), ("omega", vmem), ("pick", vmem)]
    inputs += [(name, vmem) for name in ("attn", "shard_box", "vectors", "merge", "expand", "shrink")]
    outs = [(name + "_out", shape, kind, free) for name, shape, kind in kept]
    outs += [
        ("w_out", (3, 2, 1, 4, 2, *unit), BF16, free),
        ("box_out", (PE, cols), BF16, vmem),
        ("out_full", (tokens, width), BF16, free),
        ("dctx_full", (tokens, cols), BF16, free),
        ("dh1l", (own, width), BF16, vmem),
        ("ge", (5, 2, 2, 4, 2, *unit), BF16, vmem),
        ("vsum", (VROWS, width), F32, vmem),
        ("sum_f", (4, *unit), F32, vmem),
    ]
    dma = pltpu.SemaphoreType.DMA
    scratch = [
        ("x", pltpu.VMEM((own, width), BF16)),
        ("og", pltpu.VMEM((own, width), BF16)),
        ("vec", pltpu.VMEM((VROWS, width), F32)),
        ("w", pltpu.VMEM((3, 2, 1, 4, 2, *unit), BF16)),
        ("box_gather", pltpu.VMEM((1, 2, 1, 4, 2, PE // 16, cols), F32)),
        ("vec_gather", pltpu.VMEM((1, 2, 2, 4, 2, VROWS, 128), F32)),
        ("we", pltpu.VMEM((5, 2, 2, 4, 2, *unit), BF16)),
        ("ws", pltpu.VMEM((4, 2, 2, 4, 2, *unit), BF16)),
        ("ctxx", pltpu.VMEM((2, own, cols), BF16)),
        ("gs", pltpu.VMEM((4, 2, 2, 4, 2, *unit), BF16)),
        ("fc", pltpu.VMEM((4, 2, 4, 2, *unit), BF16)),
        ("fy", pltpu.VMEM((4, 2, 4, *unit), BF16)),
        ("fx", pltpu.VMEM((4, 4, *unit), BF16)),
        ("fz", pltpu.VMEM((4, 3, *unit), BF16)),
        ("ctx_sem", dma((2, 3))),
        ("a_sem", dma((2, 3, SLOTS))),
        ("b_sem", dma((2, 1, SLOTS))),
        ("v_sem", dma((2, 1, SLOTS))),
        ("e_sem", dma((2, 5, SLOTS))),
        ("f_sem", dma((2, 4, SLOTS))),
        ("back_sem", dma((2, 4, SLOTS))),
        ("load_sem", dma((4,))),
        ("store_sem", dma((len(kept),))),
        ("swap_sem", dma((6, own // TILE))),
    ]
    names = [item[0] for item in inputs + outs + scratch]
    return pl.pallas_call(
        functools.partial(layer_kernel, heads, plan, inv_tokens, names, kept, used, feeds),
        out_shape=[jax.ShapeDtypeStruct(shape, kind) for _, shape, kind, _ in outs],
        in_specs=[item[1] for item in inputs],
        out_specs=[item[3] for item in outs],
        scratch_shapes=[item[1] for item in scratch],
        compiler_params=pltpu.CompilerParams(
            vmem_limit_bytes=VMEM_LIMIT, collective_id=0, has_side_effects=True
        ),
        name="layer_forward",
    )(x, og, corners, omega, pick, *shards)


def pair_place(cols):
    spot = lax.broadcasted_iota(jnp.int32, (cols, 2 * cols), 0)
    lane = lax.broadcasted_iota(jnp.int32, (cols, 2 * cols), 1)
    target = ((spot >> 6) << 7) + HD + (spot & (HD - 1))
    return jnp.where(lane == target, 1.0, 0.0)


def exact_dot(lhs, rhs, dims=NN):
    return lax.dot_general(
        lhs, rhs, dims, precision=lax.Precision.HIGHEST, preferred_element_type=F32
    )


def attend_back_kernel(heads, plan, inv_tokens, *refs):
    inputs, refs = refs[:12], refs[12:]
    if plan is not None:
        load_sem, held, refs = refs[-1], refs[-13:-1], refs[:-13]
        loads = [
            pltpu.make_async_copy(src, dst, load_sem.at[k]) for k, (src, dst) in enumerate(zip(inputs, held))
        ]
        early = (0, 2, 7, 11)
        for k in sorted(range(12), key=lambda k: k not in early):
            loads[k].start()
        inputs = held
    x_ref, w_ref, box_ref, *inputs = inputs
    qa_ref, qtok_ref, kvtok_ref, kt_ref, kft_ref, trig_ref, ctxt_ref, log_ref, dctx_ref = inputs
    cols = heads * HD
    tokens = x_ref.shape[0]
    pages = tokens // PAGE
    m = lax.axis_index("mp")
    piece = PAGE // 2
    pieces = 2 * pages
    lane = lax.broadcasted_iota(jnp.int32, (1, 2 * HD), 1)
    lower = lane < HD
    if plan is None:
        inp_ref, gw_ref, gbox_ref, qvsum_ref, *refs = refs
        kftok, dctxt, boxt, dtok, xt, gbox = refs
        before, after = 0, 0

        def background(number):
            pass
    else:
        dh1_ref, vsum_ref, sumf_ref, pick_ref, full_e, *refs = refs
        inp_ref, sum_e, sum_a, sum_b, sum_v, norm_ref, *refs = refs
        kftok, dctxt, boxt, dtok, xt, gbox, *refs = refs
        came, total_e, full_a, full_b, full_v, land_v, norms, *refs = refs
        ec, ey, ez, ex, ac, ay, az, bc, by, bz, *refs = refs
        e_sem, a_sem, b_sem, v_sem, n_sem, i_sem, loc_sem = refs
        place = Place()
        place.signal_all()
        fill = pltpu.make_async_copy(full_e.at[:, place.c], total_e, loc_sem.at[0])
        fill.start()
        place.wait_all()

        def finish(out):
            def put(chunk, value):
                out[chunk] = value * inv_tokens

            return put

        tree_e = Reduce(
            place, full_e, total_e, dict(c=ec, y=ey, z=ez, x=ex), 5, "cyxz", e_sem, finish(sum_e)
        )
        tree_e.lag, tree_e.held_back = 2, 1
        tree_a = Reduce(place, full_a, None, dict(c=ac, y=ay, z=az), 3, "cyz", a_sem, finish(sum_a))
        tree_b = Reduce(place, full_b, None, dict(c=bc, y=by, z=bz), 1, "cyz", b_sem, finish(sum_b))

        def block_of(rank):
            r = rank % 16
            return full_v.at[rank // 16, r // 4, (r // 2) % 2, r % 2]

        spot = (place.m, place.z, place.y, place.c)
        all_v = Everyone(place, block_of, lambda step: land_v.at[step - 1], v_sem)
        all_n = Everyone(place, lambda rank: norms.at[spot], lambda step: norms.at[spot], n_sem)

        def background(number):
            tree_e.event(number)

        background(0)
        fill.wait()
        for k in early:
            loads[k].wait()

    boxt[...] = box_ref[...].T
    gbox[...] = jnp.zeros_like(gbox)

    def prepare(page, carry):
        rows = aligned(page, PAGE)
        kftok[rows, :] = kft_ref[:, rows].T
        dctxt[:, rows] = dctx_ref[rows, :].T
        xt[:, rows] = x_ref[rows, :].T
        if plan is not None:
            pl.when(page > 0)(lambda: background(page))
        return carry

    lax.fori_loop(0, pages, prepare, 0)
    if plan is not None:
        for k in range(12):
            if k not in early:
                loads[k].wait()

    def attend(step, carry):
        page, pair = step // (heads // 2), step % (heads // 2)
        rows = aligned(page, PAGE)
        own, partner = turn_factors(trig_ref[:, rows])
        pair_lanes = aligned(pair, 2 * HD)
        query_pair = qtok_ref[rows, pair_lanes]
        dctx_pair = dctx_ref[rows, pair_lanes]
        halves = []
        boxes = []
        blank = jnp.zeros((HD, PAGE), BF16)
        for side in range(2):
            head = pair * 2 + side
            lanes = aligned(head, 2 * HD)
            key_value = kvtok_ref[rows, lanes]
            left = jnp.concatenate([kftok[rows, :], key_value], axis=1)
            score = dot(left, jnp.concatenate([qa_ref[head, :, rows], blank], axis=0))
            prob = jnp.exp(score - log_ref[head, :, rows])
            prob_low = prob.astype(BF16)
            head_rows = pl.ds(pl.multiple_of(head * HD, HD), HD)
            dctx_head = dctxt[head_rows, rows]
            grad_prob = dot(
                key_value, jnp.concatenate([blank, dctx_head], axis=0)
            )
            inner = col_sum(dctx_head.astype(F32) * ctxt_ref[head_rows, rows].astype(F32))
            grad_score = (prob * (grad_prob - inner)).astype(BF16)
            if side == 0:
                both = jnp.concatenate([query_pair[:, 0:HD], dctx_pair[:, 0:HD]], axis=1)
            else:
                both = jnp.concatenate([query_pair[:, HD:], dctx_pair[:, HD:]], axis=1)
            from_score = dot(grad_score, both)
            from_prob = dot(prob_low, both)
            grad_kv = jnp.where(lower, from_score, from_prob).astype(BF16)
            dtok[rows, pl.ds(pl.multiple_of(cols + head * 2 * HD, 2 * HD), 2 * HD)] = grad_kv
            keys = jnp.concatenate([kft_ref[:, rows], kt_ref[head_rows, rows]], axis=0)
            grad_query = dot(keys, grad_score) * HD ** (-0.5)
            feat = grad_query[0:PE]
            proj = (feat * own - swap_blocks(feat) * partner).astype(BF16)
            halves.append(grad_query[PE:] + dot(boxt[head_rows, :], proj))
            boxes.append(dot(proj, query_pair))
        gbox[:, pair_lanes] += jnp.where(lower, boxes[0], boxes[1])
        dtok[rows, pair_lanes] = jnp.concatenate(halves, axis=0).astype(BF16).T
        return carry

    def weights(chunk):
        return w_ref[chunk] if plan is None else natural(w_ref, chunk, 0)

    def spread(page):
        rows = aligned(page, PAGE)
        return sum(
            dot(dtok[rows, chunk * UNIT : (chunk + 1) * UNIT], weights(chunk), NT) for chunk in range(3)
        )

    if plan is None:
        lax.fori_loop(0, pages * (heads // 2), attend, 0)
        gbox_ref[...] = gbox[...] * HD**0.5

        def spread_page(page, carry):
            inp_ref[aligned(page, PAGE), :] = spread(page)
            return carry

        lax.fori_loop(0, pages, spread_page, 0)

        def gather(step, carry):
            lanes = aligned(step, UNIT)
            gw_ref[step] = dot(xt[...], dtok[:, lanes]).astype(BF16)
            qvsum_ref[0:1, lanes] = col_sum(dtok[:, lanes].astype(F32))
            return carry

        lax.fori_loop(0, 3, gather, 0)
        return

    def swap(index):
        rows = aligned(index, piece)
        return remote(
            inp_ref.at[rows, :], came.at[rows, :], i_sem.at[0, index], i_sem.at[1, index], place.peer["x"]
        )

    def attend_and_send(step, carry):
        attend(step, carry)
        page = step // (heads // 2)

        @pl.when(step % (heads // 2) == heads // 2 - 1)
        def _():
            value = spread(page)
            for half in range(2):
                index = 2 * page + half
                rows = aligned(index, piece)
                own = index // pages == m
                spot = aligned(index % pages, piece)
                extra = jnp.where(own, dh1_ref[spot, :].astype(F32), 0.0)
                inp_ref[rows, :] = (value[half * piece : (half + 1) * piece] + extra).astype(BF16)
                swap(index).start()

        background(step + pages)
        return carry

    lax.fori_loop(0, pages * (heads // 2), attend_and_send, 0)
    put_natural(full_b, 0, 0, gbox[...] * HD**0.5)

    def gather(step, carry):
        grad = dot(xt[...], dtok[:, aligned(step, UNIT)]).astype(BF16)
        put_natural(full_a, step, 0, grad)
        tree_a.event(step)
        tree_b.event(step)
        return carry

    lax.fori_loop(0, 3, gather, 0)

    sums = jnp.concatenate(
        [
            col_sum(dtok[:, chunk * UNIT : (chunk + 1) * UNIT].astype(F32)) for chunk in range(3)
        ],
        axis=1,
    )
    values = exact_dot(jnp.broadcast_to(sums[:, cols:], (8, 2 * cols)), pair_place(cols), NT)
    pair = jnp.concatenate([sums[:, 0:cols], values[0:1]], axis=0)
    blank = jnp.zeros_like(pair)
    pair = jnp.where(
        m == 0, jnp.concatenate([pair, blank], axis=1), jnp.concatenate([blank, pair], axis=1)
    )
    table = jnp.concatenate([vsum_ref[0:6, :], pair, vsum_ref[8:, :]], axis=0)
    mp_count, dp_count = plan
    width = table.shape[1]
    each = width // (mp_count * dp_count)
    wide_lane = lax.broadcasted_iota(jnp.int32, (VROWS, width), 1)
    for side in range(mp_count):
        parts = []
        for r in range(dp_count):
            first = (r * mp_count + side) * each
            parts.append(jnp.where((wide_lane >= first) & (wide_lane < first + each), table, 0.0))
        block = exact_dot(jnp.concatenate(parts, axis=0), pick_ref[...], NT)
        full_v[side] = block.reshape(full_v.shape[1:])
    all_v.start()

    def tail(number, carry):
        tree_a.event(number)
        tree_b.event(number)
        return carry

    lax.fori_loop(3, tree_a.events, tail, 0)
    tree_e.rest()
    all_v.wait()
    total_v = full_v[spot] + jnp.sum(land_v[...], axis=0)
    sum_v[0] = total_v * inv_tokens

    square = sum(jnp.sum(out[...] * out[...]) for out in (sum_e, sumf_ref, sum_a, sum_b, sum_v))
    norms[spot] = jnp.full((8, 128), square, F32)
    all_n.start()

    def final(number, carry):
        rows = aligned(number, piece)
        swap(number).wait()
        inp_ref[rows, :] = (inp_ref[rows, :].astype(F32) + came[rows, :].astype(F32)).astype(BF16)
        return carry

    lax.fori_loop(0, pieces, final, 0)
    all_n.wait()
    every = norms[...].reshape(-1, 8, 128)
    norm_ref[...] = jnp.sqrt(sum(every[k] for k in range(every.shape[0])))
    for tree in (tree_e, tree_a, tree_b):
        tree.drain()


def attend_backward(x, weight, box, kept, dctx, plan, inv_tokens, more=()):
    tokens, width = x.shape
    cols = weight.shape[-1]
    heads = cols // HD
    vmem = pl.BlockSpec(memory_space=pltpu.VMEM)
    scratch = [
        pltpu.VMEM((tokens, PE), BF16),
        pltpu.VMEM((cols, tokens), BF16),
        pltpu.VMEM((cols, PE), BF16),
        pltpu.VMEM((tokens, 3 * cols), BF16),
        pltpu.VMEM((width, tokens), BF16),
        pltpu.VMEM((PE, cols), F32),
    ]
    in_specs = [vmem] * 12
    if plan is None:
        shapes = [
            ((tokens, width), F32),
            ((3, width, cols), BF16),
            ((PE, cols), F32),
            ((8, 3 * cols), F32),
        ]
        extra = {}
    else:
        free = pl.BlockSpec(memory_space=pl.ANY)
        in_specs = [free] * 12 + [vmem] * 4 + [free]
        rows = width // 16
        unit = (rows, UNIT)
        tile = (PE // 16, cols)
        small = (VROWS, 128)
        shapes = [
            ((tokens, width), BF16),
            ((5, *unit), F32),
            ((3, *unit), F32),
            ((1, *tile), F32),
            ((1, *small), F32),
            ((8, 128), F32),
        ]
        scratch += [
            pltpu.VMEM((tokens, width), BF16),
            pltpu.VMEM((5, 2, 4, 2, *unit), BF16),
            pltpu.VMEM((3, 2, 1, 4, 2, *unit), BF16),
            pltpu.VMEM((1, 2, 1, 4, 2, *tile), F32),
            pltpu.VMEM((2, 4, 2, 2, *small), F32),
            pltpu.VMEM((31, *small), F32),
            pltpu.VMEM((2, 4, 2, 2, 8, 128), F32),
            pltpu.VMEM((5, 2, 4, 2, *unit), BF16),
            pltpu.VMEM((5, 2, 4, *unit), BF16),
            pltpu.VMEM((5, 3, *unit), BF16),
            pltpu.VMEM((5, 4, *unit), BF16),
            pltpu.VMEM((3, 4, 2, *unit), BF16),
            pltpu.VMEM((3, 4, *unit), BF16),
            pltpu.VMEM((3, 3, *unit), BF16),
            pltpu.VMEM((1, 4, 2, *tile), F32),
            pltpu.VMEM((1, 4, *tile), F32),
            pltpu.VMEM((1, 3, *tile), F32),
            pltpu.SemaphoreType.DMA((2, 5, SLOTS)),
            pltpu.SemaphoreType.DMA((2, 3, SLOTS)),
            pltpu.SemaphoreType.DMA((2, 1, SLOTS)),
            pltpu.SemaphoreType.DMA((2, 31)),
            pltpu.SemaphoreType.DMA((2, 31)),
            pltpu.SemaphoreType.DMA((2, 2 * (tokens // PAGE))),
            pltpu.SemaphoreType.DMA((2,)),
        ]
        scratch += [pltpu.VMEM(array.shape, array.dtype) for array in (x, weight, box, *kept, dctx)]
        scratch.append(pltpu.SemaphoreType.DMA((12,)))
        extra = dict(collective_id=2, has_side_effects=True)
    return pl.pallas_call(
        functools.partial(attend_back_kernel, heads, plan, inv_tokens),
        out_shape=[jax.ShapeDtypeStruct(s, d) for s, d in shapes],
        in_specs=in_specs,
        out_specs=[vmem] * len(shapes),
        scratch_shapes=scratch,
        compiler_params=pltpu.CompilerParams(vmem_limit_bytes=VMEM_LIMIT, **extra),
        cost_estimate=pl.CostEstimate(flops=4 * 10**10, bytes_accessed=10**8, transcendentals=10**7),
        name="attend_backward",
    )(x, weight, box, *kept, dctx, *more)


def adam_step(master, first, second, gradient, rate, decay):
    new_first = BETA_ONE * first + (1.0 - BETA_ONE) * gradient
    new_second = BETA_TWO * second + (1.0 - BETA_TWO) * gradient * gradient
    first_hat = new_first / (1.0 - BETA_ONE**STEP)
    second_hat = new_second / (1.0 - BETA_TWO**STEP)
    new_master = master - rate * (first_hat / (jnp.sqrt(second_hat) + ADAM_EPS) + decay * master)
    return (new_first, new_second, new_master)


def adam_kernel(heads, norm_ref, *refs):
    sum_e, sum_f, sum_a, sum_b, sum_v, *refs = refs
    states, outs = refs[:18], refs[18:]
    outs[-1][...] = norm_ref[0:1, 0:1]
    clip = CLIP_LIMIT / jnp.maximum(norm_ref[0:1, 0:1], CLIP_LIMIT)

    def update(first, out, gradient, at, rate, decay):
        news = adam_step(*(ref[at] for ref in states[first : first + 3]), gradient * clip, rate, decay)
        for ref, new in zip(outs[out : out + 3], news):
            ref[at] = new
        if decay:
            outs[out + 3][at] = news[2].astype(BF16)

    def heads_of(kind):
        half = heads // 2
        return jnp.concatenate(
            [
                sum_a[1 + head // half, :, (2 * (head % half) + kind) * HD : (2 * (head % half) + kind + 1) * HD]
                for head in range(heads)
            ],
            axis=1,
        )

    for index, gradient in enumerate((sum_a[0], heads_of(0), heads_of(1))):
        update(0, 0, gradient, index, RATE_MATRIX, WEIGHT_DECAY)
    update(3, 4, sum_b[0], ALL, RATE_MATRIX, WEIGHT_DECAY)
    update(6, 8, sum_e[0], ALL, RATE_MATRIX, WEIGHT_DECAY)
    for chunk in range(4):
        lanes = (ALL, slice(chunk * UNIT, (chunk + 1) * UNIT))
        update(9, 12, sum_e[1 + chunk], lanes, RATE_MATRIX, WEIGHT_DECAY)
        update(12, 16, sum_f[chunk], lanes, RATE_MATRIX, WEIGHT_DECAY)
    rows, each = states[15].shape
    update(15, 20, sum_v[0, 0:rows, 0:each], ALL, RATE_VECTOR, 0.0)


def adam_all(norm, sums, states):
    shapes = []
    for first in range(0, 18, 3):
        shapes += [(states[first].shape, F32)] * 3
        if first < 15:
            shapes.append((states[first].shape, BF16))
    vmem = pl.BlockSpec(memory_space=pltpu.VMEM)
    shapes.append(((1, 1), F32))
    return pl.pallas_call(
        functools.partial(adam_kernel, states[0].shape[2] // HD),
        out_shape=[jax.ShapeDtypeStruct(s, d) for s, d in shapes],
        in_specs=[vmem] * (6 + len(states)),
        out_specs=[vmem] * len(shapes),
        compiler_params=pltpu.CompilerParams(vmem_limit_bytes=VMEM_LIMIT),
        name="adam_all",
    )(norm, *sums, *states)


def pack_qkv(shard):
    rows, cols = shard.shape[1:]
    heads = cols // HD
    pairs = jnp.stack([shard[1].reshape(rows, heads, HD), shard[2].reshape(rows, heads, HD)], axis=2)
    pairs = pairs.reshape(rows, 2, cols)
    return jnp.stack([shard[0], pairs[:, 0], pairs[:, 1]])


def unpack_qkv(packed):
    rows, cols = packed.shape[1:]
    pairs = jnp.concatenate([packed[1], packed[2]], axis=1).reshape(rows, cols // HD, 2, HD)
    return jnp.stack(
        [packed[0], pairs[:, :, 0].reshape(rows, cols), pairs[:, :, 1].reshape(rows, cols)]
    )


def to_chunks(shard):
    rows = shard.shape[0]
    return shard.reshape(rows, -1, UNIT).transpose(1, 0, 2)


def from_chunks(chunks):
    return chunks.transpose(1, 0, 2).reshape(chunks.shape[1], -1)


def on_device(
    layer_input,
    page_boxes,
    output_grad,
    attn_proj,
    attn_first,
    attn_second,
    box_proj,
    box_first,
    box_second,
    merge_proj,
    merge_first,
    merge_second,
    expand_proj,
    expand_first,
    expand_second,
    shrink_proj,
    shrink_first,
    shrink_second,
    vectors,
    vector_first,
    vector_second,
):
    mp_count = lax.axis_size("mp")
    dp_count = lax.axis_size("dp")
    mp_index = lax.axis_index("mp")
    tokens, width = layer_input.shape
    cols = attn_proj.shape[2]
    heads = cols // HD
    own_tokens = tokens // mp_count
    inv_tokens = 1.0 / (tokens * dp_count)

    corners = page_boxes.T
    omega = (10000.0 ** (-np.arange(FREQS, dtype=np.float64) / FREQS)).astype(np.float32)[:, None]
    omega = jnp.asarray(omega)
    plan = (mp_count, dp_count) if dp_count == 16 and mp_count == 2 else None
    if plan is not None:
        each = vectors.shape[1]
        pick = np.zeros((128, width), np.float32)
        pick[np.arange(width) % each, np.arange(width)] = 1.0
        pick = jnp.asarray(pick)
        *kept, w_qkv, w_box, layer_out, dctx, dh1, g_expand, vec_sum, sum_f = layer_forward(
            layer_input,
            output_grad,
            corners,
            omega,
            pick,
            (attn_proj, box_proj, vectors, merge_proj.T, expand_proj, shrink_proj.T),
            plan,
            inv_tokens,
        )
        input_grad, sum_e, sum_a, sum_b, sum_v, norm = attend_backward(
            layer_input,
            w_qkv,
            w_box,
            kept,
            dctx,
            plan,
            inv_tokens,
            (dh1, vec_sum, sum_f, pick, g_expand),
        )
        merge = [merge_proj.T, merge_first.T, merge_second.T]
        shrink = [shrink_proj.T, shrink_first.T, shrink_second.T]
        *results, norm = adam_all(
            norm,
            (sum_e, sum_f, sum_a, sum_b, sum_v),
            [attn_proj, attn_first, attn_second, box_proj, box_first, box_second, *merge]
            + [expand_proj, expand_first, expand_second, *shrink, vectors, vector_first, vector_second],
        )
        turned = (8, 9, 10, 11, 16, 17, 18, 19)
        results = [out.T if k in turned else out for k, out in enumerate(results)]
        return (layer_out, input_grad, norm.reshape(()), *results)
    shard_qkv = pack_qkv(attn_proj).astype(BF16)
    shard_e = jnp.concatenate([merge_proj.T[None], to_chunks(expand_proj)]).astype(BF16)
    shard_f = to_chunks(shrink_proj.T).astype(BF16)
    w_qkv = lax.all_gather(shard_qkv, "dp", axis=1, tiled=True)
    w_box = lax.all_gather(box_proj.astype(BF16), "dp", axis=0, tiled=True)
    w_expand = lax.all_gather(lax.all_gather(shard_e, "dp", axis=1, tiled=True), "mp", axis=1)
    w_shrink = lax.all_gather(lax.all_gather(shard_f, "dp", axis=1, tiled=True), "mp", axis=1)
    vecs = lax.all_gather(vectors, ("dp", "mp"), axis=1, tiled=True)
    vecs = jnp.pad(vecs, ((0, VROWS - vecs.shape[0]), (0, 0)))
    *kept, context = attend_forward(layer_input, corners, omega, w_qkv, w_box, vecs)
    context = lax.all_to_all(
        context.reshape(mp_count, own_tokens, cols), "mp", split_axis=0, concat_axis=0
    )

    def own_rows(array):
        return lax.dynamic_slice_in_dim(array, mp_index * own_tokens, own_tokens)

    layer_out, dctx, dh1, g_expand, g_shrink, vec_sum = feed_both(
        own_rows(layer_input), own_rows(output_grad), context, w_expand, w_shrink, vecs
    )
    g_feed = jnp.concatenate([g_expand, g_shrink])
    layer_out = lax.all_gather(layer_out, "mp", axis=0, tiled=True)
    dctx = lax.all_to_all(dctx, "mp", split_axis=0, concat_axis=0).reshape(tokens, cols)
    part, g_qkv, g_box, qkv_sum = attend_backward(
        layer_input, w_qkv, w_box, kept, dctx, None, inv_tokens
    )
    own_part = lax.psum_scatter(part.astype(BF16), "mp", scatter_dimension=0, tiled=True)
    own_grad = (own_part.astype(F32) + dh1).astype(BF16)
    input_grad = lax.all_gather(own_grad, "mp", axis=0, tiled=True)
    shard_attn = unpack_qkv(
        lax.psum_scatter(g_qkv, "dp", scatter_dimension=1, tiled=True).astype(F32) * inv_tokens
    )
    shard_box = lax.psum_scatter(g_box, "dp", scatter_dimension=0, tiled=True) * inv_tokens
    sum_feed = lax.psum_scatter(g_feed, "dp", scatter_dimension=2, tiled=True)
    sum_feed = lax.psum_scatter(sum_feed, "mp", scatter_dimension=1, tiled=True)[:, 0]
    sum_feed = sum_feed.astype(F32) * inv_tokens
    sum_expand, sum_shrink = sum_feed[0:5], sum_feed[5:]

    def placed(row):
        return lax.dynamic_update_slice_in_dim(
            jnp.zeros((width,), F32), row, mp_index * cols, 0
        )[None, :]

    value_sum = qkv_sum[0, cols:].reshape(heads, 2, HD)[:, 1].reshape(cols)
    vector_grad = jnp.concatenate(
        [vec_sum[0:6], placed(qkv_sum[0, 0:cols]), placed(value_sum), vec_sum[8:12]]
    )
    vector_shard = (
        lax.psum_scatter(vector_grad, ("dp", "mp"), scatter_dimension=1, tiled=True) * inv_tokens
    )
    square = sum(
        jnp.sum(shard * shard)
        for shard in (shard_attn, shard_box, sum_expand, sum_shrink, vector_shard)
    )
    grad_norm = jnp.sqrt(lax.psum(square, ("dp", "mp")))
    shard_merge = sum_expand[0].T
    shard_expand = from_chunks(sum_expand[1:])
    shard_shrink = from_chunks(sum_shrink).T
    clip_scale = CLIP_LIMIT / jnp.maximum(grad_norm, CLIP_LIMIT)
    results = [layer_out, input_grad, grad_norm]
    for master, first, second, shard in (
        (attn_proj, attn_first, attn_second, shard_attn),
        (box_proj, box_first, box_second, shard_box),
        (merge_proj, merge_first, merge_second, shard_merge),
        (expand_proj, expand_first, expand_second, shard_expand),
        (shrink_proj, shrink_first, shrink_second, shard_shrink),
    ):
        new_first, new_second, new_master = adam_step(
            master, first, second, shard * clip_scale, RATE_MATRIX, WEIGHT_DECAY
        )
        results += [new_first, new_second, new_master, new_master.astype(BF16)]
    results += adam_step(
        vectors, vector_first, vector_second, vector_shard * clip_scale, RATE_VECTOR, 0.0
    )
    return tuple(results)


def solution(mesh):
    rows = P("dp", None)
    attn = P(None, "dp", "mp")
    tall = P("dp", "mp")
    wide = P("mp", "dp")
    vector = P(None, ("dp", "mp"))
    in_specs = (rows,) * 3 + (attn,) * 3 + (tall,) * 3 + (wide,) * 3 + (tall,) * 3 + (wide,) * 3
    in_specs += (vector,) * 3
    out_specs = (rows, rows, P()) + (attn,) * 4 + (tall,) * 4 + (wide,) * 4 + (tall,) * 4
    out_specs += (wide,) * 4 + (vector,) * 3
    return jax.shard_map(
        on_device, mesh=mesh, in_specs=in_specs, out_specs=out_specs, check_vma=False
    )
```

```python
import functools
import types

import jax
import jax.numpy as jnp
import numpy as np
from jax import lax
from jax.experimental import pallas as pl
from jax.experimental.pallas import tpu as pltpu
from jax.sharding import PartitionSpec as P

HD = 64
FREQS = 32
PE = 128
PAGE = 512
STEP = 10

NORM_EPS = 1e-12
CLIP_LIMIT = 0.1
BETA_ONE = 0.9
BETA_TWO = 0.999
ADAM_EPS = 1e-08
RATE_MATRIX = 0.05
RATE_VECTOR = 0.5
WEIGHT_DECAY = 0.01

F32 = jnp.float32
BF16 = jnp.bfloat16
VMEM_LIMIT = 60 * 1024 * 1024

NN = (((1,), (0,)), ((), ()))
NT = (((1,), (1,)), ((), ()))
TN = (((0,), (0,)), ((), ()))


def dot(lhs, rhs, dims=NN):
    return lax.dot_general(lhs, rhs, dims, preferred_element_type=F32)


def aligned(index, size):
    return pl.ds(pl.multiple_of(index * size, size), size)


def swap_blocks(feat):
    return jnp.concatenate(
        [
            feat[FREQS : 2 * FREQS],
            feat[0:FREQS],
            feat[3 * FREQS :],
            feat[2 * FREQS : 3 * FREQS],
        ],
        axis=0,
    )


def turn_factors(trig):
    cos_x, sin_x = trig[0:FREQS], trig[FREQS : 2 * FREQS]
    cos_y, sin_y = trig[2 * FREQS : 3 * FREQS], trig[3 * FREQS :]
    return (
        jnp.concatenate([sin_x, sin_x, sin_y, sin_y], axis=0),
        jnp.concatenate([cos_x, -cos_x, cos_y, -cos_y], axis=0),
    )


MESH = pl.DeviceIdType.MESH
ALL = slice(None)
UNIT = 384


class Place:
    def __init__(self):
        rank = lax.axis_index("dp")
        self.m = lax.axis_index("mp")
        self.z = rank // 4
        self.y = (rank // 2) % 2
        self.c = rank % 2
        self.peer = {
            "x": (rank, 1 - self.m),
            "y": (rank + 2 - 4 * self.y, self.m),
            "c": (rank + 1 - 2 * self.c, self.m),
        }
        self.far = [((rank + 4 * step) % 16, self.m) for step in (1, 2, 3)]

    def signal(self):
        barrier = pltpu.get_barrier_semaphore()
        for device in list(self.peer.values()) + self.far:
            pl.semaphore_signal(barrier, inc=1, device_id=device, device_id_type=MESH)

    def wait(self):
        pl.semaphore_wait(pltpu.get_barrier_semaphore(), 6)

    def signal_all(self):
        barrier = pltpu.get_barrier_semaphore()
        rank = self.m * 16 + lax.axis_index("dp")

        def one(step, carry):
            to = (rank + step) % 32
            pl.semaphore_signal(barrier, inc=1, device_id=(to % 16, to // 16), device_id_type=MESH)
            return carry

        lax.fori_loop(1, 32, one, 0)

    def wait_all(self):
        pl.semaphore_wait(pltpu.get_barrier_semaphore(), 31)


PART = 64


def start_rows(src, dst, rows, send_sem, recv_sem, device):
    for first in range(0, rows, PART):
        part = pl.ds(first, PART)
        remote(src.at[part, :], dst.at[part, :], send_sem, recv_sem, device).start()


def remote(src, dst, send_sem, recv_sem, device):
    return pltpu.make_async_remote_copy(
        src_ref=src,
        dst_ref=dst,
        send_sem=send_sem,
        recv_sem=recv_sem,
        device_id=device,
        device_id_type=MESH,
    )


SLOT = {"c": 0, "z": 1, "y": 4, "x": 5}
SLOTS = 6
SENT = (0, 1, 1, 1, 4, 5)


def cut(have):
    blocks = [have]
    for axis, size in (("x", 2), ("z", 4), ("y", 2)):
        if have[axis] == ALL:
            blocks = [dict(block, **{axis: spot}) for block in blocks for spot in range(size)]
    return blocks


class Tree:
    lag = 1
    held_back = 0
    together = False

    def stage(self, index, chunk):
        raise NotImplementedError

    def event(self, number):
        for index in range(self.count - 1 - self.held_back, -1, -1):
            chunk = number - index * self.lag
            if self.together:

                @pl.when(chunk == 0)
                def _(index=index):
                    for each in range(self.chunks):
                        self.stage(index, each)

            elif self.chunks == 1:
                pl.when(chunk == 0)(lambda index=index: self.stage(index, 0))
            else:
                pl.when((chunk >= 0) & (chunk < self.chunks))(
                    lambda index=index, chunk=chunk: self.stage(index, chunk)
                )

    @property
    def events(self):
        return self.chunks + (self.count - 1 - self.held_back) * self.lag

    def rest(self):
        def one(chunk, carry):
            self.stage(self.count - 1, chunk)
            return carry

        lax.fori_loop(0, self.chunks, one, 0)


class Spread(Tree):
    def __init__(self, place, ref, chunks, order, sems):
        self.chunks, self.ref, self.sems, self.place = chunks, ref, sems, place
        have = {"x": place.m if "x" in order else 0, "z": place.z, "y": place.y}
        mine = {"x": place.m, "y": place.y}
        self.own = have
        self.steps, self.axes = [], order
        for axis in order:
            if axis == "z":
                sends = [(have, place.far[step - 1], step) for step in (1, 2, 3)]
                waits = [(dict(have, z=(place.z + 4 - step) % 4), step) for step in (1, 2, 3)]
            else:
                sends = [(have, place.peer[axis], SLOT[axis])]
                waits = [(dict(have, **{axis: 1 - mine[axis]}), SLOT[axis])]
            self.steps.append((sends, waits))
            have = dict(have, **{axis: ALL})
        self.other = place.peer["c"]
        self.count = len(self.steps) + 2

    def _copy(self, chunk, have, device, slot):
        came = 0 if chunk == ALL else chunk
        block = self.ref.at[chunk, self.place.c, have["x"], have["z"], have["y"]]
        sent = self.sems.at[0, 0, SENT[slot]]
        return remote(block, block, sent, self.sems.at[1, came, slot], device)

    def _plane(self, chunk, core):
        plane = self.ref.at[chunk, core]
        came = 0 if chunk == ALL else chunk
        return remote(plane, plane, self.sems.at[0, 0, 0], self.sems.at[1, came, 0], self.other)

    def stage(self, index, chunk):
        if index == self.count - 1:
            self._plane(chunk, 1 - self.place.c).wait_recv()
            return
        came = [self.own]
        if index > 0:
            came = []
            for have, slot in self.steps[index - 1][1]:
                self._copy(chunk, have, self.other, slot).wait_recv()
                came.append(have)
        if index < len(self.steps):
            for whole, device, slot in self.steps[index][0]:
                for have in cut(whole):
                    self._copy(chunk, have, device, slot).start()
        for whole in came:
            for have in cut(whole):
                self._copy(chunk, have, self.other, 0).start()

    def drain(self):
        for axis, (sends, _) in zip(self.axes, self.steps):
            have, _, slot = sends[0]
            if axis == "z":
                have = dict(have, z=slice(0, 3))
            self._copy(ALL, have, self.other, slot).wait_send()
        self._plane(ALL, self.place.c).wait_send()


RANKS = [(c, z, y) for z in range(4) for y in range(2) for c in range(2)]


def natural(ref, chunk, side):
    return jnp.concatenate([ref[chunk, c, side, z, y] for c, z, y in RANKS], axis=0)


def put_natural(ref, chunk, side, value):
    rows = value.shape[0] // len(RANKS)
    for spot, (c, z, y) in enumerate(RANKS):
        ref[chunk, c, side, z, y] = value[spot * rows : (spot + 1) * rows]


class Reduce(Tree):
    def __init__(self, place, full, total, lands, chunks, order, sems, finish):
        self.place, self.full, self.total, self.lands = place, full, total, lands
        self.chunks, self.sems, self.finish = chunks, sems, finish
        mine = {"x": place.m, "y": place.y}
        self.across = ALL if "x" in order else 0
        have = {"x": self.across, "z": ALL, "y": ALL}
        self.order, self.haves = order, []
        for axis in order:
            before = have
            if axis != "c":
                have = dict(have, **{axis: place.z if axis == "z" else mine[axis]})
            self.haves.append((before, have))
        self.count = len(order) + 1

    def _at(self, chunk, have):
        if self.total is None:
            return self.full.at[chunk, self.place.c, have["x"], have["z"], have["y"]]
        return self.total.at[chunk, have["x"], have["z"], have["y"]]

    def _copies(self, index, chunk, blocks=False):
        axis, (before, _) = self.order[index], self.haves[index]
        place, land = self.place, self.lands[axis]

        def copy(src, dst, slot, device):
            return remote(src, dst, self.sems.at[0, 0, SENT[slot]], self.sems.at[1, chunk, slot], device)

        def copies(have, spot, axes, slot, device):
            made = []
            for block in cut({**have, "y": 0 if axis == "c" else have["y"]}) if blocks else [have]:
                if axis == "c" and blocks:
                    block = dict(block, y=ALL)
                at = [block[name] for name in axes if have[name] == ALL and block[name] != ALL]
                if axis == "c":
                    src = self.full.at[chunk, 1 - place.c, block["x"], block["z"], block["y"]]
                else:
                    src = self._at(chunk, block)
                made.append(copy(src, land.at[(chunk, *spot, *at)], slot, device))
            return made

        if axis == "c":
            return copies(before, (), "xz", SLOT[axis], place.peer[axis])
        if axis == "z":
            return [
                one
                for step in (1, 2, 3)
                for one in copies(
                    dict(before, z=(place.z + step) % 4), (step - 1,), "xy", step, place.far[step - 1]
                )
            ]
        other = 1 - (place.m if axis == "x" else place.y)
        return copies(dict(before, **{axis: other}), (), "xzy", SLOT[axis], place.peer[axis])

    def stage(self, index, chunk):
        if index > 0:
            axis, (_, have) = self.order[index - 1], self.haves[index - 1]
            land = self.lands[axis]
            for copy in self._copies(index - 1, chunk):
                copy.wait_recv()
            mine = self._at(chunk, have)
            last = index == self.count - 1
            if axis == "z":
                value = mine[...].astype(F32)
                for step in range(3):
                    value += land[chunk, step].astype(F32)
            elif last:
                value = mine[...].astype(F32) + land[chunk].astype(F32)
            else:
                value = mine[...] + land[chunk]
            if last:
                self.finish(chunk, value)
            else:
                mine[...] = value.astype(mine.dtype)
        if index < self.count - 1:
            for copy in self._copies(index, chunk, True):
                copy.start()

    def drain(self):
        for axis in self.order:
            land = self.lands[axis]
            slot = SLOT[axis]
            sent = self.sems.at[0, 0, SENT[slot]]
            remote(land, land, sent, self.sems.at[1, 0, slot], self.place.peer["c"]).wait_send()


class Everyone:
    def __init__(self, place, send_block, land_block, sems):
        self.rank = place.m * 16 + lax.axis_index("dp")
        self.send_block, self.land_block, self.sems = send_block, land_block, sems

    def _copy(self, step):
        to = (self.rank + step) % 32
        return remote(
            self.send_block(to),
            self.land_block(step),
            self.sems.at[0, step - 1],
            self.sems.at[1, step - 1],
            (to % 16, to // 16),
        )

    def _each(self, act):
        def one(step, carry):
            act(self._copy(step))
            return carry

        lax.fori_loop(1, 32, one, 0)

    def start(self):
        self._each(lambda copy: copy.start())

    def wait(self):
        self._each(lambda copy: copy.wait())


VROWS = 16


def rows_from_blocks(blocks, pick, counts):
    mp_count, dp_count = counts
    width = pick.shape[1]
    each = width // (mp_count * dp_count)
    wide = lax.dot_general(
        blocks, pick, NN, precision=lax.Precision.HIGHEST, preferred_element_type=F32
    )
    lane = lax.broadcasted_iota(jnp.int32, (VROWS, width), 1)
    table = jnp.zeros((VROWS, width), F32)
    for m in range(mp_count):
        for r, (c, z, y) in enumerate(RANKS):
            first = (r * mp_count + m) * each
            row = (((c * mp_count + m) * 4 + z) * 2 + y) * VROWS
            table += jnp.where((lane >= first) & (lane < first + each), wide[row : row + VROWS], 0.0)
    return table


def attend_setup(heads, m, box_full, vec_ref, box_heads, bias):
    cols = heads * HD
    for head in range(heads):
        box_heads[head] = box_full[:, head * HD : (head + 1) * HD]
    width = vec_ref.shape[1]
    own = jnp.where(m == 0, vec_ref[6:8, 0:cols], vec_ref[6:8, width - cols :])
    spread = exact_dot(jnp.broadcast_to(own[1:2], (8, cols)), pair_place(cols))
    bias[0:1, 0:cols] = own[0:1]
    bias[0:1, cols:] = spread[0:1]


def attend_trig(omega_ref, corner_ref, trig_ref):
    corner = corner_ref[...].astype(F32)
    angle_x = omega_ref[...] * ((corner[0:1] + corner[2:3]) * 0.5)
    angle_y = omega_ref[...] * ((corner[1:2] + corner[3:4]) * 0.5)
    trig_ref[0:FREQS, :] = jnp.cos(angle_x)
    trig_ref[FREQS : 2 * FREQS, :] = jnp.sin(angle_x)
    trig_ref[2 * FREQS : 3 * FREQS, :] = jnp.cos(angle_y)
    trig_ref[3 * FREQS :, :] = jnp.sin(angle_y)


def quiet(*args):
    return None


def attend_math(heads, r, weights, page_of, projected, attended):
    cols = heads * HD
    pages = r.x.shape[0] // PAGE

    def project(page, carry):
        rows = aligned(page, PAGE)
        tokens = r.x[rows, :]
        query = dot(tokens, weights(0)) + r.bias[0:1, 0:cols]
        query = query.astype(BF16) * HD ** (-0.5)
        r.qtok[rows, :] = query
        qa_rows = query.T
        for half in range(2):
            lanes = slice(half * cols, (half + 1) * cols)
            pair = dot(tokens, weights(1 + half)) + r.bias[0:1, cols + half * cols : 2 * cols + half * cols]
            pair = pair.astype(BF16)
            r.kvtok[rows, lanes] = pair
            turned = pair.T
            for spot in range(heads // 2):
                head_rows = slice((half * heads // 2 + spot) * HD, (half * heads // 2 + spot + 1) * HD)
                r.kt[head_rows, rows] = turned[2 * spot * HD : (2 * spot + 1) * HD]
                r.vt[head_rows, rows] = turned[(2 * spot + 1) * HD : (2 * spot + 2) * HD]
        trig = r.trig[:, rows]
        kft = trig.astype(BF16)
        r.kft[:, rows] = kft
        r.kftok[rows, :] = kft.T
        own, partner = turn_factors(trig)
        for head in range(heads):
            query_head = qa_rows[head * HD : (head + 1) * HD]
            proj = dot(r.box_heads[head], query_head)
            feat = proj * own + swap_blocks(proj) * partner
            r.qa[head, 0:PE, rows] = feat.astype(BF16)
            r.qa[head, PE : PE + HD, rows] = query_head
        projected(page)
        return carry

    lax.fori_loop(0, pages, project, 0)

    def attend(step, carry):
        turn, pair = step // (heads // 2), step % (heads // 2)
        rows = aligned(page_of(turn), PAGE)
        halves = []
        blank = jnp.zeros((HD, PAGE), BF16)
        for side in range(2):
            head = pair * 2 + side
            lanes = aligned(head, 2 * HD)
            left = jnp.concatenate([r.kftok[rows, :], r.kvtok[rows, lanes]], axis=1)
            score = dot(left, jnp.concatenate([r.qa[head, :, rows], blank], axis=0))
            top = jnp.max(score, axis=0, keepdims=True)
            weight = jnp.exp(score - top)
            total = jnp.sum(weight, axis=0, keepdims=True)
            value = r.vt[aligned(head, HD), rows]
            halves.append(dot(value, weight.astype(BF16)) * (1.0 / total))
            r.log[head, :, rows] = top + jnp.log(total)
        both = jnp.concatenate(halves, axis=0).astype(BF16)
        lanes = aligned(pair, 2 * HD)
        r.ctxt[lanes, rows] = both
        r.ctx[rows, lanes] = both.T
        attended(step, turn, pair)
        return carry

    lax.fori_loop(0, pages * (heads // 2), attend, 0)


def attend_buffers(heads, tokens):
    cols = heads * HD
    kept = [
        ("qa", (heads, PE + HD, tokens), BF16),
        ("qtok", (tokens, cols), BF16),
        ("kvtok", (tokens, 2 * cols), BF16),
        ("kt", (cols, tokens), BF16),
        ("kft", (PE, tokens), BF16),
        ("trig", (PE, tokens), F32),
        ("ctxt", (cols, tokens), BF16),
        ("log", (heads, 1, tokens), F32),
    ]
    used = [
        ("kftok", (tokens, PE), BF16),
        ("box_heads", (heads, PE, HD), BF16),
        ("bias", (8, 3 * cols), F32),
        ("ctx", (tokens, cols), BF16),
        ("vt", (cols, tokens), BF16),
    ]
    return kept, used


def attend_kernel(heads, names, *refs):
    r = types.SimpleNamespace(**dict(zip(names, refs)))
    attend_setup(heads, lax.axis_index("mp"), r.box, r.vec, r.box_heads, r.bias)
    attend_trig(r.omega, r.corner, r.trig)
    attend_math(heads, r, lambda chunk: r.w[chunk], lambda turn: turn, quiet, quiet)


def attend_forward(x, corners, omega, w_qkv, w_box, vecs):
    tokens = x.shape[0]
    heads = w_box.shape[1] // HD
    kept, used = attend_buffers(heads, tokens)
    outs = kept + [used[3]]
    scratch = used[:3] + used[4:]
    names = ["x", "corner", "omega", "w", "box", "vec"] + [item[0] for item in outs + scratch]
    vmem = pl.BlockSpec(memory_space=pltpu.VMEM)
    return pl.pallas_call(
        functools.partial(attend_kernel, heads, names),
        out_shape=[jax.ShapeDtypeStruct(shape, kind) for _, shape, kind in outs],
        in_specs=[vmem] * 6,
        out_specs=[vmem] * len(outs),
        scratch_shapes=[pltpu.VMEM(shape, kind) for _, shape, kind in scratch],
        compiler_params=pltpu.CompilerParams(vmem_limit_bytes=VMEM_LIMIT),
        name="attend_forward",
    )(x, corners, omega, w_qkv, w_box, vecs)


TILE = 256


def normal_parts(value):
    phi = 0.5 + 0.5 * lax.erf(value * 2.0 ** (-0.5))
    return phi, phi + value * (jnp.exp(value * value * -0.5) * (0.5 / np.pi) ** 0.5)


def norm_stats(value):
    mean = jnp.mean(value, axis=-1, keepdims=True)
    centred = value - mean
    var = jnp.mean(centred * centred, axis=-1, keepdims=True)
    return centred, lax.rsqrt(var + NORM_EPS)


def norm_back(grad_normed, normed, scale):
    first = jnp.mean(grad_normed, axis=-1, keepdims=True)
    second = jnp.mean(grad_normed * normed, axis=-1, keepdims=True)
    return scale * (grad_normed - first - normed * second)


def col_sum(value):
    return jnp.sum(value, axis=0, keepdims=True)


def feed_math(r, hooks):
    hook = {name: quiet for name in ("entered", "grew", "turned", "shrinks", "shrank", "left")}
    hook.update(hooks)
    tokens = r.x.shape[0]
    sides = r.ctxx.shape[0]
    steps = r.ws.shape[0]
    tiles = tokens // TILE
    wide = sides * UNIT
    sum2 = dnorm = r.sum2

    def flat(ref, chunk, side):
        return ref[chunk, side] if len(ref.shape) == 4 else natural(ref, chunk, side)

    def put(ref, chunk, side, value):
        if len(ref.shape) == 4:
            ref[chunk, side] = value
        else:
            put_natural(ref, chunk, side, value)

    def both(ref, chunk):
        return jnp.concatenate([flat(ref, chunk, side) for side in range(sides)], axis=1)

    def put_both(ref, chunk, value):
        for side in range(sides):
            put(ref, chunk, side, value[:, side * UNIT : (side + 1) * UNIT])

    def bias_at(step, side):
        first = side * steps + step
        return (pl.ds(8 + first // 2, 1), aligned(first % 2, UNIT))

    def enter(tile, carry):
        rows = aligned(tile, TILE)
        total = r.x[rows, :].astype(F32) + r.vec[4:5, :]
        for side in range(sides):
            total += dot(r.ctxx[side, rows, :], flat(r.we, 0, side), NT)
        centred, scale = norm_stats(total)
        normed = centred * scale
        r.norm1[rows, :] = normed
        r.scale1[rows, :] = scale
        shifted = normed * r.vec[0:1, :] + r.vec[1:2, :]
        r.al[rows, :] = shifted.astype(BF16)
        sum2[rows, :] = shifted + r.vec[5:6, :]
        return carry

    lax.fori_loop(0, tiles, enter, 0)
    hook["entered"]()

    def grow(step, carry):
        whole = aligned(step, wide)
        bias = jnp.concatenate([r.vec[bias_at(step, side)] for side in range(sides)], axis=1)

        def one(tile, inner):
            rows = aligned(tile, TILE)
            pre = dot(r.al[rows, :], both(r.we, 1 + step)) + bias
            phi, slope = normal_parts(pre)
            low = (pre * phi).astype(BF16)
            r.act[rows, whole] = low
            r.slope[rows, whole] = slope.astype(BF16)
            sum2[rows, :] += dot(low, both(r.ws, step), NT)
            hook["grew"](step * tiles + tile)
            return inner

        lax.fori_loop(0, tiles, one, 0)
        return carry

    lax.fori_loop(0, steps, grow, 0)
    r.vsum[...] = jnp.zeros_like(r.vsum)

    def turn(tile, carry):
        rows = aligned(tile, TILE)
        centred, scale = norm_stats(sum2[rows, :])
        normed = centred * scale
        r.out[rows, :] = (normed * r.vec[2:3, :] + r.vec[3:4, :]).astype(BF16)
        grad = r.og[rows, :].astype(F32)
        r.vsum[2:3, :] += col_sum(grad * normed)
        r.vsum[3:4, :] += col_sum(grad)
        back = norm_back(grad * r.vec[2:3, :], normed, scale)
        r.vsum[5:6, :] += col_sum(back)
        r.dh2l[rows, :] = back.astype(BF16)
        dnorm[rows, :] = back
        hook["turned"](tile)
        return carry

    lax.fori_loop(0, tiles, turn, 0)
    r.flip[...] = r.dh2l[...].T

    def grad_shrink(step, carry):
        grad = dot(r.flip[...], r.act[:, aligned(step, wide)]).astype(BF16)
        put_both(r.gs, step, grad)
        hook["shrinks"](step)
        return carry

    lax.fori_loop(0, steps, grad_shrink, 0)

    def shrink(step, carry):
        whole = aligned(step, wide)

        def one(tile, inner):
            rows = aligned(tile, TILE)
            grad = dot(r.dh2l[rows, :], both(r.ws, step))
            low = (grad * r.slope[rows, whole].astype(F32)).astype(BF16)
            r.slope[rows, whole] = low
            sums = col_sum(low.astype(F32))
            for side in range(sides):
                r.vsum[bias_at(step, side)] += sums[:, side * UNIT : (side + 1) * UNIT]
            dnorm[rows, :] += dot(low, both(r.we, 1 + step), NT)
            hook["shrank"](step * tiles + tile)
            return inner

        lax.fori_loop(0, tiles, one, 0)
        return carry

    lax.fori_loop(0, steps, shrink, 0)

    def leave(tile, carry):
        rows = aligned(tile, TILE)
        grad = dnorm[rows, :]
        normed = r.norm1[rows, :]
        r.vsum[0:1, :] += col_sum(grad * normed)
        r.vsum[1:2, :] += col_sum(grad)
        back = norm_back(grad * r.vec[0:1, :], normed, r.scale1[rows, :])
        r.vsum[4:5, :] += col_sum(back)
        low = back.astype(BF16)
        r.dh1l[rows, :] = low
        for side in range(sides):
            r.dctx[side, rows, :] = dot(low, flat(r.we, 0, side)).astype(BF16)
        hook["left"](tile)
        return carry

    lax.fori_loop(0, tiles, leave, 0)
    r.flip[...] = r.al[...].T

    def grad_expand(step, carry):
        grad = dot(r.flip[...], r.slope[:, aligned(step, wide)]).astype(BF16)
        put_both(r.ge, 1 + step, grad)
        return carry

    lax.fori_loop(0, steps, grad_expand, 0)
    r.flip[...] = r.dh1l[...].T
    for side in range(sides):
        put(r.ge, 0, side, dot(r.flip[...], r.ctxx[side]).astype(BF16))


def feed_buffers(tokens, width, hidden):
    return [
        ("norm1", (tokens, width), F32),
        ("scale1", (tokens, 1), F32),
        ("sum2", (tokens, width), F32),
        ("al", (tokens, width), BF16),
        ("act", (tokens, hidden), BF16),
        ("slope", (tokens, hidden), BF16),
        ("dh2l", (tokens, width), BF16),
        ("flip", (width, tokens), BF16),
    ]


def feed_kernel(names, *refs):
    feed_math(types.SimpleNamespace(**dict(zip(names, refs))), {})


def feed_both(x, og, ctx, w_expand, w_shrink, vecs):
    tokens, width = x.shape
    chunks, sides = w_shrink.shape[0:2]
    outs = [
        ("out", (tokens, width), BF16),
        ("dctx", (sides, tokens, UNIT), BF16),
        ("dh1l", (tokens, width), BF16),
        ("ge", (chunks + 1, sides, width, UNIT), BF16),
        ("gs", (chunks, sides, width, UNIT), BF16),
        ("vsum", (VROWS, width), F32),
    ]
    scratch = feed_buffers(tokens, width, sides * chunks * UNIT)
    names = ["x", "og", "ctxx", "we", "ws", "vec"] + [item[0] for item in outs + scratch]
    vmem = pl.BlockSpec(memory_space=pltpu.VMEM)
    return pl.pallas_call(
        functools.partial(feed_kernel, names),
        out_shape=[jax.ShapeDtypeStruct(shape, kind) for _, shape, kind in outs],
        in_specs=[vmem] * 6,
        out_specs=[vmem] * len(outs),
        scratch_shapes=[pltpu.VMEM(shape, kind) for _, shape, kind in scratch],
        compiler_params=pltpu.CompilerParams(vmem_limit_bytes=VMEM_LIMIT),
        name="feed_both",
    )(x, og, ctx, w_expand, w_shrink, vecs)


def layer_kernel(heads, plan, inv_tokens, names, kept, used, feeds, *refs):
    r = types.SimpleNamespace(**dict(zip(names, refs)))
    cols = heads * HD
    tokens = r.x_all.shape[0]
    pages = tokens // PAGE
    own_tokens = tokens // 2
    tiles = own_tokens // TILE
    place = Place()
    place.signal()
    m, peer = place.m, place.peer["x"]
    at = (place.z, place.y)
    own = aligned(m, own_tokens)
    load_x = pltpu.make_async_copy(r.x_all.at[own, :], r.x, r.load_sem.at[0])
    load_og = pltpu.make_async_copy(r.og_all.at[own, :], r.og, r.load_sem.at[1])
    load_x.start()
    load_og.start()
    r.w[(0, place.c, 0, *at)] = r.attn[0].astype(BF16)
    for half in range(2):
        r.w[(1 + half, place.c, 0, *at)] = jnp.concatenate(
            [
                r.attn[1 + kind, :, head * HD : (head + 1) * HD].astype(BF16)
                for head in range(half * heads // 2, (half + 1) * heads // 2)
                for kind in range(2)
            ],
            axis=1,
        )
    r.box_gather[(0, place.c, 0, *at)] = r.shard_box[...]
    r.vec_gather[(0, place.c, m, *at)] = jnp.zeros((VROWS, 128), F32)
    table_at = (slice(0, r.vectors.shape[0]), slice(0, r.vectors.shape[1]))
    r.vec_gather[(0, place.c, m, *at, *table_at)] = r.vectors[...]
    r.we[(0, place.c, m, *at)] = r.merge[...].astype(BF16)
    for chunk in range(4):
        lanes = slice(chunk * UNIT, (chunk + 1) * UNIT)
        r.we[(1 + chunk, place.c, m, *at)] = r.expand[:, lanes].astype(BF16)
        r.ws[(chunk, place.c, m, *at)] = r.shrink[:, lanes].astype(BF16)
    place.wait()
    tree_v = Spread(place, r.vec_gather, 1, "xzy", r.v_sem)
    tree_b = Spread(place, r.box_gather, 1, "zy", r.b_sem)
    tree_a = Spread(place, r.w, 3, "zy", r.a_sem)
    tree_e = Spread(place, r.we, 5, "zyx", r.e_sem)
    tree_f = Spread(place, r.ws, 4, "xzy", r.f_sem)
    tree_e.lag = tree_f.lag = 2
    first, late = tree_a.events, 3
    begun = first - late

    def weights_event(number):
        tree_e.event(number)
        tree_f.event(number)

    def finish(chunk, value):
        r.sum_f[chunk] = value * inv_tokens

    back_f = Reduce(
        place, r.gs, None, dict(c=r.fc, y=r.fy, z=r.fz, x=r.fx), 4, "cyzx", r.back_sem, finish
    )
    back_f.lag, back_f.held_back = 2, 1

    def attention(*scoped):
        q = types.SimpleNamespace(**dict(zip([item[0] for item in kept + used] + ["x"], scoped)))
        load_all = pltpu.make_async_copy(r.x_all, q.x, r.load_sem.at[2])
        load_all.start()

        tree_v.stage(0, 0)

        def begin(number, carry):
            tree_v.event(number + 1)
            tree_b.event(number)

            @pl.when(number == 4)
            def _():
                r.vec[...] = rows_from_blocks(
                    r.vec_gather[...].reshape(-1, 128), r.pick[...], plan
                )
                r.box_out[...] = natural(r.box_gather, 0, 0).astype(BF16)
                attend_setup(heads, m, r.box_out, r.vec, q.box_heads, q.bias)

            tree_a.event(number)
            weights_event(number - late)
            pl.when(number == 0)(lambda: attend_trig(r.omega, r.corner, q.trig))
            return carry

        lax.fori_loop(0, first, begin, 0)
        keep_w = pltpu.make_async_copy(r.w, r.w_out, r.load_sem.at[3])
        keep_w.start()
        load_all.wait()

        def projected(page):
            weights_event(begun + page)

        piece = PAGE // 2

        def swap_copy(index):
            theirs = pages * (1 - m) + index
            start_rows(
                q.ctx.at[aligned(theirs, piece), :],
                r.ctxx.at[m, aligned(index, piece), :],
                piece,
                r.ctx_sem.at[0, index],
                r.ctx_sem.at[1, index],
                peer,
            )

        def attended(step, turn, pair):
            pl.when((step % 2 == 0) & (step < 8))(lambda: weights_event(begun + pages + step // 2))

            @pl.when(step == heads // 2 - 1)
            def _():
                swap_copy(2 - 2 * m)
                swap_copy(1)

            @pl.when(step == heads - 1)
            def _():
                swap_copy(2 * m)

        attend_math(
            heads,
            q,
            lambda chunk: natural(r.w, chunk, 0),
            lambda turn: turn * m + (pages - 1 - turn) * (1 - m),
            projected,
            attended,
        )
        stores = [
            pltpu.make_async_copy(getattr(q, name), getattr(r, name + "_out"), r.store_sem.at[k])
            for k, (name, _, _) in enumerate(kept)
        ]
        for copy in stores:
            copy.start()
        r.ctxx[m] = q.ctx[own, :]
        for index in range(pages):
            copy = remote(
                q.ctx.at[aligned(index, piece), :],
                r.ctxx.at[1 - m, aligned(index, piece), :],
                r.ctx_sem.at[0, index],
                r.ctx_sem.at[1, index],
                peer,
            )
            copy.wait_recv()
            copy.wait_send()
        for copy in stores:
            copy.wait()
        keep_w.wait()

    pl.run_scoped(
        attention,
        *[pltpu.VMEM(shape, kind) for _, shape, kind in kept + used],
        pltpu.VMEM(r.x_all.shape, BF16),
    )

    def feed(*scoped):
        q = types.SimpleNamespace(**dict(zip([item[0] for item in feeds], scoped)))
        for name in ("x", "og", "we", "ws", "vec", "ctxx", "dh1l", "ge", "gs", "vsum"):
            setattr(q, name, getattr(r, name))

        def out_copies(tile):
            rows = aligned(tile, TILE)
            there = r.out_full.at[pl.ds(pl.multiple_of(m * own_tokens + tile * TILE, TILE), TILE), :]
            return (
                pltpu.make_async_copy(q.out.at[rows, :], there, r.swap_sem.at[0, tile]),
                remote(q.out.at[rows, :], there, r.swap_sem.at[1, tile], r.swap_sem.at[2, tile], peer),
            )

        def dctx_copies(tile):
            rows = aligned(tile, TILE)
            there = r.dctx_full.at[pl.ds(pl.multiple_of(m * own_tokens + tile * TILE, TILE), TILE), :]
            return (
                pltpu.make_async_copy(q.dctx.at[m, rows, :], there, r.swap_sem.at[3, tile]),
                remote(
                    q.dctx.at[1 - m, rows, :], there, r.swap_sem.at[4, tile], r.swap_sem.at[5, tile], peer
                ),
            )

        def start_out(tile):
            rows = aligned(tile, TILE)
            there = r.out_full.at[pl.ds(pl.multiple_of(m * own_tokens + tile * TILE, TILE), TILE), :]
            out_copies(tile)[0].start()
            sems = r.swap_sem.at[1, tile], r.swap_sem.at[2, tile]
            start_rows(q.out.at[rows, :], there, TILE, *sems, peer)

        def start_dctx(tile):
            rows = aligned(tile, TILE)
            there = r.dctx_full.at[pl.ds(pl.multiple_of(m * own_tokens + tile * TILE, TILE), TILE), :]
            dctx_copies(tile)[0].start()
            sems = r.swap_sem.at[4, tile], r.swap_sem.at[5, tile]
            start_rows(q.dctx.at[1 - m, rows, :], there, TILE, *sems, peer)

        def grew(number):
            pl.when(number % 3 == 1)(lambda: weights_event(begun + pages + 4 + number // 3))

        def shrank(number):
            pl.when(number % 2 == 1)(lambda: back_f.event(4 + number // 2))

        load_x.wait()
        load_og.wait()
        feed_math(
            q,
            dict(
                grew=grew,
                turned=start_out,
                shrinks=lambda step: back_f.event(step),
                shrank=shrank,
                left=start_dctx,
            ),
        )
        back_f.rest()
        back_f.drain()
        for tile in range(tiles):
            for copy in out_copies(tile) + dctx_copies(tile):
                copy.wait()

    pl.run_scoped(feed, *[pltpu.VMEM(shape, kind) for _, shape, kind in feeds])
    for tree in (tree_v, tree_b, tree_a, tree_e, tree_f):
        tree.drain()


def layer_forward(x, og, corners, omega, pick, shards, plan, inv_tokens):
    tokens, width = x.shape
    cols = shards[1].shape[1]
    heads = cols // HD
    own = tokens // 2
    unit = (width // 16, UNIT)
    kept, used = attend_buffers(heads, tokens)
    feeds = feed_buffers(own, width, 8 * UNIT)
    feeds += [("out", (own, width), BF16), ("dctx", (2, own, UNIT), BF16)]
    free = pl.BlockSpec(memory_space=pl.ANY)
    vmem = pl.BlockSpec(memory_space=pltpu.VMEM)
    inputs = [("x_all", free), ("og_all", free), ("corner", vmem), ("omega", vmem), ("pick", vmem)]
    inputs += [(name, vmem) for name in ("attn", "shard_box", "vectors", "merge", "expand", "shrink")]
    outs = [(name + "_out", shape, kind, free) for name, shape, kind in kept]
    outs += [
        ("w_out", (3, 2, 1, 4, 2, *unit), BF16, free),
        ("box_out", (PE, cols), BF16, vmem),
        ("out_full", (tokens, width), BF16, free),
        ("dctx_full", (tokens, cols), BF16, free),
        ("dh1l", (own, width), BF16, vmem),
        ("ge", (5, 2, 2, 4, 2, *unit), BF16, vmem),
        ("vsum", (VROWS, width), F32, vmem),
        ("sum_f", (4, *unit), F32, vmem),
    ]
    dma = pltpu.SemaphoreType.DMA
    scratch = [
        ("x", pltpu.VMEM((own, width), BF16)),
        ("og", pltpu.VMEM((own, width), BF16)),
        ("vec", pltpu.VMEM((VROWS, width), F32)),
        ("w", pltpu.VMEM((3, 2, 1, 4, 2, *unit), BF16)),
        ("box_gather", pltpu.VMEM((1, 2, 1, 4, 2, PE // 16, cols), F32)),
        ("vec_gather", pltpu.VMEM((1, 2, 2, 4, 2, VROWS, 128), F32)),
        ("we", pltpu.VMEM((5, 2, 2, 4, 2, *unit), BF16)),
        ("ws", pltpu.VMEM((4, 2, 2, 4, 2, *unit), BF16)),
        ("ctxx", pltpu.VMEM((2, own, cols), BF16)),
        ("gs", pltpu.VMEM((4, 2, 2, 4, 2, *unit), BF16)),
        ("fc", pltpu.VMEM((4, 2, 4, 2, *unit), BF16)),
        ("fy", pltpu.VMEM((4, 2, 4, *unit), BF16)),
        ("fz", pltpu.VMEM((4, 3, 2, *unit), BF16)),
        ("fx", pltpu.VMEM((4, *unit), BF16)),
        ("ctx_sem", dma((2, 3))),
        ("a_sem", dma((2, 3, SLOTS))),
        ("b_sem", dma((2, 1, SLOTS))),
        ("v_sem", dma((2, 1, SLOTS))),
        ("e_sem", dma((2, 5, SLOTS))),
        ("f_sem", dma((2, 4, SLOTS))),
        ("back_sem", dma((2, 4, SLOTS))),
        ("load_sem", dma((4,))),
        ("store_sem", dma((len(kept),))),
        ("swap_sem", dma((6, own // TILE))),
    ]
    names = [item[0] for item in inputs + outs + scratch]
    return pl.pallas_call(
        functools.partial(layer_kernel, heads, plan, inv_tokens, names, kept, used, feeds),
        out_shape=[jax.ShapeDtypeStruct(shape, kind) for _, shape, kind, _ in outs],
        in_specs=[item[1] for item in inputs],
        out_specs=[item[3] for item in outs],
        scratch_shapes=[item[1] for item in scratch],
        compiler_params=pltpu.CompilerParams(
            vmem_limit_bytes=VMEM_LIMIT, collective_id=0, has_side_effects=True
        ),
        name="layer_forward",
    )(x, og, corners, omega, pick, *shards)


def pair_place(cols):
    spot = lax.broadcasted_iota(jnp.int32, (cols, 2 * cols), 0)
    lane = lax.broadcasted_iota(jnp.int32, (cols, 2 * cols), 1)
    target = ((spot >> 6) << 7) + HD + (spot & (HD - 1))
    return jnp.where(lane == target, 1.0, 0.0)


def exact_dot(lhs, rhs, dims=NN):
    return lax.dot_general(
        lhs, rhs, dims, precision=lax.Precision.HIGHEST, preferred_element_type=F32
    )


def attend_back_kernel(heads, plan, inv_tokens, *refs):
    inputs, refs = refs[:12], refs[12:]
    if plan is not None:
        load_sem, held, refs = refs[-1], refs[-13:-1], refs[:-13]
        loads = [
            pltpu.make_async_copy(src, dst, load_sem.at[k]) for k, (src, dst) in enumerate(zip(inputs, held))
        ]
        early = (0, 2, 7, 11)
        for k in sorted(range(12), key=lambda k: k not in early):
            loads[k].start()
        inputs = held
    x_ref, w_ref, box_ref, *inputs = inputs
    qa_ref, qtok_ref, kvtok_ref, kt_ref, kft_ref, trig_ref, ctxt_ref, log_ref, dctx_ref = inputs
    cols = heads * HD
    tokens = x_ref.shape[0]
    pages = tokens // PAGE
    m = lax.axis_index("mp")
    piece = PAGE // 2
    pieces = 2 * pages
    lane = lax.broadcasted_iota(jnp.int32, (1, 2 * HD), 1)
    lower = lane < HD
    if plan is None:
        inp_ref, gw_ref, gbox_ref, qvsum_ref, *refs = refs
        kftok, dctxt, boxt, dtok, xt, gbox = refs
        before, after = 0, 0

        def background(number):
            pass
    else:
        dh1_ref, vsum_ref, sumf_ref, pick_ref, full_e, *refs = refs
        inp_ref, sum_e, sum_a, sum_b, sum_v, norm_ref, *refs = refs
        kftok, dctxt, boxt, dtok, xt, gbox, *refs = refs
        came, total_e, full_a, full_b, full_v, land_v, norms, *refs = refs
        ec, ey, ez, ex, ac, ay, az, bc, by, bz, *refs = refs
        e_sem, a_sem, b_sem, v_sem, n_sem, i_sem, loc_sem = refs
        place = Place()
        place.signal_all()
        fill = pltpu.make_async_copy(full_e.at[:, place.c], total_e, loc_sem.at[0])
        fill.start()
        place.wait_all()

        def finish(out):
            def put(chunk, value):
                out[chunk] = value * inv_tokens

            return put

        tree_e = Reduce(
            place, full_e, total_e, dict(c=ec, y=ey, z=ez, x=ex), 5, "cyzx", e_sem, finish(sum_e)
        )
        tree_e.lag, tree_e.held_back = 2, 1
        tree_a = Reduce(place, full_a, None, dict(c=ac, y=ay, z=az), 3, "cyz", a_sem, finish(sum_a))
        tree_b = Reduce(place, full_b, None, dict(c=bc, y=by, z=bz), 1, "cyz", b_sem, finish(sum_b))

        def block_of(rank):
            r = rank % 16
            return full_v.at[rank // 16, r // 4, (r // 2) % 2, r % 2]

        spot = (place.m, place.z, place.y, place.c)
        all_v = Everyone(place, block_of, lambda step: land_v.at[step - 1], v_sem)
        all_n = Everyone(place, lambda rank: norms.at[spot], lambda step: norms.at[spot], n_sem)

        def background(number):
            tree_e.event(number)

        background(0)
        fill.wait()
        for k in early:
            loads[k].wait()

    boxt[...] = box_ref[...].T
    gbox[...] = jnp.zeros_like(gbox)

    def prepare(page, carry):
        rows = aligned(page, PAGE)
        kftok[rows, :] = kft_ref[:, rows].T
        dctxt[:, rows] = dctx_ref[rows, :].T
        xt[:, rows] = x_ref[rows, :].T
        if plan is not None:
            pl.when(page > 0)(lambda: background(page))
        return carry

    lax.fori_loop(0, pages, prepare, 0)
    if plan is not None:
        for k in range(12):
            if k not in early:
                loads[k].wait()

    def attend(step, carry):
        page, pair = step // (heads // 2), step % (heads // 2)
        rows = aligned(page, PAGE)
        own, partner = turn_factors(trig_ref[:, rows])
        pair_lanes = aligned(pair, 2 * HD)
        query_pair = qtok_ref[rows, pair_lanes]
        dctx_pair = dctx_ref[rows, pair_lanes]
        halves = []
        boxes = []
        blank = jnp.zeros((HD, PAGE), BF16)
        for side in range(2):
            head = pair * 2 + side
            lanes = aligned(head, 2 * HD)
            key_value = kvtok_ref[rows, lanes]
            left = jnp.concatenate([kftok[rows, :], key_value], axis=1)
            score = dot(left, jnp.concatenate([qa_ref[head, :, rows], blank], axis=0))
            prob = jnp.exp(score - log_ref[head, :, rows])
            prob_low = prob.astype(BF16)
            head_rows = pl.ds(pl.multiple_of(head * HD, HD), HD)
            dctx_head = dctxt[head_rows, rows]
            grad_prob = dot(
                key_value, jnp.concatenate([blank, dctx_head], axis=0)
            )
            inner = col_sum(dctx_head.astype(F32) * ctxt_ref[head_rows, rows].astype(F32))
            grad_score = (prob * (grad_prob - inner)).astype(BF16)
            if side == 0:
                both = jnp.concatenate([query_pair[:, 0:HD], dctx_pair[:, 0:HD]], axis=1)
            else:
                both = jnp.concatenate([query_pair[:, HD:], dctx_pair[:, HD:]], axis=1)
            from_score = dot(grad_score, both)
            from_prob = dot(prob_low, both)
            grad_kv = jnp.where(lower, from_score, from_prob).astype(BF16)
            dtok[rows, pl.ds(pl.multiple_of(cols + head * 2 * HD, 2 * HD), 2 * HD)] = grad_kv
            keys = jnp.concatenate([kft_ref[:, rows], kt_ref[head_rows, rows]], axis=0)
            grad_query = dot(keys, grad_score) * HD ** (-0.5)
            feat = grad_query[0:PE]
            proj = (feat * own - swap_blocks(feat) * partner).astype(BF16)
            halves.append(grad_query[PE:] + dot(boxt[head_rows, :], proj))
            boxes.append(dot(proj, query_pair))
        gbox[:, pair_lanes] += jnp.where(lower, boxes[0], boxes[1])
        dtok[rows, pair_lanes] = jnp.concatenate(halves, axis=0).astype(BF16).T
        return carry

    def weights(chunk):
        return w_ref[chunk] if plan is None else natural(w_ref, chunk, 0)

    def spread(page):
        rows = aligned(page, PAGE)
        return sum(
            dot(dtok[rows, chunk * UNIT : (chunk + 1) * UNIT], weights(chunk), NT) for chunk in range(3)
        )

    if plan is None:
        lax.fori_loop(0, pages * (heads // 2), attend, 0)
        gbox_ref[...] = gbox[...] * HD**0.5

        def spread_page(page, carry):
            inp_ref[aligned(page, PAGE), :] = spread(page)
            return carry

        lax.fori_loop(0, pages, spread_page, 0)

        def gather(step, carry):
            lanes = aligned(step, UNIT)
            gw_ref[step] = dot(xt[...], dtok[:, lanes]).astype(BF16)
            qvsum_ref[0:1, lanes] = col_sum(dtok[:, lanes].astype(F32))
            return carry

        lax.fori_loop(0, 3, gather, 0)
        return

    def swap(index):
        rows = aligned(index, piece)
        return remote(
            inp_ref.at[rows, :], came.at[rows, :], i_sem.at[0, index], i_sem.at[1, index], place.peer["x"]
        )

    def attend_and_send(step, carry):
        attend(step, carry)
        page = step // (heads // 2)

        @pl.when(step % (heads // 2) == heads // 2 - 1)
        def _():
            value = spread(page)
            for half in range(2):
                index = 2 * page + half
                rows = aligned(index, piece)
                own = index // pages == m
                spot = aligned(index % pages, piece)
                extra = jnp.where(own, dh1_ref[spot, :].astype(F32), 0.0)
                inp_ref[rows, :] = (value[half * piece : (half + 1) * piece] + extra).astype(BF16)
                start_rows(
                    inp_ref.at[rows, :],
                    came.at[rows, :],
                    piece,
                    i_sem.at[0, index],
                    i_sem.at[1, index],
                    place.peer["x"],
                )

        background(step + pages)
        return carry

    lax.fori_loop(0, pages * (heads // 2), attend_and_send, 0)
    put_natural(full_b, 0, 0, gbox[...] * HD**0.5)

    def gather(step, carry):
        grad = dot(xt[...], dtok[:, aligned(step, UNIT)]).astype(BF16)
        put_natural(full_a, step, 0, grad)
        tree_a.event(step)
        tree_b.event(step)
        return carry

    lax.fori_loop(0, 3, gather, 0)

    sums = jnp.concatenate(
        [
            col_sum(dtok[:, chunk * UNIT : (chunk + 1) * UNIT].astype(F32)) for chunk in range(3)
        ],
        axis=1,
    )
    values = exact_dot(jnp.broadcast_to(sums[:, cols:], (8, 2 * cols)), pair_place(cols), NT)
    pair = jnp.concatenate([sums[:, 0:cols], values[0:1]], axis=0)
    blank = jnp.zeros_like(pair)
    pair = jnp.where(
        m == 0, jnp.concatenate([pair, blank], axis=1), jnp.concatenate([blank, pair], axis=1)
    )
    table = jnp.concatenate([vsum_ref[0:6, :], pair, vsum_ref[8:, :]], axis=0)
    mp_count, dp_count = plan
    width = table.shape[1]
    each = width // (mp_count * dp_count)
    wide_lane = lax.broadcasted_iota(jnp.int32, (VROWS, width), 1)
    for side in range(mp_count):
        parts = []
        for r in range(dp_count):
            first = (r * mp_count + side) * each
            parts.append(jnp.where((wide_lane >= first) & (wide_lane < first + each), table, 0.0))
        block = exact_dot(jnp.concatenate(parts, axis=0), pick_ref[...], NT)
        full_v[side] = block.reshape(full_v.shape[1:])
    all_v.start()

    def tail(number, carry):
        tree_a.event(number)
        tree_b.event(number)
        return carry

    lax.fori_loop(3, tree_a.events, tail, 0)
    tree_e.rest()
    all_v.wait()
    total_v = full_v[spot] + jnp.sum(land_v[...], axis=0)
    sum_v[0] = total_v * inv_tokens

    square = sum(jnp.sum(out[...] * out[...]) for out in (sum_e, sumf_ref, sum_a, sum_b, sum_v))
    norms[spot] = jnp.full((8, 128), square, F32)
    all_n.start()

    def final(number, carry):
        rows = aligned(number, piece)
        swap(number).wait()
        inp_ref[rows, :] = (inp_ref[rows, :].astype(F32) + came[rows, :].astype(F32)).astype(BF16)
        return carry

    lax.fori_loop(0, pieces, final, 0)
    all_n.wait()
    every = norms[...].reshape(-1, 8, 128)
    norm_ref[...] = jnp.sqrt(sum(every[k] for k in range(every.shape[0])))
    for tree in (tree_e, tree_a, tree_b):
        tree.drain()


def attend_backward(x, weight, box, kept, dctx, plan, inv_tokens, more=()):
    tokens, width = x.shape
    cols = weight.shape[-1]
    heads = cols // HD
    vmem = pl.BlockSpec(memory_space=pltpu.VMEM)
    scratch = [
        pltpu.VMEM((tokens, PE), BF16),
        pltpu.VMEM((cols, tokens), BF16),
        pltpu.VMEM((cols, PE), BF16),
        pltpu.VMEM((tokens, 3 * cols), BF16),
        pltpu.VMEM((width, tokens), BF16),
        pltpu.VMEM((PE, cols), F32),
    ]
    in_specs = [vmem] * 12
    if plan is None:
        shapes = [
            ((tokens, width), F32),
            ((3, width, cols), BF16),
            ((PE, cols), F32),
            ((8, 3 * cols), F32),
        ]
        extra = {}
    else:
        free = pl.BlockSpec(memory_space=pl.ANY)
        in_specs = [free] * 12 + [vmem] * 4 + [free]
        rows = width // 16
        unit = (rows, UNIT)
        tile = (PE // 16, cols)
        small = (VROWS, 128)
        shapes = [
            ((tokens, width), BF16),
            ((5, *unit), F32),
            ((3, *unit), F32),
            ((1, *tile), F32),
            ((1, *small), F32),
            ((8, 128), F32),
        ]
        scratch += [
            pltpu.VMEM((tokens, width), BF16),
            pltpu.VMEM((5, 2, 4, 2, *unit), BF16),
            pltpu.VMEM((3, 2, 1, 4, 2, *unit), BF16),
            pltpu.VMEM((1, 2, 1, 4, 2, *tile), F32),
            pltpu.VMEM((2, 4, 2, 2, *small), F32),
            pltpu.VMEM((31, *small), F32),
            pltpu.VMEM((2, 4, 2, 2, 8, 128), F32),
            pltpu.VMEM((5, 2, 4, 2, *unit), BF16),
            pltpu.VMEM((5, 2, 4, *unit), BF16),
            pltpu.VMEM((5, 3, 2, *unit), BF16),
            pltpu.VMEM((5, *unit), BF16),
            pltpu.VMEM((3, 4, 2, *unit), BF16),
            pltpu.VMEM((3, 4, *unit), BF16),
            pltpu.VMEM((3, 3, *unit), BF16),
            pltpu.VMEM((1, 4, 2, *tile), F32),
            pltpu.VMEM((1, 4, *tile), F32),
            pltpu.VMEM((1, 3, *tile), F32),
            pltpu.SemaphoreType.DMA((2, 5, SLOTS)),
            pltpu.SemaphoreType.DMA((2, 3, SLOTS)),
            pltpu.SemaphoreType.DMA((2, 1, SLOTS)),
            pltpu.SemaphoreType.DMA((2, 31)),
            pltpu.SemaphoreType.DMA((2, 31)),
            pltpu.SemaphoreType.DMA((2, 2 * (tokens // PAGE))),
            pltpu.SemaphoreType.DMA((2,)),
        ]
        scratch += [pltpu.VMEM(array.shape, array.dtype) for array in (x, weight, box, *kept, dctx)]
        scratch.append(pltpu.SemaphoreType.DMA((12,)))
        extra = dict(collective_id=2, has_side_effects=True)
    return pl.pallas_call(
        functools.partial(attend_back_kernel, heads, plan, inv_tokens),
        out_shape=[jax.ShapeDtypeStruct(s, d) for s, d in shapes],
        in_specs=in_specs,
        out_specs=[vmem] * len(shapes),
        scratch_shapes=scratch,
        compiler_params=pltpu.CompilerParams(vmem_limit_bytes=VMEM_LIMIT, **extra),
        cost_estimate=pl.CostEstimate(flops=4 * 10**10, bytes_accessed=10**8, transcendentals=10**7),
        name="attend_backward",
    )(x, weight, box, *kept, dctx, *more)


def adam_step(master, first, second, gradient, rate, decay):
    new_first = BETA_ONE * first + (1.0 - BETA_ONE) * gradient
    new_second = BETA_TWO * second + (1.0 - BETA_TWO) * gradient * gradient
    first_hat = new_first / (1.0 - BETA_ONE**STEP)
    second_hat = new_second / (1.0 - BETA_TWO**STEP)
    new_master = master - rate * (first_hat / (jnp.sqrt(second_hat) + ADAM_EPS) + decay * master)
    return (new_first, new_second, new_master)


def adam_kernel(heads, norm_ref, *refs):
    sum_e, sum_f, sum_a, sum_b, sum_v, *refs = refs
    states, outs = refs[:18], refs[18:]
    outs[-1][...] = norm_ref[0:1, 0:1]
    clip = CLIP_LIMIT / jnp.maximum(norm_ref[0:1, 0:1], CLIP_LIMIT)

    def update(first, out, gradient, at, rate, decay):
        news = adam_step(*(ref[at] for ref in states[first : first + 3]), gradient * clip, rate, decay)
        for ref, new in zip(outs[out : out + 3], news):
            ref[at] = new
        if decay:
            outs[out + 3][at] = news[2].astype(BF16)

    def heads_of(kind):
        half = heads // 2
        return jnp.concatenate(
            [
                sum_a[1 + head // half, :, (2 * (head % half) + kind) * HD : (2 * (head % half) + kind + 1) * HD]
                for head in range(heads)
            ],
            axis=1,
        )

    for index, gradient in enumerate((sum_a[0], heads_of(0), heads_of(1))):
        update(0, 0, gradient, index, RATE_MATRIX, WEIGHT_DECAY)
    update(3, 4, sum_b[0], ALL, RATE_MATRIX, WEIGHT_DECAY)
    update(6, 8, sum_e[0], ALL, RATE_MATRIX, WEIGHT_DECAY)
    for chunk in range(4):
        lanes = (ALL, slice(chunk * UNIT, (chunk + 1) * UNIT))
        update(9, 12, sum_e[1 + chunk], lanes, RATE_MATRIX, WEIGHT_DECAY)
        update(12, 16, sum_f[chunk], lanes, RATE_MATRIX, WEIGHT_DECAY)
    rows, each = states[15].shape
    update(15, 20, sum_v[0, 0:rows, 0:each], ALL, RATE_VECTOR, 0.0)


def adam_all(norm, sums, states):
    shapes = []
    for first in range(0, 18, 3):
        shapes += [(states[first].shape, F32)] * 3
        if first < 15:
            shapes.append((states[first].shape, BF16))
    vmem = pl.BlockSpec(memory_space=pltpu.VMEM)
    shapes.append(((1, 1), F32))
    return pl.pallas_call(
        functools.partial(adam_kernel, states[0].shape[2] // HD),
        out_shape=[jax.ShapeDtypeStruct(s, d) for s, d in shapes],
        in_specs=[vmem] * (6 + len(states)),
        out_specs=[vmem] * len(shapes),
        compiler_params=pltpu.CompilerParams(vmem_limit_bytes=VMEM_LIMIT),
        name="adam_all",
    )(norm, *sums, *states)


def pack_qkv(shard):
    rows, cols = shard.shape[1:]
    heads = cols // HD
    pairs = jnp.stack([shard[1].reshape(rows, heads, HD), shard[2].reshape(rows, heads, HD)], axis=2)
    pairs = pairs.reshape(rows, 2, cols)
    return jnp.stack([shard[0], pairs[:, 0], pairs[:, 1]])


def unpack_qkv(packed):
    rows, cols = packed.shape[1:]
    pairs = jnp.concatenate([packed[1], packed[2]], axis=1).reshape(rows, cols // HD, 2, HD)
    return jnp.stack(
        [packed[0], pairs[:, :, 0].reshape(rows, cols), pairs[:, :, 1].reshape(rows, cols)]
    )


def to_chunks(shard):
    rows = shard.shape[0]
    return shard.reshape(rows, -1, UNIT).transpose(1, 0, 2)


def from_chunks(chunks):
    return chunks.transpose(1, 0, 2).reshape(chunks.shape[1], -1)


def on_device(
    layer_input,
    page_boxes,
    output_grad,
    attn_proj,
    attn_first,
    attn_second,
    box_proj,
    box_first,
    box_second,
    merge_proj,
    merge_first,
    merge_second,
    expand_proj,
    expand_first,
    expand_second,
    shrink_proj,
    shrink_first,
    shrink_second,
    vectors,
    vector_first,
    vector_second,
):
    mp_count = lax.axis_size("mp")
    dp_count = lax.axis_size("dp")
    mp_index = lax.axis_index("mp")
    tokens, width = layer_input.shape
    cols = attn_proj.shape[2]
    heads = cols // HD
    own_tokens = tokens // mp_count
    inv_tokens = 1.0 / (tokens * dp_count)

    corners = page_boxes.T
    omega = (10000.0 ** (-np.arange(FREQS, dtype=np.float64) / FREQS)).astype(np.float32)[:, None]
    omega = jnp.asarray(omega)
    plan = (mp_count, dp_count) if dp_count == 16 and mp_count == 2 else None
    if plan is not None:
        each = vectors.shape[1]
        pick = np.zeros((128, width), np.float32)
        pick[np.arange(width) % each, np.arange(width)] = 1.0
        pick = jnp.asarray(pick)
        *kept, w_qkv, w_box, layer_out, dctx, dh1, g_expand, vec_sum, sum_f = layer_forward(
            layer_input,
            output_grad,
            corners,
            omega,
            pick,
            (attn_proj, box_proj, vectors, merge_proj.T, expand_proj, shrink_proj.T),
            plan,
            inv_tokens,
        )
        input_grad, sum_e, sum_a, sum_b, sum_v, norm = attend_backward(
            layer_input,
            w_qkv,
            w_box,
            kept,
            dctx,
            plan,
            inv_tokens,
            (dh1, vec_sum, sum_f, pick, g_expand),
        )
        merge = [merge_proj.T, merge_first.T, merge_second.T]
        shrink = [shrink_proj.T, shrink_first.T, shrink_second.T]
        *results, norm = adam_all(
            norm,
            (sum_e, sum_f, sum_a, sum_b, sum_v),
            [attn_proj, attn_first, attn_second, box_proj, box_first, box_second, *merge]
            + [expand_proj, expand_first, expand_second, *shrink, vectors, vector_first, vector_second],
        )
        turned = (8, 9, 10, 11, 16, 17, 18, 19)
        results = [out.T if k in turned else out for k, out in enumerate(results)]
        return (layer_out, input_grad, norm.reshape(()), *results)
    shard_qkv = pack_qkv(attn_proj).astype(BF16)
    shard_e = jnp.concatenate([merge_proj.T[None], to_chunks(expand_proj)]).astype(BF16)
    shard_f = to_chunks(shrink_proj.T).astype(BF16)
    w_qkv = lax.all_gather(shard_qkv, "dp", axis=1, tiled=True)
    w_box = lax.all_gather(box_proj.astype(BF16), "dp", axis=0, tiled=True)
    w_expand = lax.all_gather(lax.all_gather(shard_e, "dp", axis=1, tiled=True), "mp", axis=1)
    w_shrink = lax.all_gather(lax.all_gather(shard_f, "dp", axis=1, tiled=True), "mp", axis=1)
    vecs = lax.all_gather(vectors, ("dp", "mp"), axis=1, tiled=True)
    vecs = jnp.pad(vecs, ((0, VROWS - vecs.shape[0]), (0, 0)))
    *kept, context = attend_forward(layer_input, corners, omega, w_qkv, w_box, vecs)
    context = lax.all_to_all(
        context.reshape(mp_count, own_tokens, cols), "mp", split_axis=0, concat_axis=0
    )

    def own_rows(array):
        return lax.dynamic_slice_in_dim(array, mp_index * own_tokens, own_tokens)

    layer_out, dctx, dh1, g_expand, g_shrink, vec_sum = feed_both(
        own_rows(layer_input), own_rows(output_grad), context, w_expand, w_shrink, vecs
    )
    g_feed = jnp.concatenate([g_expand, g_shrink])
    layer_out = lax.all_gather(layer_out, "mp", axis=0, tiled=True)
    dctx = lax.all_to_all(dctx, "mp", split_axis=0, concat_axis=0).reshape(tokens, cols)
    part, g_qkv, g_box, qkv_sum = attend_backward(
        layer_input, w_qkv, w_box, kept, dctx, None, inv_tokens
    )
    own_part = lax.psum_scatter(part.astype(BF16), "mp", scatter_dimension=0, tiled=True)
    own_grad = (own_part.astype(F32) + dh1).astype(BF16)
    input_grad = lax.all_gather(own_grad, "mp", axis=0, tiled=True)
    shard_attn = unpack_qkv(
        lax.psum_scatter(g_qkv, "dp", scatter_dimension=1, tiled=True).astype(F32) * inv_tokens
    )
    shard_box = lax.psum_scatter(g_box, "dp", scatter_dimension=0, tiled=True) * inv_tokens
    sum_feed = lax.psum_scatter(g_feed, "dp", scatter_dimension=2, tiled=True)
    sum_feed = lax.psum_scatter(sum_feed, "mp", scatter_dimension=1, tiled=True)[:, 0]
    sum_feed = sum_feed.astype(F32) * inv_tokens
    sum_expand, sum_shrink = sum_feed[0:5], sum_feed[5:]

    def placed(row):
        return lax.dynamic_update_slice_in_dim(
            jnp.zeros((width,), F32), row, mp_index * cols, 0
        )[None, :]

    value_sum = qkv_sum[0, cols:].reshape(heads, 2, HD)[:, 1].reshape(cols)
    vector_grad = jnp.concatenate(
        [vec_sum[0:6], placed(qkv_sum[0, 0:cols]), placed(value_sum), vec_sum[8:12]]
    )
    vector_shard = (
        lax.psum_scatter(vector_grad, ("dp", "mp"), scatter_dimension=1, tiled=True) * inv_tokens
    )
    square = sum(
        jnp.sum(shard * shard)
        for shard in (shard_attn, shard_box, sum_expand, sum_shrink, vector_shard)
    )
    grad_norm = jnp.sqrt(lax.psum(square, ("dp", "mp")))
    shard_merge = sum_expand[0].T
    shard_expand = from_chunks(sum_expand[1:])
    shard_shrink = from_chunks(sum_shrink).T
    clip_scale = CLIP_LIMIT / jnp.maximum(grad_norm, CLIP_LIMIT)
    results = [layer_out, input_grad, grad_norm]
    for master, first, second, shard in (
        (attn_proj, attn_first, attn_second, shard_attn),
        (box_proj, box_first, box_second, shard_box),
        (merge_proj, merge_first, merge_second, shard_merge),
        (expand_proj, expand_first, expand_second, shard_expand),
        (shrink_proj, shrink_first, shrink_second, shard_shrink),
    ):
        new_first, new_second, new_master = adam_step(
            master, first, second, shard * clip_scale, RATE_MATRIX, WEIGHT_DECAY
        )
        results += [new_first, new_second, new_master, new_master.astype(BF16)]
    results += adam_step(
        vectors, vector_first, vector_second, vector_shard * clip_scale, RATE_VECTOR, 0.0
    )
    return tuple(results)


def solution(mesh):
    rows = P("dp", None)
    attn = P(None, "dp", "mp")
    tall = P("dp", "mp")
    wide = P("mp", "dp")
    vector = P(None, ("dp", "mp"))
    in_specs = (rows,) * 3 + (attn,) * 3 + (tall,) * 3 + (wide,) * 3 + (tall,) * 3 + (wide,) * 3
    in_specs += (vector,) * 3
    out_specs = (rows, rows, P()) + (attn,) * 4 + (tall,) * 4 + (wide,) * 4 + (tall,) * 4
    out_specs += (wide,) * 4 + (vector,) * 3
    return jax.shard_map(
        on_device, mesh=mesh, in_specs=in_specs, out_specs=out_specs, check_vma=False
    )
```

```python
import functools
import types

import jax
import jax.numpy as jnp
import numpy as np
from jax import lax
from jax.experimental import pallas as pl
from jax.experimental.pallas import tpu as pltpu
from jax.sharding import PartitionSpec as P

HD = 64
FREQS = 32
PE = 128
PAGE = 512
STEP = 10

NORM_EPS = 1e-12
CLIP_LIMIT = 0.1
BETA_ONE = 0.9
BETA_TWO = 0.999
ADAM_EPS = 1e-08
RATE_MATRIX = 0.05
RATE_VECTOR = 0.5
WEIGHT_DECAY = 0.01

F32 = jnp.float32
BF16 = jnp.bfloat16
VMEM_LIMIT = 60 * 1024 * 1024

NN = (((1,), (0,)), ((), ()))
NT = (((1,), (1,)), ((), ()))
TN = (((0,), (0,)), ((), ()))


def dot(lhs, rhs, dims=NN):
    return lax.dot_general(lhs, rhs, dims, preferred_element_type=F32)


def aligned(index, size):
    return pl.ds(pl.multiple_of(index * size, size), size)


def swap_blocks(feat):
    return jnp.concatenate(
        [
            feat[FREQS : 2 * FREQS],
            feat[0:FREQS],
            feat[3 * FREQS :],
            feat[2 * FREQS : 3 * FREQS],
        ],
        axis=0,
    )


def turn_factors(trig):
    cos_x, sin_x = trig[0:FREQS], trig[FREQS : 2 * FREQS]
    cos_y, sin_y = trig[2 * FREQS : 3 * FREQS], trig[3 * FREQS :]
    return (
        jnp.concatenate([sin_x, sin_x, sin_y, sin_y], axis=0),
        jnp.concatenate([cos_x, -cos_x, cos_y, -cos_y], axis=0),
    )


MESH = pl.DeviceIdType.MESH
ALL = slice(None)
UNIT = 384


class Place:
    def __init__(self):
        rank = lax.axis_index("dp")
        self.m = lax.axis_index("mp")
        self.z = rank // 4
        self.y = (rank // 2) % 2
        self.c = rank % 2
        self.peer = {
            "x": (rank, 1 - self.m),
            "y": (rank + 2 - 4 * self.y, self.m),
            "c": (rank + 1 - 2 * self.c, self.m),
        }
        self.far = [((rank + 4 * step) % 16, self.m) for step in (1, 2, 3)]

    def signal(self):
        barrier = pltpu.get_barrier_semaphore()
        for device in list(self.peer.values()) + self.far:
            pl.semaphore_signal(barrier, inc=1, device_id=device, device_id_type=MESH)

    def wait(self):
        pl.semaphore_wait(pltpu.get_barrier_semaphore(), 6)

    def signal_all(self):
        barrier = pltpu.get_barrier_semaphore()
        rank = self.m * 16 + lax.axis_index("dp")

        def one(step, carry):
            to = (rank + step) % 32
            pl.semaphore_signal(barrier, inc=1, device_id=(to % 16, to // 16), device_id_type=MESH)
            return carry

        lax.fori_loop(1, 32, one, 0)

    def wait_all(self):
        pl.semaphore_wait(pltpu.get_barrier_semaphore(), 31)


PART = 256


def start_rows(src, dst, rows, send_sem, recv_sem, device):
    for first in range(0, rows, PART):
        part = pl.ds(first, PART)
        remote(src.at[part, :], dst.at[part, :], send_sem, recv_sem, device).start()


def remote(src, dst, send_sem, recv_sem, device):
    return pltpu.make_async_remote_copy(
        src_ref=src,
        dst_ref=dst,
        send_sem=send_sem,
        recv_sem=recv_sem,
        device_id=device,
        device_id_type=MESH,
    )


SLOT = {"c": 0, "z": 1, "y": 4, "x": 5}
SLOTS = 6
SENT = (0, 1, 1, 1, 4, 5)


class Tree:
    lag = 1
    held_back = 0
    together = False

    def stage(self, index, chunk):
        raise NotImplementedError

    def event(self, number):
        for index in range(self.count - 1 - self.held_back, -1, -1):
            chunk = number - index * self.lag
            if self.together:

                @pl.when(chunk == 0)
                def _(index=index):
                    for each in range(self.chunks):
                        self.stage(index, each)

            elif self.chunks == 1:
                pl.when(chunk == 0)(lambda index=index: self.stage(index, 0))
            else:
                pl.when((chunk >= 0) & (chunk < self.chunks))(
                    lambda index=index, chunk=chunk: self.stage(index, chunk)
                )

    @property
    def events(self):
        return self.chunks + (self.count - 1 - self.held_back) * self.lag

    def rest(self):
        def one(chunk, carry):
            self.stage(self.count - 1, chunk)
            return carry

        lax.fori_loop(0, self.chunks, one, 0)


class Spread(Tree):
    def __init__(self, place, ref, chunks, order, sems):
        self.chunks, self.ref, self.sems, self.place = chunks, ref, sems, place
        have = {"x": place.m if "x" in order else 0, "z": place.z, "y": place.y}
        mine = {"x": place.m, "y": place.y}
        self.own = have
        self.steps, self.axes = [], order
        for axis in order:
            if axis == "z":
                sends = [(have, place.far[step - 1], step) for step in (1, 2, 3)]
                waits = [(dict(have, z=(place.z + 4 - step) % 4), step) for step in (1, 2, 3)]
            else:
                sends = [(have, place.peer[axis], SLOT[axis])]
                waits = [(dict(have, **{axis: 1 - mine[axis]}), SLOT[axis])]
            self.steps.append((sends, waits))
            have = dict(have, **{axis: ALL})
        self.other = place.peer["c"]
        self.count = len(self.steps) + 2

    def _copy(self, chunk, have, device, slot):
        came = 0 if chunk == ALL else chunk
        block = self.ref.at[chunk, self.place.c, have["x"], have["z"], have["y"]]
        sent = self.sems.at[0, 0, SENT[slot]]
        return remote(block, block, sent, self.sems.at[1, came, slot], device)

    def _plane(self, chunk, core):
        plane = self.ref.at[chunk, core]
        came = 0 if chunk == ALL else chunk
        return remote(plane, plane, self.sems.at[0, 0, 0], self.sems.at[1, came, 0], self.other)

    def stage(self, index, chunk):
        if index == self.count - 1:
            self._plane(chunk, 1 - self.place.c).wait_recv()
            return
        came = [self.own]
        if index > 0:
            came = []
            for have, slot in self.steps[index - 1][1]:
                self._copy(chunk, have, self.other, slot).wait_recv()
                came.append(have)
        if index < len(self.steps):
            for have, device, slot in self.steps[index][0]:
                self._copy(chunk, have, device, slot).start()
        for have in came:
            self._copy(chunk, have, self.other, 0).start()

    def drain(self):
        for axis, (sends, _) in zip(self.axes, self.steps):
            have, _, slot = sends[0]
            if axis == "z":
                have = dict(have, z=slice(0, 3))
            self._copy(ALL, have, self.other, slot).wait_send()
        self._plane(ALL, self.place.c).wait_send()


RANKS = [(c, z, y) for z in range(4) for y in range(2) for c in range(2)]


def natural(ref, chunk, side):
    return jnp.concatenate([ref[chunk, c, side, z, y] for c, z, y in RANKS], axis=0)


def put_natural(ref, chunk, side, value):
    rows = value.shape[0] // len(RANKS)
    for spot, (c, z, y) in enumerate(RANKS):
        ref[chunk, c, side, z, y] = value[spot * rows : (spot + 1) * rows]


class Reduce(Tree):
    def __init__(self, place, full, total, lands, chunks, order, sems, finish):
        self.place, self.full, self.total, self.lands = place, full, total, lands
        self.chunks, self.sems, self.finish = chunks, sems, finish
        mine = {"x": place.m, "y": place.y}
        self.across = ALL if "x" in order else 0
        have = {"x": self.across, "z": ALL, "y": ALL}
        self.order, self.haves = order, []
        for axis in order:
            before = have
            if axis != "c":
                have = dict(have, **{axis: place.z if axis == "z" else mine[axis]})
            self.haves.append((before, have))
        self.count = len(order) + 1

    def _at(self, chunk, have):
        if self.total is None:
            return self.full.at[chunk, self.place.c, have["x"], have["z"], have["y"]]
        return self.total.at[chunk, have["x"], have["z"], have["y"]]

    def _copies(self, index, chunk):
        axis, (before, _) = self.order[index], self.haves[index]
        place, land = self.place, self.lands[axis]

        def copy(src, dst, slot, device):
            return remote(src, dst, self.sems.at[0, 0, SENT[slot]], self.sems.at[1, chunk, slot], device)

        if axis == "c":
            source = self.full.at[chunk, 1 - place.c, self.across]
            return [copy(source, land.at[chunk], SLOT[axis], place.peer[axis])]
        if axis == "z":
            return [
                copy(
                    self._at(chunk, dict(before, z=(place.z + step) % 4)),
                    land.at[chunk, step - 1],
                    step,
                    place.far[step - 1],
                )
                for step in (1, 2, 3)
            ]
        other = 1 - (place.m if axis == "x" else place.y)
        source = self._at(chunk, dict(before, **{axis: other}))
        return [copy(source, land.at[chunk], SLOT[axis], place.peer[axis])]

    def stage(self, index, chunk):
        if index > 0:
            axis, (_, have) = self.order[index - 1], self.haves[index - 1]
            land = self.lands[axis]
            for copy in self._copies(index - 1, chunk):
                copy.wait_recv()
            mine = self._at(chunk, have)
            last = index == self.count - 1
            if axis == "z":
                value = mine[...].astype(F32)
                for step in range(3):
                    value += land[chunk, step].astype(F32)
            elif last:
                value = mine[...].astype(F32) + land[chunk].astype(F32)
            else:
                value = mine[...] + land[chunk]
            if last:
                self.finish(chunk, value)
            else:
                mine[...] = value.astype(mine.dtype)
        if index < self.count - 1:
            for copy in self._copies(index, chunk):
                copy.start()

    def drain(self):
        for axis in self.order:
            land = self.lands[axis]
            slot = SLOT[axis]
            sent = self.sems.at[0, 0, SENT[slot]]
            remote(land, land, sent, self.sems.at[1, 0, slot], self.place.peer["c"]).wait_send()


class Everyone:
    def __init__(self, place, send_block, land_block, sems):
        self.rank = place.m * 16 + lax.axis_index("dp")
        self.send_block, self.land_block, self.sems = send_block, land_block, sems

    def _copy(self, step):
        to = (self.rank + step) % 32
        return remote(
            self.send_block(to),
            self.land_block(step),
            self.sems.at[0, step - 1],
            self.sems.at[1, step - 1],
            (to % 16, to // 16),
        )

    def _each(self, act):
        def one(step, carry):
            act(self._copy(step))
            return carry

        lax.fori_loop(1, 32, one, 0)

    def start(self):
        self._each(lambda copy: copy.start())

    def wait(self):
        self._each(lambda copy: copy.wait())


VROWS = 16


def rows_from_blocks(blocks, pick, counts):
    mp_count, dp_count = counts
    width = pick.shape[1]
    each = width // (mp_count * dp_count)
    wide = lax.dot_general(
        blocks, pick, NN, precision=lax.Precision.HIGHEST, preferred_element_type=F32
    )
    lane = lax.broadcasted_iota(jnp.int32, (VROWS, width), 1)
    table = jnp.zeros((VROWS, width), F32)
    for m in range(mp_count):
        for r, (c, z, y) in enumerate(RANKS):
            first = (r * mp_count + m) * each
            row = (((c * mp_count + m) * 4 + z) * 2 + y) * VROWS
            table += jnp.where((lane >= first) & (lane < first + each), wide[row : row + VROWS], 0.0)
    return table


def attend_setup(heads, m, box_full, vec_ref, box_heads, bias):
    cols = heads * HD
    for head in range(heads):
        box_heads[head] = box_full[:, head * HD : (head + 1) * HD]
    width = vec_ref.shape[1]
    own = jnp.where(m == 0, vec_ref[6:8, 0:cols], vec_ref[6:8, width - cols :])
    spread = exact_dot(jnp.broadcast_to(own[1:2], (8, cols)), pair_place(cols))
    bias[0:1, 0:cols] = own[0:1]
    bias[0:1, cols:] = spread[0:1]


def attend_trig(omega_ref, corner_ref, trig_ref):
    corner = corner_ref[...].astype(F32)
    angle_x = omega_ref[...] * ((corner[0:1] + corner[2:3]) * 0.5)
    angle_y = omega_ref[...] * ((corner[1:2] + corner[3:4]) * 0.5)
    trig_ref[0:FREQS, :] = jnp.cos(angle_x)
    trig_ref[FREQS : 2 * FREQS, :] = jnp.sin(angle_x)
    trig_ref[2 * FREQS : 3 * FREQS, :] = jnp.cos(angle_y)
    trig_ref[3 * FREQS :, :] = jnp.sin(angle_y)


def quiet(*args):
    return None


def attend_math(heads, r, weights, page_of, projected, attended):
    cols = heads * HD
    pages = r.x.shape[0] // PAGE

    def project(page, carry):
        rows = aligned(page, PAGE)
        tokens = r.x[rows, :]
        query = dot(tokens, weights(0)) + r.bias[0:1, 0:cols]
        query = query.astype(BF16) * HD ** (-0.5)
        r.qtok[rows, :] = query
        qa_rows = query.T
        for half in range(2):
            lanes = slice(half * cols, (half + 1) * cols)
            pair = dot(tokens, weights(1 + half)) + r.bias[0:1, cols + half * cols : 2 * cols + half * cols]
            pair = pair.astype(BF16)
            r.kvtok[rows, lanes] = pair
            turned = pair.T
            for spot in range(heads // 2):
                head_rows = slice((half * heads // 2 + spot) * HD, (half * heads // 2 + spot + 1) * HD)
                r.kt[head_rows, rows] = turned[2 * spot * HD : (2 * spot + 1) * HD]
                r.vt[head_rows, rows] = turned[(2 * spot + 1) * HD : (2 * spot + 2) * HD]
        trig = r.trig[:, rows]
        kft = trig.astype(BF16)
        r.kft[:, rows] = kft
        r.kftok[rows, :] = kft.T
        own, partner = turn_factors(trig)
        for head in range(heads):
            query_head = qa_rows[head * HD : (head + 1) * HD]
            proj = dot(r.box_heads[head], query_head)
            feat = proj * own + swap_blocks(proj) * partner
            r.qa[head, 0:PE, rows] = feat.astype(BF16)
            r.qa[head, PE : PE + HD, rows] = query_head
        projected(page)
        return carry

    lax.fori_loop(0, pages, project, 0)

    def attend(step, carry):
        turn, pair = step // (heads // 2), step % (heads // 2)
        rows = aligned(page_of(turn), PAGE)
        halves = []
        blank = jnp.zeros((HD, PAGE), BF16)
        for side in range(2):
            head = pair * 2 + side
            lanes = aligned(head, 2 * HD)
            left = jnp.concatenate([r.kftok[rows, :], r.kvtok[rows, lanes]], axis=1)
            score = dot(left, jnp.concatenate([r.qa[head, :, rows], blank], axis=0))
            top = jnp.max(score, axis=0, keepdims=True)
            weight = jnp.exp(score - top)
            total = jnp.sum(weight, axis=0, keepdims=True)
            value = r.vt[aligned(head, HD), rows]
            halves.append(dot(value, weight.astype(BF16)) * (1.0 / total))
            r.log[head, :, rows] = top + jnp.log(total)
        both = jnp.concatenate(halves, axis=0).astype(BF16)
        lanes = aligned(pair, 2 * HD)
        r.ctxt[lanes, rows] = both
        r.ctx[rows, lanes] = both.T
        attended(step, turn, pair)
        return carry

    lax.fori_loop(0, pages * (heads // 2), attend, 0)


def attend_buffers(heads, tokens):
    cols = heads * HD
    kept = [
        ("qa", (heads, PE + HD, tokens), BF16),
        ("qtok", (tokens, cols), BF16),
        ("kvtok", (tokens, 2 * cols), BF16),
        ("kt", (cols, tokens), BF16),
        ("kft", (PE, tokens), BF16),
        ("trig", (PE, tokens), F32),
        ("ctxt", (cols, tokens), BF16),
        ("log", (heads, 1, tokens), F32),
    ]
    used = [
        ("kftok", (tokens, PE), BF16),
        ("box_heads", (heads, PE, HD), BF16),
        ("bias", (8, 3 * cols), F32),
        ("ctx", (tokens, cols), BF16),
        ("vt", (cols, tokens), BF16),
    ]
    return kept, used


def attend_kernel(heads, names, *refs):
    r = types.SimpleNamespace(**dict(zip(names, refs)))
    attend_setup(heads, lax.axis_index("mp"), r.box, r.vec, r.box_heads, r.bias)
    attend_trig(r.omega, r.corner, r.trig)
    attend_math(heads, r, lambda chunk: r.w[chunk], lambda turn: turn, quiet, quiet)


def attend_forward(x, corners, omega, w_qkv, w_box, vecs):
    tokens = x.shape[0]
    heads = w_box.shape[1] // HD
    kept, used = attend_buffers(heads, tokens)
    outs = kept + [used[3]]
    scratch = used[:3] + used[4:]
    names = ["x", "corner", "omega", "w", "box", "vec"] + [item[0] for item in outs + scratch]
    vmem = pl.BlockSpec(memory_space=pltpu.VMEM)
    return pl.pallas_call(
        functools.partial(attend_kernel, heads, names),
        out_shape=[jax.ShapeDtypeStruct(shape, kind) for _, shape, kind in outs],
        in_specs=[vmem] * 6,
        out_specs=[vmem] * len(outs),
        scratch_shapes=[pltpu.VMEM(shape, kind) for _, shape, kind in scratch],
        compiler_params=pltpu.CompilerParams(vmem_limit_bytes=VMEM_LIMIT),
        name="attend_forward",
    )(x, corners, omega, w_qkv, w_box, vecs)


TILE = 256


def normal_parts(value):
    phi = 0.5 + 0.5 * lax.erf(value * 2.0 ** (-0.5))
    return phi, phi + value * (jnp.exp(value * value * -0.5) * (0.5 / np.pi) ** 0.5)


def norm_stats(value):
    mean = jnp.mean(value, axis=-1, keepdims=True)
    centred = value - mean
    var = jnp.mean(centred * centred, axis=-1, keepdims=True)
    return centred, lax.rsqrt(var + NORM_EPS)


def norm_back(grad_normed, normed, scale):
    first = jnp.mean(grad_normed, axis=-1, keepdims=True)
    second = jnp.mean(grad_normed * normed, axis=-1, keepdims=True)
    return scale * (grad_normed - first - normed * second)


def col_sum(value):
    return jnp.sum(value, axis=0, keepdims=True)


def feed_math(r, hooks):
    hook = {name: quiet for name in ("entered", "grew", "turned", "shrinks", "shrank", "left")}
    hook.update(hooks)
    tokens = r.x.shape[0]
    sides = r.ctxx.shape[0]
    steps = r.ws.shape[0]
    tiles = tokens // TILE
    wide = sides * UNIT
    sum2 = dnorm = r.sum2

    def flat(ref, chunk, side):
        return ref[chunk, side] if len(ref.shape) == 4 else natural(ref, chunk, side)

    def put(ref, chunk, side, value):
        if len(ref.shape) == 4:
            ref[chunk, side] = value
        else:
            put_natural(ref, chunk, side, value)

    def lay_out(step):
        for plain, ref, chunk in ((r.plain_e, r.we, 1 + step), (r.plain_s, r.ws, step)):
            for side in range(sides):
                lanes = slice(side * UNIT, (side + 1) * UNIT)
                if len(ref.shape) == 4:
                    plain[:, lanes] = ref[chunk, side]
                else:
                    rows = plain.shape[0] // len(RANKS)
                    for spot, (c, z, y) in enumerate(RANKS):
                        plain[spot * rows : (spot + 1) * rows, lanes] = ref[chunk, c, side, z, y]

    def put_both(ref, chunk, value):
        for side in range(sides):
            put(ref, chunk, side, value[:, side * UNIT : (side + 1) * UNIT])

    def bias_at(step, side):
        first = side * steps + step
        return (pl.ds(8 + first // 2, 1), aligned(first % 2, UNIT))

    def enter(tile, carry):
        rows = aligned(tile, TILE)
        total = r.x[rows, :].astype(F32) + r.vec[4:5, :]
        for side in range(sides):
            total += dot(r.ctxx[side, rows, :], flat(r.we, 0, side), NT)
        centred, scale = norm_stats(total)
        normed = centred * scale
        r.norm1[rows, :] = normed
        r.scale1[rows, :] = scale
        shifted = normed * r.vec[0:1, :] + r.vec[1:2, :]
        r.al[rows, :] = shifted.astype(BF16)
        sum2[rows, :] = shifted + r.vec[5:6, :]
        return carry

    lax.fori_loop(0, tiles, enter, 0)
    hook["entered"]()

    def grow(step, carry):
        whole = aligned(step, wide)
        bias = jnp.concatenate([r.vec[bias_at(step, side)] for side in range(sides)], axis=1)
        lay_out(step)

        def one(tile, inner):
            rows = aligned(tile, TILE)
            pre = dot(r.al[rows, :], r.plain_e[...]) + bias
            phi, slope = normal_parts(pre)
            low = (pre * phi).astype(BF16)
            r.act[rows, whole] = low
            r.slope[rows, whole] = slope.astype(BF16)
            sum2[rows, :] += dot(low, r.plain_s[...], NT)
            hook["grew"](step * tiles + tile)
            return inner

        lax.fori_loop(0, tiles, one, 0)
        return carry

    lax.fori_loop(0, steps, grow, 0)
    r.vsum[...] = jnp.zeros_like(r.vsum)

    def turn(tile, carry):
        rows = aligned(tile, TILE)
        centred, scale = norm_stats(sum2[rows, :])
        normed = centred * scale
        r.out[rows, :] = (normed * r.vec[2:3, :] + r.vec[3:4, :]).astype(BF16)
        grad = r.og[rows, :].astype(F32)
        r.vsum[2:3, :] += col_sum(grad * normed)
        r.vsum[3:4, :] += col_sum(grad)
        back = norm_back(grad * r.vec[2:3, :], normed, scale)
        r.vsum[5:6, :] += col_sum(back)
        r.dh2l[rows, :] = back.astype(BF16)
        dnorm[rows, :] = back
        hook["turned"](tile)
        return carry

    lax.fori_loop(0, tiles, turn, 0)
    r.flip[...] = r.dh2l[...].T

    def grad_shrink(step, carry):
        grad = dot(r.flip[...], r.act[:, aligned(step, wide)]).astype(BF16)
        put_both(r.gs, step, grad)
        hook["shrinks"](step)
        return carry

    lax.fori_loop(0, steps, grad_shrink, 0)

    def shrink(step, carry):
        whole = aligned(step, wide)
        lay_out(step)

        def one(tile, inner):
            rows = aligned(tile, TILE)
            grad = dot(r.dh2l[rows, :], r.plain_s[...])
            low = (grad * r.slope[rows, whole].astype(F32)).astype(BF16)
            r.slope[rows, whole] = low
            sums = col_sum(low.astype(F32))
            for side in range(sides):
                r.vsum[bias_at(step, side)] += sums[:, side * UNIT : (side + 1) * UNIT]
            dnorm[rows, :] += dot(low, r.plain_e[...], NT)
            hook["shrank"](step * tiles + tile)
            return inner

        lax.fori_loop(0, tiles, one, 0)
        return carry

    lax.fori_loop(0, steps, shrink, 0)

    def leave(tile, carry):
        rows = aligned(tile, TILE)
        grad = dnorm[rows, :]
        normed = r.norm1[rows, :]
        r.vsum[0:1, :] += col_sum(grad * normed)
        r.vsum[1:2, :] += col_sum(grad)
        back = norm_back(grad * r.vec[0:1, :], normed, r.scale1[rows, :])
        r.vsum[4:5, :] += col_sum(back)
        low = back.astype(BF16)
        r.dh1l[rows, :] = low
        for side in range(sides):
            r.dctx[side, rows, :] = dot(low, flat(r.we, 0, side)).astype(BF16)
        hook["left"](tile)
        return carry

    lax.fori_loop(0, tiles, leave, 0)
    r.flip[...] = r.al[...].T

    def grad_expand(step, carry):
        grad = dot(r.flip[...], r.slope[:, aligned(step, wide)]).astype(BF16)
        put_both(r.ge, 1 + step, grad)
        return carry

    lax.fori_loop(0, steps, grad_expand, 0)
    r.flip[...] = r.dh1l[...].T
    for side in range(sides):
        put(r.ge, 0, side, dot(r.flip[...], r.ctxx[side]).astype(BF16))


def feed_buffers(tokens, width, hidden):
    return [
        ("norm1", (tokens, width), F32),
        ("scale1", (tokens, 1), F32),
        ("sum2", (tokens, width), F32),
        ("al", (tokens, width), BF16),
        ("act", (tokens, hidden), BF16),
        ("slope", (tokens, hidden), BF16),
        ("dh2l", (tokens, width), BF16),
        ("flip", (width, tokens), BF16),
        ("plain_e", (width, 2 * UNIT), BF16),
        ("plain_s", (width, 2 * UNIT), BF16),
    ]


def feed_kernel(names, *refs):
    feed_math(types.SimpleNamespace(**dict(zip(names, refs))), {})


def feed_both(x, og, ctx, w_expand, w_shrink, vecs):
    tokens, width = x.shape
    chunks, sides = w_shrink.shape[0:2]
    outs = [
        ("out", (tokens, width), BF16),
        ("dctx", (sides, tokens, UNIT), BF16),
        ("dh1l", (tokens, width), BF16),
        ("ge", (chunks + 1, sides, width, UNIT), BF16),
        ("gs", (chunks, sides, width, UNIT), BF16),
        ("vsum", (VROWS, width), F32),
    ]
    scratch = feed_buffers(tokens, width, sides * chunks * UNIT)
    names = ["x", "og", "ctxx", "we", "ws", "vec"] + [item[0] for item in outs + scratch]
    vmem = pl.BlockSpec(memory_space=pltpu.VMEM)
    return pl.pallas_call(
        functools.partial(feed_kernel, names),
        out_shape=[jax.ShapeDtypeStruct(shape, kind) for _, shape, kind in outs],
        in_specs=[vmem] * 6,
        out_specs=[vmem] * len(outs),
        scratch_shapes=[pltpu.VMEM(shape, kind) for _, shape, kind in scratch],
        compiler_params=pltpu.CompilerParams(vmem_limit_bytes=VMEM_LIMIT),
        name="feed_both",
    )(x, og, ctx, w_expand, w_shrink, vecs)


def layer_kernel(heads, plan, inv_tokens, names, kept, used, feeds, *refs):
    r = types.SimpleNamespace(**dict(zip(names, refs)))
    cols = heads * HD
    tokens = r.x_all.shape[0]
    pages = tokens // PAGE
    own_tokens = tokens // 2
    tiles = own_tokens // TILE
    place = Place()
    place.signal()
    m, peer = place.m, place.peer["x"]
    at = (place.z, place.y)
    own = aligned(m, own_tokens)
    load_x = pltpu.make_async_copy(r.x_all.at[own, :], r.x, r.load_sem.at[0])
    load_og = pltpu.make_async_copy(r.og_all.at[own, :], r.og, r.load_sem.at[1])
    load_x.start()
    load_og.start()
    r.w[(0, place.c, 0, *at)] = r.attn[0].astype(BF16)
    for half in range(2):
        r.w[(1 + half, place.c, 0, *at)] = jnp.concatenate(
            [
                r.attn[1 + kind, :, head * HD : (head + 1) * HD].astype(BF16)
                for head in range(half * heads // 2, (half + 1) * heads // 2)
                for kind in range(2)
            ],
            axis=1,
        )
    r.box_gather[(0, place.c, 0, *at)] = r.shard_box[...]
    r.vec_gather[(0, place.c, m, *at)] = jnp.zeros((VROWS, 128), F32)
    table_at = (slice(0, r.vectors.shape[0]), slice(0, r.vectors.shape[1]))
    r.vec_gather[(0, place.c, m, *at, *table_at)] = r.vectors[...]
    r.we[(0, place.c, m, *at)] = r.merge[...].astype(BF16)
    for chunk in range(4):
        lanes = slice(chunk * UNIT, (chunk + 1) * UNIT)
        r.we[(1 + chunk, place.c, m, *at)] = r.expand[:, lanes].astype(BF16)
        r.ws[(chunk, place.c, m, *at)] = r.shrink[:, lanes].astype(BF16)
    place.wait()
    tree_v = Spread(place, r.vec_gather, 1, "xzy", r.v_sem)
    tree_b = Spread(place, r.box_gather, 1, "zy", r.b_sem)
    tree_a = Spread(place, r.w, 3, "zy", r.a_sem)
    tree_e = Spread(place, r.we, 5, "zyx", r.e_sem)
    tree_f = Spread(place, r.ws, 4, "xzy", r.f_sem)
    tree_e.lag = tree_f.lag = 2
    first, late = tree_a.events, 3
    begun = first - late

    def weights_event(number):
        tree_e.event(number)
        tree_f.event(number)

    def finish(chunk, value):
        r.sum_f[chunk] = value * inv_tokens

    back_f = Reduce(
        place, r.gs, None, dict(c=r.fc, y=r.fy, z=r.fz, x=r.fx), 4, "cyzx", r.back_sem, finish
    )
    back_f.lag, back_f.held_back = 2, 1

    def attention(*scoped):
        q = types.SimpleNamespace(**dict(zip([item[0] for item in kept + used] + ["x", "plain_w"], scoped)))
        load_all = pltpu.make_async_copy(r.x_all, q.x, r.load_sem.at[2])
        load_all.start()

        tree_v.stage(0, 0)

        def begin(number, carry):
            tree_v.event(number + 1)
            tree_b.event(number)

            @pl.when(number == 4)
            def _():
                r.vec[...] = rows_from_blocks(
                    r.vec_gather[...].reshape(-1, 128), r.pick[...], plan
                )
                r.box_out[...] = natural(r.box_gather, 0, 0).astype(BF16)
                attend_setup(heads, m, r.box_out, r.vec, q.box_heads, q.bias)

            tree_a.event(number)
            weights_event(number - late)
            pl.when(number == 0)(lambda: attend_trig(r.omega, r.corner, q.trig))
            return carry

        lax.fori_loop(0, first, begin, 0)
        for chunk in range(3):
            q.plain_w[chunk] = natural(r.w, chunk, 0)
        keep_w = pltpu.make_async_copy(q.plain_w, r.w_out, r.load_sem.at[3])
        keep_w.start()
        load_all.wait()

        def projected(page):
            weights_event(begun + page)

        piece = PAGE // 2

        def swap_copy(index):
            theirs = pages * (1 - m) + index
            start_rows(
                q.ctx.at[aligned(theirs, piece), :],
                r.ctxx.at[m, aligned(index, piece), :],
                piece,
                r.ctx_sem.at[0, index],
                r.ctx_sem.at[1, index],
                peer,
            )

        def attended(step, turn, pair):
            pl.when((step % 2 == 0) & (step < 8))(lambda: weights_event(begun + pages + step // 2))

            @pl.when(step == heads // 2 - 1)
            def _():
                swap_copy(2 - 2 * m)
                swap_copy(1)

            @pl.when(step == heads - 1)
            def _():
                swap_copy(2 * m)

        attend_math(
            heads,
            q,
            lambda chunk: q.plain_w[chunk],
            lambda turn: turn * m + (pages - 1 - turn) * (1 - m),
            projected,
            attended,
        )
        stores = [
            pltpu.make_async_copy(getattr(q, name), getattr(r, name + "_out"), r.store_sem.at[k])
            for k, (name, _, _) in enumerate(kept)
        ]
        for copy in stores:
            copy.start()
        r.ctxx[m] = q.ctx[own, :]
        for index in range(pages):
            copy = remote(
                q.ctx.at[aligned(index, piece), :],
                r.ctxx.at[1 - m, aligned(index, piece), :],
                r.ctx_sem.at[0, index],
                r.ctx_sem.at[1, index],
                peer,
            )
            copy.wait_recv()
            copy.wait_send()
        for copy in stores:
            copy.wait()
        keep_w.wait()

    pl.run_scoped(
        attention,
        *[pltpu.VMEM(shape, kind) for _, shape, kind in kept + used],
        pltpu.VMEM(r.x_all.shape, BF16),
        pltpu.VMEM(r.w_out.shape, BF16),
    )

    def feed(*scoped):
        q = types.SimpleNamespace(**dict(zip([item[0] for item in feeds], scoped)))
        for name in ("x", "og", "we", "ws", "vec", "ctxx", "dh1l", "ge", "gs", "vsum"):
            setattr(q, name, getattr(r, name))

        def out_copies(tile):
            rows = aligned(tile, TILE)
            there = r.out_full.at[pl.ds(pl.multiple_of(m * own_tokens + tile * TILE, TILE), TILE), :]
            return (
                pltpu.make_async_copy(q.out.at[rows, :], there, r.swap_sem.at[0, tile]),
                remote(q.out.at[rows, :], there, r.swap_sem.at[1, tile], r.swap_sem.at[2, tile], peer),
            )

        def dctx_copies(tile):
            rows = aligned(tile, TILE)
            there = r.dctx_full.at[pl.ds(pl.multiple_of(m * own_tokens + tile * TILE, TILE), TILE), :]
            return (
                pltpu.make_async_copy(q.dctx.at[m, rows, :], there, r.swap_sem.at[3, tile]),
                remote(
                    q.dctx.at[1 - m, rows, :], there, r.swap_sem.at[4, tile], r.swap_sem.at[5, tile], peer
                ),
            )

        def start_out(tile):
            rows = aligned(tile, TILE)
            there = r.out_full.at[pl.ds(pl.multiple_of(m * own_tokens + tile * TILE, TILE), TILE), :]
            out_copies(tile)[0].start()
            sems = r.swap_sem.at[1, tile], r.swap_sem.at[2, tile]
            start_rows(q.out.at[rows, :], there, TILE, *sems, peer)

        def start_dctx(tile):
            rows = aligned(tile, TILE)
            there = r.dctx_full.at[pl.ds(pl.multiple_of(m * own_tokens + tile * TILE, TILE), TILE), :]
            dctx_copies(tile)[0].start()
            sems = r.swap_sem.at[4, tile], r.swap_sem.at[5, tile]
            start_rows(q.dctx.at[1 - m, rows, :], there, TILE, *sems, peer)

        def grew(number):
            pl.when(number % 3 == 1)(lambda: weights_event(begun + pages + 4 + number // 3))

        def shrank(number):
            pl.when(number % 2 == 1)(lambda: back_f.event(4 + number // 2))

        load_x.wait()
        load_og.wait()
        feed_math(
            q,
            dict(
                grew=grew,
                turned=start_out,
                shrinks=lambda step: back_f.event(step),
                shrank=shrank,
                left=start_dctx,
            ),
        )
        back_f.rest()
        back_f.drain()
        for tile in range(tiles):
            for copy in out_copies(tile) + dctx_copies(tile):
                copy.wait()

    pl.run_scoped(feed, *[pltpu.VMEM(shape, kind) for _, shape, kind in feeds])
    for tree in (tree_v, tree_b, tree_a, tree_e, tree_f):
        tree.drain()


def layer_forward(x, og, corners, omega, pick, shards, plan, inv_tokens):
    tokens, width = x.shape
    cols = shards[1].shape[1]
    heads = cols // HD
    own = tokens // 2
    unit = (width // 16, UNIT)
    kept, used = attend_buffers(heads, tokens)
    feeds = feed_buffers(own, width, 8 * UNIT)
    feeds += [("out", (own, width), BF16), ("dctx", (2, own, UNIT), BF16)]
    free = pl.BlockSpec(memory_space=pl.ANY)
    vmem = pl.BlockSpec(memory_space=pltpu.VMEM)
    inputs = [("x_all", free), ("og_all", free), ("corner", vmem), ("omega", vmem), ("pick", vmem)]
    inputs += [(name, vmem) for name in ("attn", "shard_box", "vectors", "merge", "expand", "shrink")]
    outs = [(name + "_out", shape, kind, free) for name, shape, kind in kept]
    outs += [
        ("w_out", (3, width, cols), BF16, free),
        ("box_out", (PE, cols), BF16, vmem),
        ("out_full", (tokens, width), BF16, free),
        ("dctx_full", (tokens, cols), BF16, free),
        ("dh1l", (own, width), BF16, vmem),
        ("ge", (5, 2, 2, 4, 2, *unit), BF16, vmem),
        ("vsum", (VROWS, width), F32, vmem),
        ("sum_f", (4, *unit), F32, vmem),
    ]
    dma = pltpu.SemaphoreType.DMA
    scratch = [
        ("x", pltpu.VMEM((own, width), BF16)),
        ("og", pltpu.VMEM((own, width), BF16)),
        ("vec", pltpu.VMEM((VROWS, width), F32)),
        ("w", pltpu.VMEM((3, 2, 1, 4, 2, *unit), BF16)),
        ("box_gather", pltpu.VMEM((1, 2, 1, 4, 2, PE // 16, cols), F32)),
        ("vec_gather", pltpu.VMEM((1, 2, 2, 4, 2, VROWS, 128), F32)),
        ("we", pltpu.VMEM((5, 2, 2, 4, 2, *unit), BF16)),
        ("ws", pltpu.VMEM((4, 2, 2, 4, 2, *unit), BF16)),
        ("ctxx", pltpu.VMEM((2, own, cols), BF16)),
        ("gs", pltpu.VMEM((4, 2, 2, 4, 2, *unit), BF16)),
        ("fc", pltpu.VMEM((4, 2, 4, 2, *unit), BF16)),
        ("fy", pltpu.VMEM((4, 2, 4, *unit), BF16)),
        ("fz", pltpu.VMEM((4, 3, 2, *unit), BF16)),
        ("fx", pltpu.VMEM((4, *unit), BF16)),
        ("ctx_sem", dma((2, 3))),
        ("a_sem", dma((2, 3, SLOTS))),
        ("b_sem", dma((2, 1, SLOTS))),
        ("v_sem", dma((2, 1, SLOTS))),
        ("e_sem", dma((2, 5, SLOTS))),
        ("f_sem", dma((2, 4, SLOTS))),
        ("back_sem", dma((2, 4, SLOTS))),
        ("load_sem", dma((4,))),
        ("store_sem", dma((len(kept),))),
        ("swap_sem", dma((6, own // TILE))),
    ]
    names = [item[0] for item in inputs + outs + scratch]
    return pl.pallas_call(
        functools.partial(layer_kernel, heads, plan, inv_tokens, names, kept, used, feeds),
        out_shape=[jax.ShapeDtypeStruct(shape, kind) for _, shape, kind, _ in outs],
        in_specs=[item[1] for item in inputs],
        out_specs=[item[3] for item in outs],
        scratch_shapes=[item[1] for item in scratch],
        compiler_params=pltpu.CompilerParams(
            vmem_limit_bytes=VMEM_LIMIT, collective_id=0, has_side_effects=True
        ),
        name="layer_forward",
    )(x, og, corners, omega, pick, *shards)


def pair_place(cols):
    spot = lax.broadcasted_iota(jnp.int32, (cols, 2 * cols), 0)
    lane = lax.broadcasted_iota(jnp.int32, (cols, 2 * cols), 1)
    target = ((spot >> 6) << 7) + HD + (spot & (HD - 1))
    return jnp.where(lane == target, 1.0, 0.0)


def exact_dot(lhs, rhs, dims=NN):
    return lax.dot_general(
        lhs, rhs, dims, precision=lax.Precision.HIGHEST, preferred_element_type=F32
    )


def attend_back_kernel(heads, plan, inv_tokens, *refs):
    inputs, refs = refs[:12], refs[12:]
    if plan is not None:
        load_sem, held, refs = refs[-1], refs[-13:-1], refs[:-13]
        loads = [
            pltpu.make_async_copy(src, dst, load_sem.at[k]) for k, (src, dst) in enumerate(zip(inputs, held))
        ]
        early = (0, 2, 7, 11)
        for k in sorted(range(12), key=lambda k: k not in early):
            loads[k].start()
        inputs = held
    x_ref, w_ref, box_ref, *inputs = inputs
    qa_ref, qtok_ref, kvtok_ref, kt_ref, kft_ref, trig_ref, ctxt_ref, log_ref, dctx_ref = inputs
    cols = heads * HD
    tokens = x_ref.shape[0]
    pages = tokens // PAGE
    m = lax.axis_index("mp")
    piece = PAGE // 2
    pieces = 2 * pages
    lane = lax.broadcasted_iota(jnp.int32, (1, 2 * HD), 1)
    lower = lane < HD
    if plan is None:
        inp_ref, gw_ref, gbox_ref, qvsum_ref, *refs = refs
        kftok, dctxt, boxt, dtok, xt, gbox = refs
        before, after = 0, 0

        def background(number):
            pass
    else:
        dh1_ref, vsum_ref, sumf_ref, pick_ref, full_e, *refs = refs
        inp_ref, sum_e, sum_a, sum_b, sum_v, norm_ref, *refs = refs
        kftok, dctxt, boxt, dtok, xt, gbox, *refs = refs
        came, total_e, full_a, full_b, full_v, land_v, norms, *refs = refs
        ec, ey, ez, ex, ac, ay, az, bc, by, bz, *refs = refs
        e_sem, a_sem, b_sem, v_sem, n_sem, i_sem, loc_sem = refs
        place = Place()
        place.signal_all()
        fill = pltpu.make_async_copy(full_e.at[:, place.c], total_e, loc_sem.at[0])
        fill.start()
        place.wait_all()

        def finish(out):
            def put(chunk, value):
                out[chunk] = value * inv_tokens

            return put

        tree_e = Reduce(
            place, full_e, total_e, dict(c=ec, y=ey, z=ez, x=ex), 5, "cyzx", e_sem, finish(sum_e)
        )
        tree_e.lag, tree_e.held_back = 2, 1
        tree_a = Reduce(place, full_a, None, dict(c=ac, y=ay, z=az), 3, "cyz", a_sem, finish(sum_a))
        tree_b = Reduce(place, full_b, None, dict(c=bc, y=by, z=bz), 1, "cyz", b_sem, finish(sum_b))

        def block_of(rank):
            r = rank % 16
            return full_v.at[rank // 16, r // 4, (r // 2) % 2, r % 2]

        spot = (place.m, place.z, place.y, place.c)
        all_v = Everyone(place, block_of, lambda step: land_v.at[step - 1], v_sem)
        all_n = Everyone(place, lambda rank: norms.at[spot], lambda step: norms.at[spot], n_sem)

        def background(number):
            tree_e.event(number)

        background(0)
        fill.wait()
        for k in early:
            loads[k].wait()

    boxt[...] = box_ref[...].T
    gbox[...] = jnp.zeros_like(gbox)

    def prepare(page, carry):
        rows = aligned(page, PAGE)
        kftok[rows, :] = kft_ref[:, rows].T
        dctxt[:, rows] = dctx_ref[rows, :].T
        xt[:, rows] = x_ref[rows, :].T
        if plan is not None:
            pl.when(page > 0)(lambda: background(page))
        return carry

    lax.fori_loop(0, pages, prepare, 0)
    if plan is not None:
        for k in range(12):
            if k not in early:
                loads[k].wait()

    def attend(step, carry):
        page, pair = step // (heads // 2), step % (heads // 2)
        rows = aligned(page, PAGE)
        own, partner = turn_factors(trig_ref[:, rows])
        pair_lanes = aligned(pair, 2 * HD)
        query_pair = qtok_ref[rows, pair_lanes]
        dctx_pair = dctx_ref[rows, pair_lanes]
        halves = []
        boxes = []
        blank = jnp.zeros((HD, PAGE), BF16)
        for side in range(2):
            head = pair * 2 + side
            lanes = aligned(head, 2 * HD)
            key_value = kvtok_ref[rows, lanes]
            left = jnp.concatenate([kftok[rows, :], key_value], axis=1)
            score = dot(left, jnp.concatenate([qa_ref[head, :, rows], blank], axis=0))
            prob = jnp.exp(score - log_ref[head, :, rows])
            prob_low = prob.astype(BF16)
            head_rows = pl.ds(pl.multiple_of(head * HD, HD), HD)
            dctx_head = dctxt[head_rows, rows]
            grad_prob = dot(
                key_value, jnp.concatenate([blank, dctx_head], axis=0)
            )
            inner = col_sum(dctx_head.astype(F32) * ctxt_ref[head_rows, rows].astype(F32))
            grad_score = (prob * (grad_prob - inner)).astype(BF16)
            if side == 0:
                both = jnp.concatenate([query_pair[:, 0:HD], dctx_pair[:, 0:HD]], axis=1)
            else:
                both = jnp.concatenate([query_pair[:, HD:], dctx_pair[:, HD:]], axis=1)
            from_score = dot(grad_score, both)
            from_prob = dot(prob_low, both)
            grad_kv = jnp.where(lower, from_score, from_prob).astype(BF16)
            dtok[rows, pl.ds(pl.multiple_of(cols + head * 2 * HD, 2 * HD), 2 * HD)] = grad_kv
            keys = jnp.concatenate([kft_ref[:, rows], kt_ref[head_rows, rows]], axis=0)
            grad_query = dot(keys, grad_score) * HD ** (-0.5)
            feat = grad_query[0:PE]
            proj = (feat * own - swap_blocks(feat) * partner).astype(BF16)
            halves.append(grad_query[PE:] + dot(boxt[head_rows, :], proj))
            boxes.append(dot(proj, query_pair))
        gbox[:, pair_lanes] += jnp.where(lower, boxes[0], boxes[1])
        dtok[rows, pair_lanes] = jnp.concatenate(halves, axis=0).astype(BF16).T
        return carry

    def spread(page):
        rows = aligned(page, PAGE)
        return sum(
            dot(dtok[rows, chunk * UNIT : (chunk + 1) * UNIT], w_ref[chunk], NT) for chunk in range(3)
        )

    if plan is None:
        lax.fori_loop(0, pages * (heads // 2), attend, 0)
        gbox_ref[...] = gbox[...] * HD**0.5

        def spread_page(page, carry):
            inp_ref[aligned(page, PAGE), :] = spread(page)
            return carry

        lax.fori_loop(0, pages, spread_page, 0)

        def gather(step, carry):
            lanes = aligned(step, UNIT)
            gw_ref[step] = dot(xt[...], dtok[:, lanes]).astype(BF16)
            qvsum_ref[0:1, lanes] = col_sum(dtok[:, lanes].astype(F32))
            return carry

        lax.fori_loop(0, 3, gather, 0)
        return

    def swap(index):
        rows = aligned(index, piece)
        return remote(
            inp_ref.at[rows, :], came.at[rows, :], i_sem.at[0, index], i_sem.at[1, index], place.peer["x"]
        )

    def attend_and_send(step, carry):
        attend(step, carry)
        page = step // (heads // 2)

        @pl.when(step % (heads // 2) == heads // 2 - 1)
        def _():
            value = spread(page)
            for half in range(2):
                index = 2 * page + half
                rows = aligned(index, piece)
                own = index // pages == m
                spot = aligned(index % pages, piece)
                extra = jnp.where(own, dh1_ref[spot, :].astype(F32), 0.0)
                inp_ref[rows, :] = (value[half * piece : (half + 1) * piece] + extra).astype(BF16)
                start_rows(
                    inp_ref.at[rows, :],
                    came.at[rows, :],
                    piece,
                    i_sem.at[0, index],
                    i_sem.at[1, index],
                    place.peer["x"],
                )

        background(step + pages)
        return carry

    lax.fori_loop(0, pages * (heads // 2), attend_and_send, 0)
    put_natural(full_b, 0, 0, gbox[...] * HD**0.5)

    def gather(step, carry):
        grad = dot(xt[...], dtok[:, aligned(step, UNIT)]).astype(BF16)
        put_natural(full_a, step, 0, grad)
        tree_a.event(step)
        tree_b.event(step)
        return carry

    lax.fori_loop(0, 3, gather, 0)

    sums = jnp.concatenate(
        [
            col_sum(dtok[:, chunk * UNIT : (chunk + 1) * UNIT].astype(F32)) for chunk in range(3)
        ],
        axis=1,
    )
    values = exact_dot(jnp.broadcast_to(sums[:, cols:], (8, 2 * cols)), pair_place(cols), NT)
    pair = jnp.concatenate([sums[:, 0:cols], values[0:1]], axis=0)
    blank = jnp.zeros_like(pair)
    pair = jnp.where(
        m == 0, jnp.concatenate([pair, blank], axis=1), jnp.concatenate([blank, pair], axis=1)
    )
    table = jnp.concatenate([vsum_ref[0:6, :], pair, vsum_ref[8:, :]], axis=0)
    mp_count, dp_count = plan
    width = table.shape[1]
    each = width // (mp_count * dp_count)
    wide_lane = lax.broadcasted_iota(jnp.int32, (VROWS, width), 1)
    for side in range(mp_count):
        parts = []
        for r in range(dp_count):
            first = (r * mp_count + side) * each
            parts.append(jnp.where((wide_lane >= first) & (wide_lane < first + each), table, 0.0))
        block = exact_dot(jnp.concatenate(parts, axis=0), pick_ref[...], NT)
        full_v[side] = block.reshape(full_v.shape[1:])
    all_v.start()

    def tail(number, carry):
        tree_a.event(number)
        tree_b.event(number)
        return carry

    lax.fori_loop(3, tree_a.events, tail, 0)
    tree_e.rest()
    all_v.wait()
    total_v = full_v[spot] + jnp.sum(land_v[...], axis=0)
    sum_v[0] = total_v * inv_tokens

    square = sum(jnp.sum(out[...] * out[...]) for out in (sum_e, sumf_ref, sum_a, sum_b, sum_v))
    norms[spot] = jnp.full((8, 128), square, F32)
    all_n.start()

    def final(number, carry):
        rows = aligned(number, piece)
        swap(number).wait()
        inp_ref[rows, :] = (inp_ref[rows, :].astype(F32) + came[rows, :].astype(F32)).astype(BF16)
        return carry

    lax.fori_loop(0, pieces, final, 0)
    all_n.wait()
    every = norms[...].reshape(-1, 8, 128)
    norm_ref[...] = jnp.sqrt(sum(every[k] for k in range(every.shape[0])))
    for tree in (tree_e, tree_a, tree_b):
        tree.drain()


def attend_backward(x, weight, box, kept, dctx, plan, inv_tokens, more=()):
    tokens, width = x.shape
    cols = weight.shape[-1]
    heads = cols // HD
    vmem = pl.BlockSpec(memory_space=pltpu.VMEM)
    scratch = [
        pltpu.VMEM((tokens, PE), BF16),
        pltpu.VMEM((cols, tokens), BF16),
        pltpu.VMEM((cols, PE), BF16),
        pltpu.VMEM((tokens, 3 * cols), BF16),
        pltpu.VMEM((width, tokens), BF16),
        pltpu.VMEM((PE, cols), F32),
    ]
    in_specs = [vmem] * 12
    if plan is None:
        shapes = [
            ((tokens, width), F32),
            ((3, width, cols), BF16),
            ((PE, cols), F32),
            ((8, 3 * cols), F32),
        ]
        extra = {}
    else:
        free = pl.BlockSpec(memory_space=pl.ANY)
        in_specs = [free] * 12 + [vmem] * 4 + [free]
        rows = width // 16
        unit = (rows, UNIT)
        tile = (PE // 16, cols)
        small = (VROWS, 128)
        shapes = [
            ((tokens, width), BF16),
            ((5, *unit), F32),
            ((3, *unit), F32),
            ((1, *tile), F32),
            ((1, *small), F32),
            ((8, 128), F32),
        ]
        scratch += [
            pltpu.VMEM((tokens, width), BF16),
            pltpu.VMEM((5, 2, 4, 2, *unit), BF16),
            pltpu.VMEM((3, 2, 1, 4, 2, *unit), BF16),
            pltpu.VMEM((1, 2, 1, 4, 2, *tile), F32),
            pltpu.VMEM((2, 4, 2, 2, *small), F32),
            pltpu.VMEM((31, *small), F32),
            pltpu.VMEM((2, 4, 2, 2, 8, 128), F32),
            pltpu.VMEM((5, 2, 4, 2, *unit), BF16),
            pltpu.VMEM((5, 2, 4, *unit), BF16),
            pltpu.VMEM((5, 3, 2, *unit), BF16),
            pltpu.VMEM((5, *unit), BF16),
            pltpu.VMEM((3, 4, 2, *unit), BF16),
            pltpu.VMEM((3, 4, *unit), BF16),
            pltpu.VMEM((3, 3, *unit), BF16),
            pltpu.VMEM((1, 4, 2, *tile), F32),
            pltpu.VMEM((1, 4, *tile), F32),
            pltpu.VMEM((1, 3, *tile), F32),
            pltpu.SemaphoreType.DMA((2, 5, SLOTS)),
            pltpu.SemaphoreType.DMA((2, 3, SLOTS)),
            pltpu.SemaphoreType.DMA((2, 1, SLOTS)),
            pltpu.SemaphoreType.DMA((2, 31)),
            pltpu.SemaphoreType.DMA((2, 31)),
            pltpu.SemaphoreType.DMA((2, 2 * (tokens // PAGE))),
            pltpu.SemaphoreType.DMA((2,)),
        ]
        scratch += [pltpu.VMEM(array.shape, array.dtype) for array in (x, weight, box, *kept, dctx)]
        scratch.append(pltpu.SemaphoreType.DMA((12,)))
        extra = dict(collective_id=2, has_side_effects=True)
    return pl.pallas_call(
        functools.partial(attend_back_kernel, heads, plan, inv_tokens),
        out_shape=[jax.ShapeDtypeStruct(s, d) for s, d in shapes],
        in_specs=in_specs,
        out_specs=[vmem] * len(shapes),
        scratch_shapes=scratch,
        compiler_params=pltpu.CompilerParams(vmem_limit_bytes=VMEM_LIMIT, **extra),
        cost_estimate=pl.CostEstimate(flops=4 * 10**10, bytes_accessed=10**8, transcendentals=10**7),
        name="attend_backward",
    )(x, weight, box, *kept, dctx, *more)


def adam_step(master, first, second, gradient, rate, decay):
    new_first = BETA_ONE * first + (1.0 - BETA_ONE) * gradient
    new_second = BETA_TWO * second + (1.0 - BETA_TWO) * gradient * gradient
    first_hat = new_first / (1.0 - BETA_ONE**STEP)
    second_hat = new_second / (1.0 - BETA_TWO**STEP)
    new_master = master - rate * (first_hat / (jnp.sqrt(second_hat) + ADAM_EPS) + decay * master)
    return (new_first, new_second, new_master)


def adam_kernel(heads, norm_ref, *refs):
    sum_e, sum_f, sum_a, sum_b, sum_v, *refs = refs
    states, outs = refs[:18], refs[18:]
    outs[-1][...] = norm_ref[0:1, 0:1]
    clip = CLIP_LIMIT / jnp.maximum(norm_ref[0:1, 0:1], CLIP_LIMIT)

    def update(first, out, gradient, at, rate, decay):
        news = adam_step(*(ref[at] for ref in states[first : first + 3]), gradient * clip, rate, decay)
        for ref, new in zip(outs[out : out + 3], news):
            ref[at] = new
        if decay:
            outs[out + 3][at] = news[2].astype(BF16)

    def heads_of(kind):
        half = heads // 2
        return jnp.concatenate(
            [
                sum_a[1 + head // half, :, (2 * (head % half) + kind) * HD : (2 * (head % half) + kind + 1) * HD]
                for head in range(heads)
            ],
            axis=1,
        )

    for index, gradient in enumerate((sum_a[0], heads_of(0), heads_of(1))):
        update(0, 0, gradient, index, RATE_MATRIX, WEIGHT_DECAY)
    update(3, 4, sum_b[0], ALL, RATE_MATRIX, WEIGHT_DECAY)
    update(6, 8, sum_e[0], ALL, RATE_MATRIX, WEIGHT_DECAY)
    for chunk in range(4):
        lanes = (ALL, slice(chunk * UNIT, (chunk + 1) * UNIT))
        update(9, 12, sum_e[1 + chunk], lanes, RATE_MATRIX, WEIGHT_DECAY)
        update(12, 16, sum_f[chunk], lanes, RATE_MATRIX, WEIGHT_DECAY)
    rows, each = states[15].shape
    update(15, 20, sum_v[0, 0:rows, 0:each], ALL, RATE_VECTOR, 0.0)


def adam_all(norm, sums, states):
    shapes = []
    for first in range(0, 18, 3):
        shapes += [(states[first].shape, F32)] * 3
        if first < 15:
            shapes.append((states[first].shape, BF16))
    vmem = pl.BlockSpec(memory_space=pltpu.VMEM)
    shapes.append(((1, 1), F32))
    return pl.pallas_call(
        functools.partial(adam_kernel, states[0].shape[2] // HD),
        out_shape=[jax.ShapeDtypeStruct(s, d) for s, d in shapes],
        in_specs=[vmem] * (6 + len(states)),
        out_specs=[vmem] * len(shapes),
        compiler_params=pltpu.CompilerParams(vmem_limit_bytes=VMEM_LIMIT),
        name="adam_all",
    )(norm, *sums, *states)


def pack_qkv(shard):
    rows, cols = shard.shape[1:]
    heads = cols // HD
    pairs = jnp.stack([shard[1].reshape(rows, heads, HD), shard[2].reshape(rows, heads, HD)], axis=2)
    pairs = pairs.reshape(rows, 2, cols)
    return jnp.stack([shard[0], pairs[:, 0], pairs[:, 1]])


def unpack_qkv(packed):
    rows, cols = packed.shape[1:]
    pairs = jnp.concatenate([packed[1], packed[2]], axis=1).reshape(rows, cols // HD, 2, HD)
    return jnp.stack(
        [packed[0], pairs[:, :, 0].reshape(rows, cols), pairs[:, :, 1].reshape(rows, cols)]
    )


def to_chunks(shard):
    rows = shard.shape[0]
    return shard.reshape(rows, -1, UNIT).transpose(1, 0, 2)


def from_chunks(chunks):
    return chunks.transpose(1, 0, 2).reshape(chunks.shape[1], -1)


def on_device(
    layer_input,
    page_boxes,
    output_grad,
    attn_proj,
    attn_first,
    attn_second,
    box_proj,
    box_first,
    box_second,
    merge_proj,
    merge_first,
    merge_second,
    expand_proj,
    expand_first,
    expand_second,
    shrink_proj,
    shrink_first,
    shrink_second,
    vectors,
    vector_first,
    vector_second,
):
    mp_count = lax.axis_size("mp")
    dp_count = lax.axis_size("dp")
    mp_index = lax.axis_index("mp")
    tokens, width = layer_input.shape
    cols = attn_proj.shape[2]
    heads = cols // HD
    own_tokens = tokens // mp_count
    inv_tokens = 1.0 / (tokens * dp_count)

    corners = page_boxes.T
    omega = (10000.0 ** (-np.arange(FREQS, dtype=np.float64) / FREQS)).astype(np.float32)[:, None]
    omega = jnp.asarray(omega)
    plan = (mp_count, dp_count) if dp_count == 16 and mp_count == 2 else None
    if plan is not None:
        each = vectors.shape[1]
        pick = np.zeros((128, width), np.float32)
        pick[np.arange(width) % each, np.arange(width)] = 1.0
        pick = jnp.asarray(pick)
        *kept, w_qkv, w_box, layer_out, dctx, dh1, g_expand, vec_sum, sum_f = layer_forward(
            layer_input,
            output_grad,
            corners,
            omega,
            pick,
            (attn_proj, box_proj, vectors, merge_proj.T, expand_proj, shrink_proj.T),
            plan,
            inv_tokens,
        )
        input_grad, sum_e, sum_a, sum_b, sum_v, norm = attend_backward(
            layer_input,
            w_qkv,
            w_box,
            kept,
            dctx,
            plan,
            inv_tokens,
            (dh1, vec_sum, sum_f, pick, g_expand),
        )
        merge = [merge_proj.T, merge_first.T, merge_second.T]
        shrink = [shrink_proj.T, shrink_first.T, shrink_second.T]
        *results, norm = adam_all(
            norm,
            (sum_e, sum_f, sum_a, sum_b, sum_v),
            [attn_proj, attn_first, attn_second, box_proj, box_first, box_second, *merge]
            + [expand_proj, expand_first, expand_second, *shrink, vectors, vector_first, vector_second],
        )
        turned = (8, 9, 10, 11, 16, 17, 18, 19)
        results = [out.T if k in turned else out for k, out in enumerate(results)]
        return (layer_out, input_grad, norm.reshape(()), *results)
    shard_qkv = pack_qkv(attn_proj).astype(BF16)
    shard_e = jnp.concatenate([merge_proj.T[None], to_chunks(expand_proj)]).astype(BF16)
    shard_f = to_chunks(shrink_proj.T).astype(BF16)
    w_qkv = lax.all_gather(shard_qkv, "dp", axis=1, tiled=True)
    w_box = lax.all_gather(box_proj.astype(BF16), "dp", axis=0, tiled=True)
    w_expand = lax.all_gather(lax.all_gather(shard_e, "dp", axis=1, tiled=True), "mp", axis=1)
    w_shrink = lax.all_gather(lax.all_gather(shard_f, "dp", axis=1, tiled=True), "mp", axis=1)
    vecs = lax.all_gather(vectors, ("dp", "mp"), axis=1, tiled=True)
    vecs = jnp.pad(vecs, ((0, VROWS - vecs.shape[0]), (0, 0)))
    *kept, context = attend_forward(layer_input, corners, omega, w_qkv, w_box, vecs)
    context = lax.all_to_all(
        context.reshape(mp_count, own_tokens, cols), "mp", split_axis=0, concat_axis=0
    )

    def own_rows(array):
        return lax.dynamic_slice_in_dim(array, mp_index * own_tokens, own_tokens)

    layer_out, dctx, dh1, g_expand, g_shrink, vec_sum = feed_both(
        own_rows(layer_input), own_rows(output_grad), context, w_expand, w_shrink, vecs
    )
    g_feed = jnp.concatenate([g_expand, g_shrink])
    layer_out = lax.all_gather(layer_out, "mp", axis=0, tiled=True)
    dctx = lax.all_to_all(dctx, "mp", split_axis=0, concat_axis=0).reshape(tokens, cols)
    part, g_qkv, g_box, qkv_sum = attend_backward(
        layer_input, w_qkv, w_box, kept, dctx, None, inv_tokens
    )
    own_part = lax.psum_scatter(part.astype(BF16), "mp", scatter_dimension=0, tiled=True)
    own_grad = (own_part.astype(F32) + dh1).astype(BF16)
    input_grad = lax.all_gather(own_grad, "mp", axis=0, tiled=True)
    shard_attn = unpack_qkv(
        lax.psum_scatter(g_qkv, "dp", scatter_dimension=1, tiled=True).astype(F32) * inv_tokens
    )
    shard_box = lax.psum_scatter(g_box, "dp", scatter_dimension=0, tiled=True) * inv_tokens
    sum_feed = lax.psum_scatter(g_feed, "dp", scatter_dimension=2, tiled=True)
    sum_feed = lax.psum_scatter(sum_feed, "mp", scatter_dimension=1, tiled=True)[:, 0]
    sum_feed = sum_feed.astype(F32) * inv_tokens
    sum_expand, sum_shrink = sum_feed[0:5], sum_feed[5:]

    def placed(row):
        return lax.dynamic_update_slice_in_dim(
            jnp.zeros((width,), F32), row, mp_index * cols, 0
        )[None, :]

    value_sum = qkv_sum[0, cols:].reshape(heads, 2, HD)[:, 1].reshape(cols)
    vector_grad = jnp.concatenate(
        [vec_sum[0:6], placed(qkv_sum[0, 0:cols]), placed(value_sum), vec_sum[8:12]]
    )
    vector_shard = (
        lax.psum_scatter(vector_grad, ("dp", "mp"), scatter_dimension=1, tiled=True) * inv_tokens
    )
    square = sum(
        jnp.sum(shard * shard)
        for shard in (shard_attn, shard_box, sum_expand, sum_shrink, vector_shard)
    )
    grad_norm = jnp.sqrt(lax.psum(square, ("dp", "mp")))
    shard_merge = sum_expand[0].T
    shard_expand = from_chunks(sum_expand[1:])
    shard_shrink = from_chunks(sum_shrink).T
    clip_scale = CLIP_LIMIT / jnp.maximum(grad_norm, CLIP_LIMIT)
    results = [layer_out, input_grad, grad_norm]
    for master, first, second, shard in (
        (attn_proj, attn_first, attn_second, shard_attn),
        (box_proj, box_first, box_second, shard_box),
        (merge_proj, merge_first, merge_second, shard_merge),
        (expand_proj, expand_first, expand_second, shard_expand),
        (shrink_proj, shrink_first, shrink_second, shard_shrink),
    ):
        new_first, new_second, new_master = adam_step(
            master, first, second, shard * clip_scale, RATE_MATRIX, WEIGHT_DECAY
        )
        results += [new_first, new_second, new_master, new_master.astype(BF16)]
    results += adam_step(
        vectors, vector_first, vector_second, vector_shard * clip_scale, RATE_VECTOR, 0.0
    )
    return tuple(results)


def solution(mesh):
    rows = P("dp", None)
    attn = P(None, "dp", "mp")
    tall = P("dp", "mp")
    wide = P("mp", "dp")
    vector = P(None, ("dp", "mp"))
    in_specs = (rows,) * 3 + (attn,) * 3 + (tall,) * 3 + (wide,) * 3 + (tall,) * 3 + (wide,) * 3
    in_specs += (vector,) * 3
    out_specs = (rows, rows, P()) + (attn,) * 4 + (tall,) * 4 + (wide,) * 4 + (tall,) * 4
    out_specs += (wide,) * 4 + (vector,) * 3
    return jax.shard_map(
        on_device, mesh=mesh, in_specs=in_specs, out_specs=out_specs, check_vma=False
    )
```

```python
import functools
import types

import jax
import jax.numpy as jnp
import numpy as np
from jax import lax
from jax.experimental import pallas as pl
from jax.experimental.pallas import tpu as pltpu
from jax.sharding import PartitionSpec as P

HD = 64
FREQS = 32
PE = 128
PAGE = 512
STEP = 10

NORM_EPS = 1e-12
CLIP_LIMIT = 0.1
BETA_ONE = 0.9
BETA_TWO = 0.999
ADAM_EPS = 1e-08
RATE_MATRIX = 0.05
RATE_VECTOR = 0.5
WEIGHT_DECAY = 0.01

F32 = jnp.float32
BF16 = jnp.bfloat16
VMEM_LIMIT = 60 * 1024 * 1024

NN = (((1,), (0,)), ((), ()))
NT = (((1,), (1,)), ((), ()))
TN = (((0,), (0,)), ((), ()))


def dot(lhs, rhs, dims=NN):
    return lax.dot_general(lhs, rhs, dims, preferred_element_type=F32)


def aligned(index, size):
    return pl.ds(pl.multiple_of(index * size, size), size)


def swap_blocks(feat):
    return jnp.concatenate(
        [
            feat[FREQS : 2 * FREQS],
            feat[0:FREQS],
            feat[3 * FREQS :],
            feat[2 * FREQS : 3 * FREQS],
        ],
        axis=0,
    )


def turn_factors(trig):
    cos_x, sin_x = trig[0:FREQS], trig[FREQS : 2 * FREQS]
    cos_y, sin_y = trig[2 * FREQS : 3 * FREQS], trig[3 * FREQS :]
    return (
        jnp.concatenate([sin_x, sin_x, sin_y, sin_y], axis=0),
        jnp.concatenate([cos_x, -cos_x, cos_y, -cos_y], axis=0),
    )


MESH = pl.DeviceIdType.MESH
ALL = slice(None)
UNIT = 384


class Place:
    def __init__(self):
        rank = lax.axis_index("dp")
        self.m = lax.axis_index("mp")
        self.z = rank // 4
        self.y = (rank // 2) % 2
        self.c = rank % 2
        self.peer = {
            "x": (rank, 1 - self.m),
            "y": (rank + 2 - 4 * self.y, self.m),
            "c": (rank + 1 - 2 * self.c, self.m),
        }
        self.far = [((rank + 4 * step) % 16, self.m) for step in (1, 2, 3)]

    def signal(self):
        barrier = pltpu.get_barrier_semaphore()
        for device in list(self.peer.values()) + self.far:
            pl.semaphore_signal(barrier, inc=1, device_id=device, device_id_type=MESH)

    def wait(self):
        pl.semaphore_wait(pltpu.get_barrier_semaphore(), 6)

    def signal_all(self):
        barrier = pltpu.get_barrier_semaphore()
        rank = self.m * 16 + lax.axis_index("dp")

        def one(step, carry):
            to = (rank + step) % 32
            pl.semaphore_signal(barrier, inc=1, device_id=(to % 16, to // 16), device_id_type=MESH)
            return carry

        lax.fori_loop(1, 32, one, 0)

    def wait_all(self):
        pl.semaphore_wait(pltpu.get_barrier_semaphore(), 31)


PART = 256


def start_rows(src, dst, rows, send_sem, recv_sem, device):
    for first in range(0, rows, PART):
        part = pl.ds(first, PART)
        remote(src.at[part, :], dst.at[part, :], send_sem, recv_sem, device).start()


def remote(src, dst, send_sem, recv_sem, device):
    return pltpu.make_async_remote_copy(
        src_ref=src,
        dst_ref=dst,
        send_sem=send_sem,
        recv_sem=recv_sem,
        device_id=device,
        device_id_type=MESH,
    )


SLOT = {"c": 0, "z": 1, "y": 4, "x": 5}
SLOTS = 6
SENT = (0, 1, 1, 1, 4, 5)


class Tree:
    lag = 1
    held_back = 0
    together = False

    def stage(self, index, chunk):
        raise NotImplementedError

    def event(self, number):
        for index in range(self.count - 1 - self.held_back, -1, -1):
            chunk = number - index * self.lag
            if self.together:

                @pl.when(chunk == 0)
                def _(index=index):
                    for each in range(self.chunks):
                        self.stage(index, each)

            elif self.chunks == 1:
                pl.when(chunk == 0)(lambda index=index: self.stage(index, 0))
            else:
                pl.when((chunk >= 0) & (chunk < self.chunks))(
                    lambda index=index, chunk=chunk: self.stage(index, chunk)
                )

    @property
    def events(self):
        return self.chunks + (self.count - 1 - self.held_back) * self.lag

    def rest(self):
        def one(chunk, carry):
            self.stage(self.count - 1, chunk)
            return carry

        lax.fori_loop(0, self.chunks, one, 0)


class Spread(Tree):
    def __init__(self, place, ref, chunks, order, sems):
        self.chunks, self.ref, self.sems, self.place = chunks, ref, sems, place
        have = {"x": place.m if "x" in order else 0, "z": place.z, "y": place.y}
        mine = {"x": place.m, "y": place.y}
        self.own = have
        self.steps, self.axes = [], order
        for axis in order:
            if axis == "z":
                sends = [(have, place.far[step - 1], step) for step in (1, 2, 3)]
                waits = [(dict(have, z=(place.z + 4 - step) % 4), step) for step in (1, 2, 3)]
            else:
                sends = [(have, place.peer[axis], SLOT[axis])]
                waits = [(dict(have, **{axis: 1 - mine[axis]}), SLOT[axis])]
            self.steps.append((sends, waits))
            have = dict(have, **{axis: ALL})
        self.other = place.peer["c"]
        self.count = len(self.steps) + 2

    def _copy(self, chunk, have, device, slot):
        came = 0 if chunk == ALL else chunk
        block = self.ref.at[chunk, self.place.c, have["x"], have["z"], have["y"]]
        sent = self.sems.at[0, 0, SENT[slot]]
        return remote(block, block, sent, self.sems.at[1, came, slot], device)

    def _plane(self, chunk, core):
        plane = self.ref.at[chunk, core]
        came = 0 if chunk == ALL else chunk
        return remote(plane, plane, self.sems.at[0, 0, 0], self.sems.at[1, came, 0], self.other)

    def stage(self, index, chunk):
        if index == self.count - 1:
            self._plane(chunk, 1 - self.place.c).wait_recv()
            return
        came = [self.own]
        if index > 0:
            came = []
            for have, slot in self.steps[index - 1][1]:
                self._copy(chunk, have, self.other, slot).wait_recv()
                came.append(have)
        if index < len(self.steps):
            for have, device, slot in self.steps[index][0]:
                self._copy(chunk, have, device, slot).start()
        for have in came:
            self._copy(chunk, have, self.other, 0).start()

    def drain(self):
        for axis, (sends, _) in zip(self.axes, self.steps):
            have, _, slot = sends[0]
            if axis == "z":
                have = dict(have, z=slice(0, 3))
            self._copy(ALL, have, self.other, slot).wait_send()
        self._plane(ALL, self.place.c).wait_send()


RANKS = [(c, z, y) for z in range(4) for y in range(2) for c in range(2)]


def natural(ref, chunk, side):
    return jnp.concatenate([ref[chunk, c, side, z, y] for c, z, y in RANKS], axis=0)


def put_natural(ref, chunk, side, value):
    rows = value.shape[0] // len(RANKS)
    for spot, (c, z, y) in enumerate(RANKS):
        ref[chunk, c, side, z, y] = value[spot * rows : (spot + 1) * rows]


class Reduce(Tree):
    def __init__(self, place, full, total, lands, chunks, order, sems, finish):
        self.place, self.full, self.total, self.lands = place, full, total, lands
        self.chunks, self.sems, self.finish = chunks, sems, finish
        mine = {"x": place.m, "y": place.y}
        self.across = ALL if "x" in order else 0
        have = {"x": self.across, "z": ALL, "y": ALL}
        self.order, self.haves = order, []
        for axis in order:
            before = have
            if axis != "c":
                have = dict(have, **{axis: place.z if axis == "z" else mine[axis]})
            self.haves.append((before, have))
        self.count = len(order) + 1

    def _at(self, chunk, have):
        if self.total is None:
            return self.full.at[chunk, self.place.c, have["x"], have["z"], have["y"]]
        return self.total.at[chunk, have["x"], have["z"], have["y"]]

    def _copies(self, index, chunk):
        axis, (before, _) = self.order[index], self.haves[index]
        place, land = self.place, self.lands[axis]

        def copy(src, dst, slot, device):
            return remote(src, dst, self.sems.at[0, 0, SENT[slot]], self.sems.at[1, chunk, slot], device)

        if axis == "c":
            source = self.full.at[chunk, 1 - place.c, self.across]
            return [copy(source, land.at[chunk], SLOT[axis], place.peer[axis])]
        if axis == "z":
            return [
                copy(
                    self._at(chunk, dict(before, z=(place.z + step) % 4)),
                    land.at[chunk, step - 1],
                    step,
                    place.far[step - 1],
                )
                for step in (1, 2, 3)
            ]
        other = 1 - (place.m if axis == "x" else place.y)
        source = self._at(chunk, dict(before, **{axis: other}))
        return [copy(source, land.at[chunk], SLOT[axis], place.peer[axis])]

    def stage(self, index, chunk):
        if index > 0:
            axis, (_, have) = self.order[index - 1], self.haves[index - 1]
            land = self.lands[axis]
            for copy in self._copies(index - 1, chunk):
                copy.wait_recv()
            mine = self._at(chunk, have)
            last = index == self.count - 1
            if axis == "z":
                value = mine[...].astype(F32)
                for step in range(3):
                    value += land[chunk, step].astype(F32)
            elif last:
                value = mine[...].astype(F32) + land[chunk].astype(F32)
            else:
                value = mine[...] + land[chunk]
            if last:
                self.finish(chunk, value)
            else:
                mine[...] = value.astype(mine.dtype)
        if index < self.count - 1:
            for copy in self._copies(index, chunk):
                copy.start()

    def drain(self):
        for axis in self.order:
            land = self.lands[axis]
            slot = SLOT[axis]
            sent = self.sems.at[0, 0, SENT[slot]]
            remote(land, land, sent, self.sems.at[1, 0, slot], self.place.peer["c"]).wait_send()


class Everyone:
    def __init__(self, place, send_block, land_block, sems):
        self.rank = place.m * 16 + lax.axis_index("dp")
        self.send_block, self.land_block, self.sems = send_block, land_block, sems

    def _copy(self, step):
        to = (self.rank + step) % 32
        return remote(
            self.send_block(to),
            self.land_block(step),
            self.sems.at[0, step - 1],
            self.sems.at[1, step - 1],
            (to % 16, to // 16),
        )

    def _each(self, act):
        def one(step, carry):
            act(self._copy(step))
            return carry

        lax.fori_loop(1, 32, one, 0)

    def start(self):
        self._each(lambda copy: copy.start())

    def wait(self):
        self._each(lambda copy: copy.wait())


VROWS = 16


def rows_from_blocks(blocks, pick, counts):
    mp_count, dp_count = counts
    width = pick.shape[1]
    each = width // (mp_count * dp_count)
    wide = lax.dot_general(
        blocks, pick, NN, precision=lax.Precision.HIGHEST, preferred_element_type=F32
    )
    lane = lax.broadcasted_iota(jnp.int32, (VROWS, width), 1)
    table = jnp.zeros((VROWS, width), F32)
    for m in range(mp_count):
        for r, (c, z, y) in enumerate(RANKS):
            first = (r * mp_count + m) * each
            row = (((c * mp_count + m) * 4 + z) * 2 + y) * VROWS
            table += jnp.where((lane >= first) & (lane < first + each), wide[row : row + VROWS], 0.0)
    return table


def attend_setup(heads, m, box_full, vec_ref, box_heads, bias):
    cols = heads * HD
    for head in range(heads):
        box_heads[head] = box_full[:, head * HD : (head + 1) * HD]
    width = vec_ref.shape[1]
    own = jnp.where(m == 0, vec_ref[6:8, 0:cols], vec_ref[6:8, width - cols :])
    spread = exact_dot(jnp.broadcast_to(own[1:2], (8, cols)), pair_place(cols))
    bias[0:1, 0:cols] = own[0:1]
    bias[0:1, cols:] = spread[0:1]


def attend_trig(omega_ref, corner_ref, trig_ref):
    corner = corner_ref[...].astype(F32)
    angle_x = omega_ref[...] * ((corner[0:1] + corner[2:3]) * 0.5)
    angle_y = omega_ref[...] * ((corner[1:2] + corner[3:4]) * 0.5)
    trig_ref[0:FREQS, :] = jnp.cos(angle_x)
    trig_ref[FREQS : 2 * FREQS, :] = jnp.sin(angle_x)
    trig_ref[2 * FREQS : 3 * FREQS, :] = jnp.cos(angle_y)
    trig_ref[3 * FREQS :, :] = jnp.sin(angle_y)


def quiet(*args):
    return None


def attend_math(heads, r, weights, page_of, projected, attended):
    cols = heads * HD
    pages = r.x.shape[0] // PAGE

    def project(page, carry):
        rows = aligned(page, PAGE)
        tokens = r.x[rows, :]
        query = dot(tokens, weights(0)) + r.bias[0:1, 0:cols]
        query = query.astype(BF16) * HD ** (-0.5)
        r.qtok[rows, :] = query
        qa_rows = query.T
        for half in range(2):
            lanes = slice(half * cols, (half + 1) * cols)
            pair = dot(tokens, weights(1 + half)) + r.bias[0:1, cols + half * cols : 2 * cols + half * cols]
            pair = pair.astype(BF16)
            r.kvtok[rows, lanes] = pair
            turned = pair.T
            for spot in range(heads // 2):
                head_rows = slice((half * heads // 2 + spot) * HD, (half * heads // 2 + spot + 1) * HD)
                r.kt[head_rows, rows] = turned[2 * spot * HD : (2 * spot + 1) * HD]
                r.vt[head_rows, rows] = turned[(2 * spot + 1) * HD : (2 * spot + 2) * HD]
        trig = r.trig[:, rows]
        kft = trig.astype(BF16)
        r.kft[:, rows] = kft
        r.kftok[rows, :] = kft.T
        own, partner = turn_factors(trig)
        for head in range(heads):
            query_head = qa_rows[head * HD : (head + 1) * HD]
            proj = dot(r.box_heads[head], query_head)
            feat = proj * own + swap_blocks(proj) * partner
            r.qa[head, 0:PE, rows] = feat.astype(BF16)
            r.qa[head, PE : PE + HD, rows] = query_head
        projected(page)
        return carry

    lax.fori_loop(0, pages, project, 0)

    def attend(step, carry):
        turn, pair = step // (heads // 2), step % (heads // 2)
        rows = aligned(page_of(turn), PAGE)
        halves = []
        blank = jnp.zeros((HD, PAGE), BF16)
        for side in range(2):
            head = pair * 2 + side
            lanes = aligned(head, 2 * HD)
            left = jnp.concatenate([r.kftok[rows, :], r.kvtok[rows, lanes]], axis=1)
            score = dot(left, jnp.concatenate([r.qa[head, :, rows], blank], axis=0))
            top = jnp.max(score, axis=0, keepdims=True)
            weight = jnp.exp(score - top)
            total = jnp.sum(weight, axis=0, keepdims=True)
            value = r.vt[aligned(head, HD), rows]
            halves.append(dot(value, weight.astype(BF16)) * (1.0 / total))
            r.log[head, :, rows] = top + jnp.log(total)
        both = jnp.concatenate(halves, axis=0).astype(BF16)
        lanes = aligned(pair, 2 * HD)
        r.ctxt[lanes, rows] = both
        r.ctx[rows, lanes] = both.T
        attended(step, turn, pair)
        return carry

    lax.fori_loop(0, pages * (heads // 2), attend, 0)


def attend_buffers(heads, tokens):
    cols = heads * HD
    kept = [
        ("qa", (heads, PE + HD, tokens), BF16),
        ("qtok", (tokens, cols), BF16),
        ("kvtok", (tokens, 2 * cols), BF16),
        ("kt", (cols, tokens), BF16),
        ("kft", (PE, tokens), BF16),
        ("trig", (PE, tokens), F32),
        ("ctxt", (cols, tokens), BF16),
        ("log", (heads, 1, tokens), F32),
    ]
    used = [
        ("kftok", (tokens, PE), BF16),
        ("box_heads", (heads, PE, HD), BF16),
        ("bias", (8, 3 * cols), F32),
        ("ctx", (tokens, cols), BF16),
        ("vt", (cols, tokens), BF16),
    ]
    return kept, used


def attend_kernel(heads, names, *refs):
    r = types.SimpleNamespace(**dict(zip(names, refs)))
    attend_setup(heads, lax.axis_index("mp"), r.box, r.vec, r.box_heads, r.bias)
    attend_trig(r.omega, r.corner, r.trig)
    attend_math(heads, r, lambda chunk: r.w[chunk], lambda turn: turn, quiet, quiet)


def attend_forward(x, corners, omega, w_qkv, w_box, vecs):
    tokens = x.shape[0]
    heads = w_box.shape[1] // HD
    kept, used = attend_buffers(heads, tokens)
    outs = kept + [used[3]]
    scratch = used[:3] + used[4:]
    names = ["x", "corner", "omega", "w", "box", "vec"] + [item[0] for item in outs + scratch]
    vmem = pl.BlockSpec(memory_space=pltpu.VMEM)
    return pl.pallas_call(
        functools.partial(attend_kernel, heads, names),
        out_shape=[jax.ShapeDtypeStruct(shape, kind) for _, shape, kind in outs],
        in_specs=[vmem] * 6,
        out_specs=[vmem] * len(outs),
        scratch_shapes=[pltpu.VMEM(shape, kind) for _, shape, kind in scratch],
        compiler_params=pltpu.CompilerParams(vmem_limit_bytes=VMEM_LIMIT),
        name="attend_forward",
    )(x, corners, omega, w_qkv, w_box, vecs)


TILE = 256


def normal_parts(value):
    phi = 0.5 + 0.5 * lax.erf(value * 2.0 ** (-0.5))
    return phi, phi + value * (jnp.exp(value * value * -0.5) * (0.5 / np.pi) ** 0.5)


def norm_stats(value):
    mean = jnp.mean(value, axis=-1, keepdims=True)
    centred = value - mean
    var = jnp.mean(centred * centred, axis=-1, keepdims=True)
    return centred, lax.rsqrt(var + NORM_EPS)


def norm_back(grad_normed, normed, scale):
    first = jnp.mean(grad_normed, axis=-1, keepdims=True)
    second = jnp.mean(grad_normed * normed, axis=-1, keepdims=True)
    return scale * (grad_normed - first - normed * second)


def col_sum(value):
    return jnp.sum(value, axis=0, keepdims=True)


def feed_math(r, hooks):
    hook = {name: quiet for name in ("entered", "grew", "turned", "shrinks", "shrank", "left", "expands")}
    hook.update(hooks)
    tokens = r.x.shape[0]
    sides = r.ctxx.shape[0]
    steps = r.ws.shape[0]
    tiles = tokens // TILE
    wide = sides * UNIT
    sum2 = dnorm = r.sum2

    def flat(ref, chunk, side):
        return ref[chunk, side] if len(ref.shape) == 4 else natural(ref, chunk, side)

    def put(ref, chunk, side, value):
        if len(ref.shape) == 4:
            ref[chunk, side] = value
        else:
            put_natural(ref, chunk, side, value)

    def lay_out(step):
        for plain, ref, chunk in ((r.plain_e, r.we, 1 + step), (r.plain_s, r.ws, step)):
            for side in range(sides):
                lanes = slice(side * UNIT, (side + 1) * UNIT)
                if len(ref.shape) == 4:
                    plain[:, lanes] = ref[chunk, side]
                else:
                    rows = plain.shape[0] // len(RANKS)
                    for spot, (c, z, y) in enumerate(RANKS):
                        plain[spot * rows : (spot + 1) * rows, lanes] = ref[chunk, c, side, z, y]

    def put_both(ref, chunk, value):
        for side in range(sides):
            put(ref, chunk, side, value[:, side * UNIT : (side + 1) * UNIT])

    def bias_at(step, side):
        first = side * steps + step
        return (pl.ds(8 + first // 2, 1), aligned(first % 2, UNIT))

    def enter(tile, carry):
        rows = aligned(tile, TILE)
        total = r.x[rows, :].astype(F32) + r.vec[4:5, :]
        for side in range(sides):
            total += dot(r.ctxx[side, rows, :], flat(r.we, 0, side), NT)
        centred, scale = norm_stats(total)
        normed = centred * scale
        r.norm1[rows, :] = normed
        r.scale1[rows, :] = scale
        shifted = normed * r.vec[0:1, :] + r.vec[1:2, :]
        r.al[rows, :] = shifted.astype(BF16)
        sum2[rows, :] = shifted + r.vec[5:6, :]
        return carry

    lax.fori_loop(0, tiles, enter, 0)
    hook["entered"]()

    def grow(step, carry):
        whole = aligned(step, wide)
        bias = jnp.concatenate([r.vec[bias_at(step, side)] for side in range(sides)], axis=1)
        lay_out(step)

        def one(tile, inner):
            rows = aligned(tile, TILE)
            pre = dot(r.al[rows, :], r.plain_e[...]) + bias
            phi, slope = normal_parts(pre)
            low = (pre * phi).astype(BF16)
            r.act[rows, whole] = low
            r.slope[rows, whole] = slope.astype(BF16)
            sum2[rows, :] += dot(low, r.plain_s[...], NT)
            hook["grew"](step * tiles + tile)
            return inner

        lax.fori_loop(0, tiles, one, 0)
        return carry

    lax.fori_loop(0, steps, grow, 0)
    r.vsum[...] = jnp.zeros_like(r.vsum)

    def turn(tile, carry):
        rows = aligned(tile, TILE)
        centred, scale = norm_stats(sum2[rows, :])
        normed = centred * scale
        r.out[rows, :] = (normed * r.vec[2:3, :] + r.vec[3:4, :]).astype(BF16)
        grad = r.og[rows, :].astype(F32)
        r.vsum[2:3, :] += col_sum(grad * normed)
        r.vsum[3:4, :] += col_sum(grad)
        back = norm_back(grad * r.vec[2:3, :], normed, scale)
        r.vsum[5:6, :] += col_sum(back)
        r.dh2l[rows, :] = back.astype(BF16)
        dnorm[rows, :] = back
        hook["turned"](tile)
        return carry

    lax.fori_loop(0, tiles, turn, 0)
    r.flip[...] = r.dh2l[...].T

    def grad_shrink(step, carry):
        grad = dot(r.flip[...], r.act[:, aligned(step, wide)]).astype(BF16)
        put_both(r.gs, step, grad)
        hook["shrinks"](step)
        return carry

    lax.fori_loop(0, steps, grad_shrink, 0)

    def shrink(step, carry):
        whole = aligned(step, wide)
        lay_out(step)

        def one(tile, inner):
            rows = aligned(tile, TILE)
            grad = dot(r.dh2l[rows, :], r.plain_s[...])
            low = (grad * r.slope[rows, whole].astype(F32)).astype(BF16)
            r.slope[rows, whole] = low
            sums = col_sum(low.astype(F32))
            for side in range(sides):
                r.vsum[bias_at(step, side)] += sums[:, side * UNIT : (side + 1) * UNIT]
            dnorm[rows, :] += dot(low, r.plain_e[...], NT)
            hook["shrank"](step * tiles + tile)
            return inner

        lax.fori_loop(0, tiles, one, 0)
        return carry

    lax.fori_loop(0, steps, shrink, 0)

    def leave(tile, carry):
        rows = aligned(tile, TILE)
        grad = dnorm[rows, :]
        normed = r.norm1[rows, :]
        r.vsum[0:1, :] += col_sum(grad * normed)
        r.vsum[1:2, :] += col_sum(grad)
        back = norm_back(grad * r.vec[0:1, :], normed, r.scale1[rows, :])
        r.vsum[4:5, :] += col_sum(back)
        low = back.astype(BF16)
        r.dh1l[rows, :] = low
        for side in range(sides):
            r.dctx[side, rows, :] = dot(low, flat(r.we, 0, side)).astype(BF16)
        hook["left"](tile)
        return carry

    lax.fori_loop(0, tiles, leave, 0)
    r.flip[...] = r.al[...].T

    def grad_expand(step, carry):
        grad = dot(r.flip[...], r.slope[:, aligned(step, wide)]).astype(BF16)
        put_both(r.ge, 1 + step, grad)
        hook["expands"](step)
        return carry

    lax.fori_loop(0, steps, grad_expand, 0)
    r.flip[...] = r.dh1l[...].T
    for side in range(sides):
        put(r.ge, 0, side, dot(r.flip[...], r.ctxx[side]).astype(BF16))


def feed_buffers(tokens, width, hidden):
    return [
        ("norm1", (tokens, width), F32),
        ("scale1", (tokens, 1), F32),
        ("sum2", (tokens, width), F32),
        ("al", (tokens, width), BF16),
        ("act", (tokens, hidden), BF16),
        ("slope", (tokens, hidden), BF16),
        ("dh2l", (tokens, width), BF16),
        ("flip", (width, tokens), BF16),
        ("plain_e", (width, 2 * UNIT), BF16),
        ("plain_s", (width, 2 * UNIT), BF16),
    ]


def feed_kernel(names, *refs):
    feed_math(types.SimpleNamespace(**dict(zip(names, refs))), {})


def feed_both(x, og, ctx, w_expand, w_shrink, vecs):
    tokens, width = x.shape
    chunks, sides = w_shrink.shape[0:2]
    outs = [
        ("out", (tokens, width), BF16),
        ("dctx", (sides, tokens, UNIT), BF16),
        ("dh1l", (tokens, width), BF16),
        ("ge", (chunks + 1, sides, width, UNIT), BF16),
        ("gs", (chunks, sides, width, UNIT), BF16),
        ("vsum", (VROWS, width), F32),
    ]
    scratch = feed_buffers(tokens, width, sides * chunks * UNIT)
    names = ["x", "og", "ctxx", "we", "ws", "vec"] + [item[0] for item in outs + scratch]
    vmem = pl.BlockSpec(memory_space=pltpu.VMEM)
    return pl.pallas_call(
        functools.partial(feed_kernel, names),
        out_shape=[jax.ShapeDtypeStruct(shape, kind) for _, shape, kind in outs],
        in_specs=[vmem] * 6,
        out_specs=[vmem] * len(outs),
        scratch_shapes=[pltpu.VMEM(shape, kind) for _, shape, kind in scratch],
        compiler_params=pltpu.CompilerParams(vmem_limit_bytes=VMEM_LIMIT),
        name="feed_both",
    )(x, og, ctx, w_expand, w_shrink, vecs)


def layer_kernel(heads, plan, inv_tokens, names, kept, used, feeds, *refs):
    r = types.SimpleNamespace(**dict(zip(names, refs)))
    cols = heads * HD
    tokens = r.x_all.shape[0]
    pages = tokens // PAGE
    own_tokens = tokens // 2
    tiles = own_tokens // TILE
    place = Place()
    place.signal()
    m, peer = place.m, place.peer["x"]
    at = (place.z, place.y)
    own = aligned(m, own_tokens)
    load_x = pltpu.make_async_copy(r.x_all.at[own, :], r.x, r.load_sem.at[0])
    load_og = pltpu.make_async_copy(r.og_all.at[own, :], r.og, r.load_sem.at[1])
    load_x.start()
    load_og.start()
    r.w[(0, place.c, 0, *at)] = r.attn[0].astype(BF16)
    for half in range(2):
        r.w[(1 + half, place.c, 0, *at)] = jnp.concatenate(
            [
                r.attn[1 + kind, :, head * HD : (head + 1) * HD].astype(BF16)
                for head in range(half * heads // 2, (half + 1) * heads // 2)
                for kind in range(2)
            ],
            axis=1,
        )
    r.box_gather[(0, place.c, 0, *at)] = r.shard_box[...]
    r.vec_gather[(0, place.c, m, *at)] = jnp.zeros((VROWS, 128), F32)
    table_at = (slice(0, r.vectors.shape[0]), slice(0, r.vectors.shape[1]))
    r.vec_gather[(0, place.c, m, *at, *table_at)] = r.vectors[...]
    r.we[(0, place.c, m, *at)] = r.merge[...].astype(BF16)
    for chunk in range(4):
        lanes = slice(chunk * UNIT, (chunk + 1) * UNIT)
        r.we[(1 + chunk, place.c, m, *at)] = r.expand[:, lanes].astype(BF16)
        r.ws[(chunk, place.c, m, *at)] = r.shrink[:, lanes].astype(BF16)
    place.wait()
    tree_v = Spread(place, r.vec_gather, 1, "xzy", r.v_sem)
    tree_b = Spread(place, r.box_gather, 1, "zy", r.b_sem)
    tree_a = Spread(place, r.w, 3, "zy", r.a_sem)
    tree_e = Spread(place, r.we, 5, "zyx", r.e_sem)
    tree_f = Spread(place, r.ws, 4, "xzy", r.f_sem)
    tree_e.lag = tree_f.lag = 2
    first, late = tree_a.events, 3
    begun = first - late

    def weights_event(number):
        tree_e.event(number)
        tree_f.event(number)

    def finish(chunk, value):
        r.sum_f[chunk] = value * inv_tokens

    back_f = Reduce(
        place, r.gs, None, dict(c=r.fc, y=r.fy, z=r.fz, x=r.fx), 4, "cyzx", r.back_sem, finish
    )
    back_f.lag, back_f.held_back = 2, 1

    def attention(*scoped):
        q = types.SimpleNamespace(**dict(zip([item[0] for item in kept + used] + ["x", "plain_w"], scoped)))
        load_all = pltpu.make_async_copy(r.x_all, q.x, r.load_sem.at[2])
        load_all.start()

        tree_v.stage(0, 0)

        def begin(number, carry):
            tree_v.event(number + 1)
            tree_b.event(number)

            @pl.when(number == 4)
            def _():
                r.vec[...] = rows_from_blocks(
                    r.vec_gather[...].reshape(-1, 128), r.pick[...], plan
                )
                r.box_out[...] = natural(r.box_gather, 0, 0).astype(BF16)
                attend_setup(heads, m, r.box_out, r.vec, q.box_heads, q.bias)

            tree_a.event(number)
            weights_event(number - late)
            pl.when(number == 0)(lambda: attend_trig(r.omega, r.corner, q.trig))
            return carry

        lax.fori_loop(0, first, begin, 0)
        for chunk in range(3):
            q.plain_w[chunk] = natural(r.w, chunk, 0)
        keep_w = pltpu.make_async_copy(q.plain_w, r.w_out, r.load_sem.at[3])
        keep_w.start()
        load_all.wait()

        def projected(page):
            pl.when(page < 2)(lambda: weights_event(begun + page))

        piece = PAGE // 2

        def swap_copy(index):
            theirs = pages * (1 - m) + index
            start_rows(
                q.ctx.at[aligned(theirs, piece), :],
                r.ctxx.at[m, aligned(index, piece), :],
                piece,
                r.ctx_sem.at[0, index],
                r.ctx_sem.at[1, index],
                peer,
            )

        def attended(step, turn, pair):
            pl.when(step % 3 == 1)(lambda: weights_event(begun + 2 + step // 3))
            pl.when(step == 8)(lambda: weights_event(begun + 5))

            @pl.when(step == heads // 2 - 1)
            def _():
                swap_copy(2 - 2 * m)
                swap_copy(1)

            @pl.when(step == heads - 1)
            def _():
                swap_copy(2 * m)

        attend_math(
            heads,
            q,
            lambda chunk: q.plain_w[chunk],
            lambda turn: turn * m + (pages - 1 - turn) * (1 - m),
            projected,
            attended,
        )
        stores = [
            pltpu.make_async_copy(getattr(q, name), getattr(r, name + "_out"), r.store_sem.at[k])
            for k, (name, _, _) in enumerate(kept)
        ]
        for copy in stores:
            copy.start()
        r.ctxx[m] = q.ctx[own, :]
        for index in range(pages):
            copy = remote(
                q.ctx.at[aligned(index, piece), :],
                r.ctxx.at[1 - m, aligned(index, piece), :],
                r.ctx_sem.at[0, index],
                r.ctx_sem.at[1, index],
                peer,
            )
            copy.wait_recv()
            copy.wait_send()
        for copy in stores:
            copy.wait()
        keep_w.wait()

    pl.run_scoped(
        attention,
        *[pltpu.VMEM(shape, kind) for _, shape, kind in kept + used],
        pltpu.VMEM(r.x_all.shape, BF16),
        pltpu.VMEM(r.w_out.shape, BF16),
    )

    def feed(*scoped):
        q = types.SimpleNamespace(**dict(zip([item[0] for item in feeds], scoped)))
        for name in ("x", "og", "we", "ws", "vec", "ctxx", "dh1l", "ge", "gs", "vsum"):
            setattr(q, name, getattr(r, name))

        def out_copies(tile):
            rows = aligned(tile, TILE)
            there = r.out_full.at[pl.ds(pl.multiple_of(m * own_tokens + tile * TILE, TILE), TILE), :]
            return (
                pltpu.make_async_copy(q.out.at[rows, :], there, r.swap_sem.at[0, tile]),
                remote(q.out.at[rows, :], there, r.swap_sem.at[1, tile], r.swap_sem.at[2, tile], peer),
            )

        def dctx_copies(tile):
            rows = aligned(tile, TILE)
            there = r.dctx_full.at[pl.ds(pl.multiple_of(m * own_tokens + tile * TILE, TILE), TILE), :]
            return (
                pltpu.make_async_copy(q.dctx.at[m, rows, :], there, r.swap_sem.at[3, tile]),
                remote(
                    q.dctx.at[1 - m, rows, :], there, r.swap_sem.at[4, tile], r.swap_sem.at[5, tile], peer
                ),
            )

        def start_out(tile):
            rows = aligned(tile, TILE)
            there = r.out_full.at[pl.ds(pl.multiple_of(m * own_tokens + tile * TILE, TILE), TILE), :]
            out_copies(tile)[0].start()
            sems = r.swap_sem.at[1, tile], r.swap_sem.at[2, tile]
            start_rows(q.out.at[rows, :], there, TILE, *sems, peer)

        def start_dctx(tile):
            rows = aligned(tile, TILE)
            there = r.dctx_full.at[pl.ds(pl.multiple_of(m * own_tokens + tile * TILE, TILE), TILE), :]
            dctx_copies(tile)[0].start()
            sems = r.swap_sem.at[4, tile], r.swap_sem.at[5, tile]
            start_rows(q.dctx.at[1 - m, rows, :], there, TILE, *sems, peer)

        def grew(number):
            pl.when(number % 3 == 1)(lambda: weights_event(begun + 7 + number // 3))

        def shrinks(step):
            pl.when(step != 2)(lambda: back_f.event(step - step // 3))

        def shrank(number):
            for spot, event in ((1, 3), (4, 4), (8, 5), (11, 6)):
                pl.when(number == spot)(lambda event=event: back_f.event(event))

        def expands(step):
            pl.when(step != 1)(lambda: back_f.event(7 + (step + 1) // 2))

        load_x.wait()
        load_og.wait()
        feed_math(
            q,
            dict(
                entered=lambda: weights_event(begun + 6),
                grew=grew,
                expands=expands,
                turned=start_out,
                shrinks=shrinks,
                shrank=shrank,
                left=start_dctx,
            ),
        )
        back_f.rest()
        back_f.drain()
        for tile in range(tiles):
            for copy in out_copies(tile) + dctx_copies(tile):
                copy.wait()

    pl.run_scoped(feed, *[pltpu.VMEM(shape, kind) for _, shape, kind in feeds])
    for tree in (tree_v, tree_b, tree_a, tree_e, tree_f):
        tree.drain()


def layer_forward(x, og, corners, omega, pick, shards, plan, inv_tokens):
    tokens, width = x.shape
    cols = shards[1].shape[1]
    heads = cols // HD
    own = tokens // 2
    unit = (width // 16, UNIT)
    kept, used = attend_buffers(heads, tokens)
    feeds = feed_buffers(own, width, 8 * UNIT)
    feeds += [("out", (own, width), BF16), ("dctx", (2, own, UNIT), BF16)]
    free = pl.BlockSpec(memory_space=pl.ANY)
    vmem = pl.BlockSpec(memory_space=pltpu.VMEM)
    inputs = [("x_all", free), ("og_all", free), ("corner", vmem), ("omega", vmem), ("pick", vmem)]
    inputs += [(name, vmem) for name in ("attn", "shard_box", "vectors", "merge", "expand", "shrink")]
    outs = [(name + "_out", shape, kind, free) for name, shape, kind in kept]
    outs += [
        ("w_out", (3, width, cols), BF16, free),
        ("box_out", (PE, cols), BF16, vmem),
        ("out_full", (tokens, width), BF16, free),
        ("dctx_full", (tokens, cols), BF16, free),
        ("dh1l", (own, width), BF16, vmem),
        ("ge", (5, 2, 2, 4, 2, *unit), BF16, vmem),
        ("vsum", (VROWS, width), F32, vmem),
        ("sum_f", (4, *unit), F32, vmem),
    ]
    dma = pltpu.SemaphoreType.DMA
    scratch = [
        ("x", pltpu.VMEM((own, width), BF16)),
        ("og", pltpu.VMEM((own, width), BF16)),
        ("vec", pltpu.VMEM((VROWS, width), F32)),
        ("w", pltpu.VMEM((3, 2, 1, 4, 2, *unit), BF16)),
        ("box_gather", pltpu.VMEM((1, 2, 1, 4, 2, PE // 16, cols), F32)),
        ("vec_gather", pltpu.VMEM((1, 2, 2, 4, 2, VROWS, 128), F32)),
        ("we", pltpu.VMEM((5, 2, 2, 4, 2, *unit), BF16)),
        ("ws", pltpu.VMEM((4, 2, 2, 4, 2, *unit), BF16)),
        ("ctxx", pltpu.VMEM((2, own, cols), BF16)),
        ("gs", pltpu.VMEM((4, 2, 2, 4, 2, *unit), BF16)),
        ("fc", pltpu.VMEM((4, 2, 4, 2, *unit), BF16)),
        ("fy", pltpu.VMEM((4, 2, 4, *unit), BF16)),
        ("fz", pltpu.VMEM((4, 3, 2, *unit), BF16)),
        ("fx", pltpu.VMEM((4, *unit), BF16)),
        ("ctx_sem", dma((2, 3))),
        ("a_sem", dma((2, 3, SLOTS))),
        ("b_sem", dma((2, 1, SLOTS))),
        ("v_sem", dma((2, 1, SLOTS))),
        ("e_sem", dma((2, 5, SLOTS))),
        ("f_sem", dma((2, 4, SLOTS))),
        ("back_sem", dma((2, 4, SLOTS))),
        ("load_sem", dma((4,))),
        ("store_sem", dma((len(kept),))),
        ("swap_sem", dma((6, own // TILE))),
    ]
    names = [item[0] for item in inputs + outs + scratch]
    return pl.pallas_call(
        functools.partial(layer_kernel, heads, plan, inv_tokens, names, kept, used, feeds),
        out_shape=[jax.ShapeDtypeStruct(shape, kind) for _, shape, kind, _ in outs],
        in_specs=[item[1] for item in inputs],
        out_specs=[item[3] for item in outs],
        scratch_shapes=[item[1] for item in scratch],
        compiler_params=pltpu.CompilerParams(
            vmem_limit_bytes=VMEM_LIMIT, collective_id=0, has_side_effects=True
        ),
        name="layer_forward",
    )(x, og, corners, omega, pick, *shards)


def pair_place(cols):
    spot = lax.broadcasted_iota(jnp.int32, (cols, 2 * cols), 0)
    lane = lax.broadcasted_iota(jnp.int32, (cols, 2 * cols), 1)
    target = ((spot >> 6) << 7) + HD + (spot & (HD - 1))
    return jnp.where(lane == target, 1.0, 0.0)


def exact_dot(lhs, rhs, dims=NN):
    return lax.dot_general(
        lhs, rhs, dims, precision=lax.Precision.HIGHEST, preferred_element_type=F32
    )


def attend_back_kernel(heads, plan, inv_tokens, *refs):
    inputs, refs = refs[:12], refs[12:]
    if plan is not None:
        load_sem, held, refs = refs[-1], refs[-13:-1], refs[:-13]
        loads = [
            pltpu.make_async_copy(src, dst, load_sem.at[k]) for k, (src, dst) in enumerate(zip(inputs, held))
        ]
        early = (0, 2, 7, 11)
        for k in sorted(range(12), key=lambda k: k not in early):
            loads[k].start()
        inputs = held
    x_ref, w_ref, box_ref, *inputs = inputs
    qa_ref, qtok_ref, kvtok_ref, kt_ref, kft_ref, trig_ref, ctxt_ref, log_ref, dctx_ref = inputs
    cols = heads * HD
    tokens = x_ref.shape[0]
    pages = tokens // PAGE
    m = lax.axis_index("mp")
    piece = PAGE // 2
    pieces = 2 * pages
    lane = lax.broadcasted_iota(jnp.int32, (1, 2 * HD), 1)
    lower = lane < HD
    if plan is None:
        inp_ref, gw_ref, gbox_ref, qvsum_ref, *refs = refs
        kftok, dctxt, boxt, dtok, xt, gbox = refs
        before, after = 0, 0

        def background(number):
            pass
    else:
        dh1_ref, vsum_ref, sumf_ref, pick_ref, full_e, *refs = refs
        inp_ref, sum_e, sum_a, sum_b, sum_v, norm_ref, *refs = refs
        kftok, dctxt, boxt, dtok, xt, gbox, *refs = refs
        came, total_e, full_a, full_b, full_v, land_v, norms, *refs = refs
        ec, ey, ez, ex, ac, ay, az, bc, by, bz, *refs = refs
        e_sem, a_sem, b_sem, v_sem, n_sem, i_sem, loc_sem = refs
        place = Place()
        place.signal_all()
        fill = pltpu.make_async_copy(full_e.at[:, place.c], total_e, loc_sem.at[0])
        fill.start()
        place.wait_all()

        def finish(out):
            def put(chunk, value):
                out[chunk] = value * inv_tokens

            return put

        tree_e = Reduce(
            place, full_e, total_e, dict(c=ec, y=ey, z=ez, x=ex), 5, "cyzx", e_sem, finish(sum_e)
        )
        tree_e.lag, tree_e.held_back = 2, 1
        tree_a = Reduce(place, full_a, None, dict(c=ac, y=ay, z=az), 3, "cyz", a_sem, finish(sum_a))
        tree_b = Reduce(place, full_b, None, dict(c=bc, y=by, z=bz), 1, "cyz", b_sem, finish(sum_b))

        def block_of(rank):
            r = rank % 16
            return full_v.at[rank // 16, r // 4, (r // 2) % 2, r % 2]

        spot = (place.m, place.z, place.y, place.c)
        all_v = Everyone(place, block_of, lambda step: land_v.at[step - 1], v_sem)
        all_n = Everyone(place, lambda rank: norms.at[spot], lambda step: norms.at[spot], n_sem)

        def background(number):
            tree_e.event(number)

        background(0)
        fill.wait()
        for k in early:
            loads[k].wait()

    boxt[...] = box_ref[...].T
    gbox[...] = jnp.zeros_like(gbox)

    def prepare(page, carry):
        rows = aligned(page, PAGE)
        kftok[rows, :] = kft_ref[:, rows].T
        dctxt[:, rows] = dctx_ref[rows, :].T
        xt[:, rows] = x_ref[rows, :].T
        if plan is not None:
            pl.when(page == pages - 1)(lambda: background(1))
        return carry

    lax.fori_loop(0, pages, prepare, 0)
    if plan is not None:
        for k in range(12):
            if k not in early:
                loads[k].wait()

    def attend(step, carry):
        page, pair = step // (heads // 2), step % (heads // 2)
        rows = aligned(page, PAGE)
        own, partner = turn_factors(trig_ref[:, rows])
        pair_lanes = aligned(pair, 2 * HD)
        query_pair = qtok_ref[rows, pair_lanes]
        dctx_pair = dctx_ref[rows, pair_lanes]
        halves = []
        boxes = []
        blank = jnp.zeros((HD, PAGE), BF16)
        for side in range(2):
            head = pair * 2 + side
            lanes = aligned(head, 2 * HD)
            key_value = kvtok_ref[rows, lanes]
            left = jnp.concatenate([kftok[rows, :], key_value], axis=1)
            score = dot(left, jnp.concatenate([qa_ref[head, :, rows], blank], axis=0))
            prob = jnp.exp(score - log_ref[head, :, rows])
            prob_low = prob.astype(BF16)
            head_rows = pl.ds(pl.multiple_of(head * HD, HD), HD)
            dctx_head = dctxt[head_rows, rows]
            grad_prob = dot(
                key_value, jnp.concatenate([blank, dctx_head], axis=0)
            )
            inner = col_sum(dctx_head.astype(F32) * ctxt_ref[head_rows, rows].astype(F32))
            grad_score = (prob * (grad_prob - inner)).astype(BF16)
            if side == 0:
                both = jnp.concatenate([query_pair[:, 0:HD], dctx_pair[:, 0:HD]], axis=1)
            else:
                both = jnp.concatenate([query_pair[:, HD:], dctx_pair[:, HD:]], axis=1)
            from_score = dot(grad_score, both)
            from_prob = dot(prob_low, both)
            grad_kv = jnp.where(lower, from_score, from_prob).astype(BF16)
            dtok[rows, pl.ds(pl.multiple_of(cols + head * 2 * HD, 2 * HD), 2 * HD)] = grad_kv
            keys = jnp.concatenate([kft_ref[:, rows], kt_ref[head_rows, rows]], axis=0)
            grad_query = dot(keys, grad_score) * HD ** (-0.5)
            feat = grad_query[0:PE]
            proj = (feat * own - swap_blocks(feat) * partner).astype(BF16)
            halves.append(grad_query[PE:] + dot(boxt[head_rows, :], proj))
            boxes.append(dot(proj, query_pair))
        gbox[:, pair_lanes] += jnp.where(lower, boxes[0], boxes[1])
        dtok[rows, pair_lanes] = jnp.concatenate(halves, axis=0).astype(BF16).T
        return carry

    def spread(page):
        rows = aligned(page, PAGE)
        return sum(
            dot(dtok[rows, chunk * UNIT : (chunk + 1) * UNIT], w_ref[chunk], NT) for chunk in range(3)
        )

    if plan is None:
        lax.fori_loop(0, pages * (heads // 2), attend, 0)
        gbox_ref[...] = gbox[...] * HD**0.5

        def spread_page(page, carry):
            inp_ref[aligned(page, PAGE), :] = spread(page)
            return carry

        lax.fori_loop(0, pages, spread_page, 0)

        def gather(step, carry):
            lanes = aligned(step, UNIT)
            gw_ref[step] = dot(xt[...], dtok[:, lanes]).astype(BF16)
            qvsum_ref[0:1, lanes] = col_sum(dtok[:, lanes].astype(F32))
            return carry

        lax.fori_loop(0, 3, gather, 0)
        return

    def swap(index):
        rows = aligned(index, piece)
        return remote(
            inp_ref.at[rows, :], came.at[rows, :], i_sem.at[0, index], i_sem.at[1, index], place.peer["x"]
        )

    def attend_and_send(step, carry):
        attend(step, carry)
        page = step // (heads // 2)

        @pl.when(step % (heads // 2) == heads // 2 - 1)
        def _():
            value = spread(page)
            for half in range(2):
                index = 2 * page + half
                rows = aligned(index, piece)
                own = index // pages == m
                spot = aligned(index % pages, piece)
                extra = jnp.where(own, dh1_ref[spot, :].astype(F32), 0.0)
                inp_ref[rows, :] = (value[half * piece : (half + 1) * piece] + extra).astype(BF16)
                start_rows(
                    inp_ref.at[rows, :],
                    came.at[rows, :],
                    piece,
                    i_sem.at[0, index],
                    i_sem.at[1, index],
                    place.peer["x"],
                )

        pl.when(step % 3 != 2)(lambda: background(2 + 2 * (step // 3) + step % 3))
        return carry

    lax.fori_loop(0, pages * (heads // 2), attend_and_send, 0)
    put_natural(full_b, 0, 0, gbox[...] * HD**0.5)

    def gather(step, carry):
        grad = dot(xt[...], dtok[:, aligned(step, UNIT)]).astype(BF16)
        put_natural(full_a, step, 0, grad)
        tree_a.event(step)
        tree_b.event(step)
        background(8 + step)
        return carry

    lax.fori_loop(0, 3, gather, 0)

    sums = jnp.concatenate(
        [
            col_sum(dtok[:, chunk * UNIT : (chunk + 1) * UNIT].astype(F32)) for chunk in range(3)
        ],
        axis=1,
    )
    values = exact_dot(jnp.broadcast_to(sums[:, cols:], (8, 2 * cols)), pair_place(cols), NT)
    pair = jnp.concatenate([sums[:, 0:cols], values[0:1]], axis=0)
    blank = jnp.zeros_like(pair)
    pair = jnp.where(
        m == 0, jnp.concatenate([pair, blank], axis=1), jnp.concatenate([blank, pair], axis=1)
    )
    table = jnp.concatenate([vsum_ref[0:6, :], pair, vsum_ref[8:, :]], axis=0)
    mp_count, dp_count = plan
    width = table.shape[1]
    each = width // (mp_count * dp_count)
    wide_lane = lax.broadcasted_iota(jnp.int32, (VROWS, width), 1)
    for side in range(mp_count):
        parts = []
        for r in range(dp_count):
            first = (r * mp_count + side) * each
            parts.append(jnp.where((wide_lane >= first) & (wide_lane < first + each), table, 0.0))
        block = exact_dot(jnp.concatenate(parts, axis=0), pick_ref[...], NT)
        full_v[side] = block.reshape(full_v.shape[1:])
    all_v.start()

    def tail(number, carry):
        tree_a.event(number)
        tree_b.event(number)
        return carry

    lax.fori_loop(3, tree_a.events, tail, 0)
    tree_e.rest()
    all_v.wait()
    total_v = full_v[spot] + jnp.sum(land_v[...], axis=0)
    sum_v[0] = total_v * inv_tokens

    square = sum(jnp.sum(out[...] * out[...]) for out in (sum_e, sumf_ref, sum_a, sum_b, sum_v))
    norms[spot] = jnp.full((8, 128), square, F32)
    all_n.start()

    def final(number, carry):
        rows = aligned(number, piece)
        swap(number).wait()
        inp_ref[rows, :] = (inp_ref[rows, :].astype(F32) + came[rows, :].astype(F32)).astype(BF16)
        return carry

    lax.fori_loop(0, pieces, final, 0)
    all_n.wait()
    every = norms[...].reshape(-1, 8, 128)
    norm_ref[...] = jnp.sqrt(sum(every[k] for k in range(every.shape[0])))
    for tree in (tree_e, tree_a, tree_b):
        tree.drain()


def attend_backward(x, weight, box, kept, dctx, plan, inv_tokens, more=()):
    tokens, width = x.shape
    cols = weight.shape[-1]
    heads = cols // HD
    vmem = pl.BlockSpec(memory_space=pltpu.VMEM)
    scratch = [
        pltpu.VMEM((tokens, PE), BF16),
        pltpu.VMEM((cols, tokens), BF16),
        pltpu.VMEM((cols, PE), BF16),
        pltpu.VMEM((tokens, 3 * cols), BF16),
        pltpu.VMEM((width, tokens), BF16),
        pltpu.VMEM((PE, cols), F32),
    ]
    in_specs = [vmem] * 12
    if plan is None:
        shapes = [
            ((tokens, width), F32),
            ((3, width, cols), BF16),
            ((PE, cols), F32),
            ((8, 3 * cols), F32),
        ]
        extra = {}
    else:
        free = pl.BlockSpec(memory_space=pl.ANY)
        in_specs = [free] * 12 + [vmem] * 4 + [free]
        rows = width // 16
        unit = (rows, UNIT)
        tile = (PE // 16, cols)
        small = (VROWS, 128)
        shapes = [
            ((tokens, width), BF16),
            ((5, *unit), F32),
            ((3, *unit), F32),
            ((1, *tile), F32),
            ((1, *small), F32),
            ((8, 128), F32),
        ]
        scratch += [
            pltpu.VMEM((tokens, width), BF16),
            pltpu.VMEM((5, 2, 4, 2, *unit), BF16),
            pltpu.VMEM((3, 2, 1, 4, 2, *unit), BF16),
            pltpu.VMEM((1, 2, 1, 4, 2, *tile), F32),
            pltpu.VMEM((2, 4, 2, 2, *small), F32),
            pltpu.VMEM((31, *small), F32),
            pltpu.VMEM((2, 4, 2, 2, 8, 128), F32),
            pltpu.VMEM((5, 2, 4, 2, *unit), BF16),
            pltpu.VMEM((5, 2, 4, *unit), BF16),
            pltpu.VMEM((5, 3, 2, *unit), BF16),
            pltpu.VMEM((5, *unit), BF16),
            pltpu.VMEM((3, 4, 2, *unit), BF16),
            pltpu.VMEM((3, 4, *unit), BF16),
            pltpu.VMEM((3, 3, *unit), BF16),
            pltpu.VMEM((1, 4, 2, *tile), F32),
            pltpu.VMEM((1, 4, *tile), F32),
            pltpu.VMEM((1, 3, *tile), F32),
            pltpu.SemaphoreType.DMA((2, 5, SLOTS)),
            pltpu.SemaphoreType.DMA((2, 3, SLOTS)),
            pltpu.SemaphoreType.DMA((2, 1, SLOTS)),
            pltpu.SemaphoreType.DMA((2, 31)),
            pltpu.SemaphoreType.DMA((2, 31)),
            pltpu.SemaphoreType.DMA((2, 2 * (tokens // PAGE))),
            pltpu.SemaphoreType.DMA((2,)),
        ]
        scratch += [pltpu.VMEM(array.shape, array.dtype) for array in (x, weight, box, *kept, dctx)]
        scratch.append(pltpu.SemaphoreType.DMA((12,)))
        extra = dict(collective_id=2, has_side_effects=True)
    return pl.pallas_call(
        functools.partial(attend_back_kernel, heads, plan, inv_tokens),
        out_shape=[jax.ShapeDtypeStruct(s, d) for s, d in shapes],
        in_specs=in_specs,
        out_specs=[vmem] * len(shapes),
        scratch_shapes=scratch,
        compiler_params=pltpu.CompilerParams(vmem_limit_bytes=VMEM_LIMIT, **extra),
        cost_estimate=pl.CostEstimate(flops=4 * 10**10, bytes_accessed=10**8, transcendentals=10**7),
        name="attend_backward",
    )(x, weight, box, *kept, dctx, *more)


def adam_step(master, first, second, gradient, rate, decay):
    new_first = BETA_ONE * first + (1.0 - BETA_ONE) * gradient
    new_second = BETA_TWO * second + (1.0 - BETA_TWO) * gradient * gradient
    first_hat = new_first / (1.0 - BETA_ONE**STEP)
    second_hat = new_second / (1.0 - BETA_TWO**STEP)
    new_master = master - rate * (first_hat / (jnp.sqrt(second_hat) + ADAM_EPS) + decay * master)
    return (new_first, new_second, new_master)


def adam_kernel(heads, norm_ref, *refs):
    sum_e, sum_f, sum_a, sum_b, sum_v, *refs = refs
    states, outs = refs[:18], refs[18:]
    outs[-1][...] = norm_ref[0:1, 0:1]
    clip = CLIP_LIMIT / jnp.maximum(norm_ref[0:1, 0:1], CLIP_LIMIT)

    def update(first, out, gradient, at, rate, decay):
        news = adam_step(*(ref[at] for ref in states[first : first + 3]), gradient * clip, rate, decay)
        for ref, new in zip(outs[out : out + 3], news):
            ref[at] = new
        if decay:
            outs[out + 3][at] = news[2].astype(BF16)

    def heads_of(kind):
        half = heads // 2
        return jnp.concatenate(
            [
                sum_a[1 + head // half, :, (2 * (head % half) + kind) * HD : (2 * (head % half) + kind + 1) * HD]
                for head in range(heads)
            ],
            axis=1,
        )

    for index, gradient in enumerate((sum_a[0], heads_of(0), heads_of(1))):
        update(0, 0, gradient, index, RATE_MATRIX, WEIGHT_DECAY)
    update(3, 4, sum_b[0], ALL, RATE_MATRIX, WEIGHT_DECAY)
    update(6, 8, sum_e[0], ALL, RATE_MATRIX, WEIGHT_DECAY)
    for chunk in range(4):
        lanes = (ALL, slice(chunk * UNIT, (chunk + 1) * UNIT))
        update(9, 12, sum_e[1 + chunk], lanes, RATE_MATRIX, WEIGHT_DECAY)
        update(12, 16, sum_f[chunk], lanes, RATE_MATRIX, WEIGHT_DECAY)
    rows, each = states[15].shape
    update(15, 20, sum_v[0, 0:rows, 0:each], ALL, RATE_VECTOR, 0.0)


def adam_all(norm, sums, states):
    shapes = []
    for first in range(0, 18, 3):
        shapes += [(states[first].shape, F32)] * 3
        if first < 15:
            shapes.append((states[first].shape, BF16))
    vmem = pl.BlockSpec(memory_space=pltpu.VMEM)
    shapes.append(((1, 1), F32))
    return pl.pallas_call(
        functools.partial(adam_kernel, states[0].shape[2] // HD),
        out_shape=[jax.ShapeDtypeStruct(s, d) for s, d in shapes],
        in_specs=[vmem] * (6 + len(states)),
        out_specs=[vmem] * len(shapes),
        compiler_params=pltpu.CompilerParams(vmem_limit_bytes=VMEM_LIMIT),
        name="adam_all",
    )(norm, *sums, *states)


def pack_qkv(shard):
    rows, cols = shard.shape[1:]
    heads = cols // HD
    pairs = jnp.stack([shard[1].reshape(rows, heads, HD), shard[2].reshape(rows, heads, HD)], axis=2)
    pairs = pairs.reshape(rows, 2, cols)
    return jnp.stack([shard[0], pairs[:, 0], pairs[:, 1]])


def unpack_qkv(packed):
    rows, cols = packed.shape[1:]
    pairs = jnp.concatenate([packed[1], packed[2]], axis=1).reshape(rows, cols // HD, 2, HD)
    return jnp.stack(
        [packed[0], pairs[:, :, 0].reshape(rows, cols), pairs[:, :, 1].reshape(rows, cols)]
    )


def to_chunks(shard):
    rows = shard.shape[0]
    return shard.reshape(rows, -1, UNIT).transpose(1, 0, 2)


def from_chunks(chunks):
    return chunks.transpose(1, 0, 2).reshape(chunks.shape[1], -1)


def on_device(
    layer_input,
    page_boxes,
    output_grad,
    attn_proj,
    attn_first,
    attn_second,
    box_proj,
    box_first,
    box_second,
    merge_proj,
    merge_first,
    merge_second,
    expand_proj,
    expand_first,
    expand_second,
    shrink_proj,
    shrink_first,
    shrink_second,
    vectors,
    vector_first,
    vector_second,
):
    mp_count = lax.axis_size("mp")
    dp_count = lax.axis_size("dp")
    mp_index = lax.axis_index("mp")
    tokens, width = layer_input.shape
    cols = attn_proj.shape[2]
    heads = cols // HD
    own_tokens = tokens // mp_count
    inv_tokens = 1.0 / (tokens * dp_count)

    corners = page_boxes.T
    omega = (10000.0 ** (-np.arange(FREQS, dtype=np.float64) / FREQS)).astype(np.float32)[:, None]
    omega = jnp.asarray(omega)
    plan = (mp_count, dp_count) if dp_count == 16 and mp_count == 2 else None
    if plan is not None:
        each = vectors.shape[1]
        pick = np.zeros((128, width), np.float32)
        pick[np.arange(width) % each, np.arange(width)] = 1.0
        pick = jnp.asarray(pick)
        *kept, w_qkv, w_box, layer_out, dctx, dh1, g_expand, vec_sum, sum_f = layer_forward(
            layer_input,
            output_grad,
            corners,
            omega,
            pick,
            (attn_proj, box_proj, vectors, merge_proj.T, expand_proj, shrink_proj.T),
            plan,
            inv_tokens,
        )
        input_grad, sum_e, sum_a, sum_b, sum_v, norm = attend_backward(
            layer_input,
            w_qkv,
            w_box,
            kept,
            dctx,
            plan,
            inv_tokens,
            (dh1, vec_sum, sum_f, pick, g_expand),
        )
        merge = [merge_proj.T, merge_first.T, merge_second.T]
        shrink = [shrink_proj.T, shrink_first.T, shrink_second.T]
        *results, norm = adam_all(
            norm,
            (sum_e, sum_f, sum_a, sum_b, sum_v),
            [attn_proj, attn_first, attn_second, box_proj, box_first, box_second, *merge]
            + [expand_proj, expand_first, expand_second, *shrink, vectors, vector_first, vector_second],
        )
        turned = (8, 9, 10, 11, 16, 17, 18, 19)
        results = [out.T if k in turned else out for k, out in enumerate(results)]
        return (layer_out, input_grad, norm.reshape(()), *results)
    shard_qkv = pack_qkv(attn_proj).astype(BF16)
    shard_e = jnp.concatenate([merge_proj.T[None], to_chunks(expand_proj)]).astype(BF16)
    shard_f = to_chunks(shrink_proj.T).astype(BF16)
    w_qkv = lax.all_gather(shard_qkv, "dp", axis=1, tiled=True)
    w_box = lax.all_gather(box_proj.astype(BF16), "dp", axis=0, tiled=True)
    w_expand = lax.all_gather(lax.all_gather(shard_e, "dp", axis=1, tiled=True), "mp", axis=1)
    w_shrink = lax.all_gather(lax.all_gather(shard_f, "dp", axis=1, tiled=True), "mp", axis=1)
    vecs = lax.all_gather(vectors, ("dp", "mp"), axis=1, tiled=True)
    vecs = jnp.pad(vecs, ((0, VROWS - vecs.shape[0]), (0, 0)))
    *kept, context = attend_forward(layer_input, corners, omega, w_qkv, w_box, vecs)
    context = lax.all_to_all(
        context.reshape(mp_count, own_tokens, cols), "mp", split_axis=0, concat_axis=0
    )

    def own_rows(array):
        return lax.dynamic_slice_in_dim(array, mp_index * own_tokens, own_tokens)

    layer_out, dctx, dh1, g_expand, g_shrink, vec_sum = feed_both(
        own_rows(layer_input), own_rows(output_grad), context, w_expand, w_shrink, vecs
    )
    g_feed = jnp.concatenate([g_expand, g_shrink])
    layer_out = lax.all_gather(layer_out, "mp", axis=0, tiled=True)
    dctx = lax.all_to_all(dctx, "mp", split_axis=0, concat_axis=0).reshape(tokens, cols)
    part, g_qkv, g_box, qkv_sum = attend_backward(
        layer_input, w_qkv, w_box, kept, dctx, None, inv_tokens
    )
    own_part = lax.psum_scatter(part.astype(BF16), "mp", scatter_dimension=0, tiled=True)
    own_grad = (own_part.astype(F32) + dh1).astype(BF16)
    input_grad = lax.all_gather(own_grad, "mp", axis=0, tiled=True)
    shard_attn = unpack_qkv(
        lax.psum_scatter(g_qkv, "dp", scatter_dimension=1, tiled=True).astype(F32) * inv_tokens
    )
    shard_box = lax.psum_scatter(g_box, "dp", scatter_dimension=0, tiled=True) * inv_tokens
    sum_feed = lax.psum_scatter(g_feed, "dp", scatter_dimension=2, tiled=True)
    sum_feed = lax.psum_scatter(sum_feed, "mp", scatter_dimension=1, tiled=True)[:, 0]
    sum_feed = sum_feed.astype(F32) * inv_tokens
    sum_expand, sum_shrink = sum_feed[0:5], sum_feed[5:]

    def placed(row):
        return lax.dynamic_update_slice_in_dim(
            jnp.zeros((width,), F32), row, mp_index * cols, 0
        )[None, :]

    value_sum = qkv_sum[0, cols:].reshape(heads, 2, HD)[:, 1].reshape(cols)
    vector_grad = jnp.concatenate(
        [vec_sum[0:6], placed(qkv_sum[0, 0:cols]), placed(value_sum), vec_sum[8:12]]
    )
    vector_shard = (
        lax.psum_scatter(vector_grad, ("dp", "mp"), scatter_dimension=1, tiled=True) * inv_tokens
    )
    square = sum(
        jnp.sum(shard * shard)
        for shard in (shard_attn, shard_box, sum_expand, sum_shrink, vector_shard)
    )
    grad_norm = jnp.sqrt(lax.psum(square, ("dp", "mp")))
    shard_merge = sum_expand[0].T
    shard_expand = from_chunks(sum_expand[1:])
    shard_shrink = from_chunks(sum_shrink).T
    clip_scale = CLIP_LIMIT / jnp.maximum(grad_norm, CLIP_LIMIT)
    results = [layer_out, input_grad, grad_norm]
    for master, first, second, shard in (
        (attn_proj, attn_first, attn_second, shard_attn),
        (box_proj, box_first, box_second, shard_box),
        (merge_proj, merge_first, merge_second, shard_merge),
        (expand_proj, expand_first, expand_second, shard_expand),
        (shrink_proj, shrink_first, shrink_second, shard_shrink),
    ):
        new_first, new_second, new_master = adam_step(
            master, first, second, shard * clip_scale, RATE_MATRIX, WEIGHT_DECAY
        )
        results += [new_first, new_second, new_master, new_master.astype(BF16)]
    results += adam_step(
        vectors, vector_first, vector_second, vector_shard * clip_scale, RATE_VECTOR, 0.0
    )
    return tuple(results)


def solution(mesh):
    rows = P("dp", None)
    attn = P(None, "dp", "mp")
    tall = P("dp", "mp")
    wide = P("mp", "dp")
    vector = P(None, ("dp", "mp"))
    in_specs = (rows,) * 3 + (attn,) * 3 + (tall,) * 3 + (wide,) * 3 + (tall,) * 3 + (wide,) * 3
    in_specs += (vector,) * 3
    out_specs = (rows, rows, P()) + (attn,) * 4 + (tall,) * 4 + (wide,) * 4 + (tall,) * 4
    out_specs += (wide,) * 4 + (vector,) * 3
    return jax.shard_map(
        on_device, mesh=mesh, in_specs=in_specs, out_specs=out_specs, check_vma=False
    )
```

```python
import functools
import types

import jax
import jax.numpy as jnp
import numpy as np
from jax import lax
from jax.experimental import pallas as pl
from jax.experimental.pallas import tpu as pltpu
from jax.sharding import PartitionSpec as P

HD = 64
FREQS = 32
PE = 128
PAGE = 512
STEP = 10

NORM_EPS = 1e-12
CLIP_LIMIT = 0.1
BETA_ONE = 0.9
BETA_TWO = 0.999
ADAM_EPS = 1e-08
RATE_MATRIX = 0.05
RATE_VECTOR = 0.5
WEIGHT_DECAY = 0.01

F32 = jnp.float32
BF16 = jnp.bfloat16
VMEM_LIMIT = 60 * 1024 * 1024

NN = (((1,), (0,)), ((), ()))
NT = (((1,), (1,)), ((), ()))
TN = (((0,), (0,)), ((), ()))


def dot(lhs, rhs, dims=NN):
    return lax.dot_general(lhs, rhs, dims, preferred_element_type=F32)


def aligned(index, size):
    return pl.ds(pl.multiple_of(index * size, size), size)


def swap_blocks(feat):
    return jnp.concatenate(
        [
            feat[FREQS : 2 * FREQS],
            feat[0:FREQS],
            feat[3 * FREQS :],
            feat[2 * FREQS : 3 * FREQS],
        ],
        axis=0,
    )


def turn_factors(trig):
    cos_x, sin_x = trig[0:FREQS], trig[FREQS : 2 * FREQS]
    cos_y, sin_y = trig[2 * FREQS : 3 * FREQS], trig[3 * FREQS :]
    return (
        jnp.concatenate([sin_x, sin_x, sin_y, sin_y], axis=0),
        jnp.concatenate([cos_x, -cos_x, cos_y, -cos_y], axis=0),
    )


MESH = pl.DeviceIdType.MESH
ALL = slice(None)
UNIT = 384


class Place:
    def __init__(self):
        rank = lax.axis_index("dp")
        self.m = lax.axis_index("mp")
        self.z = rank // 4
        self.y = (rank // 2) % 2
        self.c = rank % 2
        self.peer = {
            "x": (rank, 1 - self.m),
            "y": (rank + 2 - 4 * self.y, self.m),
            "c": (rank + 1 - 2 * self.c, self.m),
        }
        self.far = [((rank + 4 * step) % 16, self.m) for step in (1, 2, 3)]

    def signal(self):
        barrier = pltpu.get_barrier_semaphore()
        for device in list(self.peer.values()) + self.far:
            pl.semaphore_signal(barrier, inc=1, device_id=device, device_id_type=MESH)

    def wait(self):
        pl.semaphore_wait(pltpu.get_barrier_semaphore(), 6)

    def signal_all(self):
        barrier = pltpu.get_barrier_semaphore()
        rank = self.m * 16 + lax.axis_index("dp")

        def one(step, carry):
            to = (rank + step) % 32
            pl.semaphore_signal(barrier, inc=1, device_id=(to % 16, to // 16), device_id_type=MESH)
            return carry

        lax.fori_loop(1, 32, one, 0)

    def wait_all(self):
        pl.semaphore_wait(pltpu.get_barrier_semaphore(), 31)


PART = 256


def start_rows(src, dst, rows, send_sem, recv_sem, device):
    for first in range(0, rows, PART):
        part = pl.ds(first, PART)
        remote(src.at[part, :], dst.at[part, :], send_sem, recv_sem, device).start()


def remote(src, dst, send_sem, recv_sem, device):
    return pltpu.make_async_remote_copy(
        src_ref=src,
        dst_ref=dst,
        send_sem=send_sem,
        recv_sem=recv_sem,
        device_id=device,
        device_id_type=MESH,
    )


SLOT = {"c": 0, "z": 1, "y": 4, "x": 5}
SLOTS = 6
SENT = (0, 1, 1, 1, 4, 5)


class Tree:
    lag = 1
    held_back = 0
    together = False

    def stage(self, index, chunk):
        raise NotImplementedError

    def event(self, number):
        for index in range(self.count - 1 - self.held_back, -1, -1):
            chunk = number - index * self.lag
            if self.together:

                @pl.when(chunk == 0)
                def _(index=index):
                    for each in range(self.chunks):
                        self.stage(index, each)

            elif self.chunks == 1:
                pl.when(chunk == 0)(lambda index=index: self.stage(index, 0))
            else:
                pl.when((chunk >= 0) & (chunk < self.chunks))(
                    lambda index=index, chunk=chunk: self.stage(index, chunk)
                )

    @property
    def events(self):
        return self.chunks + (self.count - 1 - self.held_back) * self.lag

    def rest(self):
        def one(chunk, carry):
            self.stage(self.count - 1, chunk)
            return carry

        lax.fori_loop(0, self.chunks, one, 0)


class Spread(Tree):
    def __init__(self, place, ref, chunks, order, sems):
        self.chunks, self.ref, self.sems, self.place = chunks, ref, sems, place
        have = {"x": place.m if "x" in order else 0, "z": place.z, "y": place.y}
        mine = {"x": place.m, "y": place.y}
        self.own = have
        self.steps, self.axes = [], order
        for axis in order:
            if axis == "z":
                sends = [(have, place.far[step - 1], step) for step in (1, 2, 3)]
                waits = [(dict(have, z=(place.z + 4 - step) % 4), step) for step in (1, 2, 3)]
            else:
                sends = [(have, place.peer[axis], SLOT[axis])]
                waits = [(dict(have, **{axis: 1 - mine[axis]}), SLOT[axis])]
            self.steps.append((sends, waits))
            have = dict(have, **{axis: ALL})
        self.other = place.peer["c"]
        self.count = len(self.steps) + 2

    def _copy(self, chunk, have, device, slot):
        came = 0 if chunk == ALL else chunk
        block = self.ref.at[chunk, self.place.c, have["x"], have["z"], have["y"]]
        sent = self.sems.at[0, 0, SENT[slot]]
        return remote(block, block, sent, self.sems.at[1, came, slot], device)

    def _plane(self, chunk, core):
        plane = self.ref.at[chunk, core]
        came = 0 if chunk == ALL else chunk
        return remote(plane, plane, self.sems.at[0, 0, 0], self.sems.at[1, came, 0], self.other)

    def stage(self, index, chunk):
        if index == self.count - 1:
            self._plane(chunk, 1 - self.place.c).wait_recv()
            return
        came = [self.own]
        if index > 0:
            came = []
            for have, slot in self.steps[index - 1][1]:
                self._copy(chunk, have, self.other, slot).wait_recv()
                came.append(have)
        if index < len(self.steps):
            for have, device, slot in self.steps[index][0]:
                self._copy(chunk, have, device, slot).start()
        for have in came:
            self._copy(chunk, have, self.other, 0).start()

    def drain(self):
        for axis, (sends, _) in zip(self.axes, self.steps):
            have, _, slot = sends[0]
            if axis == "z":
                have = dict(have, z=slice(0, 3))
            self._copy(ALL, have, self.other, slot).wait_send()
        self._plane(ALL, self.place.c).wait_send()


RANKS = [(c, z, y) for z in range(4) for y in range(2) for c in range(2)]


def natural(ref, chunk, side):
    return jnp.concatenate([ref[chunk, c, side, z, y] for c, z, y in RANKS], axis=0)


def put_natural(ref, chunk, side, value):
    rows = value.shape[0] // len(RANKS)
    for spot, (c, z, y) in enumerate(RANKS):
        ref[chunk, c, side, z, y] = value[spot * rows : (spot + 1) * rows]


class Reduce(Tree):
    def __init__(self, place, full, total, lands, chunks, order, sems, finish):
        self.place, self.full, self.total, self.lands = place, full, total, lands
        self.chunks, self.sems, self.finish = chunks, sems, finish
        mine = {"x": place.m, "y": place.y}
        self.across = ALL if "x" in order else 0
        have = {"x": self.across, "z": ALL, "y": ALL}
        self.order, self.haves = order, []
        for axis in order:
            before = have
            if axis != "c":
                have = dict(have, **{axis: place.z if axis == "z" else mine[axis]})
            self.haves.append((before, have))
        self.count = len(order) + 1

    def _at(self, chunk, have):
        if self.total is None:
            return self.full.at[chunk, self.place.c, have["x"], have["z"], have["y"]]
        return self.total.at[chunk, have["x"], have["z"], have["y"]]

    def _copies(self, index, chunk):
        axis, (before, _) = self.order[index], self.haves[index]
        place, land = self.place, self.lands[axis]

        def copy(src, dst, slot, device):
            return remote(src, dst, self.sems.at[0, 0, SENT[slot]], self.sems.at[1, chunk, slot], device)

        if axis == "c":
            source = self.full.at[chunk, 1 - place.c, self.across]
            return [copy(source, land.at[chunk], SLOT[axis], place.peer[axis])]
        if axis == "z":
            return [
                copy(
                    self._at(chunk, dict(before, z=(place.z + step) % 4)),
                    land.at[chunk, step - 1],
                    step,
                    place.far[step - 1],
                )
                for step in (1, 2, 3)
            ]
        other = 1 - (place.m if axis == "x" else place.y)
        source = self._at(chunk, dict(before, **{axis: other}))
        return [copy(source, land.at[chunk], SLOT[axis], place.peer[axis])]

    def stage(self, index, chunk):
        if index > 0:
            axis, (_, have) = self.order[index - 1], self.haves[index - 1]
            land = self.lands[axis]
            for copy in self._copies(index - 1, chunk):
                copy.wait_recv()
            mine = self._at(chunk, have)
            last = index == self.count - 1
            if axis == "z":
                value = mine[...].astype(F32)
                for step in range(3):
                    value += land[chunk, step].astype(F32)
            elif last:
                value = mine[...].astype(F32) + land[chunk].astype(F32)
            else:
                value = mine[...] + land[chunk]
            if last:
                self.finish(chunk, value)
            else:
                mine[...] = value.astype(mine.dtype)
        if index < self.count - 1:
            for copy in self._copies(index, chunk):
                copy.start()

    def drain(self):
        for axis in self.order:
            land = self.lands[axis]
            slot = SLOT[axis]
            sent = self.sems.at[0, 0, SENT[slot]]
            remote(land, land, sent, self.sems.at[1, 0, slot], self.place.peer["c"]).wait_send()


class Everyone:
    def __init__(self, place, send_block, land_block, sems):
        self.rank = place.m * 16 + lax.axis_index("dp")
        self.send_block, self.land_block, self.sems = send_block, land_block, sems

    def _copy(self, step):
        to = (self.rank + step) % 32
        return remote(
            self.send_block(to),
            self.land_block(step),
            self.sems.at[0, step - 1],
            self.sems.at[1, step - 1],
            (to % 16, to // 16),
        )

    def _each(self, act):
        def one(step, carry):
            act(self._copy(step))
            return carry

        lax.fori_loop(1, 32, one, 0)

    def start(self):
        self._each(lambda copy: copy.start())

    def wait(self):
        self._each(lambda copy: copy.wait())


VROWS = 16


def rows_from_blocks(blocks, pick, counts):
    mp_count, dp_count = counts
    width = pick.shape[1]
    each = width // (mp_count * dp_count)
    wide = lax.dot_general(
        blocks, pick, NN, precision=lax.Precision.HIGHEST, preferred_element_type=F32
    )
    lane = lax.broadcasted_iota(jnp.int32, (VROWS, width), 1)
    table = jnp.zeros((VROWS, width), F32)
    for m in range(mp_count):
        for r, (c, z, y) in enumerate(RANKS):
            first = (r * mp_count + m) * each
            row = (((c * mp_count + m) * 4 + z) * 2 + y) * VROWS
            table += jnp.where((lane >= first) & (lane < first + each), wide[row : row + VROWS], 0.0)
    return table


def attend_setup(heads, m, box_full, vec_ref, box_heads, bias):
    cols = heads * HD
    for head in range(heads):
        box_heads[head] = box_full[:, head * HD : (head + 1) * HD]
    width = vec_ref.shape[1]
    own = jnp.where(m == 0, vec_ref[6:8, 0:cols], vec_ref[6:8, width - cols :])
    spread = exact_dot(jnp.broadcast_to(own[1:2], (8, cols)), pair_place(cols))
    bias[0:1, 0:cols] = own[0:1]
    bias[0:1, cols:] = spread[0:1]


def attend_trig(omega_ref, corner_ref, trig_ref):
    corner = corner_ref[...].astype(F32)
    angle_x = omega_ref[...] * ((corner[0:1] + corner[2:3]) * 0.5)
    angle_y = omega_ref[...] * ((corner[1:2] + corner[3:4]) * 0.5)
    trig_ref[0:FREQS, :] = jnp.cos(angle_x)
    trig_ref[FREQS : 2 * FREQS, :] = jnp.sin(angle_x)
    trig_ref[2 * FREQS : 3 * FREQS, :] = jnp.cos(angle_y)
    trig_ref[3 * FREQS :, :] = jnp.sin(angle_y)


def quiet(*args):
    return None


def attend_math(heads, r, weights, page_of, projected, attended):
    cols = heads * HD
    pages = r.x.shape[0] // PAGE

    def project(page, carry):
        rows = aligned(page, PAGE)
        tokens = r.x[rows, :]
        query = dot(tokens, weights(0)) + r.bias[0:1, 0:cols]
        query = query.astype(BF16) * HD ** (-0.5)
        r.qtok[rows, :] = query
        qa_rows = query.T
        for half in range(2):
            lanes = slice(half * cols, (half + 1) * cols)
            pair = dot(tokens, weights(1 + half)) + r.bias[0:1, cols + half * cols : 2 * cols + half * cols]
            pair = pair.astype(BF16)
            r.kvtok[rows, lanes] = pair
            turned = pair.T
            for spot in range(heads // 2):
                head_rows = slice((half * heads // 2 + spot) * HD, (half * heads // 2 + spot + 1) * HD)
                r.kt[head_rows, rows] = turned[2 * spot * HD : (2 * spot + 1) * HD]
                r.vt[head_rows, rows] = turned[(2 * spot + 1) * HD : (2 * spot + 2) * HD]
        trig = r.trig[:, rows]
        kft = trig.astype(BF16)
        r.kft[:, rows] = kft
        r.kftok[rows, :] = kft.T
        own, partner = turn_factors(trig)
        for head in range(heads):
            query_head = qa_rows[head * HD : (head + 1) * HD]
            proj = dot(r.box_heads[head], query_head)
            feat = proj * own + swap_blocks(proj) * partner
            r.qa[head, 0:PE, rows] = feat.astype(BF16)
            r.qa[head, PE : PE + HD, rows] = query_head
        projected(page)
        return carry

    lax.fori_loop(0, pages, project, 0)

    def attend(step, carry):
        turn, pair = step // (heads // 2), step % (heads // 2)
        rows = aligned(page_of(turn), PAGE)
        halves = []
        blank = jnp.zeros((HD, PAGE), BF16)
        for side in range(2):
            head = pair * 2 + side
            lanes = aligned(head, 2 * HD)
            left = jnp.concatenate([r.kftok[rows, :], r.kvtok[rows, lanes]], axis=1)
            score = dot(left, jnp.concatenate([r.qa[head, :, rows], blank], axis=0))
            top = jnp.max(score, axis=0, keepdims=True)
            weight = jnp.exp(score - top)
            total = jnp.sum(weight, axis=0, keepdims=True)
            value = r.vt[aligned(head, HD), rows]
            halves.append(dot(value, weight.astype(BF16)) * (1.0 / total))
            r.log[head, :, rows] = top + jnp.log(total)
        both = jnp.concatenate(halves, axis=0).astype(BF16)
        lanes = aligned(pair, 2 * HD)
        r.ctxt[lanes, rows] = both
        r.ctx[rows, lanes] = both.T
        attended(step, turn, pair)
        return carry

    lax.fori_loop(0, pages * (heads // 2), attend, 0)


def attend_buffers(heads, tokens):
    cols = heads * HD
    kept = [
        ("qa", (heads, PE + HD, tokens), BF16),
        ("qtok", (tokens, cols), BF16),
        ("kvtok", (tokens, 2 * cols), BF16),
        ("kt", (cols, tokens), BF16),
        ("kft", (PE, tokens), BF16),
        ("trig", (PE, tokens), F32),
        ("ctxt", (cols, tokens), BF16),
        ("log", (heads, 1, tokens), F32),
    ]
    used = [
        ("kftok", (tokens, PE), BF16),
        ("box_heads", (heads, PE, HD), BF16),
        ("bias", (8, 3 * cols), F32),
        ("ctx", (tokens, cols), BF16),
        ("vt", (cols, tokens), BF16),
    ]
    return kept, used


def attend_kernel(heads, names, *refs):
    r = types.SimpleNamespace(**dict(zip(names, refs)))
    attend_setup(heads, lax.axis_index("mp"), r.box, r.vec, r.box_heads, r.bias)
    attend_trig(r.omega, r.corner, r.trig)
    attend_math(heads, r, lambda chunk: r.w[chunk], lambda turn: turn, quiet, quiet)


def attend_forward(x, corners, omega, w_qkv, w_box, vecs):
    tokens = x.shape[0]
    heads = w_box.shape[1] // HD
    kept, used = attend_buffers(heads, tokens)
    outs = kept + [used[3]]
    scratch = used[:3] + used[4:]
    names = ["x", "corner", "omega", "w", "box", "vec"] + [item[0] for item in outs + scratch]
    vmem = pl.BlockSpec(memory_space=pltpu.VMEM)
    return pl.pallas_call(
        functools.partial(attend_kernel, heads, names),
        out_shape=[jax.ShapeDtypeStruct(shape, kind) for _, shape, kind in outs],
        in_specs=[vmem] * 6,
        out_specs=[vmem] * len(outs),
        scratch_shapes=[pltpu.VMEM(shape, kind) for _, shape, kind in scratch],
        compiler_params=pltpu.CompilerParams(vmem_limit_bytes=VMEM_LIMIT),
        name="attend_forward",
    )(x, corners, omega, w_qkv, w_box, vecs)


TILE = 256


def normal_parts(value):
    phi = 0.5 + 0.5 * lax.erf(value * 2.0 ** (-0.5))
    return phi, phi + value * (jnp.exp(value * value * -0.5) * (0.5 / np.pi) ** 0.5)


def norm_stats(value):
    mean = jnp.mean(value, axis=-1, keepdims=True)
    centred = value - mean
    var = jnp.mean(centred * centred, axis=-1, keepdims=True)
    return centred, lax.rsqrt(var + NORM_EPS)


def norm_back(grad_normed, normed, scale):
    first = jnp.mean(grad_normed, axis=-1, keepdims=True)
    second = jnp.mean(grad_normed * normed, axis=-1, keepdims=True)
    return scale * (grad_normed - first - normed * second)


def col_sum(value):
    return jnp.sum(value, axis=0, keepdims=True)


def feed_math(r, hooks):
    hook = {name: quiet for name in ("entered", "grew", "turned", "shrinks", "shrank", "left", "expands")}
    hook.update(hooks)
    tokens = r.x.shape[0]
    sides = r.ctxx.shape[0]
    steps = r.ws.shape[0]
    tiles = tokens // TILE
    wide = sides * UNIT
    sum2 = dnorm = r.sum2

    def flat(ref, chunk, side):
        return ref[chunk, side] if len(ref.shape) == 4 else natural(ref, chunk, side)

    def put(ref, chunk, side, value):
        if len(ref.shape) == 4:
            ref[chunk, side] = value
        else:
            put_natural(ref, chunk, side, value)

    def lay_out(step):
        for plain, ref, chunk in ((r.plain_e, r.we, 1 + step), (r.plain_s, r.ws, step)):
            for side in range(sides):
                lanes = slice(side * UNIT, (side + 1) * UNIT)
                if len(ref.shape) == 4:
                    plain[:, lanes] = ref[chunk, side]
                else:
                    rows = plain.shape[0] // len(RANKS)
                    for spot, (c, z, y) in enumerate(RANKS):
                        plain[spot * rows : (spot + 1) * rows, lanes] = ref[chunk, c, side, z, y]

    def put_both(ref, chunk, value):
        for side in range(sides):
            put(ref, chunk, side, value[:, side * UNIT : (side + 1) * UNIT])

    def bias_at(step, side):
        first = side * steps + step
        return (pl.ds(8 + first // 2, 1), aligned(first % 2, UNIT))

    def enter(tile, carry):
        rows = aligned(tile, TILE)
        total = r.x[rows, :].astype(F32) + r.vec[4:5, :]
        for side in range(sides):
            total += dot(r.ctxx[side, rows, :], flat(r.we, 0, side), NT)
        centred, scale = norm_stats(total)
        normed = centred * scale
        r.norm1[rows, :] = normed
        r.scale1[rows, :] = scale
        shifted = normed * r.vec[0:1, :] + r.vec[1:2, :]
        r.al[rows, :] = shifted.astype(BF16)
        sum2[rows, :] = shifted + r.vec[5:6, :]
        return carry

    lax.fori_loop(0, tiles, enter, 0)
    hook["entered"]()

    def grow(step, carry):
        whole = aligned(step, wide)
        bias = jnp.concatenate([r.vec[bias_at(step, side)] for side in range(sides)], axis=1)
        lay_out(step)

        def one(tile, inner):
            rows = aligned(tile, TILE)
            pre = dot(r.al[rows, :], r.plain_e[...]) + bias
            phi, slope = normal_parts(pre)
            low = (pre * phi).astype(BF16)
            r.act[rows, whole] = low
            r.slope[rows, whole] = slope.astype(BF16)
            sum2[rows, :] += dot(low, r.plain_s[...], NT)
            hook["grew"](step * tiles + tile)
            return inner

        lax.fori_loop(0, tiles, one, 0)
        return carry

    lax.fori_loop(0, steps, grow, 0)
    r.vsum[...] = jnp.zeros_like(r.vsum)

    def turn(tile, carry):
        rows = aligned(tile, TILE)
        centred, scale = norm_stats(sum2[rows, :])
        normed = centred * scale
        r.out[rows, :] = (normed * r.vec[2:3, :] + r.vec[3:4, :]).astype(BF16)
        grad = r.og[rows, :].astype(F32)
        r.vsum[2:3, :] += col_sum(grad * normed)
        r.vsum[3:4, :] += col_sum(grad)
        back = norm_back(grad * r.vec[2:3, :], normed, scale)
        r.vsum[5:6, :] += col_sum(back)
        r.dh2l[rows, :] = back.astype(BF16)
        dnorm[rows, :] = back
        hook["turned"](tile)
        return carry

    lax.fori_loop(0, tiles, turn, 0)
    r.flip[...] = r.dh2l[...].T

    def grad_shrink(step, carry):
        grad = dot(r.flip[...], r.act[:, aligned(step, wide)]).astype(BF16)
        put_both(r.gs, step, grad)
        hook["shrinks"](step)
        return carry

    lax.fori_loop(0, steps, grad_shrink, 0)

    def shrink(step, carry):
        whole = aligned(step, wide)
        lay_out(step)

        def one(tile, inner):
            rows = aligned(tile, TILE)
            grad = dot(r.dh2l[rows, :], r.plain_s[...])
            low = (grad * r.slope[rows, whole].astype(F32)).astype(BF16)
            r.slope[rows, whole] = low
            sums = col_sum(low.astype(F32))
            for side in range(sides):
                r.vsum[bias_at(step, side)] += sums[:, side * UNIT : (side + 1) * UNIT]
            dnorm[rows, :] += dot(low, r.plain_e[...], NT)
            hook["shrank"](step * tiles + tile)
            return inner

        lax.fori_loop(0, tiles, one, 0)
        return carry

    lax.fori_loop(0, steps, shrink, 0)

    def leave(tile, carry):
        rows = aligned(tile, TILE)
        grad = dnorm[rows, :]
        normed = r.norm1[rows, :]
        r.vsum[0:1, :] += col_sum(grad * normed)
        r.vsum[1:2, :] += col_sum(grad)
        back = norm_back(grad * r.vec[0:1, :], normed, r.scale1[rows, :])
        r.vsum[4:5, :] += col_sum(back)
        low = back.astype(BF16)
        r.dh1l[rows, :] = low
        for side in range(sides):
            r.dctx[side, rows, :] = dot(low, flat(r.we, 0, side)).astype(BF16)
        hook["left"](tile)
        return carry

    lax.fori_loop(0, tiles, leave, 0)
    r.flip[...] = r.al[...].T

    def grad_expand(step, carry):
        grad = dot(r.flip[...], r.slope[:, aligned(step, wide)]).astype(BF16)
        put_both(r.ge, 1 + step, grad)
        hook["expands"](step)
        return carry

    lax.fori_loop(0, steps, grad_expand, 0)
    r.flip[...] = r.dh1l[...].T
    for side in range(sides):
        put(r.ge, 0, side, dot(r.flip[...], r.ctxx[side]).astype(BF16))


def feed_buffers(tokens, width, hidden):
    return [
        ("norm1", (tokens, width), F32),
        ("scale1", (tokens, 1), F32),
        ("sum2", (tokens, width), F32),
        ("al", (tokens, width), BF16),
        ("act", (tokens, hidden), BF16),
        ("slope", (tokens, hidden), BF16),
        ("dh2l", (tokens, width), BF16),
        ("flip", (width, tokens), BF16),
        ("plain_e", (width, 2 * UNIT), BF16),
        ("plain_s", (width, 2 * UNIT), BF16),
    ]


def feed_kernel(names, *refs):
    feed_math(types.SimpleNamespace(**dict(zip(names, refs))), {})


def feed_both(x, og, ctx, w_expand, w_shrink, vecs):
    tokens, width = x.shape
    chunks, sides = w_shrink.shape[0:2]
    outs = [
        ("out", (tokens, width), BF16),
        ("dctx", (sides, tokens, UNIT), BF16),
        ("dh1l", (tokens, width), BF16),
        ("ge", (chunks + 1, sides, width, UNIT), BF16),
        ("gs", (chunks, sides, width, UNIT), BF16),
        ("vsum", (VROWS, width), F32),
    ]
    scratch = feed_buffers(tokens, width, sides * chunks * UNIT)
    names = ["x", "og", "ctxx", "we", "ws", "vec"] + [item[0] for item in outs + scratch]
    vmem = pl.BlockSpec(memory_space=pltpu.VMEM)
    return pl.pallas_call(
        functools.partial(feed_kernel, names),
        out_shape=[jax.ShapeDtypeStruct(shape, kind) for _, shape, kind in outs],
        in_specs=[vmem] * 6,
        out_specs=[vmem] * len(outs),
        scratch_shapes=[pltpu.VMEM(shape, kind) for _, shape, kind in scratch],
        compiler_params=pltpu.CompilerParams(vmem_limit_bytes=VMEM_LIMIT),
        name="feed_both",
    )(x, og, ctx, w_expand, w_shrink, vecs)


def layer_kernel(heads, plan, inv_tokens, names, kept, used, feeds, *refs):
    r = types.SimpleNamespace(**dict(zip(names, refs)))
    cols = heads * HD
    tokens = r.x_all.shape[0]
    pages = tokens // PAGE
    own_tokens = tokens // 2
    tiles = own_tokens // TILE
    place = Place()
    place.signal()
    m, peer = place.m, place.peer["x"]
    at = (place.z, place.y)
    own = aligned(m, own_tokens)
    load_x = pltpu.make_async_copy(r.x_all.at[own, :], r.x, r.load_sem.at[0])
    load_og = pltpu.make_async_copy(r.og_all.at[own, :], r.og, r.load_sem.at[1])
    load_x.start()
    load_og.start()
    r.w[(0, place.c, 0, *at)] = r.attn[0].astype(BF16)
    for half in range(2):
        r.w[(1 + half, place.c, 0, *at)] = jnp.concatenate(
            [
                r.attn[1 + kind, :, head * HD : (head + 1) * HD].astype(BF16)
                for head in range(half * heads // 2, (half + 1) * heads // 2)
                for kind in range(2)
            ],
            axis=1,
        )
    r.box_gather[(0, place.c, 0, *at)] = r.shard_box[...]
    r.vec_gather[(0, place.c, m, *at)] = jnp.zeros((VROWS, 128), F32)
    table_at = (slice(0, r.vectors.shape[0]), slice(0, r.vectors.shape[1]))
    r.vec_gather[(0, place.c, m, *at, *table_at)] = r.vectors[...]
    r.we[(0, place.c, m, *at)] = r.merge[...].astype(BF16)
    for chunk in range(4):
        lanes = slice(chunk * UNIT, (chunk + 1) * UNIT)
        r.we[(1 + chunk, place.c, m, *at)] = r.expand[:, lanes].astype(BF16)
        r.ws[(chunk, place.c, m, *at)] = r.shrink[:, lanes].astype(BF16)
    place.wait()
    tree_v = Spread(place, r.vec_gather, 1, "xzy", r.v_sem)
    tree_b = Spread(place, r.box_gather, 1, "zy", r.b_sem)
    tree_a = Spread(place, r.w, 3, "zy", r.a_sem)
    tree_e = Spread(place, r.we, 5, "zyx", r.e_sem)
    tree_f = Spread(place, r.ws, 4, "xzy", r.f_sem)
    tree_e.lag = tree_f.lag = 2
    first, late = tree_a.events, 3
    begun = first - late

    def weights_event(number):
        tree_e.event(number)
        tree_f.event(number)

    def finish(chunk, value):
        r.sum_f[chunk] = value * inv_tokens

    back_f = Reduce(
        place, r.gs, None, dict(c=r.fc, y=r.fy, z=r.fz, x=r.fx), 4, "cyzx", r.back_sem, finish
    )
    back_f.lag, back_f.held_back = 2, 1

    def attention(*scoped):
        q = types.SimpleNamespace(**dict(zip([item[0] for item in kept + used] + ["x", "plain_w"], scoped)))
        load_all = pltpu.make_async_copy(r.x_all, q.x, r.load_sem.at[2])
        load_all.start()

        tree_v.stage(0, 0)

        def begin(number, carry):
            tree_v.event(number + 1)
            tree_b.event(number)

            @pl.when(number == 4)
            def _():
                r.vec[...] = rows_from_blocks(
                    r.vec_gather[...].reshape(-1, 128), r.pick[...], plan
                )
                r.box_out[...] = natural(r.box_gather, 0, 0).astype(BF16)
                attend_setup(heads, m, r.box_out, r.vec, q.box_heads, q.bias)

            tree_a.event(number)
            weights_event(number - late)
            pl.when(number == 0)(lambda: attend_trig(r.omega, r.corner, q.trig))
            return carry

        lax.fori_loop(0, first, begin, 0)
        for chunk in range(3):
            q.plain_w[chunk] = natural(r.w, chunk, 0)
        keep_w = pltpu.make_async_copy(q.plain_w, r.w_out, r.load_sem.at[3])
        keep_w.start()
        load_all.wait()

        def projected(page):
            pl.when(page < 2)(lambda: weights_event(begun + page))

        piece = PAGE // 2

        def swap_copy(index):
            theirs = pages * (1 - m) + index
            start_rows(
                q.ctx.at[aligned(theirs, piece), :],
                r.ctxx.at[m, aligned(index, piece), :],
                piece,
                r.ctx_sem.at[0, index],
                r.ctx_sem.at[1, index],
                peer,
            )

        def attended(step, turn, pair):
            pl.when(step % 3 == 1)(lambda: weights_event(begun + 2 + step // 3))
            pl.when(step == 8)(lambda: weights_event(begun + 5))

            @pl.when(step == heads // 2 - 1)
            def _():
                swap_copy(2 - 2 * m)
                swap_copy(1)

            @pl.when(step == heads - 1)
            def _():
                swap_copy(2 * m)

        attend_math(
            heads,
            q,
            lambda chunk: q.plain_w[chunk],
            lambda turn: turn * m + (pages - 1 - turn) * (1 - m),
            projected,
            attended,
        )
        stores = [
            pltpu.make_async_copy(getattr(q, name), getattr(r, name + "_out"), r.store_sem.at[k])
            for k, (name, _, _) in enumerate(kept)
        ]
        for copy in stores:
            copy.start()
        r.ctxx[m] = q.ctx[own, :]
        for index in range(pages):
            copy = remote(
                q.ctx.at[aligned(index, piece), :],
                r.ctxx.at[1 - m, aligned(index, piece), :],
                r.ctx_sem.at[0, index],
                r.ctx_sem.at[1, index],
                peer,
            )
            copy.wait_recv()
            copy.wait_send()
        for copy in stores:
            copy.wait()
        keep_w.wait()

    pl.run_scoped(
        attention,
        *[pltpu.VMEM(shape, kind) for _, shape, kind in kept + used],
        pltpu.VMEM(r.x_all.shape, BF16),
        pltpu.VMEM(r.w_out.shape, BF16),
    )

    def feed(*scoped):
        q = types.SimpleNamespace(**dict(zip([item[0] for item in feeds], scoped)))
        for name in ("x", "og", "we", "ws", "vec", "ctxx", "dh1l", "ge", "gs", "vsum"):
            setattr(q, name, getattr(r, name))

        def out_copies(tile):
            rows = aligned(tile, TILE)
            there = r.out_full.at[pl.ds(pl.multiple_of(m * own_tokens + tile * TILE, TILE), TILE), :]
            return (
                pltpu.make_async_copy(q.out.at[rows, :], there, r.swap_sem.at[0, tile]),
                remote(q.out.at[rows, :], there, r.swap_sem.at[1, tile], r.swap_sem.at[2, tile], peer),
            )

        def dctx_copies(tile):
            rows = aligned(tile, TILE)
            there = r.dctx_full.at[pl.ds(pl.multiple_of(m * own_tokens + tile * TILE, TILE), TILE), :]
            return (
                pltpu.make_async_copy(q.dctx.at[m, rows, :], there, r.swap_sem.at[3, tile]),
                remote(
                    q.dctx.at[1 - m, rows, :], there, r.swap_sem.at[4, tile], r.swap_sem.at[5, tile], peer
                ),
            )

        def start_out(tile):
            rows = aligned(tile, TILE)
            there = r.out_full.at[pl.ds(pl.multiple_of(m * own_tokens + tile * TILE, TILE), TILE), :]
            out_copies(tile)[0].start()
            sems = r.swap_sem.at[1, tile], r.swap_sem.at[2, tile]
            start_rows(q.out.at[rows, :], there, TILE, *sems, peer)

        def start_dctx(tile):
            rows = aligned(tile, TILE)
            there = r.dctx_full.at[pl.ds(pl.multiple_of(m * own_tokens + tile * TILE, TILE), TILE), :]
            dctx_copies(tile)[0].start()
            sems = r.swap_sem.at[4, tile], r.swap_sem.at[5, tile]
            start_rows(q.dctx.at[1 - m, rows, :], there, TILE, *sems, peer)

        def grew(number):
            pl.when(number % 3 == 1)(lambda: weights_event(begun + 7 + number // 3))

        def shrinks(step):
            pl.when(step != 2)(lambda: back_f.event(step - step // 3))

        def shrank(number):
            for spot, event in ((2, 3), (6, 4), (11, 5)):
                pl.when(number == spot)(lambda event=event: back_f.event(event))

        def expands(step):
            back_f.event(6 + step)

        load_x.wait()
        load_og.wait()
        feed_math(
            q,
            dict(
                entered=lambda: weights_event(begun + 6),
                grew=grew,
                expands=expands,
                turned=start_out,
                shrinks=shrinks,
                shrank=shrank,
                left=start_dctx,
            ),
        )
        back_f.rest()
        back_f.drain()
        for tile in range(tiles):
            for copy in out_copies(tile) + dctx_copies(tile):
                copy.wait()

    pl.run_scoped(feed, *[pltpu.VMEM(shape, kind) for _, shape, kind in feeds])
    for tree in (tree_v, tree_b, tree_a, tree_e, tree_f):
        tree.drain()


def layer_forward(x, og, corners, omega, pick, shards, plan, inv_tokens):
    tokens, width = x.shape
    cols = shards[1].shape[1]
    heads = cols // HD
    own = tokens // 2
    unit = (width // 16, UNIT)
    kept, used = attend_buffers(heads, tokens)
    feeds = feed_buffers(own, width, 8 * UNIT)
    feeds += [("out", (own, width), BF16), ("dctx", (2, own, UNIT), BF16)]
    free = pl.BlockSpec(memory_space=pl.ANY)
    vmem = pl.BlockSpec(memory_space=pltpu.VMEM)
    inputs = [("x_all", free), ("og_all", free), ("corner", vmem), ("omega", vmem), ("pick", vmem)]
    inputs += [(name, vmem) for name in ("attn", "shard_box", "vectors", "merge", "expand", "shrink")]
    outs = [(name + "_out", shape, kind, free) for name, shape, kind in kept]
    outs += [
        ("w_out", (3, width, cols), BF16, free),
        ("box_out", (PE, cols), BF16, vmem),
        ("out_full", (tokens, width), BF16, free),
        ("dctx_full", (tokens, cols), BF16, free),
        ("dh1l", (own, width), BF16, vmem),
        ("ge", (5, 2, 2, 4, 2, *unit), BF16, vmem),
        ("vsum", (VROWS, width), F32, vmem),
        ("sum_f", (4, *unit), F32, vmem),
    ]
    dma = pltpu.SemaphoreType.DMA
    scratch = [
        ("x", pltpu.VMEM((own, width), BF16)),
        ("og", pltpu.VMEM((own, width), BF16)),
        ("vec", pltpu.VMEM((VROWS, width), F32)),
        ("w", pltpu.VMEM((3, 2, 1, 4, 2, *unit), BF16)),
        ("box_gather", pltpu.VMEM((1, 2, 1, 4, 2, PE // 16, cols), F32)),
        ("vec_gather", pltpu.VMEM((1, 2, 2, 4, 2, VROWS, 128), F32)),
        ("we", pltpu.VMEM((5, 2, 2, 4, 2, *unit), BF16)),
        ("ws", pltpu.VMEM((4, 2, 2, 4, 2, *unit), BF16)),
        ("ctxx", pltpu.VMEM((2, own, cols), BF16)),
        ("gs", pltpu.VMEM((4, 2, 2, 4, 2, *unit), BF16)),
        ("fc", pltpu.VMEM((4, 2, 4, 2, *unit), BF16)),
        ("fy", pltpu.VMEM((4, 2, 4, *unit), BF16)),
        ("fz", pltpu.VMEM((4, 3, 2, *unit), BF16)),
        ("fx", pltpu.VMEM((4, *unit), BF16)),
        ("ctx_sem", dma((2, 3))),
        ("a_sem", dma((2, 3, SLOTS))),
        ("b_sem", dma((2, 1, SLOTS))),
        ("v_sem", dma((2, 1, SLOTS))),
        ("e_sem", dma((2, 5, SLOTS))),
        ("f_sem", dma((2, 4, SLOTS))),
        ("back_sem", dma((2, 4, SLOTS))),
        ("load_sem", dma((4,))),
        ("store_sem", dma((len(kept),))),
        ("swap_sem", dma((6, own // TILE))),
    ]
    names = [item[0] for item in inputs + outs + scratch]
    return pl.pallas_call(
        functools.partial(layer_kernel, heads, plan, inv_tokens, names, kept, used, feeds),
        out_shape=[jax.ShapeDtypeStruct(shape, kind) for _, shape, kind, _ in outs],
        in_specs=[item[1] for item in inputs],
        out_specs=[item[3] for item in outs],
        scratch_shapes=[item[1] for item in scratch],
        compiler_params=pltpu.CompilerParams(
            vmem_limit_bytes=VMEM_LIMIT, collective_id=0, has_side_effects=True
        ),
        name="layer_forward",
    )(x, og, corners, omega, pick, *shards)


def pair_place(cols):
    spot = lax.broadcasted_iota(jnp.int32, (cols, 2 * cols), 0)
    lane = lax.broadcasted_iota(jnp.int32, (cols, 2 * cols), 1)
    target = ((spot >> 6) << 7) + HD + (spot & (HD - 1))
    return jnp.where(lane == target, 1.0, 0.0)


def exact_dot(lhs, rhs, dims=NN):
    return lax.dot_general(
        lhs, rhs, dims, precision=lax.Precision.HIGHEST, preferred_element_type=F32
    )


def attend_back_kernel(heads, plan, inv_tokens, *refs):
    inputs, refs = refs[:12], refs[12:]
    if plan is not None:
        load_sem, held, refs = refs[-1], refs[-13:-1], refs[:-13]
        loads = [
            pltpu.make_async_copy(src, dst, load_sem.at[k]) for k, (src, dst) in enumerate(zip(inputs, held))
        ]
        early = (0, 2, 7, 11)
        for k in sorted(range(12), key=lambda k: k not in early):
            loads[k].start()
        inputs = held
    x_ref, w_ref, box_ref, *inputs = inputs
    qa_ref, qtok_ref, kvtok_ref, kt_ref, kft_ref, trig_ref, ctxt_ref, log_ref, dctx_ref = inputs
    cols = heads * HD
    tokens = x_ref.shape[0]
    pages = tokens // PAGE
    m = lax.axis_index("mp")
    piece = PAGE // 2
    pieces = 2 * pages
    lane = lax.broadcasted_iota(jnp.int32, (1, 2 * HD), 1)
    lower = lane < HD
    if plan is None:
        inp_ref, gw_ref, gbox_ref, qvsum_ref, *refs = refs
        kftok, dctxt, boxt, dtok, xt, gbox = refs
        before, after = 0, 0

        def background(number):
            pass
    else:
        dh1_ref, vsum_ref, sumf_ref, pick_ref, full_e, *refs = refs
        inp_ref, sum_e, sum_a, sum_b, sum_v, norm_ref, *refs = refs
        kftok, dctxt, boxt, dtok, xt, gbox, *refs = refs
        came, total_e, full_a, full_b, full_v, land_v, norms, *refs = refs
        ec, ey, ez, ex, ac, ay, az, bc, by, bz, *refs = refs
        e_sem, a_sem, b_sem, v_sem, n_sem, i_sem, loc_sem = refs
        place = Place()
        place.signal_all()
        fill = pltpu.make_async_copy(full_e.at[:, place.c], total_e, loc_sem.at[0])
        fill.start()
        place.wait_all()

        def finish(out):
            def put(chunk, value):
                out[chunk] = value * inv_tokens

            return put

        tree_e = Reduce(
            place, full_e, total_e, dict(c=ec, y=ey, z=ez, x=ex), 5, "cyzx", e_sem, finish(sum_e)
        )
        tree_e.lag, tree_e.held_back = 2, 1
        tree_a = Reduce(place, full_a, None, dict(c=ac, y=ay, z=az), 3, "cyz", a_sem, finish(sum_a))
        tree_b = Reduce(place, full_b, None, dict(c=bc, y=by, z=bz), 1, "cyz", b_sem, finish(sum_b))

        def block_of(rank):
            r = rank % 16
            return full_v.at[rank // 16, r // 4, (r // 2) % 2, r % 2]

        spot = (place.m, place.z, place.y, place.c)
        all_v = Everyone(place, block_of, lambda step: land_v.at[step - 1], v_sem)
        all_n = Everyone(place, lambda rank: norms.at[spot], lambda step: norms.at[spot], n_sem)

        def background(number):
            tree_e.event(number)

        background(0)
        fill.wait()
        for k in early:
            loads[k].wait()

    boxt[...] = box_ref[...].T
    gbox[...] = jnp.zeros_like(gbox)

    def prepare(page, carry):
        rows = aligned(page, PAGE)
        kftok[rows, :] = kft_ref[:, rows].T
        dctxt[:, rows] = dctx_ref[rows, :].T
        xt[:, rows] = x_ref[rows, :].T
        if plan is not None:
            pl.when(page == pages - 1)(lambda: background(1))
        return carry

    lax.fori_loop(0, pages, prepare, 0)
    if plan is not None:
        for k in range(12):
            if k not in early:
                loads[k].wait()

    def attend(step, carry):
        page, pair = step // (heads // 2), step % (heads // 2)
        rows = aligned(page, PAGE)
        own, partner = turn_factors(trig_ref[:, rows])
        pair_lanes = aligned(pair, 2 * HD)
        query_pair = qtok_ref[rows, pair_lanes]
        dctx_pair = dctx_ref[rows, pair_lanes]
        halves = []
        boxes = []
        blank = jnp.zeros((HD, PAGE), BF16)
        for side in range(2):
            head = pair * 2 + side
            lanes = aligned(head, 2 * HD)
            key_value = kvtok_ref[rows, lanes]
            left = jnp.concatenate([kftok[rows, :], key_value], axis=1)
            score = dot(left, jnp.concatenate([qa_ref[head, :, rows], blank], axis=0))
            prob = jnp.exp(score - log_ref[head, :, rows])
            prob_low = prob.astype(BF16)
            head_rows = pl.ds(pl.multiple_of(head * HD, HD), HD)
            dctx_head = dctxt[head_rows, rows]
            grad_prob = dot(
                key_value, jnp.concatenate([blank, dctx_head], axis=0)
            )
            inner = col_sum(dctx_head.astype(F32) * ctxt_ref[head_rows, rows].astype(F32))
            grad_score = (prob * (grad_prob - inner)).astype(BF16)
            if side == 0:
                both = jnp.concatenate([query_pair[:, 0:HD], dctx_pair[:, 0:HD]], axis=1)
            else:
                both = jnp.concatenate([query_pair[:, HD:], dctx_pair[:, HD:]], axis=1)
            from_score = dot(grad_score, both)
            from_prob = dot(prob_low, both)
            grad_kv = jnp.where(lower, from_score, from_prob).astype(BF16)
            dtok[rows, pl.ds(pl.multiple_of(cols + head * 2 * HD, 2 * HD), 2 * HD)] = grad_kv
            keys = jnp.concatenate([kft_ref[:, rows], kt_ref[head_rows, rows]], axis=0)
            grad_query = dot(keys, grad_score) * HD ** (-0.5)
            feat = grad_query[0:PE]
            proj = (feat * own - swap_blocks(feat) * partner).astype(BF16)
            halves.append(grad_query[PE:] + dot(boxt[head_rows, :], proj))
            boxes.append(dot(proj, query_pair))
        gbox[:, pair_lanes] += jnp.where(lower, boxes[0], boxes[1])
        dtok[rows, pair_lanes] = jnp.concatenate(halves, axis=0).astype(BF16).T
        return carry

    def spread(page):
        rows = aligned(page, PAGE)
        return sum(
            dot(dtok[rows, chunk * UNIT : (chunk + 1) * UNIT], w_ref[chunk], NT) for chunk in range(3)
        )

    if plan is None:
        lax.fori_loop(0, pages * (heads // 2), attend, 0)
        gbox_ref[...] = gbox[...] * HD**0.5

        def spread_page(page, carry):
            inp_ref[aligned(page, PAGE), :] = spread(page)
            return carry

        lax.fori_loop(0, pages, spread_page, 0)

        def gather(step, carry):
            lanes = aligned(step, UNIT)
            gw_ref[step] = dot(xt[...], dtok[:, lanes]).astype(BF16)
            qvsum_ref[0:1, lanes] = col_sum(dtok[:, lanes].astype(F32))
            return carry

        lax.fori_loop(0, 3, gather, 0)
        return

    def swap(index):
        rows = aligned(index, piece)
        return remote(
            inp_ref.at[rows, :], came.at[rows, :], i_sem.at[0, index], i_sem.at[1, index], place.peer["x"]
        )

    def attend_and_send(step, carry):
        attend(step, carry)
        page = step // (heads // 2)

        @pl.when(step % (heads // 2) == heads // 2 - 1)
        def _():
            value = spread(page)
            for half in range(2):
                index = 2 * page + half
                rows = aligned(index, piece)
                own = index // pages == m
                spot = aligned(index % pages, piece)
                extra = jnp.where(own, dh1_ref[spot, :].astype(F32), 0.0)
                inp_ref[rows, :] = (value[half * piece : (half + 1) * piece] + extra).astype(BF16)
                start_rows(
                    inp_ref.at[rows, :],
                    came.at[rows, :],
                    piece,
                    i_sem.at[0, index],
                    i_sem.at[1, index],
                    place.peer["x"],
                )

        pl.when(step % 3 != 2)(lambda: background(2 + 2 * (step // 3) + step % 3))
        return carry

    lax.fori_loop(0, pages * (heads // 2), attend_and_send, 0)
    put_natural(full_b, 0, 0, gbox[...] * HD**0.5)

    def gather(step, carry):
        grad = dot(xt[...], dtok[:, aligned(step, UNIT)]).astype(BF16)
        put_natural(full_a, step, 0, grad)
        tree_a.event(step)
        tree_b.event(step)
        background(8 + step)
        return carry

    lax.fori_loop(0, 3, gather, 0)

    sums = jnp.concatenate(
        [
            col_sum(dtok[:, chunk * UNIT : (chunk + 1) * UNIT].astype(F32)) for chunk in range(3)
        ],
        axis=1,
    )
    values = exact_dot(jnp.broadcast_to(sums[:, cols:], (8, 2 * cols)), pair_place(cols), NT)
    pair = jnp.concatenate([sums[:, 0:cols], values[0:1]], axis=0)
    blank = jnp.zeros_like(pair)
    pair = jnp.where(
        m == 0, jnp.concatenate([pair, blank], axis=1), jnp.concatenate([blank, pair], axis=1)
    )
    table = jnp.concatenate([vsum_ref[0:6, :], pair, vsum_ref[8:, :]], axis=0)
    mp_count, dp_count = plan
    width = table.shape[1]
    each = width // (mp_count * dp_count)
    wide_lane = lax.broadcasted_iota(jnp.int32, (VROWS, width), 1)
    for side in range(mp_count):
        parts = []
        for r in range(dp_count):
            first = (r * mp_count + side) * each
            parts.append(jnp.where((wide_lane >= first) & (wide_lane < first + each), table, 0.0))
        block = exact_dot(jnp.concatenate(parts, axis=0), pick_ref[...], NT)
        full_v[side] = block.reshape(full_v.shape[1:])
    all_v.start()

    def tail(number, carry):
        tree_a.event(number)
        tree_b.event(number)
        return carry

    lax.fori_loop(3, tree_a.events, tail, 0)
    tree_e.rest()
    all_v.wait()
    total_v = full_v[spot] + jnp.sum(land_v[...], axis=0)
    sum_v[0] = total_v * inv_tokens

    square = sum(jnp.sum(out[...] * out[...]) for out in (sum_e, sumf_ref, sum_a, sum_b, sum_v))
    norms[spot] = jnp.full((8, 128), square, F32)
    all_n.start()

    def final(number, carry):
        rows = aligned(number, piece)
        swap(number).wait()
        inp_ref[rows, :] = (inp_ref[rows, :].astype(F32) + came[rows, :].astype(F32)).astype(BF16)
        return carry

    lax.fori_loop(0, pieces, final, 0)
    all_n.wait()
    every = norms[...].reshape(-1, 8, 128)
    norm_ref[...] = jnp.sqrt(sum(every[k] for k in range(every.shape[0])))
    for tree in (tree_e, tree_a, tree_b):
        tree.drain()


def attend_backward(x, weight, box, kept, dctx, plan, inv_tokens, more=()):
    tokens, width = x.shape
    cols = weight.shape[-1]
    heads = cols // HD
    vmem = pl.BlockSpec(memory_space=pltpu.VMEM)
    scratch = [
        pltpu.VMEM((tokens, PE), BF16),
        pltpu.VMEM((cols, tokens), BF16),
        pltpu.VMEM((cols, PE), BF16),
        pltpu.VMEM((tokens, 3 * cols), BF16),
        pltpu.VMEM((width, tokens), BF16),
        pltpu.VMEM((PE, cols), F32),
    ]
    in_specs = [vmem] * 12
    if plan is None:
        shapes = [
            ((tokens, width), F32),
            ((3, width, cols), BF16),
            ((PE, cols), F32),
            ((8, 3 * cols), F32),
        ]
        extra = {}
    else:
        free = pl.BlockSpec(memory_space=pl.ANY)
        in_specs = [free] * 12 + [vmem] * 4 + [free]
        rows = width // 16
        unit = (rows, UNIT)
        tile = (PE // 16, cols)
        small = (VROWS, 128)
        shapes = [
            ((tokens, width), BF16),
            ((5, *unit), F32),
            ((3, *unit), F32),
            ((1, *tile), F32),
            ((1, *small), F32),
            ((8, 128), F32),
        ]
        scratch += [
            pltpu.VMEM((tokens, width), BF16),
            pltpu.VMEM((5, 2, 4, 2, *unit), BF16),
            pltpu.VMEM((3, 2, 1, 4, 2, *unit), BF16),
            pltpu.VMEM((1, 2, 1, 4, 2, *tile), F32),
            pltpu.VMEM((2, 4, 2, 2, *small), F32),
            pltpu.VMEM((31, *small), F32),
            pltpu.VMEM((2, 4, 2, 2, 8, 128), F32),
            pltpu.VMEM((5, 2, 4, 2, *unit), BF16),
            pltpu.VMEM((5, 2, 4, *unit), BF16),
            pltpu.VMEM((5, 3, 2, *unit), BF16),
            pltpu.VMEM((5, *unit), BF16),
            pltpu.VMEM((3, 4, 2, *unit), BF16),
            pltpu.VMEM((3, 4, *unit), BF16),
            pltpu.VMEM((3, 3, *unit), BF16),
            pltpu.VMEM((1, 4, 2, *tile), F32),
            pltpu.VMEM((1, 4, *tile), F32),
            pltpu.VMEM((1, 3, *tile), F32),
            pltpu.SemaphoreType.DMA((2, 5, SLOTS)),
            pltpu.SemaphoreType.DMA((2, 3, SLOTS)),
            pltpu.SemaphoreType.DMA((2, 1, SLOTS)),
            pltpu.SemaphoreType.DMA((2, 31)),
            pltpu.SemaphoreType.DMA((2, 31)),
            pltpu.SemaphoreType.DMA((2, 2 * (tokens // PAGE))),
            pltpu.SemaphoreType.DMA((2,)),
        ]
        scratch += [pltpu.VMEM(array.shape, array.dtype) for array in (x, weight, box, *kept, dctx)]
        scratch.append(pltpu.SemaphoreType.DMA((12,)))
        extra = dict(collective_id=2, has_side_effects=True)
    return pl.pallas_call(
        functools.partial(attend_back_kernel, heads, plan, inv_tokens),
        out_shape=[jax.ShapeDtypeStruct(s, d) for s, d in shapes],
        in_specs=in_specs,
        out_specs=[vmem] * len(shapes),
        scratch_shapes=scratch,
        compiler_params=pltpu.CompilerParams(vmem_limit_bytes=VMEM_LIMIT, **extra),
        cost_estimate=pl.CostEstimate(flops=4 * 10**10, bytes_accessed=10**8, transcendentals=10**7),
        name="attend_backward",
    )(x, weight, box, *kept, dctx, *more)


def adam_step(master, first, second, gradient, rate, decay):
    new_first = BETA_ONE * first + (1.0 - BETA_ONE) * gradient
    new_second = BETA_TWO * second + (1.0 - BETA_TWO) * gradient * gradient
    first_hat = new_first / (1.0 - BETA_ONE**STEP)
    second_hat = new_second / (1.0 - BETA_TWO**STEP)
    new_master = master - rate * (first_hat / (jnp.sqrt(second_hat) + ADAM_EPS) + decay * master)
    return (new_first, new_second, new_master)


def adam_kernel(heads, norm_ref, *refs):
    sum_e, sum_f, sum_a, sum_b, sum_v, *refs = refs
    states, outs = refs[:18], refs[18:]
    outs[-1][...] = norm_ref[0:1, 0:1]
    clip = CLIP_LIMIT / jnp.maximum(norm_ref[0:1, 0:1], CLIP_LIMIT)

    def update(first, out, gradient, at, rate, decay):
        news = adam_step(*(ref[at] for ref in states[first : first + 3]), gradient * clip, rate, decay)
        for ref, new in zip(outs[out : out + 3], news):
            ref[at] = new
        if decay:
            outs[out + 3][at] = news[2].astype(BF16)

    def heads_of(kind):
        half = heads // 2
        return jnp.concatenate(
            [
                sum_a[1 + head // half, :, (2 * (head % half) + kind) * HD : (2 * (head % half) + kind + 1) * HD]
                for head in range(heads)
            ],
            axis=1,
        )

    for index, gradient in enumerate((sum_a[0], heads_of(0), heads_of(1))):
        update(0, 0, gradient, index, RATE_MATRIX, WEIGHT_DECAY)
    update(3, 4, sum_b[0], ALL, RATE_MATRIX, WEIGHT_DECAY)
    update(6, 8, sum_e[0], ALL, RATE_MATRIX, WEIGHT_DECAY)
    for chunk in range(4):
        lanes = (ALL, slice(chunk * UNIT, (chunk + 1) * UNIT))
        update(9, 12, sum_e[1 + chunk], lanes, RATE_MATRIX, WEIGHT_DECAY)
        update(12, 16, sum_f[chunk], lanes, RATE_MATRIX, WEIGHT_DECAY)
    rows, each = states[15].shape
    update(15, 20, sum_v[0, 0:rows, 0:each], ALL, RATE_VECTOR, 0.0)


def adam_all(norm, sums, states):
    shapes = []
    for first in range(0, 18, 3):
        shapes += [(states[first].shape, F32)] * 3
        if first < 15:
            shapes.append((states[first].shape, BF16))
    vmem = pl.BlockSpec(memory_space=pltpu.VMEM)
    shapes.append(((1, 1), F32))
    return pl.pallas_call(
        functools.partial(adam_kernel, states[0].shape[2] // HD),
        out_shape=[jax.ShapeDtypeStruct(s, d) for s, d in shapes],
        in_specs=[vmem] * (6 + len(states)),
        out_specs=[vmem] * len(shapes),
        compiler_params=pltpu.CompilerParams(vmem_limit_bytes=VMEM_LIMIT),
        name="adam_all",
    )(norm, *sums, *states)


def pack_qkv(shard):
    rows, cols = shard.shape[1:]
    heads = cols // HD
    pairs = jnp.stack([shard[1].reshape(rows, heads, HD), shard[2].reshape(rows, heads, HD)], axis=2)
    pairs = pairs.reshape(rows, 2, cols)
    return jnp.stack([shard[0], pairs[:, 0], pairs[:, 1]])


def unpack_qkv(packed):
    rows, cols = packed.shape[1:]
    pairs = jnp.concatenate([packed[1], packed[2]], axis=1).reshape(rows, cols // HD, 2, HD)
    return jnp.stack(
        [packed[0], pairs[:, :, 0].reshape(rows, cols), pairs[:, :, 1].reshape(rows, cols)]
    )


def to_chunks(shard):
    rows = shard.shape[0]
    return shard.reshape(rows, -1, UNIT).transpose(1, 0, 2)


def from_chunks(chunks):
    return chunks.transpose(1, 0, 2).reshape(chunks.shape[1], -1)


def on_device(
    layer_input,
    page_boxes,
    output_grad,
    attn_proj,
    attn_first,
    attn_second,
    box_proj,
    box_first,
    box_second,
    merge_proj,
    merge_first,
    merge_second,
    expand_proj,
    expand_first,
    expand_second,
    shrink_proj,
    shrink_first,
    shrink_second,
    vectors,
    vector_first,
    vector_second,
):
    mp_count = lax.axis_size("mp")
    dp_count = lax.axis_size("dp")
    mp_index = lax.axis_index("mp")
    tokens, width = layer_input.shape
    cols = attn_proj.shape[2]
    heads = cols // HD
    own_tokens = tokens // mp_count
    inv_tokens = 1.0 / (tokens * dp_count)

    corners = page_boxes.T
    omega = (10000.0 ** (-np.arange(FREQS, dtype=np.float64) / FREQS)).astype(np.float32)[:, None]
    omega = jnp.asarray(omega)
    plan = (mp_count, dp_count) if dp_count == 16 and mp_count == 2 else None
    if plan is not None:
        each = vectors.shape[1]
        pick = np.zeros((128, width), np.float32)
        pick[np.arange(width) % each, np.arange(width)] = 1.0
        pick = jnp.asarray(pick)
        *kept, w_qkv, w_box, layer_out, dctx, dh1, g_expand, vec_sum, sum_f = layer_forward(
            layer_input,
            output_grad,
            corners,
            omega,
            pick,
            (attn_proj, box_proj, vectors, merge_proj.T, expand_proj, shrink_proj.T),
            plan,
            inv_tokens,
        )
        input_grad, sum_e, sum_a, sum_b, sum_v, norm = attend_backward(
            layer_input,
            w_qkv,
            w_box,
            kept,
            dctx,
            plan,
            inv_tokens,
            (dh1, vec_sum, sum_f, pick, g_expand),
        )
        merge = [merge_proj.T, merge_first.T, merge_second.T]
        shrink = [shrink_proj.T, shrink_first.T, shrink_second.T]
        *results, norm = adam_all(
            norm,
            (sum_e, sum_f, sum_a, sum_b, sum_v),
            [attn_proj, attn_first, attn_second, box_proj, box_first, box_second, *merge]
            + [expand_proj, expand_first, expand_second, *shrink, vectors, vector_first, vector_second],
        )
        turned = (8, 9, 10, 11, 16, 17, 18, 19)
        results = [out.T if k in turned else out for k, out in enumerate(results)]
        return (layer_out, input_grad, norm.reshape(()), *results)
    shard_qkv = pack_qkv(attn_proj).astype(BF16)
    shard_e = jnp.concatenate([merge_proj.T[None], to_chunks(expand_proj)]).astype(BF16)
    shard_f = to_chunks(shrink_proj.T).astype(BF16)
    w_qkv = lax.all_gather(shard_qkv, "dp", axis=1, tiled=True)
    w_box = lax.all_gather(box_proj.astype(BF16), "dp", axis=0, tiled=True)
    w_expand = lax.all_gather(lax.all_gather(shard_e, "dp", axis=1, tiled=True), "mp", axis=1)
    w_shrink = lax.all_gather(lax.all_gather(shard_f, "dp", axis=1, tiled=True), "mp", axis=1)
    vecs = lax.all_gather(vectors, ("dp", "mp"), axis=1, tiled=True)
    vecs = jnp.pad(vecs, ((0, VROWS - vecs.shape[0]), (0, 0)))
    *kept, context = attend_forward(layer_input, corners, omega, w_qkv, w_box, vecs)
    context = lax.all_to_all(
        context.reshape(mp_count, own_tokens, cols), "mp", split_axis=0, concat_axis=0
    )

    def own_rows(array):
        return lax.dynamic_slice_in_dim(array, mp_index * own_tokens, own_tokens)

    layer_out, dctx, dh1, g_expand, g_shrink, vec_sum = feed_both(
        own_rows(layer_input), own_rows(output_grad), context, w_expand, w_shrink, vecs
    )
    g_feed = jnp.concatenate([g_expand, g_shrink])
    layer_out = lax.all_gather(layer_out, "mp", axis=0, tiled=True)
    dctx = lax.all_to_all(dctx, "mp", split_axis=0, concat_axis=0).reshape(tokens, cols)
    part, g_qkv, g_box, qkv_sum = attend_backward(
        layer_input, w_qkv, w_box, kept, dctx, None, inv_tokens
    )
    own_part = lax.psum_scatter(part.astype(BF16), "mp", scatter_dimension=0, tiled=True)
    own_grad = (own_part.astype(F32) + dh1).astype(BF16)
    input_grad = lax.all_gather(own_grad, "mp", axis=0, tiled=True)
    shard_attn = unpack_qkv(
        lax.psum_scatter(g_qkv, "dp", scatter_dimension=1, tiled=True).astype(F32) * inv_tokens
    )
    shard_box = lax.psum_scatter(g_box, "dp", scatter_dimension=0, tiled=True) * inv_tokens
    sum_feed = lax.psum_scatter(g_feed, "dp", scatter_dimension=2, tiled=True)
    sum_feed = lax.psum_scatter(sum_feed, "mp", scatter_dimension=1, tiled=True)[:, 0]
    sum_feed = sum_feed.astype(F32) * inv_tokens
    sum_expand, sum_shrink = sum_feed[0:5], sum_feed[5:]

    def placed(row):
        return lax.dynamic_update_slice_in_dim(
            jnp.zeros((width,), F32), row, mp_index * cols, 0
        )[None, :]

    value_sum = qkv_sum[0, cols:].reshape(heads, 2, HD)[:, 1].reshape(cols)
    vector_grad = jnp.concatenate(
        [vec_sum[0:6], placed(qkv_sum[0, 0:cols]), placed(value_sum), vec_sum[8:12]]
    )
    vector_shard = (
        lax.psum_scatter(vector_grad, ("dp", "mp"), scatter_dimension=1, tiled=True) * inv_tokens
    )
    square = sum(
        jnp.sum(shard * shard)
        for shard in (shard_attn, shard_box, sum_expand, sum_shrink, vector_shard)
    )
    grad_norm = jnp.sqrt(lax.psum(square, ("dp", "mp")))
    shard_merge = sum_expand[0].T
    shard_expand = from_chunks(sum_expand[1:])
    shard_shrink = from_chunks(sum_shrink).T
    clip_scale = CLIP_LIMIT / jnp.maximum(grad_norm, CLIP_LIMIT)
    results = [layer_out, input_grad, grad_norm]
    for master, first, second, shard in (
        (attn_proj, attn_first, attn_second, shard_attn),
        (box_proj, box_first, box_second, shard_box),
        (merge_proj, merge_first, merge_second, shard_merge),
        (expand_proj, expand_first, expand_second, shard_expand),
        (shrink_proj, shrink_first, shrink_second, shard_shrink),
    ):
        new_first, new_second, new_master = adam_step(
            master, first, second, shard * clip_scale, RATE_MATRIX, WEIGHT_DECAY
        )
        results += [new_first, new_second, new_master, new_master.astype(BF16)]
    results += adam_step(
        vectors, vector_first, vector_second, vector_shard * clip_scale, RATE_VECTOR, 0.0
    )
    return tuple(results)


def solution(mesh):
    rows = P("dp", None)
    attn = P(None, "dp", "mp")
    tall = P("dp", "mp")
    wide = P("mp", "dp")
    vector = P(None, ("dp", "mp"))
    in_specs = (rows,) * 3 + (attn,) * 3 + (tall,) * 3 + (wide,) * 3 + (tall,) * 3 + (wide,) * 3
    in_specs += (vector,) * 3
    out_specs = (rows, rows, P()) + (attn,) * 4 + (tall,) * 4 + (wide,) * 4 + (tall,) * 4
    out_specs += (wide,) * 4 + (vector,) * 3
    return jax.shard_map(
        on_device, mesh=mesh, in_specs=in_specs, out_specs=out_specs, check_vma=False
    )
```
